32 devices in a mesh: pipe: 2 (over x), dp: 16 (over z, y, core).
Axes of the slice: x: 2, y: 2, z: 4, core: 2. Of those that a mesh axis runs over, the one named last changes fastest.
Arguments:
- inputs: bfloat16 [32, 384, 1280], P('dp'), may hold values from -6 to 6
- out_grad: bfloat16 [32, 384, 1280], P('dp'), may hold values from -6 to 6
- query_counts: int32 [32], P('dp'), may hold values from 50 to 2000
- gains: bfloat16 [2, 2, 1280], P('pipe', None, 'dp'), may hold values from 0.5 to 1.5
- shifts: bfloat16 [2, 6, 1280], P('pipe', None, 'dp'), may hold values from -1.75 to 1.75
- w_qkv: bfloat16 [2, 1280, 3840], P('pipe', 'dp'), may hold values from -0.15625 to 0.15625
- w_out: bfloat16 [2, 1280, 1280], P('pipe', 'dp'), may hold values from -2 to 2
- w_up: bfloat16 [2, 1280, 5120], P('pipe', 'dp'), may hold values from -0.15625 to 0.15625
- b_up: bfloat16 [2, 5120], P('pipe', 'dp'), may hold values from -1.75 to 1.75
- w_down: bfloat16 [2, 5120, 1280], P('pipe', 'dp'), may hold values from -0.078125 to 0.078125
Outputs:
- section_outputs: bfloat16 [2, 32, 384, 1280], P('pipe', 'dp')
- input_grads: bfloat16 [2, 32, 384, 1280], P('pipe', 'dp')
- gains_grad: float32 [2, 2, 1280], P('pipe', None, 'dp')
- shifts_grad: float32 [2, 6, 1280], P('pipe', None, 'dp')
- w_qkv_grad: float32 [2, 1280, 3840], P('pipe', 'dp')
- w_out_grad: float32 [2, 1280, 1280], P('pipe', 'dp')
- w_up_grad: float32 [2, 1280, 5120], P('pipe', 'dp')
- b_up_grad: float32 [2, 5120], P('pipe', 'dp')
- w_down_grad: float32 [2, 5120, 1280], P('pipe', 'dp')
The draws below stay inside these ranges and needn't reach their ends.
Inputs may be any that keep to these rules, and one draw needn't show every extreme that they name: `query_counts`: per-cell query counts.
All inputs are finite; a program needn't handle non-finite values.
Results may differ from the reference program's by a relative error of at most 0.014.
Values may be sent and summed in bfloat16 or wider, within the bound.
A program may use at most 320 MiB of HBM per device.

```python
import math
import jax
import jax.numpy as jnp
from jax import lax

D = 1280
HEAD_DIM = 64
FF = 5120
CELL_LEN = 384
CELLS = 32
N_PIPE = 2


def set_ends(entries, stream_key, least, high):
    longest = entries.shape.index(max(entries.shape))
    spots = []
    for shift in (0, 1):
        where = [jax.random.randint(jax.random.fold_in(stream_key, axis), (), 0, length) for axis, length in enumerate(entries.shape)]
        where[longest] = (where[longest] + shift) % entries.shape[longest]
        spots.append(tuple(where))
    return entries.at[spots[0]].set(least).at[spots[1]].set(high)


def block_levels(stream_key, shape, shards, least, top_value):
    gain, own = 1.0, jax.random.fold_in(stream_key, 6)
    for axis_at, parts in shards:
        draws = jnp.exp(jax.random.uniform(jax.random.fold_in(own, axis_at), (parts,), jnp.float32, least / len(shards), top_value / len(shards)))
        gain = gain * jnp.repeat(draws, shape[axis_at] // parts).reshape([-1 if axis == axis_at else 1 for axis in range(len(shape))])
    return gain


def centred(key, shape, deviation, limit, split=(), held_as=jnp.bfloat16):
    factor_of = block_levels(key, shape, split, -0.22, 0.18) if split else 1.0
    result = jax.random.normal(key, shape, jnp.float32) * deviation * factor_of
    return jnp.minimum(jnp.maximum(result, -limit), limit).astype(held_as)


def setup_inputs(seed: int = 0) -> dict:
    streams_of = jax.random.split(jax.random.key(seed), 11)
    return {
        "inputs": centred(streams_of[0], (CELLS, CELL_LEN, D), 1.0, 6.0, ((0, 16),)),
        "out_grad": centred(streams_of[1], (CELLS, CELL_LEN, D), 1.0, 6.0, ((0, 16),)),
        "query_counts": set_ends(jax.random.randint(streams_of[2], (CELLS,), 50, 2001), jax.random.fold_in(streams_of[2], 1), 50, 2000).astype(jnp.int32),
        "gains": jnp.clip(1.0 + 0.1 * jax.random.normal(streams_of[3], (N_PIPE, 2, D), jnp.float32), 0.5, 1.5).astype(jnp.bfloat16),
        "shifts": centred(streams_of[4], (N_PIPE, 6, D), 0.3, 1.75, ((0, 2), (2, 16))),
        "w_qkv": centred(streams_of[5], (N_PIPE, D, 3 * D), D ** -0.5, 0.15625, ((0, 2), (1, 16))),
        "w_out": centred(streams_of[6], (N_PIPE, D, D), (max(D // 128, 4)) ** -0.5, 2.0, ((0, 2), (1, 16))),
        "w_up": centred(streams_of[7], (N_PIPE, D, FF), D ** -0.5, 0.15625, ((0, 2), (1, 16))),
        "b_up": centred(streams_of[8], (N_PIPE, FF), 0.3, 1.75, ((0, 2), (1, 16))),
        "w_down": centred(streams_of[9], (N_PIPE, FF, D), FF ** -0.5, 0.078125, ((0, 2), (1, 16))),
    }


highest = lax.Precision.HIGHEST

@jax.custom_vjp
def low(v):
    return lax.optimization_barrier(v.astype(jnp.bfloat16)).astype(jnp.float32)

@jax.custom_vjp
def low_back(v):
    return v

def low_keep(v):
    return (low(v), None)

def low_pass(kept, grad):
    return (grad,)

def back_keep(v):
    return (v, None)

def back_low(kept, grad):
    return (low(grad),)
low.defvjp(low_keep, low_pass)
low_back.defvjp(back_keep, back_low)

def round_both(value_in):
    return low(low_back(value_in))

def norm_rows(rows_in):
    center = rows_in - lax.optimization_barrier(jnp.mean(rows_in, axis=-1, keepdims=True))
    return center * lax.rsqrt(lax.optimization_barrier(jnp.mean(center * center, axis=-1, keepdims=True)) + 1e-05)

def layer_block(rows_in, gains, shifts, w_qkv, w_out, w_up, b_up, w_down):
    model_width = rows_in.shape[-1]
    head_count = model_width // HEAD_DIM
    length = rows_in.shape[0]
    lowered = low(norm_rows(rows_in) * gains[0] + shifts[0])
    packed = jnp.dot(lowered, w_qkv, precision=highest)
    queries = round_both(packed[:, :model_width] + shifts[1]).reshape(length, head_count, HEAD_DIM)
    key_rows = round_both(packed[:, model_width:2 * model_width]).reshape(length, head_count, HEAD_DIM)
    values = round_both(packed[:, 2 * model_width:] + shifts[2]).reshape(length, head_count, HEAD_DIM)
    scores = low_back(jnp.einsum('qhd,khd->hqk', queries, key_rows, precision=highest) * (1.0 / math.sqrt(HEAD_DIM)))
    attn_probs = low(jax.nn.softmax(scores, axis=-1))
    mixed_out = round_both(jnp.einsum('hqk,khd->qhd', attn_probs, values, precision=highest).reshape(length, model_width))
    middle = rows_in + low_back(jnp.dot(mixed_out, w_out, precision=highest) + shifts[3])
    second = low(norm_rows(middle) * gains[1] + shifts[4])
    hidden_pre = low_back(jnp.dot(second, w_up, precision=highest) + b_up)
    activated = low(jax.nn.gelu(hidden_pre, approximate=False))
    return middle + low_back(jnp.dot(activated, w_down, precision=highest) + shifts[5])

def reference(inputs, out_grad, query_counts, gains, shifts, w_qkv, w_out, w_up, b_up, w_down):
    sections = gains.shape[0]
    params = tuple((array.astype(jnp.float32) for array in (gains, shifts, w_qkv, w_out, w_up, b_up, w_down)))
    start_rows = inputs.astype(jnp.float32)
    markers = jnp.zeros((inputs.shape[0], sections - 1) + inputs.shape[1:], jnp.float32)

    def forward(start_rows, markers, *weights):

        def one_cell(element):
            rows_in, mark_rows = element
            sent_rows = []
            rows_out = rows_in
            for layer_index in range(sections):
                rows_out = layer_block(rows_in, *(weight_set[layer_index] for weight_set in weights))
                if layer_index < sections - 1:
                    rows_in = low_back(low(rows_out) + mark_rows[layer_index])
                    sent_rows.append(rows_in)
                else:
                    sent_rows.append(rows_out)
            return (rows_out, jnp.stack(sent_rows))
        return lax.map(jax.checkpoint(one_cell), (start_rows, markers))
    final_rows, pullback, sent_rows = jax.vjp(forward, start_rows, markers, *params, has_aux=True)
    weight = jnp.sqrt(query_counts.astype(jnp.float32) / 500.0)
    gradients = pullback(out_grad.astype(jnp.float32) * weight[:, None, None])
    section_outputs = jnp.swapaxes(sent_rows, 0, 1).astype(jnp.bfloat16)
    input_grads = jnp.concatenate([gradients[0][None], jnp.swapaxes(gradients[1], 0, 1)], axis=0).astype(jnp.bfloat16)
    return (section_outputs, input_grads, gradients[2], gradients[3], gradients[4], gradients[5], gradients[6], gradients[7], gradients[8])
```

```python
import functools
import math

import jax
import jax.numpy as jnp
from jax import lax
from jax.experimental import pallas as pl
from jax.experimental.pallas import tpu as pltpu
from jax.sharding import PartitionSpec as P

HEAD_DIM = 64
MESH = pl.DeviceIdType.MESH
LOW = jnp.bfloat16
F32 = jnp.float32


def ring_chip(position, chips):
    position = lax.rem(position + 2 * chips, chips)
    half = chips // 2
    return jnp.where(position < half, 2 * position, 2 * (chips - 1 - position) + 1)


def ring_place(chips):
    me = lax.axis_index("dp")
    core = lax.rem(me, 2)
    chip = me // 2
    position = jnp.where(lax.rem(chip, 2) == 0, chip // 2, chips - 1 - chip // 2)
    right = ring_chip(position + 1, chips) * 2 + core
    left = ring_chip(position - 1, chips) * 2 + core
    return (me, core, position, right, left, me + 1 - 2 * core)


def greet(devices):
    barrier = pltpu.get_barrier_semaphore()
    for device in devices:
        pl.semaphore_signal(barrier, inc=1, device_id={"dp": device}, device_id_type=MESH)
    pl.semaphore_wait(barrier, len(devices))


def gather_kernel(chips, splits, *refs):
    count = len(splits)
    shards, outs = (refs[:count], refs[count : 2 * count])
    ring_send, ring_recv, pair_send, pair_recv, own_sem = refs[2 * count :]
    half = chips // 2
    me, core, position, right, left, sibling = ring_place(chips)
    greet((left, right, sibling))

    def owner(step, way):
        return ring_chip(position - step if way == 0 else position + step, chips) * 2 + core

    def travels(item, way, step):
        return step < half or (step == half and splits[item] == way)

    def ring_copy(item, way, step):
        block = owner(step - 1, way)
        return pltpu.make_async_remote_copy(
            src_ref=shards[item] if step == 1 else outs[item].at[block],
            dst_ref=outs[item].at[block],
            send_sem=ring_send.at[item, way, step - 1],
            recv_sem=ring_recv.at[item, way, step - 1],
            device_id={"dp": right if way == 0 else left},
            device_id_type=MESH,
        )

    def pair_copy(item, offset, block, source):
        return pltpu.make_async_remote_copy(
            src_ref=source,
            dst_ref=outs[item].at[block],
            send_sem=pair_send.at[item, offset],
            recv_sem=pair_recv.at[item, offset],
            device_id={"dp": sibling},
            device_id_type=MESH,
        )

    sent, paired, kept = ([], [], [])
    for item in range(count):
        for way in (0, 1):
            if travels(item, way, 1):
                sent.append(ring_copy(item, way, 1))
                sent[-1].start()
    for item in range(count):
        paired.append(pair_copy(item, 0, me, shards[item]))
        paired[-1].start()
        kept.append(pltpu.make_async_copy(shards[item], outs[item].at[me], own_sem.at[item]))
        kept[-1].start()
    for step in range(1, half + 1):
        for item in range(count):
            for way in (0, 1):
                if not travels(item, way, step):
                    continue
                ring_copy(item, way, step).wait_recv()
                if travels(item, way, step + 1):
                    sent.append(ring_copy(item, way, step + 1))
                    sent[-1].start()
                block = owner(step, way)
                offset = step if way == 0 else chips - step
                paired.append(pair_copy(item, offset, block, outs[item].at[block]))
                paired[-1].start()
    for copy in sent:
        copy.wait_send()
    for copy in paired:
        copy.wait()
    for copy in kept:
        copy.wait()


def gather(shards, splits, count):
    chips = count // 2
    items = len(shards)
    return pl.pallas_call(
        functools.partial(gather_kernel, chips, splits),
        out_shape=[jax.ShapeDtypeStruct((count,) + shard.shape, shard.dtype) for shard in shards],
        in_specs=[pl.BlockSpec(memory_space=pl.ANY)] * items,
        out_specs=[pl.BlockSpec(memory_space=pl.ANY)] * items,
        scratch_shapes=[
            pltpu.SemaphoreType.DMA((items, 2, chips // 2)),
            pltpu.SemaphoreType.DMA((items, 2, chips // 2)),
            pltpu.SemaphoreType.DMA((items, chips)),
            pltpu.SemaphoreType.DMA((items, chips)),
            pltpu.SemaphoreType.DMA((items,)),
        ],
        compiler_params=pltpu.CompilerParams(collective_id=0, has_side_effects=True),
    )(*shards)


def scatter_kernel(chips, splits, *refs):
    count = len(splits)
    parts, outs = (refs[:count], refs[count : 2 * count])
    landed, paired, mine = (refs[2 * count : 3 * count], refs[3 * count : 4 * count], refs[4 * count : 5 * count])
    ring_send, ring_recv, pair_send, pair_recv, mine_sem = refs[5 * count :]
    half = chips // 2
    me, core, position, right, left, sibling = ring_place(chips)
    greet((left, right, sibling))

    def first(item, way):
        return 1 if splits[item] == way else 2

    def slot(item, way, step):
        return step - 1 if splits[item] == way else half + step - 2

    def offset_of(step, way):
        return half - step + 1 if way == 0 else chips - (half - step + 1)

    def pair_copy(item, offset):
        block = ring_chip(position + offset, chips) * 2 + 1 - core
        return pltpu.make_async_remote_copy(
            src_ref=parts[item].at[block],
            dst_ref=paired[item].at[offset],
            send_sem=pair_send.at[item, offset],
            recv_sem=pair_recv.at[item, offset],
            device_id={"dp": sibling},
            device_id_type=MESH,
        )

    def ring_copy(item, way, step):
        if step == first(item, way):
            source = paired[item].at[offset_of(step, way)]
        else:
            source = landed[item].at[slot(item, way, step - 1)]
        here = slot(item, way, step)
        return pltpu.make_async_remote_copy(
            src_ref=source,
            dst_ref=landed[item].at[here],
            send_sem=ring_send.at[item, here],
            recv_sem=ring_recv.at[item, here],
            device_id={"dp": right if way == 0 else left},
            device_id_type=MESH,
        )

    def load(item, offset, buffer):
        block = ring_chip(position + offset, chips) * 2 + core
        return pltpu.make_async_copy(parts[item].at[block], mine[item].at[buffer], mine_sem.at[item, buffer])

    plan, uses = ([], [0] * count)
    for step in range(1, half + 2):
        for item in range(count):
            for way in (0, 1):
                if step <= half and step >= first(item, way):
                    plan.append((step, item, way, offset_of(step, way), uses[item] % 2))
                    uses[item] += 1
            if step > half:
                plan.append((step, item, None, 0, uses[item] % 2))
                uses[item] += 1
    for step, item, way, offset, buffer in plan:
        pair_copy(item, offset).start()
    load(plan[0][1], plan[0][3], plan[0][4]).start()
    sent = []
    for number, (step, item, way, offset, buffer) in enumerate(plan):
        if number + 1 < len(plan):
            load(plan[number + 1][1], plan[number + 1][3], plan[number + 1][4]).start()
        load(item, offset, buffer).wait()
        pair_copy(item, offset).wait_recv()
        rows = parts[item].shape[1]
        kind = parts[item].dtype
        chunk = 16 if rows % 16 == 0 else rows
        from_pair, from_mine, from_ring = (paired[item], mine[item], landed[item])
        if way is None:
            ring_copy(item, 0, half).wait_recv()
            ring_copy(item, 1, half).wait_recv()
            slot_a, slot_b = (slot(item, 0, half), slot(item, 1, half))

            @pl.loop(0, rows // chunk)
            def _(index):
                here = pl.ds(pl.multiple_of(index * chunk, chunk), chunk)
                outs[item][here, :] = (
                    from_ring[slot_a, here, :].astype(F32) + from_ring[slot_b, here, :].astype(F32)
                ) + (from_mine[buffer, here, :].astype(F32) + from_pair[offset, here, :].astype(F32))

            continue
        if step == first(item, way):

            @pl.loop(0, rows // chunk)
            def _(index):
                here = pl.ds(pl.multiple_of(index * chunk, chunk), chunk)
                from_pair[offset, here, :] = (
                    from_mine[buffer, here, :].astype(F32) + from_pair[offset, here, :].astype(F32)
                ).astype(kind)

        else:
            ring_copy(item, way, step - 1).wait_recv()
            arrived = slot(item, way, step - 1)

            @pl.loop(0, rows // chunk)
            def _(index):
                here = pl.ds(pl.multiple_of(index * chunk, chunk), chunk)
                from_ring[arrived, here, :] = (
                    from_ring[arrived, here, :].astype(F32)
                    + (from_mine[buffer, here, :].astype(F32) + from_pair[offset, here, :].astype(F32))
                ).astype(kind)

        sent.append(ring_copy(item, way, step))
        sent[-1].start()
    for copy in sent:
        copy.wait_send()
    for step, item, way, offset, buffer in plan:
        pair_copy(item, offset).wait_send()


def scatter(parts, splits, count):
    chips = count // 2
    items = len(parts)
    shapes = [part.shape[1:] for part in parts]
    kinds = [part.dtype for part in parts]
    return pl.pallas_call(
        functools.partial(scatter_kernel, chips, splits),
        out_shape=[jax.ShapeDtypeStruct(shape, F32) for shape in shapes],
        in_specs=[pl.BlockSpec(memory_space=pl.ANY)] * items,
        out_specs=[pl.BlockSpec(memory_space=pltpu.VMEM)] * items,
        scratch_shapes=[pltpu.VMEM((chips - 1,) + shape, kind) for shape, kind in zip(shapes, kinds)]
        + [pltpu.VMEM((chips,) + shape, kind) for shape, kind in zip(shapes, kinds)]
        + [pltpu.VMEM((2,) + shape, kind) for shape, kind in zip(shapes, kinds)]
        + [
            pltpu.SemaphoreType.DMA((items, chips - 1)),
            pltpu.SemaphoreType.DMA((items, chips - 1)),
            pltpu.SemaphoreType.DMA((items, chips)),
            pltpu.SemaphoreType.DMA((items, chips)),
            pltpu.SemaphoreType.DMA((items, 2)),
        ],
        compiler_params=pltpu.CompilerParams(
            collective_id=1, has_side_effects=True, vmem_limit_bytes=62 * 2**20
        ),
    )(*parts)


def block_shape(rows, columns):
    return (rows, columns) if rows % 16 == 0 else (rows * columns // 128, 128)


def small_pack(gains, shifts, bias, count):
    width = gains.shape[1] // count
    ups = bias.shape[0] // gains.shape[1]
    rows = [
        gains.reshape(2, count, width).swapaxes(0, 1),
        shifts.reshape(6, count, width).swapaxes(0, 1),
        bias.reshape(count, ups, width),
    ]
    blank = jnp.zeros((count, 8 - ups, width), gains.dtype)
    return jnp.concatenate(rows + [blank], axis=1)


def small_split(blocks, ups):
    count, _, width = blocks.shape
    gains = blocks[:, 0:2].swapaxes(0, 1).reshape(2, count * width)
    shifts = blocks[:, 2:8].swapaxes(0, 1).reshape(6, count * width)
    bias = blocks[:, 8 : 8 + ups].reshape(count * ups * width)
    return (gains, shifts, bias)


def layer_norm(rows_in):
    center = rows_in - jnp.mean(rows_in, axis=-1, keepdims=True)
    inverse = lax.rsqrt(jnp.mean(center * center, axis=-1, keepdims=True) + 1e-05)
    return (center * inverse, inverse)


def norm_back(grad_rows, normed, inverse):
    return inverse * (
        grad_rows
        - jnp.mean(grad_rows, axis=-1, keepdims=True)
        - normed * jnp.mean(grad_rows * normed, axis=-1, keepdims=True)
    )


def gelu_parts(hidden_pre):
    cumulative = 0.5 * (1.0 + lax.erf(hidden_pre * (1.0 / math.sqrt(2.0))))
    slope = cumulative + hidden_pre * jnp.exp(-0.5 * hidden_pre * hidden_pre) * (
        1.0 / math.sqrt(2.0 * math.pi)
    )
    return (hidden_pre * cumulative, slope)


def split_heads(packed, model_width):
    length = packed.shape[0]
    head_count = model_width // HEAD_DIM
    queries = packed[:, :model_width].reshape(length, head_count, HEAD_DIM)
    key_rows = packed[:, model_width : 2 * model_width].reshape(length, head_count, HEAD_DIM)
    values = packed[:, 2 * model_width :].reshape(length, head_count, HEAD_DIM)
    return (queries, key_rows, values)


def attend(packed, model_width):
    queries, key_rows, values = split_heads(packed, model_width)
    scores = jnp.einsum("qhd,khd->hqk", queries, key_rows, preferred_element_type=jnp.float32) * (
        1.0 / math.sqrt(HEAD_DIM)
    )
    row_max = jnp.max(scores, axis=-1, keepdims=True)
    shifted = jnp.exp(scores - row_max)
    row_total = jnp.sum(shifted, axis=-1, keepdims=True)
    attn_probs = (shifted / row_total).astype(jnp.bfloat16)
    mixed_out = jnp.einsum("hqk,khd->qhd", attn_probs, values, preferred_element_type=jnp.float32)
    log_total = (row_max + jnp.log(row_total))[:, :, 0]
    return (mixed_out.reshape(packed.shape[0], model_width).astype(jnp.bfloat16), log_total)


def attend_back(packed, log_total, grad_mixed, model_width):
    queries, key_rows, values = split_heads(packed, model_width)
    length = packed.shape[0]
    score_scale = 1.0 / math.sqrt(HEAD_DIM)
    scores = (
        jnp.einsum("qhd,khd->hqk", queries, key_rows, preferred_element_type=jnp.float32)
        * score_scale
    )
    attn_probs = jnp.exp(scores - log_total[:, :, None])
    grad_heads = grad_mixed.reshape(length, -1, HEAD_DIM)
    grad_probs = jnp.einsum("qhd,khd->hqk", grad_heads, values, preferred_element_type=jnp.float32)
    weighted = jnp.sum(grad_probs * attn_probs, axis=-1, keepdims=True)
    grad_scores = (attn_probs * (grad_probs - weighted)).astype(jnp.bfloat16)
    grad_query = (
        jnp.einsum("hqk,khd->qhd", grad_scores, key_rows, preferred_element_type=jnp.float32)
        * score_scale
    )
    grad_key = (
        jnp.einsum("hqk,qhd->khd", grad_scores, queries, preferred_element_type=jnp.float32)
        * score_scale
    )
    grad_value = jnp.einsum(
        "hqk,qhd->khd",
        attn_probs.astype(jnp.bfloat16),
        grad_heads,
        preferred_element_type=jnp.float32,
    )
    joined = jnp.concatenate(
        [
            grad_query.reshape(length, model_width),
            grad_key.reshape(length, model_width),
            grad_value.reshape(length, model_width),
        ],
        axis=1,
    )
    return joined.astype(jnp.bfloat16)


def forward_layer(entry_rows, params):
    gain_values, shift_values, bias, w_qkv, w_out, w_up, w_down = params
    model_width = entry_rows.shape[-1]
    rows_in = entry_rows.astype(F32)
    normed, inverse = layer_norm(rows_in)
    lowered = (normed * gain_values[0] + shift_values[0]).astype(LOW)
    projected = jnp.dot(lowered, w_qkv, preferred_element_type=F32)
    extra = jnp.concatenate([shift_values[1], jnp.zeros_like(shift_values[1]), shift_values[2]])
    packed = (projected + extra).astype(LOW)
    mixed_out, log_total = attend(packed, model_width)
    middle = rows_in + jnp.dot(mixed_out, w_out, preferred_element_type=F32) + shift_values[3]
    normed_two, inverse_two = layer_norm(middle)
    second = (normed_two * gain_values[1] + shift_values[4]).astype(LOW)
    hidden_pre = jnp.dot(second, w_up, preferred_element_type=F32) + bias
    activated, slope = gelu_parts(hidden_pre)
    activated = activated.astype(LOW)
    output = middle + (jnp.dot(activated, w_down, preferred_element_type=F32) + shift_values[5])
    return (output.astype(LOW), (entry_rows, lowered, packed, log_total, mixed_out, middle, second, activated, slope.astype(LOW)))


def backward_layer(saved_items, grad_out, params):
    entry_rows, lowered, packed, log_total, mixed_out, middle, second, activated, slope = saved_items
    gain_values, shift_values, bias, w_qkv, w_out, w_up, w_down = params
    model_width = entry_rows.shape[-1]
    normed, inverse = layer_norm(entry_rows.astype(F32))
    normed_two, inverse_two = layer_norm(middle)
    grad_ff = grad_out.astype(LOW)
    grad_act = jnp.dot(grad_ff, w_down.T, preferred_element_type=F32)
    grad_inner = (grad_act * slope.astype(F32)).astype(LOW)
    grad_second = jnp.dot(grad_inner, w_up.T, preferred_element_type=F32)
    grad_middle = grad_out + norm_back(grad_second * gain_values[1], normed_two, inverse_two)
    grad_branch = grad_middle.astype(LOW)
    grad_mixed = jnp.dot(grad_branch, w_out.T, preferred_element_type=F32).astype(LOW)
    grad_packed = attend_back(packed, log_total, grad_mixed, model_width)
    grad_lowered = jnp.dot(grad_packed, w_qkv.T, preferred_element_type=F32)
    grad_rows = grad_middle + norm_back(grad_lowered * gain_values[0], normed, inverse)
    packed_sums = jnp.sum(grad_packed, axis=0, dtype=F32)
    grad_gains = jnp.stack(
        [jnp.sum(grad_lowered * normed, axis=0), jnp.sum(grad_second * normed_two, axis=0)]
    )
    grad_shifts = jnp.stack(
        [
            jnp.sum(grad_lowered, axis=0),
            packed_sums[:model_width],
            packed_sums[2 * model_width :],
            jnp.sum(grad_branch, axis=0, dtype=F32),
            jnp.sum(grad_second, axis=0),
            jnp.sum(grad_ff, axis=0, dtype=F32),
        ]
    )
    grad_bias = jnp.sum(grad_inner, axis=0, dtype=F32)
    pairs = (lowered, grad_packed, mixed_out, grad_branch, second, grad_inner, activated, grad_ff)
    return (grad_rows.astype(LOW), (grad_gains, grad_shifts, grad_bias), pairs)


def outer_sum(left_rows, right_rows):
    return lax.dot_general(
        left_rows, right_rows, (((0,), (0,)), ((), ())), preferred_element_type=F32
    )


def either(flag, run, keep):
    return lax.cond(flag, lambda kept: run(), lambda kept: kept, keep)


def blank_like(run):
    return jax.tree.map(lambda leaf: jnp.zeros(leaf.shape, leaf.dtype), jax.eval_shape(run))


def on_device(inputs, out_grad, query_counts, gains, shifts, w_qkv, w_out, w_up, b_up, w_down):
    stage = lax.axis_index("pipe")
    count = lax.axis_size("dp")
    cell_count, length, model_width = inputs.shape
    own = model_width // count
    ups = b_up.shape[1] // own
    ff_width = ups * model_width
    low_half = w_down.shape[1] // 2
    shards = [
        small_pack(gains[0], shifts[0], b_up[0], 1)[0],
        w_qkv[0].reshape(block_shape(own, 3 * model_width)),
        w_out[0].reshape(block_shape(own, model_width)),
        w_up[0].reshape(block_shape(own, ff_width)),
        w_down[0, :low_half].reshape(block_shape(low_half, model_width)),
        w_down[0, low_half:].reshape(block_shape(low_half, model_width)),
    ]
    splits = (0, 0, 0, 1, 0, 1)
    small, all_qkv, all_out, all_up, down_a, down_b = gather(shards, splits, count)
    gain_rows, shift_rows, bias = small_split(small.astype(F32), ups)
    down_parts = [part.reshape(count, 1, low_half, model_width) for part in (down_a, down_b)]
    params = (
        gain_rows,
        shift_rows,
        bias,
        all_qkv.reshape(model_width, 3 * model_width),
        all_out.reshape(model_width, model_width),
        all_up.reshape(model_width, ff_width),
        jnp.concatenate(down_parts, axis=1).reshape(ff_width, model_width),
    )
    scales = jnp.sqrt(query_counts.astype(F32) / 500.0)
    last = lax.axis_size("pipe") - 1

    def along(value, steps):
        stages = lax.axis_size("pipe")
        pairs = [(source, source + steps) for source in range(stages) if 0 <= source + steps < stages]
        return lax.ppermute(value, "pipe", pairs)

    stages = lax.axis_size("pipe")
    forward = [None] * cell_count
    arrived = [inputs[cell] for cell in range(cell_count)]
    for turn in range(stages):
        here = []
        for cell in range(cell_count):
            def run(cell=cell):
                return forward_layer(arrived[cell], params)
            if turn == 0:
                forward[cell] = either(stage == 0, run, blank_like(run))
            else:
                forward[cell] = either(stage == turn, run, forward[cell])
            if turn + 1 < stages:
                here.append(along(forward[cell][0], 1))
        arrived = here
    backward = [None] * cell_count
    incoming = [out_grad[cell].astype(F32) * scales[cell] for cell in range(cell_count)]
    for turn in range(stages):
        here = []
        for cell in range(cell_count):
            def run(cell=cell):
                return backward_layer(forward[cell][1], incoming[cell].astype(F32), params)
            if turn == 0:
                backward[cell] = either(stage == last, run, blank_like(run))
            else:
                backward[cell] = either(stage == last - turn, run, backward[cell])
            if turn + 1 < stages:
                here.append(along(backward[cell][0], -1))
        incoming = here
    section_out = jnp.stack([forward[cell][0] for cell in range(cell_count)])
    input_grads = jnp.stack([backward[cell][0] for cell in range(cell_count)])
    sums = functools.reduce(
        lambda left, right: jax.tree.map(jnp.add, left, right),
        [backward[cell][1] for cell in range(cell_count)],
    )
    sides = [
        jnp.concatenate([backward[cell][2][side] for cell in range(cell_count)]) for side in range(8)
    ]
    grads = [outer_sum(sides[at], sides[at + 1]).astype(LOW) for at in (0, 2, 4, 6)]
    down_grads = grads[3].reshape(count, 2, low_half, model_width)
    parts = [
        small_pack(*sums, count),
        grads[0].reshape((count,) + block_shape(own, 3 * model_width)),
        grads[1].reshape((count,) + block_shape(own, model_width)),
        grads[2].reshape((count,) + block_shape(own, ff_width)),
        down_grads[:, 0].reshape((count,) + block_shape(low_half, model_width)),
        down_grads[:, 1].reshape((count,) + block_shape(low_half, model_width)),
    ]
    shares = scatter(parts, splits, count)
    grad_gains, grad_shifts, grad_bias = small_split(shares[0][None], ups)
    return (
        section_out[None],
        input_grads[None],
        grad_gains[None],
        grad_shifts[None],
        shares[1].reshape(1, own, 3 * model_width),
        shares[2].reshape(1, own, model_width),
        shares[3].reshape(1, own, ff_width),
        grad_bias[None],
        jnp.concatenate([part.reshape(low_half, model_width) for part in shares[4:]])[None],
    )


def solution(mesh):
    in_specs = (
        P("dp", None, None),
        P("dp", None, None),
        P("dp"),
        P("pipe", None, "dp"),
        P("pipe", None, "dp"),
        P("pipe", "dp", None),
        P("pipe", "dp", None),
        P("pipe", "dp", None),
        P("pipe", "dp"),
        P("pipe", "dp", None),
    )
    out_specs = (
        P("pipe", "dp", None, None),
        P("pipe", "dp", None, None),
        P("pipe", None, "dp"),
        P("pipe", None, "dp"),
        P("pipe", "dp", None),
        P("pipe", "dp", None),
        P("pipe", "dp", None),
        P("pipe", "dp"),
        P("pipe", "dp", None),
    )
    return jax.shard_map(
        on_device, mesh=mesh, in_specs=in_specs, out_specs=out_specs, check_vma=False
    )
```

```python
import functools
import math

import jax
import jax.numpy as jnp
from jax import lax
from jax.experimental import pallas as pl
from jax.experimental.pallas import tpu as pltpu
from jax.sharding import PartitionSpec as P

HEAD_DIM = 64
MESH = pl.DeviceIdType.MESH
LOW = jnp.bfloat16
F32 = jnp.float32


def ring_chip(position, chips):
    position = lax.rem(position + 2 * chips, chips)
    half = chips // 2
    return jnp.where(position < half, 2 * position, 2 * (chips - 1 - position) + 1)


def ring_place(chips):
    me = lax.axis_index("dp")
    core = lax.rem(me, 2)
    chip = me // 2
    position = jnp.where(lax.rem(chip, 2) == 0, chip // 2, chips - 1 - chip // 2)
    right = ring_chip(position + 1, chips) * 2 + core
    left = ring_chip(position - 1, chips) * 2 + core
    return (me, core, position, right, left, me + 1 - 2 * core)


def greet(devices):
    barrier = pltpu.get_barrier_semaphore()
    for device in devices:
        pl.semaphore_signal(barrier, inc=1, device_id={"dp": device}, device_id_type=MESH)
    pl.semaphore_wait(barrier, len(devices))


def gather_kernel(chips, arrays, items, *refs):
    count = len(items)
    ring_send, ring_recv, pair_send, pair_recv, own_sem = refs[2 * arrays :]
    shards = [refs[array].at[pl.ds(start, rows)] for array, start, rows, _ in items]
    splits = [way for _, _, _, way in items]
    half = chips // 2
    me, core, position, right, left, sibling = ring_place(chips)
    greet((left, right, sibling))

    def out(item, block):
        array, start, rows, _ = items[item]
        return refs[arrays + array].at[block, pl.ds(start, rows)]

    def owner(step, way):
        return ring_chip(position - step if way == 0 else position + step, chips) * 2 + core

    def travels(item, way, step):
        return step < half or (step == half and splits[item] == way)

    def ring_copy(item, way, step):
        block = owner(step - 1, way)
        return pltpu.make_async_remote_copy(
            src_ref=shards[item] if step == 1 else out(item, block),
            dst_ref=out(item, block),
            send_sem=ring_send.at[item, way, step - 1],
            recv_sem=ring_recv.at[item, way, step - 1],
            device_id={"dp": right if way == 0 else left},
            device_id_type=MESH,
        )

    def pair_copy(item, offset, block, source):
        return pltpu.make_async_remote_copy(
            src_ref=source,
            dst_ref=out(item, block),
            send_sem=pair_send.at[item, offset],
            recv_sem=pair_recv.at[item, offset],
            device_id={"dp": sibling},
            device_id_type=MESH,
        )

    sent, paired, kept = ([], [], [])
    for item in range(count):
        for way in (0, 1):
            if travels(item, way, 1):
                sent.append(ring_copy(item, way, 1))
                sent[-1].start()
    for item in range(count):
        paired.append(pair_copy(item, 0, me, shards[item]))
        paired[-1].start()
        kept.append(pltpu.make_async_copy(shards[item], out(item, me), own_sem.at[item]))
        kept[-1].start()
    for step in range(1, half + 1):
        for item in range(count):
            for way in (0, 1):
                if not travels(item, way, step):
                    continue
                ring_copy(item, way, step).wait_recv()
                if travels(item, way, step + 1):
                    sent.append(ring_copy(item, way, step + 1))
                    sent[-1].start()
                block = owner(step, way)
                offset = step if way == 0 else chips - step
                paired.append(pair_copy(item, offset, block, out(item, block)))
                paired[-1].start()
    for copy in sent:
        copy.wait_send()
    for copy in paired:
        copy.wait()
    for copy in kept:
        copy.wait()


def gather(shards, items, count):
    chips = count // 2
    arrays, pieces = (len(shards), len(items))
    return pl.pallas_call(
        functools.partial(gather_kernel, chips, arrays, items),
        out_shape=[jax.ShapeDtypeStruct((count,) + shard.shape, shard.dtype) for shard in shards],
        in_specs=[pl.BlockSpec(memory_space=pl.ANY)] * arrays,
        out_specs=[pl.BlockSpec(memory_space=pl.ANY)] * arrays,
        scratch_shapes=[
            pltpu.SemaphoreType.DMA((pieces, 2, chips // 2)),
            pltpu.SemaphoreType.DMA((pieces, 2, chips // 2)),
            pltpu.SemaphoreType.DMA((pieces, chips)),
            pltpu.SemaphoreType.DMA((pieces, chips)),
            pltpu.SemaphoreType.DMA((pieces,)),
        ],
        compiler_params=pltpu.CompilerParams(collective_id=0, has_side_effects=True),
    )(*shards)


def scatter_kernel(chips, arrays, items, *refs):
    count = len(items)
    parts, outs, refs = (refs[:arrays], refs[arrays : 2 * arrays], refs[2 * arrays :])
    landed, paired, mine = (refs[:count], refs[count : 2 * count], refs[2 * count : 3 * count])
    ring_send, ring_recv, pair_send, pair_recv, mine_sem = refs[3 * count :]
    splits = [way for _, _, _, way in items]
    half = chips // 2
    me, core, position, right, left, sibling = ring_place(chips)
    greet((left, right, sibling))

    def part(item, block):
        array, start, rows, _ = items[item]
        return parts[array].at[block, pl.ds(start, rows)]

    def first(item, way):
        return 1 if splits[item] == way else 2

    def slot(item, way, step):
        return step - 1 if splits[item] == way else half + step - 2

    def offset_of(step, way):
        return half - step + 1 if way == 0 else chips - (half - step + 1)

    def pair_copy(item, offset):
        block = ring_chip(position + offset, chips) * 2 + 1 - core
        return pltpu.make_async_remote_copy(
            src_ref=part(item, block),
            dst_ref=paired[item].at[offset],
            send_sem=pair_send.at[item, offset],
            recv_sem=pair_recv.at[item, offset],
            device_id={"dp": sibling},
            device_id_type=MESH,
        )

    def ring_copy(item, way, step):
        if step == first(item, way):
            source = paired[item].at[offset_of(step, way)]
        else:
            source = landed[item].at[slot(item, way, step - 1)]
        here = slot(item, way, step)
        return pltpu.make_async_remote_copy(
            src_ref=source,
            dst_ref=landed[item].at[here],
            send_sem=ring_send.at[item, here],
            recv_sem=ring_recv.at[item, here],
            device_id={"dp": right if way == 0 else left},
            device_id_type=MESH,
        )

    def load(item, offset, buffer):
        block = ring_chip(position + offset, chips) * 2 + core
        return pltpu.make_async_copy(part(item, block), mine[item].at[buffer], mine_sem.at[item, buffer])

    plan, uses = ([], [0] * count)
    for step in range(1, half + 2):
        for item in range(count):
            for way in (0, 1):
                if step <= half and step >= first(item, way):
                    plan.append((step, item, way, offset_of(step, way), uses[item] % 2))
                    uses[item] += 1
            if step > half:
                plan.append((step, item, None, 0, uses[item] % 2))
                uses[item] += 1
    for step, item, way, offset, buffer in plan:
        pair_copy(item, offset).start()
    load(plan[0][1], plan[0][3], plan[0][4]).start()
    sent = []
    for number, (step, item, way, offset, buffer) in enumerate(plan):
        if number + 1 < len(plan):
            load(plan[number + 1][1], plan[number + 1][3], plan[number + 1][4]).start()
        load(item, offset, buffer).wait()
        pair_copy(item, offset).wait_recv()
        array, start, rows, _ = items[item]
        kind = parts[array].dtype
        chunk = 16 if rows % 16 == 0 else rows
        from_pair, from_mine, from_ring = (paired[item], mine[item], landed[item])
        if way is None:
            ring_copy(item, 0, half).wait_recv()
            ring_copy(item, 1, half).wait_recv()
            slot_a, slot_b = (slot(item, 0, half), slot(item, 1, half))

            @pl.loop(0, rows // chunk)
            def _(index):
                here = pl.ds(pl.multiple_of(index * chunk, chunk), chunk)
                outs[array][pl.ds(pl.multiple_of(start + index * chunk, chunk), chunk), :] = (
                    from_ring[slot_a, here, :].astype(F32) + from_ring[slot_b, here, :].astype(F32)
                ) + (from_mine[buffer, here, :].astype(F32) + from_pair[offset, here, :].astype(F32))

            continue
        if step == first(item, way):

            @pl.loop(0, rows // chunk)
            def _(index):
                here = pl.ds(pl.multiple_of(index * chunk, chunk), chunk)
                from_pair[offset, here, :] = (
                    from_mine[buffer, here, :].astype(F32) + from_pair[offset, here, :].astype(F32)
                ).astype(kind)

        else:
            ring_copy(item, way, step - 1).wait_recv()
            arrived = slot(item, way, step - 1)

            @pl.loop(0, rows // chunk)
            def _(index):
                here = pl.ds(pl.multiple_of(index * chunk, chunk), chunk)
                from_ring[arrived, here, :] = (
                    from_ring[arrived, here, :].astype(F32)
                    + (from_mine[buffer, here, :].astype(F32) + from_pair[offset, here, :].astype(F32))
                ).astype(kind)

        sent.append(ring_copy(item, way, step))
        sent[-1].start()
    for copy in sent:
        copy.wait_send()
    for step, item, way, offset, buffer in plan:
        pair_copy(item, offset).wait_send()


def scatter(parts, items, count):
    chips = count // 2
    arrays, pieces = (len(parts), len(items))
    shapes = [(rows,) + parts[array].shape[2:] for array, _, rows, _ in items]
    kinds = [parts[array].dtype for array, _, _, _ in items]
    return pl.pallas_call(
        functools.partial(scatter_kernel, chips, arrays, items),
        out_shape=[jax.ShapeDtypeStruct(part.shape[1:], F32) for part in parts],
        in_specs=[pl.BlockSpec(memory_space=pl.ANY)] * arrays,
        out_specs=[pl.BlockSpec(memory_space=pltpu.VMEM)] * arrays,
        scratch_shapes=[pltpu.VMEM((chips - 1,) + shape, kind) for shape, kind in zip(shapes, kinds)]
        + [pltpu.VMEM((chips,) + shape, kind) for shape, kind in zip(shapes, kinds)]
        + [pltpu.VMEM((2,) + shape, kind) for shape, kind in zip(shapes, kinds)]
        + [
            pltpu.SemaphoreType.DMA((pieces, chips - 1)),
            pltpu.SemaphoreType.DMA((pieces, chips - 1)),
            pltpu.SemaphoreType.DMA((pieces, chips)),
            pltpu.SemaphoreType.DMA((pieces, chips)),
            pltpu.SemaphoreType.DMA((pieces, 2)),
        ],
        compiler_params=pltpu.CompilerParams(
            collective_id=1, has_side_effects=True, vmem_limit_bytes=62 * 2**20
        ),
    )(*parts)


def block_shape(rows, columns):
    return (rows, columns) if rows % 16 == 0 else (rows * columns // 128, 128)


def small_pack(gains, shifts, bias, count):
    width = gains.shape[1] // count
    ups = bias.shape[0] // gains.shape[1]
    rows = [
        gains.reshape(2, count, width).swapaxes(0, 1),
        shifts.reshape(6, count, width).swapaxes(0, 1),
        bias.reshape(count, ups, width),
    ]
    blank = jnp.zeros((count, 8 - ups, width), gains.dtype)
    return jnp.concatenate(rows + [blank], axis=1)


def small_split(blocks, ups):
    count, _, width = blocks.shape
    gains = blocks[:, 0:2].swapaxes(0, 1).reshape(2, count * width)
    shifts = blocks[:, 2:8].swapaxes(0, 1).reshape(6, count * width)
    bias = blocks[:, 8 : 8 + ups].reshape(count * ups * width)
    return (gains, shifts, bias)


def row_norm(rows_in):
    center = rows_in - jnp.mean(rows_in, axis=-1, keepdims=True)
    inverse = lax.rsqrt(jnp.mean(center * center, axis=-1, keepdims=True) + 1e-05)
    return (center * inverse, inverse)


def norm_back(grad_rows, normed, inverse):
    return inverse * (
        grad_rows
        - jnp.mean(grad_rows, axis=-1, keepdims=True)
        - normed * jnp.mean(grad_rows * normed, axis=-1, keepdims=True)
    )


def gelu_parts(hidden):
    size = jnp.abs(hidden)
    turn = 1.0 / (1.0 + (0.3275911 / math.sqrt(2.0)) * size)
    bell = jnp.exp(-0.5 * hidden * hidden)
    series = turn * (
        0.5 * 0.254829592
        + turn
        * (
            0.5 * -0.284496736
            + turn * (0.5 * 1.421413741 + turn * (0.5 * -1.453152027 + turn * (0.5 * 1.061405429)))
        )
    )
    tail = series * bell
    cumulative = jnp.where(hidden < 0.0, tail, 1.0 - tail)
    slope = cumulative + hidden * bell * (1.0 / math.sqrt(2.0 * math.pi))
    return (hidden * cumulative, slope)


def dot(left, right):
    return lax.dot_general(left, right, (((1,), (0,)), ((), ())), preferred_element_type=F32)


def dot_right(left, right):
    return lax.dot_general(left, right, (((1,), (1,)), ((), ())), preferred_element_type=F32)


def dot_left(left, right):
    return lax.dot_general(left, right, (((0,), (0,)), ((), ())), preferred_element_type=F32)


class Stream:
    def __init__(self, blocks, buffers, sems):
        self.blocks, self.buffers, self.sems = (blocks, buffers, sems)
        self.depth = buffers.shape[0]
        self.started = 0
        for _ in range(min(self.depth, len(blocks))):
            self.start()

    def copy(self, number):
        slot = number % self.depth
        return pltpu.make_async_copy(self.blocks[number], self.buffers.at[slot], self.sems.at[slot])

    def start(self):
        self.copy(self.started).start()
        self.started += 1

    def take(self, number):
        self.copy(number).wait()
        return self.buffers.at[number % self.depth]

    def release(self):
        if self.started < len(self.blocks):
            self.start()


def weight_blocks(w_qkv, w_out, w_up, w_down):
    width = w_out.shape[0]
    def cut(ref, axis, number):
        window = pl.ds(number * width, width)
        return ref.at[:, window] if axis else ref.at[window, :]
    heads = [cut(w_qkv, 1, number) for number in range(3)]
    ups = [cut(w_up, 1, number) for number in range(w_up.shape[1] // width)]
    downs = [cut(w_down, 0, number) for number in range(w_down.shape[0] // width)]
    return (heads, w_out, ups, downs)


def attend(packed, mixed, width):
    length = packed.shape[0]
    side = lax.broadcasted_iota(jnp.int32, (length, 128), 1) < HEAD_DIM

    @pl.loop(0, width // 128)
    def _(pair):
        start = pl.multiple_of(pair * 128, 128)
        queries = packed[:, pl.ds(start, 128)] * jnp.asarray(1.0 / math.sqrt(HEAD_DIM), LOW)
        keys = packed[:, pl.ds(start + width, 128)]
        values = packed[:, pl.ds(start + 2 * width, 128)]
        blank = jnp.zeros_like(queries)
        parts = []
        for head in (0, 1):
            mine = jnp.where(side, queries, blank) if head == 0 else jnp.where(side, blank, queries)
            scores = dot_right(mine, keys)
            shifted = jnp.exp(scores - jnp.max(scores, axis=-1, keepdims=True))
            total = jnp.sum(shifted, axis=-1, keepdims=True)
            parts.append(dot(shifted.astype(LOW), values) * (1.0 / total))
        mixed[:, pl.ds(start, 128)] = jnp.where(side, parts[0], parts[1]).astype(LOW)


def attend_back(packed, grad_mixed, grad_packed, width):
    length = packed.shape[0]
    side = lax.broadcasted_iota(jnp.int32, (length, 128), 1) < HEAD_DIM
    scale = 1.0 / math.sqrt(HEAD_DIM)

    @pl.loop(0, width // 128)
    def _(pair):
        start = pl.multiple_of(pair * 128, 128)
        queries = packed[:, pl.ds(start, 128)]
        keys = packed[:, pl.ds(start + width, 128)]
        values = packed[:, pl.ds(start + 2 * width, 128)]
        grads = grad_mixed[:, pl.ds(start, 128)]
        blank = jnp.zeros_like(queries)
        scaled = keys * jnp.asarray(scale, LOW)
        parts = []
        for head in (0, 1):
            def mine(array):
                return jnp.where(side, array, blank) if head == 0 else jnp.where(side, blank, array)
            scores = dot_right(mine(scaled), queries)
            shifted = jnp.exp(scores - jnp.max(scores, axis=0, keepdims=True))
            probs = shifted * (1.0 / jnp.sum(shifted, axis=0, keepdims=True))
            grad_probs = dot_right(mine(values), grads)
            product = grad_probs * probs
            weighted = jnp.sum(product, axis=0, keepdims=True)
            grad_scores = (product - probs * weighted).astype(LOW)
            parts.append((dot_left(grad_scores, scaled), dot(grad_scores, queries) * scale, dot(probs.astype(LOW), grads)))
        for number in range(3):
            grad_packed[:, pl.ds(start + number * width, 128)] = jnp.where(
                side, parts[0][number], parts[1][number]
            ).astype(LOW)


def forward_kernel(cell, held, active, entry, gains, shifts, bias, w_qkv, w_out, w_up, w_down, *refs):
    sent_h = refs[held]
    out_h, lowered_h, packed_h, mixed_h, middle_h, second_h, active_h, slope_h = [
        ref.at[cell] for ref in refs[held + 1 : held + 9]
    ]
    (buffers, buffer_sems, save_sems, out_v, lowered_v, packed_v, mixed_v, middle_v) = refs[held + 9 : held + 17]
    (second_v, active_v, slope_v, hidden_v, total_v) = refs[held + 17 :]
    width = entry.shape[1]
    ups = w_up.shape[1] // width

    @pl.when(active[0] != 0)
    def _():
        heads, outer, up, down = weight_blocks(w_qkv, w_out, w_up, w_down)
        order = heads + [outer]
        place_up, place_down = ({}, {})
        for number in range(ups + 1):
            if number < ups:
                place_up[number] = len(order)
                order.append(up[number])
            if number > 0:
                place_down[number - 1] = len(order)
                order.append(down[number - 1])
        stream = Stream(order, buffers, buffer_sems)
        saves = []

        def save(source, target):
            saves.append(pltpu.make_async_copy(source, target, save_sems.at[len(saves)]))
            saves[-1].start()

        rows_in = entry[...].astype(F32)
        normed, _ = row_norm(rows_in)
        lowered_v[...] = (normed * gains[0:1, :] + shifts[0:1, :]).astype(LOW)
        save(lowered_v, lowered_h)
        for number in range(3):
            block = stream.take(number)
            window = pl.ds(number * width, width)
            part = dot(lowered_v[...], block[...])
            if number != 1:
                part = part + shifts[1 + number // 2 : 2 + number // 2, :]
            packed_v[:, window] = part.astype(LOW)
            stream.release()
        save(packed_v, packed_h)
        attend(packed_v, mixed_v, width)
        save(mixed_v, mixed_h)
        block = stream.take(3)
        middle = entry[...].astype(F32) + dot(mixed_v[...], block[...]) + shifts[3:4, :]
        middle_v[...] = middle
        stream.release()
        save(middle_v, middle_h)
        normed, _ = row_norm(middle_v[...])
        second_v[...] = (normed * gains[1:2, :] + shifts[4:5, :]).astype(LOW)
        save(second_v, second_h)
        for number in range(ups + 1):
            if number < ups:
                up_block = stream.take(place_up[number])
            if number > 0:
                down_block = stream.take(place_down[number - 1])
            if number < ups:
                hidden_v[number % 2] = dot(second_v[...], up_block[...]) + bias[0:1, pl.ds(number * width, width)]
            if number > 0:
                window = pl.ds((number - 1) * width, width)
                activated, slope = gelu_parts(hidden_v[(number - 1) % 2])
                active_v[:, window] = activated.astype(LOW)
                slope_v[:, window] = slope.astype(LOW)
                part = dot(active_v[:, window], down_block[...])
                if number == 1:
                    total_v[...] = part
                elif number < ups:
                    total_v[...] += part
                else:
                    out_v[...] = (middle_v[...] + (total_v[...] + part + shifts[5:6, :])).astype(LOW)
                save(active_v.at[:, window], active_h.at[:, window])
                save(slope_v.at[:, window], slope_h.at[:, window])
            if number < ups:
                stream.release()
            if number > 0:
                stream.release()
        save(out_v, sent_h)
        save(out_v, out_h)
        for copy in saves:
            copy.wait()


def forward_tick(active, entry, small, weights, kept, cell, cell_count):
    length, width = entry.shape
    deep = weights[2].shape[1]
    ups = deep // width
    shapes = [
        ((length, width), LOW),
        ((length, width), LOW),
        ((length, 3 * width), LOW),
        ((length, width), LOW),
        ((length, width), F32),
        ((length, width), LOW),
        ((length, deep), LOW),
        ((length, deep), LOW),
    ]
    outs = [jax.ShapeDtypeStruct(*shapes[0])] + [
        jax.ShapeDtypeStruct((cell_count,) + shape, kind) for shape, kind in shapes
    ]
    vmem, hbm = (pl.BlockSpec(memory_space=pltpu.VMEM), pl.BlockSpec(memory_space=pl.ANY))
    flops = 2 * length * width * (4 * width + 2 * deep) + 16 * length * length * width
    kept = () if kept is None else tuple(kept)
    held = len(kept)
    sent, *kept = pl.pallas_call(
        functools.partial(forward_kernel, cell, held),
        out_shape=outs,
        in_specs=[pl.BlockSpec(memory_space=pltpu.SMEM)] + [vmem] * 4 + [hbm] * (4 + held),
        out_specs=[hbm] * 9,
        input_output_aliases={9 + number: 1 + number for number in range(held)},
        scratch_shapes=[
            pltpu.VMEM((4, width, width), LOW),
            pltpu.SemaphoreType.DMA((4,)),
            pltpu.SemaphoreType.DMA((7 + 2 * ups,)),
        ]
        + [pltpu.VMEM(*shape) for shape in shapes]
        + [pltpu.VMEM((2, length, width), F32), pltpu.VMEM((length, width), F32)],
        compiler_params=pltpu.CompilerParams(vmem_limit_bytes=60 * 2**20),
        cost_estimate=pl.CostEstimate(
            flops=flops, bytes_accessed=2 * width * (4 * width + 2 * deep), transcendentals=0
        ),
    )(active, entry, *small, *weights, *kept)
    return (sent, kept)


def backward_kernel(cell, held, active, scale, grad, entry, gains, shifts, *refs):
    packed, middle, slope = [ref.at[cell] for ref in refs[:3]]
    w_qkv, w_out, w_up, w_down = refs[3:7]
    refs = refs[7 + held :]
    sent_h = refs[0]
    rows_h, packed_h, branch_h, inner_h, low_h, sums_h = [ref.at[cell] for ref in refs[1:7]]
    (buffers, buffer_sems, load_sems, save_sems, rows_v, grad_packed_v, branch_v, inner_v, low_v, sums_v) = refs[7:17]
    (packed_v, middle_v, slope_v, mixed_v, grad_act_v, total_v, grad_middle_v) = refs[17:]
    length, width = entry.shape
    ups = w_up.shape[1] // width

    @pl.when(active[0] != 0)
    def _():
        heads, outer, up, down = weight_blocks(w_qkv, w_out, w_up, w_down)
        loads = [
            pltpu.make_async_copy(slope, slope_v, load_sems.at[0]),
            pltpu.make_async_copy(middle, middle_v, load_sems.at[1]),
            pltpu.make_async_copy(packed, packed_v, load_sems.at[2]),
        ]
        loads[0].start()
        order, place_up, place_down = ([], {}, {})
        for number in range(ups + 1):
            if number < ups:
                place_down[number] = len(order)
                order.append(down[number])
            if number > 0:
                place_up[number - 1] = len(order)
                order.append(up[number - 1])
        place_out = len(order)
        order = order + [outer] + heads
        stream = Stream(order, buffers, buffer_sems)
        loads[1].start()
        loads[2].start()
        saves = []

        def save(source, target):
            saves.append(pltpu.make_async_copy(source, target, save_sems.at[len(saves)]))
            saves[-1].start()

        def column_sum(array):
            return jnp.sum(array.astype(F32), axis=0, keepdims=True)

        low_v[...] = (grad[...].astype(F32) * scale[0]).astype(LOW)
        save(low_v, low_h)
        sums_v[7:8, :] = column_sum(low_v[...])
        loads[0].wait()
        for number in range(ups + 1):
            if number < ups:
                down_block = stream.take(place_down[number])
            if number > 0:
                up_block = stream.take(place_up[number - 1])
            if number < ups:
                grad_act_v[number % 2] = dot_right(low_v[...], down_block[...])
            if number > 0:
                window = pl.ds((number - 1) * width, width)
                inner = (grad_act_v[(number - 1) % 2] * slope_v[:, window].astype(F32)).astype(LOW)
                inner_v[:, window] = inner
                sums_v[7 + number : 8 + number, :] = column_sum(inner)
                part = dot_right(inner, up_block[...])
                if number == 1:
                    total_v[...] = part
                else:
                    total_v[...] += part
                save(inner_v.at[:, window], inner_h.at[:, window])
            if number < ups:
                stream.release()
            if number > 0:
                stream.release()
        loads[1].wait()
        normed, inverse = row_norm(middle_v[...])
        grad_second = total_v[...]
        sums_v[1:2, :] = column_sum(grad_second * normed)
        sums_v[6:7, :] = column_sum(grad_second)
        grad_middle = grad[...].astype(F32) * scale[0] + norm_back(grad_second * gains[1:2, :], normed, inverse)
        grad_middle_v[...] = grad_middle
        branch_v[...] = grad_middle.astype(LOW)
        sums_v[5:6, :] = column_sum(branch_v[...])
        save(branch_v, branch_h)
        block = stream.take(place_out)
        mixed_v[...] = dot_right(branch_v[...], block[...]).astype(LOW)
        stream.release()
        loads[2].wait()
        attend_back(packed_v, mixed_v, grad_packed_v, width)
        save(grad_packed_v, packed_h)
        sums_v[3:4, :] = column_sum(grad_packed_v[:, pl.ds(0, width)])
        sums_v[4:5, :] = column_sum(grad_packed_v[:, pl.ds(2 * width, width)])
        for number in range(3):
            block = stream.take(place_out + 1 + number)
            part = dot_right(grad_packed_v[:, pl.ds(number * width, width)], block[...])
            if number == 0:
                total_v[...] = part
            else:
                total_v[...] += part
            stream.release()
        normed, inverse = row_norm(entry[...].astype(F32))
        grad_lowered = total_v[...]
        sums_v[0:1, :] = column_sum(grad_lowered * normed)
        sums_v[2:3, :] = column_sum(grad_lowered)
        rows_v[...] = (grad_middle_v[...] + norm_back(grad_lowered * gains[0:1, :], normed, inverse)).astype(LOW)
        save(sums_v, sums_h)
        save(rows_v, sent_h)
        save(rows_v, rows_h)
        for copy in saves:
            copy.wait()


def backward_tick(active, incoming, entry, small, saved, weights, kept, cell, cell_count):
    length, width = entry.shape
    deep = weights[2].shape[1]
    ups = deep // width
    shapes = [
        ((length, width), LOW),
        ((length, 3 * width), LOW),
        ((length, width), LOW),
        ((length, deep), LOW),
        ((length, width), LOW),
        ((16, width), F32),
    ]
    outs = [jax.ShapeDtypeStruct(*shapes[0])] + [
        jax.ShapeDtypeStruct((cell_count,) + shape, kind) for shape, kind in shapes
    ]
    vmem, hbm = (pl.BlockSpec(memory_space=pltpu.VMEM), pl.BlockSpec(memory_space=pl.ANY))
    smem = pl.BlockSpec(memory_space=pltpu.SMEM)
    flops = 2 * length * width * (4 * width + 2 * deep) + 40 * length * length * width
    kept = () if kept is None else tuple(kept)
    held = len(kept)
    grad, scale = incoming
    sent, *kept = pl.pallas_call(
        functools.partial(backward_kernel, cell, held),
        out_shape=outs,
        in_specs=[smem] * 2 + [vmem] * 4 + [hbm] * (7 + held),
        out_specs=[hbm] * 7,
        input_output_aliases={13 + number: 1 + number for number in range(held)},
        scratch_shapes=[
            pltpu.VMEM((4, width, width), LOW),
            pltpu.SemaphoreType.DMA((4,)),
            pltpu.SemaphoreType.DMA((3,)),
            pltpu.SemaphoreType.DMA((6 + ups,)),
        ]
        + [pltpu.VMEM(*shape) for shape in shapes]
        + [
            pltpu.VMEM((length, 3 * width), LOW),
            pltpu.VMEM((length, width), F32),
            pltpu.VMEM((length, deep), LOW),
            pltpu.VMEM((length, width), LOW),
            pltpu.VMEM((2, length, width), F32),
            pltpu.VMEM((length, width), F32),
            pltpu.VMEM((length, width), F32),
        ],
        compiler_params=pltpu.CompilerParams(vmem_limit_bytes=60 * 2**20),
        cost_estimate=pl.CostEstimate(
            flops=flops, bytes_accessed=2 * width * (4 * width + 2 * deep), transcendentals=0
        ),
    )(active, scale, grad, entry, *small[:2], *saved, *weights, *kept)
    return (sent, kept)


def on_device(inputs, out_grad, query_counts, gains, shifts, w_qkv, w_out, w_up, b_up, w_down):
    stage = lax.axis_index("pipe")
    stages = lax.axis_size("pipe")
    count = lax.axis_size("dp")
    cell_count, length, width = inputs.shape
    own = width // count
    ups = b_up.shape[1] // own
    deep = ups * width
    deep_own = w_down.shape[1]
    shapes = [
        block_shape(own, 3 * width),
        block_shape(own, width),
        block_shape(own, deep),
        block_shape(deep_own, width),
    ]
    cut = (shapes[3][0] // 2 + 15) // 16 * 16
    items = (
        (0, 0, 16, 0),
        (1, 0, shapes[0][0], 0),
        (2, 0, shapes[1][0], 0),
        (3, 0, shapes[2][0], 1),
        (4, 0, cut, 0),
        (4, cut, shapes[3][0] - cut, 1),
    )
    shards = [small_pack(gains[0], shifts[0], b_up[0], 1)[0]] + [
        array[0].reshape(shape) for array, shape in zip((w_qkv, w_out, w_up, w_down), shapes)
    ]
    packs = gather(shards, items, count)
    gain_rows, shift_rows, bias = small_split(packs[0].astype(F32), ups)
    small = (gain_rows, shift_rows, bias[None])
    weights = (
        packs[1].reshape(width, 3 * width),
        packs[2].reshape(width, width),
        packs[3].reshape(width, deep),
        packs[4].reshape(deep, width),
    )
    scales = jnp.sqrt(query_counts.astype(F32) / 500.0)

    def along(value, steps):
        pairs = [(source, source + steps) for source in range(stages) if 0 <= source + steps < stages]
        return lax.ppermute(value, "pipe", pairs)

    entries, kept = ([[inputs[cell] for cell in range(cell_count)]], None)
    for turn in range(stages):
        active = (stage == turn).astype(jnp.int32)[None]
        arrived = []
        for cell in range(cell_count):
            sent, kept = forward_tick(active, entries[turn][cell], small, weights, kept, cell, cell_count)
            if turn + 1 < stages:
                arrived.append(along(sent, 1))
        entries.append(arrived)
    section_out, lowered, packed, mixed, middle, second, activated, slope = kept
    incoming = [(out_grad[cell], scales[cell][None]) for cell in range(cell_count)]
    back = None
    for turn in range(stages - 1, -1, -1):
        active = (stage == turn).astype(jnp.int32)[None]
        arrived = []
        for cell in range(cell_count):
            sent, back = backward_tick(
                active, incoming[cell], entries[turn][cell], small, (packed, middle, slope), weights, back, cell, cell_count
            )
            if turn > 0:
                arrived.append((along(sent, -1), jnp.ones((1,), F32)))
        incoming = arrived
    input_grads, grad_packed, grad_branch, grad_inner, grad_ff, sums = back
    sums = jnp.sum(sums, axis=0)

    def product(left, right):
        return dot_left(left.reshape(cell_count * length, -1), right.reshape(cell_count * length, -1)).astype(LOW)

    parts = [
        small_pack(sums[0:2], sums[2:8], sums[8 : 8 + ups].reshape(deep), count),
        product(lowered, grad_packed).reshape((count,) + shapes[0]),
        product(mixed, grad_branch).reshape((count,) + shapes[1]),
        product(second, grad_inner).reshape((count,) + shapes[2]),
        product(activated, grad_ff).reshape((count,) + shapes[3]),
    ]
    shares = scatter(parts, items, count)
    grad_gains, grad_shifts, grad_bias = small_split(shares[0][None], ups)
    return (
        section_out[None],
        input_grads[None],
        grad_gains[None],
        grad_shifts[None],
        shares[1].reshape(1, own, 3 * width),
        shares[2].reshape(1, own, width),
        shares[3].reshape(1, own, deep),
        grad_bias[None],
        shares[4].reshape(1, deep_own, width),
    )


def solution(mesh):
    in_specs = (
        P("dp", None, None),
        P("dp", None, None),
        P("dp"),
        P("pipe", None, "dp"),
        P("pipe", None, "dp"),
        P("pipe", "dp", None),
        P("pipe", "dp", None),
        P("pipe", "dp", None),
        P("pipe", "dp"),
        P("pipe", "dp", None),
    )
    out_specs = (
        P("pipe", "dp", None, None),
        P("pipe", "dp", None, None),
        P("pipe", None, "dp"),
        P("pipe", None, "dp"),
        P("pipe", "dp", None),
        P("pipe", "dp", None),
        P("pipe", "dp", None),
        P("pipe", "dp"),
        P("pipe", "dp", None),
    )
    return jax.shard_map(
        on_device, mesh=mesh, in_specs=in_specs, out_specs=out_specs, check_vma=False
    )
```

```python
import functools
import math

import jax
import jax.numpy as jnp
from jax import lax
from jax.experimental import pallas as pl
from jax.experimental.pallas import tpu as pltpu
from jax.sharding import PartitionSpec as P

HEAD_DIM = 64
MESH = pl.DeviceIdType.MESH
LOW = jnp.bfloat16
F32 = jnp.float32


def ring_chip(position, chips):
    position = lax.rem(position + 2 * chips, chips)
    half = chips // 2
    return jnp.where(position < half, 2 * position, 2 * (chips - 1 - position) + 1)


def ring_place(chips):
    me = lax.axis_index("dp")
    core = lax.rem(me, 2)
    chip = me // 2
    position = jnp.where(lax.rem(chip, 2) == 0, chip // 2, chips - 1 - chip // 2)
    right = ring_chip(position + 1, chips) * 2 + core
    left = ring_chip(position - 1, chips) * 2 + core
    return (me, core, position, right, left, me + 1 - 2 * core)


def greet(devices):
    barrier = pltpu.get_barrier_semaphore()
    for device in devices:
        pl.semaphore_signal(barrier, inc=1, device_id={"dp": device}, device_id_type=MESH)
    pl.semaphore_wait(barrier, len(devices))


def gather_kernel(chips, arrays, items, *refs):
    count = len(items)
    ring_send, ring_recv, pair_send, pair_recv, own_sem = refs[2 * arrays :]
    shards = [refs[array].at[pl.ds(start, rows)] for array, start, rows, _ in items]
    splits = [way for _, _, _, way in items]
    half = chips // 2
    me, core, position, right, left, sibling = ring_place(chips)
    greet((left, right, sibling))

    def out(item, block):
        array, start, rows, _ = items[item]
        return refs[arrays + array].at[block, pl.ds(start, rows)]

    def owner(step, way):
        return ring_chip(position - step if way == 0 else position + step, chips) * 2 + core

    def travels(item, way, step):
        return step < half or (step == half and splits[item] == way)

    def ring_copy(item, way, step):
        block = owner(step - 1, way)
        return pltpu.make_async_remote_copy(
            src_ref=shards[item] if step == 1 else out(item, block),
            dst_ref=out(item, block),
            send_sem=ring_send.at[item, way, step - 1],
            recv_sem=ring_recv.at[item, way, step - 1],
            device_id={"dp": right if way == 0 else left},
            device_id_type=MESH,
        )

    def pair_copy(item, offset, block, source):
        return pltpu.make_async_remote_copy(
            src_ref=source,
            dst_ref=out(item, block),
            send_sem=pair_send.at[item, offset],
            recv_sem=pair_recv.at[item, offset],
            device_id={"dp": sibling},
            device_id_type=MESH,
        )

    sent, paired, kept = ([], [], [])
    for item in range(count):
        for way in (0, 1):
            if travels(item, way, 1):
                sent.append(ring_copy(item, way, 1))
                sent[-1].start()
    for item in range(count):
        paired.append(pair_copy(item, 0, me, shards[item]))
        paired[-1].start()
        kept.append(pltpu.make_async_copy(shards[item], out(item, me), own_sem.at[item]))
        kept[-1].start()
    for step in range(1, half + 1):
        for item in range(count):
            for way in (0, 1):
                if not travels(item, way, step):
                    continue
                ring_copy(item, way, step).wait_recv()
                if travels(item, way, step + 1):
                    sent.append(ring_copy(item, way, step + 1))
                    sent[-1].start()
                block = owner(step, way)
                offset = step if way == 0 else chips - step
                paired.append(pair_copy(item, offset, block, out(item, block)))
                paired[-1].start()
    for copy in sent:
        copy.wait_send()
    for copy in paired:
        copy.wait()
    for copy in kept:
        copy.wait()


def gather(shards, items, count):
    chips = count // 2
    arrays, pieces = (len(shards), len(items))
    return pl.pallas_call(
        functools.partial(gather_kernel, chips, arrays, items),
        out_shape=[jax.ShapeDtypeStruct((count,) + shard.shape, shard.dtype) for shard in shards],
        in_specs=[pl.BlockSpec(memory_space=pl.ANY)] * arrays,
        out_specs=[pl.BlockSpec(memory_space=pl.ANY)] * arrays,
        scratch_shapes=[
            pltpu.SemaphoreType.DMA((pieces, 2, chips // 2)),
            pltpu.SemaphoreType.DMA((pieces, 2, chips // 2)),
            pltpu.SemaphoreType.DMA((pieces, chips)),
            pltpu.SemaphoreType.DMA((pieces, chips)),
            pltpu.SemaphoreType.DMA((pieces,)),
        ],
        compiler_params=pltpu.CompilerParams(collective_id=0, has_side_effects=True),
    )(*shards)


def scatter_kernel(chips, arrays, items, *refs):
    count = len(items)
    parts, outs, refs = (refs[:arrays], refs[arrays : 2 * arrays], refs[2 * arrays :])
    landed, paired, mine = (refs[:count], refs[count : 2 * count], refs[2 * count : 3 * count])
    ring_send, ring_recv, pair_send, pair_recv, mine_sem = refs[3 * count :]
    splits = [way for _, _, _, way in items]
    half = chips // 2
    me, core, position, right, left, sibling = ring_place(chips)
    greet((left, right, sibling))

    def part(item, block):
        array, start, rows, _ = items[item]
        return parts[array].at[block, pl.ds(start, rows)]

    def first(item, way):
        return 1 if splits[item] == way else 2

    def slot(item, way, step):
        return step - 1 if splits[item] == way else half + step - 2

    def offset_of(step, way):
        return half - step + 1 if way == 0 else chips - (half - step + 1)

    def pair_copy(item, offset):
        block = ring_chip(position + offset, chips) * 2 + 1 - core
        return pltpu.make_async_remote_copy(
            src_ref=part(item, block),
            dst_ref=paired[item].at[offset],
            send_sem=pair_send.at[item, offset],
            recv_sem=pair_recv.at[item, offset],
            device_id={"dp": sibling},
            device_id_type=MESH,
        )

    def ring_copy(item, way, step):
        if step == first(item, way):
            source = paired[item].at[offset_of(step, way)]
        else:
            source = landed[item].at[slot(item, way, step - 1)]
        here = slot(item, way, step)
        return pltpu.make_async_remote_copy(
            src_ref=source,
            dst_ref=landed[item].at[here],
            send_sem=ring_send.at[item, here],
            recv_sem=ring_recv.at[item, here],
            device_id={"dp": right if way == 0 else left},
            device_id_type=MESH,
        )

    def load(item, offset, buffer):
        block = ring_chip(position + offset, chips) * 2 + core
        return pltpu.make_async_copy(part(item, block), mine[item].at[buffer], mine_sem.at[item, buffer])

    plan, uses = ([], [0] * count)
    for step in range(1, half + 2):
        for item in range(count):
            for way in (0, 1):
                if step <= half and step >= first(item, way):
                    plan.append((step, item, way, offset_of(step, way), uses[item] % 2))
                    uses[item] += 1
            if step > half:
                plan.append((step, item, None, 0, uses[item] % 2))
                uses[item] += 1
    for step, item, way, offset, buffer in plan:
        pair_copy(item, offset).start()
    load(plan[0][1], plan[0][3], plan[0][4]).start()
    sent = []
    for number, (step, item, way, offset, buffer) in enumerate(plan):
        if number + 1 < len(plan):
            load(plan[number + 1][1], plan[number + 1][3], plan[number + 1][4]).start()
        load(item, offset, buffer).wait()
        pair_copy(item, offset).wait_recv()
        array, start, rows, _ = items[item]
        kind = parts[array].dtype
        chunk = 16 if rows % 16 == 0 else rows
        from_pair, from_mine, from_ring = (paired[item], mine[item], landed[item])
        if way is None:
            ring_copy(item, 0, half).wait_recv()
            ring_copy(item, 1, half).wait_recv()
            slot_a, slot_b = (slot(item, 0, half), slot(item, 1, half))

            @pl.loop(0, rows // chunk)
            def _(index):
                here = pl.ds(pl.multiple_of(index * chunk, chunk), chunk)
                outs[array][pl.ds(pl.multiple_of(start + index * chunk, chunk), chunk), :] = (
                    from_ring[slot_a, here, :].astype(F32) + from_ring[slot_b, here, :].astype(F32)
                ) + (from_mine[buffer, here, :].astype(F32) + from_pair[offset, here, :].astype(F32))

            continue
        if step == first(item, way):

            @pl.loop(0, rows // chunk)
            def _(index):
                here = pl.ds(pl.multiple_of(index * chunk, chunk), chunk)
                from_pair[offset, here, :] = (
                    from_mine[buffer, here, :].astype(F32) + from_pair[offset, here, :].astype(F32)
                ).astype(kind)

        else:
            ring_copy(item, way, step - 1).wait_recv()
            arrived = slot(item, way, step - 1)

            @pl.loop(0, rows // chunk)
            def _(index):
                here = pl.ds(pl.multiple_of(index * chunk, chunk), chunk)
                from_ring[arrived, here, :] = (
                    from_ring[arrived, here, :].astype(F32)
                    + (from_mine[buffer, here, :].astype(F32) + from_pair[offset, here, :].astype(F32))
                ).astype(kind)

        sent.append(ring_copy(item, way, step))
        sent[-1].start()
    for copy in sent:
        copy.wait_send()
    for step, item, way, offset, buffer in plan:
        pair_copy(item, offset).wait_send()


def scatter(parts, items, count):
    chips = count // 2
    arrays, pieces = (len(parts), len(items))
    shapes = [(rows,) + parts[array].shape[2:] for array, _, rows, _ in items]
    kinds = [parts[array].dtype for array, _, _, _ in items]
    return pl.pallas_call(
        functools.partial(scatter_kernel, chips, arrays, items),
        out_shape=[jax.ShapeDtypeStruct(part.shape[1:], F32) for part in parts],
        in_specs=[pl.BlockSpec(memory_space=pl.ANY)] * arrays,
        out_specs=[pl.BlockSpec(memory_space=pltpu.VMEM)] * arrays,
        scratch_shapes=[pltpu.VMEM((chips - 1,) + shape, kind) for shape, kind in zip(shapes, kinds)]
        + [pltpu.VMEM((chips,) + shape, kind) for shape, kind in zip(shapes, kinds)]
        + [pltpu.VMEM((2,) + shape, kind) for shape, kind in zip(shapes, kinds)]
        + [
            pltpu.SemaphoreType.DMA((pieces, chips - 1)),
            pltpu.SemaphoreType.DMA((pieces, chips - 1)),
            pltpu.SemaphoreType.DMA((pieces, chips)),
            pltpu.SemaphoreType.DMA((pieces, chips)),
            pltpu.SemaphoreType.DMA((pieces, 2)),
        ],
        compiler_params=pltpu.CompilerParams(
            collective_id=1, has_side_effects=True, vmem_limit_bytes=62 * 2**20
        ),
    )(*parts)


def block_shape(rows, columns):
    return (rows, columns) if rows % 16 == 0 else (rows * columns // 128, 128)


def small_pack(gains, shifts, bias, count):
    width = gains.shape[1] // count
    ups = bias.shape[0] // gains.shape[1]
    rows = [
        gains.reshape(2, count, width).swapaxes(0, 1),
        shifts.reshape(6, count, width).swapaxes(0, 1),
        bias.reshape(count, ups, width),
    ]
    blank = jnp.zeros((count, 8 - ups, width), gains.dtype)
    return jnp.concatenate(rows + [blank], axis=1)


def small_split(blocks, ups):
    count, _, width = blocks.shape
    gains = blocks[:, 0:2].swapaxes(0, 1).reshape(2, count * width)
    shifts = blocks[:, 2:8].swapaxes(0, 1).reshape(6, count * width)
    bias = blocks[:, 8 : 8 + ups].reshape(count * ups * width)
    return (gains, shifts, bias)


def row_norm(rows_in):
    center = rows_in - jnp.mean(rows_in, axis=-1, keepdims=True)
    inverse = lax.rsqrt(jnp.mean(center * center, axis=-1, keepdims=True) + 1e-05)
    return (center * inverse, inverse)


def norm_back(grad_rows, normed, inverse):
    return inverse * (
        grad_rows
        - jnp.mean(grad_rows, axis=-1, keepdims=True)
        - normed * jnp.mean(grad_rows * normed, axis=-1, keepdims=True)
    )


def gelu_parts(hidden):
    size = jnp.abs(hidden)
    turn = 1.0 / (1.0 + (0.3275911 / math.sqrt(2.0)) * size)
    bell = jnp.exp(-0.5 * hidden * hidden)
    series = turn * (
        0.5 * 0.254829592
        + turn
        * (
            0.5 * -0.284496736
            + turn * (0.5 * 1.421413741 + turn * (0.5 * -1.453152027 + turn * (0.5 * 1.061405429)))
        )
    )
    tail = series * bell
    cumulative = jnp.where(hidden < 0.0, tail, 1.0 - tail)
    slope = cumulative + hidden * bell * (1.0 / math.sqrt(2.0 * math.pi))
    return (hidden * cumulative, slope)


def dot(left, right):
    return lax.dot_general(left, right, (((1,), (0,)), ((), ())), preferred_element_type=F32)


def dot_right(left, right):
    return lax.dot_general(left, right, (((1,), (1,)), ((), ())), preferred_element_type=F32)


def dot_left(left, right):
    return lax.dot_general(left, right, (((0,), (0,)), ((), ())), preferred_element_type=F32)


class Stream:
    def __init__(self, blocks, buffers, sems):
        self.blocks, self.buffers, self.sems = (blocks, buffers, sems)
        self.depth = buffers.shape[0]
        self.started = 0
        for _ in range(min(self.depth, len(blocks))):
            self.start()

    def copy(self, number):
        slot = number % self.depth
        return pltpu.make_async_copy(self.blocks[number], self.buffers.at[slot], self.sems.at[slot])

    def start(self):
        self.copy(self.started).start()
        self.started += 1

    def take(self, number):
        self.copy(number).wait()
        return self.buffers.at[number % self.depth]

    def release(self):
        if self.started < len(self.blocks):
            self.start()


def weight_blocks(w_qkv, w_out, w_up, w_down):
    width = w_out.shape[0]
    def cut(ref, axis, number):
        window = pl.ds(number * width, width)
        return ref.at[:, window] if axis else ref.at[window, :]
    heads = [cut(w_qkv, 1, number) for number in range(3)]
    ups = [cut(w_up, 1, number) for number in range(w_up.shape[1] // width)]
    downs = [cut(w_down, 0, number) for number in range(w_down.shape[0] // width)]
    return (heads, w_out, ups, downs)


def attend(packed, mixed, width):
    length = packed.shape[0]
    side = lax.broadcasted_iota(jnp.int32, (length, 128), 1) < HEAD_DIM

    @pl.loop(0, width // 128)
    def _(pair):
        start = pl.multiple_of(pair * 128, 128)
        queries = packed[:, pl.ds(start, 128)] * jnp.asarray(1.0 / math.sqrt(HEAD_DIM), LOW)
        keys = packed[:, pl.ds(start + width, 128)]
        values = packed[:, pl.ds(start + 2 * width, 128)]
        blank = jnp.zeros_like(queries)
        parts = []
        for head in (0, 1):
            mine = jnp.where(side, queries, blank) if head == 0 else jnp.where(side, blank, queries)
            scores = dot_right(mine, keys)
            shifted = jnp.exp(scores - jnp.max(scores, axis=-1, keepdims=True))
            total = jnp.sum(shifted, axis=-1, keepdims=True)
            parts.append(dot(shifted.astype(LOW), values) * (1.0 / total))
        mixed[:, pl.ds(start, 128)] = jnp.where(side, parts[0], parts[1]).astype(LOW)


def attend_back(packed, grad_mixed, grad_packed, width):
    length = packed.shape[0]
    side = lax.broadcasted_iota(jnp.int32, (length, 128), 1) < HEAD_DIM
    scale = 1.0 / math.sqrt(HEAD_DIM)

    @pl.loop(0, width // 128)
    def _(pair):
        start = pl.multiple_of(pair * 128, 128)
        queries = packed[:, pl.ds(start, 128)]
        keys = packed[:, pl.ds(start + width, 128)]
        values = packed[:, pl.ds(start + 2 * width, 128)]
        grads = grad_mixed[:, pl.ds(start, 128)]
        blank = jnp.zeros_like(queries)
        scaled = keys * jnp.asarray(scale, LOW)
        parts = []
        for head in (0, 1):
            def mine(array):
                return jnp.where(side, array, blank) if head == 0 else jnp.where(side, blank, array)
            scores = dot_right(mine(scaled), queries)
            shifted = jnp.exp(scores - jnp.max(scores, axis=0, keepdims=True))
            probs = shifted * (1.0 / jnp.sum(shifted, axis=0, keepdims=True))
            grad_probs = dot_right(mine(values), grads)
            product = grad_probs * probs
            weighted = jnp.sum(product, axis=0, keepdims=True)
            grad_scores = (product - probs * weighted).astype(LOW)
            parts.append((dot_left(grad_scores, scaled), dot(grad_scores, queries) * scale, dot(probs.astype(LOW), grads)))
        for number in range(3):
            grad_packed[:, pl.ds(start + number * width, 128)] = jnp.where(
                side, parts[0][number], parts[1][number]
            ).astype(LOW)


def forward_kernel(cell, held, active, entry, gains, shifts, bias, w_qkv, w_out, w_up, w_down, *refs):
    sent_h = refs[held]
    out_h, lowered_h, packed_h, mixed_h, middle_h, second_h, active_h, slope_h = [
        ref.at[cell] for ref in refs[held + 1 : held + 9]
    ]
    (buffers, buffer_sems, save_sems, out_v, lowered_v, packed_v, mixed_v, middle_v) = refs[held + 9 : held + 17]
    (second_v, active_v, slope_v, hidden_v, total_v) = refs[held + 17 :]
    width = entry.shape[1]
    ups = w_up.shape[1] // width

    @pl.when(active[0] != 0)
    def _():
        heads, outer, up, down = weight_blocks(w_qkv, w_out, w_up, w_down)
        order = heads + [outer]
        place_up, place_down = ({}, {})
        for number in range(ups + 1):
            if number < ups:
                place_up[number] = len(order)
                order.append(up[number])
            if number > 0:
                place_down[number - 1] = len(order)
                order.append(down[number - 1])
        stream = Stream(order, buffers, buffer_sems)
        saves = []

        def save(source, target):
            saves.append(pltpu.make_async_copy(source, target, save_sems.at[len(saves)]))
            saves[-1].start()

        rows_in = entry[...].astype(F32)
        normed, _ = row_norm(rows_in)
        lowered_v[...] = (normed * gains[0:1, :] + shifts[0:1, :]).astype(LOW)
        save(lowered_v, lowered_h)
        for number in range(3):
            block = stream.take(number)
            window = pl.ds(number * width, width)
            part = dot(lowered_v[...], block[...])
            if number != 1:
                part = part + shifts[1 + number // 2 : 2 + number // 2, :]
            packed_v[:, window] = part.astype(LOW)
            stream.release()
        save(packed_v, packed_h)
        attend(packed_v, mixed_v, width)
        save(mixed_v, mixed_h)
        block = stream.take(3)
        middle = entry[...].astype(F32) + dot(mixed_v[...], block[...]) + shifts[3:4, :]
        middle_v[...] = middle
        stream.release()
        save(middle_v, middle_h)
        normed, _ = row_norm(middle_v[...])
        second_v[...] = (normed * gains[1:2, :] + shifts[4:5, :]).astype(LOW)
        save(second_v, second_h)
        for number in range(ups + 1):
            if number < ups:
                up_block = stream.take(place_up[number])
            if number > 0:
                down_block = stream.take(place_down[number - 1])
            if number < ups:
                hidden_v[number % 2] = dot(second_v[...], up_block[...]) + bias[0:1, pl.ds(number * width, width)]
            if number > 0:
                window = pl.ds((number - 1) * width, width)
                activated, slope = gelu_parts(hidden_v[(number - 1) % 2])
                active_v[:, window] = activated.astype(LOW)
                slope_v[:, window] = slope.astype(LOW)
                part = dot(active_v[:, window], down_block[...])
                if number == 1:
                    total_v[...] = part
                elif number < ups:
                    total_v[...] += part
                else:
                    out_v[...] = (middle_v[...] + (total_v[...] + part + shifts[5:6, :])).astype(LOW)
                save(active_v.at[:, window], active_h.at[:, window])
                save(slope_v.at[:, window], slope_h.at[:, window])
            if number < ups:
                stream.release()
            if number > 0:
                stream.release()
        save(out_v, sent_h)
        save(out_v, out_h)
        for copy in saves:
            copy.wait()


def forward_tick(active, entry, small, weights, kept, cell, cell_count):
    length, width = entry.shape
    deep = weights[2].shape[1]
    ups = deep // width
    shapes = [
        ((length, width), LOW),
        ((length, width), LOW),
        ((length, 3 * width), LOW),
        ((length, width), LOW),
        ((length, width), F32),
        ((length, width), LOW),
        ((length, deep), LOW),
        ((length, deep), LOW),
    ]
    outs = [jax.ShapeDtypeStruct(*shapes[0])] + [
        jax.ShapeDtypeStruct((cell_count,) + shape, kind) for shape, kind in shapes
    ]
    vmem, hbm = (pl.BlockSpec(memory_space=pltpu.VMEM), pl.BlockSpec(memory_space=pl.ANY))
    flops = 2 * length * width * (4 * width + 2 * deep) + 16 * length * length * width
    kept = () if kept is None else tuple(kept)
    held = len(kept)
    sent, *kept = pl.pallas_call(
        functools.partial(forward_kernel, cell, held),
        out_shape=outs,
        in_specs=[pl.BlockSpec(memory_space=pltpu.SMEM)] + [vmem] * 4 + [hbm] * (4 + held),
        out_specs=[hbm] * 9,
        input_output_aliases={9 + number: 1 + number for number in range(held)},
        scratch_shapes=[
            pltpu.VMEM((4, width, width), LOW),
            pltpu.SemaphoreType.DMA((4,)),
            pltpu.SemaphoreType.DMA((7 + 2 * ups,)),
        ]
        + [pltpu.VMEM(*shape) for shape in shapes]
        + [pltpu.VMEM((2, length, width), F32), pltpu.VMEM((length, width), F32)],
        compiler_params=pltpu.CompilerParams(vmem_limit_bytes=60 * 2**20),
        cost_estimate=pl.CostEstimate(
            flops=flops, bytes_accessed=2 * width * (4 * width + 2 * deep), transcendentals=0
        ),
    )(active, entry, *small, *weights, *kept)
    return (sent, kept)


def backward_kernel(cell, held, active, scale, grad, entry, gains, shifts, *refs):
    packed, middle, slope = [ref.at[cell] for ref in refs[:3]]
    w_qkv, w_out, w_up, w_down = refs[3:7]
    refs = refs[7 + held :]
    sent_h = refs[0]
    rows_h, packed_h, branch_h, inner_h, low_h, sums_h = [ref.at[cell] for ref in refs[1:7]]
    (buffers, buffer_sems, load_sems, save_sems, rows_v, grad_packed_v, branch_v, inner_v, low_v, sums_v) = refs[7:17]
    (packed_v, middle_v, slope_v, mixed_v, grad_act_v, total_v, grad_middle_v) = refs[17:]
    length, width = entry.shape
    ups = w_up.shape[1] // width

    @pl.when(active[0] != 0)
    def _():
        heads, outer, up, down = weight_blocks(w_qkv, w_out, w_up, w_down)
        loads = [
            pltpu.make_async_copy(slope, slope_v, load_sems.at[0]),
            pltpu.make_async_copy(middle, middle_v, load_sems.at[1]),
            pltpu.make_async_copy(packed, packed_v, load_sems.at[2]),
        ]
        loads[0].start()
        order, place_up, place_down = ([], {}, {})
        for number in range(ups + 1):
            if number < ups:
                place_down[number] = len(order)
                order.append(down[number])
            if number > 0:
                place_up[number - 1] = len(order)
                order.append(up[number - 1])
        place_out = len(order)
        order = order + [outer] + heads
        stream = Stream(order, buffers, buffer_sems)
        loads[1].start()
        loads[2].start()
        saves = []

        def save(source, target):
            saves.append(pltpu.make_async_copy(source, target, save_sems.at[len(saves)]))
            saves[-1].start()

        def column_sum(array):
            return jnp.sum(array.astype(F32), axis=0, keepdims=True)

        low_v[...] = (grad[...].astype(F32) * scale[0]).astype(LOW)
        save(low_v, low_h)
        sums_v[7:8, :] = column_sum(low_v[...])
        loads[0].wait()
        for number in range(ups + 1):
            if number < ups:
                down_block = stream.take(place_down[number])
            if number > 0:
                up_block = stream.take(place_up[number - 1])
            if number < ups:
                grad_act_v[number % 2] = dot_right(low_v[...], down_block[...])
            if number > 0:
                window = pl.ds((number - 1) * width, width)
                inner = (grad_act_v[(number - 1) % 2] * slope_v[:, window].astype(F32)).astype(LOW)
                inner_v[:, window] = inner
                sums_v[7 + number : 8 + number, :] = column_sum(inner)
                part = dot_right(inner, up_block[...])
                if number == 1:
                    total_v[...] = part
                else:
                    total_v[...] += part
                save(inner_v.at[:, window], inner_h.at[:, window])
            if number < ups:
                stream.release()
            if number > 0:
                stream.release()
        loads[1].wait()
        normed, inverse = row_norm(middle_v[...])
        grad_second = total_v[...]
        sums_v[1:2, :] = column_sum(grad_second * normed)
        sums_v[6:7, :] = column_sum(grad_second)
        grad_middle = grad[...].astype(F32) * scale[0] + norm_back(grad_second * gains[1:2, :], normed, inverse)
        grad_middle_v[...] = grad_middle
        branch_v[...] = grad_middle.astype(LOW)
        sums_v[5:6, :] = column_sum(branch_v[...])
        save(branch_v, branch_h)
        block = stream.take(place_out)
        mixed_v[...] = dot_right(branch_v[...], block[...]).astype(LOW)
        stream.release()
        loads[2].wait()
        attend_back(packed_v, mixed_v, grad_packed_v, width)
        save(grad_packed_v, packed_h)
        sums_v[3:4, :] = column_sum(grad_packed_v[:, pl.ds(0, width)])
        sums_v[4:5, :] = column_sum(grad_packed_v[:, pl.ds(2 * width, width)])
        for number in range(3):
            block = stream.take(place_out + 1 + number)
            part = dot_right(grad_packed_v[:, pl.ds(number * width, width)], block[...])
            if number == 0:
                total_v[...] = part
            else:
                total_v[...] += part
            stream.release()
        normed, inverse = row_norm(entry[...].astype(F32))
        grad_lowered = total_v[...]
        sums_v[0:1, :] = column_sum(grad_lowered * normed)
        sums_v[2:3, :] = column_sum(grad_lowered)
        rows_v[...] = (grad_middle_v[...] + norm_back(grad_lowered * gains[0:1, :], normed, inverse)).astype(LOW)
        save(sums_v, sums_h)
        save(rows_v, sent_h)
        save(rows_v, rows_h)
        for copy in saves:
            copy.wait()


def backward_tick(active, incoming, entry, small, saved, weights, kept, cell, cell_count):
    length, width = entry.shape
    deep = weights[2].shape[1]
    ups = deep // width
    shapes = [
        ((length, width), LOW),
        ((length, 3 * width), LOW),
        ((length, width), LOW),
        ((length, deep), LOW),
        ((length, width), LOW),
        ((16, width), F32),
    ]
    outs = [jax.ShapeDtypeStruct(*shapes[0])] + [
        jax.ShapeDtypeStruct((cell_count,) + shape, kind) for shape, kind in shapes
    ]
    vmem, hbm = (pl.BlockSpec(memory_space=pltpu.VMEM), pl.BlockSpec(memory_space=pl.ANY))
    smem = pl.BlockSpec(memory_space=pltpu.SMEM)
    flops = 2 * length * width * (4 * width + 2 * deep) + 40 * length * length * width
    kept = () if kept is None else tuple(kept)
    held = len(kept)
    grad, scale = incoming
    sent, *kept = pl.pallas_call(
        functools.partial(backward_kernel, cell, held),
        out_shape=outs,
        in_specs=[smem] * 2 + [vmem] * 4 + [hbm] * (7 + held),
        out_specs=[hbm] * 7,
        input_output_aliases={13 + number: 1 + number for number in range(held)},
        scratch_shapes=[
            pltpu.VMEM((4, width, width), LOW),
            pltpu.SemaphoreType.DMA((4,)),
            pltpu.SemaphoreType.DMA((3,)),
            pltpu.SemaphoreType.DMA((6 + ups,)),
        ]
        + [pltpu.VMEM(*shape) for shape in shapes]
        + [
            pltpu.VMEM((length, 3 * width), LOW),
            pltpu.VMEM((length, width), F32),
            pltpu.VMEM((length, deep), LOW),
            pltpu.VMEM((length, width), LOW),
            pltpu.VMEM((2, length, width), F32),
            pltpu.VMEM((length, width), F32),
            pltpu.VMEM((length, width), F32),
        ],
        compiler_params=pltpu.CompilerParams(vmem_limit_bytes=60 * 2**20),
        cost_estimate=pl.CostEstimate(
            flops=flops, bytes_accessed=2 * width * (4 * width + 2 * deep), transcendentals=0
        ),
    )(active, scale, grad, entry, *small[:2], *saved, *weights, *kept)
    return (sent, kept)


def grads_kernel(chips, width, items, *refs):
    count = len(items)
    small_part, sides = (refs[0], refs[1:9])
    outs, parts = (refs[9:14], [small_part] + list(refs[14:18]))
    refs = refs[18:]
    landed, paired, mine = (refs[:count], refs[count : 2 * count], refs[2 * count : 3 * count])
    (big, cuts, stage, stage_down, final) = refs[3 * count : 3 * count + 5]
    (ring_send, ring_recv, pair_send, pair_recv, mine_sem, big_sem, cut_sem, stage_sem, final_sem) = refs[3 * count + 5 :]
    lowered, grad_packed, mixed, grad_branch, second, grad_inner, activated, grad_ff = sides
    splits = [way for _, _, _, way in items]
    half = chips // 2
    devices = 2 * chips
    own = width // devices
    deep_own = activated.shape[1] // devices
    cut = cuts.shape[2]
    me, core, position, right, left, sibling = ring_place(chips)

    def load_big(source, slot):
        return pltpu.make_async_copy(source, big.at[slot], big_sem.at[slot])

    def load_cut(source, index, slot):
        window = pl.ds(pl.multiple_of(index * cut, cut), cut)
        return pltpu.make_async_copy(source.at[:, window], cuts.at[slot], cut_sem.at[slot])

    load_big(grad_ff, 0).start()
    greet((left, right, sibling))

    def part(item, block):
        array, start, rows, _ = items[item]
        return parts[array].at[block, pl.ds(start, rows)]

    def first(item, way):
        return 1 if splits[item] == way else 2

    def slot_of(item, way, step):
        return step - 1 if splits[item] == way else half + step - 2

    def offset_of(step, way):
        return half - step + 1 if way == 0 else chips - (half - step + 1)

    def pair_copy(item, offset):
        block = ring_chip(position + offset, chips) * 2 + 1 - core
        return pltpu.make_async_remote_copy(
            src_ref=part(item, block),
            dst_ref=paired[item].at[offset],
            send_sem=pair_send.at[item, offset],
            recv_sem=pair_recv.at[item, offset],
            device_id={"dp": sibling},
            device_id_type=MESH,
        )

    def ring_copy(item, way, step):
        if step == first(item, way):
            source = paired[item].at[offset_of(step, way)]
        else:
            source = landed[item].at[slot_of(item, way, step - 1)]
        here = slot_of(item, way, step)
        return pltpu.make_async_remote_copy(
            src_ref=source,
            dst_ref=landed[item].at[here],
            send_sem=ring_send.at[item, here],
            recv_sem=ring_recv.at[item, here],
            device_id={"dp": right if way == 0 else left},
            device_id_type=MESH,
        )

    def load(item, offset, buffer):
        block = ring_chip(position + offset, chips) * 2 + core
        return pltpu.make_async_copy(part(item, block), mine[item].at[buffer], mine_sem.at[item, buffer])

    def starts(wanted):
        return [
            (step, item, way, offset_of(step, way))
            for step in (1, 2)
            for item in wanted
            for way in (0, 1)
            if step == first(item, way)
        ]

    downs = [item for item in range(count) if items[item][0] == 4]
    ups = [item for item in range(count) if items[item][0] == 3]
    others = [item for item in range(count) if items[item][0] < 3]
    every = downs + ups + others
    rest = [
        (step, item, way, offset_of(step, way))
        for step in range(2, half + 1)
        for item in every
        for way in (0, 1)
        if step > first(item, way)
    ] + [(half + 1, item, None, 0) for item in every]
    uses = [0] * count

    def numbered(plan):
        result = []
        for entry in plan:
            result.append(entry + (uses[entry[1]] % 2,))
            uses[entry[1]] += 1
        return result

    finals = [0]

    def fetch(entry):
        load(entry[1], entry[3], entry[4]).start()

    def work(entry):
        step, item, way, offset, buffer = entry
        array, start, rows, _ = items[item]
        load(item, offset, buffer).wait()
        pair_copy(item, offset).wait_recv()
        kind = parts[array].dtype
        columns = parts[array].shape[2]
        chunk = 16
        from_pair, from_mine, from_ring = (paired[item], mine[item], landed[item])
        if way is None:
            ring_copy(item, 0, half).wait_recv()
            ring_copy(item, 1, half).wait_recv()
            slot_a, slot_b = (slot_of(item, 0, half), slot_of(item, 1, half))
            if array == 0:
                outs[0][...] = (from_ring[slot_a] + from_ring[slot_b]) + (from_mine[buffer] + from_pair[offset])
                return
            high, wide = (min(rows, final.shape[1]), min(columns, final.shape[2]))
            for top in range(0, rows, high):
                for across in range(0, columns, wide):
                    number = finals[0]
                    finals[0] += 1
                    turn = number % final.shape[0]
                    if number >= final.shape[0]:
                        final_copies[number - final.shape[0]].wait()
                    span = pl.ds(across, wide)

                    @pl.loop(0, high // chunk)
                    def _(index):
                        here = pl.ds(pl.multiple_of(top + index * chunk, chunk), chunk)
                        final[turn, pl.ds(pl.multiple_of(index * chunk, chunk), chunk), pl.ds(0, wide)] = (
                            from_ring[slot_a, here, span].astype(F32) + from_ring[slot_b, here, span].astype(F32)
                        ) + (from_mine[buffer, here, span].astype(F32) + from_pair[offset, here, span].astype(F32))

                    final_copies.append(
                        pltpu.make_async_copy(
                            final.at[turn, pl.ds(0, high), pl.ds(0, wide)],
                            outs[array].at[pl.ds(start + top, high), span],
                            final_sem.at[turn],
                        )
                    )
                    final_copies[-1].start()
            return
        if step == first(item, way):

            @pl.loop(0, rows // chunk)
            def _(index):
                here = pl.ds(pl.multiple_of(index * chunk, chunk), chunk)
                from_pair[offset, here, :] = (
                    from_mine[buffer, here, :].astype(F32) + from_pair[offset, here, :].astype(F32)
                ).astype(kind)

        else:
            ring_copy(item, way, step - 1).wait_recv()
            arrived = slot_of(item, way, step - 1)

            @pl.loop(0, rows // chunk)
            def _(index):
                here = pl.ds(pl.multiple_of(index * chunk, chunk), chunk)
                from_ring[arrived, here, :] = (
                    from_ring[arrived, here, :].astype(F32)
                    + (from_mine[buffer, here, :].astype(F32) + from_pair[offset, here, :].astype(F32))
                ).astype(kind)

        sent.append(ring_copy(item, way, step))
        sent[-1].start()

    def run(plan):
        plan = numbered(plan)
        if plan:
            fetch(plan[0])
        for number, entry in enumerate(plan):
            if number + 1 < len(plan):
                fetch(plan[number + 1])
            work(entry)

    sent, final_copies = ([], [])
    def farthest_first(index):
        step = index // 2
        return ring_chip(position + jnp.where(lax.rem(index, 2) == 0, half - step, half + step + 1), chips)

    def keep_down(index):
        return pltpu.make_async_copy(
            stage_down.at[lax.rem(index, 2)],
            parts[4].at[pl.ds(farthest_first(index) * 2, 2)],
            stage_sem.at[lax.rem(index, 2)],
        )

    def cut_down(index):
        return load_cut(activated, farthest_first(index), lax.rem(index, 2))

    def down_products(low, high):
        @pl.loop(low, high)
        def _(index):
            slot = lax.rem(index, 2)

            @pl.when(index + 1 < chips)
            def _():
                cut_down(index + 1).start()

            cut_down(index).wait()

            @pl.when(index >= low + 2)
            def _():
                keep_down(index - 2).wait()

            product = dot_left(cuts[slot], big[0]).astype(LOW)
            for side in (0, 1):
                stage_down[slot, side] = product[side * deep_own : (side + 1) * deep_own]
            keep_down(index).start()

        for index in range(max(low, high - 2), high):
            keep_down(index).wait()

    def block(source, index, slot):
        window = pl.ds(pl.multiple_of(index * width, width), width)
        return pltpu.make_async_copy(source.at[:, window], big.at[slot], big_sem.at[slot])

    def keep(array, index):
        window = pl.ds(pl.multiple_of(index // 2 * width, width), width)
        return pltpu.make_async_copy(
            stage.at[lax.rem(index, 2)],
            parts[array].at[pl.ds(lax.rem(index, 2) * chips, chips), :, window],
            stage_sem.at[2 + lax.rem(index, 2)],
        )

    def open_products(left_side, right_side, slot):
        for index in (0, 1):
            load_cut(left_side, index, index).start()
        block(right_side, 0, slot).start()

    def products(array, left_side, right_side, shift, low, high):
        number = 2 * (right_side.shape[1] // width)
        if low == 0:
            for index in (0, 1):
                load_cut(left_side, index, index).wait()

        @pl.loop(low, high)
        def _(index):
            slot = lax.rem(index, 2)
            here = lax.rem(index // 2 + shift, 2)

            @pl.when(slot == 0)
            def _():
                block(right_side, index // 2, here).wait()

                @pl.when(index + 2 < number)
                def _():
                    block(right_side, index // 2 + 1, 1 - here).start()

            @pl.when(index >= low + 2)
            def _():
                keep(array, index - 2).wait()

            product = dot_left(cuts[slot], big[here]).astype(LOW)
            for device in range(chips):
                stage[slot, device] = product[device * own : (device + 1) * own]
            keep(array, index).start()

        for index in range(max(low, high - 2), high):
            keep(array, index).wait()

    def exchange(wanted, offsets):
        for offset in offsets:
            for item in wanted:
                pair_copy(item, offset).start()

    far = [half, half - 1, half + 1]
    near = [offset for offset in range(chips) if offset not in far]
    order = far + near

    def advance(wanted, steps):
        return [entry for entry in rest if entry[1] in wanted and entry[0] in steps]

    deep_blocks = grad_inner.shape[1] // width
    head_blocks = grad_packed.shape[1] // width
    cut_down(0).start()
    load_big(grad_ff, 0).wait()
    down_products(0, 3)
    exchange(downs, far)
    down_products(3, 5)
    run(starts(downs))
    down_products(5, chips)
    exchange(downs, near)
    open_products(second, grad_inner, 1)
    products(3, second, grad_inner, 1, 0, deep_blocks)
    run(advance(downs, (2,)))
    products(3, second, grad_inner, 1, deep_blocks, 2 * deep_blocks)
    exchange(ups, order)
    open_products(mixed, grad_branch, 1)
    run(advance(downs, (3,)))
    products(2, mixed, grad_branch, 1, 0, 2)
    open_products(lowered, grad_packed, 0)
    run(starts(ups))
    products(1, lowered, grad_packed, 0, 0, head_blocks)
    run(advance(ups, (2,)))
    products(1, lowered, grad_packed, 0, head_blocks, 2 * head_blocks)
    exchange(others, order)
    run(advance(ups, (3,)))
    run(starts(others))
    done = advance(downs, (2, 3)) + advance(ups, (2, 3))
    run([entry for entry in rest if entry not in done])
    for copy in sent:
        copy.wait_send()
    for item in every:
        for offset in range(chips):
            pair_copy(item, offset).wait_send()
    for copy in final_copies[-final.shape[0] :]:
        copy.wait()


def weight_grads(small_part, sides, items, shapes, count):
    chips = count // 2
    rows_in, width = sides[0].shape
    pieces = len(items)
    wholes = [small_part.shape[1:]] + list(shapes)
    held = [(rows,) + wholes[array][1:] for array, _, rows, _ in items]
    kinds = [F32 if array == 0 else LOW for array, _, _, _ in items]
    hbm = pl.BlockSpec(memory_space=pl.ANY)
    cut = width // 2
    flops = 2 * rows_in * sum(shape[0] * shape[1] for shape in shapes) * count
    outs = pl.pallas_call(
        functools.partial(grads_kernel, chips, width, items),
        out_shape=[jax.ShapeDtypeStruct(shape, F32) for shape in wholes]
        + [jax.ShapeDtypeStruct((count,) + tuple(shape), LOW) for shape in shapes],
        in_specs=[hbm] * 9,
        out_specs=[pl.BlockSpec(memory_space=pltpu.VMEM)] + [hbm] * 8,
        scratch_shapes=[pltpu.VMEM((chips - 1,) + shape, kind) for shape, kind in zip(held, kinds)]
        + [pltpu.VMEM((chips,) + shape, kind) for shape, kind in zip(held, kinds)]
        + [pltpu.VMEM((2,) + shape, kind) for shape, kind in zip(held, kinds)]
        + [
            pltpu.VMEM((2, rows_in, width), LOW),
            pltpu.VMEM((2, rows_in, cut), LOW),
            pltpu.VMEM((2, chips, width // count, width), LOW),
            pltpu.VMEM((2, 2, shapes[3][0], width), LOW),
            pltpu.VMEM((4, shapes[0][0], width), F32),
            pltpu.SemaphoreType.DMA((pieces, chips - 1)),
            pltpu.SemaphoreType.DMA((pieces, chips - 1)),
            pltpu.SemaphoreType.DMA((pieces, chips)),
            pltpu.SemaphoreType.DMA((pieces, chips)),
            pltpu.SemaphoreType.DMA((pieces, 2)),
            pltpu.SemaphoreType.DMA((2,)),
            pltpu.SemaphoreType.DMA((2,)),
            pltpu.SemaphoreType.DMA((4,)),
            pltpu.SemaphoreType.DMA((4,)),
        ],
        compiler_params=pltpu.CompilerParams(
            collective_id=2, has_side_effects=True, vmem_limit_bytes=62 * 2**20
        ),
        cost_estimate=pl.CostEstimate(flops=flops, bytes_accessed=8 * width * width * 12, transcendentals=0),
    )(small_part, *sides)
    return outs[:5]


def on_device(inputs, out_grad, query_counts, gains, shifts, w_qkv, w_out, w_up, b_up, w_down):
    stage = lax.axis_index("pipe")
    stages = lax.axis_size("pipe")
    count = lax.axis_size("dp")
    cell_count, length, width = inputs.shape
    own = width // count
    ups = b_up.shape[1] // own
    deep = ups * width
    deep_own = w_down.shape[1]
    shapes = [
        block_shape(own, 3 * width),
        block_shape(own, width),
        block_shape(own, deep),
        block_shape(deep_own, width),
    ]
    cut = (shapes[3][0] // 2 + 15) // 16 * 16
    items = (
        (0, 0, 16, 0),
        (1, 0, shapes[0][0], 0),
        (2, 0, shapes[1][0], 0),
        (3, 0, shapes[2][0], 1),
        (4, 0, cut, 0),
        (4, cut, shapes[3][0] - cut, 1),
    )
    shards = [small_pack(gains[0], shifts[0], b_up[0], 1)[0]] + [
        array[0].reshape(shape) for array, shape in zip((w_qkv, w_out, w_up, w_down), shapes)
    ]
    packs = gather(shards, items, count)
    gain_rows, shift_rows, bias = small_split(packs[0].astype(F32), ups)
    small = (gain_rows, shift_rows, bias[None])
    weights = (
        packs[1].reshape(width, 3 * width),
        packs[2].reshape(width, width),
        packs[3].reshape(width, deep),
        packs[4].reshape(deep, width),
    )
    scales = jnp.sqrt(query_counts.astype(F32) / 500.0)

    def along(value, steps):
        pairs = [(source, source + steps) for source in range(stages) if 0 <= source + steps < stages]
        return lax.ppermute(value, "pipe", pairs)

    entries, kept = ([[inputs[cell] for cell in range(cell_count)]], None)
    for turn in range(stages):
        active = (stage == turn).astype(jnp.int32)[None]
        arrived = []
        for cell in range(cell_count):
            sent, kept = forward_tick(active, entries[turn][cell], small, weights, kept, cell, cell_count)
            if turn + 1 < stages:
                arrived.append(along(sent, 1))
        entries.append(arrived)
    section_out, lowered, packed, mixed, middle, second, activated, slope = kept
    incoming = [(out_grad[cell], scales[cell][None]) for cell in range(cell_count)]
    back = None
    for turn in range(stages - 1, -1, -1):
        active = (stage == turn).astype(jnp.int32)[None]
        arrived = []
        for cell in range(cell_count):
            sent, back = backward_tick(
                active, incoming[cell], entries[turn][cell], small, (packed, middle, slope), weights, back, cell, cell_count
            )
            if turn > 0:
                arrived.append((along(sent, -1), jnp.ones((1,), F32)))
        incoming = arrived
    input_grads, grad_packed, grad_branch, grad_inner, grad_ff, sums = back
    sums = jnp.sum(sums, axis=0)

    small_part = small_pack(sums[0:2], sums[2:8], sums[8 : 8 + ups].reshape(deep), count)
    sides = [
        array.reshape(cell_count * length, -1)
        for array in (lowered, grad_packed, mixed, grad_branch, second, grad_inner, activated, grad_ff)
    ]
    if own % 16 == 0 and width % 256 == 0 and 4 * deep_own == width:
        shares = weight_grads(small_part, sides, items, shapes, count)
    else:
        products = [dot_left(sides[at], sides[at + 1]).astype(LOW) for at in (0, 2, 4, 6)]
        parts = [small_part] + [whole.reshape((count,) + shape) for whole, shape in zip(products, shapes)]
        shares = scatter(parts, items, count)
    grad_gains, grad_shifts, grad_bias = small_split(shares[0][None], ups)
    return (
        section_out[None],
        input_grads[None],
        grad_gains[None],
        grad_shifts[None],
        shares[1].reshape(1, own, 3 * width),
        shares[2].reshape(1, own, width),
        shares[3].reshape(1, own, deep),
        grad_bias[None],
        shares[4].reshape(1, deep_own, width),
    )


def solution(mesh):
    in_specs = (
        P("dp", None, None),
        P("dp", None, None),
        P("dp"),
        P("pipe", None, "dp"),
        P("pipe", None, "dp"),
        P("pipe", "dp", None),
        P("pipe", "dp", None),
        P("pipe", "dp", None),
        P("pipe", "dp"),
        P("pipe", "dp", None),
    )
    out_specs = (
        P("pipe", "dp", None, None),
        P("pipe", "dp", None, None),
        P("pipe", None, "dp"),
        P("pipe", None, "dp"),
        P("pipe", "dp", None),
        P("pipe", "dp", None),
        P("pipe", "dp", None),
        P("pipe", "dp"),
        P("pipe", "dp", None),
    )
    return jax.shard_map(
        on_device, mesh=mesh, in_specs=in_specs, out_specs=out_specs, check_vma=False
    )
```

```python
import functools
import math

import jax
import jax.numpy as jnp
from jax import lax
from jax.experimental import pallas as pl
from jax.experimental.pallas import tpu as pltpu
from jax.sharding import PartitionSpec as P

HEAD_DIM = 64
MESH = pl.DeviceIdType.MESH
LOW = jnp.bfloat16
F32 = jnp.float32


def ring_chip(position, chips):
    position = lax.rem(position + 2 * chips, chips)
    half = chips // 2
    return jnp.where(position < half, 2 * position, 2 * (chips - 1 - position) + 1)


def ring_place(chips):
    me = lax.axis_index("dp")
    core = lax.rem(me, 2)
    chip = me // 2
    position = jnp.where(lax.rem(chip, 2) == 0, chip // 2, chips - 1 - chip // 2)
    right = ring_chip(position + 1, chips) * 2 + core
    left = ring_chip(position - 1, chips) * 2 + core
    return (me, core, position, right, left, me + 1 - 2 * core)


def greet(devices):
    barrier = pltpu.get_barrier_semaphore()
    for device in devices:
        pl.semaphore_signal(barrier, inc=1, device_id={"dp": device}, device_id_type=MESH)
    pl.semaphore_wait(barrier, len(devices))


def gather_kernel(chips, arrays, items, *refs):
    count = len(items)
    ring_send, ring_recv, pair_send, pair_recv, own_sem = refs[2 * arrays :]
    shards = [refs[array].at[pl.ds(start, rows)] for array, start, rows, _ in items]
    splits = [way for _, _, _, way in items]
    half = chips // 2
    me, core, position, right, left, sibling = ring_place(chips)
    greet((left, right, sibling))

    def out(item, block):
        array, start, rows, _ = items[item]
        return refs[arrays + array].at[block, pl.ds(start, rows)]

    def owner(step, way):
        return ring_chip(position - step if way == 0 else position + step, chips) * 2 + core

    def travels(item, way, step):
        return step < half or (step == half and splits[item] == way)

    def ring_copy(item, way, step):
        block = owner(step - 1, way)
        return pltpu.make_async_remote_copy(
            src_ref=shards[item] if step == 1 else out(item, block),
            dst_ref=out(item, block),
            send_sem=ring_send.at[item, way, step - 1],
            recv_sem=ring_recv.at[item, way, step - 1],
            device_id={"dp": right if way == 0 else left},
            device_id_type=MESH,
        )

    def pair_copy(item, offset, block, source):
        return pltpu.make_async_remote_copy(
            src_ref=source,
            dst_ref=out(item, block),
            send_sem=pair_send.at[item, offset],
            recv_sem=pair_recv.at[item, offset],
            device_id={"dp": sibling},
            device_id_type=MESH,
        )

    sent, paired, kept = ([], [], [])
    for item in range(count):
        for way in (0, 1):
            if travels(item, way, 1):
                sent.append(ring_copy(item, way, 1))
                sent[-1].start()
    for item in range(count):
        paired.append(pair_copy(item, 0, me, shards[item]))
        paired[-1].start()
        kept.append(pltpu.make_async_copy(shards[item], out(item, me), own_sem.at[item]))
        kept[-1].start()
    for step in range(1, half + 1):
        for item in range(count):
            for way in (0, 1):
                if not travels(item, way, step):
                    continue
                ring_copy(item, way, step).wait_recv()
                if travels(item, way, step + 1):
                    sent.append(ring_copy(item, way, step + 1))
                    sent[-1].start()
                block = owner(step, way)
                offset = step if way == 0 else chips - step
                paired.append(pair_copy(item, offset, block, out(item, block)))
                paired[-1].start()
    for copy in sent:
        copy.wait_send()
    for copy in paired:
        copy.wait()
    for copy in kept:
        copy.wait()


def gather(shards, items, count):
    chips = count // 2
    arrays, pieces = (len(shards), len(items))
    return pl.pallas_call(
        functools.partial(gather_kernel, chips, arrays, items),
        out_shape=[jax.ShapeDtypeStruct((count,) + shard.shape, shard.dtype) for shard in shards],
        in_specs=[pl.BlockSpec(memory_space=pl.ANY)] * arrays,
        out_specs=[pl.BlockSpec(memory_space=pl.ANY)] * arrays,
        scratch_shapes=[
            pltpu.SemaphoreType.DMA((pieces, 2, chips // 2)),
            pltpu.SemaphoreType.DMA((pieces, 2, chips // 2)),
            pltpu.SemaphoreType.DMA((pieces, chips)),
            pltpu.SemaphoreType.DMA((pieces, chips)),
            pltpu.SemaphoreType.DMA((pieces,)),
        ],
        compiler_params=pltpu.CompilerParams(collective_id=0, has_side_effects=True),
    )(*shards)


def scatter_kernel(chips, arrays, items, *refs):
    count = len(items)
    parts, outs, refs = (refs[:arrays], refs[arrays : 2 * arrays], refs[2 * arrays :])
    landed, paired, mine = (refs[:count], refs[count : 2 * count], refs[2 * count : 3 * count])
    ring_send, ring_recv, pair_send, pair_recv, mine_sem = refs[3 * count :]
    splits = [way for _, _, _, way in items]
    half = chips // 2
    me, core, position, right, left, sibling = ring_place(chips)
    greet((left, right, sibling))

    def part(item, block):
        array, start, rows, _ = items[item]
        return parts[array].at[block, pl.ds(start, rows)]

    def first(item, way):
        return 1 if splits[item] == way else 2

    def slot(item, way, step):
        return step - 1 if splits[item] == way else half + step - 2

    def offset_of(step, way):
        return half - step + 1 if way == 0 else chips - (half - step + 1)

    def pair_copy(item, offset):
        block = ring_chip(position + offset, chips) * 2 + 1 - core
        return pltpu.make_async_remote_copy(
            src_ref=part(item, block),
            dst_ref=paired[item].at[offset],
            send_sem=pair_send.at[item, offset],
            recv_sem=pair_recv.at[item, offset],
            device_id={"dp": sibling},
            device_id_type=MESH,
        )

    def ring_copy(item, way, step):
        if step == first(item, way):
            source = paired[item].at[offset_of(step, way)]
        else:
            source = landed[item].at[slot(item, way, step - 1)]
        here = slot(item, way, step)
        return pltpu.make_async_remote_copy(
            src_ref=source,
            dst_ref=landed[item].at[here],
            send_sem=ring_send.at[item, here],
            recv_sem=ring_recv.at[item, here],
            device_id={"dp": right if way == 0 else left},
            device_id_type=MESH,
        )

    def load(item, offset, buffer):
        block = ring_chip(position + offset, chips) * 2 + core
        return pltpu.make_async_copy(part(item, block), mine[item].at[buffer], mine_sem.at[item, buffer])

    plan, uses = ([], [0] * count)
    for step in range(1, half + 2):
        for item in range(count):
            for way in (0, 1):
                if step <= half and step >= first(item, way):
                    plan.append((step, item, way, offset_of(step, way), uses[item] % 2))
                    uses[item] += 1
            if step > half:
                plan.append((step, item, None, 0, uses[item] % 2))
                uses[item] += 1
    for step, item, way, offset, buffer in plan:
        pair_copy(item, offset).start()
    load(plan[0][1], plan[0][3], plan[0][4]).start()
    sent = []
    for number, (step, item, way, offset, buffer) in enumerate(plan):
        if number + 1 < len(plan):
            load(plan[number + 1][1], plan[number + 1][3], plan[number + 1][4]).start()
        load(item, offset, buffer).wait()
        pair_copy(item, offset).wait_recv()
        array, start, rows, _ = items[item]
        kind = parts[array].dtype
        chunk = 16 if rows % 16 == 0 else rows
        from_pair, from_mine, from_ring = (paired[item], mine[item], landed[item])
        if way is None:
            ring_copy(item, 0, half).wait_recv()
            ring_copy(item, 1, half).wait_recv()
            slot_a, slot_b = (slot(item, 0, half), slot(item, 1, half))

            @pl.loop(0, rows // chunk)
            def _(index):
                here = pl.ds(pl.multiple_of(index * chunk, chunk), chunk)
                outs[array][pl.ds(pl.multiple_of(start + index * chunk, chunk), chunk), :] = (
                    from_ring[slot_a, here, :].astype(F32) + from_ring[slot_b, here, :].astype(F32)
                ) + (from_mine[buffer, here, :].astype(F32) + from_pair[offset, here, :].astype(F32))

            continue
        if step == first(item, way):

            @pl.loop(0, rows // chunk)
            def _(index):
                here = pl.ds(pl.multiple_of(index * chunk, chunk), chunk)
                from_pair[offset, here, :] = (
                    from_mine[buffer, here, :].astype(F32) + from_pair[offset, here, :].astype(F32)
                ).astype(kind)

        else:
            ring_copy(item, way, step - 1).wait_recv()
            arrived = slot(item, way, step - 1)

            @pl.loop(0, rows // chunk)
            def _(index):
                here = pl.ds(pl.multiple_of(index * chunk, chunk), chunk)
                from_ring[arrived, here, :] = (
                    from_ring[arrived, here, :].astype(F32)
                    + (from_mine[buffer, here, :].astype(F32) + from_pair[offset, here, :].astype(F32))
                ).astype(kind)

        sent.append(ring_copy(item, way, step))
        sent[-1].start()
    for copy in sent:
        copy.wait_send()
    for step, item, way, offset, buffer in plan:
        pair_copy(item, offset).wait_send()


def scatter(parts, items, count):
    chips = count // 2
    arrays, pieces = (len(parts), len(items))
    shapes = [(rows,) + parts[array].shape[2:] for array, _, rows, _ in items]
    kinds = [parts[array].dtype for array, _, _, _ in items]
    return pl.pallas_call(
        functools.partial(scatter_kernel, chips, arrays, items),
        out_shape=[jax.ShapeDtypeStruct(part.shape[1:], F32) for part in parts],
        in_specs=[pl.BlockSpec(memory_space=pl.ANY)] * arrays,
        out_specs=[pl.BlockSpec(memory_space=pltpu.VMEM)] * arrays,
        scratch_shapes=[pltpu.VMEM((chips - 1,) + shape, kind) for shape, kind in zip(shapes, kinds)]
        + [pltpu.VMEM((chips,) + shape, kind) for shape, kind in zip(shapes, kinds)]
        + [pltpu.VMEM((2,) + shape, kind) for shape, kind in zip(shapes, kinds)]
        + [
            pltpu.SemaphoreType.DMA((pieces, chips - 1)),
            pltpu.SemaphoreType.DMA((pieces, chips - 1)),
            pltpu.SemaphoreType.DMA((pieces, chips)),
            pltpu.SemaphoreType.DMA((pieces, chips)),
            pltpu.SemaphoreType.DMA((pieces, 2)),
        ],
        compiler_params=pltpu.CompilerParams(
            collective_id=1, has_side_effects=True, vmem_limit_bytes=62 * 2**20
        ),
    )(*parts)


def block_shape(rows, columns):
    return (rows, columns) if rows % 16 == 0 else (rows * columns // 128, 128)


def small_pack(gains, shifts, bias, count):
    width = gains.shape[1] // count
    ups = bias.shape[0] // gains.shape[1]
    rows = [
        gains.reshape(2, count, width).swapaxes(0, 1),
        shifts.reshape(6, count, width).swapaxes(0, 1),
        bias.reshape(count, ups, width),
    ]
    blank = jnp.zeros((count, 8 - ups, width), gains.dtype)
    return jnp.concatenate(rows + [blank], axis=1)


def small_split(blocks, ups):
    count, _, width = blocks.shape
    gains = blocks[:, 0:2].swapaxes(0, 1).reshape(2, count * width)
    shifts = blocks[:, 2:8].swapaxes(0, 1).reshape(6, count * width)
    bias = blocks[:, 8 : 8 + ups].reshape(count * ups * width)
    return (gains, shifts, bias)


def row_norm(rows_in):
    center = rows_in - jnp.mean(rows_in, axis=-1, keepdims=True)
    inverse = lax.rsqrt(jnp.mean(center * center, axis=-1, keepdims=True) + 1e-05)
    return (center * inverse, inverse)


def norm_back(grad_rows, normed, inverse):
    return inverse * (
        grad_rows
        - jnp.mean(grad_rows, axis=-1, keepdims=True)
        - normed * jnp.mean(grad_rows * normed, axis=-1, keepdims=True)
    )


def gelu_parts(hidden):
    cumulative = 0.5 * (1.0 + lax.erf(hidden * (1.0 / math.sqrt(2.0))))
    slope = cumulative + hidden * jnp.exp(-0.5 * hidden * hidden) * (1.0 / math.sqrt(2.0 * math.pi))
    return (hidden * cumulative, slope)


def dot(left, right):
    return lax.dot_general(left, right, (((1,), (0,)), ((), ())), preferred_element_type=F32)


def dot_right(left, right):
    return lax.dot_general(left, right, (((1,), (1,)), ((), ())), preferred_element_type=F32)


def dot_left(left, right):
    return lax.dot_general(left, right, (((0,), (0,)), ((), ())), preferred_element_type=F32)


class Stream:
    def __init__(self, blocks, buffers, sems):
        self.blocks, self.buffers, self.sems = (blocks, buffers, sems)
        self.depth = buffers.shape[0]
        self.started = 0
        for _ in range(min(self.depth, len(blocks))):
            self.start()

    def copy(self, number):
        slot = number % self.depth
        return pltpu.make_async_copy(self.blocks[number], self.buffers.at[slot], self.sems.at[slot])

    def start(self):
        self.copy(self.started).start()
        self.started += 1

    def take(self, number):
        self.copy(number).wait()
        return self.buffers.at[number % self.depth]

    def release(self):
        if self.started < len(self.blocks):
            self.start()


def weight_blocks(w_qkv, w_out, w_up, w_down):
    width = w_out.shape[0]
    def cut(ref, axis, number):
        window = pl.ds(number * width, width)
        return ref.at[:, window] if axis else ref.at[window, :]
    heads = [cut(w_qkv, 1, number) for number in range(3)]
    ups = [cut(w_up, 1, number) for number in range(w_up.shape[1] // width)]
    downs = [cut(w_down, 0, number) for number in range(w_down.shape[0] // width)]
    return (heads, w_out, ups, downs)


def head_masks(length):
    return lax.broadcasted_iota(jnp.int32, (length, 128), 1) < HEAD_DIM


def two_heads(array, side):
    blank = jnp.zeros_like(array)
    return jnp.concatenate([jnp.where(side, array, blank), jnp.where(side, blank, array)], axis=0)


def attend(packed, mixed, width):
    length = packed.shape[0]
    side = head_masks(length)

    def pair_of(pair):
        start = pl.multiple_of(pair * 128, 128)
        queries = packed[:, pl.ds(start, 128)] * jnp.asarray(1.0 / math.sqrt(HEAD_DIM), LOW)
        keys = two_heads(packed[:, pl.ds(start + width, 128)], side)
        values = two_heads(packed[:, pl.ds(start + 2 * width, 128)], side)
        scores = dot_right(queries, keys)
        probs, totals = ([], [])
        for head in (0, 1):
            mine = scores[:, head * length : (head + 1) * length]
            shifted = jnp.exp(mine - jnp.max(mine, axis=-1, keepdims=True))
            totals.append(1.0 / jnp.sum(shifted, axis=-1, keepdims=True))
            probs.append(shifted.astype(LOW))
        result = dot(jnp.concatenate(probs, axis=1), values)
        mixed[:, pl.ds(start, 128)] = (result * jnp.where(side, totals[0], totals[1])).astype(LOW)

    @pl.loop(0, width // 256)
    def _(index):
        pair_of(index * 2)
        pair_of(index * 2 + 1)


def attend_back(packed, grad_mixed, grad_packed, width):
    length = packed.shape[0]
    side = head_masks(length)
    scale = 1.0 / math.sqrt(HEAD_DIM)

    def pair_of(pair):
        start = pl.multiple_of(pair * 128, 128)
        queries = packed[:, pl.ds(start, 128)]
        keys = packed[:, pl.ds(start + width, 128)] * jnp.asarray(scale, LOW)
        grads = grad_mixed[:, pl.ds(start, 128)]
        keys_two = two_heads(keys, side)
        queries_two = two_heads(queries, side)
        grads_two = two_heads(grads, side)
        scores = dot_right(keys, queries_two)
        grad_probs = dot_right(packed[:, pl.ds(start + 2 * width, 128)], grads_two)
        probs, grad_scores = ([], [])
        for head in (0, 1):
            mine = slice(head * length, (head + 1) * length)
            shifted = jnp.exp(scores[:, mine] - jnp.max(scores[:, mine], axis=0, keepdims=True))
            prob = shifted * (1.0 / jnp.sum(shifted, axis=0, keepdims=True))
            product = grad_probs[:, mine] * prob
            weighted = jnp.sum(product, axis=0, keepdims=True)
            probs.append(prob.astype(LOW))
            grad_scores.append((product - prob * weighted).astype(LOW))
        beside = jnp.concatenate(grad_scores, axis=1)
        grad_packed[:, pl.ds(start, 128)] = dot_left(jnp.concatenate(grad_scores, axis=0), keys_two).astype(LOW)
        grad_packed[:, pl.ds(start + width, 128)] = (dot(beside, queries_two) * scale).astype(LOW)
        grad_packed[:, pl.ds(start + 2 * width, 128)] = dot(jnp.concatenate(probs, axis=1), grads_two).astype(LOW)

    @pl.loop(0, width // 256)
    def _(index):
        pair_of(index * 2)
        pair_of(index * 2 + 1)


def forward_kernel(cell, held, active, entry_h, gains, shifts, bias, w_qkv, w_out, w_up, w_down, *refs):
    sent_h = refs[held]
    out_h, lowered_h, packed_h, mixed_h, middle_h, second_h, active_h, slope_h = [
        ref.at[cell] for ref in refs[held + 1 : held + 9]
    ]
    (buffers, buffer_sems, save_sems, out_v, lowered_v, packed_v, mixed_v, middle_v) = refs[held + 9 : held + 17]
    (second_v, active_v, slope_v, hidden_v, total_v, entry, entry_sem) = refs[held + 17 :]
    width = entry.shape[1]
    ups = w_up.shape[1] // width

    @pl.when(active[0] != 0)
    def _():
        heads, outer, up, down = weight_blocks(w_qkv, w_out, w_up, w_down)
        order = heads + [outer]
        place_up, place_down = ({}, {})
        for number in range(ups + 1):
            if number < ups:
                place_up[number] = len(order)
                order.append(up[number])
            if number > 0:
                place_down[number - 1] = len(order)
                order.append(down[number - 1])
        fetched = pltpu.make_async_copy(entry_h, entry, entry_sem)
        fetched.start()
        saves = []

        def save(source, target):
            saves.append(pltpu.make_async_copy(source, target, save_sems.at[len(saves)]))
            saves[-1].start()

        fetched.wait()
        stream = Stream(order, buffers, buffer_sems)
        rows_in = entry[...].astype(F32)
        normed, _ = row_norm(rows_in)
        lowered_v[...] = (normed * gains[0:1, :] + shifts[0:1, :]).astype(LOW)
        save(lowered_v, lowered_h)
        for number in range(3):
            block = stream.take(number)
            window = pl.ds(number * width, width)
            part = dot(lowered_v[...], block[...])
            if number != 1:
                part = part + shifts[1 + number // 2 : 2 + number // 2, :]
            packed_v[:, window] = part.astype(LOW)
            stream.release()
        save(packed_v, packed_h)
        attend(packed_v, mixed_v, width)
        save(mixed_v, mixed_h)
        block = stream.take(3)
        middle = entry[...].astype(F32) + dot(mixed_v[...], block[...]) + shifts[3:4, :]
        middle_v[...] = middle
        stream.release()
        save(middle_v, middle_h)
        normed, _ = row_norm(middle_v[...])
        second_v[...] = (normed * gains[1:2, :] + shifts[4:5, :]).astype(LOW)
        save(second_v, second_h)
        for number in range(ups + 1):
            if number < ups:
                up_block = stream.take(place_up[number])
            if number > 0:
                down_block = stream.take(place_down[number - 1])
            if number < ups:
                hidden_v[number % 2] = dot(second_v[...], up_block[...]) + bias[0:1, pl.ds(number * width, width)]
            if number > 0:
                window = pl.ds((number - 1) * width, width)
                activated, slope = gelu_parts(hidden_v[(number - 1) % 2])
                active_v[:, window] = activated.astype(LOW)
                slope_v[:, window] = slope.astype(LOW)
                part = dot(active_v[:, window], down_block[...])
                if number == 1:
                    total_v[...] = part
                elif number < ups:
                    total_v[...] += part
                else:
                    out_v[...] = (middle_v[...] + (total_v[...] + part + shifts[5:6, :])).astype(LOW)
                save(active_v.at[:, window], active_h.at[:, window])
                save(slope_v.at[:, window], slope_h.at[:, window])
            if number < ups:
                stream.release()
            if number > 0:
                stream.release()
        save(out_v, sent_h)
        save(out_v, out_h)
        for copy in saves:
            copy.wait()


def forward_tick(active, entry, small, weights, kept, cell, cell_count):
    length, width = entry.shape
    deep = weights[2].shape[1]
    ups = deep // width
    shapes = [
        ((length, width), LOW),
        ((length, width), LOW),
        ((length, 3 * width), LOW),
        ((length, width), LOW),
        ((length, width), F32),
        ((length, width), LOW),
        ((length, deep), LOW),
        ((length, deep), LOW),
    ]
    outs = [jax.ShapeDtypeStruct(*shapes[0])] + [
        jax.ShapeDtypeStruct((cell_count,) + shape, kind) for shape, kind in shapes
    ]
    vmem, hbm = (pl.BlockSpec(memory_space=pltpu.VMEM), pl.BlockSpec(memory_space=pl.ANY))
    flops = 2 * length * width * (4 * width + 2 * deep) + 16 * length * length * width
    kept = () if kept is None else tuple(kept)
    held = len(kept)
    sent, *kept = pl.pallas_call(
        functools.partial(forward_kernel, cell, held),
        out_shape=outs,
        in_specs=[pl.BlockSpec(memory_space=pltpu.SMEM), hbm] + [vmem] * 3 + [hbm] * (4 + held),
        out_specs=[hbm] * 9,
        input_output_aliases={9 + number: 1 + number for number in range(held)},
        scratch_shapes=[
            pltpu.VMEM((4, width, width), LOW),
            pltpu.SemaphoreType.DMA((4,)),
            pltpu.SemaphoreType.DMA((7 + 2 * ups,)),
        ]
        + [pltpu.VMEM(*shape) for shape in shapes]
        + [
            pltpu.VMEM((2, length, width), F32),
            pltpu.VMEM((length, width), F32),
            pltpu.VMEM((length, width), LOW),
            pltpu.SemaphoreType.DMA,
        ],
        compiler_params=pltpu.CompilerParams(vmem_limit_bytes=60 * 2**20),
        cost_estimate=pl.CostEstimate(
            flops=flops, bytes_accessed=2 * width * (4 * width + 2 * deep), transcendentals=0
        ),
    )(active, entry, *small, *weights, *kept)
    return (sent, kept)


def backward_kernel(cell, held, active, scale, grad_h, entry_h, gains, shifts, *refs):
    packed, middle, slope = [ref.at[cell] for ref in refs[:3]]
    w_qkv, w_out, w_up, w_down = refs[3:7]
    refs = refs[7 + held :]
    sent_h = refs[0]
    rows_h, packed_h, branch_h, inner_h, low_h, sums_h = [ref.at[cell] for ref in refs[1:7]]
    (buffers, buffer_sems, load_sems, save_sems, rows_v, grad_packed_v, branch_v, inner_v, low_v, sums_v) = refs[7:17]
    (packed_v, middle_v, slope_v, mixed_v, grad_act_v, total_v, grad_middle_v, grad, entry) = refs[17:]
    length, width = entry.shape
    ups = w_up.shape[1] // width

    @pl.when(active[0] != 0)
    def _():
        heads, outer, up, down = weight_blocks(w_qkv, w_out, w_up, w_down)
        loads = [
            pltpu.make_async_copy(slope, slope_v, load_sems.at[0]),
            pltpu.make_async_copy(middle, middle_v, load_sems.at[1]),
            pltpu.make_async_copy(packed, packed_v, load_sems.at[2]),
            pltpu.make_async_copy(grad_h, grad, load_sems.at[3]),
            pltpu.make_async_copy(entry_h, entry, load_sems.at[4]),
        ]
        loads[3].start()
        order, place_up, place_down = ([], {}, {})
        for number in range(ups + 1):
            if number < ups:
                place_down[number] = len(order)
                order.append(down[number])
            if number > 0:
                place_up[number - 1] = len(order)
                order.append(up[number - 1])
        place_out = len(order)
        order = order + [outer] + heads
        saves = []

        def save(source, target):
            saves.append(pltpu.make_async_copy(source, target, save_sems.at[len(saves)]))
            saves[-1].start()

        def column_sum(array):
            return jnp.sum(array.astype(F32), axis=0, keepdims=True)

        loads[3].wait()
        stream = Stream(order, buffers, buffer_sems)
        loads[0].start()
        low_v[...] = (grad[...].astype(F32) * scale[0]).astype(LOW)
        save(low_v, low_h)
        sums_v[7:8, :] = column_sum(low_v[...])
        for number in range(ups + 1):
            if number == 1:
                loads[0].wait()
                loads[1].start()
            if number == 2:
                loads[2].start()
                loads[4].start()
            if number < ups:
                down_block = stream.take(place_down[number])
            if number > 0:
                up_block = stream.take(place_up[number - 1])
            if number < ups:
                grad_act_v[number % 2] = dot_right(low_v[...], down_block[...])
            if number > 0:
                window = pl.ds((number - 1) * width, width)
                inner = (grad_act_v[(number - 1) % 2] * slope_v[:, window].astype(F32)).astype(LOW)
                inner_v[:, window] = inner
                sums_v[7 + number : 8 + number, :] = column_sum(inner)
                part = dot_right(inner, up_block[...])
                if number == 1:
                    total_v[...] = part
                else:
                    total_v[...] += part
                save(inner_v.at[:, window], inner_h.at[:, window])
            if number < ups:
                stream.release()
            if number > 0:
                stream.release()
        loads[1].wait()
        normed, inverse = row_norm(middle_v[...])
        grad_second = total_v[...]
        sums_v[1:2, :] = column_sum(grad_second * normed)
        sums_v[6:7, :] = column_sum(grad_second)
        grad_middle = grad[...].astype(F32) * scale[0] + norm_back(grad_second * gains[1:2, :], normed, inverse)
        grad_middle_v[...] = grad_middle
        branch_v[...] = grad_middle.astype(LOW)
        sums_v[5:6, :] = column_sum(branch_v[...])
        save(branch_v, branch_h)
        block = stream.take(place_out)
        mixed_v[...] = dot_right(branch_v[...], block[...]).astype(LOW)
        stream.release()
        loads[2].wait()
        attend_back(packed_v, mixed_v, grad_packed_v, width)
        save(grad_packed_v, packed_h)
        sums_v[3:4, :] = column_sum(grad_packed_v[:, pl.ds(0, width)])
        sums_v[4:5, :] = column_sum(grad_packed_v[:, pl.ds(2 * width, width)])
        for number in range(3):
            block = stream.take(place_out + 1 + number)
            part = dot_right(grad_packed_v[:, pl.ds(number * width, width)], block[...])
            if number == 0:
                total_v[...] = part
            else:
                total_v[...] += part
            stream.release()
        loads[4].wait()
        normed, inverse = row_norm(entry[...].astype(F32))
        grad_lowered = total_v[...]
        sums_v[0:1, :] = column_sum(grad_lowered * normed)
        sums_v[2:3, :] = column_sum(grad_lowered)
        rows_v[...] = (grad_middle_v[...] + norm_back(grad_lowered * gains[0:1, :], normed, inverse)).astype(LOW)
        save(sums_v, sums_h)
        save(rows_v, sent_h)
        save(rows_v, rows_h)
        for copy in saves:
            copy.wait()


def backward_tick(active, incoming, entry, small, saved, weights, kept, cell, cell_count):
    length, width = entry.shape
    deep = weights[2].shape[1]
    ups = deep // width
    shapes = [
        ((length, width), LOW),
        ((length, 3 * width), LOW),
        ((length, width), LOW),
        ((length, deep), LOW),
        ((length, width), LOW),
        ((16, width), F32),
    ]
    outs = [jax.ShapeDtypeStruct(*shapes[0])] + [
        jax.ShapeDtypeStruct((cell_count,) + shape, kind) for shape, kind in shapes
    ]
    vmem, hbm = (pl.BlockSpec(memory_space=pltpu.VMEM), pl.BlockSpec(memory_space=pl.ANY))
    smem = pl.BlockSpec(memory_space=pltpu.SMEM)
    flops = 2 * length * width * (4 * width + 2 * deep) + 40 * length * length * width
    kept = () if kept is None else tuple(kept)
    held = len(kept)
    grad, scale = incoming
    sent, *kept = pl.pallas_call(
        functools.partial(backward_kernel, cell, held),
        out_shape=outs,
        in_specs=[smem] * 2 + [hbm] * 2 + [vmem] * 2 + [hbm] * (7 + held),
        out_specs=[hbm] * 7,
        input_output_aliases={13 + number: 1 + number for number in range(held)},
        scratch_shapes=[
            pltpu.VMEM((4, width, width), LOW),
            pltpu.SemaphoreType.DMA((4,)),
            pltpu.SemaphoreType.DMA((5,)),
            pltpu.SemaphoreType.DMA((6 + ups,)),
        ]
        + [pltpu.VMEM(*shape) for shape in shapes]
        + [
            pltpu.VMEM((length, 3 * width), LOW),
            pltpu.VMEM((length, width), F32),
            pltpu.VMEM((length, deep), LOW),
            pltpu.VMEM((length, width), LOW),
            pltpu.VMEM((2, length, width), F32),
            pltpu.VMEM((length, width), F32),
            pltpu.VMEM((length, width), F32),
            pltpu.VMEM((length, width), LOW),
            pltpu.VMEM((length, width), LOW),
        ],
        compiler_params=pltpu.CompilerParams(vmem_limit_bytes=60 * 2**20),
        cost_estimate=pl.CostEstimate(
            flops=flops, bytes_accessed=2 * width * (4 * width + 2 * deep), transcendentals=0
        ),
    )(active, scale, grad, entry, *small[:2], *saved, *weights, *kept)
    return (sent, kept)


def grads_kernel(chips, width, items, *refs):
    count = len(items)
    small_part, sides = (refs[0], refs[1:9])
    outs, parts = (refs[9:14], [small_part] + list(refs[14:18]))
    refs = refs[18:]
    landed, paired, mine = (refs[:count], refs[count : 2 * count], refs[2 * count : 3 * count])
    (big, cuts, stage, stage_down, final) = refs[3 * count : 3 * count + 5]
    (ring_send, ring_recv, pair_send, pair_recv, mine_sem, big_sem, cut_sem, stage_sem, final_sem) = refs[3 * count + 5 :]
    lowered, grad_packed, mixed, grad_branch, second, grad_inner, activated, grad_ff = sides
    splits = [way for _, _, _, way in items]
    half = chips // 2
    devices = 2 * chips
    own = width // devices
    deep_own = activated.shape[1] // devices
    cut = cuts.shape[2]
    me, core, position, right, left, sibling = ring_place(chips)

    def load_big(source, slot):
        return pltpu.make_async_copy(source, big.at[slot], big_sem.at[slot])

    def load_cut(source, index, slot):
        window = pl.ds(pl.multiple_of(index * cut, cut), cut)
        return pltpu.make_async_copy(source.at[:, window], cuts.at[slot], cut_sem.at[slot])

    load_big(grad_ff, 0).start()
    greet((left, right, sibling))

    def part(item, block):
        array, start, rows, _ = items[item]
        return parts[array].at[block, pl.ds(start, rows)]

    def first(item, way):
        return 1 if splits[item] == way else 2

    def slot_of(item, way, step):
        return step - 1 if splits[item] == way else half + step - 2

    def offset_of(step, way):
        return half - step + 1 if way == 0 else chips - (half - step + 1)

    def pair_copy(item, offset):
        block = ring_chip(position + offset, chips) * 2 + 1 - core
        return pltpu.make_async_remote_copy(
            src_ref=part(item, block),
            dst_ref=paired[item].at[offset],
            send_sem=pair_send.at[item, offset],
            recv_sem=pair_recv.at[item, offset],
            device_id={"dp": sibling},
            device_id_type=MESH,
        )

    def ring_copy(item, way, step):
        if step == first(item, way):
            source = paired[item].at[offset_of(step, way)]
        else:
            source = landed[item].at[slot_of(item, way, step - 1)]
        here = slot_of(item, way, step)
        return pltpu.make_async_remote_copy(
            src_ref=source,
            dst_ref=landed[item].at[here],
            send_sem=ring_send.at[item, here],
            recv_sem=ring_recv.at[item, here],
            device_id={"dp": right if way == 0 else left},
            device_id_type=MESH,
        )

    def load(item, offset, buffer):
        block = ring_chip(position + offset, chips) * 2 + core
        return pltpu.make_async_copy(part(item, block), mine[item].at[buffer], mine_sem.at[item, buffer])

    def starts(wanted):
        return [
            (step, item, way, offset_of(step, way))
            for step in (1, 2)
            for item in wanted
            for way in (0, 1)
            if step == first(item, way)
        ]

    downs = [item for item in range(count) if items[item][0] == 4]
    ups = [item for item in range(count) if items[item][0] == 3]
    others = [item for item in range(count) if items[item][0] < 3]
    every = downs + ups + others
    rest = [
        (step, item, way, offset_of(step, way))
        for step in range(2, half + 1)
        for item in every
        for way in (0, 1)
        if step > first(item, way)
    ] + [(half + 1, item, None, 0) for item in every]
    uses = [0] * count

    def numbered(plan):
        result = []
        for entry in plan:
            result.append(entry + (uses[entry[1]] % 2,))
            uses[entry[1]] += 1
        return result

    finals = [0]

    def fetch(entry):
        load(entry[1], entry[3], entry[4]).start()

    def work(entry):
        step, item, way, offset, buffer = entry
        array, start, rows, _ = items[item]
        load(item, offset, buffer).wait()
        pair_copy(item, offset).wait_recv()
        kind = parts[array].dtype
        columns = parts[array].shape[2]
        chunk = 16
        from_pair, from_mine, from_ring = (paired[item], mine[item], landed[item])
        if way is None:
            ring_copy(item, 0, half).wait_recv()
            ring_copy(item, 1, half).wait_recv()
            slot_a, slot_b = (slot_of(item, 0, half), slot_of(item, 1, half))
            if array == 0:
                outs[0][...] = (from_ring[slot_a] + from_ring[slot_b]) + (from_mine[buffer] + from_pair[offset])
                return
            high, wide = (min(rows, final.shape[1]), min(columns, final.shape[2]))
            for top in range(0, rows, high):
                for across in range(0, columns, wide):
                    number = finals[0]
                    finals[0] += 1
                    turn = number % final.shape[0]
                    if number >= final.shape[0]:
                        final_copies[number - final.shape[0]].wait()
                    span = pl.ds(across, wide)

                    @pl.loop(0, high // chunk)
                    def _(index):
                        here = pl.ds(pl.multiple_of(top + index * chunk, chunk), chunk)
                        final[turn, pl.ds(pl.multiple_of(index * chunk, chunk), chunk), pl.ds(0, wide)] = (
                            from_ring[slot_a, here, span].astype(F32) + from_ring[slot_b, here, span].astype(F32)
                        ) + (from_mine[buffer, here, span].astype(F32) + from_pair[offset, here, span].astype(F32))

                    final_copies.append(
                        pltpu.make_async_copy(
                            final.at[turn, pl.ds(0, high), pl.ds(0, wide)],
                            outs[array].at[pl.ds(start + top, high), span],
                            final_sem.at[turn],
                        )
                    )
                    final_copies[-1].start()
            return
        if step == first(item, way):

            @pl.loop(0, rows // chunk)
            def _(index):
                here = pl.ds(pl.multiple_of(index * chunk, chunk), chunk)
                from_pair[offset, here, :] = (
                    from_mine[buffer, here, :].astype(F32) + from_pair[offset, here, :].astype(F32)
                ).astype(kind)

        else:
            ring_copy(item, way, step - 1).wait_recv()
            arrived = slot_of(item, way, step - 1)

            @pl.loop(0, rows // chunk)
            def _(index):
                here = pl.ds(pl.multiple_of(index * chunk, chunk), chunk)
                from_ring[arrived, here, :] = (
                    from_ring[arrived, here, :].astype(F32)
                    + (from_mine[buffer, here, :].astype(F32) + from_pair[offset, here, :].astype(F32))
                ).astype(kind)

        sent.append(ring_copy(item, way, step))
        sent[-1].start()

    def run(plan):
        plan = numbered(plan)
        if plan:
            fetch(plan[0])
        for number, entry in enumerate(plan):
            if number + 1 < len(plan):
                fetch(plan[number + 1])
            work(entry)

    sent, final_copies = ([], [])
    def farthest_first(index):
        step = index // 2
        return ring_chip(position + jnp.where(lax.rem(index, 2) == 0, half - step, half + step + 1), chips)

    def keep_down(index):
        return pltpu.make_async_copy(
            stage_down.at[lax.rem(index, 2)],
            parts[4].at[pl.ds(farthest_first(index) * 2, 2)],
            stage_sem.at[lax.rem(index, 2)],
        )

    def cut_down(index):
        return load_cut(activated, farthest_first(index), lax.rem(index, 2))

    def down_products(low, high):
        @pl.loop(low, high)
        def _(index):
            slot = lax.rem(index, 2)

            @pl.when(index + 1 < chips)
            def _():
                cut_down(index + 1).start()

            cut_down(index).wait()

            @pl.when(index >= low + 2)
            def _():
                keep_down(index - 2).wait()

            product = dot_left(cuts[slot], big[0]).astype(LOW)
            for side in (0, 1):
                stage_down[slot, side] = product[side * deep_own : (side + 1) * deep_own]
            keep_down(index).start()

        for index in range(max(low, high - 2), high):
            keep_down(index).wait()

    def block(source, index, slot):
        window = pl.ds(pl.multiple_of(index * width, width), width)
        return pltpu.make_async_copy(source.at[:, window], big.at[slot], big_sem.at[slot])

    def keep(array, index):
        window = pl.ds(pl.multiple_of(index // 2 * width, width), width)
        return pltpu.make_async_copy(
            stage.at[lax.rem(index, 2)],
            parts[array].at[pl.ds(lax.rem(index, 2) * chips, chips), :, window],
            stage_sem.at[2 + lax.rem(index, 2)],
        )

    def open_products(left_side, right_side, slot):
        for index in (0, 1):
            load_cut(left_side, index, index).start()
        block(right_side, 0, slot).start()

    def products(array, left_side, right_side, shift, low, high):
        number = 2 * (right_side.shape[1] // width)
        if low == 0:
            for index in (0, 1):
                load_cut(left_side, index, index).wait()

        @pl.loop(low, high)
        def _(index):
            slot = lax.rem(index, 2)
            here = lax.rem(index // 2 + shift, 2)

            @pl.when(slot == 0)
            def _():
                block(right_side, index // 2, here).wait()

                @pl.when(index + 2 < number)
                def _():
                    block(right_side, index // 2 + 1, 1 - here).start()

            @pl.when(index >= low + 2)
            def _():
                keep(array, index - 2).wait()

            product = dot_left(cuts[slot], big[here]).astype(LOW)
            for device in range(chips):
                stage[slot, device] = product[device * own : (device + 1) * own]
            keep(array, index).start()

        for index in range(max(low, high - 2), high):
            keep(array, index).wait()

    def exchange(wanted, offsets):
        for offset in offsets:
            for item in wanted:
                pair_copy(item, offset).start()

    far = [half, half - 1, half + 1]
    near = [offset for offset in range(chips) if offset not in far]
    order = far + near

    def advance(wanted, steps):
        return [entry for entry in rest if entry[1] in wanted and entry[0] in steps]

    deep_blocks = grad_inner.shape[1] // width
    head_blocks = grad_packed.shape[1] // width
    cut_down(0).start()
    load_big(grad_ff, 0).wait()
    down_products(0, 3)
    exchange(downs, far)
    down_products(3, 5)
    run(starts(downs))
    down_products(5, chips)
    exchange(downs, near)
    open_products(second, grad_inner, 1)
    products(3, second, grad_inner, 1, 0, deep_blocks)
    run(advance(downs, (2,)))
    products(3, second, grad_inner, 1, deep_blocks, 2 * deep_blocks)
    exchange(ups, order)
    open_products(mixed, grad_branch, 1)
    run(advance(downs, (3,)))
    products(2, mixed, grad_branch, 1, 0, 2)
    open_products(lowered, grad_packed, 0)
    run(starts(ups))
    products(1, lowered, grad_packed, 0, 0, head_blocks)
    run(advance(ups, (2,)))
    products(1, lowered, grad_packed, 0, head_blocks, 2 * head_blocks)
    exchange(others, order)
    run(advance(ups, (3,)))
    run(starts(others))
    done = advance(downs, (2, 3)) + advance(ups, (2, 3))
    run([entry for entry in rest if entry not in done])
    for copy in sent:
        copy.wait_send()
    for item in every:
        for offset in range(chips):
            pair_copy(item, offset).wait_send()
    for copy in final_copies[-final.shape[0] :]:
        copy.wait()


def weight_grads(small_part, sides, items, shapes, count):
    chips = count // 2
    rows_in, width = sides[0].shape
    pieces = len(items)
    wholes = [small_part.shape[1:]] + list(shapes)
    held = [(rows,) + wholes[array][1:] for array, _, rows, _ in items]
    kinds = [F32 if array == 0 else LOW for array, _, _, _ in items]
    hbm = pl.BlockSpec(memory_space=pl.ANY)
    cut = width // 2
    flops = 2 * rows_in * sum(shape[0] * shape[1] for shape in shapes) * count
    outs = pl.pallas_call(
        functools.partial(grads_kernel, chips, width, items),
        out_shape=[jax.ShapeDtypeStruct(shape, F32) for shape in wholes]
        + [jax.ShapeDtypeStruct((count,) + tuple(shape), LOW) for shape in shapes],
        in_specs=[hbm] * 9,
        out_specs=[pl.BlockSpec(memory_space=pltpu.VMEM)] + [hbm] * 8,
        scratch_shapes=[pltpu.VMEM((chips - 1,) + shape, kind) for shape, kind in zip(held, kinds)]
        + [pltpu.VMEM((chips,) + shape, kind) for shape, kind in zip(held, kinds)]
        + [pltpu.VMEM((2,) + shape, kind) for shape, kind in zip(held, kinds)]
        + [
            pltpu.VMEM((2, rows_in, width), LOW),
            pltpu.VMEM((2, rows_in, cut), LOW),
            pltpu.VMEM((2, chips, width // count, width), LOW),
            pltpu.VMEM((2, 2, shapes[3][0], width), LOW),
            pltpu.VMEM((4, shapes[0][0], width), F32),
            pltpu.SemaphoreType.DMA((pieces, chips - 1)),
            pltpu.SemaphoreType.DMA((pieces, chips - 1)),
            pltpu.SemaphoreType.DMA((pieces, chips)),
            pltpu.SemaphoreType.DMA((pieces, chips)),
            pltpu.SemaphoreType.DMA((pieces, 2)),
            pltpu.SemaphoreType.DMA((2,)),
            pltpu.SemaphoreType.DMA((2,)),
            pltpu.SemaphoreType.DMA((4,)),
            pltpu.SemaphoreType.DMA((4,)),
        ],
        compiler_params=pltpu.CompilerParams(
            collective_id=2, has_side_effects=True, vmem_limit_bytes=62 * 2**20
        ),
        cost_estimate=pl.CostEstimate(flops=flops, bytes_accessed=8 * width * width * 12, transcendentals=0),
    )(small_part, *sides)
    return outs[:5]


def on_device(inputs, out_grad, query_counts, gains, shifts, w_qkv, w_out, w_up, b_up, w_down):
    stage = lax.axis_index("pipe")
    stages = lax.axis_size("pipe")
    count = lax.axis_size("dp")
    cell_count, length, width = inputs.shape
    own = width // count
    ups = b_up.shape[1] // own
    deep = ups * width
    deep_own = w_down.shape[1]
    shapes = [
        block_shape(own, 3 * width),
        block_shape(own, width),
        block_shape(own, deep),
        block_shape(deep_own, width),
    ]
    cut = (shapes[3][0] // 2 + 15) // 16 * 16
    items = (
        (0, 0, 16, 0),
        (1, 0, shapes[0][0], 0),
        (2, 0, shapes[1][0], 0),
        (3, 0, shapes[2][0], 1),
        (4, 0, cut, 0),
        (4, cut, shapes[3][0] - cut, 1),
    )
    shards = [small_pack(gains[0], shifts[0], b_up[0], 1)[0]] + [
        array[0].reshape(shape) for array, shape in zip((w_qkv, w_out, w_up, w_down), shapes)
    ]
    packs = gather(shards, items, count)
    gain_rows, shift_rows, bias = small_split(packs[0].astype(F32), ups)
    small = (gain_rows, shift_rows, bias[None])
    weights = (
        packs[1].reshape(width, 3 * width),
        packs[2].reshape(width, width),
        packs[3].reshape(width, deep),
        packs[4].reshape(deep, width),
    )
    scales = jnp.sqrt(query_counts.astype(F32) / 500.0)

    def along(value, steps):
        pairs = [(source, source + steps) for source in range(stages) if 0 <= source + steps < stages]
        return lax.ppermute(value, "pipe", pairs)

    entries, kept = ([[inputs[cell] for cell in range(cell_count)]], None)
    for turn in range(stages):
        active = (stage == turn).astype(jnp.int32)[None]
        arrived = []
        for cell in range(cell_count):
            sent, kept = forward_tick(active, entries[turn][cell], small, weights, kept, cell, cell_count)
            if turn + 1 < stages:
                arrived.append(along(sent, 1))
        entries.append(arrived)
    section_out, lowered, packed, mixed, middle, second, activated, slope = kept
    incoming = [(out_grad[cell], scales[cell][None]) for cell in range(cell_count)]
    back = None
    for turn in range(stages - 1, -1, -1):
        active = (stage == turn).astype(jnp.int32)[None]
        arrived = []
        for cell in range(cell_count):
            sent, back = backward_tick(
                active, incoming[cell], entries[turn][cell], small, (packed, middle, slope), weights, back, cell, cell_count
            )
            if turn > 0:
                arrived.append((along(sent, -1), jnp.ones((1,), F32)))
        incoming = arrived
    input_grads, grad_packed, grad_branch, grad_inner, grad_ff, sums = back
    sums = jnp.sum(sums, axis=0)

    small_part = small_pack(sums[0:2], sums[2:8], sums[8 : 8 + ups].reshape(deep), count)
    sides = [
        array.reshape(cell_count * length, -1)
        for array in (lowered, grad_packed, mixed, grad_branch, second, grad_inner, activated, grad_ff)
    ]
    if own % 16 == 0 and width % 256 == 0 and 4 * deep_own == width:
        shares = weight_grads(small_part, sides, items, shapes, count)
    else:
        products = [dot_left(sides[at], sides[at + 1]).astype(LOW) for at in (0, 2, 4, 6)]
        parts = [small_part] + [whole.reshape((count,) + shape) for whole, shape in zip(products, shapes)]
        shares = scatter(parts, items, count)
    grad_gains, grad_shifts, grad_bias = small_split(shares[0][None], ups)
    return (
        section_out[None],
        input_grads[None],
        grad_gains[None],
        grad_shifts[None],
        shares[1].reshape(1, own, 3 * width),
        shares[2].reshape(1, own, width),
        shares[3].reshape(1, own, deep),
        grad_bias[None],
        shares[4].reshape(1, deep_own, width),
    )


def solution(mesh):
    in_specs = (
        P("dp", None, None),
        P("dp", None, None),
        P("dp"),
        P("pipe", None, "dp"),
        P("pipe", None, "dp"),
        P("pipe", "dp", None),
        P("pipe", "dp", None),
        P("pipe", "dp", None),
        P("pipe", "dp"),
        P("pipe", "dp", None),
    )
    out_specs = (
        P("pipe", "dp", None, None),
        P("pipe", "dp", None, None),
        P("pipe", None, "dp"),
        P("pipe", None, "dp"),
        P("pipe", "dp", None),
        P("pipe", "dp", None),
        P("pipe", "dp", None),
        P("pipe", "dp"),
        P("pipe", "dp", None),
    )
    return jax.shard_map(
        on_device, mesh=mesh, in_specs=in_specs, out_specs=out_specs, check_vma=False
    )
```

```python
import functools
import math

import jax
import jax.numpy as jnp
from jax import lax
from jax.experimental import pallas as pl
from jax.experimental.pallas import tpu as pltpu
from jax.sharding import PartitionSpec as P

HEAD_DIM = 64
MESH = pl.DeviceIdType.MESH
LOW = jnp.bfloat16
F32 = jnp.float32


def ring_chip(position, chips):
    position = lax.rem(position + 2 * chips, chips)
    half = chips // 2
    return jnp.where(position < half, 2 * position, 2 * (chips - 1 - position) + 1)


def ring_place(chips):
    me = lax.axis_index("dp")
    core = lax.rem(me, 2)
    chip = me // 2
    position = jnp.where(lax.rem(chip, 2) == 0, chip // 2, chips - 1 - chip // 2)
    right = ring_chip(position + 1, chips) * 2 + core
    left = ring_chip(position - 1, chips) * 2 + core
    return (me, core, position, right, left, me + 1 - 2 * core)


def greet(devices):
    barrier = pltpu.get_barrier_semaphore()
    for device in devices:
        pl.semaphore_signal(barrier, inc=1, device_id={"dp": device}, device_id_type=MESH)
    pl.semaphore_wait(barrier, len(devices))


def gather_kernel(chips, arrays, items, *refs):
    count = len(items)
    ring_send, ring_recv, pair_send, pair_recv, own_sem = refs[2 * arrays :]
    shards = [refs[array].at[pl.ds(start, rows)] for array, start, rows, _ in items]
    splits = [way for _, _, _, way in items]
    half = chips // 2
    me, core, position, right, left, sibling = ring_place(chips)
    greet((left, right, sibling))

    def out(item, block):
        array, start, rows, _ = items[item]
        return refs[arrays + array].at[block, pl.ds(start, rows)]

    def owner(step, way):
        return ring_chip(position - step if way == 0 else position + step, chips) * 2 + core

    def travels(item, way, step):
        return step < half or (step == half and splits[item] == way)

    def ring_copy(item, way, step):
        block = owner(step - 1, way)
        return pltpu.make_async_remote_copy(
            src_ref=shards[item] if step == 1 else out(item, block),
            dst_ref=out(item, block),
            send_sem=ring_send.at[item, way, step - 1],
            recv_sem=ring_recv.at[item, way, step - 1],
            device_id={"dp": right if way == 0 else left},
            device_id_type=MESH,
        )

    def pair_copy(item, offset, block, source):
        return pltpu.make_async_remote_copy(
            src_ref=source,
            dst_ref=out(item, block),
            send_sem=pair_send.at[item, offset],
            recv_sem=pair_recv.at[item, offset],
            device_id={"dp": sibling},
            device_id_type=MESH,
        )

    sent, paired, kept = ([], [], [])
    for item in range(count):
        for way in (0, 1):
            if travels(item, way, 1):
                sent.append(ring_copy(item, way, 1))
                sent[-1].start()
    for item in range(count):
        paired.append(pair_copy(item, 0, me, shards[item]))
        paired[-1].start()
        kept.append(pltpu.make_async_copy(shards[item], out(item, me), own_sem.at[item]))
        kept[-1].start()
    for step in range(1, half + 1):
        for item in range(count):
            for way in (0, 1):
                if not travels(item, way, step):
                    continue
                ring_copy(item, way, step).wait_recv()
                if travels(item, way, step + 1):
                    sent.append(ring_copy(item, way, step + 1))
                    sent[-1].start()
                block = owner(step, way)
                offset = step if way == 0 else chips - step
                paired.append(pair_copy(item, offset, block, out(item, block)))
                paired[-1].start()
    for copy in sent:
        copy.wait_send()
    for copy in paired:
        copy.wait()
    for copy in kept:
        copy.wait()


def gather(shards, items, count):
    chips = count // 2
    arrays, pieces = (len(shards), len(items))
    return pl.pallas_call(
        functools.partial(gather_kernel, chips, arrays, items),
        out_shape=[jax.ShapeDtypeStruct((count,) + shard.shape, shard.dtype) for shard in shards],
        in_specs=[pl.BlockSpec(memory_space=pl.ANY)] * arrays,
        out_specs=[pl.BlockSpec(memory_space=pl.ANY)] * arrays,
        scratch_shapes=[
            pltpu.SemaphoreType.DMA((pieces, 2, chips // 2)),
            pltpu.SemaphoreType.DMA((pieces, 2, chips // 2)),
            pltpu.SemaphoreType.DMA((pieces, chips)),
            pltpu.SemaphoreType.DMA((pieces, chips)),
            pltpu.SemaphoreType.DMA((pieces,)),
        ],
        compiler_params=pltpu.CompilerParams(collective_id=0, has_side_effects=True),
    )(*shards)


def scatter_kernel(chips, arrays, items, *refs):
    count = len(items)
    parts, outs, refs = (refs[:arrays], refs[arrays : 2 * arrays], refs[2 * arrays :])
    landed, paired, mine = (refs[:count], refs[count : 2 * count], refs[2 * count : 3 * count])
    ring_send, ring_recv, pair_send, pair_recv, mine_sem = refs[3 * count :]
    splits = [way for _, _, _, way in items]
    half = chips // 2
    me, core, position, right, left, sibling = ring_place(chips)
    greet((left, right, sibling))

    def part(item, block):
        array, start, rows, _ = items[item]
        return parts[array].at[block, pl.ds(start, rows)]

    def first(item, way):
        return 1 if splits[item] == way else 2

    def slot(item, way, step):
        return step - 1 if splits[item] == way else half + step - 2

    def offset_of(step, way):
        return half - step + 1 if way == 0 else chips - (half - step + 1)

    def pair_copy(item, offset):
        block = ring_chip(position + offset, chips) * 2 + 1 - core
        return pltpu.make_async_remote_copy(
            src_ref=part(item, block),
            dst_ref=paired[item].at[offset],
            send_sem=pair_send.at[item, offset],
            recv_sem=pair_recv.at[item, offset],
            device_id={"dp": sibling},
            device_id_type=MESH,
        )

    def ring_copy(item, way, step):
        if step == first(item, way):
            source = paired[item].at[offset_of(step, way)]
        else:
            source = landed[item].at[slot(item, way, step - 1)]
        here = slot(item, way, step)
        return pltpu.make_async_remote_copy(
            src_ref=source,
            dst_ref=landed[item].at[here],
            send_sem=ring_send.at[item, here],
            recv_sem=ring_recv.at[item, here],
            device_id={"dp": right if way == 0 else left},
            device_id_type=MESH,
        )

    def load(item, offset, buffer):
        block = ring_chip(position + offset, chips) * 2 + core
        return pltpu.make_async_copy(part(item, block), mine[item].at[buffer], mine_sem.at[item, buffer])

    plan, uses = ([], [0] * count)
    for step in range(1, half + 2):
        for item in range(count):
            for way in (0, 1):
                if step <= half and step >= first(item, way):
                    plan.append((step, item, way, offset_of(step, way), uses[item] % 2))
                    uses[item] += 1
            if step > half:
                plan.append((step, item, None, 0, uses[item] % 2))
                uses[item] += 1
    for step, item, way, offset, buffer in plan:
        pair_copy(item, offset).start()
    load(plan[0][1], plan[0][3], plan[0][4]).start()
    sent = []
    for number, (step, item, way, offset, buffer) in enumerate(plan):
        if number + 1 < len(plan):
            load(plan[number + 1][1], plan[number + 1][3], plan[number + 1][4]).start()
        load(item, offset, buffer).wait()
        pair_copy(item, offset).wait_recv()
        array, start, rows, _ = items[item]
        kind = parts[array].dtype
        chunk = 16 if rows % 16 == 0 else rows
        from_pair, from_mine, from_ring = (paired[item], mine[item], landed[item])
        if way is None:
            ring_copy(item, 0, half).wait_recv()
            ring_copy(item, 1, half).wait_recv()
            slot_a, slot_b = (slot(item, 0, half), slot(item, 1, half))

            @pl.loop(0, rows // chunk)
            def _(index):
                here = pl.ds(pl.multiple_of(index * chunk, chunk), chunk)
                outs[array][pl.ds(pl.multiple_of(start + index * chunk, chunk), chunk), :] = (
                    from_ring[slot_a, here, :].astype(F32) + from_ring[slot_b, here, :].astype(F32)
                ) + (from_mine[buffer, here, :].astype(F32) + from_pair[offset, here, :].astype(F32))

            continue
        if step == first(item, way):

            @pl.loop(0, rows // chunk)
            def _(index):
                here = pl.ds(pl.multiple_of(index * chunk, chunk), chunk)
                from_pair[offset, here, :] = (
                    from_mine[buffer, here, :].astype(F32) + from_pair[offset, here, :].astype(F32)
                ).astype(kind)

        else:
            ring_copy(item, way, step - 1).wait_recv()
            arrived = slot(item, way, step - 1)

            @pl.loop(0, rows // chunk)
            def _(index):
                here = pl.ds(pl.multiple_of(index * chunk, chunk), chunk)
                from_ring[arrived, here, :] = (
                    from_ring[arrived, here, :].astype(F32)
                    + (from_mine[buffer, here, :].astype(F32) + from_pair[offset, here, :].astype(F32))
                ).astype(kind)

        sent.append(ring_copy(item, way, step))
        sent[-1].start()
    for copy in sent:
        copy.wait_send()
    for step, item, way, offset, buffer in plan:
        pair_copy(item, offset).wait_send()


def scatter(parts, items, count):
    chips = count // 2
    arrays, pieces = (len(parts), len(items))
    shapes = [(rows,) + parts[array].shape[2:] for array, _, rows, _ in items]
    kinds = [parts[array].dtype for array, _, _, _ in items]
    return pl.pallas_call(
        functools.partial(scatter_kernel, chips, arrays, items),
        out_shape=[jax.ShapeDtypeStruct(part.shape[1:], F32) for part in parts],
        in_specs=[pl.BlockSpec(memory_space=pl.ANY)] * arrays,
        out_specs=[pl.BlockSpec(memory_space=pltpu.VMEM)] * arrays,
        scratch_shapes=[pltpu.VMEM((chips - 1,) + shape, kind) for shape, kind in zip(shapes, kinds)]
        + [pltpu.VMEM((chips,) + shape, kind) for shape, kind in zip(shapes, kinds)]
        + [pltpu.VMEM((2,) + shape, kind) for shape, kind in zip(shapes, kinds)]
        + [
            pltpu.SemaphoreType.DMA((pieces, chips - 1)),
            pltpu.SemaphoreType.DMA((pieces, chips - 1)),
            pltpu.SemaphoreType.DMA((pieces, chips)),
            pltpu.SemaphoreType.DMA((pieces, chips)),
            pltpu.SemaphoreType.DMA((pieces, 2)),
        ],
        compiler_params=pltpu.CompilerParams(
            collective_id=1, has_side_effects=True, vmem_limit_bytes=62 * 2**20
        ),
    )(*parts)


def block_shape(rows, columns):
    return (rows, columns) if rows % 16 == 0 else (rows * columns // 128, 128)


def small_pack(gains, shifts, bias, count):
    width = gains.shape[1] // count
    ups = bias.shape[0] // gains.shape[1]
    rows = [
        gains.reshape(2, count, width).swapaxes(0, 1),
        shifts.reshape(6, count, width).swapaxes(0, 1),
        bias.reshape(count, ups, width),
    ]
    blank = jnp.zeros((count, 8 - ups, width), gains.dtype)
    return jnp.concatenate(rows + [blank], axis=1)


def small_split(blocks, ups):
    count, _, width = blocks.shape
    gains = blocks[:, 0:2].swapaxes(0, 1).reshape(2, count * width)
    shifts = blocks[:, 2:8].swapaxes(0, 1).reshape(6, count * width)
    bias = blocks[:, 8 : 8 + ups].reshape(count * ups * width)
    return (gains, shifts, bias)


def row_norm(rows_in):
    center = rows_in - jnp.mean(rows_in, axis=-1, keepdims=True)
    inverse = lax.rsqrt(jnp.mean(center * center, axis=-1, keepdims=True) + 1e-05)
    return (center * inverse, inverse)


def norm_back(grad_rows, normed, inverse):
    return inverse * (
        grad_rows
        - jnp.mean(grad_rows, axis=-1, keepdims=True)
        - normed * jnp.mean(grad_rows * normed, axis=-1, keepdims=True)
    )


def gelu_parts(hidden):
    cumulative = 0.5 * (1.0 + lax.erf(hidden * (1.0 / math.sqrt(2.0))))
    slope = cumulative + hidden * jnp.exp(-0.5 * hidden * hidden) * (1.0 / math.sqrt(2.0 * math.pi))
    return (hidden * cumulative, slope)


def dot(left, right):
    return lax.dot_general(left, right, (((1,), (0,)), ((), ())), preferred_element_type=F32)


def dot_right(left, right):
    return lax.dot_general(left, right, (((1,), (1,)), ((), ())), preferred_element_type=F32)


def dot_left(left, right):
    return lax.dot_general(left, right, (((0,), (0,)), ((), ())), preferred_element_type=F32)


class Stream:
    def __init__(self, blocks, buffers, sems):
        self.blocks, self.buffers, self.sems = (blocks, buffers, sems)
        self.depth = buffers.shape[0]
        self.started = 0
        for _ in range(min(self.depth, len(blocks))):
            self.start()

    def copy(self, number):
        slot = number % self.depth
        return pltpu.make_async_copy(self.blocks[number], self.buffers.at[slot], self.sems.at[slot])

    def start(self):
        self.copy(self.started).start()
        self.started += 1

    def take(self, number):
        self.copy(number).wait()
        return self.buffers.at[number % self.depth]

    def release(self):
        if self.started < len(self.blocks):
            self.start()


def weight_blocks(w_qkv, w_out, w_up, w_down):
    width = w_out.shape[0]
    def cut(ref, axis, number):
        window = pl.ds(number * width, width)
        return ref.at[:, window] if axis else ref.at[window, :]
    heads = [cut(w_qkv, 1, number) for number in range(3)]
    ups = [cut(w_up, 1, number) for number in range(w_up.shape[1] // width)]
    downs = [cut(w_down, 0, number) for number in range(w_down.shape[0] // width)]
    return (heads, w_out, ups, downs)


def head_masks(length):
    return lax.broadcasted_iota(jnp.int32, (length, 128), 1) < HEAD_DIM


def two_heads(array, side):
    blank = jnp.zeros_like(array)
    return jnp.concatenate([jnp.where(side, array, blank), jnp.where(side, blank, array)], axis=0)


def attend(packed, mixed, width, low=0, high=None):
    length = packed.shape[0]
    side = head_masks(length)

    def pair_of(pair):
        start = pair * 128 if isinstance(pair, int) else pl.multiple_of(pair * 128, 128)
        queries = packed[:, pl.ds(start, 128)] * jnp.asarray(1.0 / math.sqrt(HEAD_DIM), LOW)
        keys = two_heads(packed[:, pl.ds(start + width, 128)], side)
        values = two_heads(packed[:, pl.ds(start + 2 * width, 128)], side)
        scores = dot_right(queries, keys)
        probs, totals = ([], [])
        for head in (0, 1):
            mine = scores[:, head * length : (head + 1) * length]
            shifted = jnp.exp(mine - jnp.max(mine, axis=-1, keepdims=True))
            totals.append(1.0 / jnp.sum(shifted, axis=-1, keepdims=True))
            probs.append(shifted.astype(LOW))
        result = dot(jnp.concatenate(probs, axis=1), values)
        mixed[:, pl.ds(start, 128)] = (result * jnp.where(side, totals[0], totals[1])).astype(LOW)

    if high is not None:
        for pair in range(low, high):
            pair_of(pair)
        return

    @pl.loop(0, width // 256)
    def _(index):
        pair_of(index * 2)
        pair_of(index * 2 + 1)


def attend_back(packed, grad_mixed, grad_packed, width):
    length = packed.shape[0]
    side = head_masks(length)
    scale = 1.0 / math.sqrt(HEAD_DIM)

    def pair_of(pair):
        start = pl.multiple_of(pair * 128, 128)
        queries = packed[:, pl.ds(start, 128)]
        keys = packed[:, pl.ds(start + width, 128)] * jnp.asarray(scale, LOW)
        grads = grad_mixed[:, pl.ds(start, 128)]
        keys_two = two_heads(keys, side)
        queries_two = two_heads(queries, side)
        grads_two = two_heads(grads, side)
        scores = dot_right(keys, queries_two)
        grad_probs = dot_right(packed[:, pl.ds(start + 2 * width, 128)], grads_two)
        probs, grad_scores = ([], [])
        for head in (0, 1):
            mine = slice(head * length, (head + 1) * length)
            shifted = jnp.exp(scores[:, mine] - jnp.max(scores[:, mine], axis=0, keepdims=True))
            prob = shifted * (1.0 / jnp.sum(shifted, axis=0, keepdims=True))
            product = grad_probs[:, mine] * prob
            weighted = jnp.sum(product, axis=0, keepdims=True)
            probs.append(prob.astype(LOW))
            grad_scores.append((product - prob * weighted).astype(LOW))
        beside = jnp.concatenate(grad_scores, axis=1)
        grad_packed[:, pl.ds(start, 128)] = dot_left(jnp.concatenate(grad_scores, axis=0), keys_two).astype(LOW)
        grad_packed[:, pl.ds(start + width, 128)] = (dot(beside, queries_two) * scale).astype(LOW)
        grad_packed[:, pl.ds(start + 2 * width, 128)] = dot(jnp.concatenate(probs, axis=1), grads_two).astype(LOW)

    @pl.loop(0, width // 256)
    def _(index):
        pair_of(index * 2)
        pair_of(index * 2 + 1)


def forward_kernel(cell, held, active, entry_h, rows, w_qkv, w_out, w_up, w_down, *refs):
    sent_h = refs[held]
    out_h, lowered_h, packed_h, mixed_h, middle_h, second_h, active_h, slope_h = [
        ref.at[cell] for ref in refs[held + 1 : held + 9]
    ]
    (buffers, buffer_sems, save_sems, out_v, lowered_v, packed_v, mixed_v, middle_v) = refs[held + 9 : held + 17]
    (second_v, active_v, slope_v, hidden_v, total_v, entry, entry_sem) = refs[held + 17 :]
    width = entry.shape[1]
    gains, shifts, bias = (rows.at[0:2], rows.at[2:8], rows.at[8:16])
    ups = w_up.shape[1] // width

    @pl.when(active[0] != 0)
    def _():
        heads, outer, up, down = weight_blocks(w_qkv, w_out, w_up, w_down)
        order = heads + [outer]
        place_up, place_down = ({}, {})
        for number in range(ups + 1):
            if number < ups:
                place_up[number] = len(order)
                order.append(up[number])
            if number > 0:
                place_down[number - 1] = len(order)
                order.append(down[number - 1])
        fetched = pltpu.make_async_copy(entry_h, entry, entry_sem)
        fetched.start()
        saves = []

        def save(source, target):
            saves.append(pltpu.make_async_copy(source, target, save_sems.at[len(saves)]))
            saves[-1].start()

        fetched.wait()
        stream = Stream(order, buffers, buffer_sems)
        rows_in = entry[...].astype(F32)
        normed, _ = row_norm(rows_in)
        lowered_v[...] = (normed * gains[0:1, :] + shifts[0:1, :]).astype(LOW)
        save(lowered_v, lowered_h)
        for number in range(3):
            block = stream.take(number)
            window = pl.ds(number * width, width)
            part = dot(lowered_v[...], block[...])
            if number != 1:
                part = part + shifts[1 + number // 2 : 2 + number // 2, :]
            packed_v[:, window] = part.astype(LOW)
            stream.release()
        save(packed_v, packed_h)
        attend(packed_v, mixed_v, width)
        save(mixed_v, mixed_h)
        block = stream.take(3)
        middle = entry[...].astype(F32) + dot(mixed_v[...], block[...]) + shifts[3:4, :]
        middle_v[...] = middle
        stream.release()
        save(middle_v, middle_h)
        normed, _ = row_norm(middle_v[...])
        second_v[...] = (normed * gains[1:2, :] + shifts[4:5, :]).astype(LOW)
        save(second_v, second_h)
        for number in range(ups + 1):
            if number < ups:
                up_block = stream.take(place_up[number])
            if number > 0:
                down_block = stream.take(place_down[number - 1])
            if number < ups:
                hidden_v[number % 2] = dot(second_v[...], up_block[...]) + bias[number : number + 1, :]
            if number > 0:
                window = pl.ds((number - 1) * width, width)
                activated, slope = gelu_parts(hidden_v[(number - 1) % 2])
                active_v[:, window] = activated.astype(LOW)
                slope_v[:, window] = slope.astype(LOW)
                part = dot(active_v[:, window], down_block[...])
                if number == 1:
                    total_v[...] = part
                elif number < ups:
                    total_v[...] += part
                else:
                    out_v[...] = (middle_v[...] + (total_v[...] + part + shifts[5:6, :])).astype(LOW)
                save(active_v.at[:, window], active_h.at[:, window])
                save(slope_v.at[:, window], slope_h.at[:, window])
            if number < ups:
                stream.release()
            if number > 0:
                stream.release()
        save(out_v, sent_h)
        save(out_v, out_h)
        for copy in saves:
            copy.wait()


def kept_shapes(length, width, deep):
    return [
        ((length, width), LOW),
        ((length, width), LOW),
        ((length, 3 * width), LOW),
        ((length, width), LOW),
        ((length, width), F32),
        ((length, width), LOW),
        ((length, deep), LOW),
        ((length, deep), LOW),
    ]


def forward_tick(active, entry, rows, weights, kept, cell, cell_count):
    length, width = entry.shape
    deep = weights[2].shape[1]
    ups = deep // width
    shapes = kept_shapes(length, width, deep)
    outs = [jax.ShapeDtypeStruct(*shapes[0])] + [
        jax.ShapeDtypeStruct((cell_count,) + shape, kind) for shape, kind in shapes
    ]
    vmem, hbm = (pl.BlockSpec(memory_space=pltpu.VMEM), pl.BlockSpec(memory_space=pl.ANY))
    flops = 2 * length * width * (4 * width + 2 * deep) + 16 * length * length * width
    kept = () if kept is None else tuple(kept)
    held = len(kept)
    sent, *kept = pl.pallas_call(
        functools.partial(forward_kernel, cell, held),
        out_shape=outs,
        in_specs=[pl.BlockSpec(memory_space=pltpu.SMEM), hbm, vmem] + [hbm] * (4 + held),
        out_specs=[hbm] * 9,
        input_output_aliases={7 + number: 1 + number for number in range(held)},
        scratch_shapes=[
            pltpu.VMEM((4, width, width), LOW),
            pltpu.SemaphoreType.DMA((4,)),
            pltpu.SemaphoreType.DMA((7 + 2 * ups,)),
        ]
        + [pltpu.VMEM(*shape) for shape in shapes]
        + [
            pltpu.VMEM((2, length, width), F32),
            pltpu.VMEM((length, width), F32),
            pltpu.VMEM((length, width), LOW),
            pltpu.SemaphoreType.DMA,
        ],
        compiler_params=pltpu.CompilerParams(vmem_limit_bytes=60 * 2**20),
        cost_estimate=pl.CostEstimate(
            flops=flops, bytes_accessed=2 * width * (4 * width + 2 * deep), transcendentals=0
        ),
    )(active, entry, rows, *weights, *kept)
    return (sent, kept)


def backward_kernel(cell, held, active, scale, grad_h, entry_h, rows, *refs):
    packed, middle, slope = [ref.at[cell] for ref in refs[:3]]
    w_qkv, w_out, w_up, w_down = refs[3:7]
    refs = refs[7 + held :]
    sent_h = refs[0]
    rows_h, packed_h, branch_h, inner_h, low_h, sums_h = [ref.at[cell] for ref in refs[1:7]]
    (buffers, buffer_sems, load_sems, save_sems, rows_v, grad_packed_v, branch_v, inner_v, low_v, sums_v) = refs[7:17]
    (packed_v, middle_v, slope_v, mixed_v, grad_act_v, total_v, grad_middle_v, grad, entry) = refs[17:]
    gains = rows.at[0:2]
    length, width = entry.shape
    ups = w_up.shape[1] // width

    @pl.when(active[0] != 0)
    def _():
        heads, outer, up, down = weight_blocks(w_qkv, w_out, w_up, w_down)
        loads = [
            pltpu.make_async_copy(slope, slope_v, load_sems.at[0]),
            pltpu.make_async_copy(middle, middle_v, load_sems.at[1]),
            pltpu.make_async_copy(packed, packed_v, load_sems.at[2]),
            pltpu.make_async_copy(grad_h, grad, load_sems.at[3]),
            pltpu.make_async_copy(entry_h, entry, load_sems.at[4]),
        ]
        loads[3].start()
        order, place_up, place_down = ([], {}, {})
        for number in range(ups + 1):
            if number < ups:
                place_down[number] = len(order)
                order.append(down[number])
            if number > 0:
                place_up[number - 1] = len(order)
                order.append(up[number - 1])
        place_out = len(order)
        order = order + [outer] + heads
        saves = []

        def save(source, target):
            saves.append(pltpu.make_async_copy(source, target, save_sems.at[len(saves)]))
            saves[-1].start()

        def column_sum(array):
            return jnp.sum(array.astype(F32), axis=0, keepdims=True)

        loads[3].wait()
        stream = Stream(order, buffers, buffer_sems)
        loads[0].start()
        low_v[...] = (grad[...].astype(F32) * scale[0]).astype(LOW)
        save(low_v, low_h)
        sums_v[7:8, :] = column_sum(low_v[...])
        for number in range(ups + 1):
            if number == 1:
                loads[0].wait()
                loads[1].start()
            if number == 2:
                loads[2].start()
                loads[4].start()
            if number < ups:
                down_block = stream.take(place_down[number])
            if number > 0:
                up_block = stream.take(place_up[number - 1])
            if number < ups:
                grad_act_v[number % 2] = dot_right(low_v[...], down_block[...])
            if number > 0:
                window = pl.ds((number - 1) * width, width)
                inner = (grad_act_v[(number - 1) % 2] * slope_v[:, window].astype(F32)).astype(LOW)
                inner_v[:, window] = inner
                sums_v[7 + number : 8 + number, :] = column_sum(inner)
                part = dot_right(inner, up_block[...])
                if number == 1:
                    total_v[...] = part
                else:
                    total_v[...] += part
                save(inner_v.at[:, window], inner_h.at[:, window])
            if number < ups:
                stream.release()
            if number > 0:
                stream.release()
        loads[1].wait()
        normed, inverse = row_norm(middle_v[...])
        grad_second = total_v[...]
        sums_v[1:2, :] = column_sum(grad_second * normed)
        sums_v[6:7, :] = column_sum(grad_second)
        grad_middle = grad[...].astype(F32) * scale[0] + norm_back(grad_second * gains[1:2, :], normed, inverse)
        grad_middle_v[...] = grad_middle
        branch_v[...] = grad_middle.astype(LOW)
        sums_v[5:6, :] = column_sum(branch_v[...])
        save(branch_v, branch_h)
        block = stream.take(place_out)
        mixed_v[...] = dot_right(branch_v[...], block[...]).astype(LOW)
        stream.release()
        loads[2].wait()
        attend_back(packed_v, mixed_v, grad_packed_v, width)
        save(grad_packed_v, packed_h)
        sums_v[3:4, :] = column_sum(grad_packed_v[:, pl.ds(0, width)])
        sums_v[4:5, :] = column_sum(grad_packed_v[:, pl.ds(2 * width, width)])
        for number in range(3):
            block = stream.take(place_out + 1 + number)
            part = dot_right(grad_packed_v[:, pl.ds(number * width, width)], block[...])
            if number == 0:
                total_v[...] = part
            else:
                total_v[...] += part
            stream.release()
        loads[4].wait()
        normed, inverse = row_norm(entry[...].astype(F32))
        grad_lowered = total_v[...]
        sums_v[0:1, :] = column_sum(grad_lowered * normed)
        sums_v[2:3, :] = column_sum(grad_lowered)
        rows_v[...] = (grad_middle_v[...] + norm_back(grad_lowered * gains[0:1, :], normed, inverse)).astype(LOW)
        save(sums_v, sums_h)
        save(rows_v, sent_h)
        save(rows_v, rows_h)
        for copy in saves:
            copy.wait()


def backward_tick(active, incoming, entry, rows, saved, weights, kept, cell, cell_count):
    length, width = entry.shape
    deep = weights[2].shape[1]
    ups = deep // width
    shapes = [
        ((length, width), LOW),
        ((length, 3 * width), LOW),
        ((length, width), LOW),
        ((length, deep), LOW),
        ((length, width), LOW),
        ((16, width), F32),
    ]
    outs = [jax.ShapeDtypeStruct(*shapes[0])] + [
        jax.ShapeDtypeStruct((cell_count,) + shape, kind) for shape, kind in shapes
    ]
    vmem, hbm = (pl.BlockSpec(memory_space=pltpu.VMEM), pl.BlockSpec(memory_space=pl.ANY))
    smem = pl.BlockSpec(memory_space=pltpu.SMEM)
    flops = 2 * length * width * (4 * width + 2 * deep) + 40 * length * length * width
    kept = () if kept is None else tuple(kept)
    held = len(kept)
    grad, scale = incoming
    sent, *kept = pl.pallas_call(
        functools.partial(backward_kernel, cell, held),
        out_shape=outs,
        in_specs=[smem] * 2 + [hbm] * 2 + [vmem] + [hbm] * (7 + held),
        out_specs=[hbm] * 7,
        input_output_aliases={12 + number: 1 + number for number in range(held)},
        scratch_shapes=[
            pltpu.VMEM((4, width, width), LOW),
            pltpu.SemaphoreType.DMA((4,)),
            pltpu.SemaphoreType.DMA((5,)),
            pltpu.SemaphoreType.DMA((6 + ups,)),
        ]
        + [pltpu.VMEM(*shape) for shape in shapes]
        + [
            pltpu.VMEM((length, 3 * width), LOW),
            pltpu.VMEM((length, width), F32),
            pltpu.VMEM((length, deep), LOW),
            pltpu.VMEM((length, width), LOW),
            pltpu.VMEM((2, length, width), F32),
            pltpu.VMEM((length, width), F32),
            pltpu.VMEM((length, width), F32),
            pltpu.VMEM((length, width), LOW),
            pltpu.VMEM((length, width), LOW),
        ],
        compiler_params=pltpu.CompilerParams(vmem_limit_bytes=60 * 2**20),
        cost_estimate=pl.CostEstimate(
            flops=flops, bytes_accessed=2 * width * (4 * width + 2 * deep), transcendentals=0
        ),
    )(active, scale, grad, entry, rows, *saved, *weights, *kept)
    return (sent, kept)


def small_rows(small, rows, width, ups):
    devices, _, own = small.shape
    lane = lax.broadcasted_iota(jnp.int32, (own, width), 1)
    depth = lax.broadcasted_iota(jnp.int32, (own, width), 0)
    row = lax.broadcasted_iota(jnp.int32, (16, width), 0)
    across = lax.broadcasted_iota(jnp.int32, (16, width), 1)
    top = jnp.zeros((16, width), F32)
    for device in range(devices):
        spot = jnp.where(lane == depth + device * own, 1.0, 0.0).astype(LOW)
        top = top + dot(small[device], spot)
    rows[0:8, :] = top[0:8]
    share = devices // ups
    for block in range(ups):
        total = jnp.zeros((1, width), F32)
        for index in range(share):
            start = index * ups * own
            spot = jnp.zeros((own, width), F32)
            for up in range(ups):
                spot = spot + jnp.where(lane == depth + (start + up * own), 1.0, 0.0)
            low = start + (row - 8) * own
            inside = (row >= 8) & (row < 8 + ups) & (across >= low) & (across < low + own)
            placed = dot(small[block * share + index], spot.astype(LOW))
            total = total + jnp.sum(jnp.where(inside, placed, 0.0), axis=0, keepdims=True)
        rows[8 + block : 9 + block, :] = total


def gather_forward_kernel(chips, items, groups, cells, *refs):
    shards, inputs_h = (refs[:5], refs[5])
    outs, rows_h, arrived_h, later_h = (refs[6:11], refs[11], refs[12], refs[13])
    out_h, lowered_h, packed_h, mixed_h, middle_h, second_h, active_h, slope_h = refs[14:22]
    (ring_send, ring_recv, pair_send, pair_recv, own_sem, hop_send, hop_recv) = refs[22:29]
    (load_sem, save_sem, wide_sem, deep_sem) = refs[29:33]
    (small_v, rows_v, entry_v, out_v, lowered_v, packed_v, mixed_v, middle_v, second_v, active_v, slope_v) = refs[33:44]
    (total_v, hidden_v, wide_v, deep_v) = refs[44:]
    length, width = entry_v.shape[1:]
    ups = active_v.shape[2] // width
    half = chips // 2
    me, core, position, right, left, sibling = ring_place(chips)
    stage = lax.axis_index("pipe")
    first = stage == 0
    barrier = pltpu.get_barrier_semaphore()
    for device in (left, right, sibling):
        pl.semaphore_signal(barrier, inc=1, device_id={"dp": device}, device_id_type=MESH)
    pl.semaphore_signal(barrier, inc=1, device_id={"pipe": 1 - stage}, device_id_type=MESH)
    pl.semaphore_wait(barrier, 4)

    def shard(item):
        array, start, rows, _ = items[item]
        return shards[array].at[pl.ds(start, rows)]

    def out(item, block):
        array, start, rows, _ = items[item]
        return outs[array].at[block, pl.ds(start, rows)]

    def owner(step, way):
        return ring_chip(position - step if way == 0 else position + step, chips) * 2 + core

    def travels(item, way, step):
        return step < half or (step == half and items[item][3] == way)

    def ring_copy(item, way, step):
        block = owner(step - 1, way)
        return pltpu.make_async_remote_copy(
            src_ref=shard(item) if step == 1 else out(item, block),
            dst_ref=out(item, block),
            send_sem=ring_send.at[item, way, step - 1],
            recv_sem=ring_recv.at[item, way, step - 1],
            device_id={"dp": right if way == 0 else left},
            device_id_type=MESH,
        )

    def pair_copy(item, offset, block, source):
        return pltpu.make_async_remote_copy(
            src_ref=source,
            dst_ref=out(item, block),
            send_sem=pair_send.at[item, offset],
            recv_sem=pair_recv.at[item, offset],
            device_id={"dp": sibling},
            device_id_type=MESH,
        )

    def own_copy(item):
        return pltpu.make_async_copy(shard(item), out(item, me), own_sem.at[item])

    sent, paired = ([], [])

    def open_group(group):
        for item in group:
            for way in (0, 1):
                if travels(item, way, 1):
                    sent.append(ring_copy(item, way, 1))
                    sent[-1].start()
        for item in group:
            paired.append(pair_copy(item, 0, me, shard(item)))
            paired[-1].start()
            own_copy(item).start()

    def ring_step(item, way, step):
        ring_copy(item, way, step).wait_recv()
        if travels(item, way, step + 1):
            sent.append(ring_copy(item, way, step + 1))
            sent[-1].start()
        block = owner(step, way)
        offset = step if way == 0 else chips - step
        paired.append(pair_copy(item, offset, block, out(item, block)))
        paired[-1].start()

    def pair_arrived(item, offset):
        block = ring_chip(position - offset, chips) * 2 + core
        pair_copy(item, offset, block, out(item, block)).wait_recv()

    saves = []

    def save(source, target):
        number = len(saves)
        saves.append(lambda: pltpu.make_async_copy(source(), target(), save_sem.at[number]))
        saves[-1]().start()

    def entry_load(cell):
        return pltpu.make_async_copy(inputs_h.at[cell], entry_v.at[cell], load_sem.at[cell])

    def wide_load(array, column, slot):
        source = outs[array].at[:, :, pl.ds(column * width, width)]
        return pltpu.make_async_copy(source, wide_v.at[slot], wide_sem.at[slot])

    def wide(slot):
        return wide_v[slot].reshape(width, width)

    def gains(number):
        return rows_v[number : number + 1, :]

    def shifts(number):
        return rows_v[2 + number : 3 + number, :]

    def begin(cell):
        def step():
            entry_load(cell).wait()
            normed, _ = row_norm(entry_v[cell].astype(F32))
            lowered_v[cell] = (normed * gains(0) + shifts(0)).astype(LOW)
            save(lambda: lowered_v.at[cell], lambda: lowered_h.at[cell])

        return step

    def project(cell, number):
        def step():
            if cell == 0:
                wide_load(1, number, number).wait()
            part = dot(lowered_v[cell], wide(number))
            if number != 1:
                part = part + shifts(1 + number // 2)
            packed_v[cell, :, pl.ds(number * width, width)] = part.astype(LOW)
            if number == 2:
                save(lambda: packed_v.at[cell], lambda: packed_h.at[cell])

        return step

    def mix(cell, low, high, last):
        def step():
            attend(packed_v.at[cell], mixed_v.at[cell], width, low, high)
            if last:
                save(lambda: mixed_v.at[cell], lambda: mixed_h.at[cell])

        return step

    def join(cell):
        def step():
            if cell == 0:
                wide_load(2, 0, 3).wait()
            middle_v[cell] = entry_v[cell].astype(F32) + dot(mixed_v[cell], wide(3)) + shifts(3)
            save(lambda: middle_v.at[cell], lambda: middle_h.at[cell])

        return step

    def renorm(cell):
        def step():
            middle = middle_v[cell]
            normed, _ = row_norm(middle)
            second_v[cell] = (normed * gains(1) + shifts(4)).astype(LOW)
            total_v[cell] = middle + shifts(5)
            save(lambda: second_v.at[cell], lambda: second_h.at[cell])

        return step

    def rise(cell, number):
        def step():
            if cell == 0:
                wide_load(3, number, number).wait()
            hidden_v[...] = dot(second_v[cell], wide(number)) + rows_v[8 + number : 9 + number, :]

        return step

    def bend(cell, number):
        def step():
            window = pl.ds(number * width, width)
            activated, slope = gelu_parts(hidden_v[...])
            active_v[cell, :, window] = activated.astype(LOW)
            slope_v[cell, :, window] = slope.astype(LOW)
            if number == ups - 1:
                save(lambda: active_v.at[cell], lambda: active_h.at[cell])
                save(lambda: slope_v.at[cell], lambda: slope_h.at[cell])

        return step

    deep_rows = deep_v.shape[1] * deep_v.shape[2]

    def deep_load(offset, slot):
        chip = ring_chip(position - offset, chips)
        return pltpu.make_async_copy(outs[4].at[pl.ds(chip * 2, 2)], deep_v.at[slot], deep_sem.at[slot])

    def fall(cell, offset, slot):
        def step():
            if cell == 0:
                deep_load(offset, slot).wait()
            chip = ring_chip(position - offset, chips)
            window = pl.ds(pl.multiple_of(chip * deep_rows, 128), deep_rows)
            total_v[cell] += dot(active_v[cell, :, window], deep_v[slot].reshape(deep_rows, width))

        return step

    def hop():
        return pltpu.make_async_remote_copy(
            src_ref=out_v.at[0],
            dst_ref=arrived_h,
            send_sem=hop_send,
            recv_sem=hop_recv,
            device_id={"pipe": 1 - stage},
            device_id_type=MESH,
        )

    def finish(cell):
        def step():
            out_v[cell] = total_v[cell].astype(LOW)
            if cell == 0:
                hop().start()
            else:
                save(lambda: out_v.at[cell], lambda: later_h)
            save(lambda: out_v.at[cell], lambda: out_h.at[cell])

        return step

    def on_first(step):
        pl.when(first)(step)

    queue = []

    def ready(group, steps, loads):
        for item in group:
            own_copy(item).wait()
            for offset in range(chips):
                pair_arrived(item, offset)

        @pl.when(first)
        def _():
            for load in loads:
                load().start()

        queue.extend(steps)

    pairs = width // 128
    heads = []
    for cell in range(cells):
        heads.append(begin(cell))
        heads += [project(cell, number) for number in range(3)]
        heads += [mix(cell, low, low + 2, low + 2 >= pairs) for low in range(0, pairs, 2)]
    joins = [make(cell) for cell in range(cells) for make in (join, renorm)]
    def load_ups():
        for number in range(ups):
            wide_load(3, number, number).start()

    climbs = [load_ups]
    climbs += [make(cell, number) for number in range(ups) for cell in range(cells) for make in (rise, bend)]

    @pl.when(first)
    def _():
        for cell in range(cells):
            entry_load(cell).start()

    def lay_rows():
        copy = pltpu.make_async_copy(outs[0], small_v, load_sem.at[cells])
        copy.start()
        copy.wait()
        small_rows(small_v, rows_v, width, ups)
        pltpu.make_async_copy(rows_v, rows_h, load_sem.at[cells + 1]).start()

    def ready_small():
        for item in groups[0]:
            if items[item][0] == 0:
                own_copy(item).wait()
                for offset in range(chips):
                    pair_arrived(item, offset)
        lay_rows()

    plan = []
    for number, group in enumerate(groups):
        for step in range(1, half + 1):
            if step == half and number + 1 < len(groups):
                plan.append(("open", number + 1))
            for item in group:
                for way in (0, 1):
                    if travels(item, way, step):
                        plan.append(("ring", item, way, step))
            if number == len(groups) - 1:
                plan.append(("deep", step))
        plan.append(("done", number))
    open_group(groups[0])
    late = []
    slots = [0]

    def deep_ready(offsets):
        for offset in offsets:
            for item in groups[-1]:
                if offset == 0:
                    own_copy(item).wait()
                pair_arrived(item, offset)
            slot = slots[0] % deep_v.shape[0]
            slots[0] += 1

            def opening(offset=offset, slot=slot):
                deep_load(offset, slot).start()

            queue.append(opening)
            queue.extend(fall(cell, offset, slot) for cell in range(cells))

    def serve(limit):
        for _ in range(limit):
            if queue:
                on_first(queue.pop(0))

    for entry in plan:
        if entry[0] == "open":
            open_group(groups[entry[1]])
        elif entry[0] == "ring":
            ring_step(*entry[1:])
            for wait in list(late):
                wait[0] -= 1
                if wait[0] == 0:
                    wait[1]()
                    late.remove(wait)
            serve(3 if entry[1] in groups[-1] else 2)
        elif entry[0] == "done":
            if entry[1] == 0:
                rest = [item for item in groups[0] if items[item][0] != 0]
                late.append([1, ready_small])
                late.append(
                    [
                        2,
                        lambda: ready(
                            rest,
                            heads + joins,
                            [functools.partial(wide_load, 1, number, number) for number in range(3)]
                            + [functools.partial(wide_load, 2, 0, 3)],
                        ),
                    ]
                )
            elif entry[1] == 1:
                late.append([2, lambda: ready(groups[1], climbs, [])])
        elif entry[0] == "deep":
            step = entry[1]
            if step == 1:
                late.append([3, lambda: deep_ready([0])])
            if step < half:
                late.append([2, lambda step=step: deep_ready([step, chips - step])])
            else:
                for wait in late:
                    wait[1]()
                serve(len(queue))
                deep_ready([half])
    serve(len(queue))
    for cell in range(cells):
        on_first(finish(cell))
    for copy in sent:
        copy.wait_send()
    for copy in paired:
        copy.wait_send()
    pltpu.make_async_copy(rows_v, rows_h, load_sem.at[cells + 1]).wait()

    @pl.when(first)
    def _():
        for copy in saves:
            copy().wait()
        hop().wait_send()

    @pl.when(jnp.logical_not(first))
    def _():
        hop().wait_recv()


def gather_forward(shards, inputs, items, groups, count):
    chips = count // 2
    cells, length, width = inputs.shape
    deep = shards[3].shape[1]
    ups = deep // width
    pieces = len(items)
    shapes = kept_shapes(length, width, deep)
    hbm = pl.BlockSpec(memory_space=pl.ANY)
    flops = 2 * cells * length * width * (4 * width + 2 * deep)
    outs = pl.pallas_call(
        functools.partial(gather_forward_kernel, chips, items, groups, cells),
        out_shape=[jax.ShapeDtypeStruct((count,) + shard.shape, shard.dtype) for shard in shards]
        + [
            jax.ShapeDtypeStruct((16, width), F32),
            jax.ShapeDtypeStruct((length, width), LOW),
            jax.ShapeDtypeStruct((length, width), LOW),
        ]
        + [jax.ShapeDtypeStruct((cells,) + shape, kind) for shape, kind in shapes],
        in_specs=[hbm] * 6,
        out_specs=[hbm] * 16,
        scratch_shapes=[
            pltpu.SemaphoreType.DMA((pieces, 2, chips // 2)),
            pltpu.SemaphoreType.DMA((pieces, 2, chips // 2)),
            pltpu.SemaphoreType.DMA((pieces, chips)),
            pltpu.SemaphoreType.DMA((pieces, chips)),
            pltpu.SemaphoreType.DMA((pieces,)),
            pltpu.SemaphoreType.DMA,
            pltpu.SemaphoreType.DMA,
            pltpu.SemaphoreType.DMA((cells + 2,)),
            pltpu.SemaphoreType.DMA((9 * cells,)),
            pltpu.SemaphoreType.DMA((4,)),
            pltpu.SemaphoreType.DMA((2,)),
            pltpu.VMEM((count,) + shards[0].shape, LOW),
            pltpu.VMEM((16, width), F32),
            pltpu.VMEM((cells, length, width), LOW),
        ]
        + [pltpu.VMEM((cells,) + shape, kind) for shape, kind in shapes]
        + [
            pltpu.VMEM((cells, length, width), F32),
            pltpu.VMEM((length, width), F32),
            pltpu.VMEM((4, count, width // count, width), LOW),
            pltpu.VMEM((2, 2, shards[4].shape[0], width), LOW),
        ],
        compiler_params=pltpu.CompilerParams(
            collective_id=3, has_side_effects=True, vmem_limit_bytes=62 * 2**20
        ),
        cost_estimate=pl.CostEstimate(flops=flops, bytes_accessed=8 * width * (4 * width + 2 * deep), transcendentals=0),
    )(*shards, inputs)
    return (outs[:5], outs[5], outs[6], outs[7], list(outs[8:]))


def grads_kernel(chips, width, items, *refs):
    count = len(items)
    small_part, sides = (refs[0], refs[1:9])
    outs, parts = (refs[9:14], [small_part] + list(refs[14:18]))
    refs = refs[18:]
    landed, paired, mine = (refs[:count], refs[count : 2 * count], refs[2 * count : 3 * count])
    (big, cuts, stage, stage_down, final) = refs[3 * count : 3 * count + 5]
    (ring_send, ring_recv, pair_send, pair_recv, mine_sem, big_sem, cut_sem, stage_sem, final_sem) = refs[3 * count + 5 :]
    lowered, grad_packed, mixed, grad_branch, second, grad_inner, activated, grad_ff = sides
    splits = [way for _, _, _, way in items]
    half = chips // 2
    devices = 2 * chips
    own = width // devices
    deep_own = activated.shape[1] // devices
    cut = cuts.shape[2]
    me, core, position, right, left, sibling = ring_place(chips)

    def load_big(source, slot):
        return pltpu.make_async_copy(source, big.at[slot], big_sem.at[slot])

    def load_cut(source, index, slot):
        window = pl.ds(pl.multiple_of(index * cut, cut), cut)
        return pltpu.make_async_copy(source.at[:, window], cuts.at[slot], cut_sem.at[slot])

    load_big(grad_ff, 0).start()
    greet((left, right, sibling))

    def part(item, block):
        array, start, rows, _ = items[item]
        return parts[array].at[block, pl.ds(start, rows)]

    def first(item, way):
        return 1 if splits[item] == way else 2

    def slot_of(item, way, step):
        return step - 1 if splits[item] == way else half + step - 2

    def offset_of(step, way):
        return half - step + 1 if way == 0 else chips - (half - step + 1)

    def pair_copy(item, offset):
        block = ring_chip(position + offset, chips) * 2 + 1 - core
        return pltpu.make_async_remote_copy(
            src_ref=part(item, block),
            dst_ref=paired[item].at[offset],
            send_sem=pair_send.at[item, offset],
            recv_sem=pair_recv.at[item, offset],
            device_id={"dp": sibling},
            device_id_type=MESH,
        )

    def ring_copy(item, way, step):
        if step == first(item, way):
            source = paired[item].at[offset_of(step, way)]
        else:
            source = landed[item].at[slot_of(item, way, step - 1)]
        here = slot_of(item, way, step)
        return pltpu.make_async_remote_copy(
            src_ref=source,
            dst_ref=landed[item].at[here],
            send_sem=ring_send.at[item, here],
            recv_sem=ring_recv.at[item, here],
            device_id={"dp": right if way == 0 else left},
            device_id_type=MESH,
        )

    def load(item, offset, buffer):
        block = ring_chip(position + offset, chips) * 2 + core
        return pltpu.make_async_copy(part(item, block), mine[item].at[buffer], mine_sem.at[item, buffer])

    def starts(wanted):
        return [
            (step, item, way, offset_of(step, way))
            for step in (1, 2)
            for item in wanted
            for way in (0, 1)
            if step == first(item, way)
        ]

    downs = [item for item in range(count) if items[item][0] == 4]
    ups = [item for item in range(count) if items[item][0] == 3]
    others = [item for item in range(count) if items[item][0] < 3]
    every = downs + ups + others
    rest = [
        (step, item, way, offset_of(step, way))
        for step in range(2, half + 1)
        for item in every
        for way in (0, 1)
        if step > first(item, way)
    ] + [(half + 1, item, None, 0) for item in every]
    uses = [0] * count

    def numbered(plan):
        result = []
        for entry in plan:
            result.append(entry + (uses[entry[1]] % 2,))
            uses[entry[1]] += 1
        return result

    finals = [0]

    def fetch(entry):
        load(entry[1], entry[3], entry[4]).start()

    def work(entry):
        step, item, way, offset, buffer = entry
        array, start, rows, _ = items[item]
        load(item, offset, buffer).wait()
        pair_copy(item, offset).wait_recv()
        kind = parts[array].dtype
        columns = parts[array].shape[2]
        chunk = 16
        from_pair, from_mine, from_ring = (paired[item], mine[item], landed[item])
        if way is None:
            ring_copy(item, 0, half).wait_recv()
            ring_copy(item, 1, half).wait_recv()
            slot_a, slot_b = (slot_of(item, 0, half), slot_of(item, 1, half))
            if array == 0:
                outs[0][...] = (from_ring[slot_a] + from_ring[slot_b]) + (from_mine[buffer] + from_pair[offset])
                return
            high, wide = (min(rows, final.shape[1]), min(columns, final.shape[2]))
            for top in range(0, rows, high):
                for across in range(0, columns, wide):
                    number = finals[0]
                    finals[0] += 1
                    turn = number % final.shape[0]
                    if number >= final.shape[0]:
                        final_copies[number - final.shape[0]].wait()
                    span = pl.ds(across, wide)

                    @pl.loop(0, high // chunk)
                    def _(index):
                        here = pl.ds(pl.multiple_of(top + index * chunk, chunk), chunk)
                        final[turn, pl.ds(pl.multiple_of(index * chunk, chunk), chunk), pl.ds(0, wide)] = (
                            from_ring[slot_a, here, span].astype(F32) + from_ring[slot_b, here, span].astype(F32)
                        ) + (from_mine[buffer, here, span].astype(F32) + from_pair[offset, here, span].astype(F32))

                    final_copies.append(
                        pltpu.make_async_copy(
                            final.at[turn, pl.ds(0, high), pl.ds(0, wide)],
                            outs[array].at[pl.ds(start + top, high), span],
                            final_sem.at[turn],
                        )
                    )
                    final_copies[-1].start()
            return
        if step == first(item, way):

            @pl.loop(0, rows // chunk)
            def _(index):
                here = pl.ds(pl.multiple_of(index * chunk, chunk), chunk)
                from_pair[offset, here, :] = (
                    from_mine[buffer, here, :].astype(F32) + from_pair[offset, here, :].astype(F32)
                ).astype(kind)

        else:
            ring_copy(item, way, step - 1).wait_recv()
            arrived = slot_of(item, way, step - 1)

            @pl.loop(0, rows // chunk)
            def _(index):
                here = pl.ds(pl.multiple_of(index * chunk, chunk), chunk)
                from_ring[arrived, here, :] = (
                    from_ring[arrived, here, :].astype(F32)
                    + (from_mine[buffer, here, :].astype(F32) + from_pair[offset, here, :].astype(F32))
                ).astype(kind)

        sent.append(ring_copy(item, way, step))
        sent[-1].start()

    def run(plan):
        plan = numbered(plan)
        if plan:
            fetch(plan[0])
        for number, entry in enumerate(plan):
            if number + 1 < len(plan):
                fetch(plan[number + 1])
            work(entry)

    sent, final_copies = ([], [])
    def farthest_first(index):
        step = index // 2
        return ring_chip(position + jnp.where(lax.rem(index, 2) == 0, half - step, half + step + 1), chips)

    def keep_down(index):
        return pltpu.make_async_copy(
            stage_down.at[lax.rem(index, 2)],
            parts[4].at[pl.ds(farthest_first(index) * 2, 2)],
            stage_sem.at[lax.rem(index, 2)],
        )

    def cut_down(index):
        return load_cut(activated, farthest_first(index), lax.rem(index, 2))

    def down_products(low, high):
        @pl.loop(low, high)
        def _(index):
            slot = lax.rem(index, 2)

            @pl.when(index + 1 < chips)
            def _():
                cut_down(index + 1).start()

            cut_down(index).wait()

            @pl.when(index >= low + 2)
            def _():
                keep_down(index - 2).wait()

            product = dot_left(cuts[slot], big[0]).astype(LOW)
            for side in (0, 1):
                stage_down[slot, side] = product[side * deep_own : (side + 1) * deep_own]
            keep_down(index).start()

        for index in range(max(low, high - 2), high):
            keep_down(index).wait()

    def block(source, index, slot):
        window = pl.ds(pl.multiple_of(index * width, width), width)
        return pltpu.make_async_copy(source.at[:, window], big.at[slot], big_sem.at[slot])

    def keep(array, index):
        window = pl.ds(pl.multiple_of(index // 2 * width, width), width)
        return pltpu.make_async_copy(
            stage.at[lax.rem(index, 2)],
            parts[array].at[pl.ds(lax.rem(index, 2) * chips, chips), :, window],
            stage_sem.at[2 + lax.rem(index, 2)],
        )

    def open_products(left_side, right_side, slot):
        for index in (0, 1):
            load_cut(left_side, index, index).start()
        block(right_side, 0, slot).start()

    def products(array, left_side, right_side, shift, low, high):
        number = 2 * (right_side.shape[1] // width)
        if low == 0:
            for index in (0, 1):
                load_cut(left_side, index, index).wait()

        @pl.loop(low, high)
        def _(index):
            slot = lax.rem(index, 2)
            here = lax.rem(index // 2 + shift, 2)

            @pl.when(slot == 0)
            def _():
                block(right_side, index // 2, here).wait()

                @pl.when(index + 2 < number)
                def _():
                    block(right_side, index // 2 + 1, 1 - here).start()

            @pl.when(index >= low + 2)
            def _():
                keep(array, index - 2).wait()

            product = dot_left(cuts[slot], big[here]).astype(LOW)
            for device in range(chips):
                stage[slot, device] = product[device * own : (device + 1) * own]
            keep(array, index).start()

        for index in range(max(low, high - 2), high):
            keep(array, index).wait()

    def exchange(wanted, offsets):
        for offset in offsets:
            for item in wanted:
                pair_copy(item, offset).start()

    far = [half, half - 1, half + 1]
    near = [offset for offset in range(chips) if offset not in far]
    order = far + near

    def advance(wanted, steps):
        return [entry for entry in rest if entry[1] in wanted and entry[0] in steps]

    deep_blocks = grad_inner.shape[1] // width
    head_blocks = grad_packed.shape[1] // width
    cut_down(0).start()
    load_big(grad_ff, 0).wait()
    down_products(0, 3)
    exchange(downs, far)
    down_products(3, 5)
    run(starts(downs))
    down_products(5, chips)
    exchange(downs, near)
    open_products(second, grad_inner, 1)
    products(3, second, grad_inner, 1, 0, deep_blocks)
    run(advance(downs, (2,)))
    products(3, second, grad_inner, 1, deep_blocks, 2 * deep_blocks)
    exchange(ups, order)
    open_products(mixed, grad_branch, 1)
    run(advance(downs, (3,)))
    products(2, mixed, grad_branch, 1, 0, 2)
    open_products(lowered, grad_packed, 0)
    run(starts(ups))
    products(1, lowered, grad_packed, 0, 0, head_blocks)
    run(advance(ups, (2,)))
    products(1, lowered, grad_packed, 0, head_blocks, 2 * head_blocks)
    exchange(others, order)
    run(advance(ups, (3,)))
    run(starts(others))
    done = advance(downs, (2, 3)) + advance(ups, (2, 3))
    run([entry for entry in rest if entry not in done])
    for copy in sent:
        copy.wait_send()
    for item in every:
        for offset in range(chips):
            pair_copy(item, offset).wait_send()
    for copy in final_copies[-final.shape[0] :]:
        copy.wait()


def weight_grads(small_part, sides, items, shapes, count):
    chips = count // 2
    rows_in, width = sides[0].shape
    pieces = len(items)
    wholes = [small_part.shape[1:]] + list(shapes)
    held = [(rows,) + wholes[array][1:] for array, _, rows, _ in items]
    kinds = [F32 if array == 0 else LOW for array, _, _, _ in items]
    hbm = pl.BlockSpec(memory_space=pl.ANY)
    cut = width // 2
    flops = 2 * rows_in * sum(shape[0] * shape[1] for shape in shapes) * count
    outs = pl.pallas_call(
        functools.partial(grads_kernel, chips, width, items),
        out_shape=[jax.ShapeDtypeStruct(shape, F32) for shape in wholes]
        + [jax.ShapeDtypeStruct((count,) + tuple(shape), LOW) for shape in shapes],
        in_specs=[hbm] * 9,
        out_specs=[pl.BlockSpec(memory_space=pltpu.VMEM)] + [hbm] * 8,
        scratch_shapes=[pltpu.VMEM((chips - 1,) + shape, kind) for shape, kind in zip(held, kinds)]
        + [pltpu.VMEM((chips,) + shape, kind) for shape, kind in zip(held, kinds)]
        + [pltpu.VMEM((2,) + shape, kind) for shape, kind in zip(held, kinds)]
        + [
            pltpu.VMEM((2, rows_in, width), LOW),
            pltpu.VMEM((2, rows_in, cut), LOW),
            pltpu.VMEM((2, chips, width // count, width), LOW),
            pltpu.VMEM((2, 2, shapes[3][0], width), LOW),
            pltpu.VMEM((4, shapes[0][0], width), F32),
            pltpu.SemaphoreType.DMA((pieces, chips - 1)),
            pltpu.SemaphoreType.DMA((pieces, chips - 1)),
            pltpu.SemaphoreType.DMA((pieces, chips)),
            pltpu.SemaphoreType.DMA((pieces, chips)),
            pltpu.SemaphoreType.DMA((pieces, 2)),
            pltpu.SemaphoreType.DMA((2,)),
            pltpu.SemaphoreType.DMA((2,)),
            pltpu.SemaphoreType.DMA((4,)),
            pltpu.SemaphoreType.DMA((4,)),
        ],
        compiler_params=pltpu.CompilerParams(
            collective_id=2, has_side_effects=True, vmem_limit_bytes=62 * 2**20
        ),
        cost_estimate=pl.CostEstimate(flops=flops, bytes_accessed=8 * width * width * 12, transcendentals=0),
    )(small_part, *sides)
    return outs[:5]


def on_device(inputs, out_grad, query_counts, gains, shifts, w_qkv, w_out, w_up, b_up, w_down):
    stage = lax.axis_index("pipe")
    stages = lax.axis_size("pipe")
    count = lax.axis_size("dp")
    cell_count, length, width = inputs.shape
    own = width // count
    ups = b_up.shape[1] // own
    deep = ups * width
    deep_own = w_down.shape[1]
    shapes = [
        block_shape(own, 3 * width),
        block_shape(own, width),
        block_shape(own, deep),
        block_shape(deep_own, width),
    ]
    cut = (shapes[3][0] // 2 + 15) // 16 * 16
    items = (
        (0, 0, 16, 0),
        (1, 0, shapes[0][0], 0),
        (2, 0, shapes[1][0], 0),
        (3, 0, shapes[2][0], 1),
        (4, 0, cut, 0),
        (4, cut, shapes[3][0] - cut, 1),
    )
    shards = [small_pack(gains[0], shifts[0], b_up[0], 1)[0]] + [
        array[0].reshape(shape) for array, shape in zip((w_qkv, w_out, w_up, w_down), shapes)
    ]
    fused = stages == 2 and cell_count == 2 and own % 16 == 0 and width % 256 == 0 and 4 * deep_own == width
    if fused:
        piece = own // 2 // 16 * 16
        arrivals = (
            (0, 0, 16, 0),
            (1, 0, own - piece, 0),
            (1, own - piece, piece, 1),
            (2, 0, own, 1),
            (3, 0, own - piece, 0),
            (3, own - piece, piece, 1),
            (4, 0, cut, 0),
            (4, cut, deep_own - cut, 1),
        )
        packs, rows, arrived, later, kept = gather_forward(
            shards, inputs, arrivals, ((0, 1, 2, 3), (4, 5), (6, 7)), count
        )
    else:
        packs = gather(shards, items, count)
        gain_rows, shift_rows, bias = small_split(packs[0].astype(F32), ups)
        blank = jnp.zeros((8 - ups, width), F32)
        rows = jnp.concatenate([gain_rows, shift_rows, bias.reshape(ups, width), blank])
    weights = (
        packs[1].reshape(width, 3 * width),
        packs[2].reshape(width, width),
        packs[3].reshape(width, deep),
        packs[4].reshape(deep, width),
    )
    scales = jnp.sqrt(query_counts.astype(F32) / 500.0)

    def along(value, steps):
        pairs = [(source, source + steps) for source in range(stages) if 0 <= source + steps < stages]
        return lax.ppermute(value, "pipe", pairs)

    entries = [[inputs[cell] for cell in range(cell_count)]]
    if fused:
        entries.append([arrived] + [along(later, 1)])
    else:
        kept = None
    for turn in range(1 if fused else 0, stages):
        active = (stage == turn).astype(jnp.int32)[None]
        arrived = []
        for cell in range(cell_count):
            sent, kept = forward_tick(active, entries[turn][cell], rows, weights, kept, cell, cell_count)
            if turn + 1 < stages:
                arrived.append(along(sent, 1))
        entries.append(arrived)
    section_out, lowered, packed, mixed, middle, second, activated, slope = kept
    incoming = [(out_grad[cell], scales[cell][None]) for cell in range(cell_count)]
    back = None
    for turn in range(stages - 1, -1, -1):
        active = (stage == turn).astype(jnp.int32)[None]
        arrived = []
        for cell in range(cell_count):
            sent, back = backward_tick(
                active, incoming[cell], entries[turn][cell], rows, (packed, middle, slope), weights, back, cell, cell_count
            )
            if turn > 0:
                arrived.append((along(sent, -1), jnp.ones((1,), F32)))
        incoming = arrived
    input_grads, grad_packed, grad_branch, grad_inner, grad_ff, sums = back
    sums = jnp.sum(sums, axis=0)

    small_part = small_pack(sums[0:2], sums[2:8], sums[8 : 8 + ups].reshape(deep), count)
    sides = [
        array.reshape(cell_count * length, -1)
        for array in (lowered, grad_packed, mixed, grad_branch, second, grad_inner, activated, grad_ff)
    ]
    if fused:
        shares = weight_grads(small_part, sides, items, shapes, count)
    else:
        products = [dot_left(sides[at], sides[at + 1]).astype(LOW) for at in (0, 2, 4, 6)]
        parts = [small_part] + [whole.reshape((count,) + shape) for whole, shape in zip(products, shapes)]
        shares = scatter(parts, items, count)
    grad_gains, grad_shifts, grad_bias = small_split(shares[0][None], ups)
    return (
        section_out[None],
        input_grads[None],
        grad_gains[None],
        grad_shifts[None],
        shares[1].reshape(1, own, 3 * width),
        shares[2].reshape(1, own, width),
        shares[3].reshape(1, own, deep),
        grad_bias[None],
        shares[4].reshape(1, deep_own, width),
    )


def solution(mesh):
    in_specs = (
        P("dp", None, None),
        P("dp", None, None),
        P("dp"),
        P("pipe", None, "dp"),
        P("pipe", None, "dp"),
        P("pipe", "dp", None),
        P("pipe", "dp", None),
        P("pipe", "dp", None),
        P("pipe", "dp"),
        P("pipe", "dp", None),
    )
    out_specs = (
        P("pipe", "dp", None, None),
        P("pipe", "dp", None, None),
        P("pipe", None, "dp"),
        P("pipe", None, "dp"),
        P("pipe", "dp", None),
        P("pipe", "dp", None),
        P("pipe", "dp", None),
        P("pipe", "dp"),
        P("pipe", "dp", None),
    )
    return jax.shard_map(
        on_device, mesh=mesh, in_specs=in_specs, out_specs=out_specs, check_vma=False
    )
```

```python
import functools
import math

import jax
import jax.numpy as jnp
from jax import lax
from jax.experimental import pallas as pl
from jax.experimental.pallas import tpu as pltpu
from jax.sharding import PartitionSpec as P

HEAD_DIM = 64
MESH = pl.DeviceIdType.MESH
LOW = jnp.bfloat16
F32 = jnp.float32


def ring_chip(position, chips):
    position = lax.rem(position + 2 * chips, chips)
    half = chips // 2
    return jnp.where(position < half, 2 * position, 2 * (chips - 1 - position) + 1)


def ring_place(chips):
    me = lax.axis_index("dp")
    core = lax.rem(me, 2)
    chip = me // 2
    position = jnp.where(lax.rem(chip, 2) == 0, chip // 2, chips - 1 - chip // 2)
    right = ring_chip(position + 1, chips) * 2 + core
    left = ring_chip(position - 1, chips) * 2 + core
    return (me, core, position, right, left, me + 1 - 2 * core)


def greet(devices):
    barrier = pltpu.get_barrier_semaphore()
    for device in devices:
        pl.semaphore_signal(barrier, inc=1, device_id={"dp": device}, device_id_type=MESH)
    pl.semaphore_wait(barrier, len(devices))


def gather_kernel(chips, arrays, items, *refs):
    count = len(items)
    ring_send, ring_recv, pair_send, pair_recv, own_sem = refs[2 * arrays :]
    shards = [refs[array].at[pl.ds(start, rows)] for array, start, rows, _ in items]
    splits = [way for _, _, _, way in items]
    half = chips // 2
    me, core, position, right, left, sibling = ring_place(chips)
    greet((left, right, sibling))

    def out(item, block):
        array, start, rows, _ = items[item]
        return refs[arrays + array].at[block, pl.ds(start, rows)]

    def owner(step, way):
        return ring_chip(position - step if way == 0 else position + step, chips) * 2 + core

    def travels(item, way, step):
        return step < half or (step == half and splits[item] == way)

    def ring_copy(item, way, step):
        block = owner(step - 1, way)
        return pltpu.make_async_remote_copy(
            src_ref=shards[item] if step == 1 else out(item, block),
            dst_ref=out(item, block),
            send_sem=ring_send.at[item, way, step - 1],
            recv_sem=ring_recv.at[item, way, step - 1],
            device_id={"dp": right if way == 0 else left},
            device_id_type=MESH,
        )

    def pair_copy(item, offset, block, source):
        return pltpu.make_async_remote_copy(
            src_ref=source,
            dst_ref=out(item, block),
            send_sem=pair_send.at[item, offset],
            recv_sem=pair_recv.at[item, offset],
            device_id={"dp": sibling},
            device_id_type=MESH,
        )

    sent, paired, kept = ([], [], [])
    for item in range(count):
        for way in (0, 1):
            if travels(item, way, 1):
                sent.append(ring_copy(item, way, 1))
                sent[-1].start()
    for item in range(count):
        paired.append(pair_copy(item, 0, me, shards[item]))
        paired[-1].start()
        kept.append(pltpu.make_async_copy(shards[item], out(item, me), own_sem.at[item]))
        kept[-1].start()
    for step in range(1, half + 1):
        for item in range(count):
            for way in (0, 1):
                if not travels(item, way, step):
                    continue
                ring_copy(item, way, step).wait_recv()
                if travels(item, way, step + 1):
                    sent.append(ring_copy(item, way, step + 1))
                    sent[-1].start()
                block = owner(step, way)
                offset = step if way == 0 else chips - step
                paired.append(pair_copy(item, offset, block, out(item, block)))
                paired[-1].start()
    for copy in sent:
        copy.wait_send()
    for copy in paired:
        copy.wait()
    for copy in kept:
        copy.wait()


def gather(shards, items, count):
    chips = count // 2
    arrays, pieces = (len(shards), len(items))
    return pl.pallas_call(
        functools.partial(gather_kernel, chips, arrays, items),
        out_shape=[jax.ShapeDtypeStruct((count,) + shard.shape, shard.dtype) for shard in shards],
        in_specs=[pl.BlockSpec(memory_space=pl.ANY)] * arrays,
        out_specs=[pl.BlockSpec(memory_space=pl.ANY)] * arrays,
        scratch_shapes=[
            pltpu.SemaphoreType.DMA((pieces, 2, chips // 2)),
            pltpu.SemaphoreType.DMA((pieces, 2, chips // 2)),
            pltpu.SemaphoreType.DMA((pieces, chips)),
            pltpu.SemaphoreType.DMA((pieces, chips)),
            pltpu.SemaphoreType.DMA((pieces,)),
        ],
        compiler_params=pltpu.CompilerParams(collective_id=0, has_side_effects=True),
    )(*shards)


def scatter_kernel(chips, arrays, items, *refs):
    count = len(items)
    parts, outs, refs = (refs[:arrays], refs[arrays : 2 * arrays], refs[2 * arrays :])
    landed, paired, mine = (refs[:count], refs[count : 2 * count], refs[2 * count : 3 * count])
    ring_send, ring_recv, pair_send, pair_recv, mine_sem = refs[3 * count :]
    splits = [way for _, _, _, way in items]
    half = chips // 2
    me, core, position, right, left, sibling = ring_place(chips)
    greet((left, right, sibling))

    def part(item, block):
        array, start, rows, _ = items[item]
        return parts[array].at[block, pl.ds(start, rows)]

    def first(item, way):
        return 1 if splits[item] == way else 2

    def slot(item, way, step):
        return step - 1 if splits[item] == way else half + step - 2

    def offset_of(step, way):
        return half - step + 1 if way == 0 else chips - (half - step + 1)

    def pair_copy(item, offset):
        block = ring_chip(position + offset, chips) * 2 + 1 - core
        return pltpu.make_async_remote_copy(
            src_ref=part(item, block),
            dst_ref=paired[item].at[offset],
            send_sem=pair_send.at[item, offset],
            recv_sem=pair_recv.at[item, offset],
            device_id={"dp": sibling},
            device_id_type=MESH,
        )

    def ring_copy(item, way, step):
        if step == first(item, way):
            source = paired[item].at[offset_of(step, way)]
        else:
            source = landed[item].at[slot(item, way, step - 1)]
        here = slot(item, way, step)
        return pltpu.make_async_remote_copy(
            src_ref=source,
            dst_ref=landed[item].at[here],
            send_sem=ring_send.at[item, here],
            recv_sem=ring_recv.at[item, here],
            device_id={"dp": right if way == 0 else left},
            device_id_type=MESH,
        )

    def load(item, offset, buffer):
        block = ring_chip(position + offset, chips) * 2 + core
        return pltpu.make_async_copy(part(item, block), mine[item].at[buffer], mine_sem.at[item, buffer])

    plan, uses = ([], [0] * count)
    for step in range(1, half + 2):
        for item in range(count):
            for way in (0, 1):
                if step <= half and step >= first(item, way):
                    plan.append((step, item, way, offset_of(step, way), uses[item] % 2))
                    uses[item] += 1
            if step > half:
                plan.append((step, item, None, 0, uses[item] % 2))
                uses[item] += 1
    for step, item, way, offset, buffer in plan:
        pair_copy(item, offset).start()
    load(plan[0][1], plan[0][3], plan[0][4]).start()
    sent = []
    for number, (step, item, way, offset, buffer) in enumerate(plan):
        if number + 1 < len(plan):
            load(plan[number + 1][1], plan[number + 1][3], plan[number + 1][4]).start()
        load(item, offset, buffer).wait()
        pair_copy(item, offset).wait_recv()
        array, start, rows, _ = items[item]
        kind = parts[array].dtype
        chunk = 16 if rows % 16 == 0 else rows
        from_pair, from_mine, from_ring = (paired[item], mine[item], landed[item])
        if way is None:
            ring_copy(item, 0, half).wait_recv()
            ring_copy(item, 1, half).wait_recv()
            slot_a, slot_b = (slot(item, 0, half), slot(item, 1, half))

            @pl.loop(0, rows // chunk)
            def _(index):
                here = pl.ds(pl.multiple_of(index * chunk, chunk), chunk)
                outs[array][pl.ds(pl.multiple_of(start + index * chunk, chunk), chunk), :] = (
                    from_ring[slot_a, here, :].astype(F32) + from_ring[slot_b, here, :].astype(F32)
                ) + (from_mine[buffer, here, :].astype(F32) + from_pair[offset, here, :].astype(F32))

            continue
        if step == first(item, way):

            @pl.loop(0, rows // chunk)
            def _(index):
                here = pl.ds(pl.multiple_of(index * chunk, chunk), chunk)
                from_pair[offset, here, :] = (
                    from_mine[buffer, here, :].astype(F32) + from_pair[offset, here, :].astype(F32)
                ).astype(kind)

        else:
            ring_copy(item, way, step - 1).wait_recv()
            arrived = slot(item, way, step - 1)

            @pl.loop(0, rows // chunk)
            def _(index):
                here = pl.ds(pl.multiple_of(index * chunk, chunk), chunk)
                from_ring[arrived, here, :] = (
                    from_ring[arrived, here, :].astype(F32)
                    + (from_mine[buffer, here, :].astype(F32) + from_pair[offset, here, :].astype(F32))
                ).astype(kind)

        sent.append(ring_copy(item, way, step))
        sent[-1].start()
    for copy in sent:
        copy.wait_send()
    for step, item, way, offset, buffer in plan:
        pair_copy(item, offset).wait_send()


def scatter(parts, items, count):
    chips = count // 2
    arrays, pieces = (len(parts), len(items))
    shapes = [(rows,) + parts[array].shape[2:] for array, _, rows, _ in items]
    kinds = [parts[array].dtype for array, _, _, _ in items]
    return pl.pallas_call(
        functools.partial(scatter_kernel, chips, arrays, items),
        out_shape=[jax.ShapeDtypeStruct(part.shape[1:], F32) for part in parts],
        in_specs=[pl.BlockSpec(memory_space=pl.ANY)] * arrays,
        out_specs=[pl.BlockSpec(memory_space=pltpu.VMEM)] * arrays,
        scratch_shapes=[pltpu.VMEM((chips - 1,) + shape, kind) for shape, kind in zip(shapes, kinds)]
        + [pltpu.VMEM((chips,) + shape, kind) for shape, kind in zip(shapes, kinds)]
        + [pltpu.VMEM((2,) + shape, kind) for shape, kind in zip(shapes, kinds)]
        + [
            pltpu.SemaphoreType.DMA((pieces, chips - 1)),
            pltpu.SemaphoreType.DMA((pieces, chips - 1)),
            pltpu.SemaphoreType.DMA((pieces, chips)),
            pltpu.SemaphoreType.DMA((pieces, chips)),
            pltpu.SemaphoreType.DMA((pieces, 2)),
        ],
        compiler_params=pltpu.CompilerParams(
            collective_id=1, has_side_effects=True, vmem_limit_bytes=62 * 2**20
        ),
    )(*parts)


def block_shape(rows, columns):
    return (rows, columns) if rows % 16 == 0 else (rows * columns // 128, 128)


def small_pack(gains, shifts, bias, count):
    width = gains.shape[1] // count
    ups = bias.shape[0] // gains.shape[1]
    rows = [
        gains.reshape(2, count, width).swapaxes(0, 1),
        shifts.reshape(6, count, width).swapaxes(0, 1),
        bias.reshape(count, ups, width),
    ]
    blank = jnp.zeros((count, 8 - ups, width), gains.dtype)
    return jnp.concatenate(rows + [blank], axis=1)


def small_split(blocks, ups):
    count, _, width = blocks.shape
    gains = blocks[:, 0:2].swapaxes(0, 1).reshape(2, count * width)
    shifts = blocks[:, 2:8].swapaxes(0, 1).reshape(6, count * width)
    bias = blocks[:, 8 : 8 + ups].reshape(count * ups * width)
    return (gains, shifts, bias)


def row_norm(rows_in):
    center = rows_in - jnp.mean(rows_in, axis=-1, keepdims=True)
    inverse = lax.rsqrt(jnp.mean(center * center, axis=-1, keepdims=True) + 1e-05)
    return (center * inverse, inverse)


def norm_back(grad_rows, normed, inverse):
    return inverse * (
        grad_rows
        - jnp.mean(grad_rows, axis=-1, keepdims=True)
        - normed * jnp.mean(grad_rows * normed, axis=-1, keepdims=True)
    )


def gelu_parts(hidden):
    cumulative = 0.5 * (1.0 + lax.erf(hidden * (1.0 / math.sqrt(2.0))))
    slope = cumulative + hidden * jnp.exp(-0.5 * hidden * hidden) * (1.0 / math.sqrt(2.0 * math.pi))
    return (hidden * cumulative, slope)


def dot(left, right):
    return lax.dot_general(left, right, (((1,), (0,)), ((), ())), preferred_element_type=F32)


def dot_right(left, right):
    return lax.dot_general(left, right, (((1,), (1,)), ((), ())), preferred_element_type=F32)


def dot_left(left, right):
    return lax.dot_general(left, right, (((0,), (0,)), ((), ())), preferred_element_type=F32)


class Stream:
    def __init__(self, blocks, buffers, sems):
        self.blocks, self.buffers, self.sems = (blocks, buffers, sems)
        self.depth = buffers.shape[0]
        self.started = 0
        for _ in range(min(self.depth, len(blocks))):
            self.start()

    def copy(self, number):
        slot = number % self.depth
        return pltpu.make_async_copy(self.blocks[number], self.buffers.at[slot], self.sems.at[slot])

    def start(self):
        self.copy(self.started).start()
        self.started += 1

    def take(self, number):
        self.copy(number).wait()
        return self.buffers.at[number % self.depth]

    def release(self):
        if self.started < len(self.blocks):
            self.start()


def weight_blocks(w_qkv, w_out, w_up, w_down):
    width = w_out.shape[0]
    def cut(ref, axis, number):
        window = pl.ds(number * width, width)
        return ref.at[:, window] if axis else ref.at[window, :]
    heads = [cut(w_qkv, 1, number) for number in range(3)]
    ups = [cut(w_up, 1, number) for number in range(w_up.shape[1] // width)]
    downs = [cut(w_down, 0, number) for number in range(w_down.shape[0] // width)]
    return (heads, w_out, ups, downs)


def head_masks(length):
    return lax.broadcasted_iota(jnp.int32, (length, 128), 1) < HEAD_DIM


def two_heads(array, side):
    blank = jnp.zeros_like(array)
    return jnp.concatenate([jnp.where(side, array, blank), jnp.where(side, blank, array)], axis=0)


def attend(packed, mixed, width, low=0, high=None):
    length = packed.shape[0]
    side = head_masks(length)

    def pair_of(pair):
        start = pair * 128 if isinstance(pair, int) else pl.multiple_of(pair * 128, 128)
        queries = packed[:, pl.ds(start, 128)] * jnp.asarray(1.0 / math.sqrt(HEAD_DIM), LOW)
        keys = two_heads(packed[:, pl.ds(start + width, 128)], side)
        values = two_heads(packed[:, pl.ds(start + 2 * width, 128)], side)
        scores = dot_right(queries, keys)
        probs, totals = ([], [])
        for head in (0, 1):
            mine = scores[:, head * length : (head + 1) * length]
            shifted = jnp.exp(mine - jnp.max(mine, axis=-1, keepdims=True))
            totals.append(1.0 / jnp.sum(shifted, axis=-1, keepdims=True))
            probs.append(shifted.astype(LOW))
        result = dot(jnp.concatenate(probs, axis=1), values)
        mixed[:, pl.ds(start, 128)] = (result * jnp.where(side, totals[0], totals[1])).astype(LOW)

    if high is not None:
        for pair in range(low, high):
            pair_of(pair)
        return

    @pl.loop(0, width // 256)
    def _(index):
        pair_of(index * 2)
        pair_of(index * 2 + 1)


def attend_back(packed, grad_mixed, grad_packed, width, low=0, high=None):
    length = packed.shape[0]
    side = head_masks(length)
    scale = 1.0 / math.sqrt(HEAD_DIM)

    def pair_of(pair):
        start = pair * 128 if isinstance(pair, int) else pl.multiple_of(pair * 128, 128)
        queries = packed[:, pl.ds(start, 128)]
        keys = packed[:, pl.ds(start + width, 128)] * jnp.asarray(scale, LOW)
        grads = grad_mixed[:, pl.ds(start, 128)]
        keys_two = two_heads(keys, side)
        queries_two = two_heads(queries, side)
        grads_two = two_heads(grads, side)
        scores = dot_right(keys, queries_two)
        grad_probs = dot_right(packed[:, pl.ds(start + 2 * width, 128)], grads_two)
        probs, grad_scores = ([], [])
        for head in (0, 1):
            mine = slice(head * length, (head + 1) * length)
            shifted = jnp.exp(scores[:, mine] - jnp.max(scores[:, mine], axis=0, keepdims=True))
            prob = shifted * (1.0 / jnp.sum(shifted, axis=0, keepdims=True))
            product = grad_probs[:, mine] * prob
            weighted = jnp.sum(product, axis=0, keepdims=True)
            probs.append(prob.astype(LOW))
            grad_scores.append((product - prob * weighted).astype(LOW))
        beside = jnp.concatenate(grad_scores, axis=1)
        grad_packed[:, pl.ds(start, 128)] = dot_left(jnp.concatenate(grad_scores, axis=0), keys_two).astype(LOW)
        grad_packed[:, pl.ds(start + width, 128)] = (dot(beside, queries_two) * scale).astype(LOW)
        grad_packed[:, pl.ds(start + 2 * width, 128)] = dot(jnp.concatenate(probs, axis=1), grads_two).astype(LOW)

    if high is not None:
        for pair in range(low, high):
            pair_of(pair)
        return

    @pl.loop(0, width // 256)
    def _(index):
        pair_of(index * 2)
        pair_of(index * 2 + 1)


def forward_kernel(cell, held, active, entry_h, rows, w_qkv, w_out, w_up, w_down, *refs):
    sent_h = refs[held]
    out_h, lowered_h, packed_h, mixed_h, middle_h, second_h, active_h, slope_h = [
        ref.at[cell] for ref in refs[held + 1 : held + 9]
    ]
    (buffers, buffer_sems, save_sems, out_v, lowered_v, packed_v, mixed_v, middle_v) = refs[held + 9 : held + 17]
    (second_v, active_v, slope_v, hidden_v, total_v, entry, entry_sem) = refs[held + 17 :]
    width = entry.shape[1]
    gains, shifts, bias = (rows.at[0:2], rows.at[2:8], rows.at[8:16])
    ups = w_up.shape[1] // width

    @pl.when(active[0] != 0)
    def _():
        heads, outer, up, down = weight_blocks(w_qkv, w_out, w_up, w_down)
        order = heads + [outer]
        place_up, place_down = ({}, {})
        for number in range(ups + 1):
            if number < ups:
                place_up[number] = len(order)
                order.append(up[number])
            if number > 0:
                place_down[number - 1] = len(order)
                order.append(down[number - 1])
        fetched = pltpu.make_async_copy(entry_h, entry, entry_sem)
        fetched.start()
        saves = []

        def save(source, target):
            saves.append(pltpu.make_async_copy(source, target, save_sems.at[len(saves)]))
            saves[-1].start()

        fetched.wait()
        stream = Stream(order, buffers, buffer_sems)
        rows_in = entry[...].astype(F32)
        normed, _ = row_norm(rows_in)
        lowered_v[...] = (normed * gains[0:1, :] + shifts[0:1, :]).astype(LOW)
        save(lowered_v, lowered_h)
        for number in range(3):
            block = stream.take(number)
            window = pl.ds(number * width, width)
            part = dot(lowered_v[...], block[...])
            if number != 1:
                part = part + shifts[1 + number // 2 : 2 + number // 2, :]
            packed_v[:, window] = part.astype(LOW)
            stream.release()
        save(packed_v, packed_h)
        attend(packed_v, mixed_v, width)
        save(mixed_v, mixed_h)
        block = stream.take(3)
        middle = entry[...].astype(F32) + dot(mixed_v[...], block[...]) + shifts[3:4, :]
        middle_v[...] = middle
        stream.release()
        save(middle_v, middle_h)
        normed, _ = row_norm(middle_v[...])
        second_v[...] = (normed * gains[1:2, :] + shifts[4:5, :]).astype(LOW)
        save(second_v, second_h)
        for number in range(ups + 1):
            if number < ups:
                up_block = stream.take(place_up[number])
            if number > 0:
                down_block = stream.take(place_down[number - 1])
            if number < ups:
                hidden_v[number % 2] = dot(second_v[...], up_block[...]) + bias[number : number + 1, :]
            if number > 0:
                window = pl.ds((number - 1) * width, width)
                activated, slope = gelu_parts(hidden_v[(number - 1) % 2])
                active_v[:, window] = activated.astype(LOW)
                slope_v[:, window] = slope.astype(LOW)
                part = dot(active_v[:, window], down_block[...])
                if number == 1:
                    total_v[...] = part
                elif number < ups:
                    total_v[...] += part
                else:
                    out_v[...] = (middle_v[...] + (total_v[...] + part + shifts[5:6, :])).astype(LOW)
                save(active_v.at[:, window], active_h.at[:, window])
                save(slope_v.at[:, window], slope_h.at[:, window])
            if number < ups:
                stream.release()
            if number > 0:
                stream.release()
        save(out_v, sent_h)
        save(out_v, out_h)
        for copy in saves:
            copy.wait()


def kept_shapes(length, width, deep):
    return [
        ((length, width), LOW),
        ((length, width), LOW),
        ((length, 3 * width), LOW),
        ((length, width), LOW),
        ((length, width), F32),
        ((length, width), LOW),
        ((length, deep), LOW),
        ((length, deep), LOW),
    ]


def forward_tick(active, entry, rows, weights, kept, cell, cell_count):
    length, width = entry.shape
    deep = weights[2].shape[1]
    ups = deep // width
    shapes = kept_shapes(length, width, deep)
    outs = [jax.ShapeDtypeStruct(*shapes[0])] + [
        jax.ShapeDtypeStruct((cell_count,) + shape, kind) for shape, kind in shapes
    ]
    vmem, hbm = (pl.BlockSpec(memory_space=pltpu.VMEM), pl.BlockSpec(memory_space=pl.ANY))
    flops = 2 * length * width * (4 * width + 2 * deep) + 16 * length * length * width
    kept = () if kept is None else tuple(kept)
    held = len(kept)
    sent, *kept = pl.pallas_call(
        functools.partial(forward_kernel, cell, held),
        out_shape=outs,
        in_specs=[pl.BlockSpec(memory_space=pltpu.SMEM), hbm, vmem] + [hbm] * (4 + held),
        out_specs=[hbm] * 9,
        input_output_aliases={7 + number: 1 + number for number in range(held)},
        scratch_shapes=[
            pltpu.VMEM((4, width, width), LOW),
            pltpu.SemaphoreType.DMA((4,)),
            pltpu.SemaphoreType.DMA((7 + 2 * ups,)),
        ]
        + [pltpu.VMEM(*shape) for shape in shapes]
        + [
            pltpu.VMEM((2, length, width), F32),
            pltpu.VMEM((length, width), F32),
            pltpu.VMEM((length, width), LOW),
            pltpu.SemaphoreType.DMA,
        ],
        compiler_params=pltpu.CompilerParams(vmem_limit_bytes=60 * 2**20),
        cost_estimate=pl.CostEstimate(
            flops=flops, bytes_accessed=2 * width * (4 * width + 2 * deep), transcendentals=0
        ),
    )(active, entry, rows, *weights, *kept)
    return (sent, kept)


def backward_kernel(cell, held, active, scale, grad_h, entry_h, rows, *refs):
    packed, middle, slope = [ref.at[cell] for ref in refs[:3]]
    w_qkv, w_out, w_up, w_down = refs[3:7]
    refs = refs[7 + held :]
    sent_h = refs[0]
    rows_h, packed_h, branch_h, inner_h, low_h, sums_h = [ref.at[cell] for ref in refs[1:7]]
    (buffers, buffer_sems, load_sems, save_sems, rows_v, grad_packed_v, branch_v, inner_v, low_v, sums_v) = refs[7:17]
    (packed_v, middle_v, slope_v, mixed_v, grad_act_v, total_v, grad_middle_v, grad, entry) = refs[17:]
    gains = rows.at[0:2]
    length, width = entry.shape
    ups = w_up.shape[1] // width

    @pl.when(active[0] != 0)
    def _():
        heads, outer, up, down = weight_blocks(w_qkv, w_out, w_up, w_down)
        loads = [
            pltpu.make_async_copy(slope, slope_v, load_sems.at[0]),
            pltpu.make_async_copy(middle, middle_v, load_sems.at[1]),
            pltpu.make_async_copy(packed, packed_v, load_sems.at[2]),
            pltpu.make_async_copy(grad_h, grad, load_sems.at[3]),
            pltpu.make_async_copy(entry_h, entry, load_sems.at[4]),
        ]
        loads[3].start()
        order, place_up, place_down = ([], {}, {})
        for number in range(ups + 1):
            if number < ups:
                place_down[number] = len(order)
                order.append(down[number])
            if number > 0:
                place_up[number - 1] = len(order)
                order.append(up[number - 1])
        place_out = len(order)
        order = order + [outer] + heads
        saves = []

        def save(source, target):
            saves.append(pltpu.make_async_copy(source, target, save_sems.at[len(saves)]))
            saves[-1].start()

        def column_sum(array):
            return jnp.sum(array.astype(F32), axis=0, keepdims=True)

        loads[3].wait()
        stream = Stream(order, buffers, buffer_sems)
        loads[0].start()
        low_v[...] = (grad[...].astype(F32) * scale[0]).astype(LOW)
        save(low_v, low_h)
        sums_v[7:8, :] = column_sum(low_v[...])
        for number in range(ups + 1):
            if number == 1:
                loads[0].wait()
                loads[1].start()
            if number == 2:
                loads[2].start()
                loads[4].start()
            if number < ups:
                down_block = stream.take(place_down[number])
            if number > 0:
                up_block = stream.take(place_up[number - 1])
            if number < ups:
                grad_act_v[number % 2] = dot_right(low_v[...], down_block[...])
            if number > 0:
                window = pl.ds((number - 1) * width, width)
                inner = (grad_act_v[(number - 1) % 2] * slope_v[:, window].astype(F32)).astype(LOW)
                inner_v[:, window] = inner
                sums_v[7 + number : 8 + number, :] = column_sum(inner)
                part = dot_right(inner, up_block[...])
                if number == 1:
                    total_v[...] = part
                else:
                    total_v[...] += part
                save(inner_v.at[:, window], inner_h.at[:, window])
            if number < ups:
                stream.release()
            if number > 0:
                stream.release()
        loads[1].wait()
        normed, inverse = row_norm(middle_v[...])
        grad_second = total_v[...]
        sums_v[1:2, :] = column_sum(grad_second * normed)
        sums_v[6:7, :] = column_sum(grad_second)
        grad_middle = grad[...].astype(F32) * scale[0] + norm_back(grad_second * gains[1:2, :], normed, inverse)
        grad_middle_v[...] = grad_middle
        branch_v[...] = grad_middle.astype(LOW)
        sums_v[5:6, :] = column_sum(branch_v[...])
        save(branch_v, branch_h)
        block = stream.take(place_out)
        mixed_v[...] = dot_right(branch_v[...], block[...]).astype(LOW)
        stream.release()
        loads[2].wait()
        attend_back(packed_v, mixed_v, grad_packed_v, width)
        save(grad_packed_v, packed_h)
        sums_v[3:4, :] = column_sum(grad_packed_v[:, pl.ds(0, width)])
        sums_v[4:5, :] = column_sum(grad_packed_v[:, pl.ds(2 * width, width)])
        for number in range(3):
            block = stream.take(place_out + 1 + number)
            part = dot_right(grad_packed_v[:, pl.ds(number * width, width)], block[...])
            if number == 0:
                total_v[...] = part
            else:
                total_v[...] += part
            stream.release()
        loads[4].wait()
        normed, inverse = row_norm(entry[...].astype(F32))
        grad_lowered = total_v[...]
        sums_v[0:1, :] = column_sum(grad_lowered * normed)
        sums_v[2:3, :] = column_sum(grad_lowered)
        rows_v[...] = (grad_middle_v[...] + norm_back(grad_lowered * gains[0:1, :], normed, inverse)).astype(LOW)
        save(sums_v, sums_h)
        save(rows_v, sent_h)
        save(rows_v, rows_h)
        for copy in saves:
            copy.wait()


def backward_tick(active, incoming, entry, rows, saved, weights, kept, cell, cell_count):
    length, width = entry.shape
    deep = weights[2].shape[1]
    ups = deep // width
    shapes = [
        ((length, width), LOW),
        ((length, 3 * width), LOW),
        ((length, width), LOW),
        ((length, deep), LOW),
        ((length, width), LOW),
        ((16, width), F32),
    ]
    outs = [jax.ShapeDtypeStruct(*shapes[0])] + [
        jax.ShapeDtypeStruct((cell_count,) + shape, kind) for shape, kind in shapes
    ]
    vmem, hbm = (pl.BlockSpec(memory_space=pltpu.VMEM), pl.BlockSpec(memory_space=pl.ANY))
    smem = pl.BlockSpec(memory_space=pltpu.SMEM)
    flops = 2 * length * width * (4 * width + 2 * deep) + 40 * length * length * width
    kept = () if kept is None else tuple(kept)
    held = len(kept)
    grad, scale = incoming
    sent, *kept = pl.pallas_call(
        functools.partial(backward_kernel, cell, held),
        out_shape=outs,
        in_specs=[smem] * 2 + [hbm] * 2 + [vmem] + [hbm] * (7 + held),
        out_specs=[hbm] * 7,
        input_output_aliases={12 + number: 1 + number for number in range(held)},
        scratch_shapes=[
            pltpu.VMEM((4, width, width), LOW),
            pltpu.SemaphoreType.DMA((4,)),
            pltpu.SemaphoreType.DMA((5,)),
            pltpu.SemaphoreType.DMA((6 + ups,)),
        ]
        + [pltpu.VMEM(*shape) for shape in shapes]
        + [
            pltpu.VMEM((length, 3 * width), LOW),
            pltpu.VMEM((length, width), F32),
            pltpu.VMEM((length, deep), LOW),
            pltpu.VMEM((length, width), LOW),
            pltpu.VMEM((2, length, width), F32),
            pltpu.VMEM((length, width), F32),
            pltpu.VMEM((length, width), F32),
            pltpu.VMEM((length, width), LOW),
            pltpu.VMEM((length, width), LOW),
        ],
        compiler_params=pltpu.CompilerParams(vmem_limit_bytes=60 * 2**20),
        cost_estimate=pl.CostEstimate(
            flops=flops, bytes_accessed=2 * width * (4 * width + 2 * deep), transcendentals=0
        ),
    )(active, scale, grad, entry, rows, *saved, *weights, *kept)
    return (sent, kept)


def small_rows(small, rows, width, ups):
    devices, _, own = small.shape
    lane = lax.broadcasted_iota(jnp.int32, (own, width), 1)
    depth = lax.broadcasted_iota(jnp.int32, (own, width), 0)
    row = lax.broadcasted_iota(jnp.int32, (16, width), 0)
    across = lax.broadcasted_iota(jnp.int32, (16, width), 1)
    top = jnp.zeros((16, width), F32)
    for device in range(devices):
        spot = jnp.where(lane == depth + device * own, 1.0, 0.0).astype(LOW)
        top = top + dot(small[device], spot)
    rows[0:8, :] = top[0:8]
    share = devices // ups
    for block in range(ups):
        total = jnp.zeros((1, width), F32)
        for index in range(share):
            start = index * ups * own
            spot = jnp.zeros((own, width), F32)
            for up in range(ups):
                spot = spot + jnp.where(lane == depth + (start + up * own), 1.0, 0.0)
            low = start + (row - 8) * own
            inside = (row >= 8) & (row < 8 + ups) & (across >= low) & (across < low + own)
            placed = dot(small[block * share + index], spot.astype(LOW))
            total = total + jnp.sum(jnp.where(inside, placed, 0.0), axis=0, keepdims=True)
        rows[8 + block : 9 + block, :] = total


def gather_forward_kernel(chips, items, groups, cells, *refs):
    shards, inputs_h = (refs[:5], refs[5])
    outs, rows_h, arrived_h, later_h = (refs[6:11], refs[11], refs[12], refs[13])
    out_h, lowered_h, packed_h, mixed_h, middle_h, second_h, active_h, slope_h = refs[14:22]
    (ring_send, ring_recv, pair_send, pair_recv, own_sem, hop_send, hop_recv) = refs[22:29]
    (load_sem, save_sem, wide_sem, deep_sem) = refs[29:33]
    (small_v, rows_v, entry_v, out_v, lowered_v, packed_v, mixed_v, middle_v, second_v, active_v, slope_v) = refs[33:44]
    (total_v, hidden_v, wide_v, deep_v) = refs[44:]
    length, width = entry_v.shape[1:]
    ups = active_v.shape[2] // width
    half = chips // 2
    me, core, position, right, left, sibling = ring_place(chips)
    stage = lax.axis_index("pipe")
    first = stage == 0
    barrier = pltpu.get_barrier_semaphore()
    for device in (left, right, sibling):
        pl.semaphore_signal(barrier, inc=1, device_id={"dp": device}, device_id_type=MESH)
    pl.semaphore_signal(barrier, inc=1, device_id={"pipe": 1 - stage}, device_id_type=MESH)
    pl.semaphore_wait(barrier, 4)

    def shard(item):
        array, start, rows, _ = items[item]
        return shards[array].at[pl.ds(start, rows)]

    def out(item, block):
        array, start, rows, _ = items[item]
        return outs[array].at[block, pl.ds(start, rows)]

    def owner(step, way):
        return ring_chip(position - step if way == 0 else position + step, chips) * 2 + core

    def travels(item, way, step):
        return step < half or (step == half and items[item][3] == way)

    def ring_copy(item, way, step):
        block = owner(step - 1, way)
        return pltpu.make_async_remote_copy(
            src_ref=shard(item) if step == 1 else out(item, block),
            dst_ref=out(item, block),
            send_sem=ring_send.at[item, way, step - 1],
            recv_sem=ring_recv.at[item, way, step - 1],
            device_id={"dp": right if way == 0 else left},
            device_id_type=MESH,
        )

    def pair_copy(item, offset, block, source):
        return pltpu.make_async_remote_copy(
            src_ref=source,
            dst_ref=out(item, block),
            send_sem=pair_send.at[item, offset],
            recv_sem=pair_recv.at[item, offset],
            device_id={"dp": sibling},
            device_id_type=MESH,
        )

    def own_copy(item):
        return pltpu.make_async_copy(shard(item), out(item, me), own_sem.at[item])

    sent, paired = ([], [])

    def open_group(group):
        for item in group:
            for way in (0, 1):
                if travels(item, way, 1):
                    sent.append(ring_copy(item, way, 1))
                    sent[-1].start()
        for item in group:
            paired.append(pair_copy(item, 0, me, shard(item)))
            paired[-1].start()
            own_copy(item).start()

    def ring_step(item, way, step):
        ring_copy(item, way, step).wait_recv()
        if travels(item, way, step + 1):
            sent.append(ring_copy(item, way, step + 1))
            sent[-1].start()
        block = owner(step, way)
        offset = step if way == 0 else chips - step
        paired.append(pair_copy(item, offset, block, out(item, block)))
        paired[-1].start()

    def pair_arrived(item, offset):
        block = ring_chip(position - offset, chips) * 2 + core
        pair_copy(item, offset, block, out(item, block)).wait_recv()

    saves = []

    def save(source, target):
        number = len(saves)
        saves.append(lambda: pltpu.make_async_copy(source(), target(), save_sem.at[number]))
        saves[-1]().start()

    def entry_load(cell):
        return pltpu.make_async_copy(inputs_h.at[cell], entry_v.at[cell], load_sem.at[cell])

    def wide_load(array, column, slot):
        source = outs[array].at[:, :, pl.ds(column * width, width)]
        return pltpu.make_async_copy(source, wide_v.at[slot], wide_sem.at[slot])

    def wide(slot):
        return wide_v[slot].reshape(width, width)

    def gains(number):
        return rows_v[number : number + 1, :]

    def shifts(number):
        return rows_v[2 + number : 3 + number, :]

    def begin(cell):
        def step():
            entry_load(cell).wait()
            normed, _ = row_norm(entry_v[cell].astype(F32))
            lowered_v[cell] = (normed * gains(0) + shifts(0)).astype(LOW)
            save(lambda: lowered_v.at[cell], lambda: lowered_h.at[cell])

        return step

    def project(cell, number):
        def step():
            if cell == 0:
                wide_load(1, number, number).wait()
            part = dot(lowered_v[cell], wide(number))
            if number != 1:
                part = part + shifts(1 + number // 2)
            packed_v[cell, :, pl.ds(number * width, width)] = part.astype(LOW)
            if number == 2:
                save(lambda: packed_v.at[cell], lambda: packed_h.at[cell])

        return step

    def mix(cell, low, high, last):
        def step():
            attend(packed_v.at[cell], mixed_v.at[cell], width, low, high)
            if last:
                save(lambda: mixed_v.at[cell], lambda: mixed_h.at[cell])

        return step

    def join(cell):
        def step():
            if cell == 0:
                wide_load(2, 0, 3).wait()
            middle_v[cell] = entry_v[cell].astype(F32) + dot(mixed_v[cell], wide(3)) + shifts(3)
            save(lambda: middle_v.at[cell], lambda: middle_h.at[cell])

        return step

    def renorm(cell):
        def step():
            middle = middle_v[cell]
            normed, _ = row_norm(middle)
            second_v[cell] = (normed * gains(1) + shifts(4)).astype(LOW)
            total_v[cell] = middle + shifts(5)
            save(lambda: second_v.at[cell], lambda: second_h.at[cell])

        return step

    def rise(cell, number):
        def step():
            if cell == 0:
                wide_load(3, number, number).wait()
            hidden_v[...] = dot(second_v[cell], wide(number)) + rows_v[8 + number : 9 + number, :]

        return step

    def bend(cell, number):
        def step():
            window = pl.ds(number * width, width)
            activated, slope = gelu_parts(hidden_v[...])
            active_v[cell, :, window] = activated.astype(LOW)
            slope_v[cell, :, window] = slope.astype(LOW)
            if number == ups - 1:
                save(lambda: active_v.at[cell], lambda: active_h.at[cell])
                save(lambda: slope_v.at[cell], lambda: slope_h.at[cell])

        return step

    deep_rows = deep_v.shape[1] * deep_v.shape[2]

    def deep_load(offset, slot):
        chip = ring_chip(position - offset, chips)
        return pltpu.make_async_copy(outs[4].at[pl.ds(chip * 2, 2)], deep_v.at[slot], deep_sem.at[slot])

    def fall(cell, offset, slot):
        def step():
            if cell == 0:
                deep_load(offset, slot).wait()
            chip = ring_chip(position - offset, chips)
            window = pl.ds(pl.multiple_of(chip * deep_rows, 128), deep_rows)
            total_v[cell] += dot(active_v[cell, :, window], deep_v[slot].reshape(deep_rows, width))

        return step

    def hop():
        return pltpu.make_async_remote_copy(
            src_ref=out_v.at[0],
            dst_ref=arrived_h,
            send_sem=hop_send,
            recv_sem=hop_recv,
            device_id={"pipe": 1 - stage},
            device_id_type=MESH,
        )

    def finish(cell):
        def step():
            out_v[cell] = total_v[cell].astype(LOW)
            if cell == 0:
                hop().start()
            else:
                save(lambda: out_v.at[cell], lambda: later_h)
            save(lambda: out_v.at[cell], lambda: out_h.at[cell])

        return step

    def on_first(step):
        pl.when(first)(step)

    queue = []

    def ready(group, steps, loads):
        for item in group:
            own_copy(item).wait()
            for offset in range(chips):
                pair_arrived(item, offset)

        @pl.when(first)
        def _():
            for load in loads:
                load().start()

        queue.extend(steps)

    pairs = width // 128
    heads = []
    for cell in range(cells):
        heads.append(begin(cell))
        heads += [project(cell, number) for number in range(3)]
        heads += [mix(cell, low, low + 2, low + 2 >= pairs) for low in range(0, pairs, 2)]
    joins = [make(cell) for cell in range(cells) for make in (join, renorm)]
    def load_ups():
        for number in range(ups):
            wide_load(3, number, number).start()

    climbs = [load_ups]
    climbs += [make(cell, number) for number in range(ups) for cell in range(cells) for make in (rise, bend)]

    @pl.when(first)
    def _():
        for cell in range(cells):
            entry_load(cell).start()

    def lay_rows():
        copy = pltpu.make_async_copy(outs[0], small_v, load_sem.at[cells])
        copy.start()
        copy.wait()
        small_rows(small_v, rows_v, width, ups)
        pltpu.make_async_copy(rows_v, rows_h, load_sem.at[cells + 1]).start()

    def ready_small():
        for item in groups[0]:
            if items[item][0] == 0:
                own_copy(item).wait()
                for offset in range(chips):
                    pair_arrived(item, offset)
        lay_rows()

    plan = []
    for number, group in enumerate(groups):
        for step in range(1, half + 1):
            if step == half and number + 1 < len(groups):
                plan.append(("open", number + 1))
            for item in group:
                for way in (0, 1):
                    if travels(item, way, step):
                        plan.append(("ring", item, way, step))
            if number == len(groups) - 1:
                plan.append(("deep", step))
        plan.append(("done", number))
    open_group(groups[0])
    late = []
    slots = [0]

    def deep_ready(offsets):
        for offset in offsets:
            for item in groups[-1]:
                if offset == 0:
                    own_copy(item).wait()
                pair_arrived(item, offset)
            slot = slots[0] % deep_v.shape[0]
            slots[0] += 1

            def opening(offset=offset, slot=slot):
                deep_load(offset, slot).start()

            queue.append(opening)
            queue.extend(fall(cell, offset, slot) for cell in range(cells))

    def serve(limit):
        for _ in range(limit):
            if queue:
                on_first(queue.pop(0))

    for entry in plan:
        if entry[0] == "open":
            open_group(groups[entry[1]])
        elif entry[0] == "ring":
            ring_step(*entry[1:])
            for wait in list(late):
                wait[0] -= 1
                if wait[0] == 0:
                    wait[1]()
                    late.remove(wait)
            serve(3 if entry[1] in groups[-1] else 2)
        elif entry[0] == "done":
            if entry[1] == 0:
                rest = [item for item in groups[0] if items[item][0] != 0]
                late.append([1, ready_small])
                late.append(
                    [
                        2,
                        lambda: ready(
                            rest,
                            heads + joins,
                            [functools.partial(wide_load, 1, number, number) for number in range(3)]
                            + [functools.partial(wide_load, 2, 0, 3)],
                        ),
                    ]
                )
            elif entry[1] == 1:
                late.append([2, lambda: ready(groups[1], climbs, [])])
        elif entry[0] == "deep":
            step = entry[1]
            if step == 1:
                late.append([3, lambda: deep_ready([0])])
            if step < half:
                late.append([2, lambda step=step: deep_ready([step, chips - step])])
            else:
                for wait in late:
                    wait[1]()
                serve(len(queue))
                deep_ready([half])
    serve(len(queue))
    for cell in range(cells):
        on_first(finish(cell))
    for copy in sent:
        copy.wait_send()
    for copy in paired:
        copy.wait_send()
    pltpu.make_async_copy(rows_v, rows_h, load_sem.at[cells + 1]).wait()

    @pl.when(first)
    def _():
        for copy in saves:
            copy().wait()
        hop().wait_send()

    @pl.when(jnp.logical_not(first))
    def _():
        hop().wait_recv()


def gather_forward(shards, inputs, items, groups, count):
    chips = count // 2
    cells, length, width = inputs.shape
    deep = shards[3].shape[1]
    ups = deep // width
    pieces = len(items)
    shapes = kept_shapes(length, width, deep)
    hbm = pl.BlockSpec(memory_space=pl.ANY)
    flops = 2 * cells * length * width * (4 * width + 2 * deep)
    outs = pl.pallas_call(
        functools.partial(gather_forward_kernel, chips, items, groups, cells),
        out_shape=[jax.ShapeDtypeStruct((count,) + shard.shape, shard.dtype) for shard in shards]
        + [
            jax.ShapeDtypeStruct((16, width), F32),
            jax.ShapeDtypeStruct((length, width), LOW),
            jax.ShapeDtypeStruct((length, width), LOW),
        ]
        + [jax.ShapeDtypeStruct((cells,) + shape, kind) for shape, kind in shapes],
        in_specs=[hbm] * 6,
        out_specs=[hbm] * 16,
        scratch_shapes=[
            pltpu.SemaphoreType.DMA((pieces, 2, chips // 2)),
            pltpu.SemaphoreType.DMA((pieces, 2, chips // 2)),
            pltpu.SemaphoreType.DMA((pieces, chips)),
            pltpu.SemaphoreType.DMA((pieces, chips)),
            pltpu.SemaphoreType.DMA((pieces,)),
            pltpu.SemaphoreType.DMA,
            pltpu.SemaphoreType.DMA,
            pltpu.SemaphoreType.DMA((cells + 2,)),
            pltpu.SemaphoreType.DMA((9 * cells,)),
            pltpu.SemaphoreType.DMA((4,)),
            pltpu.SemaphoreType.DMA((2,)),
            pltpu.VMEM((count,) + shards[0].shape, LOW),
            pltpu.VMEM((16, width), F32),
            pltpu.VMEM((cells, length, width), LOW),
        ]
        + [pltpu.VMEM((cells,) + shape, kind) for shape, kind in shapes]
        + [
            pltpu.VMEM((cells, length, width), F32),
            pltpu.VMEM((length, width), F32),
            pltpu.VMEM((4, count, width // count, width), LOW),
            pltpu.VMEM((2, 2, shards[4].shape[0], width), LOW),
        ],
        compiler_params=pltpu.CompilerParams(
            collective_id=3, has_side_effects=True, vmem_limit_bytes=62 * 2**20
        ),
        cost_estimate=pl.CostEstimate(flops=flops, bytes_accessed=8 * width * (4 * width + 2 * deep), transcendentals=0),
    )(*shards, inputs)
    return (outs[:5], outs[5], outs[6], outs[7], list(outs[8:]))


class RingSum:
    def __init__(self, chips, items, parts, outs, landed, paired, mine, final, sems):
        self.chips, self.items, self.parts, self.outs = (chips, items, parts, outs)
        self.landed, self.paired, self.mine, self.final = (landed, paired, mine, final)
        self.ring_send, self.ring_recv, self.pair_send, self.pair_recv, self.mine_sem, self.final_sem = sems
        self.half = chips // 2
        self.me, self.core, self.position, self.right, self.left, self.sibling = ring_place(chips)
        self.sent, self.final_copies, self.exchanged = ([], [], [])
        self.uses = [0] * len(items)
        self.fetched = None

    def part(self, item, block):
        array, start, rows, _ = self.items[item]
        return self.parts[array].at[block, pl.ds(start, rows)]

    def first(self, item, way):
        return 1 if self.items[item][3] == way else 2

    def slot_of(self, item, way, step):
        return step - 1 if self.items[item][3] == way else self.half + step - 2

    def offset_of(self, step, way):
        return self.half - step + 1 if way == 0 else self.chips - (self.half - step + 1)

    def pair_copy(self, item, offset):
        block = ring_chip(self.position + offset, self.chips) * 2 + 1 - self.core
        return pltpu.make_async_remote_copy(
            src_ref=self.part(item, block),
            dst_ref=self.paired[item].at[offset],
            send_sem=self.pair_send.at[item, offset],
            recv_sem=self.pair_recv.at[item, offset],
            device_id={"dp": self.sibling},
            device_id_type=MESH,
        )

    def ring_copy(self, item, way, step):
        if step == self.first(item, way):
            source = self.paired[item].at[self.offset_of(step, way)]
        else:
            source = self.landed[item].at[self.slot_of(item, way, step - 1)]
        here = self.slot_of(item, way, step)
        return pltpu.make_async_remote_copy(
            src_ref=source,
            dst_ref=self.landed[item].at[here],
            send_sem=self.ring_send.at[item, here],
            recv_sem=self.ring_recv.at[item, here],
            device_id={"dp": self.right if way == 0 else self.left},
            device_id_type=MESH,
        )

    def load(self, item, offset, buffer):
        block = ring_chip(self.position + offset, self.chips) * 2 + self.core
        return pltpu.make_async_copy(self.part(item, block), self.mine[item].at[buffer], self.mine_sem.at[item, buffer])

    def exchange(self, wanted, offsets):
        for offset in offsets:
            for item in wanted:
                self.pair_copy(item, offset).start()
                self.exchanged.append((item, offset))

    def starts(self, wanted):
        return [
            (step, item, way, self.offset_of(step, way))
            for step in (1, 2)
            for item in wanted
            for way in (0, 1)
            if step == self.first(item, way)
        ]

    def rest(self, wanted):
        return [
            (step, item, way, self.offset_of(step, way))
            for step in range(2, self.half + 1)
            for item in wanted
            for way in (0, 1)
            if step > self.first(item, way)
        ] + [(self.half + 1, item, None, 0) for item in wanted]

    def run(self, plan, between=None):
        numbered = []
        for entry in plan:
            numbered.append(entry + (self.uses[entry[1]] % 2,))
            self.uses[entry[1]] += 1
        for number, entry in enumerate(numbered):
            if number == 0:
                self.load(entry[1], entry[3], entry[4]).start()
            if number + 1 < len(numbered):
                later = numbered[number + 1]
                self.load(later[1], later[3], later[4]).start()
            self.work(entry)
            if between is not None:
                between()

    def work(self, entry):
        step, item, way, offset, buffer = entry
        array, start, rows, _ = self.items[item]
        half, final = (self.half, self.final)
        self.load(item, offset, buffer).wait()
        self.pair_copy(item, offset).wait_recv()
        kind = self.parts[array].dtype
        columns = self.parts[array].shape[2]
        chunk = 16
        from_pair, from_mine, from_ring = (self.paired[item], self.mine[item], self.landed[item])
        if way is None:
            self.ring_copy(item, 0, half).wait_recv()
            self.ring_copy(item, 1, half).wait_recv()
            slot_a, slot_b = (self.slot_of(item, 0, half), self.slot_of(item, 1, half))
            if kind == F32:
                self.outs[array][...] = (from_ring[slot_a] + from_ring[slot_b]) + (from_mine[buffer] + from_pair[offset])
                return
            high, wide = (min(rows, final.shape[1]), min(columns, final.shape[2]))
            for top in range(0, rows, high):
                for across in range(0, columns, wide):
                    number = len(self.final_copies)
                    turn = number % final.shape[0]
                    if number >= final.shape[0]:
                        self.final_copies[number - final.shape[0]].wait()
                    span = pl.ds(across, wide)

                    @pl.loop(0, high // chunk)
                    def _(index):
                        here = pl.ds(pl.multiple_of(top + index * chunk, chunk), chunk)
                        final[turn, pl.ds(pl.multiple_of(index * chunk, chunk), chunk), pl.ds(0, wide)] = (
                            from_ring[slot_a, here, span].astype(F32) + from_ring[slot_b, here, span].astype(F32)
                        ) + (from_mine[buffer, here, span].astype(F32) + from_pair[offset, here, span].astype(F32))

                    self.final_copies.append(
                        pltpu.make_async_copy(
                            final.at[turn, pl.ds(0, high), pl.ds(0, wide)],
                            self.outs[array].at[pl.ds(start + top, high), span],
                            self.final_sem.at[turn],
                        )
                    )
                    self.final_copies[-1].start()
            return
        if step == self.first(item, way):

            @pl.loop(0, rows // chunk)
            def _(index):
                here = pl.ds(pl.multiple_of(index * chunk, chunk), chunk)
                from_pair[offset, here, :] = (
                    from_mine[buffer, here, :].astype(F32) + from_pair[offset, here, :].astype(F32)
                ).astype(kind)

        else:
            self.ring_copy(item, way, step - 1).wait_recv()
            arrived = self.slot_of(item, way, step - 1)

            @pl.loop(0, rows // chunk)
            def _(index):
                here = pl.ds(pl.multiple_of(index * chunk, chunk), chunk)
                from_ring[arrived, here, :] = (
                    from_ring[arrived, here, :].astype(F32)
                    + (from_mine[buffer, here, :].astype(F32) + from_pair[offset, here, :].astype(F32))
                ).astype(kind)

        self.sent.append(self.ring_copy(item, way, step))
        self.sent[-1].start()

    def close(self):
        for copy in self.sent:
            copy.wait_send()
        for item, offset in self.exchanged:
            self.pair_copy(item, offset).wait_send()
        for copy in self.final_copies[-self.final.shape[0] :]:
            copy.wait()


def ring_scratch(chips, items, shapes, kinds, pieces_rows):
    held = [(rows,) + tuple(shapes[array][1:]) for array, _, rows, _ in items]
    kinds = [kinds[array] for array, _, _, _ in items]
    pieces = len(items)
    return (
        [pltpu.VMEM((chips - 1,) + shape, kind) for shape, kind in zip(held, kinds)]
        + [pltpu.VMEM((chips,) + shape, kind) for shape, kind in zip(held, kinds)]
        + [pltpu.VMEM((2,) + shape, kind) for shape, kind in zip(held, kinds)]
        + [pltpu.VMEM(pieces_rows, F32)]
        + [
            pltpu.SemaphoreType.DMA((pieces, chips - 1)),
            pltpu.SemaphoreType.DMA((pieces, chips - 1)),
            pltpu.SemaphoreType.DMA((pieces, chips)),
            pltpu.SemaphoreType.DMA((pieces, chips)),
            pltpu.SemaphoreType.DMA((pieces, 2)),
            pltpu.SemaphoreType.DMA((pieces_rows[0],)),
        ]
    )


class Products:
    def __init__(self, chips, width, own, cuts, big, stage, cut_sem, big_sem, stage_sem):
        self.chips, self.width, self.own = (chips, width, own)
        self.cuts, self.big, self.stage = (cuts, big, stage)
        self.cut_sem, self.big_sem, self.stage_sem = (cut_sem, big_sem, stage_sem)

    def load_cut(self, source, index, slot):
        cut = self.cuts.shape[2]
        window = pl.ds(pl.multiple_of(index * cut, cut), cut)
        return pltpu.make_async_copy(source.at[:, window], self.cuts.at[slot], self.cut_sem.at[slot])

    def block(self, source, index, slot):
        window = pl.ds(pl.multiple_of(index * self.width, self.width), self.width)
        return pltpu.make_async_copy(source.at[:, window], self.big.at[slot], self.big_sem.at[slot])

    def keep(self, target, index):
        window = pl.ds(pl.multiple_of(index // 2 * self.width, self.width), self.width)
        return pltpu.make_async_copy(
            self.stage.at[lax.rem(index, 2)],
            target.at[pl.ds(lax.rem(index, 2) * self.chips, self.chips), :, window],
            self.stage_sem.at[lax.rem(index, 2)],
        )

    def open(self, left, right, slot):
        for index in (0, 1):
            self.load_cut(left, index, index).start()
        self.block(right, 0, slot).start()

    def run(self, target, left, right, shift, low, high):
        number = 2 * (right.shape[1] // self.width)
        if low == 0:
            for index in (0, 1):
                self.load_cut(left, index, index).wait()

        @pl.loop(low, high)
        def _(index):
            slot = lax.rem(index, 2)
            here = lax.rem(index // 2 + shift, 2)

            @pl.when(slot == 0)
            def _():
                self.block(right, index // 2, here).wait()

                @pl.when(index + 2 < number)
                def _():
                    self.block(right, index // 2 + 1, 1 - here).start()

            @pl.when(index >= low + 2)
            def _():
                self.keep(target, index - 2).wait()

            product = dot_left(self.cuts[slot], self.big[here]).astype(LOW)
            for device in range(self.chips):
                self.stage[slot, device] = product[device * self.own : (device + 1) * self.own]
            self.keep(target, index).start()

        for index in range(max(low, high - 2), high):
            self.keep(target, index).wait()


def other_grads_kernel(chips, width, items, *refs):
    count = len(items)
    small_part, up_part, lowered, grad_packed, mixed, grad_branch = refs[:6]
    outs = refs[6:10]
    parts = [small_part, refs[10], refs[11], up_part]
    refs = refs[12:]
    landed, paired, mine, final = (refs[:count], refs[count : 2 * count], refs[2 * count : 3 * count], refs[3 * count])
    sems = refs[3 * count + 1 : 3 * count + 7]
    big, cuts, stage, big_sem, cut_sem, stage_sem = refs[3 * count + 7 :]
    ring = RingSum(chips, items, parts, outs, landed, paired, mine, final, sems)
    products = Products(chips, width, width // (2 * chips), cuts, big, stage, cut_sem, big_sem, stage_sem)
    products.open(mixed, grad_branch, 1)
    greet((ring.left, ring.right, ring.sibling))
    half = ring.half
    far = [half, half - 1, half + 1]
    order = far + [offset for offset in range(chips) if offset not in far]
    ups = [item for item in range(count) if items[item][0] == 3]
    others = [item for item in range(count) if items[item][0] < 3]
    smalls = [item for item in others if items[item][0] == 0]
    heads = [item for item in others if items[item][0] > 0]
    head_blocks = grad_packed.shape[1] // width
    ring.exchange(ups, order)
    ring.exchange(smalls, order)
    products.run(parts[2], mixed, grad_branch, 1, 0, 2)
    products.open(lowered, grad_packed, 0)
    ring.run(ring.starts(ups))
    ring.run(ring.starts(smalls))
    products.run(parts[1], lowered, grad_packed, 0, 0, head_blocks)
    rest = ring.rest(ups + heads + smalls)
    early = [entry for entry in rest if entry[1] in ups and entry[0] == 2]
    ring.run(early)
    products.run(parts[1], lowered, grad_packed, 0, head_blocks, 2 * head_blocks)
    ring.exchange(heads, order)
    soon = [entry for entry in rest if entry[1] in ups and entry[0] == 3]
    ring.run(soon)
    ring.run(ring.starts(heads))
    ring.run([entry for entry in rest if entry not in early + soon])
    ring.close()


def other_grads(small_part, up_part, sides, items, shapes, count):
    chips = count // 2
    rows_in, width = sides[0].shape
    wholes = [small_part.shape[1:]] + [tuple(shape) for shape in shapes[:3]]
    hbm = pl.BlockSpec(memory_space=pl.ANY)
    cut = width // 2
    flops = 2 * rows_in * 4 * width * width
    outs = pl.pallas_call(
        functools.partial(other_grads_kernel, chips, width, items),
        out_shape=[jax.ShapeDtypeStruct(shape, F32) for shape in wholes]
        + [jax.ShapeDtypeStruct((count,) + shape, LOW) for shape in wholes[1:3]],
        in_specs=[hbm] * 6,
        out_specs=[pl.BlockSpec(memory_space=pltpu.VMEM)] + [hbm] * 5,
        scratch_shapes=ring_scratch(chips, items, wholes, [F32, LOW, LOW, LOW], (4, shapes[0][0], width))
        + [
            pltpu.VMEM((2, rows_in, width), LOW),
            pltpu.VMEM((2, rows_in, cut), LOW),
            pltpu.VMEM((2, chips, width // count, width), LOW),
            pltpu.SemaphoreType.DMA((2,)),
            pltpu.SemaphoreType.DMA((2,)),
            pltpu.SemaphoreType.DMA((2,)),
        ],
        compiler_params=pltpu.CompilerParams(
            collective_id=2, has_side_effects=True, vmem_limit_bytes=62 * 2**20
        ),
        cost_estimate=pl.CostEstimate(flops=flops, bytes_accessed=80 * width * width, transcendentals=0),
    )(small_part, up_part, *sides)
    return outs[:4]


def last_backward_kernel(chips, items, cell, *refs):
    count = len(items)
    (grad_h, entry_h, rows, packed_h, middle_h, slope_h, w_qkv, w_out, w_up, w_down) = refs[:10]
    (activated_h, grad_ff_h, second_h) = refs[10:13]
    refs = refs[13 + 5 :]
    rows_o, packed_o, branch_o, inner_o, sums_o = refs[:5]
    share_o, down_part, up_part = refs[5:8]
    refs = refs[8:]
    landed, paired, mine, final = (refs[:count], refs[count : 2 * count], refs[2 * count : 3 * count], refs[3 * count])
    sems = refs[3 * count + 1 : 3 * count + 7]
    (big, cuts, stage, stage_down, big_sem, cut_sem, stage_sem) = refs[3 * count + 7 : 3 * count + 14]
    (buffers, buffer_sems, load_sems, save_sems, slope_sems, inner_sems) = refs[3 * count + 14 : 3 * count + 20]
    (grad, entry, packed_v, middle_v, slope_v, inner_v, grad_packed_v, mixed_v, branch_v, grad_act_v, total_v, sums_v) = refs[
        3 * count + 20 :
    ]
    length, width = grad.shape
    devices = 2 * chips
    deep_own = down_part.shape[1]
    ups = w_up.shape[1] // width
    first = lax.axis_index("pipe") == 0
    ring = RingSum(chips, items, [down_part], [share_o], landed, paired, mine, final, sems)
    half, position = (ring.half, ring.position)
    products = Products(chips, width, width // devices, cuts, big, stage, cut_sem, big_sem, stage_sem)
    gains = rows.at[0:2]

    def farthest_first(index):
        step = index // 2
        return ring_chip(position + jnp.where(lax.rem(index, 2) == 0, half - step, half + step + 1), chips)

    def keep_down(index):
        return pltpu.make_async_copy(
            stage_down.at[lax.rem(index, 2)],
            down_part.at[pl.ds(farthest_first(index) * 2, 2)],
            stage_sem.at[2 + lax.rem(index, 2)],
        )

    def cut_down(index):
        return products.load_cut(activated_h, farthest_first(index), lax.rem(index, 2))

    def down_products(low, high):
        @pl.loop(low, high)
        def _(index):
            slot = lax.rem(index, 2)

            @pl.when(index + 1 < chips)
            def _():
                cut_down(index + 1).start()

            cut_down(index).wait()

            @pl.when(index >= low + 2)
            def _():
                keep_down(index - 2).wait()

            product = dot_left(cuts[slot], big[0]).astype(LOW)
            for side in (0, 1):
                stage_down[slot, side] = product[side * deep_own : (side + 1) * deep_own]
            keep_down(index).start()

        for index in range(max(low, high - 2), high):
            keep_down(index).wait()

    def here(ref, at):
        return ref.at[pl.ds(at * length, length)]

    def ff_load(at):
        return pltpu.make_async_copy(here(grad_ff_h, at), here(big.at[0], at), load_sems.at[at])

    def ff_arrived():
        return pltpu.make_async_copy(grad_h, here(big.at[0], cell), load_sems.at[cell])

    for at in range(cell):
        ff_load(at).start()
    pl.when(first)(lambda: ff_arrived().start())
    pl.when(jnp.logical_not(first))(lambda: ff_load(cell).start())
    cut_down(0).start()

    def own_load(number):
        source, target = (
            (grad_h, grad),
            (entry_h, entry),
            (middle_h.at[cell], middle_v),
            (packed_h.at[cell], packed_v),
        )[number]
        return pltpu.make_async_copy(source, target, load_sems.at[cell + 1 + number])

    def slope_load(number):
        window = pl.ds(number * width, width)
        return pltpu.make_async_copy(
            slope_h.at[cell].at[:, window], slope_v.at[number % 2], slope_sems.at[number % 2]
        )

    order, place_up, place_down = ([], {}, {})
    for number in range(ups + 1):
        if number < ups:
            place_down[number] = len(order)
            order.append((w_down, 0, number))
        if number > 0:
            place_up[number - 1] = len(order)
            order.append((w_up, 1, number - 1))
    place_out = len(order)
    order = order + [(w_out, 0, 0)] + [(w_qkv, 1, number) for number in range(3)]
    depth = buffers.shape[0]

    def weight_load(number):
        ref, axis, at = order[number]
        window = pl.ds(at * width, width)
        source = ref.at[:, window] if axis else ref.at[window, :]
        return pltpu.make_async_copy(source, buffers.at[number % depth], buffer_sems.at[number % depth])

    def take(number):
        weight_load(number).wait()
        return buffers.at[number % depth]

    def release(number):
        if number + depth < len(order):
            weight_load(number + depth).start()

    def save(number, wait=False):
        source, target = (
            (branch_v, branch_o.at[cell]),
            (grad_packed_v, packed_o.at[cell]),
            (sums_v, sums_o.at[cell]),
            (mixed_v, rows_o.at[cell]),
        )[number]
        copy = pltpu.make_async_copy(source, target, save_sems.at[number])
        copy.wait() if wait else copy.start()

    def inner_save(number):
        window = pl.ds(number * width, width)
        return pltpu.make_async_copy(
            inner_v.at[number % 2], inner_o.at[pl.ds(cell * length, length), window], inner_sems.at[number % 2]
        )

    def column_sum(array):
        return jnp.sum(array.astype(F32), axis=0, keepdims=True)

    def begin():
        own_load(0).start()
        slope_load(0).start()
        for number in range(depth):
            weight_load(number).start()
        for number in (1, 2, 3):
            own_load(number).start()
        own_load(0).wait()
        sums_v[7:8, :] = column_sum(grad[...])

    def climb(number):
        def step():
            if number < ups:
                down_block = take(place_down[number])
                grad_act_v[number % 2] = dot_right(grad[...], down_block[...])
                release(place_down[number])
            if number > 0:
                at = number - 1
                slope_load(at).wait()
                if at + 1 < ups:
                    slope_load(at + 1).start()
                up_block = take(place_up[at])
                if at >= 2:
                    inner_save(at - 2).wait()
                inner = (grad_act_v[at % 2] * slope_v[at % 2].astype(F32)).astype(LOW)
                inner_v[at % 2] = inner
                sums_v[8 + at : 9 + at, :] = column_sum(inner)
                part = dot_right(inner, up_block[...])
                if at == 0:
                    total_v[...] = part
                else:
                    total_v[...] += part
                inner_save(at).start()
                release(place_up[at])

        return step

    def turn():
        own_load(2).wait()
        normed, inverse = row_norm(middle_v[...])
        grad_second = total_v[...]
        sums_v[1:2, :] = column_sum(grad_second * normed)
        sums_v[6:7, :] = column_sum(grad_second)
        grad_middle = grad[...].astype(F32) + norm_back(grad_second * gains[1:2, :], normed, inverse)
        middle_v[...] = grad_middle
        branch_v[...] = grad_middle.astype(LOW)
        sums_v[5:6, :] = column_sum(branch_v[...])
        save(0)
        for at in range(max(0, ups - 2), ups):
            inner_save(at).wait()

    def outer():
        block = take(place_out)
        mixed_v[...] = dot_right(branch_v[...], block[...]).astype(LOW)
        release(place_out)
        own_load(3).wait()

    def heads(low, high):
        def step():
            attend_back(packed_v, mixed_v, grad_packed_v, width, low, high)

        return step

    def sums():
        save(1)
        sums_v[3:4, :] = column_sum(grad_packed_v[:, pl.ds(0, width)])
        sums_v[4:5, :] = column_sum(grad_packed_v[:, pl.ds(2 * width, width)])

    def lower(number):
        def step():
            block = take(place_out + 1 + number)
            part = dot_right(grad_packed_v[:, pl.ds(number * width, width)], block[...])
            if number == 0:
                total_v[...] = part
            else:
                total_v[...] += part
            release(place_out + 1 + number)

        return step

    def finish():
        own_load(1).wait()
        normed, inverse = row_norm(entry[...].astype(F32))
        grad_lowered = total_v[...]
        sums_v[0:1, :] = column_sum(grad_lowered * normed)
        sums_v[2:3, :] = column_sum(grad_lowered)
        mixed_v[...] = (middle_v[...] + norm_back(grad_lowered * gains[0:1, :], normed, inverse)).astype(LOW)
        save(2)
        save(3)

    queue = [(True, climb(number)) for number in range(ups + 1)] + [(True, turn)]
    queue.append((False, lambda: products.open(second_h, inner_o, 1)))
    for low in range(0, 2 * ups, 2):
        queue.append((False, lambda low=low: products.run(up_part, second_h, inner_o, 1, low, low + 2)))
    queue.append((True, outer))
    pairs = width // 128
    queue += [(True, heads(low, low + 2)) for low in range(0, pairs, 2)]
    queue.append((True, sums))
    queue += [(True, lower(number)) for number in range(3)] + [(True, finish)]

    def serve():
        if queue:
            own, step = queue.pop(0)
            if own:
                pl.when(first)(step)
            else:
                step()

    greet((ring.left, ring.right, ring.sibling))
    far = [half, half - 1, half + 1]
    near = [offset for offset in range(chips) if offset not in far]
    every = list(range(count))
    for at in range(cell + 1):
        ff_load(at).wait()
    down_products(0, 3)
    ring.exchange(every, far)
    down_products(3, 5)
    pl.when(first)(begin)
    ring.run(ring.starts(every))
    down_products(5, chips)
    ring.exchange(every, near)
    for _ in range(3):
        serve()
    ring.run(ring.rest(every), lambda: (serve(), serve()))
    while queue:
        serve()
    ring.close()

    @pl.when(first)
    def _():
        for number in range(4):
            save(number, wait=True)


def last_backward(arrived, entry, rows, saved, weights, kept, sides, items, down_shape, own, count):
    chips = count // 2
    length, width = entry.shape
    deep = weights[2].shape[1]
    ups = deep // width
    cells = kept[0].shape[0]
    rows_in = cells * length
    hbm = pl.BlockSpec(memory_space=pl.ANY)
    cut = width // 2
    flops = 2 * length * width * (4 * width + 2 * deep) + 4 * rows_in * width * deep
    outs = pl.pallas_call(
        functools.partial(last_backward_kernel, chips, items, cells - 1),
        out_shape=[jax.ShapeDtypeStruct(array.shape, array.dtype) for array in kept]
        + [
            jax.ShapeDtypeStruct(down_shape, F32),
            jax.ShapeDtypeStruct((count,) + tuple(down_shape), LOW),
            jax.ShapeDtypeStruct((count, own, deep), LOW),
        ],
        in_specs=[hbm] * 2 + [pl.BlockSpec(memory_space=pltpu.VMEM)] + [hbm] * 15,
        out_specs=[hbm] * 8,
        input_output_aliases={13 + number: number for number in range(5)},
        scratch_shapes=ring_scratch(chips, items, [down_shape], [LOW], (4, 80, width))
        + [
            pltpu.VMEM((2, rows_in, width), LOW),
            pltpu.VMEM((2, rows_in, cut), LOW),
            pltpu.VMEM((2, chips, own, width), LOW),
            pltpu.VMEM((2, 2, down_shape[0], width), LOW),
            pltpu.SemaphoreType.DMA((2,)),
            pltpu.SemaphoreType.DMA((2,)),
            pltpu.SemaphoreType.DMA((4,)),
            pltpu.VMEM((2, width, width), LOW),
            pltpu.SemaphoreType.DMA((2,)),
            pltpu.SemaphoreType.DMA((cells + 4,)),
            pltpu.SemaphoreType.DMA((4,)),
            pltpu.SemaphoreType.DMA((2,)),
            pltpu.SemaphoreType.DMA((2,)),
            pltpu.VMEM((length, width), LOW),
            pltpu.VMEM((length, width), LOW),
            pltpu.VMEM((length, 3 * width), LOW),
            pltpu.VMEM((length, width), F32),
            pltpu.VMEM((2, length, width), LOW),
            pltpu.VMEM((2, length, width), LOW),
            pltpu.VMEM((length, 3 * width), LOW),
            pltpu.VMEM((length, width), LOW),
            pltpu.VMEM((length, width), LOW),
            pltpu.VMEM((2, length, width), F32),
            pltpu.VMEM((length, width), F32),
            pltpu.VMEM((16, width), F32),
        ],
        compiler_params=pltpu.CompilerParams(
            collective_id=4, has_side_effects=True, vmem_limit_bytes=62 * 2**20
        ),
        cost_estimate=pl.CostEstimate(flops=flops, bytes_accessed=80 * width * width, transcendentals=0),
    )(arrived, entry, rows, *saved, *weights, *sides, *kept)
    return (list(outs[:5]), outs[5], outs[7])


def on_device(inputs, out_grad, query_counts, gains, shifts, w_qkv, w_out, w_up, b_up, w_down):
    stage = lax.axis_index("pipe")
    stages = lax.axis_size("pipe")
    count = lax.axis_size("dp")
    cell_count, length, width = inputs.shape
    own = width // count
    ups = b_up.shape[1] // own
    deep = ups * width
    deep_own = w_down.shape[1]
    shapes = [
        block_shape(own, 3 * width),
        block_shape(own, width),
        block_shape(own, deep),
        block_shape(deep_own, width),
    ]
    cut = (shapes[3][0] // 2 + 15) // 16 * 16
    items = (
        (0, 0, 16, 0),
        (1, 0, shapes[0][0], 0),
        (2, 0, shapes[1][0], 0),
        (3, 0, shapes[2][0], 1),
        (4, 0, cut, 0),
        (4, cut, shapes[3][0] - cut, 1),
    )
    shards = [small_pack(gains[0], shifts[0], b_up[0], 1)[0]] + [
        array[0].reshape(shape) for array, shape in zip((w_qkv, w_out, w_up, w_down), shapes)
    ]
    fused = stages == 2 and cell_count == 2 and own % 16 == 0 and width % 256 == 0 and 4 * deep_own == width
    if fused:
        piece = own // 2 // 16 * 16
        arrivals = (
            (0, 0, 16, 0),
            (1, 0, own - piece, 0),
            (1, own - piece, piece, 1),
            (2, 0, own, 1),
            (3, 0, own - piece, 0),
            (3, own - piece, piece, 1),
            (4, 0, cut, 0),
            (4, cut, deep_own - cut, 1),
        )
        packs, rows, arrived, later, kept = gather_forward(
            shards, inputs, arrivals, ((0, 1, 2, 3), (4, 5), (6, 7)), count
        )
    else:
        packs = gather(shards, items, count)
        gain_rows, shift_rows, bias = small_split(packs[0].astype(F32), ups)
        blank = jnp.zeros((8 - ups, width), F32)
        rows = jnp.concatenate([gain_rows, shift_rows, bias.reshape(ups, width), blank])
    weights = (
        packs[1].reshape(width, 3 * width),
        packs[2].reshape(width, width),
        packs[3].reshape(width, deep),
        packs[4].reshape(deep, width),
    )
    scales = jnp.sqrt(query_counts.astype(F32) / 500.0)

    def along(value, steps):
        pairs = [(source, source + steps) for source in range(stages) if 0 <= source + steps < stages]
        return lax.ppermute(value, "pipe", pairs)

    entries = [[inputs[cell] for cell in range(cell_count)]]
    if fused:
        entries.append([arrived] + [along(later, 1)])
    else:
        kept = None
    for turn in range(1 if fused else 0, stages):
        active = (stage == turn).astype(jnp.int32)[None]
        arrived = []
        for cell in range(cell_count):
            sent, kept = forward_tick(active, entries[turn][cell], rows, weights, kept, cell, cell_count)
            if turn + 1 < stages:
                arrived.append(along(sent, 1))
        entries.append(arrived)
    section_out, lowered, packed, mixed, middle, second, activated, slope = kept
    incoming = [(out_grad[cell], scales[cell][None]) for cell in range(cell_count)]
    back = None
    for turn in range(stages - 1, -1, -1):
        active = (stage == turn).astype(jnp.int32)[None]
        arrived = []
        for cell in range(cell_count):
            if fused and turn == 0 and cell == cell_count - 1:
                continue
            sent, back = backward_tick(
                active, incoming[cell], entries[turn][cell], rows, (packed, middle, slope), weights, back, cell, cell_count
            )
            if turn > 0:
                arrived.append((along(sent, -1), jnp.ones((1,), F32)))
        incoming = arrived if turn > 0 else incoming

    def flat(array):
        return array.reshape(cell_count * length, -1)

    input_grads, grad_packed, grad_branch, grad_inner, grad_ff, sums = back
    if fused:
        (input_grads, grad_packed, grad_branch, grad_inner, sums), down_share, up_part = last_backward(
            incoming[-1][0],
            entries[0][-1],
            rows,
            (packed, middle, slope),
            weights,
            (input_grads, grad_packed, grad_branch, flat(grad_inner), sums),
            (flat(activated), flat(grad_ff), flat(second)),
            ((0, 0, cut, 0), (0, cut, deep_own - cut, 1)),
            shapes[3],
            own,
            count,
        )
    sums = jnp.sum(sums, axis=0)
    small_part = small_pack(sums[0:2], sums[2:8], sums[8 : 8 + ups].reshape(deep), count)
    if fused:
        shares = other_grads(
            small_part, up_part, [flat(array) for array in (lowered, grad_packed, mixed, grad_branch)], items[:4], shapes, count
        )
        shares = list(shares) + [down_share]
    else:
        sides = [flat(array) for array in (lowered, grad_packed, mixed, grad_branch, second, grad_inner, activated, grad_ff)]
        products = [dot_left(sides[at], sides[at + 1]).astype(LOW) for at in (0, 2, 4, 6)]
        parts = [small_part] + [whole.reshape((count,) + shape) for whole, shape in zip(products, shapes)]
        shares = scatter(parts, items, count)
    grad_gains, grad_shifts, grad_bias = small_split(shares[0][None], ups)
    return (
        section_out[None],
        input_grads[None],
        grad_gains[None],
        grad_shifts[None],
        shares[1].reshape(1, own, 3 * width),
        shares[2].reshape(1, own, width),
        shares[3].reshape(1, own, deep),
        grad_bias[None],
        shares[4].reshape(1, deep_own, width),
    )


def solution(mesh):
    in_specs = (
        P("dp", None, None),
        P("dp", None, None),
        P("dp"),
        P("pipe", None, "dp"),
        P("pipe", None, "dp"),
        P("pipe", "dp", None),
        P("pipe", "dp", None),
        P("pipe", "dp", None),
        P("pipe", "dp"),
        P("pipe", "dp", None),
    )
    out_specs = (
        P("pipe", "dp", None, None),
        P("pipe", "dp", None, None),
        P("pipe", None, "dp"),
        P("pipe", None, "dp"),
        P("pipe", "dp", None),
        P("pipe", "dp", None),
        P("pipe", "dp", None),
        P("pipe", "dp"),
        P("pipe", "dp", None),
    )
    return jax.shard_map(
        on_device, mesh=mesh, in_specs=in_specs, out_specs=out_specs, check_vma=False
    )
```

```python
import functools
import math

import jax
import jax.numpy as jnp
from jax import lax
from jax.experimental import pallas as pl
from jax.experimental.pallas import tpu as pltpu
from jax.sharding import PartitionSpec as P

HEAD_DIM = 64
MESH = pl.DeviceIdType.MESH
LOW = jnp.bfloat16
F32 = jnp.float32


def ring_chip(position, chips):
    position = lax.rem(position + 2 * chips, chips)
    half = chips // 2
    return jnp.where(position < half, 2 * position, 2 * (chips - 1 - position) + 1)


def ring_place(chips):
    me = lax.axis_index("dp")
    core = lax.rem(me, 2)
    chip = me // 2
    position = jnp.where(lax.rem(chip, 2) == 0, chip // 2, chips - 1 - chip // 2)
    right = ring_chip(position + 1, chips) * 2 + core
    left = ring_chip(position - 1, chips) * 2 + core
    return (me, core, position, right, left, me + 1 - 2 * core)


def greet(devices):
    barrier = pltpu.get_barrier_semaphore()
    for device in devices:
        pl.semaphore_signal(barrier, inc=1, device_id={"dp": device}, device_id_type=MESH)
    pl.semaphore_wait(barrier, len(devices))


def gather_kernel(chips, arrays, items, *refs):
    count = len(items)
    ring_send, ring_recv, pair_send, pair_recv, own_sem = refs[2 * arrays :]
    shards = [refs[array].at[pl.ds(start, rows)] for array, start, rows, _ in items]
    splits = [way for _, _, _, way in items]
    half = chips // 2
    me, core, position, right, left, sibling = ring_place(chips)
    greet((left, right, sibling))

    def out(item, block):
        array, start, rows, _ = items[item]
        return refs[arrays + array].at[block, pl.ds(start, rows)]

    def owner(step, way):
        return ring_chip(position - step if way == 0 else position + step, chips) * 2 + core

    def travels(item, way, step):
        return step < half or (step == half and splits[item] == way)

    def ring_copy(item, way, step):
        block = owner(step - 1, way)
        return pltpu.make_async_remote_copy(
            src_ref=shards[item] if step == 1 else out(item, block),
            dst_ref=out(item, block),
            send_sem=ring_send.at[item, way, step - 1],
            recv_sem=ring_recv.at[item, way, step - 1],
            device_id={"dp": right if way == 0 else left},
            device_id_type=MESH,
        )

    def pair_copy(item, offset, block, source):
        return pltpu.make_async_remote_copy(
            src_ref=source,
            dst_ref=out(item, block),
            send_sem=pair_send.at[item, offset],
            recv_sem=pair_recv.at[item, offset],
            device_id={"dp": sibling},
            device_id_type=MESH,
        )

    sent, paired, kept = ([], [], [])
    for item in range(count):
        for way in (0, 1):
            if travels(item, way, 1):
                sent.append(ring_copy(item, way, 1))
                sent[-1].start()
    for item in range(count):
        paired.append(pair_copy(item, 0, me, shards[item]))
        paired[-1].start()
        kept.append(pltpu.make_async_copy(shards[item], out(item, me), own_sem.at[item]))
        kept[-1].start()
    for step in range(1, half + 1):
        for item in range(count):
            for way in (0, 1):
                if not travels(item, way, step):
                    continue
                ring_copy(item, way, step).wait_recv()
                if travels(item, way, step + 1):
                    sent.append(ring_copy(item, way, step + 1))
                    sent[-1].start()
                block = owner(step, way)
                offset = step if way == 0 else chips - step
                paired.append(pair_copy(item, offset, block, out(item, block)))
                paired[-1].start()
    for copy in sent:
        copy.wait_send()
    for copy in paired:
        copy.wait()
    for copy in kept:
        copy.wait()


def gather(shards, items, count):
    chips = count // 2
    arrays, pieces = (len(shards), len(items))
    return pl.pallas_call(
        functools.partial(gather_kernel, chips, arrays, items),
        out_shape=[jax.ShapeDtypeStruct((count,) + shard.shape, shard.dtype) for shard in shards],
        in_specs=[pl.BlockSpec(memory_space=pl.ANY)] * arrays,
        out_specs=[pl.BlockSpec(memory_space=pl.ANY)] * arrays,
        scratch_shapes=[
            pltpu.SemaphoreType.DMA((pieces, 2, chips // 2)),
            pltpu.SemaphoreType.DMA((pieces, 2, chips // 2)),
            pltpu.SemaphoreType.DMA((pieces, chips)),
            pltpu.SemaphoreType.DMA((pieces, chips)),
            pltpu.SemaphoreType.DMA((pieces,)),
        ],
        compiler_params=pltpu.CompilerParams(collective_id=0, has_side_effects=True),
    )(*shards)


def scatter_kernel(chips, arrays, items, *refs):
    count = len(items)
    parts, outs, refs = (refs[:arrays], refs[arrays : 2 * arrays], refs[2 * arrays :])
    landed, paired, mine = (refs[:count], refs[count : 2 * count], refs[2 * count : 3 * count])
    ring_send, ring_recv, pair_send, pair_recv, mine_sem = refs[3 * count :]
    splits = [way for _, _, _, way in items]
    half = chips // 2
    me, core, position, right, left, sibling = ring_place(chips)
    greet((left, right, sibling))

    def part(item, block):
        array, start, rows, _ = items[item]
        return parts[array].at[block, pl.ds(start, rows)]

    def first(item, way):
        return 1 if splits[item] == way else 2

    def slot(item, way, step):
        return step - 1 if splits[item] == way else half + step - 2

    def offset_of(step, way):
        return half - step + 1 if way == 0 else chips - (half - step + 1)

    def pair_copy(item, offset):
        block = ring_chip(position + offset, chips) * 2 + 1 - core
        return pltpu.make_async_remote_copy(
            src_ref=part(item, block),
            dst_ref=paired[item].at[offset],
            send_sem=pair_send.at[item, offset],
            recv_sem=pair_recv.at[item, offset],
            device_id={"dp": sibling},
            device_id_type=MESH,
        )

    def ring_copy(item, way, step):
        if step == first(item, way):
            source = paired[item].at[offset_of(step, way)]
        else:
            source = landed[item].at[slot(item, way, step - 1)]
        here = slot(item, way, step)
        return pltpu.make_async_remote_copy(
            src_ref=source,
            dst_ref=landed[item].at[here],
            send_sem=ring_send.at[item, here],
            recv_sem=ring_recv.at[item, here],
            device_id={"dp": right if way == 0 else left},
            device_id_type=MESH,
        )

    def load(item, offset, buffer):
        block = ring_chip(position + offset, chips) * 2 + core
        return pltpu.make_async_copy(part(item, block), mine[item].at[buffer], mine_sem.at[item, buffer])

    plan, uses = ([], [0] * count)
    for step in range(1, half + 2):
        for item in range(count):
            for way in (0, 1):
                if step <= half and step >= first(item, way):
                    plan.append((step, item, way, offset_of(step, way), uses[item] % 2))
                    uses[item] += 1
            if step > half:
                plan.append((step, item, None, 0, uses[item] % 2))
                uses[item] += 1
    for step, item, way, offset, buffer in plan:
        pair_copy(item, offset).start()
    load(plan[0][1], plan[0][3], plan[0][4]).start()
    sent = []
    for number, (step, item, way, offset, buffer) in enumerate(plan):
        if number + 1 < len(plan):
            load(plan[number + 1][1], plan[number + 1][3], plan[number + 1][4]).start()
        load(item, offset, buffer).wait()
        pair_copy(item, offset).wait_recv()
        array, start, rows, _ = items[item]
        kind = parts[array].dtype
        chunk = 16 if rows % 16 == 0 else rows
        from_pair, from_mine, from_ring = (paired[item], mine[item], landed[item])
        if way is None:
            ring_copy(item, 0, half).wait_recv()
            ring_copy(item, 1, half).wait_recv()
            slot_a, slot_b = (slot(item, 0, half), slot(item, 1, half))

            @pl.loop(0, rows // chunk)
            def _(index):
                here = pl.ds(pl.multiple_of(index * chunk, chunk), chunk)
                outs[array][pl.ds(pl.multiple_of(start + index * chunk, chunk), chunk), :] = (
                    from_ring[slot_a, here, :].astype(F32) + from_ring[slot_b, here, :].astype(F32)
                ) + (from_mine[buffer, here, :].astype(F32) + from_pair[offset, here, :].astype(F32))

            continue
        if step == first(item, way):

            @pl.loop(0, rows // chunk)
            def _(index):
                here = pl.ds(pl.multiple_of(index * chunk, chunk), chunk)
                from_pair[offset, here, :] = (
                    from_mine[buffer, here, :].astype(F32) + from_pair[offset, here, :].astype(F32)
                ).astype(kind)

        else:
            ring_copy(item, way, step - 1).wait_recv()
            arrived = slot(item, way, step - 1)

            @pl.loop(0, rows // chunk)
            def _(index):
                here = pl.ds(pl.multiple_of(index * chunk, chunk), chunk)
                from_ring[arrived, here, :] = (
                    from_ring[arrived, here, :].astype(F32)
                    + (from_mine[buffer, here, :].astype(F32) + from_pair[offset, here, :].astype(F32))
                ).astype(kind)

        sent.append(ring_copy(item, way, step))
        sent[-1].start()
    for copy in sent:
        copy.wait_send()
    for step, item, way, offset, buffer in plan:
        pair_copy(item, offset).wait_send()


def scatter(parts, items, count):
    chips = count // 2
    arrays, pieces = (len(parts), len(items))
    shapes = [(rows,) + parts[array].shape[2:] for array, _, rows, _ in items]
    kinds = [parts[array].dtype for array, _, _, _ in items]
    return pl.pallas_call(
        functools.partial(scatter_kernel, chips, arrays, items),
        out_shape=[jax.ShapeDtypeStruct(part.shape[1:], F32) for part in parts],
        in_specs=[pl.BlockSpec(memory_space=pl.ANY)] * arrays,
        out_specs=[pl.BlockSpec(memory_space=pltpu.VMEM)] * arrays,
        scratch_shapes=[pltpu.VMEM((chips - 1,) + shape, kind) for shape, kind in zip(shapes, kinds)]
        + [pltpu.VMEM((chips,) + shape, kind) for shape, kind in zip(shapes, kinds)]
        + [pltpu.VMEM((2,) + shape, kind) for shape, kind in zip(shapes, kinds)]
        + [
            pltpu.SemaphoreType.DMA((pieces, chips - 1)),
            pltpu.SemaphoreType.DMA((pieces, chips - 1)),
            pltpu.SemaphoreType.DMA((pieces, chips)),
            pltpu.SemaphoreType.DMA((pieces, chips)),
            pltpu.SemaphoreType.DMA((pieces, 2)),
        ],
        compiler_params=pltpu.CompilerParams(
            collective_id=1, has_side_effects=True, vmem_limit_bytes=62 * 2**20
        ),
    )(*parts)


def block_shape(rows, columns):
    return (rows, columns) if rows % 16 == 0 else (rows * columns // 128, 128)


def small_pack(gains, shifts, bias, count):
    width = gains.shape[1] // count
    ups = bias.shape[0] // gains.shape[1]
    rows = [
        gains.reshape(2, count, width).swapaxes(0, 1),
        shifts.reshape(6, count, width).swapaxes(0, 1),
        bias.reshape(count, ups, width),
    ]
    blank = jnp.zeros((count, 8 - ups, width), gains.dtype)
    return jnp.concatenate(rows + [blank], axis=1)


def small_split(blocks, ups):
    count, _, width = blocks.shape
    gains = blocks[:, 0:2].swapaxes(0, 1).reshape(2, count * width)
    shifts = blocks[:, 2:8].swapaxes(0, 1).reshape(6, count * width)
    bias = blocks[:, 8 : 8 + ups].reshape(count * ups * width)
    return (gains, shifts, bias)


def row_norm(rows_in):
    center = rows_in - jnp.mean(rows_in, axis=-1, keepdims=True)
    inverse = lax.rsqrt(jnp.mean(center * center, axis=-1, keepdims=True) + 1e-05)
    return (center * inverse, inverse)


def norm_back(grad_rows, normed, inverse):
    return inverse * (
        grad_rows
        - jnp.mean(grad_rows, axis=-1, keepdims=True)
        - normed * jnp.mean(grad_rows * normed, axis=-1, keepdims=True)
    )


def gelu_parts(hidden):
    cumulative = 0.5 * (1.0 + lax.erf(hidden * (1.0 / math.sqrt(2.0))))
    slope = cumulative + hidden * jnp.exp(-0.5 * hidden * hidden) * (1.0 / math.sqrt(2.0 * math.pi))
    return (hidden * cumulative, slope)


def dot(left, right):
    return lax.dot_general(left, right, (((1,), (0,)), ((), ())), preferred_element_type=F32)


def dot_right(left, right):
    return lax.dot_general(left, right, (((1,), (1,)), ((), ())), preferred_element_type=F32)


def dot_left(left, right):
    return lax.dot_general(left, right, (((0,), (0,)), ((), ())), preferred_element_type=F32)


class Stream:
    def __init__(self, blocks, buffers, sems):
        self.blocks, self.buffers, self.sems = (blocks, buffers, sems)
        self.depth = buffers.shape[0]
        self.started = 0
        for _ in range(min(self.depth, len(blocks))):
            self.start()

    def copy(self, number):
        slot = number % self.depth
        return pltpu.make_async_copy(self.blocks[number], self.buffers.at[slot], self.sems.at[slot])

    def start(self):
        self.copy(self.started).start()
        self.started += 1

    def take(self, number):
        self.copy(number).wait()
        return self.buffers.at[number % self.depth]

    def release(self):
        if self.started < len(self.blocks):
            self.start()


def weight_blocks(w_qkv, w_out, w_up, w_down):
    width = w_out.shape[0]
    def cut(ref, axis, number):
        window = pl.ds(number * width, width)
        return ref.at[:, window] if axis else ref.at[window, :]
    heads = [cut(w_qkv, 1, number) for number in range(3)]
    ups = [cut(w_up, 1, number) for number in range(w_up.shape[1] // width)]
    downs = [cut(w_down, 0, number) for number in range(w_down.shape[0] // width)]
    return (heads, w_out, ups, downs)


def head_masks(length):
    return lax.broadcasted_iota(jnp.int32, (length, 128), 1) < HEAD_DIM


def two_heads(array, side):
    blank = jnp.zeros_like(array)
    return jnp.concatenate([jnp.where(side, array, blank), jnp.where(side, blank, array)], axis=0)


def attend(packed, mixed, width, low=0, high=None):
    length = packed.shape[0]
    side = head_masks(length)

    def pair_of(pair):
        start = pair * 128 if isinstance(pair, int) else pl.multiple_of(pair * 128, 128)
        queries = packed[:, pl.ds(start, 128)] * jnp.asarray(1.0 / math.sqrt(HEAD_DIM), LOW)
        keys = two_heads(packed[:, pl.ds(start + width, 128)], side)
        values = two_heads(packed[:, pl.ds(start + 2 * width, 128)], side)
        scores = dot_right(queries, keys)
        probs, totals = ([], [])
        for head in (0, 1):
            mine = scores[:, head * length : (head + 1) * length]
            shifted = jnp.exp(mine - jnp.max(mine, axis=-1, keepdims=True))
            totals.append(1.0 / jnp.sum(shifted, axis=-1, keepdims=True))
            probs.append(shifted.astype(LOW))
        result = dot(jnp.concatenate(probs, axis=1), values)
        mixed[:, pl.ds(start, 128)] = (result * jnp.where(side, totals[0], totals[1])).astype(LOW)

    if high is not None:
        for pair in range(low, high):
            pair_of(pair)
        return

    @pl.loop(0, width // 256)
    def _(index):
        pair_of(index * 2)
        pair_of(index * 2 + 1)


def attend_back(packed, grad_mixed, grad_packed, width, low=0, high=None):
    length = packed.shape[0]
    side = head_masks(length)
    scale = 1.0 / math.sqrt(HEAD_DIM)

    def pair_of(pair):
        start = pair * 128 if isinstance(pair, int) else pl.multiple_of(pair * 128, 128)
        queries = packed[:, pl.ds(start, 128)]
        keys = packed[:, pl.ds(start + width, 128)] * jnp.asarray(scale, LOW)
        grads = grad_mixed[:, pl.ds(start, 128)]
        keys_two = two_heads(keys, side)
        queries_two = two_heads(queries, side)
        grads_two = two_heads(grads, side)
        scores = dot_right(keys, queries_two)
        grad_probs = dot_right(packed[:, pl.ds(start + 2 * width, 128)], grads_two)
        probs, grad_scores = ([], [])
        for head in (0, 1):
            mine = slice(head * length, (head + 1) * length)
            shifted = jnp.exp(scores[:, mine] - jnp.max(scores[:, mine], axis=0, keepdims=True))
            prob = shifted * (1.0 / jnp.sum(shifted, axis=0, keepdims=True))
            product = grad_probs[:, mine] * prob
            weighted = jnp.sum(product, axis=0, keepdims=True)
            probs.append(prob.astype(LOW))
            grad_scores.append((product - prob * weighted).astype(LOW))
        beside = jnp.concatenate(grad_scores, axis=1)
        grad_packed[:, pl.ds(start, 128)] = dot_left(jnp.concatenate(grad_scores, axis=0), keys_two).astype(LOW)
        grad_packed[:, pl.ds(start + width, 128)] = (dot(beside, queries_two) * scale).astype(LOW)
        grad_packed[:, pl.ds(start + 2 * width, 128)] = dot(jnp.concatenate(probs, axis=1), grads_two).astype(LOW)

    if high is not None:
        for pair in range(low, high):
            pair_of(pair)
        return

    @pl.loop(0, width // 256)
    def _(index):
        pair_of(index * 2)
        pair_of(index * 2 + 1)


def forward_kernel(cell, held, active, entry_h, rows, w_qkv, w_out, w_up, w_down, *refs):
    sent_h = refs[held]
    out_h, lowered_h, packed_h, mixed_h, middle_h, second_h, active_h, slope_h = [
        ref.at[cell] for ref in refs[held + 1 : held + 9]
    ]
    (buffers, buffer_sems, save_sems, out_v, lowered_v, packed_v, mixed_v, middle_v) = refs[held + 9 : held + 17]
    (second_v, active_v, slope_v, hidden_v, total_v, entry, entry_sem) = refs[held + 17 :]
    width = entry.shape[1]
    gains, shifts, bias = (rows.at[0:2], rows.at[2:8], rows.at[8:16])
    ups = w_up.shape[1] // width

    @pl.when(active[0] != 0)
    def _():
        heads, outer, up, down = weight_blocks(w_qkv, w_out, w_up, w_down)
        order = heads + [outer]
        place_up, place_down = ({}, {})
        for number in range(ups + 1):
            if number < ups:
                place_up[number] = len(order)
                order.append(up[number])
            if number > 0:
                place_down[number - 1] = len(order)
                order.append(down[number - 1])
        fetched = pltpu.make_async_copy(entry_h, entry, entry_sem)
        fetched.start()
        saves = []

        def save(source, target):
            saves.append(pltpu.make_async_copy(source, target, save_sems.at[len(saves)]))
            saves[-1].start()

        fetched.wait()
        stream = Stream(order, buffers, buffer_sems)
        rows_in = entry[...].astype(F32)
        normed, _ = row_norm(rows_in)
        lowered_v[...] = (normed * gains[0:1, :] + shifts[0:1, :]).astype(LOW)
        save(lowered_v, lowered_h)
        for number in range(3):
            block = stream.take(number)
            window = pl.ds(number * width, width)
            part = dot(lowered_v[...], block[...])
            if number != 1:
                part = part + shifts[1 + number // 2 : 2 + number // 2, :]
            packed_v[:, window] = part.astype(LOW)
            stream.release()
        save(packed_v, packed_h)
        attend(packed_v, mixed_v, width)
        save(mixed_v, mixed_h)
        block = stream.take(3)
        middle = entry[...].astype(F32) + dot(mixed_v[...], block[...]) + shifts[3:4, :]
        middle_v[...] = middle
        stream.release()
        save(middle_v, middle_h)
        normed, _ = row_norm(middle_v[...])
        second_v[...] = (normed * gains[1:2, :] + shifts[4:5, :]).astype(LOW)
        save(second_v, second_h)
        for number in range(ups + 1):
            if number < ups:
                up_block = stream.take(place_up[number])
            if number > 0:
                down_block = stream.take(place_down[number - 1])
            if number < ups:
                hidden_v[number % 2] = dot(second_v[...], up_block[...]) + bias[number : number + 1, :]
            if number > 0:
                window = pl.ds((number - 1) * width, width)
                activated, slope = gelu_parts(hidden_v[(number - 1) % 2])
                active_v[:, window] = activated.astype(LOW)
                slope_v[:, window] = slope.astype(LOW)
                part = dot(active_v[:, window], down_block[...])
                if number == 1:
                    total_v[...] = part
                elif number < ups:
                    total_v[...] += part
                else:
                    out_v[...] = (middle_v[...] + (total_v[...] + part + shifts[5:6, :])).astype(LOW)
                save(active_v.at[:, window], active_h.at[:, window])
                save(slope_v.at[:, window], slope_h.at[:, window])
            if number < ups:
                stream.release()
            if number > 0:
                stream.release()
        save(out_v, sent_h)
        save(out_v, out_h)
        for copy in saves:
            copy.wait()


def kept_shapes(length, width, deep):
    return [
        ((length, width), LOW),
        ((length, width), LOW),
        ((length, 3 * width), LOW),
        ((length, width), LOW),
        ((length, width), F32),
        ((length, width), LOW),
        ((length, deep), LOW),
        ((length, deep), LOW),
    ]


def forward_tick(active, entry, rows, weights, kept, cell, cell_count):
    length, width = entry.shape
    deep = weights[2].shape[1]
    ups = deep // width
    shapes = kept_shapes(length, width, deep)
    outs = [jax.ShapeDtypeStruct(*shapes[0])] + [
        jax.ShapeDtypeStruct((cell_count,) + shape, kind) for shape, kind in shapes
    ]
    vmem, hbm = (pl.BlockSpec(memory_space=pltpu.VMEM), pl.BlockSpec(memory_space=pl.ANY))
    flops = 2 * length * width * (4 * width + 2 * deep) + 16 * length * length * width
    kept = () if kept is None else tuple(kept)
    held = len(kept)
    sent, *kept = pl.pallas_call(
        functools.partial(forward_kernel, cell, held),
        out_shape=outs,
        in_specs=[pl.BlockSpec(memory_space=pltpu.SMEM), hbm, vmem] + [hbm] * (4 + held),
        out_specs=[hbm] * 9,
        input_output_aliases={7 + number: 1 + number for number in range(held)},
        scratch_shapes=[
            pltpu.VMEM((4, width, width), LOW),
            pltpu.SemaphoreType.DMA((4,)),
            pltpu.SemaphoreType.DMA((7 + 2 * ups,)),
        ]
        + [pltpu.VMEM(*shape) for shape in shapes]
        + [
            pltpu.VMEM((2, length, width), F32),
            pltpu.VMEM((length, width), F32),
            pltpu.VMEM((length, width), LOW),
            pltpu.SemaphoreType.DMA,
        ],
        compiler_params=pltpu.CompilerParams(vmem_limit_bytes=60 * 2**20),
        cost_estimate=pl.CostEstimate(
            flops=flops, bytes_accessed=2 * width * (4 * width + 2 * deep), transcendentals=0
        ),
    )(active, entry, rows, *weights, *kept)
    return (sent, kept)


def backward_kernel(cell, held, active, scale, grad_h, entry_h, rows, *refs):
    packed, middle, slope = [ref.at[cell] for ref in refs[:3]]
    w_qkv, w_out, w_up, w_down = refs[3:7]
    refs = refs[7 + held :]
    sent_h = refs[0]
    rows_h, packed_h, branch_h, inner_h, low_h, sums_h = [ref.at[cell] for ref in refs[1:7]]
    (buffers, buffer_sems, load_sems, save_sems, rows_v, grad_packed_v, branch_v, inner_v, low_v, sums_v) = refs[7:17]
    (packed_v, middle_v, slope_v, mixed_v, grad_act_v, total_v, grad_middle_v, grad, entry) = refs[17:]
    gains = rows.at[0:2]
    length, width = entry.shape
    ups = w_up.shape[1] // width

    @pl.when(active[0] != 0)
    def _():
        heads, outer, up, down = weight_blocks(w_qkv, w_out, w_up, w_down)
        loads = [
            pltpu.make_async_copy(slope, slope_v, load_sems.at[0]),
            pltpu.make_async_copy(middle, middle_v, load_sems.at[1]),
            pltpu.make_async_copy(packed, packed_v, load_sems.at[2]),
            pltpu.make_async_copy(grad_h, grad, load_sems.at[3]),
            pltpu.make_async_copy(entry_h, entry, load_sems.at[4]),
        ]
        loads[3].start()
        order, place_up, place_down = ([], {}, {})
        for number in range(ups + 1):
            if number < ups:
                place_down[number] = len(order)
                order.append(down[number])
            if number > 0:
                place_up[number - 1] = len(order)
                order.append(up[number - 1])
        place_out = len(order)
        order = order + [outer] + heads
        saves = []

        def save(source, target):
            saves.append(pltpu.make_async_copy(source, target, save_sems.at[len(saves)]))
            saves[-1].start()

        def column_sum(array):
            return jnp.sum(array.astype(F32), axis=0, keepdims=True)

        loads[3].wait()
        stream = Stream(order, buffers, buffer_sems)
        loads[0].start()
        low_v[...] = (grad[...].astype(F32) * scale[0]).astype(LOW)
        save(low_v, low_h)
        sums_v[7:8, :] = column_sum(low_v[...])
        for number in range(ups + 1):
            if number == 1:
                loads[0].wait()
                loads[1].start()
            if number == 2:
                loads[2].start()
                loads[4].start()
            if number < ups:
                down_block = stream.take(place_down[number])
            if number > 0:
                up_block = stream.take(place_up[number - 1])
            if number < ups:
                grad_act_v[number % 2] = dot_right(low_v[...], down_block[...])
            if number > 0:
                window = pl.ds((number - 1) * width, width)
                inner = (grad_act_v[(number - 1) % 2] * slope_v[:, window].astype(F32)).astype(LOW)
                inner_v[:, window] = inner
                sums_v[7 + number : 8 + number, :] = column_sum(inner)
                part = dot_right(inner, up_block[...])
                if number == 1:
                    total_v[...] = part
                else:
                    total_v[...] += part
                save(inner_v.at[:, window], inner_h.at[:, window])
            if number < ups:
                stream.release()
            if number > 0:
                stream.release()
        loads[1].wait()
        normed, inverse = row_norm(middle_v[...])
        grad_second = total_v[...]
        sums_v[1:2, :] = column_sum(grad_second * normed)
        sums_v[6:7, :] = column_sum(grad_second)
        grad_middle = grad[...].astype(F32) * scale[0] + norm_back(grad_second * gains[1:2, :], normed, inverse)
        grad_middle_v[...] = grad_middle
        branch_v[...] = grad_middle.astype(LOW)
        sums_v[5:6, :] = column_sum(branch_v[...])
        save(branch_v, branch_h)
        block = stream.take(place_out)
        mixed_v[...] = dot_right(branch_v[...], block[...]).astype(LOW)
        stream.release()
        loads[2].wait()
        attend_back(packed_v, mixed_v, grad_packed_v, width)
        save(grad_packed_v, packed_h)
        sums_v[3:4, :] = column_sum(grad_packed_v[:, pl.ds(0, width)])
        sums_v[4:5, :] = column_sum(grad_packed_v[:, pl.ds(2 * width, width)])
        for number in range(3):
            block = stream.take(place_out + 1 + number)
            part = dot_right(grad_packed_v[:, pl.ds(number * width, width)], block[...])
            if number == 0:
                total_v[...] = part
            else:
                total_v[...] += part
            stream.release()
        loads[4].wait()
        normed, inverse = row_norm(entry[...].astype(F32))
        grad_lowered = total_v[...]
        sums_v[0:1, :] = column_sum(grad_lowered * normed)
        sums_v[2:3, :] = column_sum(grad_lowered)
        rows_v[...] = (grad_middle_v[...] + norm_back(grad_lowered * gains[0:1, :], normed, inverse)).astype(LOW)
        save(sums_v, sums_h)
        save(rows_v, sent_h)
        save(rows_v, rows_h)
        for copy in saves:
            copy.wait()


def backward_tick(active, incoming, entry, rows, saved, weights, kept, cell, cell_count):
    length, width = entry.shape
    deep = weights[2].shape[1]
    ups = deep // width
    shapes = [
        ((length, width), LOW),
        ((length, 3 * width), LOW),
        ((length, width), LOW),
        ((length, deep), LOW),
        ((length, width), LOW),
        ((16, width), F32),
    ]
    outs = [jax.ShapeDtypeStruct(*shapes[0])] + [
        jax.ShapeDtypeStruct((cell_count,) + shape, kind) for shape, kind in shapes
    ]
    vmem, hbm = (pl.BlockSpec(memory_space=pltpu.VMEM), pl.BlockSpec(memory_space=pl.ANY))
    smem = pl.BlockSpec(memory_space=pltpu.SMEM)
    flops = 2 * length * width * (4 * width + 2 * deep) + 40 * length * length * width
    kept = () if kept is None else tuple(kept)
    held = len(kept)
    grad, scale = incoming
    sent, *kept = pl.pallas_call(
        functools.partial(backward_kernel, cell, held),
        out_shape=outs,
        in_specs=[smem] * 2 + [hbm] * 2 + [vmem] + [hbm] * (7 + held),
        out_specs=[hbm] * 7,
        input_output_aliases={12 + number: 1 + number for number in range(held)},
        scratch_shapes=[
            pltpu.VMEM((4, width, width), LOW),
            pltpu.SemaphoreType.DMA((4,)),
            pltpu.SemaphoreType.DMA((5,)),
            pltpu.SemaphoreType.DMA((6 + ups,)),
        ]
        + [pltpu.VMEM(*shape) for shape in shapes]
        + [
            pltpu.VMEM((length, 3 * width), LOW),
            pltpu.VMEM((length, width), F32),
            pltpu.VMEM((length, deep), LOW),
            pltpu.VMEM((length, width), LOW),
            pltpu.VMEM((2, length, width), F32),
            pltpu.VMEM((length, width), F32),
            pltpu.VMEM((length, width), F32),
            pltpu.VMEM((length, width), LOW),
            pltpu.VMEM((length, width), LOW),
        ],
        compiler_params=pltpu.CompilerParams(vmem_limit_bytes=60 * 2**20),
        cost_estimate=pl.CostEstimate(
            flops=flops, bytes_accessed=2 * width * (4 * width + 2 * deep), transcendentals=0
        ),
    )(active, scale, grad, entry, rows, *saved, *weights, *kept)
    return (sent, kept)


def small_rows(small, rows, width, ups):
    devices, _, own = small.shape
    lane = lax.broadcasted_iota(jnp.int32, (own, width), 1)
    depth = lax.broadcasted_iota(jnp.int32, (own, width), 0)
    row = lax.broadcasted_iota(jnp.int32, (16, width), 0)
    across = lax.broadcasted_iota(jnp.int32, (16, width), 1)
    top = jnp.zeros((16, width), F32)
    for device in range(devices):
        spot = jnp.where(lane == depth + device * own, 1.0, 0.0).astype(LOW)
        top = top + dot(small[device], spot)
    rows[0:8, :] = top[0:8]
    share = devices // ups
    for block in range(ups):
        total = jnp.zeros((1, width), F32)
        for index in range(share):
            start = index * ups * own
            spot = jnp.zeros((own, width), F32)
            for up in range(ups):
                spot = spot + jnp.where(lane == depth + (start + up * own), 1.0, 0.0)
            low = start + (row - 8) * own
            inside = (row >= 8) & (row < 8 + ups) & (across >= low) & (across < low + own)
            placed = dot(small[block * share + index], spot.astype(LOW))
            total = total + jnp.sum(jnp.where(inside, placed, 0.0), axis=0, keepdims=True)
        rows[8 + block : 9 + block, :] = total


def gather_forward_kernel(chips, items, groups, cells, *refs):
    shards, inputs_h = (refs[:5], refs[5])
    outs, rows_h, arrived_h, later_h = (refs[6:11], refs[11], refs[12], refs[13])
    out_h, lowered_h, packed_h, mixed_h, middle_h, second_h, active_h, slope_h = refs[14:22]
    (ring_send, ring_recv, pair_send, pair_recv, own_sem, hop_send, hop_recv) = refs[22:29]
    (load_sem, save_sem, wide_sem, deep_sem) = refs[29:33]
    (small_v, rows_v, entry_v, out_v, lowered_v, packed_v, mixed_v, middle_v, second_v, active_v, slope_v) = refs[33:44]
    (total_v, hidden_v, wide_v, deep_v) = refs[44:]
    length, width = entry_v.shape[1:]
    ups = active_v.shape[2] // width
    half = chips // 2
    me, core, position, right, left, sibling = ring_place(chips)
    stage = lax.axis_index("pipe")
    first = stage == 0
    barrier = pltpu.get_barrier_semaphore()
    for device in (left, right, sibling):
        pl.semaphore_signal(barrier, inc=1, device_id={"dp": device}, device_id_type=MESH)
    pl.semaphore_signal(barrier, inc=1, device_id={"pipe": 1 - stage}, device_id_type=MESH)
    pl.semaphore_wait(barrier, 4)

    def shard(item):
        array, start, rows, _ = items[item]
        return shards[array].at[pl.ds(start, rows)]

    def out(item, block):
        array, start, rows, _ = items[item]
        return outs[array].at[block, pl.ds(start, rows)]

    def owner(step, way):
        return ring_chip(position - step if way == 0 else position + step, chips) * 2 + core

    def travels(item, way, step):
        return step < half or (step == half and items[item][3] == way)

    def ring_copy(item, way, step):
        block = owner(step - 1, way)
        return pltpu.make_async_remote_copy(
            src_ref=shard(item) if step == 1 else out(item, block),
            dst_ref=out(item, block),
            send_sem=ring_send.at[item, way, step - 1],
            recv_sem=ring_recv.at[item, way, step - 1],
            device_id={"dp": right if way == 0 else left},
            device_id_type=MESH,
        )

    def pair_copy(item, offset, block, source):
        return pltpu.make_async_remote_copy(
            src_ref=source,
            dst_ref=out(item, block),
            send_sem=pair_send.at[item, offset],
            recv_sem=pair_recv.at[item, offset],
            device_id={"dp": sibling},
            device_id_type=MESH,
        )

    def own_copy(item):
        return pltpu.make_async_copy(shard(item), out(item, me), own_sem.at[item])

    sent, paired = ([], [])

    def open_group(group):
        for item in group:
            for way in (0, 1):
                if travels(item, way, 1):
                    sent.append(ring_copy(item, way, 1))
                    sent[-1].start()
        for item in group:
            paired.append(pair_copy(item, 0, me, shard(item)))
            paired[-1].start()
            own_copy(item).start()

    def ring_step(item, way, step):
        ring_copy(item, way, step).wait_recv()
        if travels(item, way, step + 1):
            sent.append(ring_copy(item, way, step + 1))
            sent[-1].start()
        block = owner(step, way)
        offset = step if way == 0 else chips - step
        paired.append(pair_copy(item, offset, block, out(item, block)))
        paired[-1].start()

    def pair_arrived(item, offset):
        block = ring_chip(position - offset, chips) * 2 + core
        pair_copy(item, offset, block, out(item, block)).wait_recv()

    saves = []

    def save(source, target):
        number = len(saves)
        saves.append(lambda: pltpu.make_async_copy(source(), target(), save_sem.at[number]))
        saves[-1]().start()

    def entry_load(cell):
        return pltpu.make_async_copy(inputs_h.at[cell], entry_v.at[cell], load_sem.at[cell])

    def wide_load(array, column, slot):
        source = outs[array].at[:, :, pl.ds(column * width, width)]
        return pltpu.make_async_copy(source, wide_v.at[slot], wide_sem.at[slot])

    def wide(slot):
        return wide_v[slot].reshape(width, width)

    def gains(number):
        return rows_v[number : number + 1, :]

    def shifts(number):
        return rows_v[2 + number : 3 + number, :]

    def begin(cell):
        def step():
            entry_load(cell).wait()
            normed, _ = row_norm(entry_v[cell].astype(F32))
            lowered_v[cell] = (normed * gains(0) + shifts(0)).astype(LOW)
            save(lambda: lowered_v.at[cell], lambda: lowered_h.at[cell])

        return step

    def project(cell, number):
        def step():
            if cell == 0:
                wide_load(1, number, number).wait()
            part = dot(lowered_v[cell], wide(number))
            if number != 1:
                part = part + shifts(1 + number // 2)
            packed_v[cell, :, pl.ds(number * width, width)] = part.astype(LOW)
            if number == 2:
                save(lambda: packed_v.at[cell], lambda: packed_h.at[cell])

        return step

    def mix(cell, low, high, last):
        def step():
            attend(packed_v.at[cell], mixed_v.at[cell], width, low, high)
            if last:
                save(lambda: mixed_v.at[cell], lambda: mixed_h.at[cell])

        return step

    def join(cell):
        def step():
            if cell == 0:
                wide_load(2, 0, 3).wait()
            middle_v[cell] = entry_v[cell].astype(F32) + dot(mixed_v[cell], wide(3)) + shifts(3)
            save(lambda: middle_v.at[cell], lambda: middle_h.at[cell])

        return step

    def renorm(cell):
        def step():
            middle = middle_v[cell]
            normed, _ = row_norm(middle)
            second_v[cell] = (normed * gains(1) + shifts(4)).astype(LOW)
            total_v[cell] = middle + shifts(5)
            save(lambda: second_v.at[cell], lambda: second_h.at[cell])

        return step

    def rise(cell, number):
        def step():
            if cell == 0:
                wide_load(3, number, number).wait()
            hidden_v[...] = dot(second_v[cell], wide(number)) + rows_v[8 + number : 9 + number, :]

        return step

    def bend(cell, number):
        def step():
            window = pl.ds(number * width, width)
            activated, slope = gelu_parts(hidden_v[...])
            active_v[cell, :, window] = activated.astype(LOW)
            slope_v[cell, :, window] = slope.astype(LOW)
            if number == ups - 1:
                save(lambda: active_v.at[cell], lambda: active_h.at[cell])
                save(lambda: slope_v.at[cell], lambda: slope_h.at[cell])

        return step

    deep_rows = deep_v.shape[1] * deep_v.shape[2]

    def deep_load(offset, slot):
        chip = ring_chip(position - offset, chips)
        return pltpu.make_async_copy(outs[4].at[pl.ds(chip * 2, 2)], deep_v.at[slot], deep_sem.at[slot])

    def fall(cell, offset, slot):
        def step():
            if cell == 0:
                deep_load(offset, slot).wait()
            chip = ring_chip(position - offset, chips)
            window = pl.ds(pl.multiple_of(chip * deep_rows, 128), deep_rows)
            total_v[cell] += dot(active_v[cell, :, window], deep_v[slot].reshape(deep_rows, width))

        return step

    def hop():
        return pltpu.make_async_remote_copy(
            src_ref=out_v.at[0],
            dst_ref=arrived_h,
            send_sem=hop_send,
            recv_sem=hop_recv,
            device_id={"pipe": 1 - stage},
            device_id_type=MESH,
        )

    def finish(cell):
        def step():
            out_v[cell] = total_v[cell].astype(LOW)
            if cell == 0:
                hop().start()
            else:
                save(lambda: out_v.at[cell], lambda: later_h)
            save(lambda: out_v.at[cell], lambda: out_h.at[cell])

        return step

    def on_first(step):
        pl.when(first)(step)

    queue = []

    def ready(group, steps, loads):
        for item in group:
            own_copy(item).wait()
            for offset in range(chips):
                pair_arrived(item, offset)

        @pl.when(first)
        def _():
            for load in loads:
                load().start()

        queue.extend(steps)

    pairs = width // 128
    heads = []
    for cell in range(cells):
        heads.append(begin(cell))
        heads += [project(cell, number) for number in range(3)]
        heads += [mix(cell, low, low + 2, low + 2 >= pairs) for low in range(0, pairs, 2)]
    joins = [make(cell) for cell in range(cells) for make in (join, renorm)]
    def load_ups():
        for number in range(ups):
            wide_load(3, number, number).start()

    climbs = [load_ups]
    climbs += [make(cell, number) for number in range(ups) for cell in range(cells) for make in (rise, bend)]

    @pl.when(first)
    def _():
        for cell in range(cells):
            entry_load(cell).start()

    def lay_rows():
        copy = pltpu.make_async_copy(outs[0], small_v, load_sem.at[cells])
        copy.start()
        copy.wait()
        small_rows(small_v, rows_v, width, ups)
        pltpu.make_async_copy(rows_v, rows_h, load_sem.at[cells + 1]).start()

    def ready_small():
        for item in groups[0]:
            if items[item][0] == 0:
                own_copy(item).wait()
                for offset in range(chips):
                    pair_arrived(item, offset)
        lay_rows()

    plan = []
    for number, group in enumerate(groups):
        for step in range(1, half + 1):
            if step == half and number + 1 < len(groups):
                plan.append(("open", number + 1))
            for item in group:
                for way in (0, 1):
                    if travels(item, way, step):
                        plan.append(("ring", item, way, step))
            if number == len(groups) - 1:
                plan.append(("deep", step))
        plan.append(("done", number))
    open_group(groups[0])
    late = []
    slots = [0]

    def deep_ready(offsets):
        for offset in offsets:
            for item in groups[-1]:
                if offset == 0:
                    own_copy(item).wait()
                pair_arrived(item, offset)
            slot = slots[0] % deep_v.shape[0]
            slots[0] += 1

            def opening(offset=offset, slot=slot):
                deep_load(offset, slot).start()

            queue.append(opening)
            queue.extend(fall(cell, offset, slot) for cell in range(cells))

    def serve(limit):
        for _ in range(limit):
            if queue:
                on_first(queue.pop(0))

    for entry in plan:
        if entry[0] == "open":
            open_group(groups[entry[1]])
        elif entry[0] == "ring":
            ring_step(*entry[1:])
            for wait in list(late):
                wait[0] -= 1
                if wait[0] == 0:
                    wait[1]()
                    late.remove(wait)
            serve(3 if entry[1] in groups[-1] else 2)
        elif entry[0] == "done":
            if entry[1] == 0:
                rest = [item for item in groups[0] if items[item][0] != 0]
                late.append([1, ready_small])
                late.append(
                    [
                        2,
                        lambda: ready(
                            rest,
                            heads + joins,
                            [functools.partial(wide_load, 1, number, number) for number in range(3)]
                            + [functools.partial(wide_load, 2, 0, 3)],
                        ),
                    ]
                )
            elif entry[1] == 1:
                late.append([2, lambda: ready(groups[1], climbs, [])])
        elif entry[0] == "deep":
            step = entry[1]
            if step == 1:
                late.append([3, lambda: deep_ready([0])])
            if step < half:
                late.append([2, lambda step=step: deep_ready([step, chips - step])])
            else:
                for wait in late:
                    wait[1]()
                serve(len(queue))
                deep_ready([half])
    serve(len(queue))
    for cell in range(cells):
        on_first(finish(cell))
    for copy in sent:
        copy.wait_send()
    for copy in paired:
        copy.wait_send()
    pltpu.make_async_copy(rows_v, rows_h, load_sem.at[cells + 1]).wait()

    @pl.when(first)
    def _():
        for copy in saves:
            copy().wait()
        hop().wait_send()

    @pl.when(jnp.logical_not(first))
    def _():
        hop().wait_recv()


def gather_forward(shards, inputs, items, groups, count):
    chips = count // 2
    cells, length, width = inputs.shape
    deep = shards[3].shape[1]
    ups = deep // width
    pieces = len(items)
    shapes = kept_shapes(length, width, deep)
    hbm = pl.BlockSpec(memory_space=pl.ANY)
    flops = 2 * cells * length * width * (4 * width + 2 * deep)
    outs = pl.pallas_call(
        functools.partial(gather_forward_kernel, chips, items, groups, cells),
        out_shape=[jax.ShapeDtypeStruct((count,) + shard.shape, shard.dtype) for shard in shards]
        + [
            jax.ShapeDtypeStruct((16, width), F32),
            jax.ShapeDtypeStruct((length, width), LOW),
            jax.ShapeDtypeStruct((length, width), LOW),
        ]
        + [jax.ShapeDtypeStruct((cells,) + shape, kind) for shape, kind in shapes],
        in_specs=[hbm] * 6,
        out_specs=[hbm] * 16,
        scratch_shapes=[
            pltpu.SemaphoreType.DMA((pieces, 2, chips // 2)),
            pltpu.SemaphoreType.DMA((pieces, 2, chips // 2)),
            pltpu.SemaphoreType.DMA((pieces, chips)),
            pltpu.SemaphoreType.DMA((pieces, chips)),
            pltpu.SemaphoreType.DMA((pieces,)),
            pltpu.SemaphoreType.DMA,
            pltpu.SemaphoreType.DMA,
            pltpu.SemaphoreType.DMA((cells + 2,)),
            pltpu.SemaphoreType.DMA((9 * cells,)),
            pltpu.SemaphoreType.DMA((4,)),
            pltpu.SemaphoreType.DMA((2,)),
            pltpu.VMEM((count,) + shards[0].shape, LOW),
            pltpu.VMEM((16, width), F32),
            pltpu.VMEM((cells, length, width), LOW),
        ]
        + [pltpu.VMEM((cells,) + shape, kind) for shape, kind in shapes]
        + [
            pltpu.VMEM((cells, length, width), F32),
            pltpu.VMEM((length, width), F32),
            pltpu.VMEM((4, count, width // count, width), LOW),
            pltpu.VMEM((2, 2, shards[4].shape[0], width), LOW),
        ],
        compiler_params=pltpu.CompilerParams(
            collective_id=3, has_side_effects=True, vmem_limit_bytes=62 * 2**20
        ),
        cost_estimate=pl.CostEstimate(flops=flops, bytes_accessed=8 * width * (4 * width + 2 * deep), transcendentals=0),
    )(*shards, inputs)
    return (outs[:5], outs[5], outs[6], outs[7], list(outs[8:]))


class RingSum:
    def __init__(self, chips, items, parts, outs, landed, paired, buffers, final, sems):
        self.chips, self.items, self.parts, self.outs = (chips, items, parts, outs)
        self.landed, self.paired, self.final = (landed, paired, final)
        self.mine, self.pairs, self.rings = buffers
        self.ring_send, self.ring_recv, self.pair_send, self.pair_recv, self.load_sem, self.final_sem = sems
        self.half = chips // 2
        self.me, self.core, self.position, self.right, self.left, self.sibling = ring_place(chips)
        self.sent, self.final_copies, self.exchanged = ({}, [], [])
        self.uses = [0] * len(items)

    def part(self, item, block):
        array, start, rows, _ = self.items[item]
        return self.parts[array].at[block, pl.ds(start, rows)]

    def first(self, item, way):
        return 1 if self.items[item][3] == way else 2

    def slot_of(self, item, way, step):
        return step - 1 if self.items[item][3] == way else self.half + step - 2

    def offset_of(self, step, way):
        return self.half - step + 1 if way == 0 else self.chips - (self.half - step + 1)

    def pair_copy(self, item, offset):
        block = ring_chip(self.position + offset, self.chips) * 2 + 1 - self.core
        return pltpu.make_async_remote_copy(
            src_ref=self.part(item, block),
            dst_ref=self.paired[item].at[offset],
            send_sem=self.pair_send.at[item, offset],
            recv_sem=self.pair_recv.at[item, offset],
            device_id={"dp": self.sibling},
            device_id_type=MESH,
        )

    def ring_copy(self, item, way, step, buffer=0):
        here = self.slot_of(item, way, step)
        return pltpu.make_async_remote_copy(
            src_ref=self.mine[item].at[buffer],
            dst_ref=self.landed[item].at[here],
            send_sem=self.ring_send.at[item, here],
            recv_sem=self.ring_recv.at[item, here],
            device_id={"dp": self.right if way == 0 else self.left},
            device_id_type=MESH,
        )

    def load_mine(self, item, offset, buffer):
        block = ring_chip(self.position + offset, self.chips) * 2 + self.core
        return pltpu.make_async_copy(self.part(item, block), self.mine[item].at[buffer], self.load_sem.at[item, buffer])

    def load_pair(self, item, offset, buffer):
        return pltpu.make_async_copy(
            self.paired[item].at[offset], self.pairs[item].at[buffer], self.load_sem.at[item, 2 + buffer]
        )

    def load_ring(self, item, way, step, buffer):
        return pltpu.make_async_copy(
            self.landed[item].at[self.slot_of(item, way, step)], self.rings[item].at[buffer], self.load_sem.at[item, 4 + buffer]
        )

    def exchange(self, wanted, offsets):
        for offset in offsets:
            for item in wanted:
                self.pair_copy(item, offset).start()
                self.exchanged.append((item, offset))

    def starts(self, wanted):
        return [
            (step, item, way, self.offset_of(step, way))
            for step in (1, 2)
            for item in wanted
            for way in (0, 1)
            if step == self.first(item, way)
        ]

    def rest(self, wanted, steps):
        return [
            (step, item, way, self.offset_of(step, way))
            for step in steps
            if step <= self.half
            for item in wanted
            for way in (0, 1)
            if step > self.first(item, way)
        ] + [(step, item, None, 0) for step in steps if step > self.half for item in wanted]

    def fetch(self, entry):
        step, item, way, offset, buffer = entry
        if (item, buffer) in self.sent:
            self.sent.pop((item, buffer)).wait_send()
        self.load_mine(item, offset, buffer).start()
        self.pair_copy(item, offset).wait_recv()
        self.load_pair(item, offset, buffer).start()

    def run(self, plan, between=None):
        numbered = []
        for entry in plan:
            numbered.append(entry + (self.uses[entry[1]] % 2,))
            self.uses[entry[1]] += 1
        for number, entry in enumerate(numbered):
            if number == 0:
                self.fetch(entry)
            if number + 1 < len(numbered):
                self.fetch(numbered[number + 1])
            self.work(entry)
            if between is not None:
                between()

    def work(self, entry):
        step, item, way, offset, buffer = entry
        array, start, rows, _ = self.items[item]
        half, final = (self.half, self.final)
        kind = self.parts[array].dtype
        columns = self.parts[array].shape[2]
        chunk = 16
        mine, pairs, rings = (self.mine[item], self.pairs[item], self.rings[item])
        if way is None:
            for side in (0, 1):
                self.ring_copy(item, side, half).wait_recv()
                self.load_ring(item, side, half, side).start()
            self.load_mine(item, offset, buffer).wait()
            self.load_pair(item, offset, buffer).wait()
            for side in (0, 1):
                self.load_ring(item, side, half, side).wait()
            if kind == F32:
                self.outs[array][...] = (rings[0] + rings[1]) + (mine[buffer] + pairs[buffer])
                return
            high, wide = (min(rows, final.shape[1]), min(columns, final.shape[2]))
            for top in range(0, rows, high):
                for across in range(0, columns, wide):
                    number = len(self.final_copies)
                    turn = number % final.shape[0]
                    if number >= final.shape[0]:
                        self.final_copies[number - final.shape[0]].wait()
                    span = pl.ds(across, wide)

                    @pl.loop(0, high // chunk)
                    def _(index):
                        here = pl.ds(pl.multiple_of(top + index * chunk, chunk), chunk)
                        final[turn, pl.ds(pl.multiple_of(index * chunk, chunk), chunk), pl.ds(0, wide)] = (
                            rings[0, here, span].astype(F32) + rings[1, here, span].astype(F32)
                        ) + (mine[buffer, here, span].astype(F32) + pairs[buffer, here, span].astype(F32))

                    self.final_copies.append(
                        pltpu.make_async_copy(
                            final.at[turn, pl.ds(0, high), pl.ds(0, wide)],
                            self.outs[array].at[pl.ds(start + top, high), span],
                            self.final_sem.at[turn],
                        )
                    )
                    self.final_copies[-1].start()
            return
        carried = step > self.first(item, way)
        if carried:
            self.ring_copy(item, way, step - 1).wait_recv()
            self.load_ring(item, way, step - 1, buffer).start()
        self.load_mine(item, offset, buffer).wait()
        self.load_pair(item, offset, buffer).wait()
        if carried:
            self.load_ring(item, way, step - 1, buffer).wait()

        @pl.loop(0, rows // chunk)
        def _(index):
            here = pl.ds(pl.multiple_of(index * chunk, chunk), chunk)
            total = mine[buffer, here, :].astype(F32) + pairs[buffer, here, :].astype(F32)
            if carried:
                total = rings[buffer, here, :].astype(F32) + total
            mine[buffer, here, :] = total.astype(kind)

        copy = self.ring_copy(item, way, step, buffer)
        copy.start()
        self.sent[(item, buffer)] = copy

    def close(self):
        for copy in self.sent.values():
            copy.wait_send()
        for item, offset in self.exchanged:
            self.pair_copy(item, offset).wait_send()
        for copy in self.final_copies[-self.final.shape[0] :]:
            copy.wait()


class Products:
    def __init__(self, chips, width, own, cuts, big, stage, cut_sem, big_sem, stage_sem):
        self.chips, self.width, self.own = (chips, width, own)
        self.cuts, self.big, self.stage = (cuts, big, stage)
        self.cut_sem, self.big_sem, self.stage_sem = (cut_sem, big_sem, stage_sem)

    def load_cut(self, source, index, slot):
        cut = self.cuts.shape[2]
        window = pl.ds(pl.multiple_of(index * cut, cut), cut)
        return pltpu.make_async_copy(source.at[:, window], self.cuts.at[slot], self.cut_sem.at[slot])

    def block(self, source, index, slot):
        window = pl.ds(pl.multiple_of(index * self.width, self.width), self.width)
        return pltpu.make_async_copy(source.at[:, window], self.big.at[slot], self.big_sem.at[slot])

    def keep(self, target, index):
        window = pl.ds(pl.multiple_of(index // 2 * self.width, self.width), self.width)
        return pltpu.make_async_copy(
            self.stage.at[lax.rem(index, 2)],
            target.at[pl.ds(lax.rem(index, 2) * self.chips, self.chips), :, window],
            self.stage_sem.at[lax.rem(index, 2)],
        )

    def open(self, left, right, slot):
        for index in (0, 1):
            self.load_cut(left, index, index).start()
        self.block(right, 0, slot).start()

    def run(self, target, left, right, shift, low, high):
        number = 2 * (right.shape[1] // self.width)
        if low == 0:
            for index in (0, 1):
                self.load_cut(left, index, index).wait()

        @pl.loop(low, high)
        def _(index):
            slot = lax.rem(index, 2)
            here = lax.rem(index // 2 + shift, 2)

            @pl.when(slot == 0)
            def _():
                self.block(right, index // 2, here).wait()

                @pl.when(index + 2 < number)
                def _():
                    self.block(right, index // 2 + 1, 1 - here).start()

            @pl.when(index >= low + 2)
            def _():
                self.keep(target, index - 2).wait()

            product = dot_left(self.cuts[slot], self.big[here]).astype(LOW)
            for device in range(self.chips):
                self.stage[slot, device] = product[device * self.own : (device + 1) * self.own]
            self.keep(target, index).start()

        for index in range(max(low, high - 2), high):
            self.keep(target, index).wait()


def last_backward_kernel(chips, items, cell, *refs):
    count = len(items)
    (grad_h, entry_h, rows, packed_h, middle_h, slope_h, w_qkv, w_out, w_up, w_down) = refs[:10]
    (activated_h, grad_ff_h, second_h, mixed_h, lowered_h) = refs[10:15]
    refs = refs[15 + 5 :]
    rows_o, packed_o, branch_o, inner_o, sums_o = refs[:5]
    outs, parts = (refs[5:10], refs[10:14])
    landed, paired = (refs[14 : 14 + count], refs[14 + count : 14 + 2 * count])
    refs = refs[14 + 2 * count :]
    ring_buffers = (refs[:count], refs[count : 2 * count], refs[2 * count : 3 * count])
    final, small_v, both_v = refs[3 * count : 3 * count + 3]
    sems = refs[3 * count + 3 : 3 * count + 9]
    refs = refs[3 * count + 9 :]
    (big, cuts, stage, stage_down, big_sem, cut_sem, stage_sem) = refs[:7]
    (buffers, buffer_sems, load_sems, save_sems, slope_sems, inner_sems) = refs[7:13]
    (grad, entry, packed_v, middle_v, slope_v, inner_v, grad_packed_v, mixed_v, branch_v, grad_act_v, total_v, sums_v) = refs[13:]
    parts = [small_v] + list(parts)
    down_part, up_part = (parts[4], parts[3])
    length, width = grad.shape
    devices = 2 * chips
    deep_own = down_part.shape[1]
    ups = w_up.shape[1] // width
    first = lax.axis_index("pipe") == 0
    ring = RingSum(chips, items, parts, outs, landed, paired, ring_buffers, final, sems)
    half, position = (ring.half, ring.position)
    products = Products(chips, width, width // devices, cuts, big, stage, cut_sem, big_sem, stage_sem)
    gains = rows.at[0:2]

    def farthest_first(index):
        step = index // 2
        return ring_chip(position + jnp.where(lax.rem(index, 2) == 0, half - step, half + step + 1), chips)

    def keep_down(index):
        return pltpu.make_async_copy(
            stage_down.at[lax.rem(index, 2)],
            down_part.at[pl.ds(farthest_first(index) * 2, 2)],
            stage_sem.at[2 + lax.rem(index, 2)],
        )

    def cut_down(index):
        return products.load_cut(activated_h, farthest_first(index), lax.rem(index, 2))

    def down_products(low, high):
        @pl.loop(low, high)
        def _(index):
            slot = lax.rem(index, 2)

            @pl.when(index + 1 < chips)
            def _():
                cut_down(index + 1).start()

            cut_down(index).wait()

            @pl.when(index >= low + 2)
            def _():
                keep_down(index - 2).wait()

            product = dot_left(cuts[slot], big[0]).astype(LOW)
            for side in (0, 1):
                stage_down[slot, side] = product[side * deep_own : (side + 1) * deep_own]
            keep_down(index).start()

        for index in range(max(low, high - 2), high):
            keep_down(index).wait()

    def here(ref, at):
        return ref.at[pl.ds(at * length, length)]

    def ff_load(at):
        return pltpu.make_async_copy(here(grad_ff_h, at), here(big.at[0], at), load_sems.at[at])

    def ff_arrived():
        return pltpu.make_async_copy(grad_h, here(big.at[0], cell), load_sems.at[cell])

    for at in range(cell):
        ff_load(at).start()
    pl.when(first)(lambda: ff_arrived().start())
    pl.when(jnp.logical_not(first))(lambda: ff_load(cell).start())
    cut_down(0).start()

    def own_load(number):
        source, target = (
            (grad_h, grad),
            (entry_h, entry),
            (middle_h.at[cell], middle_v),
            (packed_h.at[cell], packed_v),
        )[number]
        return pltpu.make_async_copy(source, target, load_sems.at[cell + 1 + number])

    def slope_load(number):
        window = pl.ds(number * width, width)
        return pltpu.make_async_copy(
            slope_h.at[cell].at[:, window], slope_v.at[number % 2], slope_sems.at[number % 2]
        )

    order, place_up, place_down = ([], {}, {})
    for number in range(ups + 1):
        if number < ups:
            place_down[number] = len(order)
            order.append((w_down, 0, number))
        if number > 0:
            place_up[number - 1] = len(order)
            order.append((w_up, 1, number - 1))
    place_out = len(order)
    order = order + [(w_out, 0, 0)] + [(w_qkv, 1, number) for number in range(3)]
    depth = buffers.shape[0]

    def weight_load(number):
        ref, axis, at = order[number]
        window = pl.ds(at * width, width)
        source = ref.at[:, window] if axis else ref.at[window, :]
        return pltpu.make_async_copy(source, buffers.at[number % depth], buffer_sems.at[number % depth])

    def take(number):
        weight_load(number).wait()
        return buffers.at[number % depth]

    def release(number):
        if number + depth < len(order):
            weight_load(number + depth).start()

    def save(number, wait=False):
        source, target = (
            (branch_v, branch_o.at[pl.ds(cell * length, length)]),
            (grad_packed_v, packed_o.at[pl.ds(cell * length, length)]),
            (sums_v, sums_o.at[cell]),
            (mixed_v, rows_o.at[cell]),
        )[number]
        copy = pltpu.make_async_copy(source, target, save_sems.at[number])
        copy.wait() if wait else copy.start()

    def inner_save(number):
        window = pl.ds(number * width, width)
        return pltpu.make_async_copy(
            inner_v.at[number % 2], inner_o.at[pl.ds(cell * length, length), window], inner_sems.at[number % 2]
        )

    def column_sum(array):
        return jnp.sum(array.astype(F32), axis=0, keepdims=True)

    def begin():
        own_load(0).start()
        slope_load(0).start()
        for number in range(depth):
            weight_load(number).start()
        for number in (1, 2, 3):
            own_load(number).start()
        own_load(0).wait()
        sums_v[7:8, :] = column_sum(grad[...])

    def climb(number):
        def step():
            if number < ups:
                down_block = take(place_down[number])
                grad_act_v[number % 2] = dot_right(grad[...], down_block[...])
                release(place_down[number])
            if number > 0:
                at = number - 1
                slope_load(at).wait()
                if at + 1 < ups:
                    slope_load(at + 1).start()
                up_block = take(place_up[at])
                if at >= 2:
                    inner_save(at - 2).wait()
                inner = (grad_act_v[at % 2] * slope_v[at % 2].astype(F32)).astype(LOW)
                inner_v[at % 2] = inner
                sums_v[8 + at : 9 + at, :] = column_sum(inner)
                part = dot_right(inner, up_block[...])
                if at == 0:
                    total_v[...] = part
                else:
                    total_v[...] += part
                inner_save(at).start()
                release(place_up[at])

        return step

    def turn():
        own_load(2).wait()
        normed, inverse = row_norm(middle_v[...])
        grad_second = total_v[...]
        sums_v[1:2, :] = column_sum(grad_second * normed)
        sums_v[6:7, :] = column_sum(grad_second)
        grad_middle = grad[...].astype(F32) + norm_back(grad_second * gains[1:2, :], normed, inverse)
        middle_v[...] = grad_middle
        branch_v[...] = grad_middle.astype(LOW)
        sums_v[5:6, :] = column_sum(branch_v[...])
        save(0)
        save(0, wait=True)
        for at in range(max(0, ups - 2), ups):
            inner_save(at).wait()

    def outer():
        block = take(place_out)
        mixed_v[...] = dot_right(branch_v[...], block[...]).astype(LOW)
        release(place_out)
        own_load(3).wait()

    def heads(low, high):
        def step():
            attend_back(packed_v, mixed_v, grad_packed_v, width, low, high)

        return step

    def sums():
        save(1)
        sums_v[3:4, :] = column_sum(grad_packed_v[:, pl.ds(0, width)])
        sums_v[4:5, :] = column_sum(grad_packed_v[:, pl.ds(2 * width, width)])
        save(1, wait=True)

    def lower(number):
        def step():
            block = take(place_out + 1 + number)
            part = dot_right(grad_packed_v[:, pl.ds(number * width, width)], block[...])
            if number == 0:
                total_v[...] = part
            else:
                total_v[...] += part
            release(place_out + 1 + number)

        return step

    def finish():
        own_load(1).wait()
        normed, inverse = row_norm(entry[...].astype(F32))
        grad_lowered = total_v[...]
        sums_v[0:1, :] = column_sum(grad_lowered * normed)
        sums_v[2:3, :] = column_sum(grad_lowered)
        mixed_v[...] = (middle_v[...] + norm_back(grad_lowered * gains[0:1, :], normed, inverse)).astype(LOW)
        save(2)
        save(3)

    def lay_small():
        @pl.when(first)
        def _():
            save(2, wait=True)

        copy = pltpu.make_async_copy(sums_o, both_v, load_sems.at[0])
        copy.start()
        copy.wait()
        sums = both_v[0]
        for at in range(1, cell + 1):
            sums = sums + both_v[at]
        own = width // devices
        windows = [pltpu.roll(sums, (width - at * own) % width, 1)[:, :own] for at in range(devices)]
        share = devices // ups
        for device in range(devices):
            small_v[device, 0:8, :] = windows[device][0:8]
            for up in range(ups):
                row = 8 + device // share
                small_v[device, 8 + up : 9 + up, :] = windows[device % share * ups + up][row : row + 1]
            small_v[device, 8 + ups : 16, :] = jnp.zeros((8 - ups, own), F32)

    pairs = width // 128
    head_blocks = packed_o.shape[1] // width
    downs = [item for item in range(count) if items[item][0] == 4]
    up_items = [item for item in range(count) if items[item][0] == 3]
    outers = [item for item in range(count) if items[item][0] == 2]
    head_items = [item for item in range(count) if items[item][0] == 1]
    smalls = [item for item in range(count) if items[item][0] == 0]
    far = [half, half - 1, half + 1]
    near = [offset for offset in range(chips) if offset not in far]
    everywhere = far + near

    def work(*steps):
        for step in steps:
            pl.when(first)(step)

    def up_products(low, high):
        products.run(up_part, second_h, inner_o, 1, low, high)

    def head_products(low, high):
        products.run(parts[1], lowered_h, packed_o, 0, low, high)

    greet((ring.left, ring.right, ring.sibling))
    for at in range(cell + 1):
        ff_load(at).wait()
    down_products(0, 3)
    ring.exchange(downs, far)
    down_products(3, 5)
    work(begin)
    ring.run(ring.starts(downs))
    down_products(5, chips)
    ring.exchange(downs, near)
    later = [climb(number) for number in range(ups + 1)] + [turn]

    def between():
        if later:
            work(later.pop(0))

    work(later.pop(0), later.pop(0))
    ring.run(ring.rest(downs, (2,)), between)
    ring.run(ring.rest(downs, (3,)), between)
    while later:
        between()
    products.open(second_h, inner_o, 1)
    up_products(0, ups)
    ring.run(ring.rest(downs, (4,))[:2])
    up_products(ups, 2 * ups)
    ring.exchange(up_items, everywhere)
    products.open(mixed_h, branch_o, 1)
    ring.run(ring.rest(downs, (4,))[2:])
    products.run(parts[2], mixed_h, branch_o, 1, 0, 2)
    ring.exchange(outers, everywhere)
    ring.run(ring.starts(up_items))
    later = [outer] + [heads(low, low + 2) for low in range(0, pairs, 2)] + [sums]
    work(later.pop(0), later.pop(0))
    ring.run(ring.starts(outers), between)
    ring.run(ring.rest(up_items + outers, (2,)), between)
    while later:
        between()
    products.open(lowered_h, packed_o, 0)
    head_products(0, head_blocks)
    ring.run(ring.rest(up_items + outers, (3,))[:2])
    head_products(head_blocks, 2 * head_blocks)
    ring.exchange(head_items, everywhere)
    ring.run(ring.rest(up_items + outers, (3,))[2:])
    ring.run(ring.starts(head_items))
    later = [lower(number) for number in range(3)] + [finish]
    ring.run(ring.rest(head_items, (2,)), between)
    while later:
        between()
    lay_small()
    ring.exchange(smalls, everywhere)
    ring.run(ring.rest(up_items + outers, (4,)))
    ring.run(ring.starts(smalls))
    ring.run(ring.rest(head_items, (3,)))
    ring.run(ring.rest(smalls, (2, 3)))
    ring.run(ring.rest(downs + up_items, (half + 1,)))
    ring.run(ring.rest(smalls + head_items, (4,)))
    ring.run(ring.rest(outers + smalls + head_items, (half + 1,)))
    ring.close()

    @pl.when(first)
    def _():
        save(3, wait=True)


def last_backward(arrived, entry, rows, saved, weights, kept, sides, items, shapes, count):
    chips = count // 2
    length, width = arrived.shape
    deep = weights[2].shape[1]
    cells = kept[0].shape[0]
    rows_in = cells * length
    own = width // count
    hbm = pl.BlockSpec(memory_space=pl.ANY)
    cut = width // 2
    wholes = [(16, own)] + [tuple(shape) for shape in shapes]
    held = [(many,) + wholes[array][1:] for array, _, many, _ in items]
    kinds = [F32 if array == 0 else LOW for array, _, _, _ in items]
    pieces = len(items)
    flops = 2 * length * width * (4 * width + 2 * deep) + 2 * rows_in * width * (4 * width + 2 * deep)
    outs = pl.pallas_call(
        functools.partial(last_backward_kernel, chips, items, cells - 1),
        out_shape=[jax.ShapeDtypeStruct(array.shape, array.dtype) for array in kept]
        + [jax.ShapeDtypeStruct(shape, F32) for shape in wholes]
        + [jax.ShapeDtypeStruct((count,) + shape, LOW) for shape in wholes[1:]]
        + [jax.ShapeDtypeStruct((chips - 1,) + shape, kind) for shape, kind in zip(held, kinds)]
        + [jax.ShapeDtypeStruct((chips,) + shape, kind) for shape, kind in zip(held, kinds)],
        in_specs=[hbm] * 2 + [pl.BlockSpec(memory_space=pltpu.VMEM)] + [hbm] * 17,
        out_specs=[hbm] * 5 + [pl.BlockSpec(memory_space=pltpu.VMEM)] + [hbm] * (8 + 2 * pieces),
        input_output_aliases={15 + number: number for number in range(5)},
        scratch_shapes=[pltpu.VMEM((2,) + shape, kind) for shape, kind in zip(held, kinds)] * 3
        + [
            pltpu.VMEM((4, 80, width), F32),
            pltpu.VMEM((count, 16, own), F32),
            pltpu.VMEM((cells, 16, width), F32),
            pltpu.SemaphoreType.DMA((pieces, chips - 1)),
            pltpu.SemaphoreType.DMA((pieces, chips - 1)),
            pltpu.SemaphoreType.DMA((pieces, chips)),
            pltpu.SemaphoreType.DMA((pieces, chips)),
            pltpu.SemaphoreType.DMA((pieces, 6)),
            pltpu.SemaphoreType.DMA((4,)),
            pltpu.VMEM((2, rows_in, width), LOW),
            pltpu.VMEM((2, rows_in, cut), LOW),
            pltpu.VMEM((2, chips, own, width), LOW),
            pltpu.VMEM((2, 2, shapes[3][0], width), LOW),
            pltpu.SemaphoreType.DMA((2,)),
            pltpu.SemaphoreType.DMA((2,)),
            pltpu.SemaphoreType.DMA((4,)),
            pltpu.VMEM((2, width, width), LOW),
            pltpu.SemaphoreType.DMA((2,)),
            pltpu.SemaphoreType.DMA((cells + 4,)),
            pltpu.SemaphoreType.DMA((4,)),
            pltpu.SemaphoreType.DMA((2,)),
            pltpu.SemaphoreType.DMA((2,)),
            pltpu.VMEM((length, width), LOW),
            pltpu.VMEM((length, width), LOW),
            pltpu.VMEM((length, 3 * width), LOW),
            pltpu.VMEM((length, width), F32),
            pltpu.VMEM((2, length, width), LOW),
            pltpu.VMEM((2, length, width), LOW),
            pltpu.VMEM((length, 3 * width), LOW),
            pltpu.VMEM((length, width), LOW),
            pltpu.VMEM((length, width), LOW),
            pltpu.VMEM((2, length, width), F32),
            pltpu.VMEM((length, width), F32),
            pltpu.VMEM((16, width), F32),
        ],
        compiler_params=pltpu.CompilerParams(
            collective_id=2, has_side_effects=True, vmem_limit_bytes=62 * 2**20
        ),
        cost_estimate=pl.CostEstimate(flops=flops, bytes_accessed=160 * width * width, transcendentals=0),
    )(arrived, entry, rows, *saved, *weights, *sides, *kept)
    return (list(outs[:5]), outs[5:10])


def on_device(inputs, out_grad, query_counts, gains, shifts, w_qkv, w_out, w_up, b_up, w_down):
    stage = lax.axis_index("pipe")
    stages = lax.axis_size("pipe")
    count = lax.axis_size("dp")
    cell_count, length, width = inputs.shape
    own = width // count
    ups = b_up.shape[1] // own
    deep = ups * width
    deep_own = w_down.shape[1]
    shapes = [
        block_shape(own, 3 * width),
        block_shape(own, width),
        block_shape(own, deep),
        block_shape(deep_own, width),
    ]
    cut = (shapes[3][0] // 2 + 15) // 16 * 16
    items = (
        (0, 0, 16, 0),
        (1, 0, shapes[0][0], 0),
        (2, 0, shapes[1][0], 0),
        (3, 0, shapes[2][0], 1),
        (4, 0, cut, 0),
        (4, cut, shapes[3][0] - cut, 1),
    )
    shards = [small_pack(gains[0], shifts[0], b_up[0], 1)[0]] + [
        array[0].reshape(shape) for array, shape in zip((w_qkv, w_out, w_up, w_down), shapes)
    ]
    fused = stages == 2 and cell_count == 2 and own % 16 == 0 and width % 256 == 0 and 4 * deep_own == width
    if fused:
        piece = own // 2 // 16 * 16
        arrivals = (
            (0, 0, 16, 0),
            (1, 0, own - piece, 0),
            (1, own - piece, piece, 1),
            (2, 0, own, 1),
            (3, 0, own - piece, 0),
            (3, own - piece, piece, 1),
            (4, 0, cut, 0),
            (4, cut, deep_own - cut, 1),
        )
        packs, rows, arrived, later, kept = gather_forward(
            shards, inputs, arrivals, ((0, 1, 2, 3), (4, 5), (6, 7)), count
        )
    else:
        packs = gather(shards, items, count)
        gain_rows, shift_rows, bias = small_split(packs[0].astype(F32), ups)
        blank = jnp.zeros((8 - ups, width), F32)
        rows = jnp.concatenate([gain_rows, shift_rows, bias.reshape(ups, width), blank])
    weights = (
        packs[1].reshape(width, 3 * width),
        packs[2].reshape(width, width),
        packs[3].reshape(width, deep),
        packs[4].reshape(deep, width),
    )
    scales = jnp.sqrt(query_counts.astype(F32) / 500.0)

    def along(value, steps):
        pairs = [(source, source + steps) for source in range(stages) if 0 <= source + steps < stages]
        return lax.ppermute(value, "pipe", pairs)

    entries = [[inputs[cell] for cell in range(cell_count)]]
    if fused:
        entries.append([arrived] + [along(later, 1)])
    else:
        kept = None
    for turn in range(1 if fused else 0, stages):
        active = (stage == turn).astype(jnp.int32)[None]
        arrived = []
        for cell in range(cell_count):
            sent, kept = forward_tick(active, entries[turn][cell], rows, weights, kept, cell, cell_count)
            if turn + 1 < stages:
                arrived.append(along(sent, 1))
        entries.append(arrived)
    section_out, lowered, packed, mixed, middle, second, activated, slope = kept
    incoming = [(out_grad[cell], scales[cell][None]) for cell in range(cell_count)]
    back = None
    for turn in range(stages - 1, -1, -1):
        active = (stage == turn).astype(jnp.int32)[None]
        arrived = []
        for cell in range(cell_count):
            if fused and turn == 0 and cell == cell_count - 1:
                continue
            sent, back = backward_tick(
                active, incoming[cell], entries[turn][cell], rows, (packed, middle, slope), weights, back, cell, cell_count
            )
            if turn > 0:
                arrived.append((along(sent, -1), jnp.ones((1,), F32)))
        incoming = arrived if turn > 0 else incoming

    def flat(array):
        return array.reshape(cell_count * length, -1)

    input_grads, grad_packed, grad_branch, grad_inner, grad_ff, sums = back
    if fused:
        (input_grads, grad_packed, grad_branch, grad_inner, sums), shares = last_backward(
            incoming[-1][0],
            entries[0][-1],
            rows,
            (packed, middle, slope),
            weights,
            (input_grads, flat(grad_packed), flat(grad_branch), flat(grad_inner), sums),
            [flat(array) for array in (activated, grad_ff, second, mixed, lowered)],
            items,
            shapes,
            count,
        )
    else:
        sums = jnp.sum(sums, axis=0)
        small_part = small_pack(sums[0:2], sums[2:8], sums[8 : 8 + ups].reshape(deep), count)
        sides = [flat(array) for array in (lowered, grad_packed, mixed, grad_branch, second, grad_inner, activated, grad_ff)]
        products = [dot_left(sides[at], sides[at + 1]).astype(LOW) for at in (0, 2, 4, 6)]
        parts = [small_part] + [whole.reshape((count,) + shape) for whole, shape in zip(products, shapes)]
        shares = scatter(parts, items, count)
    grad_gains, grad_shifts, grad_bias = small_split(shares[0][None], ups)
    return (
        section_out[None],
        input_grads[None],
        grad_gains[None],
        grad_shifts[None],
        shares[1].reshape(1, own, 3 * width),
        shares[2].reshape(1, own, width),
        shares[3].reshape(1, own, deep),
        grad_bias[None],
        shares[4].reshape(1, deep_own, width),
    )


def solution(mesh):
    in_specs = (
        P("dp", None, None),
        P("dp", None, None),
        P("dp"),
        P("pipe", None, "dp"),
        P("pipe", None, "dp"),
        P("pipe", "dp", None),
        P("pipe", "dp", None),
        P("pipe", "dp", None),
        P("pipe", "dp"),
        P("pipe", "dp", None),
    )
    out_specs = (
        P("pipe", "dp", None, None),
        P("pipe", "dp", None, None),
        P("pipe", None, "dp"),
        P("pipe", None, "dp"),
        P("pipe", "dp", None),
        P("pipe", "dp", None),
        P("pipe", "dp", None),
        P("pipe", "dp"),
        P("pipe", "dp", None),
    )
    return jax.shard_map(
        on_device, mesh=mesh, in_specs=in_specs, out_specs=out_specs, check_vma=False
    )
```

```python
import functools
import math

import jax
import jax.numpy as jnp
from jax import lax
from jax.experimental import pallas as pl
from jax.experimental.pallas import tpu as pltpu
from jax.sharding import PartitionSpec as P

HEAD_DIM = 64
MESH = pl.DeviceIdType.MESH
LOW = jnp.bfloat16
F32 = jnp.float32


def ring_chip(position, chips):
    position = lax.rem(position + 2 * chips, chips)
    half = chips // 2
    return jnp.where(position < half, 2 * position, 2 * (chips - 1 - position) + 1)


def ring_place(chips):
    me = lax.axis_index("dp")
    core = lax.rem(me, 2)
    chip = me // 2
    position = jnp.where(lax.rem(chip, 2) == 0, chip // 2, chips - 1 - chip // 2)
    right = ring_chip(position + 1, chips) * 2 + core
    left = ring_chip(position - 1, chips) * 2 + core
    return (me, core, position, right, left, me + 1 - 2 * core)


def greet(devices):
    barrier = pltpu.get_barrier_semaphore()
    for device in devices:
        pl.semaphore_signal(barrier, inc=1, device_id={"dp": device}, device_id_type=MESH)
    pl.semaphore_wait(barrier, len(devices))


def gather_kernel(chips, arrays, items, *refs):
    count = len(items)
    ring_send, ring_recv, pair_send, pair_recv, own_sem = refs[2 * arrays :]
    shards = [refs[array].at[pl.ds(start, rows)] for array, start, rows, _ in items]
    splits = [way for _, _, _, way in items]
    half = chips // 2
    me, core, position, right, left, sibling = ring_place(chips)
    greet((left, right, sibling))

    def out(item, block):
        array, start, rows, _ = items[item]
        return refs[arrays + array].at[block, pl.ds(start, rows)]

    def owner(step, way):
        return ring_chip(position - step if way == 0 else position + step, chips) * 2 + core

    def travels(item, way, step):
        return step < half or (step == half and splits[item] == way)

    def ring_copy(item, way, step):
        block = owner(step - 1, way)
        return pltpu.make_async_remote_copy(
            src_ref=shards[item] if step == 1 else out(item, block),
            dst_ref=out(item, block),
            send_sem=ring_send.at[item, way, step - 1],
            recv_sem=ring_recv.at[item, way, step - 1],
            device_id={"dp": right if way == 0 else left},
            device_id_type=MESH,
        )

    def pair_copy(item, offset, block, source):
        return pltpu.make_async_remote_copy(
            src_ref=source,
            dst_ref=out(item, block),
            send_sem=pair_send.at[item, offset],
            recv_sem=pair_recv.at[item, offset],
            device_id={"dp": sibling},
            device_id_type=MESH,
        )

    sent, paired, kept = ([], [], [])
    for item in range(count):
        for way in (0, 1):
            if travels(item, way, 1):
                sent.append(ring_copy(item, way, 1))
                sent[-1].start()
    for item in range(count):
        paired.append(pair_copy(item, 0, me, shards[item]))
        paired[-1].start()
        kept.append(pltpu.make_async_copy(shards[item], out(item, me), own_sem.at[item]))
        kept[-1].start()
    for step in range(1, half + 1):
        for item in range(count):
            for way in (0, 1):
                if not travels(item, way, step):
                    continue
                ring_copy(item, way, step).wait_recv()
                if travels(item, way, step + 1):
                    sent.append(ring_copy(item, way, step + 1))
                    sent[-1].start()
                block = owner(step, way)
                offset = step if way == 0 else chips - step
                paired.append(pair_copy(item, offset, block, out(item, block)))
                paired[-1].start()
    for copy in sent:
        copy.wait_send()
    for copy in paired:
        copy.wait()
    for copy in kept:
        copy.wait()


def gather(shards, items, count):
    chips = count // 2
    arrays, pieces = (len(shards), len(items))
    return pl.pallas_call(
        functools.partial(gather_kernel, chips, arrays, items),
        out_shape=[jax.ShapeDtypeStruct((count,) + shard.shape, shard.dtype) for shard in shards],
        in_specs=[pl.BlockSpec(memory_space=pl.ANY)] * arrays,
        out_specs=[pl.BlockSpec(memory_space=pl.ANY)] * arrays,
        scratch_shapes=[
            pltpu.SemaphoreType.DMA((pieces, 2, chips // 2)),
            pltpu.SemaphoreType.DMA((pieces, 2, chips // 2)),
            pltpu.SemaphoreType.DMA((pieces, chips)),
            pltpu.SemaphoreType.DMA((pieces, chips)),
            pltpu.SemaphoreType.DMA((pieces,)),
        ],
        compiler_params=pltpu.CompilerParams(collective_id=0, has_side_effects=True),
    )(*shards)


def scatter_kernel(chips, arrays, items, *refs):
    count = len(items)
    parts, outs, refs = (refs[:arrays], refs[arrays : 2 * arrays], refs[2 * arrays :])
    landed, paired, mine = (refs[:count], refs[count : 2 * count], refs[2 * count : 3 * count])
    ring_send, ring_recv, pair_send, pair_recv, mine_sem = refs[3 * count :]
    splits = [way for _, _, _, way in items]
    half = chips // 2
    me, core, position, right, left, sibling = ring_place(chips)
    greet((left, right, sibling))

    def part(item, block):
        array, start, rows, _ = items[item]
        return parts[array].at[block, pl.ds(start, rows)]

    def first(item, way):
        return 1 if splits[item] == way else 2

    def slot(item, way, step):
        return step - 1 if splits[item] == way else half + step - 2

    def offset_of(step, way):
        return half - step + 1 if way == 0 else chips - (half - step + 1)

    def pair_copy(item, offset):
        block = ring_chip(position + offset, chips) * 2 + 1 - core
        return pltpu.make_async_remote_copy(
            src_ref=part(item, block),
            dst_ref=paired[item].at[offset],
            send_sem=pair_send.at[item, offset],
            recv_sem=pair_recv.at[item, offset],
            device_id={"dp": sibling},
            device_id_type=MESH,
        )

    def ring_copy(item, way, step):
        if step == first(item, way):
            source = paired[item].at[offset_of(step, way)]
        else:
            source = landed[item].at[slot(item, way, step - 1)]
        here = slot(item, way, step)
        return pltpu.make_async_remote_copy(
            src_ref=source,
            dst_ref=landed[item].at[here],
            send_sem=ring_send.at[item, here],
            recv_sem=ring_recv.at[item, here],
            device_id={"dp": right if way == 0 else left},
            device_id_type=MESH,
        )

    def load(item, offset, buffer):
        block = ring_chip(position + offset, chips) * 2 + core
        return pltpu.make_async_copy(part(item, block), mine[item].at[buffer], mine_sem.at[item, buffer])

    plan, uses = ([], [0] * count)
    for step in range(1, half + 2):
        for item in range(count):
            for way in (0, 1):
                if step <= half and step >= first(item, way):
                    plan.append((step, item, way, offset_of(step, way), uses[item] % 2))
                    uses[item] += 1
            if step > half:
                plan.append((step, item, None, 0, uses[item] % 2))
                uses[item] += 1
    for step, item, way, offset, buffer in plan:
        pair_copy(item, offset).start()
    load(plan[0][1], plan[0][3], plan[0][4]).start()
    sent = []
    for number, (step, item, way, offset, buffer) in enumerate(plan):
        if number + 1 < len(plan):
            load(plan[number + 1][1], plan[number + 1][3], plan[number + 1][4]).start()
        load(item, offset, buffer).wait()
        pair_copy(item, offset).wait_recv()
        array, start, rows, _ = items[item]
        kind = parts[array].dtype
        chunk = 16 if rows % 16 == 0 else rows
        from_pair, from_mine, from_ring = (paired[item], mine[item], landed[item])
        if way is None:
            ring_copy(item, 0, half).wait_recv()
            ring_copy(item, 1, half).wait_recv()
            slot_a, slot_b = (slot(item, 0, half), slot(item, 1, half))

            @pl.loop(0, rows // chunk)
            def _(index):
                here = pl.ds(pl.multiple_of(index * chunk, chunk), chunk)
                outs[array][pl.ds(pl.multiple_of(start + index * chunk, chunk), chunk), :] = (
                    from_ring[slot_a, here, :].astype(F32) + from_ring[slot_b, here, :].astype(F32)
                ) + (from_mine[buffer, here, :].astype(F32) + from_pair[offset, here, :].astype(F32))

            continue
        if step == first(item, way):

            @pl.loop(0, rows // chunk)
            def _(index):
                here = pl.ds(pl.multiple_of(index * chunk, chunk), chunk)
                from_pair[offset, here, :] = (
                    from_mine[buffer, here, :].astype(F32) + from_pair[offset, here, :].astype(F32)
                ).astype(kind)

        else:
            ring_copy(item, way, step - 1).wait_recv()
            arrived = slot(item, way, step - 1)

            @pl.loop(0, rows // chunk)
            def _(index):
                here = pl.ds(pl.multiple_of(index * chunk, chunk), chunk)
                from_ring[arrived, here, :] = (
                    from_ring[arrived, here, :].astype(F32)
                    + (from_mine[buffer, here, :].astype(F32) + from_pair[offset, here, :].astype(F32))
                ).astype(kind)

        sent.append(ring_copy(item, way, step))
        sent[-1].start()
    for copy in sent:
        copy.wait_send()
    for step, item, way, offset, buffer in plan:
        pair_copy(item, offset).wait_send()


def scatter(parts, items, count):
    chips = count // 2
    arrays, pieces = (len(parts), len(items))
    shapes = [(rows,) + parts[array].shape[2:] for array, _, rows, _ in items]
    kinds = [parts[array].dtype for array, _, _, _ in items]
    return pl.pallas_call(
        functools.partial(scatter_kernel, chips, arrays, items),
        out_shape=[jax.ShapeDtypeStruct(part.shape[1:], F32) for part in parts],
        in_specs=[pl.BlockSpec(memory_space=pl.ANY)] * arrays,
        out_specs=[pl.BlockSpec(memory_space=pltpu.VMEM)] * arrays,
        scratch_shapes=[pltpu.VMEM((chips - 1,) + shape, kind) for shape, kind in zip(shapes, kinds)]
        + [pltpu.VMEM((chips,) + shape, kind) for shape, kind in zip(shapes, kinds)]
        + [pltpu.VMEM((2,) + shape, kind) for shape, kind in zip(shapes, kinds)]
        + [
            pltpu.SemaphoreType.DMA((pieces, chips - 1)),
            pltpu.SemaphoreType.DMA((pieces, chips - 1)),
            pltpu.SemaphoreType.DMA((pieces, chips)),
            pltpu.SemaphoreType.DMA((pieces, chips)),
            pltpu.SemaphoreType.DMA((pieces, 2)),
        ],
        compiler_params=pltpu.CompilerParams(
            collective_id=1, has_side_effects=True, vmem_limit_bytes=62 * 2**20
        ),
    )(*parts)


def block_shape(rows, columns):
    return (rows, columns) if rows % 16 == 0 else (rows * columns // 128, 128)


def small_pack(gains, shifts, bias, count):
    width = gains.shape[1] // count
    ups = bias.shape[0] // gains.shape[1]
    rows = [
        gains.reshape(2, count, width).swapaxes(0, 1),
        shifts.reshape(6, count, width).swapaxes(0, 1),
        bias.reshape(count, ups, width),
    ]
    blank = jnp.zeros((count, 8 - ups, width), gains.dtype)
    return jnp.concatenate(rows + [blank], axis=1)


def small_split(blocks, ups):
    count, _, width = blocks.shape
    gains = blocks[:, 0:2].swapaxes(0, 1).reshape(2, count * width)
    shifts = blocks[:, 2:8].swapaxes(0, 1).reshape(6, count * width)
    bias = blocks[:, 8 : 8 + ups].reshape(count * ups * width)
    return (gains, shifts, bias)


def row_norm(rows_in):
    center = rows_in - jnp.mean(rows_in, axis=-1, keepdims=True)
    inverse = lax.rsqrt(jnp.mean(center * center, axis=-1, keepdims=True) + 1e-05)
    return (center * inverse, inverse)


def norm_back(grad_rows, normed, inverse):
    return inverse * (
        grad_rows
        - jnp.mean(grad_rows, axis=-1, keepdims=True)
        - normed * jnp.mean(grad_rows * normed, axis=-1, keepdims=True)
    )


def gelu_parts(hidden):
    cumulative = 0.5 * (1.0 + lax.erf(hidden * (1.0 / math.sqrt(2.0))))
    slope = cumulative + hidden * jnp.exp(-0.5 * hidden * hidden) * (1.0 / math.sqrt(2.0 * math.pi))
    return (hidden * cumulative, slope)


def dot(left, right):
    return lax.dot_general(left, right, (((1,), (0,)), ((), ())), preferred_element_type=F32)


def dot_right(left, right):
    return lax.dot_general(left, right, (((1,), (1,)), ((), ())), preferred_element_type=F32)


def dot_left(left, right):
    return lax.dot_general(left, right, (((0,), (0,)), ((), ())), preferred_element_type=F32)


class Stream:
    def __init__(self, blocks, buffers, sems):
        self.blocks, self.buffers, self.sems = (blocks, buffers, sems)
        self.depth = buffers.shape[0]
        self.started = 0
        for _ in range(min(self.depth, len(blocks))):
            self.start()

    def copy(self, number):
        slot = number % self.depth
        return pltpu.make_async_copy(self.blocks[number], self.buffers.at[slot], self.sems.at[slot])

    def start(self):
        self.copy(self.started).start()
        self.started += 1

    def take(self, number):
        self.copy(number).wait()
        return self.buffers.at[number % self.depth]

    def release(self):
        if self.started < len(self.blocks):
            self.start()


def weight_blocks(w_qkv, w_out, w_up, w_down):
    width = w_out.shape[0]
    def cut(ref, axis, number):
        window = pl.ds(number * width, width)
        return ref.at[:, window] if axis else ref.at[window, :]
    heads = [cut(w_qkv, 1, number) for number in range(3)]
    ups = [cut(w_up, 1, number) for number in range(w_up.shape[1] // width)]
    downs = [cut(w_down, 0, number) for number in range(w_down.shape[0] // width)]
    return (heads, w_out, ups, downs)


def head_masks(length):
    return lax.broadcasted_iota(jnp.int32, (length, 128), 1) < HEAD_DIM


def two_heads(array, side):
    blank = jnp.zeros_like(array)
    return jnp.concatenate([jnp.where(side, array, blank), jnp.where(side, blank, array)], axis=0)


def attend(packed, mixed, width, low=0, high=None):
    length = packed.shape[0]
    side = head_masks(length)

    def pair_of(pair):
        start = pair * 128 if isinstance(pair, int) else pl.multiple_of(pair * 128, 128)
        queries = packed[:, pl.ds(start, 128)] * jnp.asarray(1.0 / math.sqrt(HEAD_DIM), LOW)
        keys = two_heads(packed[:, pl.ds(start + width, 128)], side)
        values = two_heads(packed[:, pl.ds(start + 2 * width, 128)], side)
        scores = dot_right(queries, keys)
        probs, totals = ([], [])
        for head in (0, 1):
            mine = scores[:, head * length : (head + 1) * length]
            shifted = jnp.exp(mine - jnp.max(mine, axis=-1, keepdims=True))
            totals.append(1.0 / jnp.sum(shifted, axis=-1, keepdims=True))
            probs.append(shifted.astype(LOW))
        result = dot(jnp.concatenate(probs, axis=1), values)
        mixed[:, pl.ds(start, 128)] = (result * jnp.where(side, totals[0], totals[1])).astype(LOW)

    if high is not None:
        for pair in range(low, high):
            pair_of(pair)
        return

    @pl.loop(0, width // 256)
    def _(index):
        pair_of(index * 2)
        pair_of(index * 2 + 1)


def attend_back(packed, grad_mixed, grad_packed, width, low=0, high=None):
    length = packed.shape[0]
    side = head_masks(length)
    scale = 1.0 / math.sqrt(HEAD_DIM)

    def pair_of(pair):
        start = pair * 128 if isinstance(pair, int) else pl.multiple_of(pair * 128, 128)
        queries = packed[:, pl.ds(start, 128)]
        keys = packed[:, pl.ds(start + width, 128)] * jnp.asarray(scale, LOW)
        grads = grad_mixed[:, pl.ds(start, 128)]
        keys_two = two_heads(keys, side)
        queries_two = two_heads(queries, side)
        grads_two = two_heads(grads, side)
        scores = dot_right(keys, queries_two)
        grad_probs = dot_right(packed[:, pl.ds(start + 2 * width, 128)], grads_two)
        probs, grad_scores = ([], [])
        for head in (0, 1):
            mine = slice(head * length, (head + 1) * length)
            shifted = jnp.exp(scores[:, mine] - jnp.max(scores[:, mine], axis=0, keepdims=True))
            prob = shifted * (1.0 / jnp.sum(shifted, axis=0, keepdims=True))
            product = grad_probs[:, mine] * prob
            weighted = jnp.sum(product, axis=0, keepdims=True)
            probs.append(prob.astype(LOW))
            grad_scores.append((product - prob * weighted).astype(LOW))
        beside = jnp.concatenate(grad_scores, axis=1)
        grad_packed[:, pl.ds(start, 128)] = dot_left(jnp.concatenate(grad_scores, axis=0), keys_two).astype(LOW)
        grad_packed[:, pl.ds(start + width, 128)] = (dot(beside, queries_two) * scale).astype(LOW)
        grad_packed[:, pl.ds(start + 2 * width, 128)] = dot(jnp.concatenate(probs, axis=1), grads_two).astype(LOW)

    if high is not None:
        for pair in range(low, high):
            pair_of(pair)
        return

    @pl.loop(0, width // 256)
    def _(index):
        pair_of(index * 2)
        pair_of(index * 2 + 1)


def forward_kernel(cell, held, active, entry_h, rows, w_qkv, w_out, w_up, w_down, *refs):
    sent_h = refs[held]
    out_h, lowered_h, packed_h, mixed_h, middle_h, second_h, active_h, slope_h = [
        ref.at[cell] for ref in refs[held + 1 : held + 9]
    ]
    (buffers, buffer_sems, save_sems, out_v, lowered_v, packed_v, mixed_v, middle_v) = refs[held + 9 : held + 17]
    (second_v, active_v, slope_v, hidden_v, total_v, entry, entry_sem) = refs[held + 17 :]
    width = entry.shape[1]
    gains, shifts, bias = (rows.at[0:2], rows.at[2:8], rows.at[8:16])
    ups = w_up.shape[1] // width

    @pl.when(active[0] != 0)
    def _():
        heads, outer, up, down = weight_blocks(w_qkv, w_out, w_up, w_down)
        order = heads + [outer]
        place_up, place_down = ({}, {})
        for number in range(ups + 1):
            if number < ups:
                place_up[number] = len(order)
                order.append(up[number])
            if number > 0:
                place_down[number - 1] = len(order)
                order.append(down[number - 1])
        fetched = pltpu.make_async_copy(entry_h, entry, entry_sem)
        fetched.start()
        saves = []

        def save(source, target):
            saves.append(pltpu.make_async_copy(source, target, save_sems.at[len(saves)]))
            saves[-1].start()

        fetched.wait()
        stream = Stream(order, buffers, buffer_sems)
        rows_in = entry[...].astype(F32)
        normed, _ = row_norm(rows_in)
        lowered_v[...] = (normed * gains[0:1, :] + shifts[0:1, :]).astype(LOW)
        save(lowered_v, lowered_h)
        for number in range(3):
            block = stream.take(number)
            window = pl.ds(number * width, width)
            part = dot(lowered_v[...], block[...])
            if number != 1:
                part = part + shifts[1 + number // 2 : 2 + number // 2, :]
            packed_v[:, window] = part.astype(LOW)
            stream.release()
        save(packed_v, packed_h)
        attend(packed_v, mixed_v, width)
        save(mixed_v, mixed_h)
        block = stream.take(3)
        middle = entry[...].astype(F32) + dot(mixed_v[...], block[...]) + shifts[3:4, :]
        middle_v[...] = middle
        stream.release()
        save(middle_v, middle_h)
        normed, _ = row_norm(middle_v[...])
        second_v[...] = (normed * gains[1:2, :] + shifts[4:5, :]).astype(LOW)
        save(second_v, second_h)
        for number in range(ups + 1):
            if number < ups:
                up_block = stream.take(place_up[number])
            if number > 0:
                down_block = stream.take(place_down[number - 1])
            if number < ups:
                hidden_v[number % 2] = dot(second_v[...], up_block[...]) + bias[number : number + 1, :]
            if number > 0:
                window = pl.ds((number - 1) * width, width)
                activated, slope = gelu_parts(hidden_v[(number - 1) % 2])
                active_v[:, window] = activated.astype(LOW)
                slope_v[:, window] = slope.astype(LOW)
                part = dot(active_v[:, window], down_block[...])
                if number == 1:
                    total_v[...] = part
                elif number < ups:
                    total_v[...] += part
                else:
                    out_v[...] = (middle_v[...] + (total_v[...] + part + shifts[5:6, :])).astype(LOW)
                save(active_v.at[:, window], active_h.at[:, window])
                save(slope_v.at[:, window], slope_h.at[:, window])
            if number < ups:
                stream.release()
            if number > 0:
                stream.release()
        save(out_v, sent_h)
        save(out_v, out_h)
        for copy in saves:
            copy.wait()


def kept_shapes(length, width, deep):
    return [
        ((length, width), LOW),
        ((length, width), LOW),
        ((length, 3 * width), LOW),
        ((length, width), LOW),
        ((length, width), F32),
        ((length, width), LOW),
        ((length, deep), LOW),
        ((length, deep), LOW),
    ]


def forward_tick(active, entry, rows, weights, kept, cell, cell_count):
    length, width = entry.shape
    deep = weights[2].shape[1]
    ups = deep // width
    shapes = kept_shapes(length, width, deep)
    outs = [jax.ShapeDtypeStruct(*shapes[0])] + [
        jax.ShapeDtypeStruct((cell_count,) + shape, kind) for shape, kind in shapes
    ]
    vmem, hbm = (pl.BlockSpec(memory_space=pltpu.VMEM), pl.BlockSpec(memory_space=pl.ANY))
    flops = 2 * length * width * (4 * width + 2 * deep) + 16 * length * length * width
    kept = () if kept is None else tuple(kept)
    held = len(kept)
    sent, *kept = pl.pallas_call(
        functools.partial(forward_kernel, cell, held),
        out_shape=outs,
        in_specs=[pl.BlockSpec(memory_space=pltpu.SMEM), hbm, vmem] + [hbm] * (4 + held),
        out_specs=[hbm] * 9,
        input_output_aliases={7 + number: 1 + number for number in range(held)},
        scratch_shapes=[
            pltpu.VMEM((4, width, width), LOW),
            pltpu.SemaphoreType.DMA((4,)),
            pltpu.SemaphoreType.DMA((7 + 2 * ups,)),
        ]
        + [pltpu.VMEM(*shape) for shape in shapes]
        + [
            pltpu.VMEM((2, length, width), F32),
            pltpu.VMEM((length, width), F32),
            pltpu.VMEM((length, width), LOW),
            pltpu.SemaphoreType.DMA,
        ],
        compiler_params=pltpu.CompilerParams(vmem_limit_bytes=60 * 2**20),
        cost_estimate=pl.CostEstimate(
            flops=flops, bytes_accessed=2 * width * (4 * width + 2 * deep), transcendentals=0
        ),
    )(active, entry, rows, *weights, *kept)
    return (sent, kept)


def backward_kernel(cell, held, active, scale, grad_h, entry_h, rows, *refs):
    packed, middle, slope = [ref.at[cell] for ref in refs[:3]]
    w_qkv, w_out, w_up, w_down = refs[3:7]
    refs = refs[7 + held :]
    sent_h = refs[0]
    rows_h, packed_h, branch_h, inner_h, low_h, sums_h = [ref.at[cell] for ref in refs[1:7]]
    (buffers, buffer_sems, load_sems, save_sems, rows_v, grad_packed_v, branch_v, inner_v, low_v, sums_v) = refs[7:17]
    (packed_v, middle_v, slope_v, mixed_v, grad_act_v, total_v, grad_middle_v, grad, entry) = refs[17:]
    gains = rows.at[0:2]
    length, width = entry.shape
    ups = w_up.shape[1] // width

    @pl.when(active[0] != 0)
    def _():
        heads, outer, up, down = weight_blocks(w_qkv, w_out, w_up, w_down)
        loads = [
            pltpu.make_async_copy(slope, slope_v, load_sems.at[0]),
            pltpu.make_async_copy(middle, middle_v, load_sems.at[1]),
            pltpu.make_async_copy(packed, packed_v, load_sems.at[2]),
            pltpu.make_async_copy(grad_h, grad, load_sems.at[3]),
            pltpu.make_async_copy(entry_h, entry, load_sems.at[4]),
        ]
        loads[3].start()
        order, place_up, place_down = ([], {}, {})
        for number in range(ups + 1):
            if number < ups:
                place_down[number] = len(order)
                order.append(down[number])
            if number > 0:
                place_up[number - 1] = len(order)
                order.append(up[number - 1])
        place_out = len(order)
        order = order + [outer] + heads
        saves = []

        def save(source, target):
            saves.append(pltpu.make_async_copy(source, target, save_sems.at[len(saves)]))
            saves[-1].start()

        def column_sum(array):
            return jnp.sum(array.astype(F32), axis=0, keepdims=True)

        loads[3].wait()
        stream = Stream(order, buffers, buffer_sems)
        loads[0].start()
        low_v[...] = (grad[...].astype(F32) * scale[0]).astype(LOW)
        save(low_v, low_h)
        sums_v[7:8, :] = column_sum(low_v[...])
        for number in range(ups + 1):
            if number == 1:
                loads[0].wait()
                loads[1].start()
            if number == 2:
                loads[2].start()
                loads[4].start()
            if number < ups:
                down_block = stream.take(place_down[number])
            if number > 0:
                up_block = stream.take(place_up[number - 1])
            if number < ups:
                grad_act_v[number % 2] = dot_right(low_v[...], down_block[...])
            if number > 0:
                window = pl.ds((number - 1) * width, width)
                inner = (grad_act_v[(number - 1) % 2] * slope_v[:, window].astype(F32)).astype(LOW)
                inner_v[:, window] = inner
                sums_v[7 + number : 8 + number, :] = column_sum(inner)
                part = dot_right(inner, up_block[...])
                if number == 1:
                    total_v[...] = part
                else:
                    total_v[...] += part
                save(inner_v.at[:, window], inner_h.at[:, window])
            if number < ups:
                stream.release()
            if number > 0:
                stream.release()
        loads[1].wait()
        normed, inverse = row_norm(middle_v[...])
        grad_second = total_v[...]
        sums_v[1:2, :] = column_sum(grad_second * normed)
        sums_v[6:7, :] = column_sum(grad_second)
        grad_middle = grad[...].astype(F32) * scale[0] + norm_back(grad_second * gains[1:2, :], normed, inverse)
        grad_middle_v[...] = grad_middle
        branch_v[...] = grad_middle.astype(LOW)
        sums_v[5:6, :] = column_sum(branch_v[...])
        save(branch_v, branch_h)
        block = stream.take(place_out)
        mixed_v[...] = dot_right(branch_v[...], block[...]).astype(LOW)
        stream.release()
        loads[2].wait()
        attend_back(packed_v, mixed_v, grad_packed_v, width)
        save(grad_packed_v, packed_h)
        sums_v[3:4, :] = column_sum(grad_packed_v[:, pl.ds(0, width)])
        sums_v[4:5, :] = column_sum(grad_packed_v[:, pl.ds(2 * width, width)])
        for number in range(3):
            block = stream.take(place_out + 1 + number)
            part = dot_right(grad_packed_v[:, pl.ds(number * width, width)], block[...])
            if number == 0:
                total_v[...] = part
            else:
                total_v[...] += part
            stream.release()
        loads[4].wait()
        normed, inverse = row_norm(entry[...].astype(F32))
        grad_lowered = total_v[...]
        sums_v[0:1, :] = column_sum(grad_lowered * normed)
        sums_v[2:3, :] = column_sum(grad_lowered)
        rows_v[...] = (grad_middle_v[...] + norm_back(grad_lowered * gains[0:1, :], normed, inverse)).astype(LOW)
        save(sums_v, sums_h)
        save(rows_v, sent_h)
        save(rows_v, rows_h)
        for copy in saves:
            copy.wait()


def backward_tick(active, incoming, entry, rows, saved, weights, kept, cell, cell_count):
    length, width = entry.shape
    deep = weights[2].shape[1]
    ups = deep // width
    shapes = [
        ((length, width), LOW),
        ((length, 3 * width), LOW),
        ((length, width), LOW),
        ((length, deep), LOW),
        ((length, width), LOW),
        ((16, width), F32),
    ]
    outs = [jax.ShapeDtypeStruct(*shapes[0])] + [
        jax.ShapeDtypeStruct((cell_count,) + shape, kind) for shape, kind in shapes
    ]
    vmem, hbm = (pl.BlockSpec(memory_space=pltpu.VMEM), pl.BlockSpec(memory_space=pl.ANY))
    smem = pl.BlockSpec(memory_space=pltpu.SMEM)
    flops = 2 * length * width * (4 * width + 2 * deep) + 40 * length * length * width
    kept = () if kept is None else tuple(kept)
    held = len(kept)
    grad, scale = incoming
    sent, *kept = pl.pallas_call(
        functools.partial(backward_kernel, cell, held),
        out_shape=outs,
        in_specs=[smem] * 2 + [hbm] * 2 + [vmem] + [hbm] * (7 + held),
        out_specs=[hbm] * 7,
        input_output_aliases={12 + number: 1 + number for number in range(held)},
        scratch_shapes=[
            pltpu.VMEM((4, width, width), LOW),
            pltpu.SemaphoreType.DMA((4,)),
            pltpu.SemaphoreType.DMA((5,)),
            pltpu.SemaphoreType.DMA((6 + ups,)),
        ]
        + [pltpu.VMEM(*shape) for shape in shapes]
        + [
            pltpu.VMEM((length, 3 * width), LOW),
            pltpu.VMEM((length, width), F32),
            pltpu.VMEM((length, deep), LOW),
            pltpu.VMEM((length, width), LOW),
            pltpu.VMEM((2, length, width), F32),
            pltpu.VMEM((length, width), F32),
            pltpu.VMEM((length, width), F32),
            pltpu.VMEM((length, width), LOW),
            pltpu.VMEM((length, width), LOW),
        ],
        compiler_params=pltpu.CompilerParams(vmem_limit_bytes=60 * 2**20),
        cost_estimate=pl.CostEstimate(
            flops=flops, bytes_accessed=2 * width * (4 * width + 2 * deep), transcendentals=0
        ),
    )(active, scale, grad, entry, rows, *saved, *weights, *kept)
    return (sent, kept)


def small_rows(small, rows, width, ups):
    devices, _, own = small.shape
    lane = lax.broadcasted_iota(jnp.int32, (own, width), 1)
    depth = lax.broadcasted_iota(jnp.int32, (own, width), 0)
    row = lax.broadcasted_iota(jnp.int32, (16, width), 0)
    across = lax.broadcasted_iota(jnp.int32, (16, width), 1)
    top = jnp.zeros((16, width), F32)
    for device in range(devices):
        spot = jnp.where(lane == depth + device * own, 1.0, 0.0).astype(LOW)
        top = top + dot(small[device], spot)
    rows[0:8, :] = top[0:8]
    share = devices // ups
    for block in range(ups):
        total = jnp.zeros((1, width), F32)
        for index in range(share):
            start = index * ups * own
            spot = jnp.zeros((own, width), F32)
            for up in range(ups):
                spot = spot + jnp.where(lane == depth + (start + up * own), 1.0, 0.0)
            low = start + (row - 8) * own
            inside = (row >= 8) & (row < 8 + ups) & (across >= low) & (across < low + own)
            placed = dot(small[block * share + index], spot.astype(LOW))
            total = total + jnp.sum(jnp.where(inside, placed, 0.0), axis=0, keepdims=True)
        rows[8 + block : 9 + block, :] = total


def gather_forward_kernel(chips, items, groups, cells, *refs):
    shards, inputs_h = (refs[:5], refs[5])
    outs, rows_h, arrived_h, later_h = (refs[6:11], refs[11], refs[12], refs[13])
    out_h, lowered_h, packed_h, mixed_h, middle_h, second_h, active_h, slope_h = refs[14:22]
    (ring_send, ring_recv, pair_send, pair_recv, own_sem, hop_send, hop_recv) = refs[22:29]
    (load_sem, save_sem, wide_sem, deep_sem) = refs[29:33]
    (small_v, rows_v, entry_v, out_v, lowered_v, packed_v, mixed_v, middle_v, second_v, active_v, slope_v) = refs[33:44]
    (total_v, hidden_v, wide_v, deep_v) = refs[44:]
    length, width = entry_v.shape[1:]
    ups = active_v.shape[2] // width
    half = chips // 2
    me, core, position, right, left, sibling = ring_place(chips)
    stage = lax.axis_index("pipe")
    first = stage == 0
    barrier = pltpu.get_barrier_semaphore()
    for device in (left, right, sibling):
        pl.semaphore_signal(barrier, inc=1, device_id={"dp": device}, device_id_type=MESH)
    pl.semaphore_signal(barrier, inc=1, device_id={"pipe": 1 - stage}, device_id_type=MESH)
    pl.semaphore_wait(barrier, 4)

    def shard(item):
        array, start, rows, _ = items[item]
        return shards[array].at[pl.ds(start, rows)]

    def out(item, block):
        array, start, rows, _ = items[item]
        return outs[array].at[block, pl.ds(start, rows)]

    def owner(step, way):
        return ring_chip(position - step if way == 0 else position + step, chips) * 2 + core

    def travels(item, way, step):
        return step < half or (step == half and items[item][3] == way)

    def ring_copy(item, way, step):
        block = owner(step - 1, way)
        return pltpu.make_async_remote_copy(
            src_ref=shard(item) if step == 1 else out(item, block),
            dst_ref=out(item, block),
            send_sem=ring_send.at[item, way, step - 1],
            recv_sem=ring_recv.at[item, way, step - 1],
            device_id={"dp": right if way == 0 else left},
            device_id_type=MESH,
        )

    def pair_copy(item, offset, block, source):
        return pltpu.make_async_remote_copy(
            src_ref=source,
            dst_ref=out(item, block),
            send_sem=pair_send.at[item, offset],
            recv_sem=pair_recv.at[item, offset],
            device_id={"dp": sibling},
            device_id_type=MESH,
        )

    def own_copy(item):
        return pltpu.make_async_copy(shard(item), out(item, me), own_sem.at[item])

    sent, paired = ([], [])

    def open_group(group):
        for item in group:
            for way in (0, 1):
                if travels(item, way, 1):
                    sent.append(ring_copy(item, way, 1))
                    sent[-1].start()
        for item in group:
            paired.append(pair_copy(item, 0, me, shard(item)))
            paired[-1].start()
            own_copy(item).start()

    def ring_step(item, way, step):
        ring_copy(item, way, step).wait_recv()
        if travels(item, way, step + 1):
            sent.append(ring_copy(item, way, step + 1))
            sent[-1].start()
        block = owner(step, way)
        offset = step if way == 0 else chips - step
        paired.append(pair_copy(item, offset, block, out(item, block)))
        paired[-1].start()

    def pair_arrived(item, offset):
        block = ring_chip(position - offset, chips) * 2 + core
        pair_copy(item, offset, block, out(item, block)).wait_recv()

    saves = []

    def save(source, target):
        number = len(saves)
        saves.append(lambda: pltpu.make_async_copy(source(), target(), save_sem.at[number]))
        saves[-1]().start()

    def entry_load(cell):
        return pltpu.make_async_copy(inputs_h.at[cell], entry_v.at[cell], load_sem.at[cell])

    def wide_load(array, column, slot):
        source = outs[array].at[:, :, pl.ds(column * width, width)]
        return pltpu.make_async_copy(source, wide_v.at[slot], wide_sem.at[slot])

    def wide(slot):
        return wide_v[slot].reshape(width, width)

    def gains(number):
        return rows_v[number : number + 1, :]

    def shifts(number):
        return rows_v[2 + number : 3 + number, :]

    def begin(cell):
        def step():
            entry_load(cell).wait()
            normed, _ = row_norm(entry_v[cell].astype(F32))
            lowered_v[cell] = (normed * gains(0) + shifts(0)).astype(LOW)
            save(lambda: lowered_v.at[cell], lambda: lowered_h.at[cell])

        return step

    def project(cell, number):
        def step():
            if cell == 0:
                wide_load(1, number, number).wait()
            part = dot(lowered_v[cell], wide(number))
            if number != 1:
                part = part + shifts(1 + number // 2)
            packed_v[cell, :, pl.ds(number * width, width)] = part.astype(LOW)
            if number == 2:
                save(lambda: packed_v.at[cell], lambda: packed_h.at[cell])

        return step

    def mix(cell, low, high, last):
        def step():
            attend(packed_v.at[cell], mixed_v.at[cell], width, low, high)
            if last:
                save(lambda: mixed_v.at[cell], lambda: mixed_h.at[cell])

        return step

    def join(cell):
        def step():
            if cell == 0:
                wide_load(2, 0, 3).wait()
            middle_v[cell] = entry_v[cell].astype(F32) + dot(mixed_v[cell], wide(3)) + shifts(3)
            save(lambda: middle_v.at[cell], lambda: middle_h.at[cell])

        return step

    def renorm(cell):
        def step():
            middle = middle_v[cell]
            normed, _ = row_norm(middle)
            second_v[cell] = (normed * gains(1) + shifts(4)).astype(LOW)
            total_v[cell] = middle + shifts(5)
            save(lambda: second_v.at[cell], lambda: second_h.at[cell])

        return step

    def rise(cell, number):
        def step():
            if cell == 0:
                wide_load(3, number, number).wait()
            hidden_v[...] = dot(second_v[cell], wide(number)) + rows_v[8 + number : 9 + number, :]

        return step

    def bend(cell, number):
        def step():
            window = pl.ds(number * width, width)
            activated, slope = gelu_parts(hidden_v[...])
            active_v[cell, :, window] = activated.astype(LOW)
            slope_v[cell, :, window] = slope.astype(LOW)
            if number == ups - 1:
                save(lambda: active_v.at[cell], lambda: active_h.at[cell])
                save(lambda: slope_v.at[cell], lambda: slope_h.at[cell])

        return step

    deep_rows = deep_v.shape[1] * deep_v.shape[2]

    def deep_load(offset, slot):
        chip = ring_chip(position - offset, chips)
        return pltpu.make_async_copy(outs[4].at[pl.ds(chip * 2, 2)], deep_v.at[slot], deep_sem.at[slot])

    def fall(cell, offset, slot):
        def step():
            if cell == 0:
                deep_load(offset, slot).wait()
            chip = ring_chip(position - offset, chips)
            window = pl.ds(pl.multiple_of(chip * deep_rows, 128), deep_rows)
            total_v[cell] += dot(active_v[cell, :, window], deep_v[slot].reshape(deep_rows, width))

        return step

    def hop():
        return pltpu.make_async_remote_copy(
            src_ref=out_v.at[0],
            dst_ref=arrived_h,
            send_sem=hop_send,
            recv_sem=hop_recv,
            device_id={"pipe": 1 - stage},
            device_id_type=MESH,
        )

    def finish(cell):
        def step():
            out_v[cell] = total_v[cell].astype(LOW)
            if cell == 0:
                hop().start()
            else:
                save(lambda: out_v.at[cell], lambda: later_h)
            save(lambda: out_v.at[cell], lambda: out_h.at[cell])

        return step

    def on_first(step):
        pl.when(first)(step)

    queue = []

    def ready(group, steps, loads):
        for item in group:
            own_copy(item).wait()
            for offset in range(chips):
                pair_arrived(item, offset)

        @pl.when(first)
        def _():
            for load in loads:
                load().start()

        queue.extend(steps)

    pairs = width // 128
    heads = []
    for cell in range(cells):
        heads.append(begin(cell))
        heads += [project(cell, number) for number in range(3)]
        heads += [mix(cell, low, low + 2, low + 2 >= pairs) for low in range(0, pairs, 2)]
    joins = [make(cell) for cell in range(cells) for make in (join, renorm)]
    def load_ups():
        for number in range(ups):
            wide_load(3, number, number).start()

    climbs = [load_ups]
    climbs += [make(cell, number) for number in range(ups) for cell in range(cells) for make in (rise, bend)]

    @pl.when(first)
    def _():
        for cell in range(cells):
            entry_load(cell).start()

    def lay_rows():
        copy = pltpu.make_async_copy(outs[0], small_v, load_sem.at[cells])
        copy.start()
        copy.wait()
        small_rows(small_v, rows_v, width, ups)
        pltpu.make_async_copy(rows_v, rows_h, load_sem.at[cells + 1]).start()

    def ready_small():
        for item in groups[0]:
            if items[item][0] == 0:
                own_copy(item).wait()
                for offset in range(chips):
                    pair_arrived(item, offset)
        lay_rows()

    plan = []
    for number, group in enumerate(groups):
        for step in range(1, half + 1):
            if step == half and number + 1 < len(groups):
                plan.append(("open", number + 1))
            for item in group:
                for way in (0, 1):
                    if travels(item, way, step):
                        plan.append(("ring", item, way, step))
            if number == len(groups) - 1:
                plan.append(("deep", step))
        plan.append(("done", number))
    open_group(groups[0])
    late = []
    slots = [0]

    def deep_ready(offsets):
        for offset in offsets:
            for item in groups[-1]:
                if offset == 0:
                    own_copy(item).wait()
                pair_arrived(item, offset)
            slot = slots[0] % deep_v.shape[0]
            slots[0] += 1

            def opening(offset=offset, slot=slot):
                deep_load(offset, slot).start()

            queue.append(opening)
            queue.extend(fall(cell, offset, slot) for cell in range(cells))

    def serve(limit):
        for _ in range(limit):
            if queue:
                on_first(queue.pop(0))

    for entry in plan:
        if entry[0] == "open":
            open_group(groups[entry[1]])
        elif entry[0] == "ring":
            ring_step(*entry[1:])
            for wait in list(late):
                wait[0] -= 1
                if wait[0] == 0:
                    wait[1]()
                    late.remove(wait)
            serve(3 if entry[1] in groups[-1] else 2)
        elif entry[0] == "done":
            if entry[1] == 0:
                rest = [item for item in groups[0] if items[item][0] != 0]
                late.append([1, ready_small])
                late.append(
                    [
                        2,
                        lambda: ready(
                            rest,
                            heads + joins,
                            [functools.partial(wide_load, 1, number, number) for number in range(3)]
                            + [functools.partial(wide_load, 2, 0, 3)],
                        ),
                    ]
                )
            elif entry[1] == 1:
                late.append([2, lambda: ready(groups[1], climbs, [])])
        elif entry[0] == "deep":
            step = entry[1]
            if step == 1:
                late.append([3, lambda: deep_ready([0])])
            if step < half:
                late.append([2, lambda step=step: deep_ready([step, chips - step])])
            else:
                for wait in late:
                    wait[1]()
                serve(len(queue))
                deep_ready([half])
    serve(len(queue))
    for cell in range(cells):
        on_first(finish(cell))
    for copy in sent:
        copy.wait_send()
    for copy in paired:
        copy.wait_send()
    pltpu.make_async_copy(rows_v, rows_h, load_sem.at[cells + 1]).wait()

    @pl.when(first)
    def _():
        for copy in saves:
            copy().wait()
        hop().wait_send()

    @pl.when(jnp.logical_not(first))
    def _():
        hop().wait_recv()


def gather_forward(shards, inputs, items, groups, count):
    chips = count // 2
    cells, length, width = inputs.shape
    deep = shards[3].shape[1]
    ups = deep // width
    pieces = len(items)
    shapes = kept_shapes(length, width, deep)
    hbm = pl.BlockSpec(memory_space=pl.ANY)
    flops = 2 * cells * length * width * (4 * width + 2 * deep)
    outs = pl.pallas_call(
        functools.partial(gather_forward_kernel, chips, items, groups, cells),
        out_shape=[jax.ShapeDtypeStruct((count,) + shard.shape, shard.dtype) for shard in shards]
        + [
            jax.ShapeDtypeStruct((16, width), F32),
            jax.ShapeDtypeStruct((length, width), LOW),
            jax.ShapeDtypeStruct((length, width), LOW),
        ]
        + [jax.ShapeDtypeStruct((cells,) + shape, kind) for shape, kind in shapes],
        in_specs=[hbm] * 6,
        out_specs=[hbm] * 16,
        scratch_shapes=[
            pltpu.SemaphoreType.DMA((pieces, 2, chips // 2)),
            pltpu.SemaphoreType.DMA((pieces, 2, chips // 2)),
            pltpu.SemaphoreType.DMA((pieces, chips)),
            pltpu.SemaphoreType.DMA((pieces, chips)),
            pltpu.SemaphoreType.DMA((pieces,)),
            pltpu.SemaphoreType.DMA,
            pltpu.SemaphoreType.DMA,
            pltpu.SemaphoreType.DMA((cells + 2,)),
            pltpu.SemaphoreType.DMA((9 * cells,)),
            pltpu.SemaphoreType.DMA((4,)),
            pltpu.SemaphoreType.DMA((2,)),
            pltpu.VMEM((count,) + shards[0].shape, LOW),
            pltpu.VMEM((16, width), F32),
            pltpu.VMEM((cells, length, width), LOW),
        ]
        + [pltpu.VMEM((cells,) + shape, kind) for shape, kind in shapes]
        + [
            pltpu.VMEM((cells, length, width), F32),
            pltpu.VMEM((length, width), F32),
            pltpu.VMEM((4, count, width // count, width), LOW),
            pltpu.VMEM((2, 2, shards[4].shape[0], width), LOW),
        ],
        compiler_params=pltpu.CompilerParams(
            collective_id=3, has_side_effects=True, vmem_limit_bytes=62 * 2**20
        ),
        cost_estimate=pl.CostEstimate(flops=flops, bytes_accessed=8 * width * (4 * width + 2 * deep), transcendentals=0),
    )(*shards, inputs)
    return (outs[:5], outs[5], outs[6], outs[7], list(outs[8:]))


class RingSum:
    def __init__(self, chips, items, parts, outs, landed, paired, buffers, final, sems):
        self.chips, self.items, self.parts, self.outs = (chips, items, parts, outs)
        self.landed, self.paired, self.final = (landed, paired, final)
        self.mine, self.pairs, self.rings = buffers
        self.ring_send, self.ring_recv, self.pair_send, self.pair_recv, self.load_sem, self.final_sem = sems
        self.half = chips // 2
        self.me, self.core, self.position, self.right, self.left, self.sibling = ring_place(chips)
        self.sent, self.final_copies, self.exchanged = ({}, [], [])
        self.uses = [0] * len(items)

    def part(self, item, block):
        array, start, rows, _ = self.items[item]
        return self.parts[array].at[block, pl.ds(start, rows)]

    def first(self, item, way):
        return 1 if self.items[item][3] == way else 2

    def slot_of(self, item, way, step):
        return step - 1 if self.items[item][3] == way else self.half + step - 2

    def offset_of(self, step, way):
        return self.half - step + 1 if way == 0 else self.chips - (self.half - step + 1)

    def pair_copy(self, item, offset):
        block = ring_chip(self.position + offset, self.chips) * 2 + 1 - self.core
        return pltpu.make_async_remote_copy(
            src_ref=self.part(item, block),
            dst_ref=self.paired[item].at[offset],
            send_sem=self.pair_send.at[item, offset],
            recv_sem=self.pair_recv.at[item, offset],
            device_id={"dp": self.sibling},
            device_id_type=MESH,
        )

    def ring_copy(self, item, way, step, buffer=0):
        here = self.slot_of(item, way, step)
        return pltpu.make_async_remote_copy(
            src_ref=self.mine[item].at[buffer],
            dst_ref=self.landed[item].at[here],
            send_sem=self.ring_send.at[item, here],
            recv_sem=self.ring_recv.at[item, here],
            device_id={"dp": self.right if way == 0 else self.left},
            device_id_type=MESH,
        )

    def load_mine(self, item, offset, buffer):
        block = ring_chip(self.position + offset, self.chips) * 2 + self.core
        return pltpu.make_async_copy(self.part(item, block), self.mine[item].at[buffer], self.load_sem.at[item, buffer])

    def load_pair(self, item, offset, buffer):
        return pltpu.make_async_copy(
            self.paired[item].at[offset], self.pairs[item].at[buffer], self.load_sem.at[item, 2 + buffer]
        )

    def load_ring(self, item, way, step, buffer):
        return pltpu.make_async_copy(
            self.landed[item].at[self.slot_of(item, way, step)], self.rings[item].at[buffer], self.load_sem.at[item, 4 + buffer]
        )

    def starts(self, wanted):
        return [
            (step, item, way, self.offset_of(step, way))
            for step in (1, 2)
            for item in wanted
            for way in (0, 1)
            if step == self.first(item, way)
        ]

    def rest(self, wanted, steps):
        return [
            (step, item, way, self.offset_of(step, way))
            for step in steps
            if step <= self.half
            for item in wanted
            for way in (0, 1)
            if step > self.first(item, way)
        ] + [(step, item, None, 0) for step in steps if step > self.half for item in wanted]

    def fetch(self, entry):
        step, item, way, offset, buffer = entry
        if (item, buffer) in self.sent:
            self.sent.pop((item, buffer)).wait_send()
        self.load_mine(item, offset, buffer).start()
        self.pair_copy(item, offset).wait_recv()
        self.load_pair(item, offset, buffer).start()

    def bytes_of(self, item):
        array, _, rows, _ = self.items[item]
        return rows * self.parts[array].shape[2] * self.parts[array].dtype.itemsize

    def arrange(self, steps, ends):
        waiting = self.starts(range(len(self.items)))
        waiting += self.rest(range(len(self.items)), range(2, self.half + 2))
        opened, arrival, sends, used = ({}, {}, {}, [0] * len(self.items))
        clock, link, order, steps = (0.0, [0.0, 0.0], [], list(steps))

        def ready_at(entry):
            step, item, way, offset = entry
            if (item, offset) not in opened:
                return None
            when = opened[(item, offset)]
            sides = (0, 1) if way is None else ((way,) if step > self.first(item, way) else ())
            for side in sides:
                if (item, side, step - 1) not in arrival:
                    return None
                when = max(when, arrival[(item, side, step - 1)])
            return max(when, sends.get((item, used[item] - 2), 0.0))

        while waiting or steps:
            best = None
            for entry in waiting:
                when = ready_at(entry)
                if when is None or (entry[2] is None and (steps or any(other[2] is not None for other in waiting if ready_at(other) is not None and ready_at(other) <= clock))):
                    continue
                backlog = 0.0 if entry[2] is None else max(0.0, link[entry[2]] - max(clock, when))
                rank = (max(when, clock) + 0.5 * backlog, entry[0])
                if best is None or rank < best[0]:
                    best = (rank, entry, when)
            far_off = best is None or best[2] > clock + 0.3
            idle = best is not None and best[1][2] is not None and link[best[1][2]] > clock + ends
            if steps and (far_off or idle):
                spent, step, opens = steps.pop(0)
                clock += spent
                for item, offset in opens:
                    opened[(item, offset)] = clock + 2.0 + self.bytes_of(item) / 2e5
                order.append((step, opens))
                continue
            _, entry, when = best
            waiting.remove(entry)
            step, item, way, offset = entry
            clock = max(clock, when) + 0.8 + self.bytes_of(item) * 1.6e-6
            if way is not None:
                link[way] = max(clock, link[way]) + 2 * self.bytes_of(item) / 9.4e4
                arrival[(item, way, step)] = link[way] + 1.5
                sends[(item, used[item])] = link[way]
            order.append(entry + (used[item] % 2,))
            used[item] += 1
        return order, clock

    def follow(self, order):
        entries = [number for number, action in enumerate(order) if len(action) == 5]
        fetched = set()
        for number, action in enumerate(order):
            if len(action) == 2:
                step, opens = action
                step()
                for item, offset in opens:
                    self.pair_copy(item, offset).start()
                    self.exchanged.append((item, offset))
                continue
            if number not in fetched:
                self.fetch(action)
                fetched.add(number)
            if number + 1 in entries:
                following = order[number + 1]
                if following[1] != action[1]:
                    self.fetch(following)
                    fetched.add(number + 1)
            self.work(action)

    def work(self, entry):
        step, item, way, offset, buffer = entry
        array, start, rows, _ = self.items[item]
        half, final = (self.half, self.final)
        kind = self.parts[array].dtype
        columns = self.parts[array].shape[2]
        chunk = 16
        mine, pairs, rings = (self.mine[item], self.pairs[item], self.rings[item])
        if way is None:
            for side in (0, 1):
                self.ring_copy(item, side, half).wait_recv()
                self.load_ring(item, side, half, side).start()
            self.load_mine(item, offset, buffer).wait()
            self.load_pair(item, offset, buffer).wait()
            for side in (0, 1):
                self.load_ring(item, side, half, side).wait()
            if kind == F32:
                self.outs[array][...] = (rings[0] + rings[1]) + (mine[buffer] + pairs[buffer])
                return
            high, wide = (min(rows, final.shape[1]), min(columns, final.shape[2]))
            for top in range(0, rows, high):
                for across in range(0, columns, wide):
                    number = len(self.final_copies)
                    turn = number % final.shape[0]
                    if number >= final.shape[0]:
                        self.final_copies[number - final.shape[0]].wait()
                    span = pl.ds(across, wide)

                    @pl.loop(0, high // chunk)
                    def _(index):
                        here = pl.ds(pl.multiple_of(top + index * chunk, chunk), chunk)
                        final[turn, pl.ds(pl.multiple_of(index * chunk, chunk), chunk), pl.ds(0, wide)] = (
                            rings[0, here, span].astype(F32) + rings[1, here, span].astype(F32)
                        ) + (mine[buffer, here, span].astype(F32) + pairs[buffer, here, span].astype(F32))

                    self.final_copies.append(
                        pltpu.make_async_copy(
                            final.at[turn, pl.ds(0, high), pl.ds(0, wide)],
                            self.outs[array].at[pl.ds(start + top, high), span],
                            self.final_sem.at[turn],
                        )
                    )
                    self.final_copies[-1].start()
            return
        carried = step > self.first(item, way)
        if carried:
            self.ring_copy(item, way, step - 1).wait_recv()
            self.load_ring(item, way, step - 1, buffer).start()
        self.load_mine(item, offset, buffer).wait()
        self.load_pair(item, offset, buffer).wait()
        if carried:
            self.load_ring(item, way, step - 1, buffer).wait()

        @pl.loop(0, rows // chunk)
        def _(index):
            here = pl.ds(pl.multiple_of(index * chunk, chunk), chunk)
            total = mine[buffer, here, :].astype(F32) + pairs[buffer, here, :].astype(F32)
            if carried:
                total = rings[buffer, here, :].astype(F32) + total
            mine[buffer, here, :] = total.astype(kind)

        copy = self.ring_copy(item, way, step, buffer)
        copy.start()
        self.sent[(item, buffer)] = copy

    def close(self):
        for copy in self.sent.values():
            copy.wait_send()
        for item, offset in self.exchanged:
            self.pair_copy(item, offset).wait_send()
        for copy in self.final_copies[-self.final.shape[0] :]:
            copy.wait()


class Products:
    def __init__(self, chips, width, own, cuts, big, stage, cut_sem, big_sem, stage_sem):
        self.chips, self.width, self.own = (chips, width, own)
        self.cuts, self.big, self.stage = (cuts, big, stage)
        self.cut_sem, self.big_sem, self.stage_sem = (cut_sem, big_sem, stage_sem)

    def load_cut(self, source, index, slot):
        cut = self.cuts.shape[2]
        window = pl.ds(pl.multiple_of(index * cut, cut), cut)
        return pltpu.make_async_copy(source.at[:, window], self.cuts.at[slot], self.cut_sem.at[slot])

    def block(self, source, index, slot):
        window = pl.ds(pl.multiple_of(index * self.width, self.width), self.width)
        return pltpu.make_async_copy(source.at[:, window], self.big.at[slot], self.big_sem.at[slot])

    def keep(self, target, index):
        window = pl.ds(index // 2 * self.width, self.width)
        return pltpu.make_async_copy(
            self.stage.at[index % 2],
            target.at[pl.ds(index % 2 * self.chips, self.chips), :, window],
            self.stage_sem.at[index % 2],
        )

    def open(self, left, right, slot):
        for index in (0, 1):
            self.load_cut(left, index, index).start()
        self.block(right, 0, slot).start()

    def run(self, target, left, right, shift, index):
        number = 2 * (right.shape[1] // self.width)
        slot, here = (index % 2, (index // 2 + shift) % 2)
        if index == 0:
            for side in (0, 1):
                self.load_cut(left, side, side).wait()
        if slot == 0:
            self.block(right, index // 2, here).wait()
            if index + 2 < number:
                self.block(right, index // 2 + 1, 1 - here).start()
        if index >= 2:
            self.keep(target, index - 2).wait()
        product = dot_left(self.cuts[slot], self.big[here]).astype(LOW)
        for device in range(self.chips):
            self.stage[slot, device] = product[device * self.own : (device + 1) * self.own]
        self.keep(target, index).start()

    def close(self, target, right):
        number = 2 * (right.shape[1] // self.width)
        for index in (number - 2, number - 1):
            self.keep(target, index).wait()


def last_backward_kernel(chips, items, cell, *refs):
    count = len(items)
    (grad_h, entry_h, rows, packed_h, middle_h, slope_h, w_qkv, w_out, w_up, w_down) = refs[:10]
    (activated_h, grad_ff_h, second_h, mixed_h, lowered_h) = refs[10:15]
    refs = refs[15 + 5 :]
    rows_o, packed_o, branch_o, inner_o, sums_o = refs[:5]
    outs, parts = (refs[5:10], refs[10:14])
    landed, paired = (refs[14 : 14 + count], refs[14 + count : 14 + 2 * count])
    refs = refs[14 + 2 * count :]
    ring_buffers = (refs[:count], refs[count : 2 * count], refs[2 * count : 3 * count])
    final, small_v, both_v = refs[3 * count : 3 * count + 3]
    sems = refs[3 * count + 3 : 3 * count + 9]
    refs = refs[3 * count + 9 :]
    (big, cuts, stage, stage_down, big_sem, cut_sem, stage_sem) = refs[:7]
    (buffers, buffer_sems, load_sems, save_sems, slope_sems, inner_sems) = refs[7:13]
    (grad, entry, packed_v, middle_v, slope_v, inner_v, grad_packed_v, mixed_v, branch_v, grad_act_v, total_v, sums_v) = refs[13:]
    parts = [small_v] + list(parts)
    down_part, up_part = (parts[4], parts[3])
    length, width = grad.shape
    devices = 2 * chips
    deep_own = down_part.shape[1]
    ups = w_up.shape[1] // width
    first = lax.axis_index("pipe") == 0
    ring = RingSum(chips, items, parts, outs, landed, paired, ring_buffers, final, sems)
    half, position = (ring.half, ring.position)
    products = Products(chips, width, width // devices, cuts, big, stage, cut_sem, big_sem, stage_sem)
    gains = rows.at[0:2]

    def farthest_first(index):
        step = index // 2
        return ring_chip(position + (half - step if index % 2 == 0 else half + step + 1), chips)

    def keep_down(index):
        return pltpu.make_async_copy(
            stage_down.at[index % 2],
            down_part.at[pl.ds(farthest_first(index) * 2, 2)],
            stage_sem.at[2 + index % 2],
        )

    def cut_down(index):
        return products.load_cut(activated_h, farthest_first(index), index % 2)

    def down_product(index):
        def step():
            slot = index % 2
            if index == 0:
                for at in range(cell + 1):
                    ff_load(at).wait()
            if index + 1 < chips:
                cut_down(index + 1).start()
            cut_down(index).wait()
            if index == 2 or index >= 5:
                keep_down(index - 2).wait()
            product = dot_left(cuts[slot], big[0]).astype(LOW)
            for side in (0, 1):
                stage_down[slot, side] = product[side * deep_own : (side + 1) * deep_own]
            keep_down(index).start()
            if index == 2:
                for at in (1, 2):
                    keep_down(at).wait()
            if index == chips - 1:
                for at in (chips - 2, chips - 1):
                    keep_down(at).wait()

        return step

    def here(ref, at):
        return ref.at[pl.ds(at * length, length)]

    def ff_load(at):
        return pltpu.make_async_copy(here(grad_ff_h, at), here(big.at[0], at), load_sems.at[at])

    def ff_arrived():
        return pltpu.make_async_copy(grad_h, here(big.at[0], cell), load_sems.at[cell])

    for at in range(cell):
        ff_load(at).start()
    pl.when(first)(lambda: ff_arrived().start())
    pl.when(jnp.logical_not(first))(lambda: ff_load(cell).start())
    cut_down(0).start()

    def own_load(number):
        source, target = (
            (grad_h, grad),
            (entry_h, entry),
            (middle_h.at[cell], middle_v),
            (packed_h.at[cell], packed_v),
        )[number]
        return pltpu.make_async_copy(source, target, load_sems.at[cell + 1 + number])

    def slope_load(number):
        window = pl.ds(number * width, width)
        return pltpu.make_async_copy(
            slope_h.at[cell].at[:, window], slope_v.at[number % 2], slope_sems.at[number % 2]
        )

    order, place_up, place_down = ([], {}, {})
    for number in range(ups + 1):
        if number < ups:
            place_down[number] = len(order)
            order.append((w_down, 0, number))
        if number > 0:
            place_up[number - 1] = len(order)
            order.append((w_up, 1, number - 1))
    place_out = len(order)
    order = order + [(w_out, 0, 0)] + [(w_qkv, 1, number) for number in range(3)]
    depth = buffers.shape[0]

    def weight_load(number):
        ref, axis, at = order[number]
        window = pl.ds(at * width, width)
        source = ref.at[:, window] if axis else ref.at[window, :]
        return pltpu.make_async_copy(source, buffers.at[number % depth], buffer_sems.at[number % depth])

    def take(number):
        weight_load(number).wait()
        return buffers.at[number % depth]

    def release(number):
        if number + depth < len(order):
            weight_load(number + depth).start()

    def save(number, wait=False):
        source, target = (
            (branch_v, branch_o.at[pl.ds(cell * length, length)]),
            (grad_packed_v, packed_o.at[pl.ds(cell * length, length)]),
            (sums_v, sums_o.at[cell]),
            (mixed_v, rows_o.at[cell]),
        )[number]
        copy = pltpu.make_async_copy(source, target, save_sems.at[number])
        copy.wait() if wait else copy.start()

    def inner_save(number):
        window = pl.ds(number * width, width)
        return pltpu.make_async_copy(
            inner_v.at[number % 2], inner_o.at[pl.ds(cell * length, length), window], inner_sems.at[number % 2]
        )

    def column_sum(array):
        return jnp.sum(array.astype(F32), axis=0, keepdims=True)

    def begin():
        own_load(0).start()
        slope_load(0).start()
        for number in range(depth):
            weight_load(number).start()
        for number in (1, 2, 3):
            own_load(number).start()
        own_load(0).wait()
        sums_v[7:8, :] = column_sum(grad[...])

    def climb(number):
        def step():
            if number < ups:
                down_block = take(place_down[number])
                grad_act_v[number % 2] = dot_right(grad[...], down_block[...])
                release(place_down[number])
            if number > 0:
                at = number - 1
                slope_load(at).wait()
                if at + 1 < ups:
                    slope_load(at + 1).start()
                up_block = take(place_up[at])
                if at >= 2:
                    inner_save(at - 2).wait()
                inner = (grad_act_v[at % 2] * slope_v[at % 2].astype(F32)).astype(LOW)
                inner_v[at % 2] = inner
                sums_v[8 + at : 9 + at, :] = column_sum(inner)
                part = dot_right(inner, up_block[...])
                if at == 0:
                    total_v[...] = part
                else:
                    total_v[...] += part
                inner_save(at).start()
                release(place_up[at])

        return step

    def turn():
        own_load(2).wait()
        normed, inverse = row_norm(middle_v[...])
        grad_second = total_v[...]
        sums_v[1:2, :] = column_sum(grad_second * normed)
        sums_v[6:7, :] = column_sum(grad_second)
        grad_middle = grad[...].astype(F32) + norm_back(grad_second * gains[1:2, :], normed, inverse)
        middle_v[...] = grad_middle
        branch_v[...] = grad_middle.astype(LOW)
        sums_v[5:6, :] = column_sum(branch_v[...])
        save(0)
        save(0, wait=True)
        for at in range(max(0, ups - 2), ups):
            inner_save(at).wait()

    def outer():
        block = take(place_out)
        mixed_v[...] = dot_right(branch_v[...], block[...]).astype(LOW)
        release(place_out)
        own_load(3).wait()

    def heads(low, high):
        def step():
            attend_back(packed_v, mixed_v, grad_packed_v, width, low, high)

        return step

    def sums():
        save(1)
        sums_v[3:4, :] = column_sum(grad_packed_v[:, pl.ds(0, width)])
        sums_v[4:5, :] = column_sum(grad_packed_v[:, pl.ds(2 * width, width)])
        save(1, wait=True)

    def lower(number):
        def step():
            block = take(place_out + 1 + number)
            part = dot_right(grad_packed_v[:, pl.ds(number * width, width)], block[...])
            if number == 0:
                total_v[...] = part
            else:
                total_v[...] += part
            release(place_out + 1 + number)

        return step

    def finish():
        own_load(1).wait()
        normed, inverse = row_norm(entry[...].astype(F32))
        grad_lowered = total_v[...]
        sums_v[0:1, :] = column_sum(grad_lowered * normed)
        sums_v[2:3, :] = column_sum(grad_lowered)
        mixed_v[...] = (middle_v[...] + norm_back(grad_lowered * gains[0:1, :], normed, inverse)).astype(LOW)
        save(2)
        save(3)

    def lay_small():
        @pl.when(first)
        def _():
            save(2, wait=True)

        copy = pltpu.make_async_copy(sums_o, both_v, load_sems.at[0])
        copy.start()
        copy.wait()
        sums = both_v[0]
        for at in range(1, cell + 1):
            sums = sums + both_v[at]
        own = width // devices
        windows = [pltpu.roll(sums, (width - at * own) % width, 1)[:, :own] for at in range(devices)]
        share = devices // ups
        for device in range(devices):
            small_v[device, 0:8, :] = windows[device][0:8]
            for up in range(ups):
                row = 8 + device // share
                small_v[device, 8 + up : 9 + up, :] = windows[device % share * ups + up][row : row + 1]
            small_v[device, 8 + ups : 16, :] = jnp.zeros((8 - ups, own), F32)

    pairs = width // 128
    downs = [item for item in range(count) if items[item][0] == 4]
    up_items = [item for item in range(count) if items[item][0] == 3]
    outers = [item for item in range(count) if items[item][0] == 2]
    head_items = [item for item in range(count) if items[item][0] == 1]
    smalls = [item for item in range(count) if items[item][0] == 0]
    far = [half, half - 1, half + 1]
    near = [offset for offset in range(chips) if offset not in far]
    everywhere = far + near

    def only_first(step):
        return lambda: pl.when(first)(step)

    def product(target, left, right, shift, index):
        def step():
            products.run(target, left, right, shift, index)
            if index + 1 == 2 * (right.shape[1] // width):
                products.close(target, right)

        return step

    def all_of(wanted, offsets):
        return [(item, offset) for offset in offsets for item in wanted]

    def opening(left, right, shift):
        return lambda: products.open(left, right, shift)

    def blocks(target, left, right, shift, wanted):
        number = 2 * (right.shape[1] // width)
        made = [(0.3, opening(left, right, shift), [])]
        for index in range(number):
            opens = all_of(wanted, everywhere) if index + 1 == number else []
            made.append((1.8, product(target, left, right, shift, index), opens))
        return made

    steps = [(1.8, down_product(index), all_of(downs, far) if index == 2 else []) for index in range(3)]
    steps.append((0.3, only_first(begin), []))
    for index in range(3, chips):
        steps.append((1.8, down_product(index), all_of(downs, near) if index == chips - 1 else []))
    steps += [(1.7 if number in (0, ups) else 3.0, only_first(climb(number)), []) for number in range(ups + 1)]
    steps.append((2.5, only_first(turn), []))
    steps += blocks(up_part, second_h, inner_o, 1, up_items)
    steps += blocks(parts[2], mixed_h, branch_o, 1, outers)
    steps.append((1.7, only_first(outer), []))
    steps += [(1.25, only_first(heads(low, low + 1)), []) for low in range(pairs)]
    steps.append((0.8, only_first(sums), []))
    steps += blocks(parts[1], lowered_h, packed_o, 0, head_items)
    steps += [(1.5, only_first(lower(number)), []) for number in range(3)]
    steps.append((2.5, only_first(finish), []))
    steps.append((2.0, lay_small, all_of(smalls, everywhere)))
    greet((ring.left, ring.right, ring.sibling))
    schedule, _ = ring.arrange(steps, 8.0)
    ring.follow(schedule)
    ring.close()

    @pl.when(first)
    def _():
        save(3, wait=True)


def last_backward(arrived, entry, rows, saved, weights, kept, sides, items, shapes, count):
    chips = count // 2
    length, width = arrived.shape
    deep = weights[2].shape[1]
    cells = kept[0].shape[0]
    rows_in = cells * length
    own = width // count
    hbm = pl.BlockSpec(memory_space=pl.ANY)
    cut = width // 2
    wholes = [(16, own)] + [tuple(shape) for shape in shapes]
    held = [(many,) + wholes[array][1:] for array, _, many, _ in items]
    kinds = [F32 if array == 0 else LOW for array, _, _, _ in items]
    pieces = len(items)
    flops = 2 * length * width * (4 * width + 2 * deep) + 2 * rows_in * width * (4 * width + 2 * deep)
    outs = pl.pallas_call(
        functools.partial(last_backward_kernel, chips, items, cells - 1),
        out_shape=[jax.ShapeDtypeStruct(array.shape, array.dtype) for array in kept]
        + [jax.ShapeDtypeStruct(shape, F32) for shape in wholes]
        + [jax.ShapeDtypeStruct((count,) + shape, LOW) for shape in wholes[1:]]
        + [jax.ShapeDtypeStruct((chips - 1,) + shape, kind) for shape, kind in zip(held, kinds)]
        + [jax.ShapeDtypeStruct((chips,) + shape, kind) for shape, kind in zip(held, kinds)],
        in_specs=[hbm] * 2 + [pl.BlockSpec(memory_space=pltpu.VMEM)] + [hbm] * 17,
        out_specs=[hbm] * 5 + [pl.BlockSpec(memory_space=pltpu.VMEM)] + [hbm] * (8 + 2 * pieces),
        input_output_aliases={15 + number: number for number in range(5)},
        scratch_shapes=[pltpu.VMEM((2,) + shape, kind) for shape, kind in zip(held, kinds)] * 3
        + [
            pltpu.VMEM((4, 80, width), F32),
            pltpu.VMEM((count, 16, own), F32),
            pltpu.VMEM((cells, 16, width), F32),
            pltpu.SemaphoreType.DMA((pieces, chips - 1)),
            pltpu.SemaphoreType.DMA((pieces, chips - 1)),
            pltpu.SemaphoreType.DMA((pieces, chips)),
            pltpu.SemaphoreType.DMA((pieces, chips)),
            pltpu.SemaphoreType.DMA((pieces, 6)),
            pltpu.SemaphoreType.DMA((4,)),
            pltpu.VMEM((2, rows_in, width), LOW),
            pltpu.VMEM((2, rows_in, cut), LOW),
            pltpu.VMEM((2, chips, own, width), LOW),
            pltpu.VMEM((2, 2, shapes[3][0], width), LOW),
            pltpu.SemaphoreType.DMA((2,)),
            pltpu.SemaphoreType.DMA((2,)),
            pltpu.SemaphoreType.DMA((4,)),
            pltpu.VMEM((2, width, width), LOW),
            pltpu.SemaphoreType.DMA((2,)),
            pltpu.SemaphoreType.DMA((cells + 4,)),
            pltpu.SemaphoreType.DMA((4,)),
            pltpu.SemaphoreType.DMA((2,)),
            pltpu.SemaphoreType.DMA((2,)),
            pltpu.VMEM((length, width), LOW),
            pltpu.VMEM((length, width), LOW),
            pltpu.VMEM((length, 3 * width), LOW),
            pltpu.VMEM((length, width), F32),
            pltpu.VMEM((2, length, width), LOW),
            pltpu.VMEM((2, length, width), LOW),
            pltpu.VMEM((length, 3 * width), LOW),
            pltpu.VMEM((length, width), LOW),
            pltpu.VMEM((length, width), LOW),
            pltpu.VMEM((2, length, width), F32),
            pltpu.VMEM((length, width), F32),
            pltpu.VMEM((16, width), F32),
        ],
        compiler_params=pltpu.CompilerParams(
            collective_id=2, has_side_effects=True, vmem_limit_bytes=62 * 2**20
        ),
        cost_estimate=pl.CostEstimate(flops=flops, bytes_accessed=160 * width * width, transcendentals=0),
    )(arrived, entry, rows, *saved, *weights, *sides, *kept)
    return (list(outs[:5]), outs[5:10])


def on_device(inputs, out_grad, query_counts, gains, shifts, w_qkv, w_out, w_up, b_up, w_down):
    stage = lax.axis_index("pipe")
    stages = lax.axis_size("pipe")
    count = lax.axis_size("dp")
    cell_count, length, width = inputs.shape
    own = width // count
    ups = b_up.shape[1] // own
    deep = ups * width
    deep_own = w_down.shape[1]
    shapes = [
        block_shape(own, 3 * width),
        block_shape(own, width),
        block_shape(own, deep),
        block_shape(deep_own, width),
    ]
    cut = (shapes[3][0] // 2 + 15) // 16 * 16
    items = (
        (0, 0, 16, 0),
        (1, 0, shapes[0][0], 0),
        (2, 0, shapes[1][0], 0),
        (3, 0, shapes[2][0], 1),
        (4, 0, cut, 0),
        (4, cut, shapes[3][0] - cut, 1),
    )
    shards = [small_pack(gains[0], shifts[0], b_up[0], 1)[0]] + [
        array[0].reshape(shape) for array, shape in zip((w_qkv, w_out, w_up, w_down), shapes)
    ]
    fused = stages == 2 and cell_count == 2 and own % 16 == 0 and width % 256 == 0 and 4 * deep_own == width
    if fused:
        piece = own // 2 // 16 * 16
        arrivals = (
            (0, 0, 16, 0),
            (1, 0, own - piece, 0),
            (1, own - piece, piece, 1),
            (2, 0, own, 1),
            (3, 0, own - piece, 0),
            (3, own - piece, piece, 1),
            (4, 0, cut, 0),
            (4, cut, deep_own - cut, 1),
        )
        packs, rows, arrived, later, kept = gather_forward(
            shards, inputs, arrivals, ((0, 1, 2, 3), (4, 5), (6, 7)), count
        )
    else:
        packs = gather(shards, items, count)
        gain_rows, shift_rows, bias = small_split(packs[0].astype(F32), ups)
        blank = jnp.zeros((8 - ups, width), F32)
        rows = jnp.concatenate([gain_rows, shift_rows, bias.reshape(ups, width), blank])
    weights = (
        packs[1].reshape(width, 3 * width),
        packs[2].reshape(width, width),
        packs[3].reshape(width, deep),
        packs[4].reshape(deep, width),
    )
    scales = jnp.sqrt(query_counts.astype(F32) / 500.0)

    def along(value, steps):
        pairs = [(source, source + steps) for source in range(stages) if 0 <= source + steps < stages]
        return lax.ppermute(value, "pipe", pairs)

    entries = [[inputs[cell] for cell in range(cell_count)]]
    if fused:
        entries.append([arrived] + [along(later, 1)])
    else:
        kept = None
    for turn in range(1 if fused else 0, stages):
        active = (stage == turn).astype(jnp.int32)[None]
        arrived = []
        for cell in range(cell_count):
            sent, kept = forward_tick(active, entries[turn][cell], rows, weights, kept, cell, cell_count)
            if turn + 1 < stages:
                arrived.append(along(sent, 1))
        entries.append(arrived)
    section_out, lowered, packed, mixed, middle, second, activated, slope = kept
    incoming = [(out_grad[cell], scales[cell][None]) for cell in range(cell_count)]
    back = None
    for turn in range(stages - 1, -1, -1):
        active = (stage == turn).astype(jnp.int32)[None]
        arrived = []
        for cell in range(cell_count):
            if fused and turn == 0 and cell == cell_count - 1:
                continue
            sent, back = backward_tick(
                active, incoming[cell], entries[turn][cell], rows, (packed, middle, slope), weights, back, cell, cell_count
            )
            if turn > 0:
                arrived.append((along(sent, -1), jnp.ones((1,), F32)))
        incoming = arrived if turn > 0 else incoming

    def flat(array):
        return array.reshape(cell_count * length, -1)

    input_grads, grad_packed, grad_branch, grad_inner, grad_ff, sums = back
    if fused:
        (input_grads, grad_packed, grad_branch, grad_inner, sums), shares = last_backward(
            incoming[-1][0],
            entries[0][-1],
            rows,
            (packed, middle, slope),
            weights,
            (input_grads, flat(grad_packed), flat(grad_branch), flat(grad_inner), sums),
            [flat(array) for array in (activated, grad_ff, second, mixed, lowered)],
            arrivals,
            shapes,
            count,
        )
    else:
        sums = jnp.sum(sums, axis=0)
        small_part = small_pack(sums[0:2], sums[2:8], sums[8 : 8 + ups].reshape(deep), count)
        sides = [flat(array) for array in (lowered, grad_packed, mixed, grad_branch, second, grad_inner, activated, grad_ff)]
        products = [dot_left(sides[at], sides[at + 1]).astype(LOW) for at in (0, 2, 4, 6)]
        parts = [small_part] + [whole.reshape((count,) + shape) for whole, shape in zip(products, shapes)]
        shares = scatter(parts, items, count)
    grad_gains, grad_shifts, grad_bias = small_split(shares[0][None], ups)
    return (
        section_out[None],
        input_grads[None],
        grad_gains[None],
        grad_shifts[None],
        shares[1].reshape(1, own, 3 * width),
        shares[2].reshape(1, own, width),
        shares[3].reshape(1, own, deep),
        grad_bias[None],
        shares[4].reshape(1, deep_own, width),
    )


def solution(mesh):
    in_specs = (
        P("dp", None, None),
        P("dp", None, None),
        P("dp"),
        P("pipe", None, "dp"),
        P("pipe", None, "dp"),
        P("pipe", "dp", None),
        P("pipe", "dp", None),
        P("pipe", "dp", None),
        P("pipe", "dp"),
        P("pipe", "dp", None),
    )
    out_specs = (
        P("pipe", "dp", None, None),
        P("pipe", "dp", None, None),
        P("pipe", None, "dp"),
        P("pipe", None, "dp"),
        P("pipe", "dp", None),
        P("pipe", "dp", None),
        P("pipe", "dp", None),
        P("pipe", "dp"),
        P("pipe", "dp", None),
    )
    return jax.shard_map(
        on_device, mesh=mesh, in_specs=in_specs, out_specs=out_specs, check_vma=False
    )
```

```python
import functools
import math

import jax
import jax.numpy as jnp
from jax import lax
from jax.experimental import pallas as pl
from jax.experimental.pallas import tpu as pltpu
from jax.sharding import PartitionSpec as P

HEAD_DIM = 64
MESH = pl.DeviceIdType.MESH
LOW = jnp.bfloat16
F32 = jnp.float32


def ring_chip(position, chips):
    position = lax.rem(position + 2 * chips, chips)
    half = chips // 2
    return jnp.where(position < half, 2 * position, 2 * (chips - 1 - position) + 1)


def ring_place(chips):
    me = lax.axis_index("dp")
    core = lax.rem(me, 2)
    chip = me // 2
    position = jnp.where(lax.rem(chip, 2) == 0, chip // 2, chips - 1 - chip // 2)
    right = ring_chip(position + 1, chips) * 2 + core
    left = ring_chip(position - 1, chips) * 2 + core
    return (me, core, position, right, left, me + 1 - 2 * core)


def greet(devices):
    barrier = pltpu.get_barrier_semaphore()
    for device in devices:
        pl.semaphore_signal(barrier, inc=1, device_id={"dp": device}, device_id_type=MESH)
    pl.semaphore_wait(barrier, len(devices))


def gather_kernel(chips, arrays, items, *refs):
    count = len(items)
    ring_send, ring_recv, pair_send, pair_recv, own_sem = refs[2 * arrays :]
    shards = [refs[array].at[pl.ds(start, rows)] for array, start, rows, _ in items]
    splits = [way for _, _, _, way in items]
    half = chips // 2
    me, core, position, right, left, sibling = ring_place(chips)
    greet((left, right, sibling))

    def out(item, block):
        array, start, rows, _ = items[item]
        return refs[arrays + array].at[block, pl.ds(start, rows)]

    def owner(step, way):
        return ring_chip(position - step if way == 0 else position + step, chips) * 2 + core

    def travels(item, way, step):
        return step < half or (step == half and splits[item] == way)

    def ring_copy(item, way, step):
        block = owner(step - 1, way)
        return pltpu.make_async_remote_copy(
            src_ref=shards[item] if step == 1 else out(item, block),
            dst_ref=out(item, block),
            send_sem=ring_send.at[item, way, step - 1],
            recv_sem=ring_recv.at[item, way, step - 1],
            device_id={"dp": right if way == 0 else left},
            device_id_type=MESH,
        )

    def pair_copy(item, offset, block, source):
        return pltpu.make_async_remote_copy(
            src_ref=source,
            dst_ref=out(item, block),
            send_sem=pair_send.at[item, offset],
            recv_sem=pair_recv.at[item, offset],
            device_id={"dp": sibling},
            device_id_type=MESH,
        )

    sent, paired, kept = ([], [], [])
    for item in range(count):
        for way in (0, 1):
            if travels(item, way, 1):
                sent.append(ring_copy(item, way, 1))
                sent[-1].start()
    for item in range(count):
        paired.append(pair_copy(item, 0, me, shards[item]))
        paired[-1].start()
        kept.append(pltpu.make_async_copy(shards[item], out(item, me), own_sem.at[item]))
        kept[-1].start()
    for step in range(1, half + 1):
        for item in range(count):
            for way in (0, 1):
                if not travels(item, way, step):
                    continue
                ring_copy(item, way, step).wait_recv()
                if travels(item, way, step + 1):
                    sent.append(ring_copy(item, way, step + 1))
                    sent[-1].start()
                block = owner(step, way)
                offset = step if way == 0 else chips - step
                paired.append(pair_copy(item, offset, block, out(item, block)))
                paired[-1].start()
    for copy in sent:
        copy.wait_send()
    for copy in paired:
        copy.wait()
    for copy in kept:
        copy.wait()


def gather(shards, items, count):
    chips = count // 2
    arrays, pieces = (len(shards), len(items))
    return pl.pallas_call(
        functools.partial(gather_kernel, chips, arrays, items),
        out_shape=[jax.ShapeDtypeStruct((count,) + shard.shape, shard.dtype) for shard in shards],
        in_specs=[pl.BlockSpec(memory_space=pl.ANY)] * arrays,
        out_specs=[pl.BlockSpec(memory_space=pl.ANY)] * arrays,
        scratch_shapes=[
            pltpu.SemaphoreType.DMA((pieces, 2, chips // 2)),
            pltpu.SemaphoreType.DMA((pieces, 2, chips // 2)),
            pltpu.SemaphoreType.DMA((pieces, chips)),
            pltpu.SemaphoreType.DMA((pieces, chips)),
            pltpu.SemaphoreType.DMA((pieces,)),
        ],
        compiler_params=pltpu.CompilerParams(collective_id=0, has_side_effects=True),
    )(*shards)


def scatter_kernel(chips, arrays, items, *refs):
    count = len(items)
    parts, outs, refs = (refs[:arrays], refs[arrays : 2 * arrays], refs[2 * arrays :])
    landed, paired, mine = (refs[:count], refs[count : 2 * count], refs[2 * count : 3 * count])
    ring_send, ring_recv, pair_send, pair_recv, mine_sem = refs[3 * count :]
    splits = [way for _, _, _, way in items]
    half = chips // 2
    me, core, position, right, left, sibling = ring_place(chips)
    greet((left, right, sibling))

    def part(item, block):
        array, start, rows, _ = items[item]
        return parts[array].at[block, pl.ds(start, rows)]

    def first(item, way):
        return 1 if splits[item] == way else 2

    def slot(item, way, step):
        return step - 1 if splits[item] == way else half + step - 2

    def offset_of(step, way):
        return half - step + 1 if way == 0 else chips - (half - step + 1)

    def pair_copy(item, offset):
        block = ring_chip(position + offset, chips) * 2 + 1 - core
        return pltpu.make_async_remote_copy(
            src_ref=part(item, block),
            dst_ref=paired[item].at[offset],
            send_sem=pair_send.at[item, offset],
            recv_sem=pair_recv.at[item, offset],
            device_id={"dp": sibling},
            device_id_type=MESH,
        )

    def ring_copy(item, way, step):
        if step == first(item, way):
            source = paired[item].at[offset_of(step, way)]
        else:
            source = landed[item].at[slot(item, way, step - 1)]
        here = slot(item, way, step)
        return pltpu.make_async_remote_copy(
            src_ref=source,
            dst_ref=landed[item].at[here],
            send_sem=ring_send.at[item, here],
            recv_sem=ring_recv.at[item, here],
            device_id={"dp": right if way == 0 else left},
            device_id_type=MESH,
        )

    def load(item, offset, buffer):
        block = ring_chip(position + offset, chips) * 2 + core
        return pltpu.make_async_copy(part(item, block), mine[item].at[buffer], mine_sem.at[item, buffer])

    plan, uses = ([], [0] * count)
    for step in range(1, half + 2):
        for item in range(count):
            for way in (0, 1):
                if step <= half and step >= first(item, way):
                    plan.append((step, item, way, offset_of(step, way), uses[item] % 2))
                    uses[item] += 1
            if step > half:
                plan.append((step, item, None, 0, uses[item] % 2))
                uses[item] += 1
    for step, item, way, offset, buffer in plan:
        pair_copy(item, offset).start()
    load(plan[0][1], plan[0][3], plan[0][4]).start()
    sent = []
    for number, (step, item, way, offset, buffer) in enumerate(plan):
        if number + 1 < len(plan):
            load(plan[number + 1][1], plan[number + 1][3], plan[number + 1][4]).start()
        load(item, offset, buffer).wait()
        pair_copy(item, offset).wait_recv()
        array, start, rows, _ = items[item]
        kind = parts[array].dtype
        chunk = 16 if rows % 16 == 0 else rows
        from_pair, from_mine, from_ring = (paired[item], mine[item], landed[item])
        if way is None:
            ring_copy(item, 0, half).wait_recv()
            ring_copy(item, 1, half).wait_recv()
            slot_a, slot_b = (slot(item, 0, half), slot(item, 1, half))

            @pl.loop(0, rows // chunk)
            def _(index):
                here = pl.ds(pl.multiple_of(index * chunk, chunk), chunk)
                outs[array][pl.ds(pl.multiple_of(start + index * chunk, chunk), chunk), :] = (
                    from_ring[slot_a, here, :].astype(F32) + from_ring[slot_b, here, :].astype(F32)
                ) + (from_mine[buffer, here, :].astype(F32) + from_pair[offset, here, :].astype(F32))

            continue
        if step == first(item, way):

            @pl.loop(0, rows // chunk)
            def _(index):
                here = pl.ds(pl.multiple_of(index * chunk, chunk), chunk)
                from_pair[offset, here, :] = (
                    from_mine[buffer, here, :].astype(F32) + from_pair[offset, here, :].astype(F32)
                ).astype(kind)

        else:
            ring_copy(item, way, step - 1).wait_recv()
            arrived = slot(item, way, step - 1)

            @pl.loop(0, rows // chunk)
            def _(index):
                here = pl.ds(pl.multiple_of(index * chunk, chunk), chunk)
                from_ring[arrived, here, :] = (
                    from_ring[arrived, here, :].astype(F32)
                    + (from_mine[buffer, here, :].astype(F32) + from_pair[offset, here, :].astype(F32))
                ).astype(kind)

        sent.append(ring_copy(item, way, step))
        sent[-1].start()
    for copy in sent:
        copy.wait_send()
    for step, item, way, offset, buffer in plan:
        pair_copy(item, offset).wait_send()


def scatter(parts, items, count):
    chips = count // 2
    arrays, pieces = (len(parts), len(items))
    shapes = [(rows,) + parts[array].shape[2:] for array, _, rows, _ in items]
    kinds = [parts[array].dtype for array, _, _, _ in items]
    return pl.pallas_call(
        functools.partial(scatter_kernel, chips, arrays, items),
        out_shape=[jax.ShapeDtypeStruct(part.shape[1:], F32) for part in parts],
        in_specs=[pl.BlockSpec(memory_space=pl.ANY)] * arrays,
        out_specs=[pl.BlockSpec(memory_space=pltpu.VMEM)] * arrays,
        scratch_shapes=[pltpu.VMEM((chips - 1,) + shape, kind) for shape, kind in zip(shapes, kinds)]
        + [pltpu.VMEM((chips,) + shape, kind) for shape, kind in zip(shapes, kinds)]
        + [pltpu.VMEM((2,) + shape, kind) for shape, kind in zip(shapes, kinds)]
        + [
            pltpu.SemaphoreType.DMA((pieces, chips - 1)),
            pltpu.SemaphoreType.DMA((pieces, chips - 1)),
            pltpu.SemaphoreType.DMA((pieces, chips)),
            pltpu.SemaphoreType.DMA((pieces, chips)),
            pltpu.SemaphoreType.DMA((pieces, 2)),
        ],
        compiler_params=pltpu.CompilerParams(
            collective_id=1, has_side_effects=True, vmem_limit_bytes=62 * 2**20
        ),
    )(*parts)


def block_shape(rows, columns):
    return (rows, columns) if rows % 16 == 0 else (rows * columns // 128, 128)


def small_pack(gains, shifts, bias, count):
    width = gains.shape[1] // count
    ups = bias.shape[0] // gains.shape[1]
    rows = [
        gains.reshape(2, count, width).swapaxes(0, 1),
        shifts.reshape(6, count, width).swapaxes(0, 1),
        bias.reshape(count, ups, width),
    ]
    blank = jnp.zeros((count, 8 - ups, width), gains.dtype)
    return jnp.concatenate(rows + [blank], axis=1)


def small_split(blocks, ups):
    count, _, width = blocks.shape
    gains = blocks[:, 0:2].swapaxes(0, 1).reshape(2, count * width)
    shifts = blocks[:, 2:8].swapaxes(0, 1).reshape(6, count * width)
    bias = blocks[:, 8 : 8 + ups].reshape(count * ups * width)
    return (gains, shifts, bias)


def row_norm(rows_in):
    center = rows_in - jnp.mean(rows_in, axis=-1, keepdims=True)
    inverse = lax.rsqrt(jnp.mean(center * center, axis=-1, keepdims=True) + 1e-05)
    return (center * inverse, inverse)


def norm_back(grad_rows, normed, inverse):
    return inverse * (
        grad_rows
        - jnp.mean(grad_rows, axis=-1, keepdims=True)
        - normed * jnp.mean(grad_rows * normed, axis=-1, keepdims=True)
    )


def gelu_parts(hidden):
    cumulative = 0.5 * (1.0 + lax.erf(hidden * (1.0 / math.sqrt(2.0))))
    slope = cumulative + hidden * jnp.exp(-0.5 * hidden * hidden) * (1.0 / math.sqrt(2.0 * math.pi))
    return (hidden * cumulative, slope)


def dot(left, right):
    return lax.dot_general(left, right, (((1,), (0,)), ((), ())), preferred_element_type=F32)


def dot_right(left, right):
    return lax.dot_general(left, right, (((1,), (1,)), ((), ())), preferred_element_type=F32)


def dot_left(left, right):
    return lax.dot_general(left, right, (((0,), (0,)), ((), ())), preferred_element_type=F32)


class Stream:
    def __init__(self, blocks, buffers, sems):
        self.blocks, self.buffers, self.sems = (blocks, buffers, sems)
        self.depth = buffers.shape[0]
        self.started = 0
        for _ in range(min(self.depth, len(blocks))):
            self.start()

    def copy(self, number):
        slot = number % self.depth
        return pltpu.make_async_copy(self.blocks[number], self.buffers.at[slot], self.sems.at[slot])

    def start(self):
        self.copy(self.started).start()
        self.started += 1

    def take(self, number):
        self.copy(number).wait()
        return self.buffers.at[number % self.depth]

    def release(self):
        if self.started < len(self.blocks):
            self.start()


def weight_blocks(w_qkv, w_out, w_up, w_down):
    width = w_out.shape[0]
    def cut(ref, axis, number):
        window = pl.ds(number * width, width)
        return ref.at[:, window] if axis else ref.at[window, :]
    heads = [cut(w_qkv, 1, number) for number in range(3)]
    ups = [cut(w_up, 1, number) for number in range(w_up.shape[1] // width)]
    downs = [cut(w_down, 0, number) for number in range(w_down.shape[0] // width)]
    return (heads, w_out, ups, downs)


def head_masks(length):
    return lax.broadcasted_iota(jnp.int32, (length, 128), 1) < HEAD_DIM


def two_heads(array, side):
    blank = jnp.zeros_like(array)
    return jnp.concatenate([jnp.where(side, array, blank), jnp.where(side, blank, array)], axis=0)


def attend(packed, mixed, width, low=0, high=None):
    length = packed.shape[0]
    side = head_masks(length)

    def pair_of(pair):
        start = pair * 128 if isinstance(pair, int) else pl.multiple_of(pair * 128, 128)
        queries = packed[:, pl.ds(start, 128)] * jnp.asarray(1.0 / math.sqrt(HEAD_DIM), LOW)
        keys = two_heads(packed[:, pl.ds(start + width, 128)], side)
        values = two_heads(packed[:, pl.ds(start + 2 * width, 128)], side)
        scores = dot_right(queries, keys)
        probs, totals = ([], [])
        for head in (0, 1):
            mine = scores[:, head * length : (head + 1) * length]
            shifted = jnp.exp(mine - jnp.max(mine, axis=-1, keepdims=True))
            totals.append(1.0 / jnp.sum(shifted, axis=-1, keepdims=True))
            probs.append(shifted.astype(LOW))
        result = dot(jnp.concatenate(probs, axis=1), values)
        mixed[:, pl.ds(start, 128)] = (result * jnp.where(side, totals[0], totals[1])).astype(LOW)

    if high is not None:
        for pair in range(low, high):
            pair_of(pair)
        return

    @pl.loop(0, width // 256)
    def _(index):
        pair_of(index * 2)
        pair_of(index * 2 + 1)


def attend_back(packed, grad_mixed, grad_packed, width, low=0, high=None):
    length = packed.shape[0]
    side = head_masks(length)
    scale = 1.0 / math.sqrt(HEAD_DIM)

    def pair_of(pair):
        start = pair * 128 if isinstance(pair, int) else pl.multiple_of(pair * 128, 128)
        queries = packed[:, pl.ds(start, 128)]
        keys = packed[:, pl.ds(start + width, 128)] * jnp.asarray(scale, LOW)
        grads = grad_mixed[:, pl.ds(start, 128)]
        keys_two = two_heads(keys, side)
        queries_two = two_heads(queries, side)
        grads_two = two_heads(grads, side)
        scores = dot_right(keys, queries_two)
        grad_probs = dot_right(packed[:, pl.ds(start + 2 * width, 128)], grads_two)
        probs, grad_scores = ([], [])
        for head in (0, 1):
            mine = slice(head * length, (head + 1) * length)
            shifted = jnp.exp(scores[:, mine] - jnp.max(scores[:, mine], axis=0, keepdims=True))
            prob = shifted * (1.0 / jnp.sum(shifted, axis=0, keepdims=True))
            product = grad_probs[:, mine] * prob
            weighted = jnp.sum(product, axis=0, keepdims=True)
            probs.append(prob.astype(LOW))
            grad_scores.append((product - prob * weighted).astype(LOW))
        beside = jnp.concatenate(grad_scores, axis=1)
        grad_packed[:, pl.ds(start, 128)] = dot_left(jnp.concatenate(grad_scores, axis=0), keys_two).astype(LOW)
        grad_packed[:, pl.ds(start + width, 128)] = (dot(beside, queries_two) * scale).astype(LOW)
        grad_packed[:, pl.ds(start + 2 * width, 128)] = dot(jnp.concatenate(probs, axis=1), grads_two).astype(LOW)

    if high is not None:
        for pair in range(low, high):
            pair_of(pair)
        return

    @pl.loop(0, width // 256)
    def _(index):
        pair_of(index * 2)
        pair_of(index * 2 + 1)


def forward_kernel(cell, held, at, active, entry_h, rows, w_qkv, w_out, w_up, w_down, *refs):
    sent_h = refs[held]
    out_h, lowered_h, packed_h, mixed_h, middle_h, second_h, active_h, slope_h = [
        ref.at[cell] for ref in refs[held + 1 : held + 9]
    ]
    (buffers, buffer_sems, save_sems, out_v, lowered_v, packed_v, mixed_v, middle_v) = refs[held + 9 : held + 17]
    (second_v, active_v, slope_v, hidden_v, total_v, entry, entry_sem) = refs[held + 17 :]
    entry = entry_h if at is None else entry
    width = entry.shape[1]
    gains, shifts, bias = (rows.at[0:2], rows.at[2:8], rows.at[8:16])
    ups = w_up.shape[1] // width

    @pl.when(active[0] != 0)
    def _():
        heads, outer, up, down = weight_blocks(w_qkv, w_out, w_up, w_down)
        order = heads + [outer]
        place_up, place_down = ({}, {})
        for number in range(ups + 1):
            if number < ups:
                place_up[number] = len(order)
                order.append(up[number])
            if number > 0:
                place_down[number - 1] = len(order)
                order.append(down[number - 1])
        if at is not None:
            fetched = pltpu.make_async_copy(entry_h.at[at], entry, entry_sem)
            fetched.start()
        saves = []

        def save(source, target):
            saves.append(pltpu.make_async_copy(source, target, save_sems.at[len(saves)]))
            saves[-1].start()

        if at is not None:
            fetched.wait()
        stream = Stream(order, buffers, buffer_sems)
        rows_in = entry[...].astype(F32)
        normed, _ = row_norm(rows_in)
        lowered_v[...] = (normed * gains[0:1, :] + shifts[0:1, :]).astype(LOW)
        save(lowered_v, lowered_h)
        for number in range(3):
            block = stream.take(number)
            window = pl.ds(number * width, width)
            part = dot(lowered_v[...], block[...])
            if number != 1:
                part = part + shifts[1 + number // 2 : 2 + number // 2, :]
            packed_v[:, window] = part.astype(LOW)
            stream.release()
        save(packed_v, packed_h)
        attend(packed_v, mixed_v, width)
        save(mixed_v, mixed_h)
        block = stream.take(3)
        middle = entry[...].astype(F32) + dot(mixed_v[...], block[...]) + shifts[3:4, :]
        middle_v[...] = middle
        stream.release()
        save(middle_v, middle_h)
        normed, _ = row_norm(middle_v[...])
        second_v[...] = (normed * gains[1:2, :] + shifts[4:5, :]).astype(LOW)
        save(second_v, second_h)
        for number in range(ups + 1):
            if number < ups:
                up_block = stream.take(place_up[number])
            if number > 0:
                down_block = stream.take(place_down[number - 1])
            if number < ups:
                hidden_v[number % 2] = dot(second_v[...], up_block[...]) + bias[number : number + 1, :]
            if number > 0:
                window = pl.ds((number - 1) * width, width)
                activated, slope = gelu_parts(hidden_v[(number - 1) % 2])
                active_v[:, window] = activated.astype(LOW)
                slope_v[:, window] = slope.astype(LOW)
                part = dot(active_v[:, window], down_block[...])
                if number == 1:
                    total_v[...] = part
                elif number < ups:
                    total_v[...] += part
                else:
                    out_v[...] = (middle_v[...] + (total_v[...] + part + shifts[5:6, :])).astype(LOW)
                save(active_v.at[:, window], active_h.at[:, window])
                save(slope_v.at[:, window], slope_h.at[:, window])
            if number < ups:
                stream.release()
            if number > 0:
                stream.release()
        save(out_v, sent_h)
        save(out_v, out_h)
        for copy in saves:
            copy.wait()


def kept_shapes(length, width, deep):
    return [
        ((length, width), LOW),
        ((length, width), LOW),
        ((length, 3 * width), LOW),
        ((length, width), LOW),
        ((length, width), F32),
        ((length, width), LOW),
        ((length, deep), LOW),
        ((length, deep), LOW),
    ]


def forward_tick(active, entry, rows, weights, kept, cell, cell_count):
    entry, at = entry
    length, width = entry.shape[-2:]
    deep = weights[2].shape[1]
    ups = deep // width
    shapes = kept_shapes(length, width, deep)
    outs = [jax.ShapeDtypeStruct(*shapes[0])] + [
        jax.ShapeDtypeStruct((cell_count,) + shape, kind) for shape, kind in shapes
    ]
    vmem, hbm = (pl.BlockSpec(memory_space=pltpu.VMEM), pl.BlockSpec(memory_space=pl.ANY))
    flops = 2 * length * width * (4 * width + 2 * deep) + 16 * length * length * width
    kept = () if kept is None else tuple(kept)
    held = len(kept)
    sent, *kept = pl.pallas_call(
        functools.partial(forward_kernel, cell, held, at),
        out_shape=outs,
        in_specs=[pl.BlockSpec(memory_space=pltpu.SMEM), vmem if at is None else hbm, vmem] + [hbm] * (4 + held),
        out_specs=[hbm] * 9,
        input_output_aliases={7 + number: 1 + number for number in range(held)},
        scratch_shapes=[
            pltpu.VMEM((4, width, width), LOW),
            pltpu.SemaphoreType.DMA((4,)),
            pltpu.SemaphoreType.DMA((7 + 2 * ups,)),
        ]
        + [pltpu.VMEM(*shape) for shape in shapes]
        + [
            pltpu.VMEM((2, length, width), F32),
            pltpu.VMEM((length, width), F32),
            pltpu.VMEM((length, width), LOW),
            pltpu.SemaphoreType.DMA,
        ],
        compiler_params=pltpu.CompilerParams(vmem_limit_bytes=60 * 2**20),
        cost_estimate=pl.CostEstimate(
            flops=flops, bytes_accessed=2 * width * (4 * width + 2 * deep), transcendentals=0
        ),
    )(active, entry, rows, *weights, *kept)
    return (sent, kept)


def backward_kernel(cell, held, grad_at, entry_at, active, scale, grad_h, entry_h, rows, *refs):
    packed, middle, slope = [ref.at[cell] for ref in refs[:3]]
    w_qkv, w_out, w_up, w_down = refs[3:7]
    refs = refs[7 + held :]
    sent_h = refs[0]
    rows_h, packed_h, branch_h, inner_h, low_h, sums_h = [ref.at[cell] for ref in refs[1:7]]
    (buffers, buffer_sems, load_sems, save_sems, rows_v, grad_packed_v, branch_v, inner_v, low_v, sums_v) = refs[7:17]
    (packed_v, middle_v, slope_v, mixed_v, grad_act_v, total_v, grad_middle_v, grad, entry) = refs[17:]
    gains = rows.at[0:2]
    grad = grad_h if grad_at is None else grad
    entry_h = entry_h if entry_at is None else entry_h.at[entry_at]
    length, width = entry.shape
    ups = w_up.shape[1] // width

    @pl.when(active[0] != 0)
    def _():
        heads, outer, up, down = weight_blocks(w_qkv, w_out, w_up, w_down)
        loads = [
            pltpu.make_async_copy(slope, slope_v, load_sems.at[0]),
            pltpu.make_async_copy(middle, middle_v, load_sems.at[1]),
            pltpu.make_async_copy(packed, packed_v, load_sems.at[2]),
            pltpu.make_async_copy(entry_h, entry, load_sems.at[3]),
        ]
        if grad_at is not None:
            loads.append(pltpu.make_async_copy(grad_h.at[grad_at], grad, load_sems.at[4]))
            loads[4].start()
        order, place_up, place_down = ([], {}, {})
        for number in range(ups + 1):
            if number < ups:
                place_down[number] = len(order)
                order.append(down[number])
            if number > 0:
                place_up[number - 1] = len(order)
                order.append(up[number - 1])
        place_out = len(order)
        order = order + [outer] + heads
        saves = []

        def save(source, target):
            saves.append(pltpu.make_async_copy(source, target, save_sems.at[len(saves)]))
            saves[-1].start()

        def column_sum(array):
            return jnp.sum(array.astype(F32), axis=0, keepdims=True)

        if grad_at is not None:
            loads[4].wait()
        stream = Stream(order, buffers, buffer_sems)
        loads[0].start()
        low_v[...] = (grad[...].astype(F32) * scale[0]).astype(LOW)
        save(low_v, low_h)
        sums_v[7:8, :] = column_sum(low_v[...])
        for number in range(ups + 1):
            if number == 1:
                loads[0].wait()
                loads[1].start()
            if number == 2:
                loads[2].start()
                loads[3].start()
            if number < ups:
                down_block = stream.take(place_down[number])
            if number > 0:
                up_block = stream.take(place_up[number - 1])
            if number < ups:
                grad_act_v[number % 2] = dot_right(low_v[...], down_block[...])
            if number > 0:
                window = pl.ds((number - 1) * width, width)
                inner = (grad_act_v[(number - 1) % 2] * slope_v[:, window].astype(F32)).astype(LOW)
                inner_v[:, window] = inner
                sums_v[7 + number : 8 + number, :] = column_sum(inner)
                part = dot_right(inner, up_block[...])
                if number == 1:
                    total_v[...] = part
                else:
                    total_v[...] += part
                save(inner_v.at[:, window], inner_h.at[:, window])
            if number < ups:
                stream.release()
            if number > 0:
                stream.release()
        loads[1].wait()
        normed, inverse = row_norm(middle_v[...])
        grad_second = total_v[...]
        sums_v[1:2, :] = column_sum(grad_second * normed)
        sums_v[6:7, :] = column_sum(grad_second)
        grad_middle = grad[...].astype(F32) * scale[0] + norm_back(grad_second * gains[1:2, :], normed, inverse)
        grad_middle_v[...] = grad_middle
        branch_v[...] = grad_middle.astype(LOW)
        sums_v[5:6, :] = column_sum(branch_v[...])
        save(branch_v, branch_h)
        block = stream.take(place_out)
        mixed_v[...] = dot_right(branch_v[...], block[...]).astype(LOW)
        stream.release()
        loads[2].wait()
        attend_back(packed_v, mixed_v, grad_packed_v, width)
        save(grad_packed_v, packed_h)
        sums_v[3:4, :] = column_sum(grad_packed_v[:, pl.ds(0, width)])
        sums_v[4:5, :] = column_sum(grad_packed_v[:, pl.ds(2 * width, width)])
        for number in range(3):
            block = stream.take(place_out + 1 + number)
            part = dot_right(grad_packed_v[:, pl.ds(number * width, width)], block[...])
            if number == 0:
                total_v[...] = part
            else:
                total_v[...] += part
            stream.release()
        loads[3].wait()
        normed, inverse = row_norm(entry[...].astype(F32))
        grad_lowered = total_v[...]
        sums_v[0:1, :] = column_sum(grad_lowered * normed)
        sums_v[2:3, :] = column_sum(grad_lowered)
        rows_v[...] = (grad_middle_v[...] + norm_back(grad_lowered * gains[0:1, :], normed, inverse)).astype(LOW)
        save(sums_v, sums_h)
        save(rows_v, sent_h)
        save(rows_v, rows_h)
        for copy in saves:
            copy.wait()


def backward_tick(active, incoming, entry, rows, saved, weights, kept, cell, cell_count):
    entry, entry_at = entry
    (grad, grad_at), scale = incoming
    length, width = entry.shape[-2:]
    deep = weights[2].shape[1]
    ups = deep // width
    shapes = [
        ((length, width), LOW),
        ((length, 3 * width), LOW),
        ((length, width), LOW),
        ((length, deep), LOW),
        ((length, width), LOW),
        ((16, width), F32),
    ]
    outs = [jax.ShapeDtypeStruct(*shapes[0])] + [
        jax.ShapeDtypeStruct((cell_count,) + shape, kind) for shape, kind in shapes
    ]
    vmem, hbm = (pl.BlockSpec(memory_space=pltpu.VMEM), pl.BlockSpec(memory_space=pl.ANY))
    smem = pl.BlockSpec(memory_space=pltpu.SMEM)
    flops = 2 * length * width * (4 * width + 2 * deep) + 40 * length * length * width
    kept = () if kept is None else tuple(kept)
    held = len(kept)
    sent, *kept = pl.pallas_call(
        functools.partial(backward_kernel, cell, held, grad_at, entry_at),
        out_shape=outs,
        in_specs=[smem] * 2 + [vmem if grad_at is None else hbm, hbm, vmem] + [hbm] * (7 + held),
        out_specs=[hbm] * 7,
        input_output_aliases={12 + number: 1 + number for number in range(held)},
        scratch_shapes=[
            pltpu.VMEM((4, width, width), LOW),
            pltpu.SemaphoreType.DMA((4,)),
            pltpu.SemaphoreType.DMA((5,)),
            pltpu.SemaphoreType.DMA((6 + ups,)),
        ]
        + [pltpu.VMEM(*shape) for shape in shapes]
        + [
            pltpu.VMEM((length, 3 * width), LOW),
            pltpu.VMEM((length, width), F32),
            pltpu.VMEM((length, deep), LOW),
            pltpu.VMEM((length, width), LOW),
            pltpu.VMEM((2, length, width), F32),
            pltpu.VMEM((length, width), F32),
            pltpu.VMEM((length, width), F32),
            pltpu.VMEM((length, width), LOW),
            pltpu.VMEM((length, width), LOW),
        ],
        compiler_params=pltpu.CompilerParams(vmem_limit_bytes=60 * 2**20),
        cost_estimate=pl.CostEstimate(
            flops=flops, bytes_accessed=2 * width * (4 * width + 2 * deep), transcendentals=0
        ),
    )(active, scale, grad, entry, rows, *saved, *weights, *kept)
    return (sent, kept)


def small_rows(small, rows, width, ups):
    devices, _, own = small.shape
    lane = lax.broadcasted_iota(jnp.int32, (own, width), 1)
    depth = lax.broadcasted_iota(jnp.int32, (own, width), 0)
    row = lax.broadcasted_iota(jnp.int32, (16, width), 0)
    across = lax.broadcasted_iota(jnp.int32, (16, width), 1)
    top = jnp.zeros((16, width), F32)
    for device in range(devices):
        spot = jnp.where(lane == depth + device * own, 1.0, 0.0).astype(LOW)
        top = top + dot(small[device], spot)
    rows[0:8, :] = top[0:8]
    share = devices // ups
    for block in range(ups):
        total = jnp.zeros((1, width), F32)
        for index in range(share):
            start = index * ups * own
            spot = jnp.zeros((own, width), F32)
            for up in range(ups):
                spot = spot + jnp.where(lane == depth + (start + up * own), 1.0, 0.0)
            low = start + (row - 8) * own
            inside = (row >= 8) & (row < 8 + ups) & (across >= low) & (across < low + own)
            placed = dot(small[block * share + index], spot.astype(LOW))
            total = total + jnp.sum(jnp.where(inside, placed, 0.0), axis=0, keepdims=True)
        rows[8 + block : 9 + block, :] = total


def gather_forward_kernel(chips, items, groups, cells, *refs):
    shards, inputs_h = (refs[:5], refs[5])
    outs, rows_h, arrived_h, later_h = (refs[6:11], refs[11], refs[12], refs[13])
    out_h, lowered_h, packed_h, mixed_h, middle_h, second_h, active_h, slope_h = refs[14:22]
    (ring_send, ring_recv, pair_send, pair_recv, own_sem, hop_send, hop_recv) = refs[22:29]
    (load_sem, save_sem, wide_sem, deep_sem) = refs[29:33]
    (small_v, rows_v, entry_v, out_v, lowered_v, packed_v, mixed_v, middle_v, second_v, active_v, slope_v) = refs[33:44]
    (total_v, hidden_v, wide_v, deep_v) = refs[44:]
    length, width = entry_v.shape[1:]
    ups = active_v.shape[2] // width
    half = chips // 2
    me, core, position, right, left, sibling = ring_place(chips)
    stage = lax.axis_index("pipe")
    first = stage == 0
    barrier = pltpu.get_barrier_semaphore()
    for device in (left, right, sibling):
        pl.semaphore_signal(barrier, inc=1, device_id={"dp": device}, device_id_type=MESH)
    pl.semaphore_signal(barrier, inc=1, device_id={"pipe": 1 - stage}, device_id_type=MESH)
    pl.semaphore_wait(barrier, 4)

    def shard(item):
        array, start, rows, _ = items[item]
        return shards[array].at[pl.ds(start, rows)]

    def out(item, block):
        array, start, rows, _ = items[item]
        return outs[array].at[block, pl.ds(start, rows)]

    def owner(step, way):
        return ring_chip(position - step if way == 0 else position + step, chips) * 2 + core

    def travels(item, way, step):
        return step < half or (step == half and items[item][3] == way)

    def ring_copy(item, way, step):
        block = owner(step - 1, way)
        return pltpu.make_async_remote_copy(
            src_ref=shard(item) if step == 1 else out(item, block),
            dst_ref=out(item, block),
            send_sem=ring_send.at[item, way, step - 1],
            recv_sem=ring_recv.at[item, way, step - 1],
            device_id={"dp": right if way == 0 else left},
            device_id_type=MESH,
        )

    def pair_copy(item, offset, block, source):
        return pltpu.make_async_remote_copy(
            src_ref=source,
            dst_ref=out(item, block),
            send_sem=pair_send.at[item, offset],
            recv_sem=pair_recv.at[item, offset],
            device_id={"dp": sibling},
            device_id_type=MESH,
        )

    def own_copy(item):
        return pltpu.make_async_copy(shard(item), out(item, me), own_sem.at[item])

    sent, paired = ([], [])

    def open_group(group):
        for item in group:
            for way in (0, 1):
                if travels(item, way, 1):
                    sent.append(ring_copy(item, way, 1))
                    sent[-1].start()
        for item in group:
            paired.append(pair_copy(item, 0, me, shard(item)))
            paired[-1].start()
            own_copy(item).start()

    def ring_step(item, way, step):
        ring_copy(item, way, step).wait_recv()
        if travels(item, way, step + 1):
            sent.append(ring_copy(item, way, step + 1))
            sent[-1].start()
        block = owner(step, way)
        offset = step if way == 0 else chips - step
        paired.append(pair_copy(item, offset, block, out(item, block)))
        paired[-1].start()

    def pair_arrived(item, offset):
        block = ring_chip(position - offset, chips) * 2 + core
        pair_copy(item, offset, block, out(item, block)).wait_recv()

    saves = []

    def save(source, target):
        number = len(saves)
        saves.append(lambda: pltpu.make_async_copy(source(), target(), save_sem.at[number]))
        saves[-1]().start()

    def entry_load(cell):
        return pltpu.make_async_copy(inputs_h.at[cell], entry_v.at[cell], load_sem.at[cell])

    def wide_load(array, column, slot):
        source = outs[array].at[:, :, pl.ds(column * width, width)]
        return pltpu.make_async_copy(source, wide_v.at[slot], wide_sem.at[slot])

    def wide(slot):
        return wide_v[slot].reshape(width, width)

    def gains(number):
        return rows_v[number : number + 1, :]

    def shifts(number):
        return rows_v[2 + number : 3 + number, :]

    def begin(cell):
        def step():
            entry_load(cell).wait()
            normed, _ = row_norm(entry_v[cell].astype(F32))
            lowered_v[cell] = (normed * gains(0) + shifts(0)).astype(LOW)
            save(lambda: lowered_v.at[cell], lambda: lowered_h.at[cell])

        return step

    def project(cell, number):
        def step():
            if cell == 0:
                wide_load(1, number, number).wait()
            part = dot(lowered_v[cell], wide(number))
            if number != 1:
                part = part + shifts(1 + number // 2)
            packed_v[cell, :, pl.ds(number * width, width)] = part.astype(LOW)
            if number == 2:
                save(lambda: packed_v.at[cell], lambda: packed_h.at[cell])

        return step

    def mix(cell, low, high, last):
        def step():
            attend(packed_v.at[cell], mixed_v.at[cell], width, low, high)
            if last:
                save(lambda: mixed_v.at[cell], lambda: mixed_h.at[cell])

        return step

    def join(cell):
        def step():
            if cell == 0:
                wide_load(2, 0, 3).wait()
            middle_v[cell] = entry_v[cell].astype(F32) + dot(mixed_v[cell], wide(3)) + shifts(3)
            save(lambda: middle_v.at[cell], lambda: middle_h.at[cell])

        return step

    def renorm(cell):
        def step():
            middle = middle_v[cell]
            normed, _ = row_norm(middle)
            second_v[cell] = (normed * gains(1) + shifts(4)).astype(LOW)
            total_v[cell] = middle + shifts(5)
            save(lambda: second_v.at[cell], lambda: second_h.at[cell])

        return step

    def rise(cell, number):
        def step():
            if cell == 0:
                wide_load(3, number, number).wait()
            hidden_v[...] = dot(second_v[cell], wide(number)) + rows_v[8 + number : 9 + number, :]

        return step

    def bend(cell, number):
        def step():
            window = pl.ds(number * width, width)
            activated, slope = gelu_parts(hidden_v[...])
            active_v[cell, :, window] = activated.astype(LOW)
            slope_v[cell, :, window] = slope.astype(LOW)
            if number == ups - 1:
                save(lambda: active_v.at[cell], lambda: active_h.at[cell])
                save(lambda: slope_v.at[cell], lambda: slope_h.at[cell])

        return step

    deep_rows = deep_v.shape[1] * deep_v.shape[2]

    def deep_load(offset, slot):
        chip = ring_chip(position - offset, chips)
        return pltpu.make_async_copy(outs[4].at[pl.ds(chip * 2, 2)], deep_v.at[slot], deep_sem.at[slot])

    def fall(cell, offset, slot):
        def step():
            if cell == 0:
                deep_load(offset, slot).wait()
            chip = ring_chip(position - offset, chips)
            window = pl.ds(pl.multiple_of(chip * deep_rows, 128), deep_rows)
            total_v[cell] += dot(active_v[cell, :, window], deep_v[slot].reshape(deep_rows, width))

        return step

    def hop():
        return pltpu.make_async_remote_copy(
            src_ref=out_v.at[0],
            dst_ref=arrived_h,
            send_sem=hop_send,
            recv_sem=hop_recv,
            device_id={"pipe": 1 - stage},
            device_id_type=MESH,
        )

    def finish(cell):
        def step():
            out_v[cell] = total_v[cell].astype(LOW)
            if cell == 0:
                hop().start()
            else:
                save(lambda: out_v.at[cell], lambda: later_h)
            save(lambda: out_v.at[cell], lambda: out_h.at[cell])

        return step

    def on_first(step):
        pl.when(first)(step)

    queue = []

    def ready(group, steps, loads):
        for item in group:
            own_copy(item).wait()
            for offset in range(chips):
                pair_arrived(item, offset)

        @pl.when(first)
        def _():
            for load in loads:
                load().start()

        queue.extend(steps)

    pairs = width // 128
    heads = []
    for cell in range(cells):
        heads.append(begin(cell))
        heads += [project(cell, number) for number in range(3)]
        heads += [mix(cell, low, low + 2, low + 2 >= pairs) for low in range(0, pairs, 2)]
    joins = [make(cell) for cell in range(cells) for make in (join, renorm)]
    def load_ups():
        for number in range(ups):
            wide_load(3, number, number).start()

    climbs = [load_ups]
    climbs += [make(cell, number) for number in range(ups) for cell in range(cells) for make in (rise, bend)]

    @pl.when(first)
    def _():
        for cell in range(cells):
            entry_load(cell).start()

    def lay_rows():
        copy = pltpu.make_async_copy(outs[0], small_v, load_sem.at[cells])
        copy.start()
        copy.wait()
        small_rows(small_v, rows_v, width, ups)
        pltpu.make_async_copy(rows_v, rows_h, load_sem.at[cells + 1]).start()

    def ready_small():
        for item in groups[0]:
            if items[item][0] == 0:
                own_copy(item).wait()
                for offset in range(chips):
                    pair_arrived(item, offset)
        lay_rows()

    plan = []
    for number, group in enumerate(groups):
        for step in range(1, half + 1):
            if step == half and number + 1 < len(groups):
                plan.append(("open", number + 1))
            for item in group:
                for way in (0, 1):
                    if travels(item, way, step):
                        plan.append(("ring", item, way, step))
            if number == len(groups) - 1:
                plan.append(("deep", step))
        plan.append(("done", number))
    open_group(groups[0])
    late = []
    slots = [0]

    def deep_ready(offsets):
        for offset in offsets:
            for item in groups[-1]:
                if offset == 0:
                    own_copy(item).wait()
                pair_arrived(item, offset)
            slot = slots[0] % deep_v.shape[0]
            slots[0] += 1

            def opening(offset=offset, slot=slot):
                deep_load(offset, slot).start()

            queue.append(opening)
            queue.extend(fall(cell, offset, slot) for cell in range(cells))

    def serve(limit):
        for _ in range(limit):
            if queue:
                on_first(queue.pop(0))

    for entry in plan:
        if entry[0] == "open":
            open_group(groups[entry[1]])
        elif entry[0] == "ring":
            ring_step(*entry[1:])
            for wait in list(late):
                wait[0] -= 1
                if wait[0] == 0:
                    wait[1]()
                    late.remove(wait)
            serve(3 if entry[1] in groups[-1] else 2)
        elif entry[0] == "done":
            if entry[1] == 0:
                rest = [item for item in groups[0] if items[item][0] != 0]
                late.append([1, ready_small])
                late.append(
                    [
                        2,
                        lambda: ready(
                            rest,
                            heads + joins,
                            [functools.partial(wide_load, 1, number, number) for number in range(3)]
                            + [functools.partial(wide_load, 2, 0, 3)],
                        ),
                    ]
                )
            elif entry[1] == 1:
                late.append([2, lambda: ready(groups[1], climbs, [])])
        elif entry[0] == "deep":
            step = entry[1]
            if step == 1:
                late.append([3, lambda: deep_ready([0])])
            if step < half:
                late.append([2, lambda step=step: deep_ready([step, chips - step])])
            else:
                for wait in late:
                    wait[1]()
                serve(len(queue))
                deep_ready([half])
    serve(len(queue))
    for cell in range(cells):
        on_first(finish(cell))
    for copy in sent:
        copy.wait_send()
    for copy in paired:
        copy.wait_send()
    pltpu.make_async_copy(rows_v, rows_h, load_sem.at[cells + 1]).wait()

    @pl.when(first)
    def _():
        for copy in saves:
            copy().wait()
        hop().wait_send()

    @pl.when(jnp.logical_not(first))
    def _():
        hop().wait_recv()


def gather_forward(shards, inputs, items, groups, count):
    chips = count // 2
    cells, length, width = inputs.shape
    deep = shards[3].shape[1]
    ups = deep // width
    pieces = len(items)
    shapes = kept_shapes(length, width, deep)
    hbm = pl.BlockSpec(memory_space=pl.ANY)
    flops = 2 * cells * length * width * (4 * width + 2 * deep)
    outs = pl.pallas_call(
        functools.partial(gather_forward_kernel, chips, items, groups, cells),
        out_shape=[jax.ShapeDtypeStruct((count,) + shard.shape, shard.dtype) for shard in shards]
        + [
            jax.ShapeDtypeStruct((16, width), F32),
            jax.ShapeDtypeStruct((length, width), LOW),
            jax.ShapeDtypeStruct((length, width), LOW),
        ]
        + [jax.ShapeDtypeStruct((cells,) + shape, kind) for shape, kind in shapes],
        in_specs=[hbm] * 6,
        out_specs=[hbm] * 16,
        scratch_shapes=[
            pltpu.SemaphoreType.DMA((pieces, 2, chips // 2)),
            pltpu.SemaphoreType.DMA((pieces, 2, chips // 2)),
            pltpu.SemaphoreType.DMA((pieces, chips)),
            pltpu.SemaphoreType.DMA((pieces, chips)),
            pltpu.SemaphoreType.DMA((pieces,)),
            pltpu.SemaphoreType.DMA,
            pltpu.SemaphoreType.DMA,
            pltpu.SemaphoreType.DMA((cells + 2,)),
            pltpu.SemaphoreType.DMA((9 * cells,)),
            pltpu.SemaphoreType.DMA((4,)),
            pltpu.SemaphoreType.DMA((2,)),
            pltpu.VMEM((count,) + shards[0].shape, LOW),
            pltpu.VMEM((16, width), F32),
            pltpu.VMEM((cells, length, width), LOW),
        ]
        + [pltpu.VMEM((cells,) + shape, kind) for shape, kind in shapes]
        + [
            pltpu.VMEM((cells, length, width), F32),
            pltpu.VMEM((length, width), F32),
            pltpu.VMEM((4, count, width // count, width), LOW),
            pltpu.VMEM((2, 2, shards[4].shape[0], width), LOW),
        ],
        compiler_params=pltpu.CompilerParams(
            collective_id=3, has_side_effects=True, vmem_limit_bytes=62 * 2**20
        ),
        cost_estimate=pl.CostEstimate(flops=flops, bytes_accessed=8 * width * (4 * width + 2 * deep), transcendentals=0),
    )(*shards, inputs)
    return (outs[:5], outs[5], outs[6], outs[7], list(outs[8:]))


class RingSum:
    def __init__(self, chips, items, parts, outs, landed, paired, buffers, final, sems):
        self.chips, self.items, self.parts, self.outs = (chips, items, parts, outs)
        self.landed, self.paired, self.final = (landed, paired, final)
        self.mine, self.pairs, self.rings = buffers
        self.ring_send, self.ring_recv, self.pair_send, self.pair_recv, self.load_sem, self.final_sem = sems
        self.half = chips // 2
        self.me, self.core, self.position, self.right, self.left, self.sibling = ring_place(chips)
        self.sent, self.final_copies, self.exchanged = ({}, [], [])
        self.uses = [0] * len(items)

    def part(self, item, block):
        array, start, rows, _ = self.items[item]
        return self.parts[array].at[block, pl.ds(start, rows)]

    def first(self, item, way):
        return 1 if self.items[item][3] == way else 2

    def slot_of(self, item, way, step):
        return step - 1 if self.items[item][3] == way else self.half + step - 2

    def offset_of(self, step, way):
        return self.half - step + 1 if way == 0 else self.chips - (self.half - step + 1)

    def pair_copy(self, item, offset):
        block = ring_chip(self.position + offset, self.chips) * 2 + 1 - self.core
        return pltpu.make_async_remote_copy(
            src_ref=self.part(item, block),
            dst_ref=self.paired[item].at[offset],
            send_sem=self.pair_send.at[item, offset],
            recv_sem=self.pair_recv.at[item, offset],
            device_id={"dp": self.sibling},
            device_id_type=MESH,
        )

    def ring_copy(self, item, way, step, buffer=0):
        here = self.slot_of(item, way, step)
        return pltpu.make_async_remote_copy(
            src_ref=self.mine[item].at[buffer],
            dst_ref=self.landed[item].at[here],
            send_sem=self.ring_send.at[item, here],
            recv_sem=self.ring_recv.at[item, here],
            device_id={"dp": self.right if way == 0 else self.left},
            device_id_type=MESH,
        )

    def load_mine(self, item, offset, buffer):
        block = ring_chip(self.position + offset, self.chips) * 2 + self.core
        return pltpu.make_async_copy(self.part(item, block), self.mine[item].at[buffer], self.load_sem.at[item, buffer])

    def load_pair(self, item, offset, buffer):
        return pltpu.make_async_copy(
            self.paired[item].at[offset], self.pairs[item].at[buffer], self.load_sem.at[item, 2 + buffer]
        )

    def load_ring(self, item, way, step, buffer):
        return pltpu.make_async_copy(
            self.landed[item].at[self.slot_of(item, way, step)], self.rings[item].at[buffer], self.load_sem.at[item, 4 + buffer]
        )

    def starts(self, wanted):
        return [
            (step, item, way, self.offset_of(step, way))
            for step in (1, 2)
            for item in wanted
            for way in (0, 1)
            if step == self.first(item, way)
        ]

    def rest(self, wanted, steps):
        return [
            (step, item, way, self.offset_of(step, way))
            for step in steps
            if step <= self.half
            for item in wanted
            for way in (0, 1)
            if step > self.first(item, way)
        ] + [(step, item, None, 0) for step in steps if step > self.half for item in wanted]

    def fetch(self, entry):
        step, item, way, offset, buffer = entry
        if (item, buffer) in self.sent:
            self.sent.pop((item, buffer)).wait_send()
        self.load_mine(item, offset, buffer).start()
        self.pair_copy(item, offset).wait_recv()
        self.load_pair(item, offset, buffer).start()

    def bytes_of(self, item):
        array, _, rows, _ = self.items[item]
        return rows * self.parts[array].shape[2] * self.parts[array].dtype.itemsize

    def arrange(self, steps, ends):
        waiting = self.starts(range(len(self.items)))
        waiting += self.rest(range(len(self.items)), range(2, self.half + 2))
        opened, arrival, sends, used = ({}, {}, {}, [0] * len(self.items))
        clock, link, order, steps = (0.0, [0.0, 0.0], [], list(steps))

        def ready_at(entry):
            step, item, way, offset = entry
            if (item, offset) not in opened:
                return None
            when = opened[(item, offset)]
            sides = (0, 1) if way is None else ((way,) if step > self.first(item, way) else ())
            for side in sides:
                if (item, side, step - 1) not in arrival:
                    return None
                when = max(when, arrival[(item, side, step - 1)])
            return max(when, sends.get((item, used[item] - 2), 0.0))

        while waiting or steps:
            best = None
            for entry in waiting:
                when = ready_at(entry)
                if when is None or (entry[2] is None and (steps or any(other[2] is not None for other in waiting if ready_at(other) is not None and ready_at(other) <= clock))):
                    continue
                backlog = 0.0 if entry[2] is None else max(0.0, link[entry[2]] - max(clock, when))
                rank = (max(when, clock) + 0.5 * backlog, entry[0])
                if best is None or rank < best[0]:
                    best = (rank, entry, when)
            far_off = best is None or best[2] > clock + 0.3
            idle = best is not None and best[1][2] is not None and link[best[1][2]] > clock + ends
            if steps and (far_off or idle):
                spent, step, opens = steps.pop(0)
                clock += spent
                for item, offset in opens:
                    opened[(item, offset)] = clock + 2.0 + self.bytes_of(item) / 2e5
                order.append((step, opens))
                continue
            _, entry, when = best
            waiting.remove(entry)
            step, item, way, offset = entry
            clock = max(clock, when) + 0.8 + self.bytes_of(item) * 1.6e-6
            if way is not None:
                link[way] = max(clock, link[way]) + 2 * self.bytes_of(item) / 9.4e4
                arrival[(item, way, step)] = link[way] + 1.5
                sends[(item, used[item])] = link[way]
            order.append(entry + (used[item] % 2,))
            used[item] += 1
        return order, clock

    def follow(self, order):
        entries = [number for number, action in enumerate(order) if len(action) == 5]
        fetched = set()
        for number, action in enumerate(order):
            if len(action) == 2:
                step, opens = action
                step()
                for item, offset in opens:
                    self.pair_copy(item, offset).start()
                    self.exchanged.append((item, offset))
                continue
            if number not in fetched:
                self.fetch(action)
                fetched.add(number)
            if number + 1 in entries:
                following = order[number + 1]
                if following[1] != action[1]:
                    self.fetch(following)
                    fetched.add(number + 1)
            self.work(action)

    def work(self, entry):
        step, item, way, offset, buffer = entry
        array, start, rows, _ = self.items[item]
        half, final = (self.half, self.final)
        kind = self.parts[array].dtype
        columns = self.parts[array].shape[2]
        chunk = 16
        mine, pairs, rings = (self.mine[item], self.pairs[item], self.rings[item])
        if way is None:
            for side in (0, 1):
                self.ring_copy(item, side, half).wait_recv()
                self.load_ring(item, side, half, side).start()
            self.load_mine(item, offset, buffer).wait()
            self.load_pair(item, offset, buffer).wait()
            for side in (0, 1):
                self.load_ring(item, side, half, side).wait()
            if kind == F32:
                total = (rings[0] + rings[1]) + (mine[buffer] + pairs[buffer])
                top = 0
                for out in self.outs[array]:
                    out[...] = total[top : top + out.shape[0]]
                    top += out.shape[0]
                return
            high, wide = (min(rows, final.shape[1]), min(columns, final.shape[2]))
            for top in range(0, rows, high):
                for across in range(0, columns, wide):
                    number = len(self.final_copies)
                    turn = number % final.shape[0]
                    if number >= final.shape[0]:
                        self.final_copies[number - final.shape[0]].wait()
                    span = pl.ds(across, wide)

                    @pl.loop(0, high // chunk)
                    def _(index):
                        here = pl.ds(pl.multiple_of(top + index * chunk, chunk), chunk)
                        final[turn, pl.ds(pl.multiple_of(index * chunk, chunk), chunk), pl.ds(0, wide)] = (
                            rings[0, here, span].astype(F32) + rings[1, here, span].astype(F32)
                        ) + (mine[buffer, here, span].astype(F32) + pairs[buffer, here, span].astype(F32))

                    self.final_copies.append(
                        pltpu.make_async_copy(
                            final.at[turn, pl.ds(0, high), pl.ds(0, wide)],
                            self.outs[array].at[pl.ds(start + top, high), span],
                            self.final_sem.at[turn],
                        )
                    )
                    self.final_copies[-1].start()
            return
        carried = step > self.first(item, way)
        if carried:
            self.ring_copy(item, way, step - 1).wait_recv()
            self.load_ring(item, way, step - 1, buffer).start()
        self.load_mine(item, offset, buffer).wait()
        self.load_pair(item, offset, buffer).wait()
        if carried:
            self.load_ring(item, way, step - 1, buffer).wait()

        @pl.loop(0, rows // chunk)
        def _(index):
            here = pl.ds(pl.multiple_of(index * chunk, chunk), chunk)
            total = mine[buffer, here, :].astype(F32) + pairs[buffer, here, :].astype(F32)
            if carried:
                total = rings[buffer, here, :].astype(F32) + total
            mine[buffer, here, :] = total.astype(kind)

        copy = self.ring_copy(item, way, step, buffer)
        copy.start()
        self.sent[(item, buffer)] = copy

    def close(self):
        for copy in self.sent.values():
            copy.wait_send()
        for item, offset in self.exchanged:
            self.pair_copy(item, offset).wait_send()
        for copy in self.final_copies[-self.final.shape[0] :]:
            copy.wait()


class Products:
    def __init__(self, chips, width, own, cuts, big, stage, cut_sem, big_sem, stage_sem):
        self.chips, self.width, self.own = (chips, width, own)
        self.cuts, self.big, self.stage = (cuts, big, stage)
        self.cut_sem, self.big_sem, self.stage_sem = (cut_sem, big_sem, stage_sem)

    def load_cut(self, source, index, slot):
        cut = self.cuts.shape[2]
        window = pl.ds(pl.multiple_of(index * cut, cut), cut)
        return pltpu.make_async_copy(source.at[:, window], self.cuts.at[slot], self.cut_sem.at[slot])

    def block(self, source, index, slot):
        window = pl.ds(pl.multiple_of(index * self.width, self.width), self.width)
        return pltpu.make_async_copy(source.at[:, window], self.big.at[slot], self.big_sem.at[slot])

    def keep(self, target, index):
        window = pl.ds(index // 2 * self.width, self.width)
        return pltpu.make_async_copy(
            self.stage.at[index % 2],
            target.at[pl.ds(index % 2 * self.chips, self.chips), :, window],
            self.stage_sem.at[index % 2],
        )

    def open(self, left, right, slot):
        for index in (0, 1):
            self.load_cut(left, index, index).start()
        self.block(right, 0, slot).start()

    def run(self, target, left, right, shift, index):
        number = 2 * (right.shape[1] // self.width)
        slot, here = (index % 2, (index // 2 + shift) % 2)
        if index == 0:
            for side in (0, 1):
                self.load_cut(left, side, side).wait()
        if slot == 0:
            self.block(right, index // 2, here).wait()
            if index + 2 < number:
                self.block(right, index // 2 + 1, 1 - here).start()
        if index >= 2:
            self.keep(target, index - 2).wait()
        product = dot_left(self.cuts[slot], self.big[here]).astype(LOW)
        for device in range(self.chips):
            self.stage[slot, device] = product[device * self.own : (device + 1) * self.own]
        self.keep(target, index).start()

    def close(self, target, right):
        number = 2 * (right.shape[1] // self.width)
        for index in (number - 2, number - 1):
            self.keep(target, index).wait()


def last_backward_kernel(chips, items, cell, *refs):
    count = len(items)
    (grad, entry_h, rows, packed_h, middle_h, slope_h, w_qkv, w_out, w_up, w_down) = refs[:10]
    (activated_h, grad_ff_h, second_h, mixed_h, lowered_h) = refs[10:15]
    refs = refs[15 + 5 :]
    rows_o, packed_o, branch_o, inner_o, sums_o = refs[:5]
    outs, parts = ([refs[5:8]] + list(refs[8:12]), refs[12:16])
    landed, paired = (refs[16 : 16 + count], refs[16 + count : 16 + 2 * count])
    refs = refs[16 + 2 * count :]
    ring_buffers = (refs[:count], refs[count : 2 * count], refs[2 * count : 3 * count])
    final, small_v, both_v = refs[3 * count : 3 * count + 3]
    sems = refs[3 * count + 3 : 3 * count + 9]
    refs = refs[3 * count + 9 :]
    (big, cuts, stage, stage_down, big_sem, cut_sem, stage_sem) = refs[:7]
    (buffers, buffer_sems, load_sems, save_sems, slope_sems, inner_sems) = refs[7:13]
    (entry, packed_v, middle_v, slope_v, inner_v, grad_packed_v, mixed_v, branch_v, grad_act_v, total_v, sums_v) = refs[13:]
    parts = [small_v] + list(parts)
    down_part, up_part = (parts[4], parts[3])
    length, width = grad.shape
    devices = 2 * chips
    deep_own = down_part.shape[1]
    ups = w_up.shape[1] // width
    first = lax.axis_index("pipe") == 0
    ring = RingSum(chips, items, parts, outs, landed, paired, ring_buffers, final, sems)
    half, position = (ring.half, ring.position)
    products = Products(chips, width, width // devices, cuts, big, stage, cut_sem, big_sem, stage_sem)
    gains = rows.at[0:2]

    def farthest_first(index):
        step = index // 2
        return ring_chip(position + (half - step if index % 2 == 0 else half + step + 1), chips)

    def keep_down(index):
        return pltpu.make_async_copy(
            stage_down.at[index % 2],
            down_part.at[pl.ds(farthest_first(index) * 2, 2)],
            stage_sem.at[2 + index % 2],
        )

    def cut_down(index):
        return products.load_cut(activated_h, farthest_first(index), index % 2)

    def down_product(index):
        def step():
            slot = index % 2
            if index == 0:
                for at in range(cell + 1):
                    ff_load(at).wait()
            if index + 1 < chips:
                cut_down(index + 1).start()
            cut_down(index).wait()
            if index == 2 or index >= 5:
                keep_down(index - 2).wait()
            product = dot_left(cuts[slot], big[0]).astype(LOW)
            for side in (0, 1):
                stage_down[slot, side] = product[side * deep_own : (side + 1) * deep_own]
            keep_down(index).start()
            if index == 2:
                for at in (1, 2):
                    keep_down(at).wait()
            if index == chips - 1:
                for at in (chips - 2, chips - 1):
                    keep_down(at).wait()

        return step

    def here(ref, at):
        return ref.at[pl.ds(at * length, length)]

    def ff_load(at):
        return pltpu.make_async_copy(here(grad_ff_h, at), here(big.at[0], at), load_sems.at[at])

    def ff_arrived():
        return pltpu.make_async_copy(grad, here(big.at[0], cell), load_sems.at[cell])

    for at in range(cell):
        ff_load(at).start()
    pl.when(first)(lambda: ff_arrived().start())
    pl.when(jnp.logical_not(first))(lambda: ff_load(cell).start())
    cut_down(0).start()

    def own_load(number):
        source, target = ((entry_h, entry), (middle_h, middle_v), (packed_h, packed_v))[number - 1]
        return pltpu.make_async_copy(source.at[cell], target, load_sems.at[cell + 1 + number])

    def slope_load(number):
        window = pl.ds(number * width, width)
        return pltpu.make_async_copy(
            slope_h.at[cell].at[:, window], slope_v.at[number % 2], slope_sems.at[number % 2]
        )

    order, place_up, place_down = ([], {}, {})
    for number in range(ups + 1):
        if number < ups:
            place_down[number] = len(order)
            order.append((w_down, 0, number))
        if number > 0:
            place_up[number - 1] = len(order)
            order.append((w_up, 1, number - 1))
    place_out = len(order)
    order = order + [(w_out, 0, 0)] + [(w_qkv, 1, number) for number in range(3)]
    depth = buffers.shape[0]

    def weight_load(number):
        ref, axis, at = order[number]
        window = pl.ds(at * width, width)
        source = ref.at[:, window] if axis else ref.at[window, :]
        return pltpu.make_async_copy(source, buffers.at[number % depth], buffer_sems.at[number % depth])

    def take(number):
        weight_load(number).wait()
        return buffers.at[number % depth]

    def release(number):
        if number + depth < len(order):
            weight_load(number + depth).start()

    def save(number, wait=False):
        source, target = (
            (branch_v, branch_o.at[pl.ds(cell * length, length)]),
            (grad_packed_v, packed_o.at[pl.ds(cell * length, length)]),
            (sums_v, sums_o.at[cell]),
            (mixed_v, rows_o.at[cell]),
        )[number]
        copy = pltpu.make_async_copy(source, target, save_sems.at[number])
        copy.wait() if wait else copy.start()

    def inner_save(number):
        window = pl.ds(number * width, width)
        return pltpu.make_async_copy(
            inner_v.at[number % 2], inner_o.at[pl.ds(cell * length, length), window], inner_sems.at[number % 2]
        )

    def column_sum(array):
        return jnp.sum(array.astype(F32), axis=0, keepdims=True)

    def begin():
        slope_load(0).start()
        for number in range(depth):
            weight_load(number).start()
        for number in (1, 2, 3):
            own_load(number).start()
        sums_v[7:8, :] = column_sum(grad[...])

    def climb(number):
        def step():
            if number < ups:
                down_block = take(place_down[number])
                grad_act_v[number % 2] = dot_right(grad[...], down_block[...])
                release(place_down[number])
            if number > 0:
                at = number - 1
                slope_load(at).wait()
                if at + 1 < ups:
                    slope_load(at + 1).start()
                up_block = take(place_up[at])
                if at >= 2:
                    inner_save(at - 2).wait()
                inner = (grad_act_v[at % 2] * slope_v[at % 2].astype(F32)).astype(LOW)
                inner_v[at % 2] = inner
                sums_v[8 + at : 9 + at, :] = column_sum(inner)
                part = dot_right(inner, up_block[...])
                if at == 0:
                    total_v[...] = part
                else:
                    total_v[...] += part
                inner_save(at).start()
                release(place_up[at])

        return step

    def turn():
        own_load(2).wait()
        normed, inverse = row_norm(middle_v[...])
        grad_second = total_v[...]
        sums_v[1:2, :] = column_sum(grad_second * normed)
        sums_v[6:7, :] = column_sum(grad_second)
        grad_middle = grad[...].astype(F32) + norm_back(grad_second * gains[1:2, :], normed, inverse)
        middle_v[...] = grad_middle
        branch_v[...] = grad_middle.astype(LOW)
        sums_v[5:6, :] = column_sum(branch_v[...])
        save(0)
        save(0, wait=True)
        for at in range(max(0, ups - 2), ups):
            inner_save(at).wait()

    def outer():
        block = take(place_out)
        mixed_v[...] = dot_right(branch_v[...], block[...]).astype(LOW)
        release(place_out)
        own_load(3).wait()

    def heads(low, high):
        def step():
            attend_back(packed_v, mixed_v, grad_packed_v, width, low, high)

        return step

    def sums():
        save(1)
        sums_v[3:4, :] = column_sum(grad_packed_v[:, pl.ds(0, width)])
        sums_v[4:5, :] = column_sum(grad_packed_v[:, pl.ds(2 * width, width)])
        save(1, wait=True)

    def lower(number):
        def step():
            block = take(place_out + 1 + number)
            part = dot_right(grad_packed_v[:, pl.ds(number * width, width)], block[...])
            if number == 0:
                total_v[...] = part
            else:
                total_v[...] += part
            release(place_out + 1 + number)

        return step

    def finish():
        own_load(1).wait()
        normed, inverse = row_norm(entry[...].astype(F32))
        grad_lowered = total_v[...]
        sums_v[0:1, :] = column_sum(grad_lowered * normed)
        sums_v[2:3, :] = column_sum(grad_lowered)
        mixed_v[...] = (middle_v[...] + norm_back(grad_lowered * gains[0:1, :], normed, inverse)).astype(LOW)
        save(2)
        save(3)

    def lay_small():
        @pl.when(first)
        def _():
            save(2, wait=True)

        copy = pltpu.make_async_copy(sums_o, both_v, load_sems.at[0])
        copy.start()
        copy.wait()
        sums = both_v[0]
        for at in range(1, cell + 1):
            sums = sums + both_v[at]
        own = width // devices
        windows = [pltpu.roll(sums, (width - at * own) % width, 1)[:, :own] for at in range(devices)]
        share = devices // ups
        for device in range(devices):
            small_v[device, 0:8, :] = windows[device][0:8]
            for up in range(ups):
                row = 8 + device // share
                small_v[device, 8 + up : 9 + up, :] = windows[device % share * ups + up][row : row + 1]
            small_v[device, 8 + ups : 16, :] = jnp.zeros((8 - ups, own), F32)

    pairs = width // 128
    downs = [item for item in range(count) if items[item][0] == 4]
    up_items = [item for item in range(count) if items[item][0] == 3]
    outers = [item for item in range(count) if items[item][0] == 2]
    head_items = [item for item in range(count) if items[item][0] == 1]
    smalls = [item for item in range(count) if items[item][0] == 0]
    far = [half, half - 1, half + 1]
    near = [offset for offset in range(chips) if offset not in far]
    everywhere = far + near

    def only_first(step):
        return lambda: pl.when(first)(step)

    def product(target, left, right, shift, index):
        def step():
            products.run(target, left, right, shift, index)
            if index + 1 == 2 * (right.shape[1] // width):
                products.close(target, right)

        return step

    def all_of(wanted, offsets):
        return [(item, offset) for offset in offsets for item in wanted]

    def opening(left, right, shift):
        return lambda: products.open(left, right, shift)

    def blocks(target, left, right, shift, wanted):
        number = 2 * (right.shape[1] // width)
        made = [(0.3, opening(left, right, shift), [])]
        for index in range(number):
            opens = all_of(wanted, everywhere) if index + 1 == number else []
            made.append((1.8, product(target, left, right, shift, index), opens))
        return made

    steps = [(1.8, down_product(index), all_of(downs, far) if index == 2 else []) for index in range(3)]
    steps.append((0.3, only_first(begin), []))
    for index in range(3, chips):
        steps.append((1.8, down_product(index), all_of(downs, near) if index == chips - 1 else []))
    steps += [(1.7 if number in (0, ups) else 3.0, only_first(climb(number)), []) for number in range(ups + 1)]
    steps.append((2.5, only_first(turn), []))
    steps += blocks(up_part, second_h, inner_o, 1, up_items)
    steps += blocks(parts[2], mixed_h, branch_o, 1, outers)
    steps.append((1.7, only_first(outer), []))
    steps += [(1.25, only_first(heads(low, low + 1)), []) for low in range(pairs)]
    steps.append((0.8, only_first(sums), []))
    steps += blocks(parts[1], lowered_h, packed_o, 0, head_items)
    steps += [(1.5, only_first(lower(number)), []) for number in range(3)]
    steps.append((2.5, only_first(finish), []))
    steps.append((2.0, lay_small, all_of(smalls, everywhere)))
    greet((ring.left, ring.right, ring.sibling))
    schedule, _ = ring.arrange(steps, 8.0)
    ring.follow(schedule)
    ring.close()

    @pl.when(first)
    def _():
        save(3, wait=True)


def last_backward(arrived, entry, rows, saved, weights, kept, sides, items, shapes, count):
    chips = count // 2
    length, width = arrived.shape
    deep = weights[2].shape[1]
    cells = kept[0].shape[0]
    rows_in = cells * length
    own = width // count
    vmem, hbm = (pl.BlockSpec(memory_space=pltpu.VMEM), pl.BlockSpec(memory_space=pl.ANY))
    cut = width // 2
    wholes = [(16, own)] + [tuple(shape) for shape in shapes]
    held = [(many,) + wholes[array][1:] for array, _, many, _ in items]
    kinds = [F32 if array == 0 else LOW for array, _, _, _ in items]
    pieces = len(items)
    flops = 2 * length * width * (4 * width + 2 * deep) + 2 * rows_in * width * (4 * width + 2 * deep)
    outs = pl.pallas_call(
        functools.partial(last_backward_kernel, chips, items, cells - 1),
        out_shape=[jax.ShapeDtypeStruct(array.shape, array.dtype) for array in kept]
        + [jax.ShapeDtypeStruct((many, own), F32) for many in (2, 6, deep // width)]
        + [jax.ShapeDtypeStruct(shape, F32) for shape in wholes[1:]]
        + [jax.ShapeDtypeStruct((count,) + shape, LOW) for shape in wholes[1:]]
        + [jax.ShapeDtypeStruct((chips - 1,) + shape, kind) for shape, kind in zip(held, kinds)]
        + [jax.ShapeDtypeStruct((chips,) + shape, kind) for shape, kind in zip(held, kinds)],
        in_specs=[vmem, hbm, vmem] + [hbm] * 17,
        out_specs=[hbm] * 5 + [vmem] * 3 + [hbm] * (8 + 2 * pieces),
        input_output_aliases={15 + number: number for number in range(5)},
        scratch_shapes=[pltpu.VMEM((2,) + shape, kind) for shape, kind in zip(held, kinds)] * 3
        + [
            pltpu.VMEM((4, 80, width), F32),
            pltpu.VMEM((count, 16, own), F32),
            pltpu.VMEM((cells, 16, width), F32),
            pltpu.SemaphoreType.DMA((pieces, chips - 1)),
            pltpu.SemaphoreType.DMA((pieces, chips - 1)),
            pltpu.SemaphoreType.DMA((pieces, chips)),
            pltpu.SemaphoreType.DMA((pieces, chips)),
            pltpu.SemaphoreType.DMA((pieces, 6)),
            pltpu.SemaphoreType.DMA((4,)),
            pltpu.VMEM((2, rows_in, width), LOW),
            pltpu.VMEM((2, rows_in, cut), LOW),
            pltpu.VMEM((2, chips, own, width), LOW),
            pltpu.VMEM((2, 2, shapes[3][0], width), LOW),
            pltpu.SemaphoreType.DMA((2,)),
            pltpu.SemaphoreType.DMA((2,)),
            pltpu.SemaphoreType.DMA((4,)),
            pltpu.VMEM((2, width, width), LOW),
            pltpu.SemaphoreType.DMA((2,)),
            pltpu.SemaphoreType.DMA((cells + 4,)),
            pltpu.SemaphoreType.DMA((4,)),
            pltpu.SemaphoreType.DMA((2,)),
            pltpu.SemaphoreType.DMA((2,)),
            pltpu.VMEM((length, width), LOW),
            pltpu.VMEM((length, 3 * width), LOW),
            pltpu.VMEM((length, width), F32),
            pltpu.VMEM((2, length, width), LOW),
            pltpu.VMEM((2, length, width), LOW),
            pltpu.VMEM((length, 3 * width), LOW),
            pltpu.VMEM((length, width), LOW),
            pltpu.VMEM((length, width), LOW),
            pltpu.VMEM((2, length, width), F32),
            pltpu.VMEM((length, width), F32),
            pltpu.VMEM((16, width), F32),
        ],
        compiler_params=pltpu.CompilerParams(
            collective_id=2, has_side_effects=True, vmem_limit_bytes=62 * 2**20
        ),
        cost_estimate=pl.CostEstimate(flops=flops, bytes_accessed=160 * width * width, transcendentals=0),
    )(arrived, entry, rows, *saved, *weights, *sides, *kept)
    return (list(outs[:5]), outs[5:8], outs[8:12])


def on_device(inputs, out_grad, query_counts, gains, shifts, w_qkv, w_out, w_up, b_up, w_down):
    stage = lax.axis_index("pipe")
    stages = lax.axis_size("pipe")
    count = lax.axis_size("dp")
    cell_count, length, width = inputs.shape
    own = width // count
    ups = b_up.shape[1] // own
    deep = ups * width
    deep_own = w_down.shape[1]
    shapes = [
        block_shape(own, 3 * width),
        block_shape(own, width),
        block_shape(own, deep),
        block_shape(deep_own, width),
    ]
    cut = (shapes[3][0] // 2 + 15) // 16 * 16
    items = (
        (0, 0, 16, 0),
        (1, 0, shapes[0][0], 0),
        (2, 0, shapes[1][0], 0),
        (3, 0, shapes[2][0], 1),
        (4, 0, cut, 0),
        (4, cut, shapes[3][0] - cut, 1),
    )
    shards = [small_pack(gains[0], shifts[0], b_up[0], 1)[0]] + [
        array[0].reshape(shape) for array, shape in zip((w_qkv, w_out, w_up, w_down), shapes)
    ]
    fused = stages == 2 and cell_count == 2 and own % 16 == 0 and width % 256 == 0 and 4 * deep_own == width
    if fused:
        piece = own // 2 // 16 * 16
        arrivals = (
            (0, 0, 16, 0),
            (1, 0, own - piece, 0),
            (1, own - piece, piece, 1),
            (2, 0, own, 1),
            (3, 0, own - piece, 0),
            (3, own - piece, piece, 1),
            (4, 0, cut, 0),
            (4, cut, deep_own - cut, 1),
        )
        packs, rows, arrived, later, kept = gather_forward(
            shards, inputs, arrivals, ((0, 1, 2, 3), (4, 5), (6, 7)), count
        )
    else:
        packs = gather(shards, items, count)
        gain_rows, shift_rows, bias = small_split(packs[0].astype(F32), ups)
        blank = jnp.zeros((8 - ups, width), F32)
        rows = jnp.concatenate([gain_rows, shift_rows, bias.reshape(ups, width), blank])
    weights = (
        packs[1].reshape(width, 3 * width),
        packs[2].reshape(width, width),
        packs[3].reshape(width, deep),
        packs[4].reshape(deep, width),
    )
    scales = jnp.sqrt(query_counts.astype(F32) / 500.0)

    def along(value, steps):
        pairs = [(source, source + steps) for source in range(stages) if 0 <= source + steps < stages]
        return lax.ppermute(value, "pipe", pairs)

    entries = [[(inputs, cell) for cell in range(cell_count)]]
    if fused:
        entries.append([(arrived, None), (along(later, 1), None)])
    else:
        kept = None
    for turn in range(1 if fused else 0, stages):
        active = (stage == turn).astype(jnp.int32)[None]
        arrived = []
        for cell in range(cell_count):
            sent, kept = forward_tick(active, entries[turn][cell], rows, weights, kept, cell, cell_count)
            if turn + 1 < stages:
                arrived.append((along(sent, 1), None))
        entries.append(arrived)
    section_out, lowered, packed, mixed, middle, second, activated, slope = kept
    incoming = [((out_grad, cell), scales[cell][None]) for cell in range(cell_count)]
    back = None
    for turn in range(stages - 1, -1, -1):
        active = (stage == turn).astype(jnp.int32)[None]
        arrived = []
        for cell in range(cell_count):
            if fused and turn == 0 and cell == cell_count - 1:
                continue
            sent, back = backward_tick(
                active, incoming[cell], entries[turn][cell], rows, (packed, middle, slope), weights, back, cell, cell_count
            )
            if turn > 0:
                arrived.append(((along(sent, -1), None), jnp.ones((1,), F32)))
        incoming = arrived if turn > 0 else incoming

    def flat(array):
        return array.reshape(cell_count * length, -1)

    input_grads, grad_packed, grad_branch, grad_inner, grad_ff, sums = back
    if fused:
        (input_grads, _, _, _, _), (grad_gains, grad_shifts, grad_bias), shares = last_backward(
            incoming[-1][0][0],
            inputs,
            rows,
            (packed, middle, slope),
            weights,
            (input_grads, flat(grad_packed), flat(grad_branch), flat(grad_inner), sums),
            [flat(array) for array in (activated, grad_ff, second, mixed, lowered)],
            arrivals,
            shapes,
            count,
        )
    else:
        sums = jnp.sum(sums, axis=0)
        small_part = small_pack(sums[0:2], sums[2:8], sums[8 : 8 + ups].reshape(deep), count)
        sides = [flat(array) for array in (lowered, grad_packed, mixed, grad_branch, second, grad_inner, activated, grad_ff)]
        products = [dot_left(sides[at], sides[at + 1]).astype(LOW) for at in (0, 2, 4, 6)]
        parts = [small_part] + [whole.reshape((count,) + shape) for whole, shape in zip(products, shapes)]
        small_share, *shares = scatter(parts, items, count)
        grad_gains, grad_shifts, grad_bias = small_split(small_share[None], ups)
    return (
        section_out[None],
        input_grads[None],
        grad_gains[None],
        grad_shifts[None],
        shares[0].reshape(1, own, 3 * width),
        shares[1].reshape(1, own, width),
        shares[2].reshape(1, own, deep),
        grad_bias.reshape(1, ups * own),
        shares[3].reshape(1, deep_own, width),
    )


def solution(mesh):
    in_specs = (
        P("dp", None, None),
        P("dp", None, None),
        P("dp"),
        P("pipe", None, "dp"),
        P("pipe", None, "dp"),
        P("pipe", "dp", None),
        P("pipe", "dp", None),
        P("pipe", "dp", None),
        P("pipe", "dp"),
        P("pipe", "dp", None),
    )
    out_specs = (
        P("pipe", "dp", None, None),
        P("pipe", "dp", None, None),
        P("pipe", None, "dp"),
        P("pipe", None, "dp"),
        P("pipe", "dp", None),
        P("pipe", "dp", None),
        P("pipe", "dp", None),
        P("pipe", "dp"),
        P("pipe", "dp", None),
    )
    return jax.shard_map(
        on_device, mesh=mesh, in_specs=in_specs, out_specs=out_specs, check_vma=False
    )
```

```python
import functools
import math

import jax
import jax.numpy as jnp
from jax import lax
from jax.experimental import pallas as pl
from jax.experimental.pallas import tpu as pltpu
from jax.sharding import PartitionSpec as P

HEAD_DIM = 64
MESH = pl.DeviceIdType.MESH
LOW = jnp.bfloat16
F32 = jnp.float32


def ring_chip(position, chips):
    position = lax.rem(position + 2 * chips, chips)
    half = chips // 2
    return jnp.where(position < half, 2 * position, 2 * (chips - 1 - position) + 1)


def ring_place(chips):
    me = lax.axis_index("dp")
    core = lax.rem(me, 2)
    chip = me // 2
    position = jnp.where(lax.rem(chip, 2) == 0, chip // 2, chips - 1 - chip // 2)
    right = ring_chip(position + 1, chips) * 2 + core
    left = ring_chip(position - 1, chips) * 2 + core
    return (me, core, position, right, left, me + 1 - 2 * core)


def greet(devices):
    barrier = pltpu.get_barrier_semaphore()
    for device in devices:
        pl.semaphore_signal(barrier, inc=1, device_id={"dp": device}, device_id_type=MESH)
    pl.semaphore_wait(barrier, len(devices))


def gather_kernel(chips, arrays, items, *refs):
    count = len(items)
    ring_send, ring_recv, pair_send, pair_recv, own_sem = refs[2 * arrays :]
    shards = [refs[array].at[pl.ds(start, rows)] for array, start, rows, _ in items]
    splits = [way for _, _, _, way in items]
    half = chips // 2
    me, core, position, right, left, sibling = ring_place(chips)
    greet((left, right, sibling))

    def out(item, block):
        array, start, rows, _ = items[item]
        return refs[arrays + array].at[block, pl.ds(start, rows)]

    def owner(step, way):
        return ring_chip(position - step if way == 0 else position + step, chips) * 2 + core

    def travels(item, way, step):
        return step < half or (step == half and splits[item] == way)

    def ring_copy(item, way, step):
        block = owner(step - 1, way)
        return pltpu.make_async_remote_copy(
            src_ref=shards[item] if step == 1 else out(item, block),
            dst_ref=out(item, block),
            send_sem=ring_send.at[item, way, step - 1],
            recv_sem=ring_recv.at[item, way, step - 1],
            device_id={"dp": right if way == 0 else left},
            device_id_type=MESH,
        )

    def pair_copy(item, offset, block, source):
        return pltpu.make_async_remote_copy(
            src_ref=source,
            dst_ref=out(item, block),
            send_sem=pair_send.at[item, offset],
            recv_sem=pair_recv.at[item, offset],
            device_id={"dp": sibling},
            device_id_type=MESH,
        )

    sent, paired, kept = ([], [], [])
    for item in range(count):
        for way in (0, 1):
            if travels(item, way, 1):
                sent.append(ring_copy(item, way, 1))
                sent[-1].start()
    for item in range(count):
        paired.append(pair_copy(item, 0, me, shards[item]))
        paired[-1].start()
        kept.append(pltpu.make_async_copy(shards[item], out(item, me), own_sem.at[item]))
        kept[-1].start()
    for step in range(1, half + 1):
        for item in range(count):
            for way in (0, 1):
                if not travels(item, way, step):
                    continue
                ring_copy(item, way, step).wait_recv()
                if travels(item, way, step + 1):
                    sent.append(ring_copy(item, way, step + 1))
                    sent[-1].start()
                block = owner(step, way)
                offset = step if way == 0 else chips - step
                paired.append(pair_copy(item, offset, block, out(item, block)))
                paired[-1].start()
    for copy in sent:
        copy.wait_send()
    for copy in paired:
        copy.wait()
    for copy in kept:
        copy.wait()


def gather(shards, items, count):
    chips = count // 2
    arrays, pieces = (len(shards), len(items))
    return pl.pallas_call(
        functools.partial(gather_kernel, chips, arrays, items),
        out_shape=[jax.ShapeDtypeStruct((count,) + shard.shape, shard.dtype) for shard in shards],
        in_specs=[pl.BlockSpec(memory_space=pl.ANY)] * arrays,
        out_specs=[pl.BlockSpec(memory_space=pl.ANY)] * arrays,
        scratch_shapes=[
            pltpu.SemaphoreType.DMA((pieces, 2, chips // 2)),
            pltpu.SemaphoreType.DMA((pieces, 2, chips // 2)),
            pltpu.SemaphoreType.DMA((pieces, chips)),
            pltpu.SemaphoreType.DMA((pieces, chips)),
            pltpu.SemaphoreType.DMA((pieces,)),
        ],
        compiler_params=pltpu.CompilerParams(collective_id=0, has_side_effects=True),
    )(*shards)


def scatter_kernel(chips, arrays, items, *refs):
    count = len(items)
    parts, outs, refs = (refs[:arrays], refs[arrays : 2 * arrays], refs[2 * arrays :])
    landed, paired, mine = (refs[:count], refs[count : 2 * count], refs[2 * count : 3 * count])
    ring_send, ring_recv, pair_send, pair_recv, mine_sem = refs[3 * count :]
    splits = [way for _, _, _, way in items]
    half = chips // 2
    me, core, position, right, left, sibling = ring_place(chips)
    greet((left, right, sibling))

    def part(item, block):
        array, start, rows, _ = items[item]
        return parts[array].at[block, pl.ds(start, rows)]

    def first(item, way):
        return 1 if splits[item] == way else 2

    def slot(item, way, step):
        return step - 1 if splits[item] == way else half + step - 2

    def offset_of(step, way):
        return half - step + 1 if way == 0 else chips - (half - step + 1)

    def pair_copy(item, offset):
        block = ring_chip(position + offset, chips) * 2 + 1 - core
        return pltpu.make_async_remote_copy(
            src_ref=part(item, block),
            dst_ref=paired[item].at[offset],
            send_sem=pair_send.at[item, offset],
            recv_sem=pair_recv.at[item, offset],
            device_id={"dp": sibling},
            device_id_type=MESH,
        )

    def ring_copy(item, way, step):
        if step == first(item, way):
            source = paired[item].at[offset_of(step, way)]
        else:
            source = landed[item].at[slot(item, way, step - 1)]
        here = slot(item, way, step)
        return pltpu.make_async_remote_copy(
            src_ref=source,
            dst_ref=landed[item].at[here],
            send_sem=ring_send.at[item, here],
            recv_sem=ring_recv.at[item, here],
            device_id={"dp": right if way == 0 else left},
            device_id_type=MESH,
        )

    def load(item, offset, buffer):
        block = ring_chip(position + offset, chips) * 2 + core
        return pltpu.make_async_copy(part(item, block), mine[item].at[buffer], mine_sem.at[item, buffer])

    plan, uses = ([], [0] * count)
    for step in range(1, half + 2):
        for item in range(count):
            for way in (0, 1):
                if step <= half and step >= first(item, way):
                    plan.append((step, item, way, offset_of(step, way), uses[item] % 2))
                    uses[item] += 1
            if step > half:
                plan.append((step, item, None, 0, uses[item] % 2))
                uses[item] += 1
    for step, item, way, offset, buffer in plan:
        pair_copy(item, offset).start()
    load(plan[0][1], plan[0][3], plan[0][4]).start()
    sent = []
    for number, (step, item, way, offset, buffer) in enumerate(plan):
        if number + 1 < len(plan):
            load(plan[number + 1][1], plan[number + 1][3], plan[number + 1][4]).start()
        load(item, offset, buffer).wait()
        pair_copy(item, offset).wait_recv()
        array, start, rows, _ = items[item]
        kind = parts[array].dtype
        chunk = 16 if rows % 16 == 0 else rows
        from_pair, from_mine, from_ring = (paired[item], mine[item], landed[item])
        if way is None:
            ring_copy(item, 0, half).wait_recv()
            ring_copy(item, 1, half).wait_recv()
            slot_a, slot_b = (slot(item, 0, half), slot(item, 1, half))

            @pl.loop(0, rows // chunk)
            def _(index):
                here = pl.ds(pl.multiple_of(index * chunk, chunk), chunk)
                outs[array][pl.ds(pl.multiple_of(start + index * chunk, chunk), chunk), :] = (
                    from_ring[slot_a, here, :].astype(F32) + from_ring[slot_b, here, :].astype(F32)
                ) + (from_mine[buffer, here, :].astype(F32) + from_pair[offset, here, :].astype(F32))

            continue
        if step == first(item, way):

            @pl.loop(0, rows // chunk)
            def _(index):
                here = pl.ds(pl.multiple_of(index * chunk, chunk), chunk)
                from_pair[offset, here, :] = (
                    from_mine[buffer, here, :].astype(F32) + from_pair[offset, here, :].astype(F32)
                ).astype(kind)

        else:
            ring_copy(item, way, step - 1).wait_recv()
            arrived = slot(item, way, step - 1)

            @pl.loop(0, rows // chunk)
            def _(index):
                here = pl.ds(pl.multiple_of(index * chunk, chunk), chunk)
                from_ring[arrived, here, :] = (
                    from_ring[arrived, here, :].astype(F32)
                    + (from_mine[buffer, here, :].astype(F32) + from_pair[offset, here, :].astype(F32))
                ).astype(kind)

        sent.append(ring_copy(item, way, step))
        sent[-1].start()
    for copy in sent:
        copy.wait_send()
    for step, item, way, offset, buffer in plan:
        pair_copy(item, offset).wait_send()


def scatter(parts, items, count):
    chips = count // 2
    arrays, pieces = (len(parts), len(items))
    shapes = [(rows,) + parts[array].shape[2:] for array, _, rows, _ in items]
    kinds = [parts[array].dtype for array, _, _, _ in items]
    return pl.pallas_call(
        functools.partial(scatter_kernel, chips, arrays, items),
        out_shape=[jax.ShapeDtypeStruct(part.shape[1:], F32) for part in parts],
        in_specs=[pl.BlockSpec(memory_space=pl.ANY)] * arrays,
        out_specs=[pl.BlockSpec(memory_space=pltpu.VMEM)] * arrays,
        scratch_shapes=[pltpu.VMEM((chips - 1,) + shape, kind) for shape, kind in zip(shapes, kinds)]
        + [pltpu.VMEM((chips,) + shape, kind) for shape, kind in zip(shapes, kinds)]
        + [pltpu.VMEM((2,) + shape, kind) for shape, kind in zip(shapes, kinds)]
        + [
            pltpu.SemaphoreType.DMA((pieces, chips - 1)),
            pltpu.SemaphoreType.DMA((pieces, chips - 1)),
            pltpu.SemaphoreType.DMA((pieces, chips)),
            pltpu.SemaphoreType.DMA((pieces, chips)),
            pltpu.SemaphoreType.DMA((pieces, 2)),
        ],
        compiler_params=pltpu.CompilerParams(
            collective_id=1, has_side_effects=True, vmem_limit_bytes=62 * 2**20
        ),
    )(*parts)


def block_shape(rows, columns):
    return (rows, columns) if rows % 16 == 0 else (rows * columns // 128, 128)


def small_pack(gains, shifts, bias, count):
    width = gains.shape[1] // count
    ups = bias.shape[0] // gains.shape[1]
    rows = [
        gains.reshape(2, count, width).swapaxes(0, 1),
        shifts.reshape(6, count, width).swapaxes(0, 1),
        bias.reshape(count, ups, width),
    ]
    blank = jnp.zeros((count, 8 - ups, width), gains.dtype)
    return jnp.concatenate(rows + [blank], axis=1)


def small_split(blocks, ups):
    count, _, width = blocks.shape
    gains = blocks[:, 0:2].swapaxes(0, 1).reshape(2, count * width)
    shifts = blocks[:, 2:8].swapaxes(0, 1).reshape(6, count * width)
    bias = blocks[:, 8 : 8 + ups].reshape(count * ups * width)
    return (gains, shifts, bias)


def row_norm(rows_in):
    center = rows_in - jnp.mean(rows_in, axis=-1, keepdims=True)
    inverse = lax.rsqrt(jnp.mean(center * center, axis=-1, keepdims=True) + 1e-05)
    return (center * inverse, inverse)


def norm_back(grad_rows, normed, inverse):
    return inverse * (
        grad_rows
        - jnp.mean(grad_rows, axis=-1, keepdims=True)
        - normed * jnp.mean(grad_rows * normed, axis=-1, keepdims=True)
    )


def gelu_parts(hidden):
    cumulative = 0.5 * (1.0 + lax.erf(hidden * (1.0 / math.sqrt(2.0))))
    slope = cumulative + hidden * jnp.exp(-0.5 * hidden * hidden) * (1.0 / math.sqrt(2.0 * math.pi))
    return (hidden * cumulative, slope)


def dot(left, right):
    return lax.dot_general(left, right, (((1,), (0,)), ((), ())), preferred_element_type=F32)


def dot_right(left, right):
    return lax.dot_general(left, right, (((1,), (1,)), ((), ())), preferred_element_type=F32)


def dot_left(left, right):
    return lax.dot_general(left, right, (((0,), (0,)), ((), ())), preferred_element_type=F32)


class Stream:
    def __init__(self, blocks, buffers, sems):
        self.blocks, self.buffers, self.sems = (blocks, buffers, sems)
        self.depth = buffers.shape[0]
        self.started = 0
        for _ in range(min(self.depth, len(blocks))):
            self.start()

    def copy(self, number):
        slot = number % self.depth
        return pltpu.make_async_copy(self.blocks[number], self.buffers.at[slot], self.sems.at[slot])

    def start(self):
        self.copy(self.started).start()
        self.started += 1

    def take(self, number):
        self.copy(number).wait()
        return self.buffers.at[number % self.depth]

    def release(self):
        if self.started < len(self.blocks):
            self.start()


def weight_blocks(w_qkv, w_out, w_up, w_down):
    width = w_out.shape[0]
    def cut(ref, axis, number):
        window = pl.ds(number * width, width)
        return ref.at[:, window] if axis else ref.at[window, :]
    heads = [cut(w_qkv, 1, number) for number in range(3)]
    ups = [cut(w_up, 1, number) for number in range(w_up.shape[1] // width)]
    downs = [cut(w_down, 0, number) for number in range(w_down.shape[0] // width)]
    return (heads, w_out, ups, downs)


def head_masks(length):
    return lax.broadcasted_iota(jnp.int32, (length, 128), 1) < HEAD_DIM


def two_heads(array, side):
    blank = jnp.zeros_like(array)
    return jnp.concatenate([jnp.where(side, array, blank), jnp.where(side, blank, array)], axis=0)


def attend(packed, mixed, width, low=0, high=None):
    length = packed.shape[0]
    side = head_masks(length)

    def pair_of(pair):
        start = pair * 128 if isinstance(pair, int) else pl.multiple_of(pair * 128, 128)
        queries = packed[:, pl.ds(start, 128)] * jnp.asarray(1.0 / math.sqrt(HEAD_DIM), LOW)
        keys = two_heads(packed[:, pl.ds(start + width, 128)], side)
        values = two_heads(packed[:, pl.ds(start + 2 * width, 128)], side)
        scores = dot_right(queries, keys)
        probs, totals = ([], [])
        for head in (0, 1):
            mine = scores[:, head * length : (head + 1) * length]
            shifted = jnp.exp(mine - jnp.max(mine, axis=-1, keepdims=True))
            totals.append(1.0 / jnp.sum(shifted, axis=-1, keepdims=True))
            probs.append(shifted.astype(LOW))
        result = dot(jnp.concatenate(probs, axis=1), values)
        mixed[:, pl.ds(start, 128)] = (result * jnp.where(side, totals[0], totals[1])).astype(LOW)

    if high is not None:
        for pair in range(low, high):
            pair_of(pair)
        return

    @pl.loop(0, width // 256)
    def _(index):
        pair_of(index * 2)
        pair_of(index * 2 + 1)


def attend_back(packed, grad_mixed, grad_packed, width, low=0, high=None):
    length = packed.shape[0]
    side = head_masks(length)
    scale = 1.0 / math.sqrt(HEAD_DIM)

    def pair_of(pair):
        start = pair * 128 if isinstance(pair, int) else pl.multiple_of(pair * 128, 128)
        queries = packed[:, pl.ds(start, 128)]
        keys = packed[:, pl.ds(start + width, 128)] * jnp.asarray(scale, LOW)
        grads = grad_mixed[:, pl.ds(start, 128)]
        keys_two = two_heads(keys, side)
        queries_two = two_heads(queries, side)
        grads_two = two_heads(grads, side)
        scores = dot_right(keys, queries_two)
        grad_probs = dot_right(packed[:, pl.ds(start + 2 * width, 128)], grads_two)
        probs, grad_scores = ([], [])
        for head in (0, 1):
            mine = slice(head * length, (head + 1) * length)
            shifted = jnp.exp(scores[:, mine] - jnp.max(scores[:, mine], axis=0, keepdims=True))
            prob = shifted * (1.0 / jnp.sum(shifted, axis=0, keepdims=True))
            product = grad_probs[:, mine] * prob
            weighted = jnp.sum(product, axis=0, keepdims=True)
            probs.append(prob.astype(LOW))
            grad_scores.append((product - prob * weighted).astype(LOW))
        beside = jnp.concatenate(grad_scores, axis=1)
        grad_packed[:, pl.ds(start, 128)] = dot_left(jnp.concatenate(grad_scores, axis=0), keys_two).astype(LOW)
        grad_packed[:, pl.ds(start + width, 128)] = (dot(beside, queries_two) * scale).astype(LOW)
        grad_packed[:, pl.ds(start + 2 * width, 128)] = dot(jnp.concatenate(probs, axis=1), grads_two).astype(LOW)

    if high is not None:
        for pair in range(low, high):
            pair_of(pair)
        return

    @pl.loop(0, width // 256)
    def _(index):
        pair_of(index * 2)
        pair_of(index * 2 + 1)


def forward_kernel(cell, held, at, active, entry_h, rows, w_qkv, w_out, w_up, w_down, *refs):
    sent_h = refs[held]
    out_h, lowered_h, packed_h, mixed_h, middle_h, second_h, active_h, slope_h = [
        ref.at[cell] for ref in refs[held + 1 : held + 9]
    ]
    (buffers, buffer_sems, save_sems, out_v, lowered_v, packed_v, mixed_v, middle_v) = refs[held + 9 : held + 17]
    (second_v, active_v, slope_v, hidden_v, total_v, entry, entry_sem) = refs[held + 17 :]
    entry = entry_h if at is None else entry
    width = entry.shape[1]
    gains, shifts, bias = (rows.at[0:2], rows.at[2:8], rows.at[8:16])
    ups = w_up.shape[1] // width

    @pl.when(active[0] != 0)
    def _():
        heads, outer, up, down = weight_blocks(w_qkv, w_out, w_up, w_down)
        order = heads + [outer]
        place_up, place_down = ({}, {})
        for number in range(ups + 1):
            if number < ups:
                place_up[number] = len(order)
                order.append(up[number])
            if number > 0:
                place_down[number - 1] = len(order)
                order.append(down[number - 1])
        if at is not None:
            fetched = pltpu.make_async_copy(entry_h.at[at], entry, entry_sem)
            fetched.start()
        saves = []

        def save(source, target):
            saves.append(pltpu.make_async_copy(source, target, save_sems.at[len(saves)]))
            saves[-1].start()

        if at is not None:
            fetched.wait()
        stream = Stream(order, buffers, buffer_sems)
        rows_in = entry[...].astype(F32)
        normed, _ = row_norm(rows_in)
        lowered_v[...] = (normed * gains[0:1, :] + shifts[0:1, :]).astype(LOW)
        save(lowered_v, lowered_h)
        for number in range(3):
            block = stream.take(number)
            window = pl.ds(number * width, width)
            part = dot(lowered_v[...], block[...])
            if number != 1:
                part = part + shifts[1 + number // 2 : 2 + number // 2, :]
            packed_v[:, window] = part.astype(LOW)
            stream.release()
        save(packed_v, packed_h)
        attend(packed_v, mixed_v, width)
        save(mixed_v, mixed_h)
        block = stream.take(3)
        middle = entry[...].astype(F32) + dot(mixed_v[...], block[...]) + shifts[3:4, :]
        middle_v[...] = middle
        stream.release()
        save(middle_v, middle_h)
        normed, _ = row_norm(middle_v[...])
        second_v[...] = (normed * gains[1:2, :] + shifts[4:5, :]).astype(LOW)
        save(second_v, second_h)
        for number in range(ups + 1):
            if number < ups:
                up_block = stream.take(place_up[number])
            if number > 0:
                down_block = stream.take(place_down[number - 1])
            if number < ups:
                hidden_v[number % 2] = dot(second_v[...], up_block[...]) + bias[number : number + 1, :]
            if number > 0:
                window = pl.ds((number - 1) * width, width)
                activated, slope = gelu_parts(hidden_v[(number - 1) % 2])
                active_v[:, window] = activated.astype(LOW)
                slope_v[:, window] = slope.astype(LOW)
                part = dot(active_v[:, window], down_block[...])
                if number == 1:
                    total_v[...] = part
                elif number < ups:
                    total_v[...] += part
                else:
                    out_v[...] = (middle_v[...] + (total_v[...] + part + shifts[5:6, :])).astype(LOW)
                save(active_v.at[:, window], active_h.at[:, window])
                save(slope_v.at[:, window], slope_h.at[:, window])
            if number < ups:
                stream.release()
            if number > 0:
                stream.release()
        save(out_v, sent_h)
        save(out_v, out_h)
        for copy in saves:
            copy.wait()


def kept_shapes(length, width, deep):
    return [
        ((length, width), LOW),
        ((length, width), LOW),
        ((length, 3 * width), LOW),
        ((length, width), LOW),
        ((length, width), F32),
        ((length, width), LOW),
        ((length, deep), LOW),
        ((length, deep), LOW),
    ]


def forward_tick(active, entry, rows, weights, kept, cell, cell_count):
    entry, at = entry
    length, width = entry.shape[-2:]
    deep = weights[2].shape[1]
    ups = deep // width
    shapes = kept_shapes(length, width, deep)
    outs = [jax.ShapeDtypeStruct(*shapes[0])] + [
        jax.ShapeDtypeStruct((cell_count,) + shape, kind) for shape, kind in shapes
    ]
    vmem, hbm = (pl.BlockSpec(memory_space=pltpu.VMEM), pl.BlockSpec(memory_space=pl.ANY))
    flops = 2 * length * width * (4 * width + 2 * deep) + 16 * length * length * width
    kept = () if kept is None else tuple(kept)
    held = len(kept)
    sent, *kept = pl.pallas_call(
        functools.partial(forward_kernel, cell, held, at),
        out_shape=outs,
        in_specs=[pl.BlockSpec(memory_space=pltpu.SMEM), vmem if at is None else hbm, vmem] + [hbm] * (4 + held),
        out_specs=[hbm] * 9,
        input_output_aliases={7 + number: 1 + number for number in range(held)},
        scratch_shapes=[
            pltpu.VMEM((4, width, width), LOW),
            pltpu.SemaphoreType.DMA((4,)),
            pltpu.SemaphoreType.DMA((7 + 2 * ups,)),
        ]
        + [pltpu.VMEM(*shape) for shape in shapes]
        + [
            pltpu.VMEM((2, length, width), F32),
            pltpu.VMEM((length, width), F32),
            pltpu.VMEM((length, width), LOW),
            pltpu.SemaphoreType.DMA,
        ],
        compiler_params=pltpu.CompilerParams(vmem_limit_bytes=60 * 2**20),
        cost_estimate=pl.CostEstimate(
            flops=flops, bytes_accessed=2 * width * (4 * width + 2 * deep), transcendentals=0
        ),
    )(active, entry, rows, *weights, *kept)
    return (sent, kept)


def backward_kernel(cell, held, grad_at, entry_at, active, scale, grad_h, entry_h, rows, *refs):
    packed, middle, slope = [ref.at[cell] for ref in refs[:3]]
    w_qkv, w_out, w_up, w_down = refs[3:7]
    refs = refs[7 + held :]
    sent_h = refs[0]
    rows_h, packed_h, branch_h, inner_h, low_h, sums_h = [ref.at[cell] for ref in refs[1:7]]
    (buffers, buffer_sems, load_sems, save_sems, rows_v, grad_packed_v, branch_v, inner_v, low_v, sums_v) = refs[7:17]
    (packed_v, middle_v, slope_v, mixed_v, grad_act_v, total_v, grad_middle_v, grad, entry) = refs[17:]
    gains = rows.at[0:2]
    grad = grad_h if grad_at is None else grad
    entry_h = entry_h if entry_at is None else entry_h.at[entry_at]
    length, width = entry.shape
    ups = w_up.shape[1] // width

    @pl.when(active[0] != 0)
    def _():
        heads, outer, up, down = weight_blocks(w_qkv, w_out, w_up, w_down)
        loads = [
            pltpu.make_async_copy(slope, slope_v, load_sems.at[0]),
            pltpu.make_async_copy(middle, middle_v, load_sems.at[1]),
            pltpu.make_async_copy(packed, packed_v, load_sems.at[2]),
            pltpu.make_async_copy(entry_h, entry, load_sems.at[3]),
        ]
        if grad_at is not None:
            loads.append(pltpu.make_async_copy(grad_h.at[grad_at], grad, load_sems.at[4]))
            loads[4].start()
        order, place_up, place_down = ([], {}, {})
        for number in range(ups + 1):
            if number < ups:
                place_down[number] = len(order)
                order.append(down[number])
            if number > 0:
                place_up[number - 1] = len(order)
                order.append(up[number - 1])
        place_out = len(order)
        order = order + [outer] + heads
        saves = []

        def save(source, target):
            saves.append(pltpu.make_async_copy(source, target, save_sems.at[len(saves)]))
            saves[-1].start()

        def column_sum(array):
            return jnp.sum(array.astype(F32), axis=0, keepdims=True)

        if grad_at is not None:
            loads[4].wait()
        stream = Stream(order, buffers, buffer_sems)
        loads[0].start()
        low_v[...] = (grad[...].astype(F32) * scale[0]).astype(LOW)
        save(low_v, low_h)
        sums_v[7:8, :] = column_sum(low_v[...])
        for number in range(ups + 1):
            if number == 1:
                loads[0].wait()
                loads[1].start()
            if number == 2:
                loads[2].start()
                loads[3].start()
            if number < ups:
                down_block = stream.take(place_down[number])
            if number > 0:
                up_block = stream.take(place_up[number - 1])
            if number < ups:
                grad_act_v[number % 2] = dot_right(low_v[...], down_block[...])
            if number > 0:
                window = pl.ds((number - 1) * width, width)
                inner = (grad_act_v[(number - 1) % 2] * slope_v[:, window].astype(F32)).astype(LOW)
                inner_v[:, window] = inner
                sums_v[7 + number : 8 + number, :] = column_sum(inner)
                part = dot_right(inner, up_block[...])
                if number == 1:
                    total_v[...] = part
                else:
                    total_v[...] += part
                save(inner_v.at[:, window], inner_h.at[:, window])
            if number < ups:
                stream.release()
            if number > 0:
                stream.release()
        loads[1].wait()
        normed, inverse = row_norm(middle_v[...])
        grad_second = total_v[...]
        sums_v[1:2, :] = column_sum(grad_second * normed)
        sums_v[6:7, :] = column_sum(grad_second)
        grad_middle = grad[...].astype(F32) * scale[0] + norm_back(grad_second * gains[1:2, :], normed, inverse)
        grad_middle_v[...] = grad_middle
        branch_v[...] = grad_middle.astype(LOW)
        sums_v[5:6, :] = column_sum(branch_v[...])
        save(branch_v, branch_h)
        block = stream.take(place_out)
        mixed_v[...] = dot_right(branch_v[...], block[...]).astype(LOW)
        stream.release()
        loads[2].wait()
        attend_back(packed_v, mixed_v, grad_packed_v, width)
        save(grad_packed_v, packed_h)
        sums_v[3:4, :] = column_sum(grad_packed_v[:, pl.ds(0, width)])
        sums_v[4:5, :] = column_sum(grad_packed_v[:, pl.ds(2 * width, width)])
        for number in range(3):
            block = stream.take(place_out + 1 + number)
            part = dot_right(grad_packed_v[:, pl.ds(number * width, width)], block[...])
            if number == 0:
                total_v[...] = part
            else:
                total_v[...] += part
            stream.release()
        loads[3].wait()
        normed, inverse = row_norm(entry[...].astype(F32))
        grad_lowered = total_v[...]
        sums_v[0:1, :] = column_sum(grad_lowered * normed)
        sums_v[2:3, :] = column_sum(grad_lowered)
        rows_v[...] = (grad_middle_v[...] + norm_back(grad_lowered * gains[0:1, :], normed, inverse)).astype(LOW)
        save(sums_v, sums_h)
        save(rows_v, sent_h)
        save(rows_v, rows_h)
        for copy in saves:
            copy.wait()


def backward_tick(active, incoming, entry, rows, saved, weights, kept, cell, cell_count):
    entry, entry_at = entry
    (grad, grad_at), scale = incoming
    length, width = entry.shape[-2:]
    deep = weights[2].shape[1]
    ups = deep // width
    shapes = [
        ((length, width), LOW),
        ((length, 3 * width), LOW),
        ((length, width), LOW),
        ((length, deep), LOW),
        ((length, width), LOW),
        ((16, width), F32),
    ]
    outs = [jax.ShapeDtypeStruct(*shapes[0])] + [
        jax.ShapeDtypeStruct((cell_count,) + shape, kind) for shape, kind in shapes
    ]
    vmem, hbm = (pl.BlockSpec(memory_space=pltpu.VMEM), pl.BlockSpec(memory_space=pl.ANY))
    smem = pl.BlockSpec(memory_space=pltpu.SMEM)
    flops = 2 * length * width * (4 * width + 2 * deep) + 40 * length * length * width
    kept = () if kept is None else tuple(kept)
    held = len(kept)
    sent, *kept = pl.pallas_call(
        functools.partial(backward_kernel, cell, held, grad_at, entry_at),
        out_shape=outs,
        in_specs=[smem] * 2 + [vmem if grad_at is None else hbm, hbm, vmem] + [hbm] * (7 + held),
        out_specs=[hbm] * 7,
        input_output_aliases={12 + number: 1 + number for number in range(held)},
        scratch_shapes=[
            pltpu.VMEM((4, width, width), LOW),
            pltpu.SemaphoreType.DMA((4,)),
            pltpu.SemaphoreType.DMA((5,)),
            pltpu.SemaphoreType.DMA((6 + ups,)),
        ]
        + [pltpu.VMEM(*shape) for shape in shapes]
        + [
            pltpu.VMEM((length, 3 * width), LOW),
            pltpu.VMEM((length, width), F32),
            pltpu.VMEM((length, deep), LOW),
            pltpu.VMEM((length, width), LOW),
            pltpu.VMEM((2, length, width), F32),
            pltpu.VMEM((length, width), F32),
            pltpu.VMEM((length, width), F32),
            pltpu.VMEM((length, width), LOW),
            pltpu.VMEM((length, width), LOW),
        ],
        compiler_params=pltpu.CompilerParams(vmem_limit_bytes=60 * 2**20),
        cost_estimate=pl.CostEstimate(
            flops=flops, bytes_accessed=2 * width * (4 * width + 2 * deep), transcendentals=0
        ),
    )(active, scale, grad, entry, rows, *saved, *weights, *kept)
    return (sent, kept)


def small_rows(small, rows, width, ups):
    devices, _, own = small.shape
    lane = lax.broadcasted_iota(jnp.int32, (own, width), 1)
    depth = lax.broadcasted_iota(jnp.int32, (own, width), 0)
    row = lax.broadcasted_iota(jnp.int32, (16, width), 0)
    across = lax.broadcasted_iota(jnp.int32, (16, width), 1)
    top = jnp.zeros((16, width), F32)
    for device in range(devices):
        spot = jnp.where(lane == depth + device * own, 1.0, 0.0).astype(LOW)
        top = top + dot(small[device], spot)
    rows[0:8, :] = top[0:8]
    share = devices // ups
    for block in range(ups):
        total = jnp.zeros((1, width), F32)
        for index in range(share):
            start = index * ups * own
            spot = jnp.zeros((own, width), F32)
            for up in range(ups):
                spot = spot + jnp.where(lane == depth + (start + up * own), 1.0, 0.0)
            low = start + (row - 8) * own
            inside = (row >= 8) & (row < 8 + ups) & (across >= low) & (across < low + own)
            placed = dot(small[block * share + index], spot.astype(LOW))
            total = total + jnp.sum(jnp.where(inside, placed, 0.0), axis=0, keepdims=True)
        rows[8 + block : 9 + block, :] = total


def gather_forward_kernel(chips, items, groups, cells, *refs):
    shards, inputs_h = (refs[:5], refs[5])
    outs, rows_h, arrived_h = (refs[6:11], refs[11], refs[12])
    out_h, lowered_h, packed_h, mixed_h, middle_h, second_h, active_h, slope_h = refs[13:21]
    (ring_send, ring_recv, pair_send, pair_recv, own_sem, hop_send, hop_recv) = refs[21:28]
    (load_sem, save_sem, wide_sem, deep_sem) = refs[28:32]
    (small_v, rows_v, entry_v, out_v, lowered_v, packed_v, mixed_v, middle_v, second_v, active_v, slope_v) = refs[32:43]
    (total_v, hidden_v, wide_v, deep_v) = refs[43:]
    length, width = entry_v.shape[1:]
    ups = active_v.shape[2] // width
    half = chips // 2
    me, core, position, right, left, sibling = ring_place(chips)
    stage = lax.axis_index("pipe")
    first = stage == 0
    barrier = pltpu.get_barrier_semaphore()
    for device in (left, right, sibling):
        pl.semaphore_signal(barrier, inc=1, device_id={"dp": device}, device_id_type=MESH)
    pl.semaphore_signal(barrier, inc=1, device_id={"pipe": 1 - stage}, device_id_type=MESH)
    pl.semaphore_wait(barrier, 4)

    def shard(item):
        array, start, rows, _ = items[item]
        return shards[array].at[pl.ds(start, rows)]

    def out(item, block):
        array, start, rows, _ = items[item]
        return outs[array].at[block, pl.ds(start, rows)]

    def owner(step, way):
        return ring_chip(position - step if way == 0 else position + step, chips) * 2 + core

    def travels(item, way, step):
        return step < half or (step == half and items[item][3] == way)

    def ring_copy(item, way, step):
        block = owner(step - 1, way)
        return pltpu.make_async_remote_copy(
            src_ref=shard(item) if step == 1 else out(item, block),
            dst_ref=out(item, block),
            send_sem=ring_send.at[item, way, step - 1],
            recv_sem=ring_recv.at[item, way, step - 1],
            device_id={"dp": right if way == 0 else left},
            device_id_type=MESH,
        )

    def pair_copy(item, offset, block, source):
        return pltpu.make_async_remote_copy(
            src_ref=source,
            dst_ref=out(item, block),
            send_sem=pair_send.at[item, offset],
            recv_sem=pair_recv.at[item, offset],
            device_id={"dp": sibling},
            device_id_type=MESH,
        )

    def own_copy(item):
        return pltpu.make_async_copy(shard(item), out(item, me), own_sem.at[item])

    sent, paired = ([], [])

    def open_group(group):
        for item in group:
            for way in (0, 1):
                if travels(item, way, 1):
                    sent.append(ring_copy(item, way, 1))
                    sent[-1].start()
        for item in group:
            paired.append(pair_copy(item, 0, me, shard(item)))
            paired[-1].start()
            own_copy(item).start()

    def ring_step(item, way, step):
        ring_copy(item, way, step).wait_recv()
        if travels(item, way, step + 1):
            sent.append(ring_copy(item, way, step + 1))
            sent[-1].start()
        block = owner(step, way)
        offset = step if way == 0 else chips - step
        paired.append(pair_copy(item, offset, block, out(item, block)))
        paired[-1].start()

    def pair_arrived(item, offset):
        block = ring_chip(position - offset, chips) * 2 + core
        pair_copy(item, offset, block, out(item, block)).wait_recv()

    saves = [[], []]
    runner = [0]

    def save(source, target):
        number = len(saves[0]) + len(saves[1])
        saves[runner[0]].append(lambda: pltpu.make_async_copy(source(), target(), save_sem.at[number]))
        saves[runner[0]][-1]().start()

    def entry_load(cell):
        return pltpu.make_async_copy(inputs_h.at[cell], entry_v.at[cell], load_sem.at[cell])

    def wide_load(array, column, slot):
        source = outs[array].at[:, :, pl.ds(column * width, width)]
        return pltpu.make_async_copy(source, wide_v.at[slot], wide_sem.at[slot])

    def wide(slot):
        return wide_v[slot].reshape(width, width)

    def gains(number):
        return rows_v[number : number + 1, :]

    def shifts(number):
        return rows_v[2 + number : 3 + number, :]

    def begin(cell):
        def step():
            if runner[0] == 0:
                entry_load(cell).wait()
            normed, _ = row_norm(entry_v[cell].astype(F32))
            lowered_v[cell] = (normed * gains(0) + shifts(0)).astype(LOW)
            save(lambda: lowered_v.at[cell], lambda: lowered_h.at[cell])

        return step

    def project(cell, number):
        def step():
            if cell == 0:
                wide_load(1, number, number).wait()
            part = dot(lowered_v[cell], wide(number))
            if number != 1:
                part = part + shifts(1 + number // 2)
            packed_v[cell, :, pl.ds(number * width, width)] = part.astype(LOW)
            if number == 2:
                save(lambda: packed_v.at[cell], lambda: packed_h.at[cell])

        return step

    def mix(cell, low, high, last):
        def step():
            attend(packed_v.at[cell], mixed_v.at[cell], width, low, high)
            if last:
                save(lambda: mixed_v.at[cell], lambda: mixed_h.at[cell])

        return step

    def join(cell):
        def step():
            if cell == 0:
                wide_load(2, 0, 3).wait()
            middle_v[cell] = entry_v[cell].astype(F32) + dot(mixed_v[cell], wide(3)) + shifts(3)
            save(lambda: middle_v.at[cell], lambda: middle_h.at[cell])

        return step

    def renorm(cell):
        def step():
            middle = middle_v[cell]
            normed, _ = row_norm(middle)
            second_v[cell] = (normed * gains(1) + shifts(4)).astype(LOW)
            total_v[cell] = middle + shifts(5)
            save(lambda: second_v.at[cell], lambda: second_h.at[cell])

        return step

    def rise(cell, number):
        def step():
            if cell == 0:
                wide_load(3, number, number).wait()
            hidden_v[...] = dot(second_v[cell], wide(number)) + rows_v[8 + number : 9 + number, :]

        return step

    def bend(cell, number):
        def step():
            window = pl.ds(number * width, width)
            activated, slope = gelu_parts(hidden_v[...])
            active_v[cell, :, window] = activated.astype(LOW)
            slope_v[cell, :, window] = slope.astype(LOW)
            if number == ups - 1:
                save(lambda: active_v.at[cell], lambda: active_h.at[cell])
                save(lambda: slope_v.at[cell], lambda: slope_h.at[cell])

        return step

    deep_rows = deep_v.shape[1] * deep_v.shape[2]

    def deep_load(offset, slot):
        chip = ring_chip(position - offset, chips)
        return pltpu.make_async_copy(outs[4].at[pl.ds(chip * 2, 2)], deep_v.at[slot], deep_sem.at[slot])

    def fall(cell, offset, slot):
        def step():
            if cell == 0:
                deep_load(offset, slot).wait()
            chip = ring_chip(position - offset, chips)
            window = pl.ds(pl.multiple_of(chip * deep_rows, 128), deep_rows)
            total_v[cell] += dot(active_v[cell, :, window], deep_v[slot].reshape(deep_rows, width))

        return step

    def hop(cell):
        return pltpu.make_async_remote_copy(
            src_ref=out_v.at[cell],
            dst_ref=entry_v.at[cell],
            send_sem=hop_send.at[cell],
            recv_sem=hop_recv.at[cell],
            device_id={"pipe": 1 - stage},
            device_id_type=MESH,
        )

    def finish(cell):
        def step():
            out_v[cell] = total_v[cell].astype(LOW)
            if runner[0] == 0 and cell == 0:
                hop(0).start()
            save(lambda: out_v.at[cell], lambda: out_h.at[cell])

        return step

    def on_first(step):
        pl.when(first)(step)

    queue = []

    def ready(group, steps, loads):
        for item in group:
            own_copy(item).wait()
            for offset in range(chips):
                pair_arrived(item, offset)

        for load in loads:
            load().start()

        queue.extend(steps)

    pairs = width // 128
    heads = []
    for cell in range(cells):
        heads.append(begin(cell))
        heads += [project(cell, number) for number in range(3)]
        heads += [mix(cell, low, low + 2, low + 2 >= pairs) for low in range(0, pairs, 2)]
    joins = [make(cell) for cell in range(cells) for make in (join, renorm)]
    def load_ups():
        for number in range(ups):
            wide_load(3, number, number).start()

    climbs = [load_ups]
    climbs += [make(cell, number) for number in range(ups) for cell in range(cells) for make in (rise, bend)]

    @pl.when(first)
    def _():
        for cell in range(cells):
            entry_load(cell).start()

    def lay_rows():
        copy = pltpu.make_async_copy(outs[0], small_v, load_sem.at[cells])
        copy.start()
        copy.wait()
        small_rows(small_v, rows_v, width, ups)
        pltpu.make_async_copy(rows_v, rows_h, load_sem.at[cells + 1]).start()

    def ready_small():
        for item in groups[0]:
            if items[item][0] == 0:
                own_copy(item).wait()
                for offset in range(chips):
                    pair_arrived(item, offset)
        lay_rows()

    plan = []
    for number, group in enumerate(groups):
        for step in range(1, half + 1):
            if step == half and number + 1 < len(groups):
                plan.append(("open", number + 1))
            for item in group:
                for way in (0, 1):
                    if travels(item, way, step):
                        plan.append(("ring", item, way, step))
            if number == len(groups) - 1:
                plan.append(("deep", step))
        plan.append(("done", number))
    open_group(groups[0])
    late = []
    slots = [0]

    def deep_ready(offsets):
        for offset in offsets:
            for item in groups[-1]:
                if offset == 0:
                    own_copy(item).wait()
                pair_arrived(item, offset)
            slot = slots[0] % deep_v.shape[0]
            slots[0] += 1

            def opening(offset=offset, slot=slot):
                deep_load(offset, slot).start()

            queue.append(opening)
            queue.extend(fall(cell, offset, slot) for cell in range(cells))

    def serve(limit):
        for _ in range(limit):
            if queue:
                on_first(queue.pop(0))

    for entry in plan:
        if entry[0] == "open":
            open_group(groups[entry[1]])
        elif entry[0] == "ring":
            ring_step(*entry[1:])
            for wait in list(late):
                wait[0] -= 1
                if wait[0] == 0:
                    wait[1]()
                    late.remove(wait)
            serve(3 if entry[1] in groups[-1] else 2)
        elif entry[0] == "done":
            if entry[1] == 0:
                rest = [item for item in groups[0] if items[item][0] != 0]
                late.append([1, ready_small])
                late.append(
                    [
                        2,
                        lambda: ready(
                            rest,
                            heads + joins,
                            [functools.partial(wide_load, 1, number, number) for number in range(3)]
                            + [functools.partial(wide_load, 2, 0, 3)],
                        ),
                    ]
                )
            elif entry[1] == 1:
                late.append([2, lambda: ready(groups[1], climbs, [])])
        elif entry[0] == "deep":
            step = entry[1]
            if step == 1:
                late.append([3, lambda: deep_ready([0])])
            if step < half:
                late.append([2, lambda step=step: deep_ready([step, chips - step])])
            else:
                for wait in late:
                    wait[1]()
                serve(len(queue))
                deep_ready([half])
    serve(len(queue))
    for cell in range(cells):
        on_first(finish(cell))
    for copy in sent:
        copy.wait_send()
    for copy in paired:
        copy.wait_send()
    pltpu.make_async_copy(rows_v, rows_h, load_sem.at[cells + 1]).wait()

    @pl.when(first)
    def _():
        for cell in range(cells):
            if cell > 0:
                hop(cell).start()
            hop(cell).wait_send()
        for copy in saves[0]:
            copy().wait()

    @pl.when(jnp.logical_not(first))
    def _():
        runner[0] = 1

        def arrive(cell):
            hop(cell).wait_recv()
            save(lambda: entry_v.at[cell], lambda: arrived_h.at[cell])

        arrive(0)
        begin(0)()
        for number in range(3):
            project(0, number)()
            if number < ups:
                wide_load(3, number, number).start()
        attend(packed_v.at[0], mixed_v.at[0], width)
        mix(0, 0, 0, True)()
        join(0)()
        for number in range(3, ups):
            wide_load(3, number, number).start()
        for offset in (0, 1):
            deep_load(offset, offset).start()
        renorm(0)()
        for number in range(ups):
            rise(0, number)()
            bend(0, number)()
        for offset in range(chips):
            fall(0, offset, offset % 2)()
            if offset + 2 < chips:
                deep_load(offset + 2, offset % 2).start()
        finish(0)()
        for cell in range(1, cells):
            arrive(cell)
        for copy in saves[1]:
            copy().wait()


def gather_forward(shards, inputs, items, groups, count):
    chips = count // 2
    cells, length, width = inputs.shape
    deep = shards[3].shape[1]
    ups = deep // width
    pieces = len(items)
    shapes = kept_shapes(length, width, deep)
    hbm = pl.BlockSpec(memory_space=pl.ANY)
    flops = 2 * cells * length * width * (4 * width + 2 * deep)
    outs = pl.pallas_call(
        functools.partial(gather_forward_kernel, chips, items, groups, cells),
        out_shape=[jax.ShapeDtypeStruct((count,) + shard.shape, shard.dtype) for shard in shards]
        + [
            jax.ShapeDtypeStruct((16, width), F32),
            jax.ShapeDtypeStruct((cells, length, width), LOW),
        ]
        + [jax.ShapeDtypeStruct((cells,) + shape, kind) for shape, kind in shapes],
        in_specs=[hbm] * 6,
        out_specs=[hbm] * 15,
        scratch_shapes=[
            pltpu.SemaphoreType.DMA((pieces, 2, chips // 2)),
            pltpu.SemaphoreType.DMA((pieces, 2, chips // 2)),
            pltpu.SemaphoreType.DMA((pieces, chips)),
            pltpu.SemaphoreType.DMA((pieces, chips)),
            pltpu.SemaphoreType.DMA((pieces,)),
            pltpu.SemaphoreType.DMA((cells,)),
            pltpu.SemaphoreType.DMA((cells,)),
            pltpu.SemaphoreType.DMA((cells + 2,)),
            pltpu.SemaphoreType.DMA((9 * cells + 9 + cells,)),
            pltpu.SemaphoreType.DMA((4,)),
            pltpu.SemaphoreType.DMA((2,)),
            pltpu.VMEM((count,) + shards[0].shape, LOW),
            pltpu.VMEM((16, width), F32),
            pltpu.VMEM((cells, length, width), LOW),
        ]
        + [pltpu.VMEM((cells,) + shape, kind) for shape, kind in shapes]
        + [
            pltpu.VMEM((cells, length, width), F32),
            pltpu.VMEM((length, width), F32),
            pltpu.VMEM((4, count, width // count, width), LOW),
            pltpu.VMEM((2, 2, shards[4].shape[0], width), LOW),
        ],
        compiler_params=pltpu.CompilerParams(
            collective_id=3, has_side_effects=True, vmem_limit_bytes=62 * 2**20
        ),
        cost_estimate=pl.CostEstimate(flops=flops, bytes_accessed=8 * width * (4 * width + 2 * deep), transcendentals=0),
    )(*shards, inputs)
    return (outs[:5], outs[5], outs[6], list(outs[7:]))


class RingSum:
    def __init__(self, chips, items, parts, outs, landed, paired, buffers, final, sems):
        self.chips, self.items, self.parts, self.outs = (chips, items, parts, outs)
        self.landed, self.paired, self.final = (landed, paired, final)
        self.mine, self.pairs, self.rings = buffers
        self.ring_send, self.ring_recv, self.pair_send, self.pair_recv, self.load_sem, self.final_sem = sems
        self.half = chips // 2
        self.me, self.core, self.position, self.right, self.left, self.sibling = ring_place(chips)
        self.sent, self.final_copies, self.exchanged = ({}, [], [])
        self.uses = [0] * len(items)

    def part(self, item, block):
        array, start, rows, _ = self.items[item]
        return self.parts[array].at[block, pl.ds(start, rows)]

    def first(self, item, way):
        return 1 if self.items[item][3] == way else 2

    def slot_of(self, item, way, step):
        return step - 1 if self.items[item][3] == way else self.half + step - 2

    def offset_of(self, step, way):
        return self.half - step + 1 if way == 0 else self.chips - (self.half - step + 1)

    def pair_copy(self, item, offset):
        block = ring_chip(self.position + offset, self.chips) * 2 + 1 - self.core
        return pltpu.make_async_remote_copy(
            src_ref=self.part(item, block),
            dst_ref=self.paired[item].at[offset],
            send_sem=self.pair_send.at[item, offset],
            recv_sem=self.pair_recv.at[item, offset],
            device_id={"dp": self.sibling},
            device_id_type=MESH,
        )

    def ring_copy(self, item, way, step, buffer=0):
        here = self.slot_of(item, way, step)
        return pltpu.make_async_remote_copy(
            src_ref=self.mine[item].at[buffer],
            dst_ref=self.landed[item].at[here],
            send_sem=self.ring_send.at[item, here],
            recv_sem=self.ring_recv.at[item, here],
            device_id={"dp": self.right if way == 0 else self.left},
            device_id_type=MESH,
        )

    def load_mine(self, item, offset, buffer):
        block = ring_chip(self.position + offset, self.chips) * 2 + self.core
        return pltpu.make_async_copy(self.part(item, block), self.mine[item].at[buffer], self.load_sem.at[item, buffer])

    def load_pair(self, item, offset, buffer):
        return pltpu.make_async_copy(
            self.paired[item].at[offset], self.pairs[item].at[buffer], self.load_sem.at[item, 2 + buffer]
        )

    def load_ring(self, item, way, step, buffer):
        return pltpu.make_async_copy(
            self.landed[item].at[self.slot_of(item, way, step)], self.rings[item].at[buffer], self.load_sem.at[item, 4 + buffer]
        )

    def starts(self, wanted):
        return [
            (step, item, way, self.offset_of(step, way))
            for step in (1, 2)
            for item in wanted
            for way in (0, 1)
            if step == self.first(item, way)
        ]

    def rest(self, wanted, steps):
        return [
            (step, item, way, self.offset_of(step, way))
            for step in steps
            if step <= self.half
            for item in wanted
            for way in (0, 1)
            if step > self.first(item, way)
        ] + [(step, item, None, 0) for step in steps if step > self.half for item in wanted]

    def fetch(self, entry):
        step, item, way, offset, buffer = entry
        if (item, buffer) in self.sent:
            self.sent.pop((item, buffer)).wait_send()
        self.load_mine(item, offset, buffer).start()
        self.pair_copy(item, offset).wait_recv()
        self.load_pair(item, offset, buffer).start()

    def bytes_of(self, item):
        array, _, rows, _ = self.items[item]
        return rows * self.parts[array].shape[2] * self.parts[array].dtype.itemsize

    def arrange(self, steps, ends):
        waiting = self.starts(range(len(self.items)))
        waiting += self.rest(range(len(self.items)), range(2, self.half + 2))
        opened, arrival, sends, used = ({}, {}, {}, [0] * len(self.items))
        clock, link, order, steps = (0.0, [0.0, 0.0], [], list(steps))

        def ready_at(entry):
            step, item, way, offset = entry
            if (item, offset) not in opened:
                return None
            when = opened[(item, offset)]
            sides = (0, 1) if way is None else ((way,) if step > self.first(item, way) else ())
            for side in sides:
                if (item, side, step - 1) not in arrival:
                    return None
                when = max(when, arrival[(item, side, step - 1)])
            return max(when, sends.get((item, used[item] - 2), 0.0))

        while waiting or steps:
            best = None
            for entry in waiting:
                when = ready_at(entry)
                if when is None or (entry[2] is None and (steps or any(other[2] is not None for other in waiting if ready_at(other) is not None and ready_at(other) <= clock))):
                    continue
                backlog = 0.0 if entry[2] is None else max(0.0, link[entry[2]] - max(clock, when))
                rank = (max(when, clock) + 0.5 * backlog, entry[0])
                if best is None or rank < best[0]:
                    best = (rank, entry, when)
            far_off = best is None or best[2] > clock + 0.3
            idle = best is not None and best[1][2] is not None and link[best[1][2]] > clock + ends
            if steps and (far_off or idle):
                spent, step, opens = steps.pop(0)
                clock += spent
                for item, offset in opens:
                    opened[(item, offset)] = clock + 2.0 + self.bytes_of(item) / 2e5
                order.append((step, opens))
                continue
            _, entry, when = best
            waiting.remove(entry)
            step, item, way, offset = entry
            clock = max(clock, when) + 0.8 + self.bytes_of(item) * 1.6e-6
            if way is not None:
                link[way] = max(clock, link[way]) + 2 * self.bytes_of(item) / 9.1e4
                arrival[(item, way, step)] = link[way] + 1.5
                sends[(item, used[item])] = link[way]
            order.append(entry + (used[item] % 2,))
            used[item] += 1
        return order, clock

    def follow(self, order):
        entries = [number for number, action in enumerate(order) if len(action) == 5]
        fetched = set()
        for number, action in enumerate(order):
            if len(action) == 2:
                step, opens = action
                step()
                for item, offset in opens:
                    self.pair_copy(item, offset).start()
                    self.exchanged.append((item, offset))
                continue
            if number not in fetched:
                self.fetch(action)
                fetched.add(number)
            if number + 1 in entries:
                following = order[number + 1]
                if following[1] != action[1]:
                    self.fetch(following)
                    fetched.add(number + 1)
            self.work(action)

    def work(self, entry):
        step, item, way, offset, buffer = entry
        array, start, rows, _ = self.items[item]
        half, final = (self.half, self.final)
        kind = self.parts[array].dtype
        columns = self.parts[array].shape[2]
        chunk = 16
        mine, pairs, rings = (self.mine[item], self.pairs[item], self.rings[item])
        if way is None:
            for side in (0, 1):
                self.ring_copy(item, side, half).wait_recv()
                self.load_ring(item, side, half, side).start()
            self.load_mine(item, offset, buffer).wait()
            self.load_pair(item, offset, buffer).wait()
            for side in (0, 1):
                self.load_ring(item, side, half, side).wait()
            if kind == F32:
                total = (rings[0] + rings[1]) + (mine[buffer] + pairs[buffer])
                top = 0
                for out in self.outs[array]:
                    out[...] = total[top : top + out.shape[0]]
                    top += out.shape[0]
                return
            high, wide = (min(rows, final.shape[1]), min(columns, final.shape[2]))
            for top in range(0, rows, high):
                for across in range(0, columns, wide):
                    number = len(self.final_copies)
                    turn = number % final.shape[0]
                    if number >= final.shape[0]:
                        self.final_copies[number - final.shape[0]].wait()
                    span = pl.ds(across, wide)

                    @pl.loop(0, high // chunk)
                    def _(index):
                        here = pl.ds(pl.multiple_of(top + index * chunk, chunk), chunk)
                        final[turn, pl.ds(pl.multiple_of(index * chunk, chunk), chunk), pl.ds(0, wide)] = (
                            rings[0, here, span].astype(F32) + rings[1, here, span].astype(F32)
                        ) + (mine[buffer, here, span].astype(F32) + pairs[buffer, here, span].astype(F32))

                    self.final_copies.append(
                        pltpu.make_async_copy(
                            final.at[turn, pl.ds(0, high), pl.ds(0, wide)],
                            self.outs[array].at[pl.ds(start + top, high), span],
                            self.final_sem.at[turn],
                        )
                    )
                    self.final_copies[-1].start()
            return
        carried = step > self.first(item, way)
        if carried:
            self.ring_copy(item, way, step - 1).wait_recv()
            self.load_ring(item, way, step - 1, buffer).start()
        self.load_mine(item, offset, buffer).wait()
        self.load_pair(item, offset, buffer).wait()
        if carried:
            self.load_ring(item, way, step - 1, buffer).wait()

        @pl.loop(0, rows // chunk)
        def _(index):
            here = pl.ds(pl.multiple_of(index * chunk, chunk), chunk)
            total = mine[buffer, here, :].astype(F32) + pairs[buffer, here, :].astype(F32)
            if carried:
                total = rings[buffer, here, :].astype(F32) + total
            mine[buffer, here, :] = total.astype(kind)

        copy = self.ring_copy(item, way, step, buffer)
        copy.start()
        self.sent[(item, buffer)] = copy

    def close(self):
        for copy in self.sent.values():
            copy.wait_send()
        for item, offset in self.exchanged:
            self.pair_copy(item, offset).wait_send()
        for copy in self.final_copies[-self.final.shape[0] :]:
            copy.wait()


class Products:
    def __init__(self, chips, width, own, cuts, big, stage, cut_sem, big_sem, stage_sem):
        self.chips, self.width, self.own = (chips, width, own)
        self.cuts, self.big, self.stage = (cuts, big, stage)
        self.cut_sem, self.big_sem, self.stage_sem = (cut_sem, big_sem, stage_sem)

    def load_cut(self, source, index, slot):
        cut = self.cuts.shape[2]
        window = pl.ds(pl.multiple_of(index * cut, cut), cut)
        return pltpu.make_async_copy(source.at[:, window], self.cuts.at[slot], self.cut_sem.at[slot])

    def block(self, source, index, slot):
        window = pl.ds(pl.multiple_of(index * self.width, self.width), self.width)
        return pltpu.make_async_copy(source.at[:, window], self.big.at[slot], self.big_sem.at[slot])

    def keep(self, target, index):
        window = pl.ds(index // 2 * self.width, self.width)
        return pltpu.make_async_copy(
            self.stage.at[index % 2],
            target.at[pl.ds(index % 2 * self.chips, self.chips), :, window],
            self.stage_sem.at[index % 2],
        )

    def open(self, left, right, slot):
        for index in (0, 1):
            self.load_cut(left, index, index).start()
        self.block(right, 0, slot).start()

    def run(self, target, left, right, shift, index):
        number = 2 * (right.shape[1] // self.width)
        slot, here = (index % 2, (index // 2 + shift) % 2)
        if index == 0:
            for side in (0, 1):
                self.load_cut(left, side, side).wait()
        if slot == 0:
            self.block(right, index // 2, here).wait()
            if index + 2 < number:
                self.block(right, index // 2 + 1, 1 - here).start()
        if index >= 2:
            self.keep(target, index - 2).wait()
        product = dot_left(self.cuts[slot], self.big[here]).astype(LOW)
        for device in range(self.chips):
            self.stage[slot, device] = product[device * self.own : (device + 1) * self.own]
        self.keep(target, index).start()

    def close(self, target, right):
        number = 2 * (right.shape[1] // self.width)
        for index in (number - 2, number - 1):
            self.keep(target, index).wait()


def last_backward_kernel(chips, items, cell, *refs):
    count = len(items)
    (grad, entry_h, rows, packed_h, middle_h, slope_h, w_qkv, w_out, w_up, w_down) = refs[:10]
    (activated_h, grad_ff_h, second_h, mixed_h, lowered_h) = refs[10:15]
    refs = refs[15 + 5 :]
    rows_o, packed_o, branch_o, inner_o, sums_o = refs[:5]
    outs, parts = ([refs[5:8]] + list(refs[8:12]), refs[12:16])
    landed, paired = (refs[16 : 16 + count], refs[16 + count : 16 + 2 * count])
    refs = refs[16 + 2 * count :]
    ring_buffers = (refs[:count], refs[count : 2 * count], refs[2 * count : 3 * count])
    final, small_v, both_v = refs[3 * count : 3 * count + 3]
    sems = refs[3 * count + 3 : 3 * count + 9]
    refs = refs[3 * count + 9 :]
    (big, cuts, stage, stage_down, big_sem, cut_sem, stage_sem) = refs[:7]
    (buffers, buffer_sems, load_sems, save_sems, slope_sems, inner_sems) = refs[7:13]
    (entry, packed_v, middle_v, slope_v, inner_v, grad_packed_v, mixed_v, branch_v, grad_act_v, total_v, sums_v) = refs[13:]
    parts = [small_v] + list(parts)
    down_part, up_part = (parts[4], parts[3])
    length, width = grad.shape
    devices = 2 * chips
    deep_own = down_part.shape[1]
    ups = w_up.shape[1] // width
    first = lax.axis_index("pipe") == 0
    ring = RingSum(chips, items, parts, outs, landed, paired, ring_buffers, final, sems)
    half, position = (ring.half, ring.position)
    products = Products(chips, width, width // devices, cuts, big, stage, cut_sem, big_sem, stage_sem)
    gains = rows.at[0:2]

    def farthest_first(index):
        step = index // 2
        return ring_chip(position + (half - step if index % 2 == 0 else half + step + 1), chips)

    def keep_down(index):
        return pltpu.make_async_copy(
            stage_down.at[index % 2],
            down_part.at[pl.ds(farthest_first(index) * 2, 2)],
            stage_sem.at[2 + index % 2],
        )

    def cut_down(index):
        return products.load_cut(activated_h, farthest_first(index), index % 2)

    def down_product(index):
        def step():
            slot = index % 2
            if index == 0:
                for at in range(cell + 1):
                    ff_load(at).wait()
            if index + 1 < chips:
                cut_down(index + 1).start()
            cut_down(index).wait()
            product = dot_left(cuts[slot], big[0]).astype(LOW)
            for side in (0, 1):
                stage_down[slot, side] = product[side * deep_own : (side + 1) * deep_own]
            keep_down(index).start()
            if index > 0:
                keep_down(index - 1).wait()

        return step

    def last_down():
        keep_down(chips - 1).wait()

    def far_offset(index):
        return (half - index // 2 if index % 2 == 0 else half + index // 2 + 1) % chips

    def here(ref, at):
        return ref.at[pl.ds(at * length, length)]

    def ff_load(at):
        return pltpu.make_async_copy(here(grad_ff_h, at), here(big.at[0], at), load_sems.at[at])

    def ff_arrived():
        return pltpu.make_async_copy(grad, here(big.at[0], cell), load_sems.at[cell])

    for at in range(cell):
        ff_load(at).start()
    pl.when(first)(lambda: ff_arrived().start())
    pl.when(jnp.logical_not(first))(lambda: ff_load(cell).start())
    cut_down(0).start()

    def own_load(number):
        source, target = ((entry_h, entry), (middle_h, middle_v), (packed_h, packed_v))[number - 1]
        return pltpu.make_async_copy(source.at[cell], target, load_sems.at[cell + 1 + number])

    def slope_load(number):
        window = pl.ds(number * width, width)
        return pltpu.make_async_copy(
            slope_h.at[cell].at[:, window], slope_v.at[number % 2], slope_sems.at[number % 2]
        )

    order, place_up, place_down = ([], {}, {})
    for number in range(ups + 1):
        if number < ups:
            place_down[number] = len(order)
            order.append((w_down, 0, number))
        if number > 0:
            place_up[number - 1] = len(order)
            order.append((w_up, 1, number - 1))
    place_out = len(order)
    order = order + [(w_out, 0, 0)] + [(w_qkv, 1, number) for number in range(3)]
    depth = buffers.shape[0]

    def weight_load(number):
        ref, axis, at = order[number]
        window = pl.ds(at * width, width)
        source = ref.at[:, window] if axis else ref.at[window, :]
        return pltpu.make_async_copy(source, buffers.at[number % depth], buffer_sems.at[number % depth])

    def take(number):
        weight_load(number).wait()
        return buffers.at[number % depth]

    def release(number):
        if number + depth < len(order):
            weight_load(number + depth).start()

    def save(number, wait=False):
        source, target = (
            (branch_v, branch_o.at[pl.ds(cell * length, length)]),
            (grad_packed_v, packed_o.at[pl.ds(cell * length, length)]),
            (sums_v, sums_o.at[cell]),
            (mixed_v, rows_o.at[cell]),
        )[number]
        copy = pltpu.make_async_copy(source, target, save_sems.at[number])
        copy.wait() if wait else copy.start()

    def inner_save(number):
        window = pl.ds(number * width, width)
        return pltpu.make_async_copy(
            inner_v.at[number % 2], inner_o.at[pl.ds(cell * length, length), window], inner_sems.at[number % 2]
        )

    def column_sum(array):
        return jnp.sum(array.astype(F32), axis=0, keepdims=True)

    def begin():
        slope_load(0).start()
        for number in range(depth):
            weight_load(number).start()
        for number in (1, 2, 3):
            own_load(number).start()
        sums_v[7:8, :] = column_sum(grad[...])

    def climb(number):
        def step():
            if number < ups:
                down_block = take(place_down[number])
                grad_act_v[number % 2] = dot_right(grad[...], down_block[...])
                release(place_down[number])
            if number > 0:
                at = number - 1
                slope_load(at).wait()
                if at + 1 < ups:
                    slope_load(at + 1).start()
                up_block = take(place_up[at])
                if at >= 2:
                    inner_save(at - 2).wait()
                inner = (grad_act_v[at % 2] * slope_v[at % 2].astype(F32)).astype(LOW)
                inner_v[at % 2] = inner
                sums_v[8 + at : 9 + at, :] = column_sum(inner)
                part = dot_right(inner, up_block[...])
                if at == 0:
                    total_v[...] = part
                else:
                    total_v[...] += part
                inner_save(at).start()
                release(place_up[at])

        return step

    def turn():
        own_load(2).wait()
        normed, inverse = row_norm(middle_v[...])
        grad_second = total_v[...]
        sums_v[1:2, :] = column_sum(grad_second * normed)
        sums_v[6:7, :] = column_sum(grad_second)
        grad_middle = grad[...].astype(F32) + norm_back(grad_second * gains[1:2, :], normed, inverse)
        middle_v[...] = grad_middle
        branch_v[...] = grad_middle.astype(LOW)
        sums_v[5:6, :] = column_sum(branch_v[...])
        save(0)
        save(0, wait=True)
        for at in range(max(0, ups - 2), ups):
            inner_save(at).wait()

    def outer():
        block = take(place_out)
        mixed_v[...] = dot_right(branch_v[...], block[...]).astype(LOW)
        release(place_out)
        own_load(3).wait()

    def heads(low, high):
        def step():
            attend_back(packed_v, mixed_v, grad_packed_v, width, low, high)

        return step

    def sums():
        save(1)
        sums_v[3:4, :] = column_sum(grad_packed_v[:, pl.ds(0, width)])
        sums_v[4:5, :] = column_sum(grad_packed_v[:, pl.ds(2 * width, width)])
        save(1, wait=True)

    def lower(number):
        def step():
            block = take(place_out + 1 + number)
            part = dot_right(grad_packed_v[:, pl.ds(number * width, width)], block[...])
            if number == 0:
                total_v[...] = part
            else:
                total_v[...] += part
            release(place_out + 1 + number)

        return step

    def finish():
        own_load(1).wait()
        normed, inverse = row_norm(entry[...].astype(F32))
        grad_lowered = total_v[...]
        sums_v[0:1, :] = column_sum(grad_lowered * normed)
        sums_v[2:3, :] = column_sum(grad_lowered)
        mixed_v[...] = (middle_v[...] + norm_back(grad_lowered * gains[0:1, :], normed, inverse)).astype(LOW)
        save(2)
        save(3)

    def lay_small():
        @pl.when(first)
        def _():
            save(2, wait=True)

        copy = pltpu.make_async_copy(sums_o, both_v, load_sems.at[0])
        copy.start()
        copy.wait()
        sums = both_v[0]
        for at in range(1, cell + 1):
            sums = sums + both_v[at]
        own = width // devices
        windows = [pltpu.roll(sums, (width - at * own) % width, 1)[:, :own] for at in range(devices)]
        share = devices // ups
        for device in range(devices):
            small_v[device, 0:8, :] = windows[device][0:8]
            for up in range(ups):
                row = 8 + device // share
                small_v[device, 8 + up : 9 + up, :] = windows[device % share * ups + up][row : row + 1]
            small_v[device, 8 + ups : 16, :] = jnp.zeros((8 - ups, own), F32)

    pairs = width // 128
    downs = [item for item in range(count) if items[item][0] == 4]
    up_items = [item for item in range(count) if items[item][0] == 3]
    outers = [item for item in range(count) if items[item][0] == 2]
    head_items = [item for item in range(count) if items[item][0] == 1]
    smalls = [item for item in range(count) if items[item][0] == 0]
    everywhere = [far_offset(index) for index in range(chips)]

    def only_first(step):
        return lambda: pl.when(first)(step)

    def product(target, left, right, shift, index):
        def step():
            products.run(target, left, right, shift, index)
            if index + 1 == 2 * (right.shape[1] // width):
                products.close(target, right)

        return step

    def all_of(wanted, offsets):
        return [(item, offset) for offset in offsets for item in wanted]

    def opening(left, right, shift):
        return lambda: products.open(left, right, shift)

    def blocks(target, left, right, shift, wanted):
        number = 2 * (right.shape[1] // width)
        made = [(0.3, opening(left, right, shift), [])]
        for index in range(number):
            opens = all_of(wanted, everywhere) if index + 1 == number else []
            made.append((1.9, product(target, left, right, shift, index), opens))
        return made

    steps = []
    for index in range(chips):
        steps.append((1.9, down_product(index), all_of(downs, [far_offset(index - 1)] if index else [])))
        if index == 3:
            steps.append((0.3, only_first(begin), []))
    steps.append((0.7, last_down, all_of(downs, [far_offset(chips - 1)])))
    steps += [(2.0 if number in (0, ups) else 3.5, only_first(climb(number)), []) for number in range(ups + 1)]
    steps.append((3.0, only_first(turn), []))
    steps += blocks(up_part, second_h, inner_o, 1, up_items)
    steps += blocks(parts[2], mixed_h, branch_o, 1, outers)
    steps.append((1.7, only_first(outer), []))
    steps += [(2.5, only_first(heads(low, low + 2)), []) for low in range(0, pairs, 2)]
    steps.append((0.8, only_first(sums), []))
    steps += blocks(parts[1], lowered_h, packed_o, 0, head_items)
    steps += [(1.8, only_first(lower(number)), []) for number in range(3)]
    steps.append((3.0, only_first(finish), []))
    steps.append((2.0, lay_small, all_of(smalls, everywhere)))
    greet((ring.left, ring.right, ring.sibling))
    schedule, _ = ring.arrange(steps, 8.0)
    ring.follow(schedule)
    ring.close()

    @pl.when(first)
    def _():
        save(3, wait=True)


def last_backward(arrived, entry, rows, saved, weights, kept, sides, items, shapes, count):
    chips = count // 2
    length, width = arrived.shape
    deep = weights[2].shape[1]
    cells = kept[0].shape[0]
    rows_in = cells * length
    own = width // count
    vmem, hbm = (pl.BlockSpec(memory_space=pltpu.VMEM), pl.BlockSpec(memory_space=pl.ANY))
    cut = width // 2
    wholes = [(16, own)] + [tuple(shape) for shape in shapes]
    held = [(many,) + wholes[array][1:] for array, _, many, _ in items]
    kinds = [F32 if array == 0 else LOW for array, _, _, _ in items]
    pieces = len(items)
    flops = 2 * length * width * (4 * width + 2 * deep) + 2 * rows_in * width * (4 * width + 2 * deep)
    outs = pl.pallas_call(
        functools.partial(last_backward_kernel, chips, items, cells - 1),
        out_shape=[jax.ShapeDtypeStruct(array.shape, array.dtype) for array in kept]
        + [jax.ShapeDtypeStruct((many, own), F32) for many in (2, 6, deep // width)]
        + [jax.ShapeDtypeStruct(shape, F32) for shape in wholes[1:]]
        + [jax.ShapeDtypeStruct((count,) + shape, LOW) for shape in wholes[1:]]
        + [jax.ShapeDtypeStruct((chips - 1,) + shape, kind) for shape, kind in zip(held, kinds)]
        + [jax.ShapeDtypeStruct((chips,) + shape, kind) for shape, kind in zip(held, kinds)],
        in_specs=[vmem, hbm, vmem] + [hbm] * 17,
        out_specs=[hbm] * 5 + [vmem] * 3 + [hbm] * (8 + 2 * pieces),
        input_output_aliases={15 + number: number for number in range(5)},
        scratch_shapes=[pltpu.VMEM((2,) + shape, kind) for shape, kind in zip(held, kinds)] * 3
        + [
            pltpu.VMEM((4, 80, width), F32),
            pltpu.VMEM((count, 16, own), F32),
            pltpu.VMEM((cells, 16, width), F32),
            pltpu.SemaphoreType.DMA((pieces, chips - 1)),
            pltpu.SemaphoreType.DMA((pieces, chips - 1)),
            pltpu.SemaphoreType.DMA((pieces, chips)),
            pltpu.SemaphoreType.DMA((pieces, chips)),
            pltpu.SemaphoreType.DMA((pieces, 6)),
            pltpu.SemaphoreType.DMA((4,)),
            pltpu.VMEM((2, rows_in, width), LOW),
            pltpu.VMEM((2, rows_in, cut), LOW),
            pltpu.VMEM((2, chips, own, width), LOW),
            pltpu.VMEM((2, 2, shapes[3][0], width), LOW),
            pltpu.SemaphoreType.DMA((2,)),
            pltpu.SemaphoreType.DMA((2,)),
            pltpu.SemaphoreType.DMA((4,)),
            pltpu.VMEM((2, width, width), LOW),
            pltpu.SemaphoreType.DMA((2,)),
            pltpu.SemaphoreType.DMA((cells + 4,)),
            pltpu.SemaphoreType.DMA((4,)),
            pltpu.SemaphoreType.DMA((2,)),
            pltpu.SemaphoreType.DMA((2,)),
            pltpu.VMEM((length, width), LOW),
            pltpu.VMEM((length, 3 * width), LOW),
            pltpu.VMEM((length, width), F32),
            pltpu.VMEM((2, length, width), LOW),
            pltpu.VMEM((2, length, width), LOW),
            pltpu.VMEM((length, 3 * width), LOW),
            pltpu.VMEM((length, width), LOW),
            pltpu.VMEM((length, width), LOW),
            pltpu.VMEM((2, length, width), F32),
            pltpu.VMEM((length, width), F32),
            pltpu.VMEM((16, width), F32),
        ],
        compiler_params=pltpu.CompilerParams(
            collective_id=2, has_side_effects=True, vmem_limit_bytes=62 * 2**20
        ),
        cost_estimate=pl.CostEstimate(flops=flops, bytes_accessed=160 * width * width, transcendentals=0),
    )(arrived, entry, rows, *saved, *weights, *sides, *kept)
    return (list(outs[:5]), outs[5:8], outs[8:12])


def on_device(inputs, out_grad, query_counts, gains, shifts, w_qkv, w_out, w_up, b_up, w_down):
    stage = lax.axis_index("pipe")
    stages = lax.axis_size("pipe")
    count = lax.axis_size("dp")
    cell_count, length, width = inputs.shape
    own = width // count
    ups = b_up.shape[1] // own
    deep = ups * width
    deep_own = w_down.shape[1]
    shapes = [
        block_shape(own, 3 * width),
        block_shape(own, width),
        block_shape(own, deep),
        block_shape(deep_own, width),
    ]
    cut = (shapes[3][0] // 2 + 15) // 16 * 16
    items = (
        (0, 0, 16, 0),
        (1, 0, shapes[0][0], 0),
        (2, 0, shapes[1][0], 0),
        (3, 0, shapes[2][0], 1),
        (4, 0, cut, 0),
        (4, cut, shapes[3][0] - cut, 1),
    )
    shards = [small_pack(gains[0], shifts[0], b_up[0], 1)[0]] + [
        array[0].reshape(shape) for array, shape in zip((w_qkv, w_out, w_up, w_down), shapes)
    ]
    fused = stages == 2 and cell_count == 2 and own % 16 == 0 and width % 256 == 0 and 4 * deep_own == width
    if fused:
        piece = own // 2 // 16 * 16
        arrivals = (
            (0, 0, 16, 0),
            (1, 0, own - piece, 0),
            (1, own - piece, piece, 1),
            (2, 0, own, 1),
            (3, 0, own - piece, 0),
            (3, own - piece, piece, 1),
            (4, 0, cut, 0),
            (4, cut, deep_own - cut, 1),
        )
        packs, rows, arrived, kept = gather_forward(
            shards, inputs, arrivals, ((0, 1, 2, 3), (4, 5), (6, 7)), count
        )
    else:
        packs = gather(shards, items, count)
        gain_rows, shift_rows, bias = small_split(packs[0].astype(F32), ups)
        blank = jnp.zeros((8 - ups, width), F32)
        rows = jnp.concatenate([gain_rows, shift_rows, bias.reshape(ups, width), blank])
    weights = (
        packs[1].reshape(width, 3 * width),
        packs[2].reshape(width, width),
        packs[3].reshape(width, deep),
        packs[4].reshape(deep, width),
    )
    scales = jnp.sqrt(query_counts.astype(F32) / 500.0)

    def along(value, steps):
        pairs = [(source, source + steps) for source in range(stages) if 0 <= source + steps < stages]
        return lax.ppermute(value, "pipe", pairs)

    entries = [[(inputs, cell) for cell in range(cell_count)]]
    if fused:
        entries.append([(arrived, cell) for cell in range(cell_count)])
    else:
        kept = None
    for turn in range(1 if fused else 0, stages):
        active = (stage == turn).astype(jnp.int32)[None]
        arrived = []
        for cell in range(1 if fused else 0, cell_count):
            sent, kept = forward_tick(active, entries[turn][cell], rows, weights, kept, cell, cell_count)
            if turn + 1 < stages:
                arrived.append((along(sent, 1), None))
        entries.append(arrived)
    section_out, lowered, packed, mixed, middle, second, activated, slope = kept
    incoming = [((out_grad, cell), scales[cell][None]) for cell in range(cell_count)]
    back = None
    for turn in range(stages - 1, -1, -1):
        active = (stage == turn).astype(jnp.int32)[None]
        arrived = []
        for cell in range(cell_count):
            if fused and turn == 0 and cell == cell_count - 1:
                continue
            sent, back = backward_tick(
                active, incoming[cell], entries[turn][cell], rows, (packed, middle, slope), weights, back, cell, cell_count
            )
            if turn > 0:
                arrived.append(((along(sent, -1), None), jnp.ones((1,), F32)))
        incoming = arrived if turn > 0 else incoming

    def flat(array):
        return array.reshape(cell_count * length, -1)

    input_grads, grad_packed, grad_branch, grad_inner, grad_ff, sums = back
    if fused:
        (input_grads, _, _, _, _), (grad_gains, grad_shifts, grad_bias), shares = last_backward(
            incoming[-1][0][0],
            inputs,
            rows,
            (packed, middle, slope),
            weights,
            (input_grads, flat(grad_packed), flat(grad_branch), flat(grad_inner), sums),
            [flat(array) for array in (activated, grad_ff, second, mixed, lowered)],
            arrivals,
            shapes,
            count,
        )
    else:
        sums = jnp.sum(sums, axis=0)
        small_part = small_pack(sums[0:2], sums[2:8], sums[8 : 8 + ups].reshape(deep), count)
        sides = [flat(array) for array in (lowered, grad_packed, mixed, grad_branch, second, grad_inner, activated, grad_ff)]
        products = [dot_left(sides[at], sides[at + 1]).astype(LOW) for at in (0, 2, 4, 6)]
        parts = [small_part] + [whole.reshape((count,) + shape) for whole, shape in zip(products, shapes)]
        small_share, *shares = scatter(parts, items, count)
        grad_gains, grad_shifts, grad_bias = small_split(small_share[None], ups)
    return (
        section_out[None],
        input_grads[None],
        grad_gains[None],
        grad_shifts[None],
        shares[0].reshape(1, own, 3 * width),
        shares[1].reshape(1, own, width),
        shares[2].reshape(1, own, deep),
        grad_bias.reshape(1, ups * own),
        shares[3].reshape(1, deep_own, width),
    )


def solution(mesh):
    in_specs = (
        P("dp", None, None),
        P("dp", None, None),
        P("dp"),
        P("pipe", None, "dp"),
        P("pipe", None, "dp"),
        P("pipe", "dp", None),
        P("pipe", "dp", None),
        P("pipe", "dp", None),
        P("pipe", "dp"),
        P("pipe", "dp", None),
    )
    out_specs = (
        P("pipe", "dp", None, None),
        P("pipe", "dp", None, None),
        P("pipe", None, "dp"),
        P("pipe", None, "dp"),
        P("pipe", "dp", None),
        P("pipe", "dp", None),
        P("pipe", "dp", None),
        P("pipe", "dp"),
        P("pipe", "dp", None),
    )
    return jax.shard_map(
        on_device, mesh=mesh, in_specs=in_specs, out_specs=out_specs, check_vma=False
    )
```

```python
import functools
import math

import jax
import jax.numpy as jnp
from jax import lax
from jax.experimental import pallas as pl
from jax.experimental.pallas import tpu as pltpu
from jax.sharding import PartitionSpec as P

HEAD_DIM = 64
MESH = pl.DeviceIdType.MESH
LOW = jnp.bfloat16
F32 = jnp.float32


def ring_chip(position, chips):
    position = lax.rem(position + 2 * chips, chips)
    half = chips // 2
    return jnp.where(position < half, 2 * position, 2 * (chips - 1 - position) + 1)


def ring_place(chips):
    me = lax.axis_index("dp")
    core = lax.rem(me, 2)
    chip = me // 2
    position = jnp.where(lax.rem(chip, 2) == 0, chip // 2, chips - 1 - chip // 2)
    right = ring_chip(position + 1, chips) * 2 + core
    left = ring_chip(position - 1, chips) * 2 + core
    return (me, core, position, right, left, me + 1 - 2 * core)


def greet(devices):
    barrier = pltpu.get_barrier_semaphore()
    for device in devices:
        pl.semaphore_signal(barrier, inc=1, device_id={"dp": device}, device_id_type=MESH)
    pl.semaphore_wait(barrier, len(devices))


def gather_kernel(chips, arrays, items, *refs):
    count = len(items)
    ring_send, ring_recv, pair_send, pair_recv, own_sem = refs[2 * arrays :]
    shards = [refs[array].at[pl.ds(start, rows)] for array, start, rows, _ in items]
    splits = [way for _, _, _, way in items]
    half = chips // 2
    me, core, position, right, left, sibling = ring_place(chips)
    greet((left, right, sibling))

    def out(item, block):
        array, start, rows, _ = items[item]
        return refs[arrays + array].at[block, pl.ds(start, rows)]

    def owner(step, way):
        return ring_chip(position - step if way == 0 else position + step, chips) * 2 + core

    def travels(item, way, step):
        return step < half or (step == half and splits[item] == way)

    def ring_copy(item, way, step):
        block = owner(step - 1, way)
        return pltpu.make_async_remote_copy(
            src_ref=shards[item] if step == 1 else out(item, block),
            dst_ref=out(item, block),
            send_sem=ring_send.at[item, way, step - 1],
            recv_sem=ring_recv.at[item, way, step - 1],
            device_id={"dp": right if way == 0 else left},
            device_id_type=MESH,
        )

    def pair_copy(item, offset, block, source):
        return pltpu.make_async_remote_copy(
            src_ref=source,
            dst_ref=out(item, block),
            send_sem=pair_send.at[item, offset],
            recv_sem=pair_recv.at[item, offset],
            device_id={"dp": sibling},
            device_id_type=MESH,
        )

    sent, paired, kept = ([], [], [])
    for item in range(count):
        for way in (0, 1):
            if travels(item, way, 1):
                sent.append(ring_copy(item, way, 1))
                sent[-1].start()
    for item in range(count):
        paired.append(pair_copy(item, 0, me, shards[item]))
        paired[-1].start()
        kept.append(pltpu.make_async_copy(shards[item], out(item, me), own_sem.at[item]))
        kept[-1].start()
    for step in range(1, half + 1):
        for item in range(count):
            for way in (0, 1):
                if not travels(item, way, step):
                    continue
                ring_copy(item, way, step).wait_recv()
                if travels(item, way, step + 1):
                    sent.append(ring_copy(item, way, step + 1))
                    sent[-1].start()
                block = owner(step, way)
                offset = step if way == 0 else chips - step
                paired.append(pair_copy(item, offset, block, out(item, block)))
                paired[-1].start()
    for copy in sent:
        copy.wait_send()
    for copy in paired:
        copy.wait()
    for copy in kept:
        copy.wait()


def gather(shards, items, count):
    chips = count // 2
    arrays, pieces = (len(shards), len(items))
    return pl.pallas_call(
        functools.partial(gather_kernel, chips, arrays, items),
        out_shape=[jax.ShapeDtypeStruct((count,) + shard.shape, shard.dtype) for shard in shards],
        in_specs=[pl.BlockSpec(memory_space=pl.ANY)] * arrays,
        out_specs=[pl.BlockSpec(memory_space=pl.ANY)] * arrays,
        scratch_shapes=[
            pltpu.SemaphoreType.DMA((pieces, 2, chips // 2)),
            pltpu.SemaphoreType.DMA((pieces, 2, chips // 2)),
            pltpu.SemaphoreType.DMA((pieces, chips)),
            pltpu.SemaphoreType.DMA((pieces, chips)),
            pltpu.SemaphoreType.DMA((pieces,)),
        ],
        compiler_params=pltpu.CompilerParams(collective_id=0, has_side_effects=True),
    )(*shards)


def scatter_kernel(chips, arrays, items, *refs):
    count = len(items)
    parts, outs, refs = (refs[:arrays], refs[arrays : 2 * arrays], refs[2 * arrays :])
    landed, paired, mine = (refs[:count], refs[count : 2 * count], refs[2 * count : 3 * count])
    ring_send, ring_recv, pair_send, pair_recv, mine_sem = refs[3 * count :]
    splits = [way for _, _, _, way in items]
    half = chips // 2
    me, core, position, right, left, sibling = ring_place(chips)
    greet((left, right, sibling))

    def part(item, block):
        array, start, rows, _ = items[item]
        return parts[array].at[block, pl.ds(start, rows)]

    def first(item, way):
        return 1 if splits[item] == way else 2

    def slot(item, way, step):
        return step - 1 if splits[item] == way else half + step - 2

    def offset_of(step, way):
        return half - step + 1 if way == 0 else chips - (half - step + 1)

    def pair_copy(item, offset):
        block = ring_chip(position + offset, chips) * 2 + 1 - core
        return pltpu.make_async_remote_copy(
            src_ref=part(item, block),
            dst_ref=paired[item].at[offset],
            send_sem=pair_send.at[item, offset],
            recv_sem=pair_recv.at[item, offset],
            device_id={"dp": sibling},
            device_id_type=MESH,
        )

    def ring_copy(item, way, step):
        if step == first(item, way):
            source = paired[item].at[offset_of(step, way)]
        else:
            source = landed[item].at[slot(item, way, step - 1)]
        here = slot(item, way, step)
        return pltpu.make_async_remote_copy(
            src_ref=source,
            dst_ref=landed[item].at[here],
            send_sem=ring_send.at[item, here],
            recv_sem=ring_recv.at[item, here],
            device_id={"dp": right if way == 0 else left},
            device_id_type=MESH,
        )

    def load(item, offset, buffer):
        block = ring_chip(position + offset, chips) * 2 + core
        return pltpu.make_async_copy(part(item, block), mine[item].at[buffer], mine_sem.at[item, buffer])

    plan, uses = ([], [0] * count)
    for step in range(1, half + 2):
        for item in range(count):
            for way in (0, 1):
                if step <= half and step >= first(item, way):
                    plan.append((step, item, way, offset_of(step, way), uses[item] % 2))
                    uses[item] += 1
            if step > half:
                plan.append((step, item, None, 0, uses[item] % 2))
                uses[item] += 1
    for step, item, way, offset, buffer in plan:
        pair_copy(item, offset).start()
    load(plan[0][1], plan[0][3], plan[0][4]).start()
    sent = []
    for number, (step, item, way, offset, buffer) in enumerate(plan):
        if number + 1 < len(plan):
            load(plan[number + 1][1], plan[number + 1][3], plan[number + 1][4]).start()
        load(item, offset, buffer).wait()
        pair_copy(item, offset).wait_recv()
        array, start, rows, _ = items[item]
        kind = parts[array].dtype
        chunk = 16 if rows % 16 == 0 else rows
        from_pair, from_mine, from_ring = (paired[item], mine[item], landed[item])
        if way is None:
            ring_copy(item, 0, half).wait_recv()
            ring_copy(item, 1, half).wait_recv()
            slot_a, slot_b = (slot(item, 0, half), slot(item, 1, half))

            @pl.loop(0, rows // chunk)
            def _(index):
                here = pl.ds(pl.multiple_of(index * chunk, chunk), chunk)
                outs[array][pl.ds(pl.multiple_of(start + index * chunk, chunk), chunk), :] = (
                    from_ring[slot_a, here, :].astype(F32) + from_ring[slot_b, here, :].astype(F32)
                ) + (from_mine[buffer, here, :].astype(F32) + from_pair[offset, here, :].astype(F32))

            continue
        if step == first(item, way):

            @pl.loop(0, rows // chunk)
            def _(index):
                here = pl.ds(pl.multiple_of(index * chunk, chunk), chunk)
                from_pair[offset, here, :] = (
                    from_mine[buffer, here, :].astype(F32) + from_pair[offset, here, :].astype(F32)
                ).astype(kind)

        else:
            ring_copy(item, way, step - 1).wait_recv()
            arrived = slot(item, way, step - 1)

            @pl.loop(0, rows // chunk)
            def _(index):
                here = pl.ds(pl.multiple_of(index * chunk, chunk), chunk)
                from_ring[arrived, here, :] = (
                    from_ring[arrived, here, :].astype(F32)
                    + (from_mine[buffer, here, :].astype(F32) + from_pair[offset, here, :].astype(F32))
                ).astype(kind)

        sent.append(ring_copy(item, way, step))
        sent[-1].start()
    for copy in sent:
        copy.wait_send()
    for step, item, way, offset, buffer in plan:
        pair_copy(item, offset).wait_send()


def scatter(parts, items, count):
    chips = count // 2
    arrays, pieces = (len(parts), len(items))
    shapes = [(rows,) + parts[array].shape[2:] for array, _, rows, _ in items]
    kinds = [parts[array].dtype for array, _, _, _ in items]
    return pl.pallas_call(
        functools.partial(scatter_kernel, chips, arrays, items),
        out_shape=[jax.ShapeDtypeStruct(part.shape[1:], F32) for part in parts],
        in_specs=[pl.BlockSpec(memory_space=pl.ANY)] * arrays,
        out_specs=[pl.BlockSpec(memory_space=pltpu.VMEM)] * arrays,
        scratch_shapes=[pltpu.VMEM((chips - 1,) + shape, kind) for shape, kind in zip(shapes, kinds)]
        + [pltpu.VMEM((chips,) + shape, kind) for shape, kind in zip(shapes, kinds)]
        + [pltpu.VMEM((2,) + shape, kind) for shape, kind in zip(shapes, kinds)]
        + [
            pltpu.SemaphoreType.DMA((pieces, chips - 1)),
            pltpu.SemaphoreType.DMA((pieces, chips - 1)),
            pltpu.SemaphoreType.DMA((pieces, chips)),
            pltpu.SemaphoreType.DMA((pieces, chips)),
            pltpu.SemaphoreType.DMA((pieces, 2)),
        ],
        compiler_params=pltpu.CompilerParams(
            collective_id=1, has_side_effects=True, vmem_limit_bytes=62 * 2**20
        ),
    )(*parts)


def block_shape(rows, columns):
    return (rows, columns) if rows % 16 == 0 else (rows * columns // 128, 128)


def small_pack(gains, shifts, bias, count):
    width = gains.shape[1] // count
    ups = bias.shape[0] // gains.shape[1]
    rows = [
        gains.reshape(2, count, width).swapaxes(0, 1),
        shifts.reshape(6, count, width).swapaxes(0, 1),
        bias.reshape(count, ups, width),
    ]
    blank = jnp.zeros((count, 8 - ups, width), gains.dtype)
    return jnp.concatenate(rows + [blank], axis=1)


def small_split(blocks, ups):
    count, _, width = blocks.shape
    gains = blocks[:, 0:2].swapaxes(0, 1).reshape(2, count * width)
    shifts = blocks[:, 2:8].swapaxes(0, 1).reshape(6, count * width)
    bias = blocks[:, 8 : 8 + ups].reshape(count * ups * width)
    return (gains, shifts, bias)


def row_norm(rows_in):
    center = rows_in - jnp.mean(rows_in, axis=-1, keepdims=True)
    inverse = lax.rsqrt(jnp.mean(center * center, axis=-1, keepdims=True) + 1e-05)
    return (center * inverse, inverse)


def norm_back(grad_rows, normed, inverse):
    return inverse * (
        grad_rows
        - jnp.mean(grad_rows, axis=-1, keepdims=True)
        - normed * jnp.mean(grad_rows * normed, axis=-1, keepdims=True)
    )


def gelu_parts(hidden):
    cumulative = 0.5 * (1.0 + lax.erf(hidden * (1.0 / math.sqrt(2.0))))
    slope = cumulative + hidden * jnp.exp(-0.5 * hidden * hidden) * (1.0 / math.sqrt(2.0 * math.pi))
    return (hidden * cumulative, slope)


def dot(left, right):
    return lax.dot_general(left, right, (((1,), (0,)), ((), ())), preferred_element_type=F32)


def dot_right(left, right):
    return lax.dot_general(left, right, (((1,), (1,)), ((), ())), preferred_element_type=F32)


def dot_left(left, right):
    return lax.dot_general(left, right, (((0,), (0,)), ((), ())), preferred_element_type=F32)


class Stream:
    def __init__(self, blocks, buffers, sems):
        self.blocks, self.buffers, self.sems = (blocks, buffers, sems)
        self.depth = buffers.shape[0]
        self.started = 0
        for _ in range(min(self.depth, len(blocks))):
            self.start()

    def copy(self, number):
        slot = number % self.depth
        return pltpu.make_async_copy(self.blocks[number], self.buffers.at[slot], self.sems.at[slot])

    def start(self):
        self.copy(self.started).start()
        self.started += 1

    def take(self, number):
        self.copy(number).wait()
        return self.buffers.at[number % self.depth]

    def release(self):
        if self.started < len(self.blocks):
            self.start()


def weight_blocks(w_qkv, w_out, w_up, w_down):
    width = w_out.shape[0]
    def cut(ref, axis, number):
        window = pl.ds(number * width, width)
        return ref.at[:, window] if axis else ref.at[window, :]
    heads = [cut(w_qkv, 1, number) for number in range(3)]
    ups = [cut(w_up, 1, number) for number in range(w_up.shape[1] // width)]
    downs = [cut(w_down, 0, number) for number in range(w_down.shape[0] // width)]
    return (heads, w_out, ups, downs)


def head_masks(length):
    return lax.broadcasted_iota(jnp.int32, (length, 128), 1) < HEAD_DIM


def two_heads(array, side):
    blank = jnp.zeros_like(array)
    return jnp.concatenate([jnp.where(side, array, blank), jnp.where(side, blank, array)], axis=0)


def attend(packed, mixed, width, low=0, high=None):
    length = packed.shape[0]
    side = head_masks(length)

    def pair_of(pair):
        start = pair * 128 if isinstance(pair, int) else pl.multiple_of(pair * 128, 128)
        queries = packed[:, pl.ds(start, 128)] * jnp.asarray(1.0 / math.sqrt(HEAD_DIM), LOW)
        keys = two_heads(packed[:, pl.ds(start + width, 128)], side)
        values = two_heads(packed[:, pl.ds(start + 2 * width, 128)], side)
        scores = dot_right(queries, keys)
        probs, totals = ([], [])
        for head in (0, 1):
            mine = scores[:, head * length : (head + 1) * length]
            shifted = jnp.exp(mine - jnp.max(mine, axis=-1, keepdims=True))
            totals.append(1.0 / jnp.sum(shifted, axis=-1, keepdims=True))
            probs.append(shifted.astype(LOW))
        result = dot(jnp.concatenate(probs, axis=1), values)
        mixed[:, pl.ds(start, 128)] = (result * jnp.where(side, totals[0], totals[1])).astype(LOW)

    if high is not None:
        for pair in range(low, high):
            pair_of(pair)
        return

    @pl.loop(0, width // 256)
    def _(index):
        pair_of(index * 2)
        pair_of(index * 2 + 1)


def attend_back(packed, grad_mixed, grad_packed, width, low=0, high=None):
    length = packed.shape[0]
    side = head_masks(length)
    scale = 1.0 / math.sqrt(HEAD_DIM)

    def pair_of(pair):
        start = pair * 128 if isinstance(pair, int) else pl.multiple_of(pair * 128, 128)
        queries = packed[:, pl.ds(start, 128)]
        keys = packed[:, pl.ds(start + width, 128)] * jnp.asarray(scale, LOW)
        grads = grad_mixed[:, pl.ds(start, 128)]
        keys_two = two_heads(keys, side)
        queries_two = two_heads(queries, side)
        grads_two = two_heads(grads, side)
        scores = dot_right(keys, queries_two)
        grad_probs = dot_right(packed[:, pl.ds(start + 2 * width, 128)], grads_two)
        probs, grad_scores = ([], [])
        for head in (0, 1):
            mine = slice(head * length, (head + 1) * length)
            shifted = jnp.exp(scores[:, mine] - jnp.max(scores[:, mine], axis=0, keepdims=True))
            prob = shifted * (1.0 / jnp.sum(shifted, axis=0, keepdims=True))
            product = grad_probs[:, mine] * prob
            weighted = jnp.sum(product, axis=0, keepdims=True)
            probs.append(prob.astype(LOW))
            grad_scores.append((product - prob * weighted).astype(LOW))
        beside = jnp.concatenate(grad_scores, axis=1)
        grad_packed[:, pl.ds(start, 128)] = dot_left(jnp.concatenate(grad_scores, axis=0), keys_two).astype(LOW)
        grad_packed[:, pl.ds(start + width, 128)] = (dot(beside, queries_two) * scale).astype(LOW)
        grad_packed[:, pl.ds(start + 2 * width, 128)] = dot(jnp.concatenate(probs, axis=1), grads_two).astype(LOW)

    if high is not None:
        for pair in range(low, high):
            pair_of(pair)
        return

    @pl.loop(0, width // 256)
    def _(index):
        pair_of(index * 2)
        pair_of(index * 2 + 1)


def forward_kernel(cell, held, at, active, entry_h, rows, w_qkv, w_out, w_up, w_down, *refs):
    sent_h = refs[held]
    out_h, lowered_h, packed_h, mixed_h, middle_h, second_h, active_h, slope_h = [
        ref.at[cell] for ref in refs[held + 1 : held + 9]
    ]
    (buffers, buffer_sems, save_sems, out_v, lowered_v, packed_v, mixed_v, middle_v) = refs[held + 9 : held + 17]
    (second_v, active_v, slope_v, hidden_v, total_v, entry, entry_sem) = refs[held + 17 :]
    entry = entry_h if at is None else entry
    width = entry.shape[1]
    gains, shifts, bias = (rows.at[0:2], rows.at[2:8], rows.at[8:16])
    ups = w_up.shape[1] // width

    @pl.when(active[0] != 0)
    def _():
        heads, outer, up, down = weight_blocks(w_qkv, w_out, w_up, w_down)
        order = heads + [outer]
        place_up, place_down = ({}, {})
        for number in range(ups + 1):
            if number < ups:
                place_up[number] = len(order)
                order.append(up[number])
            if number > 0:
                place_down[number - 1] = len(order)
                order.append(down[number - 1])
        if at is not None:
            fetched = pltpu.make_async_copy(entry_h.at[at], entry, entry_sem)
            fetched.start()
        saves = []

        def save(source, target):
            saves.append(pltpu.make_async_copy(source, target, save_sems.at[len(saves)]))
            saves[-1].start()

        if at is not None:
            fetched.wait()
        stream = Stream(order, buffers, buffer_sems)
        rows_in = entry[...].astype(F32)
        normed, _ = row_norm(rows_in)
        lowered_v[...] = (normed * gains[0:1, :] + shifts[0:1, :]).astype(LOW)
        save(lowered_v, lowered_h)
        for number in range(3):
            block = stream.take(number)
            window = pl.ds(number * width, width)
            part = dot(lowered_v[...], block[...])
            if number != 1:
                part = part + shifts[1 + number // 2 : 2 + number // 2, :]
            packed_v[:, window] = part.astype(LOW)
            stream.release()
        save(packed_v, packed_h)
        attend(packed_v, mixed_v, width)
        save(mixed_v, mixed_h)
        block = stream.take(3)
        middle = entry[...].astype(F32) + dot(mixed_v[...], block[...]) + shifts[3:4, :]
        middle_v[...] = middle
        stream.release()
        save(middle_v, middle_h)
        normed, _ = row_norm(middle_v[...])
        second_v[...] = (normed * gains[1:2, :] + shifts[4:5, :]).astype(LOW)
        save(second_v, second_h)
        for number in range(ups + 1):
            if number < ups:
                up_block = stream.take(place_up[number])
            if number > 0:
                down_block = stream.take(place_down[number - 1])
            if number < ups:
                hidden_v[number % 2] = dot(second_v[...], up_block[...]) + bias[number : number + 1, :]
            if number > 0:
                window = pl.ds((number - 1) * width, width)
                activated, slope = gelu_parts(hidden_v[(number - 1) % 2])
                active_v[:, window] = activated.astype(LOW)
                slope_v[:, window] = slope.astype(LOW)
                part = dot(active_v[:, window], down_block[...])
                if number == 1:
                    total_v[...] = part
                elif number < ups:
                    total_v[...] += part
                else:
                    out_v[...] = (middle_v[...] + (total_v[...] + part + shifts[5:6, :])).astype(LOW)
                save(active_v.at[:, window], active_h.at[:, window])
                save(slope_v.at[:, window], slope_h.at[:, window])
            if number < ups:
                stream.release()
            if number > 0:
                stream.release()
        save(out_v, sent_h)
        save(out_v, out_h)
        for copy in saves:
            copy.wait()


def kept_shapes(length, width, deep):
    return [
        ((length, width), LOW),
        ((length, width), LOW),
        ((length, 3 * width), LOW),
        ((length, width), LOW),
        ((length, width), F32),
        ((length, width), LOW),
        ((length, deep), LOW),
        ((length, deep), LOW),
    ]


def forward_tick(active, entry, rows, weights, kept, cell, cell_count):
    entry, at = entry
    length, width = entry.shape[-2:]
    deep = weights[2].shape[1]
    ups = deep // width
    shapes = kept_shapes(length, width, deep)
    outs = [jax.ShapeDtypeStruct(*shapes[0])] + [
        jax.ShapeDtypeStruct((cell_count,) + shape, kind) for shape, kind in shapes
    ]
    vmem, hbm = (pl.BlockSpec(memory_space=pltpu.VMEM), pl.BlockSpec(memory_space=pl.ANY))
    flops = 2 * length * width * (4 * width + 2 * deep) + 16 * length * length * width
    kept = () if kept is None else tuple(kept)
    held = len(kept)
    sent, *kept = pl.pallas_call(
        functools.partial(forward_kernel, cell, held, at),
        out_shape=outs,
        in_specs=[pl.BlockSpec(memory_space=pltpu.SMEM), vmem if at is None else hbm, vmem] + [hbm] * (4 + held),
        out_specs=[hbm] * 9,
        input_output_aliases={7 + number: 1 + number for number in range(held)},
        scratch_shapes=[
            pltpu.VMEM((4, width, width), LOW),
            pltpu.SemaphoreType.DMA((4,)),
            pltpu.SemaphoreType.DMA((7 + 2 * ups,)),
        ]
        + [pltpu.VMEM(*shape) for shape in shapes]
        + [
            pltpu.VMEM((2, length, width), F32),
            pltpu.VMEM((length, width), F32),
            pltpu.VMEM((length, width), LOW),
            pltpu.SemaphoreType.DMA,
        ],
        compiler_params=pltpu.CompilerParams(vmem_limit_bytes=60 * 2**20),
        cost_estimate=pl.CostEstimate(
            flops=flops, bytes_accessed=2 * width * (4 * width + 2 * deep), transcendentals=0
        ),
    )(active, entry, rows, *weights, *kept)
    return (sent, kept)


def backward_kernel(cell, held, grad_at, entry_at, active, scale, grad_h, entry_h, rows, *refs):
    packed, middle, slope = [ref.at[cell] for ref in refs[:3]]
    w_qkv, w_out, w_up, w_down = refs[3:7]
    refs = refs[7 + held :]
    sent_h = refs[0]
    rows_h, packed_h, branch_h, inner_h, low_h, sums_h = [ref.at[cell] for ref in refs[1:7]]
    (buffers, buffer_sems, load_sems, save_sems, rows_v, grad_packed_v, branch_v, inner_v, low_v, sums_v) = refs[7:17]
    (packed_v, middle_v, slope_v, mixed_v, grad_act_v, total_v, grad_middle_v, grad, entry) = refs[17:]
    gains = rows.at[0:2]
    grad = grad_h if grad_at is None else grad
    entry_h = entry_h if entry_at is None else entry_h.at[entry_at]
    length, width = entry.shape
    ups = w_up.shape[1] // width

    @pl.when(active[0] != 0)
    def _():
        heads, outer, up, down = weight_blocks(w_qkv, w_out, w_up, w_down)
        loads = [
            pltpu.make_async_copy(slope, slope_v, load_sems.at[0]),
            pltpu.make_async_copy(middle, middle_v, load_sems.at[1]),
            pltpu.make_async_copy(packed, packed_v, load_sems.at[2]),
            pltpu.make_async_copy(entry_h, entry, load_sems.at[3]),
        ]
        if grad_at is not None:
            loads.append(pltpu.make_async_copy(grad_h.at[grad_at], grad, load_sems.at[4]))
            loads[4].start()
        order, place_up, place_down = ([], {}, {})
        for number in range(ups + 1):
            if number < ups:
                place_down[number] = len(order)
                order.append(down[number])
            if number > 0:
                place_up[number - 1] = len(order)
                order.append(up[number - 1])
        place_out = len(order)
        order = order + [outer] + heads
        saves = []

        def save(source, target):
            saves.append(pltpu.make_async_copy(source, target, save_sems.at[len(saves)]))
            saves[-1].start()

        def column_sum(array):
            return jnp.sum(array.astype(F32), axis=0, keepdims=True)

        if grad_at is not None:
            loads[4].wait()
        stream = Stream(order, buffers, buffer_sems)
        loads[0].start()
        low_v[...] = (grad[...].astype(F32) * scale[0]).astype(LOW)
        save(low_v, low_h)
        sums_v[7:8, :] = column_sum(low_v[...])
        for number in range(ups + 1):
            if number == 1:
                loads[0].wait()
                loads[1].start()
            if number == 2:
                loads[2].start()
                loads[3].start()
            if number < ups:
                down_block = stream.take(place_down[number])
            if number > 0:
                up_block = stream.take(place_up[number - 1])
            if number < ups:
                grad_act_v[number % 2] = dot_right(low_v[...], down_block[...])
            if number > 0:
                window = pl.ds((number - 1) * width, width)
                inner = (grad_act_v[(number - 1) % 2] * slope_v[:, window].astype(F32)).astype(LOW)
                inner_v[:, window] = inner
                sums_v[7 + number : 8 + number, :] = column_sum(inner)
                part = dot_right(inner, up_block[...])
                if number == 1:
                    total_v[...] = part
                else:
                    total_v[...] += part
                save(inner_v.at[:, window], inner_h.at[:, window])
            if number < ups:
                stream.release()
            if number > 0:
                stream.release()
        loads[1].wait()
        normed, inverse = row_norm(middle_v[...])
        grad_second = total_v[...]
        sums_v[1:2, :] = column_sum(grad_second * normed)
        sums_v[6:7, :] = column_sum(grad_second)
        grad_middle = grad[...].astype(F32) * scale[0] + norm_back(grad_second * gains[1:2, :], normed, inverse)
        grad_middle_v[...] = grad_middle
        branch_v[...] = grad_middle.astype(LOW)
        sums_v[5:6, :] = column_sum(branch_v[...])
        save(branch_v, branch_h)
        block = stream.take(place_out)
        mixed_v[...] = dot_right(branch_v[...], block[...]).astype(LOW)
        stream.release()
        loads[2].wait()
        attend_back(packed_v, mixed_v, grad_packed_v, width)
        save(grad_packed_v, packed_h)
        sums_v[3:4, :] = column_sum(grad_packed_v[:, pl.ds(0, width)])
        sums_v[4:5, :] = column_sum(grad_packed_v[:, pl.ds(2 * width, width)])
        for number in range(3):
            block = stream.take(place_out + 1 + number)
            part = dot_right(grad_packed_v[:, pl.ds(number * width, width)], block[...])
            if number == 0:
                total_v[...] = part
            else:
                total_v[...] += part
            stream.release()
        loads[3].wait()
        normed, inverse = row_norm(entry[...].astype(F32))
        grad_lowered = total_v[...]
        sums_v[0:1, :] = column_sum(grad_lowered * normed)
        sums_v[2:3, :] = column_sum(grad_lowered)
        rows_v[...] = (grad_middle_v[...] + norm_back(grad_lowered * gains[0:1, :], normed, inverse)).astype(LOW)
        save(sums_v, sums_h)
        save(rows_v, sent_h)
        save(rows_v, rows_h)
        for copy in saves:
            copy.wait()


def backward_tick(active, incoming, entry, rows, saved, weights, kept, cell, cell_count):
    entry, entry_at = entry
    (grad, grad_at), scale = incoming
    length, width = entry.shape[-2:]
    deep = weights[2].shape[1]
    ups = deep // width
    shapes = [
        ((length, width), LOW),
        ((length, 3 * width), LOW),
        ((length, width), LOW),
        ((length, deep), LOW),
        ((length, width), LOW),
        ((16, width), F32),
    ]
    outs = [jax.ShapeDtypeStruct(*shapes[0])] + [
        jax.ShapeDtypeStruct((cell_count,) + shape, kind) for shape, kind in shapes
    ]
    vmem, hbm = (pl.BlockSpec(memory_space=pltpu.VMEM), pl.BlockSpec(memory_space=pl.ANY))
    smem = pl.BlockSpec(memory_space=pltpu.SMEM)
    flops = 2 * length * width * (4 * width + 2 * deep) + 40 * length * length * width
    kept = () if kept is None else tuple(kept)
    held = len(kept)
    sent, *kept = pl.pallas_call(
        functools.partial(backward_kernel, cell, held, grad_at, entry_at),
        out_shape=outs,
        in_specs=[smem] * 2 + [vmem if grad_at is None else hbm, hbm, vmem] + [hbm] * (7 + held),
        out_specs=[hbm] * 7,
        input_output_aliases={12 + number: 1 + number for number in range(held)},
        scratch_shapes=[
            pltpu.VMEM((4, width, width), LOW),
            pltpu.SemaphoreType.DMA((4,)),
            pltpu.SemaphoreType.DMA((5,)),
            pltpu.SemaphoreType.DMA((6 + ups,)),
        ]
        + [pltpu.VMEM(*shape) for shape in shapes]
        + [
            pltpu.VMEM((length, 3 * width), LOW),
            pltpu.VMEM((length, width), F32),
            pltpu.VMEM((length, deep), LOW),
            pltpu.VMEM((length, width), LOW),
            pltpu.VMEM((2, length, width), F32),
            pltpu.VMEM((length, width), F32),
            pltpu.VMEM((length, width), F32),
            pltpu.VMEM((length, width), LOW),
            pltpu.VMEM((length, width), LOW),
        ],
        compiler_params=pltpu.CompilerParams(vmem_limit_bytes=60 * 2**20),
        cost_estimate=pl.CostEstimate(
            flops=flops, bytes_accessed=2 * width * (4 * width + 2 * deep), transcendentals=0
        ),
    )(active, scale, grad, entry, rows, *saved, *weights, *kept)
    return (sent, kept)


def small_rows(small, rows, width, ups):
    devices, _, own = small.shape
    lane = lax.broadcasted_iota(jnp.int32, (own, width), 1)
    depth = lax.broadcasted_iota(jnp.int32, (own, width), 0)
    row = lax.broadcasted_iota(jnp.int32, (16, width), 0)
    across = lax.broadcasted_iota(jnp.int32, (16, width), 1)
    top = jnp.zeros((16, width), F32)
    for device in range(devices):
        spot = jnp.where(lane == depth + device * own, 1.0, 0.0).astype(LOW)
        top = top + dot(small[device], spot)
    rows[0:8, :] = top[0:8]
    share = devices // ups
    for block in range(ups):
        total = jnp.zeros((1, width), F32)
        for index in range(share):
            start = index * ups * own
            spot = jnp.zeros((own, width), F32)
            for up in range(ups):
                spot = spot + jnp.where(lane == depth + (start + up * own), 1.0, 0.0)
            low = start + (row - 8) * own
            inside = (row >= 8) & (row < 8 + ups) & (across >= low) & (across < low + own)
            placed = dot(small[block * share + index], spot.astype(LOW))
            total = total + jnp.sum(jnp.where(inside, placed, 0.0), axis=0, keepdims=True)
        rows[8 + block : 9 + block, :] = total


def gather_forward_kernel(chips, items, groups, cells, *refs):
    shards, inputs_h = (refs[:5], refs[5])
    outs, rows_h, arrived_h, later_h = (refs[6:11], refs[11], refs[12], refs[13])
    out_h, lowered_h, packed_h, mixed_h, middle_h, second_h, active_h, slope_h = refs[14:22]
    (ring_send, ring_recv, pair_send, pair_recv, own_sem, hop_send, hop_recv) = refs[22:29]
    (load_sem, save_sem, wide_sem, deep_sem) = refs[29:33]
    (small_v, rows_v, entry_v, out_v, lowered_v, packed_v, mixed_v, middle_v, second_v, active_v, slope_v) = refs[33:44]
    (total_v, hidden_v, wide_v, deep_v) = refs[44:]
    length, width = entry_v.shape[1:]
    ups = active_v.shape[2] // width
    half = chips // 2
    me, core, position, right, left, sibling = ring_place(chips)
    stage = lax.axis_index("pipe")
    first = stage == 0
    barrier = pltpu.get_barrier_semaphore()
    for device in (left, right, sibling):
        pl.semaphore_signal(barrier, inc=1, device_id={"dp": device}, device_id_type=MESH)
    pl.semaphore_signal(barrier, inc=1, device_id={"pipe": 1 - stage}, device_id_type=MESH)
    pl.semaphore_wait(barrier, 4)

    def shard(item):
        array, start, rows, _ = items[item]
        return shards[array].at[pl.ds(start, rows)]

    def out(item, block):
        array, start, rows, _ = items[item]
        return outs[array].at[block, pl.ds(start, rows)]

    def owner(step, way):
        return ring_chip(position - step if way == 0 else position + step, chips) * 2 + core

    def travels(item, way, step):
        return step < half or (step == half and items[item][3] == way)

    def ring_copy(item, way, step):
        block = owner(step - 1, way)
        return pltpu.make_async_remote_copy(
            src_ref=shard(item) if step == 1 else out(item, block),
            dst_ref=out(item, block),
            send_sem=ring_send.at[item, way, step - 1],
            recv_sem=ring_recv.at[item, way, step - 1],
            device_id={"dp": right if way == 0 else left},
            device_id_type=MESH,
        )

    def pair_copy(item, offset, block, source):
        return pltpu.make_async_remote_copy(
            src_ref=source,
            dst_ref=out(item, block),
            send_sem=pair_send.at[item, offset],
            recv_sem=pair_recv.at[item, offset],
            device_id={"dp": sibling},
            device_id_type=MESH,
        )

    def own_copy(item):
        return pltpu.make_async_copy(shard(item), out(item, me), own_sem.at[item])

    sent, paired = ([], [])

    def open_group(group):
        for item in group:
            for way in (0, 1):
                if travels(item, way, 1):
                    sent.append(ring_copy(item, way, 1))
                    sent[-1].start()
        for item in group:
            paired.append(pair_copy(item, 0, me, shard(item)))
            paired[-1].start()
            own_copy(item).start()

    def ring_step(item, way, step):
        ring_copy(item, way, step).wait_recv()
        if travels(item, way, step + 1):
            sent.append(ring_copy(item, way, step + 1))
            sent[-1].start()
        block = owner(step, way)
        offset = step if way == 0 else chips - step
        paired.append(pair_copy(item, offset, block, out(item, block)))
        paired[-1].start()

    def pair_arrived(item, offset):
        block = ring_chip(position - offset, chips) * 2 + core
        pair_copy(item, offset, block, out(item, block)).wait_recv()

    saves = []

    def save(source, target):
        number = len(saves)
        saves.append(lambda: pltpu.make_async_copy(source(), target(), save_sem.at[number]))
        saves[-1]().start()

    def entry_load(cell):
        return pltpu.make_async_copy(inputs_h.at[cell], entry_v.at[cell], load_sem.at[cell])

    def wide_load(array, column, slot):
        source = outs[array].at[:, :, pl.ds(column * width, width)]
        return pltpu.make_async_copy(source, wide_v.at[slot], wide_sem.at[slot])

    def wide(slot):
        return wide_v[slot].reshape(width, width)

    def gains(number):
        return rows_v[number : number + 1, :]

    def shifts(number):
        return rows_v[2 + number : 3 + number, :]

    def begin(cell):
        def step():
            entry_load(cell).wait()
            normed, _ = row_norm(entry_v[cell].astype(F32))
            lowered_v[cell] = (normed * gains(0) + shifts(0)).astype(LOW)
            save(lambda: lowered_v.at[cell], lambda: lowered_h.at[cell])

        return step

    def project(cell, number):
        def step():
            if cell == 0:
                wide_load(1, number, number).wait()
            part = dot(lowered_v[cell], wide(number))
            if number != 1:
                part = part + shifts(1 + number // 2)
            packed_v[cell, :, pl.ds(number * width, width)] = part.astype(LOW)
            if number == 2:
                save(lambda: packed_v.at[cell], lambda: packed_h.at[cell])

        return step

    def mix(cell, low, high, last):
        def step():
            attend(packed_v.at[cell], mixed_v.at[cell], width, low, high)
            if last:
                save(lambda: mixed_v.at[cell], lambda: mixed_h.at[cell])

        return step

    def join(cell):
        def step():
            if cell == 0:
                wide_load(2, 0, 3).wait()
            middle_v[cell] = entry_v[cell].astype(F32) + dot(mixed_v[cell], wide(3)) + shifts(3)
            save(lambda: middle_v.at[cell], lambda: middle_h.at[cell])

        return step

    def renorm(cell):
        def step():
            middle = middle_v[cell]
            normed, _ = row_norm(middle)
            second_v[cell] = (normed * gains(1) + shifts(4)).astype(LOW)
            total_v[cell] = middle + shifts(5)
            save(lambda: second_v.at[cell], lambda: second_h.at[cell])

        return step

    def rise(cell, number):
        def step():
            if cell == 0:
                wide_load(3, number, number).wait()
            hidden_v[...] = dot(second_v[cell], wide(number)) + rows_v[8 + number : 9 + number, :]

        return step

    def bend(cell, number):
        def step():
            window = pl.ds(number * width, width)
            activated, slope = gelu_parts(hidden_v[...])
            active_v[cell, :, window] = activated.astype(LOW)
            slope_v[cell, :, window] = slope.astype(LOW)
            if number == ups - 1:
                save(lambda: active_v.at[cell], lambda: active_h.at[cell])
                save(lambda: slope_v.at[cell], lambda: slope_h.at[cell])

        return step

    deep_rows = deep_v.shape[1] * deep_v.shape[2]

    def deep_load(offset, slot):
        chip = ring_chip(position - offset, chips)
        return pltpu.make_async_copy(outs[4].at[pl.ds(chip * 2, 2)], deep_v.at[slot], deep_sem.at[slot])

    def fall(cell, offset, slot):
        def step():
            if cell == 0:
                deep_load(offset, slot).wait()
            chip = ring_chip(position - offset, chips)
            window = pl.ds(pl.multiple_of(chip * deep_rows, 128), deep_rows)
            total_v[cell] += dot(active_v[cell, :, window], deep_v[slot].reshape(deep_rows, width))

        return step

    def hop():
        return pltpu.make_async_remote_copy(
            src_ref=out_v.at[0],
            dst_ref=arrived_h,
            send_sem=hop_send,
            recv_sem=hop_recv,
            device_id={"pipe": 1 - stage},
            device_id_type=MESH,
        )

    def finish(cell):
        def step():
            out_v[cell] = total_v[cell].astype(LOW)
            if cell == 0:
                hop().start()
            else:
                save(lambda: out_v.at[cell], lambda: later_h)
            save(lambda: out_v.at[cell], lambda: out_h.at[cell])

        return step

    def on_first(step):
        pl.when(first)(step)

    queue = []

    def ready(group, steps, loads):
        for item in group:
            own_copy(item).wait()
            for offset in range(chips):
                pair_arrived(item, offset)

        @pl.when(first)
        def _():
            for load in loads:
                load().start()

        queue.extend(steps)

    pairs = width // 128
    heads = []
    for cell in range(cells):
        heads.append(begin(cell))
        heads += [project(cell, number) for number in range(3)]
        heads += [mix(cell, low, low + 2, low + 2 >= pairs) for low in range(0, pairs, 2)]
    joins = [make(cell) for cell in range(cells) for make in (join, renorm)]
    def load_ups():
        for number in range(ups):
            wide_load(3, number, number).start()

    climbs = [load_ups]
    climbs += [make(cell, number) for number in range(ups) for cell in range(cells) for make in (rise, bend)]

    @pl.when(first)
    def _():
        for cell in range(cells):
            entry_load(cell).start()

    def lay_rows():
        copy = pltpu.make_async_copy(outs[0], small_v, load_sem.at[cells])
        copy.start()
        copy.wait()
        small_rows(small_v, rows_v, width, ups)
        pltpu.make_async_copy(rows_v, rows_h, load_sem.at[cells + 1]).start()

    def ready_small():
        for item in groups[0]:
            if items[item][0] == 0:
                own_copy(item).wait()
                for offset in range(chips):
                    pair_arrived(item, offset)
        lay_rows()

    plan = []
    for number, group in enumerate(groups):
        for step in range(1, half + 1):
            if step == half and number + 1 < len(groups):
                plan.append(("open", number + 1))
            for item in group:
                for way in (0, 1):
                    if travels(item, way, step):
                        plan.append(("ring", item, way, step))
            if number == len(groups) - 1:
                plan.append(("deep", step))
        plan.append(("done", number))
    open_group(groups[0])
    late = []
    slots = [0]

    def deep_ready(offsets):
        for offset in offsets:
            for item in groups[-1]:
                if offset == 0:
                    own_copy(item).wait()
                pair_arrived(item, offset)
            slot = slots[0] % deep_v.shape[0]
            slots[0] += 1

            def opening(offset=offset, slot=slot):
                deep_load(offset, slot).start()

            queue.append(opening)
            queue.extend(fall(cell, offset, slot) for cell in range(cells))

    def serve(limit):
        for _ in range(limit):
            if queue:
                on_first(queue.pop(0))

    for entry in plan:
        if entry[0] == "open":
            open_group(groups[entry[1]])
        elif entry[0] == "ring":
            ring_step(*entry[1:])
            for wait in list(late):
                wait[0] -= 1
                if wait[0] == 0:
                    wait[1]()
                    late.remove(wait)
            serve(3 if entry[1] in groups[-1] else 2)
        elif entry[0] == "done":
            if entry[1] == 0:
                rest = [item for item in groups[0] if items[item][0] != 0]
                late.append([1, ready_small])
                late.append(
                    [
                        2,
                        lambda: ready(
                            rest,
                            heads + joins,
                            [functools.partial(wide_load, 1, number, number) for number in range(3)]
                            + [functools.partial(wide_load, 2, 0, 3)],
                        ),
                    ]
                )
            elif entry[1] == 1:
                late.append([2, lambda: ready(groups[1], climbs, [])])
        elif entry[0] == "deep":
            step = entry[1]
            if step == 1:
                late.append([3, lambda: deep_ready([0])])
            if step < half:
                late.append([2, lambda step=step: deep_ready([step, chips - step])])
            else:
                for wait in late:
                    wait[1]()
                serve(len(queue))
                deep_ready([half])
    serve(len(queue))
    for cell in range(cells):
        on_first(finish(cell))
    for copy in sent:
        copy.wait_send()
    for copy in paired:
        copy.wait_send()
    pltpu.make_async_copy(rows_v, rows_h, load_sem.at[cells + 1]).wait()

    @pl.when(first)
    def _():
        for copy in saves:
            copy().wait()
        hop().wait_send()

    @pl.when(jnp.logical_not(first))
    def _():
        hop().wait_recv()


def gather_forward(shards, inputs, items, groups, count):
    chips = count // 2
    cells, length, width = inputs.shape
    deep = shards[3].shape[1]
    ups = deep // width
    pieces = len(items)
    shapes = kept_shapes(length, width, deep)
    hbm = pl.BlockSpec(memory_space=pl.ANY)
    flops = 2 * cells * length * width * (4 * width + 2 * deep)
    outs = pl.pallas_call(
        functools.partial(gather_forward_kernel, chips, items, groups, cells),
        out_shape=[jax.ShapeDtypeStruct((count,) + shard.shape, shard.dtype) for shard in shards]
        + [
            jax.ShapeDtypeStruct((16, width), F32),
            jax.ShapeDtypeStruct((length, width), LOW),
            jax.ShapeDtypeStruct((length, width), LOW),
        ]
        + [jax.ShapeDtypeStruct((cells,) + shape, kind) for shape, kind in shapes],
        in_specs=[hbm] * 6,
        out_specs=[hbm] * 16,
        scratch_shapes=[
            pltpu.SemaphoreType.DMA((pieces, 2, chips // 2)),
            pltpu.SemaphoreType.DMA((pieces, 2, chips // 2)),
            pltpu.SemaphoreType.DMA((pieces, chips)),
            pltpu.SemaphoreType.DMA((pieces, chips)),
            pltpu.SemaphoreType.DMA((pieces,)),
            pltpu.SemaphoreType.DMA,
            pltpu.SemaphoreType.DMA,
            pltpu.SemaphoreType.DMA((cells + 2,)),
            pltpu.SemaphoreType.DMA((9 * cells,)),
            pltpu.SemaphoreType.DMA((4,)),
            pltpu.SemaphoreType.DMA((2,)),
            pltpu.VMEM((count,) + shards[0].shape, LOW),
            pltpu.VMEM((16, width), F32),
            pltpu.VMEM((cells, length, width), LOW),
        ]
        + [pltpu.VMEM((cells,) + shape, kind) for shape, kind in shapes]
        + [
            pltpu.VMEM((cells, length, width), F32),
            pltpu.VMEM((length, width), F32),
            pltpu.VMEM((4, count, width // count, width), LOW),
            pltpu.VMEM((2, 2, shards[4].shape[0], width), LOW),
        ],
        compiler_params=pltpu.CompilerParams(
            collective_id=3, has_side_effects=True, vmem_limit_bytes=62 * 2**20
        ),
        cost_estimate=pl.CostEstimate(flops=flops, bytes_accessed=8 * width * (4 * width + 2 * deep), transcendentals=0),
    )(*shards, inputs)
    return (outs[:5], outs[5], outs[6], outs[7], list(outs[8:]))


class RingSum:
    def __init__(self, chips, items, parts, outs, landed, paired, buffers, final, sems):
        self.chips, self.items, self.parts, self.outs = (chips, items, parts, outs)
        self.landed, self.paired, self.final = (landed, paired, final)
        self.mine, self.pairs, self.rings = buffers
        self.ring_send, self.ring_recv, self.pair_send, self.pair_recv, self.load_sem, self.final_sem = sems
        self.half = chips // 2
        self.me, self.core, self.position, self.right, self.left, self.sibling = ring_place(chips)
        self.sent, self.final_copies, self.exchanged = ({}, [], [])
        self.uses = [0] * len(items)

    def part(self, item, block):
        array, start, rows, _ = self.items[item]
        return self.parts[array].at[block, pl.ds(start, rows)]

    def first(self, item, way):
        return 1 if self.items[item][3] == way else 2

    def slot_of(self, item, way, step):
        return step - 1 if self.items[item][3] == way else self.half + step - 2

    def offset_of(self, step, way):
        return self.half - step + 1 if way == 0 else self.chips - (self.half - step + 1)

    def pair_copy(self, item, offset):
        block = ring_chip(self.position + offset, self.chips) * 2 + 1 - self.core
        return pltpu.make_async_remote_copy(
            src_ref=self.part(item, block),
            dst_ref=self.paired[item].at[offset],
            send_sem=self.pair_send.at[item, offset],
            recv_sem=self.pair_recv.at[item, offset],
            device_id={"dp": self.sibling},
            device_id_type=MESH,
        )

    def ring_copy(self, item, way, step, buffer=0):
        here = self.slot_of(item, way, step)
        return pltpu.make_async_remote_copy(
            src_ref=self.mine[item].at[buffer],
            dst_ref=self.landed[item].at[here],
            send_sem=self.ring_send.at[item, here],
            recv_sem=self.ring_recv.at[item, here],
            device_id={"dp": self.right if way == 0 else self.left},
            device_id_type=MESH,
        )

    def load_mine(self, item, offset, buffer):
        block = ring_chip(self.position + offset, self.chips) * 2 + self.core
        return pltpu.make_async_copy(self.part(item, block), self.mine[item].at[buffer], self.load_sem.at[item, buffer])

    def load_pair(self, item, offset, buffer):
        return pltpu.make_async_copy(
            self.paired[item].at[offset], self.pairs[item].at[buffer], self.load_sem.at[item, 2 + buffer]
        )

    def load_ring(self, item, way, step, buffer):
        return pltpu.make_async_copy(
            self.landed[item].at[self.slot_of(item, way, step)], self.rings[item].at[buffer], self.load_sem.at[item, 4 + buffer]
        )

    def starts(self, wanted):
        return [
            (step, item, way, self.offset_of(step, way))
            for step in (1, 2)
            for item in wanted
            for way in (0, 1)
            if step == self.first(item, way)
        ]

    def rest(self, wanted, steps):
        return [
            (step, item, way, self.offset_of(step, way))
            for step in steps
            if step <= self.half
            for item in wanted
            for way in (0, 1)
            if step > self.first(item, way)
        ] + [(step, item, None, 0) for step in steps if step > self.half for item in wanted]

    def fetch(self, entry):
        step, item, way, offset, buffer = entry
        if (item, buffer) in self.sent:
            self.sent.pop((item, buffer)).wait_send()
        self.load_mine(item, offset, buffer).start()
        self.pair_copy(item, offset).wait_recv()
        self.load_pair(item, offset, buffer).start()

    def bytes_of(self, item):
        array, _, rows, _ = self.items[item]
        return rows * self.parts[array].shape[2] * self.parts[array].dtype.itemsize

    def arrange(self, steps, ends):
        waiting = self.starts(range(len(self.items)))
        waiting += self.rest(range(len(self.items)), range(2, self.half + 2))
        opened, arrival, sends, used = ({}, {}, {}, [0] * len(self.items))
        clock, link, order, steps = (0.0, [0.0, 0.0], [], list(steps))

        def ready_at(entry):
            step, item, way, offset = entry
            if (item, offset) not in opened:
                return None
            when = opened[(item, offset)]
            sides = (0, 1) if way is None else ((way,) if step > self.first(item, way) else ())
            for side in sides:
                if (item, side, step - 1) not in arrival:
                    return None
                when = max(when, arrival[(item, side, step - 1)])
            return max(when, sends.get((item, used[item] - 2), 0.0))

        while waiting or steps:
            best = None
            for entry in waiting:
                when = ready_at(entry)
                if when is None or (entry[2] is None and (steps or any(other[2] is not None for other in waiting if ready_at(other) is not None and ready_at(other) <= clock))):
                    continue
                backlog = 0.0 if entry[2] is None else max(0.0, link[entry[2]] - max(clock, when))
                rank = (max(when, clock) + 0.5 * backlog, entry[0])
                if best is None or rank < best[0]:
                    best = (rank, entry, when)
            far_off = best is None or best[2] > clock + 0.3
            idle = best is not None and best[1][2] is not None and link[best[1][2]] > clock + ends
            if steps and (far_off or idle):
                spent, step, opens = steps.pop(0)
                clock += spent
                for item, offset in opens:
                    opened[(item, offset)] = clock + 2.0 + self.bytes_of(item) / 2e5
                order.append((step, opens))
                continue
            _, entry, when = best
            waiting.remove(entry)
            step, item, way, offset = entry
            clock = max(clock, when) + 0.8 + self.bytes_of(item) * 1.6e-6
            if way is not None:
                link[way] = max(clock, link[way]) + 2 * self.bytes_of(item) / 9.1e4
                arrival[(item, way, step)] = link[way] + 1.5
                sends[(item, used[item])] = link[way]
            order.append(entry + (used[item] % 2,))
            used[item] += 1
        return order, clock

    def follow(self, order):
        entries = [number for number, action in enumerate(order) if len(action) == 5]
        fetched = set()
        for number, action in enumerate(order):
            if len(action) == 2:
                step, opens = action
                step()
                for item, offset in opens:
                    self.pair_copy(item, offset).start()
                    self.exchanged.append((item, offset))
                continue
            if number not in fetched:
                self.fetch(action)
                fetched.add(number)
            if number + 1 in entries:
                following = order[number + 1]
                if following[1] != action[1]:
                    self.fetch(following)
                    fetched.add(number + 1)
            self.work(action)

    def work(self, entry):
        step, item, way, offset, buffer = entry
        array, start, rows, _ = self.items[item]
        half, final = (self.half, self.final)
        kind = self.parts[array].dtype
        columns = self.parts[array].shape[2]
        chunk = 16
        mine, pairs, rings = (self.mine[item], self.pairs[item], self.rings[item])
        if way is None:
            for side in (0, 1):
                self.ring_copy(item, side, half).wait_recv()
                self.load_ring(item, side, half, side).start()
            self.load_mine(item, offset, buffer).wait()
            self.load_pair(item, offset, buffer).wait()
            for side in (0, 1):
                self.load_ring(item, side, half, side).wait()
            if kind == F32:
                total = (rings[0] + rings[1]) + (mine[buffer] + pairs[buffer])
                gains, shifts, bias = self.outs[array]
                gains[...] = total[0:2]
                for row in range(6):
                    shifts[row] = total[2 + row : 3 + row]
                ups = bias.shape[1] // total.shape[1]
                bias[...] = jnp.concatenate([total[8 + up : 9 + up] for up in range(ups)], axis=1)
                return
            high, wide = (min(rows, final.shape[1]), min(columns, final.shape[2]))
            for top in range(0, rows, high):
                for across in range(0, columns, wide):
                    number = len(self.final_copies)
                    turn = number % final.shape[0]
                    if number >= final.shape[0]:
                        self.final_copies[number - final.shape[0]].wait()
                    span = pl.ds(across, wide)

                    @pl.loop(0, high // chunk)
                    def _(index):
                        here = pl.ds(pl.multiple_of(top + index * chunk, chunk), chunk)
                        final[turn, pl.ds(pl.multiple_of(index * chunk, chunk), chunk), pl.ds(0, wide)] = (
                            rings[0, here, span].astype(F32) + rings[1, here, span].astype(F32)
                        ) + (mine[buffer, here, span].astype(F32) + pairs[buffer, here, span].astype(F32))

                    self.final_copies.append(
                        pltpu.make_async_copy(
                            final.at[turn, pl.ds(0, high), pl.ds(0, wide)],
                            self.outs[array].at[pl.ds(start + top, high), span],
                            self.final_sem.at[turn],
                        )
                    )
                    self.final_copies[-1].start()
            return
        carried = step > self.first(item, way)
        if carried:
            self.ring_copy(item, way, step - 1).wait_recv()
            self.load_ring(item, way, step - 1, buffer).start()
        self.load_mine(item, offset, buffer).wait()
        self.load_pair(item, offset, buffer).wait()
        if carried:
            self.load_ring(item, way, step - 1, buffer).wait()

        @pl.loop(0, rows // chunk)
        def _(index):
            here = pl.ds(pl.multiple_of(index * chunk, chunk), chunk)
            total = mine[buffer, here, :].astype(F32) + pairs[buffer, here, :].astype(F32)
            if carried:
                total = rings[buffer, here, :].astype(F32) + total
            mine[buffer, here, :] = total.astype(kind)

        copy = self.ring_copy(item, way, step, buffer)
        copy.start()
        self.sent[(item, buffer)] = copy

    def close(self):
        for copy in self.sent.values():
            copy.wait_send()
        for item, offset in self.exchanged:
            self.pair_copy(item, offset).wait_send()
        for copy in self.final_copies[-self.final.shape[0] :]:
            copy.wait()


class Products:
    def __init__(self, chips, width, own, cuts, big, stage, cut_sem, big_sem, stage_sem):
        self.chips, self.width, self.own = (chips, width, own)
        self.cuts, self.big, self.stage = (cuts, big, stage)
        self.cut_sem, self.big_sem, self.stage_sem = (cut_sem, big_sem, stage_sem)

    def load_cut(self, source, index, slot):
        cut = self.cuts.shape[2]
        window = pl.ds(pl.multiple_of(index * cut, cut), cut)
        return pltpu.make_async_copy(source.at[:, window], self.cuts.at[slot], self.cut_sem.at[slot])

    def block(self, source, index, slot):
        window = pl.ds(pl.multiple_of(index * self.width, self.width), self.width)
        return pltpu.make_async_copy(source.at[:, window], self.big.at[slot], self.big_sem.at[slot])

    def keep(self, target, index):
        window = pl.ds(index // 2 * self.width, self.width)
        return pltpu.make_async_copy(
            self.stage.at[index % 2],
            target.at[pl.ds(index % 2 * self.chips, self.chips), :, window],
            self.stage_sem.at[index % 2],
        )

    def open(self, left, right, slot):
        for index in (0, 1):
            self.load_cut(left, index, index).start()
        self.block(right, 0, slot).start()

    def run(self, target, left, right, shift, index):
        number = 2 * (right.shape[1] // self.width)
        slot, here = (index % 2, (index // 2 + shift) % 2)
        if index == 0:
            for side in (0, 1):
                self.load_cut(left, side, side).wait()
        if slot == 0:
            self.block(right, index // 2, here).wait()
            if index + 2 < number:
                self.block(right, index // 2 + 1, 1 - here).start()
        if index >= 2:
            self.keep(target, index - 2).wait()
        product = dot_left(self.cuts[slot], self.big[here]).astype(LOW)
        for device in range(self.chips):
            self.stage[slot, device] = product[device * self.own : (device + 1) * self.own]
        self.keep(target, index).start()

    def close(self, target, right):
        number = 2 * (right.shape[1] // self.width)
        for index in (number - 2, number - 1):
            self.keep(target, index).wait()


def last_backward_kernel(chips, items, cell, *refs):
    count = len(items)
    (grad, entry_h, rows, packed_h, middle_h, slope_h, w_qkv, w_out, w_up, w_down) = refs[:10]
    (activated_h, grad_ff_h, second_h, mixed_h, lowered_h) = refs[10:15]
    refs = refs[15 + 5 :]
    rows_o, packed_o, branch_o, inner_o, sums_o = refs[:5]
    outs, parts = ([refs[5:8]] + list(refs[8:12]), refs[12:16])
    landed, paired = (refs[16 : 16 + count], refs[16 + count : 16 + 2 * count])
    refs = refs[16 + 2 * count :]
    ring_buffers = (refs[:count], refs[count : 2 * count], refs[2 * count : 3 * count])
    final, small_v, both_v = refs[3 * count : 3 * count + 3]
    sems = refs[3 * count + 3 : 3 * count + 9]
    refs = refs[3 * count + 9 :]
    (big, cuts, stage, stage_down, big_sem, cut_sem, stage_sem) = refs[:7]
    (buffers, buffer_sems, load_sems, save_sems, slope_sems, inner_sems) = refs[7:13]
    (entry, packed_v, middle_v, slope_v, inner_v, grad_packed_v, mixed_v, branch_v, grad_act_v, total_v, sums_v) = refs[13:]
    parts = [small_v] + list(parts)
    down_part, up_part = (parts[4], parts[3])
    length, width = grad.shape
    devices = 2 * chips
    deep_own = down_part.shape[1]
    ups = w_up.shape[1] // width
    first = lax.axis_index("pipe") == 0
    ring = RingSum(chips, items, parts, outs, landed, paired, ring_buffers, final, sems)
    half, position = (ring.half, ring.position)
    products = Products(chips, width, width // devices, cuts, big, stage, cut_sem, big_sem, stage_sem)
    gains = rows.at[0:2]

    def farthest_first(index):
        step = index // 2
        return ring_chip(position + (half - step if index % 2 == 0 else half + step + 1), chips)

    def keep_down(index):
        return pltpu.make_async_copy(
            stage_down.at[index % 2],
            down_part.at[pl.ds(farthest_first(index) * 2, 2)],
            stage_sem.at[2 + index % 2],
        )

    def cut_down(index):
        return products.load_cut(activated_h, farthest_first(index), index % 2)

    def down_product(index):
        def step():
            slot = index % 2
            if index == 0:
                for at in range(cell + 1):
                    ff_load(at).wait()
            if index + 1 < chips:
                cut_down(index + 1).start()
            cut_down(index).wait()
            product = dot_left(cuts[slot], big[0]).astype(LOW)
            for side in (0, 1):
                stage_down[slot, side] = product[side * deep_own : (side + 1) * deep_own]
            keep_down(index).start()
            if index > 0:
                keep_down(index - 1).wait()

        return step

    def last_down():
        keep_down(chips - 1).wait()

    def far_offset(index):
        return (half - index // 2 if index % 2 == 0 else half + index // 2 + 1) % chips

    def here(ref, at):
        return ref.at[pl.ds(at * length, length)]

    def ff_load(at):
        return pltpu.make_async_copy(here(grad_ff_h, at), here(big.at[0], at), load_sems.at[at])

    def ff_arrived():
        return pltpu.make_async_copy(grad, here(big.at[0], cell), load_sems.at[cell])

    for at in range(cell):
        ff_load(at).start()
    pl.when(first)(lambda: ff_arrived().start())
    pl.when(jnp.logical_not(first))(lambda: ff_load(cell).start())
    cut_down(0).start()

    def own_load(number):
        source, target = ((entry_h, entry), (middle_h, middle_v), (packed_h, packed_v))[number - 1]
        return pltpu.make_async_copy(source.at[cell], target, load_sems.at[cell + 1 + number])

    def slope_load(number):
        window = pl.ds(number * width, width)
        return pltpu.make_async_copy(
            slope_h.at[cell].at[:, window], slope_v.at[number % 2], slope_sems.at[number % 2]
        )

    order, place_up, place_down = ([], {}, {})
    for number in range(ups + 1):
        if number < ups:
            place_down[number] = len(order)
            order.append((w_down, 0, number))
        if number > 0:
            place_up[number - 1] = len(order)
            order.append((w_up, 1, number - 1))
    place_out = len(order)
    order = order + [(w_out, 0, 0)] + [(w_qkv, 1, number) for number in range(3)]
    depth = buffers.shape[0]

    def weight_load(number):
        ref, axis, at = order[number]
        window = pl.ds(at * width, width)
        source = ref.at[:, window] if axis else ref.at[window, :]
        return pltpu.make_async_copy(source, buffers.at[number % depth], buffer_sems.at[number % depth])

    def take(number):
        weight_load(number).wait()
        return buffers.at[number % depth]

    def release(number):
        if number + depth < len(order):
            weight_load(number + depth).start()

    def save(number, wait=False):
        source, target = (
            (branch_v, branch_o.at[pl.ds(cell * length, length)]),
            (grad_packed_v, packed_o.at[pl.ds(cell * length, length)]),
            (sums_v, sums_o.at[cell]),
            (mixed_v, rows_o.at[cell]),
        )[number]
        copy = pltpu.make_async_copy(source, target, save_sems.at[number])
        copy.wait() if wait else copy.start()

    def inner_save(number):
        window = pl.ds(number * width, width)
        return pltpu.make_async_copy(
            inner_v.at[number % 2], inner_o.at[pl.ds(cell * length, length), window], inner_sems.at[number % 2]
        )

    def column_sum(array):
        return jnp.sum(array.astype(F32), axis=0, keepdims=True)

    def begin():
        slope_load(0).start()
        for number in range(depth):
            weight_load(number).start()
        for number in (1, 2, 3):
            own_load(number).start()
        sums_v[7:8, :] = column_sum(grad[...])

    def climb(number):
        def step():
            if number < ups:
                down_block = take(place_down[number])
                grad_act_v[number % 2] = dot_right(grad[...], down_block[...])
                release(place_down[number])
            if number > 0:
                at = number - 1
                slope_load(at).wait()
                if at + 1 < ups:
                    slope_load(at + 1).start()
                up_block = take(place_up[at])
                if at >= 2:
                    inner_save(at - 2).wait()
                inner = (grad_act_v[at % 2] * slope_v[at % 2].astype(F32)).astype(LOW)
                inner_v[at % 2] = inner
                sums_v[8 + at : 9 + at, :] = column_sum(inner)
                part = dot_right(inner, up_block[...])
                if at == 0:
                    total_v[...] = part
                else:
                    total_v[...] += part
                inner_save(at).start()
                release(place_up[at])

        return step

    def turn():
        own_load(2).wait()
        normed, inverse = row_norm(middle_v[...])
        grad_second = total_v[...]
        sums_v[1:2, :] = column_sum(grad_second * normed)
        sums_v[6:7, :] = column_sum(grad_second)
        grad_middle = grad[...].astype(F32) + norm_back(grad_second * gains[1:2, :], normed, inverse)
        middle_v[...] = grad_middle
        branch_v[...] = grad_middle.astype(LOW)
        sums_v[5:6, :] = column_sum(branch_v[...])
        save(0)
        save(0, wait=True)
        for at in range(max(0, ups - 2), ups):
            inner_save(at).wait()

    def outer():
        block = take(place_out)
        mixed_v[...] = dot_right(branch_v[...], block[...]).astype(LOW)
        release(place_out)
        own_load(3).wait()

    def heads(low, high):
        def step():
            attend_back(packed_v, mixed_v, grad_packed_v, width, low, high)

        return step

    def sums():
        save(1)
        sums_v[3:4, :] = column_sum(grad_packed_v[:, pl.ds(0, width)])
        sums_v[4:5, :] = column_sum(grad_packed_v[:, pl.ds(2 * width, width)])
        save(1, wait=True)

    def lower(number):
        def step():
            block = take(place_out + 1 + number)
            part = dot_right(grad_packed_v[:, pl.ds(number * width, width)], block[...])
            if number == 0:
                total_v[...] = part
            else:
                total_v[...] += part
            release(place_out + 1 + number)

        return step

    def finish():
        own_load(1).wait()
        normed, inverse = row_norm(entry[...].astype(F32))
        grad_lowered = total_v[...]
        sums_v[0:1, :] = column_sum(grad_lowered * normed)
        sums_v[2:3, :] = column_sum(grad_lowered)
        mixed_v[...] = (middle_v[...] + norm_back(grad_lowered * gains[0:1, :], normed, inverse)).astype(LOW)
        save(2)
        save(3)

    def lay_small():
        @pl.when(first)
        def _():
            save(2, wait=True)

        copy = pltpu.make_async_copy(sums_o, both_v, load_sems.at[0])
        copy.start()
        copy.wait()
        sums = both_v[0]
        for at in range(1, cell + 1):
            sums = sums + both_v[at]
        own = width // devices
        windows = [pltpu.roll(sums, (width - at * own) % width, 1)[:, :own] for at in range(devices)]
        share = devices // ups
        for device in range(devices):
            small_v[device, 0:8, :] = windows[device][0:8]
            for up in range(ups):
                row = 8 + device // share
                small_v[device, 8 + up : 9 + up, :] = windows[device % share * ups + up][row : row + 1]
            small_v[device, 8 + ups : 16, :] = jnp.zeros((8 - ups, own), F32)

    pairs = width // 128
    downs = [item for item in range(count) if items[item][0] == 4]
    up_items = [item for item in range(count) if items[item][0] == 3]
    outers = [item for item in range(count) if items[item][0] == 2]
    head_items = [item for item in range(count) if items[item][0] == 1]
    smalls = [item for item in range(count) if items[item][0] == 0]
    everywhere = [far_offset(index) for index in range(chips)]

    def only_first(step):
        return lambda: pl.when(first)(step)

    def product(target, left, right, shift, index):
        def step():
            products.run(target, left, right, shift, index)
            if index + 1 == 2 * (right.shape[1] // width):
                products.close(target, right)

        return step

    def all_of(wanted, offsets):
        return [(item, offset) for offset in offsets for item in wanted]

    def opening(left, right, shift):
        return lambda: products.open(left, right, shift)

    def blocks(target, left, right, shift, wanted):
        number = 2 * (right.shape[1] // width)
        made = [(0.3, opening(left, right, shift), [])]
        for index in range(number):
            opens = all_of(wanted, everywhere) if index + 1 == number else []
            made.append((1.9, product(target, left, right, shift, index), opens))
        return made

    steps = []
    for index in range(chips):
        steps.append((1.9, down_product(index), all_of(downs, [far_offset(index - 1)] if index else [])))
        if index == 3:
            steps.append((0.3, only_first(begin), []))
    steps.append((0.7, last_down, all_of(downs, [far_offset(chips - 1)])))
    steps += [(2.0 if number in (0, ups) else 3.5, only_first(climb(number)), []) for number in range(ups + 1)]
    steps.append((3.0, only_first(turn), []))
    steps += blocks(up_part, second_h, inner_o, 1, up_items)
    steps += blocks(parts[2], mixed_h, branch_o, 1, outers)
    steps.append((1.7, only_first(outer), []))
    steps += [(2.5, only_first(heads(low, low + 2)), []) for low in range(0, pairs, 2)]
    steps.append((0.8, only_first(sums), []))
    steps += blocks(parts[1], lowered_h, packed_o, 0, head_items)
    steps += [(1.8, only_first(lower(number)), []) for number in range(3)]
    steps.append((3.0, only_first(finish), []))
    steps.append((2.0, lay_small, all_of(smalls, everywhere)))
    greet((ring.left, ring.right, ring.sibling))
    schedule, _ = ring.arrange(steps, 8.0)
    ring.follow(schedule)
    ring.close()

    @pl.when(first)
    def _():
        save(3, wait=True)


def last_backward(arrived, entry, rows, saved, weights, kept, sides, items, shapes, count):
    chips = count // 2
    length, width = arrived.shape
    deep = weights[2].shape[1]
    cells = kept[0].shape[0]
    rows_in = cells * length
    own = width // count
    vmem, hbm = (pl.BlockSpec(memory_space=pltpu.VMEM), pl.BlockSpec(memory_space=pl.ANY))
    cut = width // 2
    wholes = [(16, own)] + [tuple(shape) for shape in shapes]
    held = [(many,) + wholes[array][1:] for array, _, many, _ in items]
    kinds = [F32 if array == 0 else LOW for array, _, _, _ in items]
    pieces = len(items)
    flops = 2 * length * width * (4 * width + 2 * deep) + 2 * rows_in * width * (4 * width + 2 * deep)
    outs = pl.pallas_call(
        functools.partial(last_backward_kernel, chips, items, cells - 1),
        out_shape=[jax.ShapeDtypeStruct(array.shape, array.dtype) for array in kept]
        + [jax.ShapeDtypeStruct(shape, F32) for shape in ((2, own), (6, 1, own), (1, deep // count))]
        + [jax.ShapeDtypeStruct(shape, F32) for shape in wholes[1:]]
        + [jax.ShapeDtypeStruct((count,) + shape, LOW) for shape in wholes[1:]]
        + [jax.ShapeDtypeStruct((chips - 1,) + shape, kind) for shape, kind in zip(held, kinds)]
        + [jax.ShapeDtypeStruct((chips,) + shape, kind) for shape, kind in zip(held, kinds)],
        in_specs=[vmem, hbm, vmem] + [hbm] * 17,
        out_specs=[hbm] * 5 + [vmem] * 3 + [hbm] * (8 + 2 * pieces),
        input_output_aliases={15 + number: number for number in range(5)},
        scratch_shapes=[pltpu.VMEM((2,) + shape, kind) for shape, kind in zip(held, kinds)] * 3
        + [
            pltpu.VMEM((4, 80, width), F32),
            pltpu.VMEM((count, 16, own), F32),
            pltpu.VMEM((cells, 16, width), F32),
            pltpu.SemaphoreType.DMA((pieces, chips - 1)),
            pltpu.SemaphoreType.DMA((pieces, chips - 1)),
            pltpu.SemaphoreType.DMA((pieces, chips)),
            pltpu.SemaphoreType.DMA((pieces, chips)),
            pltpu.SemaphoreType.DMA((pieces, 6)),
            pltpu.SemaphoreType.DMA((4,)),
            pltpu.VMEM((2, rows_in, width), LOW),
            pltpu.VMEM((2, rows_in, cut), LOW),
            pltpu.VMEM((2, chips, own, width), LOW),
            pltpu.VMEM((2, 2, shapes[3][0], width), LOW),
            pltpu.SemaphoreType.DMA((2,)),
            pltpu.SemaphoreType.DMA((2,)),
            pltpu.SemaphoreType.DMA((4,)),
            pltpu.VMEM((2, width, width), LOW),
            pltpu.SemaphoreType.DMA((2,)),
            pltpu.SemaphoreType.DMA((cells + 4,)),
            pltpu.SemaphoreType.DMA((4,)),
            pltpu.SemaphoreType.DMA((2,)),
            pltpu.SemaphoreType.DMA((2,)),
            pltpu.VMEM((length, width), LOW),
            pltpu.VMEM((length, 3 * width), LOW),
            pltpu.VMEM((length, width), F32),
            pltpu.VMEM((2, length, width), LOW),
            pltpu.VMEM((2, length, width), LOW),
            pltpu.VMEM((length, 3 * width), LOW),
            pltpu.VMEM((length, width), LOW),
            pltpu.VMEM((length, width), LOW),
            pltpu.VMEM((2, length, width), F32),
            pltpu.VMEM((length, width), F32),
            pltpu.VMEM((16, width), F32),
        ],
        compiler_params=pltpu.CompilerParams(
            collective_id=2, has_side_effects=True, vmem_limit_bytes=62 * 2**20
        ),
        cost_estimate=pl.CostEstimate(flops=flops, bytes_accessed=160 * width * width, transcendentals=0),
    )(arrived, entry, rows, *saved, *weights, *sides, *kept)
    return (list(outs[:5]), outs[5:8], outs[8:12])


def on_device(inputs, out_grad, query_counts, gains, shifts, w_qkv, w_out, w_up, b_up, w_down):
    stage = lax.axis_index("pipe")
    stages = lax.axis_size("pipe")
    count = lax.axis_size("dp")
    cell_count, length, width = inputs.shape
    own = width // count
    ups = b_up.shape[1] // own
    deep = ups * width
    deep_own = w_down.shape[1]
    shapes = [
        block_shape(own, 3 * width),
        block_shape(own, width),
        block_shape(own, deep),
        block_shape(deep_own, width),
    ]
    cut = (shapes[3][0] // 2 + 15) // 16 * 16
    items = (
        (0, 0, 16, 0),
        (1, 0, shapes[0][0], 0),
        (2, 0, shapes[1][0], 0),
        (3, 0, shapes[2][0], 1),
        (4, 0, cut, 0),
        (4, cut, shapes[3][0] - cut, 1),
    )
    shards = [small_pack(gains[0], shifts[0], b_up[0], 1)[0]] + [
        array[0].reshape(shape) for array, shape in zip((w_qkv, w_out, w_up, w_down), shapes)
    ]
    fused = stages == 2 and cell_count == 2 and own % 16 == 0 and width % 256 == 0 and 4 * deep_own == width
    if fused:
        piece = own // 2 // 16 * 16
        arrivals = (
            (0, 0, 16, 0),
            (1, 0, own - piece, 0),
            (1, own - piece, piece, 1),
            (2, 0, own, 1),
            (3, 0, own - piece, 0),
            (3, own - piece, piece, 1),
            (4, 0, cut, 0),
            (4, cut, deep_own - cut, 1),
        )
        packs, rows, arrived, later, kept = gather_forward(
            shards, inputs, arrivals, ((0, 1, 2, 3), (4, 5), (6, 7)), count
        )
    else:
        packs = gather(shards, items, count)
        gain_rows, shift_rows, bias = small_split(packs[0].astype(F32), ups)
        blank = jnp.zeros((8 - ups, width), F32)
        rows = jnp.concatenate([gain_rows, shift_rows, bias.reshape(ups, width), blank])
    weights = (
        packs[1].reshape(width, 3 * width),
        packs[2].reshape(width, width),
        packs[3].reshape(width, deep),
        packs[4].reshape(deep, width),
    )
    scales = jnp.sqrt(query_counts.astype(F32) / 500.0)

    def along(value, steps):
        pairs = [(source, source + steps) for source in range(stages) if 0 <= source + steps < stages]
        return lax.ppermute(value, "pipe", pairs)

    entries = [[(inputs, cell) for cell in range(cell_count)]]
    if fused:
        entries.append([(arrived, None), (along(later, 1), None)])
    else:
        kept = None
    for turn in range(1 if fused else 0, stages):
        active = (stage == turn).astype(jnp.int32)[None]
        arrived = []
        for cell in range(cell_count):
            sent, kept = forward_tick(active, entries[turn][cell], rows, weights, kept, cell, cell_count)
            if turn + 1 < stages:
                arrived.append((along(sent, 1), None))
        entries.append(arrived)
    section_out, lowered, packed, mixed, middle, second, activated, slope = kept
    incoming = [((out_grad, cell), scales[cell][None]) for cell in range(cell_count)]
    back = None
    for turn in range(stages - 1, -1, -1):
        active = (stage == turn).astype(jnp.int32)[None]
        arrived = []
        for cell in range(cell_count):
            if fused and turn == 0 and cell == cell_count - 1:
                continue
            sent, back = backward_tick(
                active, incoming[cell], entries[turn][cell], rows, (packed, middle, slope), weights, back, cell, cell_count
            )
            if turn > 0:
                arrived.append(((along(sent, -1), None), jnp.ones((1,), F32)))
        incoming = arrived if turn > 0 else incoming

    def flat(array):
        return array.reshape(cell_count * length, -1)

    input_grads, grad_packed, grad_branch, grad_inner, grad_ff, sums = back
    if fused:
        (input_grads, _, _, _, _), (grad_gains, grad_shifts, grad_bias), shares = last_backward(
            incoming[-1][0][0],
            inputs,
            rows,
            (packed, middle, slope),
            weights,
            (input_grads, flat(grad_packed), flat(grad_branch), flat(grad_inner), sums),
            [flat(array) for array in (activated, grad_ff, second, mixed, lowered)],
            arrivals,
            shapes,
            count,
        )
    else:
        sums = jnp.sum(sums, axis=0)
        small_part = small_pack(sums[0:2], sums[2:8], sums[8 : 8 + ups].reshape(deep), count)
        sides = [flat(array) for array in (lowered, grad_packed, mixed, grad_branch, second, grad_inner, activated, grad_ff)]
        products = [dot_left(sides[at], sides[at + 1]).astype(LOW) for at in (0, 2, 4, 6)]
        parts = [small_part] + [whole.reshape((count,) + shape) for whole, shape in zip(products, shapes)]
        small_share, *shares = scatter(parts, items, count)
        grad_gains, grad_shifts, grad_bias = small_split(small_share[None], ups)
        grad_shifts = grad_shifts[:, None]
    return (
        section_out[None],
        input_grads[None],
        grad_gains[None],
        grad_shifts.swapaxes(0, 1),
        shares[0].reshape(1, own, 3 * width),
        shares[1].reshape(1, own, width),
        shares[2].reshape(1, own, deep),
        grad_bias.reshape(1, ups * own),
        shares[3].reshape(1, deep_own, width),
    )


def solution(mesh):
    in_specs = (
        P("dp", None, None),
        P("dp", None, None),
        P("dp"),
        P("pipe", None, "dp"),
        P("pipe", None, "dp"),
        P("pipe", "dp", None),
        P("pipe", "dp", None),
        P("pipe", "dp", None),
        P("pipe", "dp"),
        P("pipe", "dp", None),
    )
    out_specs = (
        P("pipe", "dp", None, None),
        P("pipe", "dp", None, None),
        P("pipe", None, "dp"),
        P("pipe", None, "dp"),
        P("pipe", "dp", None),
        P("pipe", "dp", None),
        P("pipe", "dp", None),
        P("pipe", "dp"),
        P("pipe", "dp", None),
    )
    return jax.shard_map(
        on_device, mesh=mesh, in_specs=in_specs, out_specs=out_specs, check_vma=False
    )
```

```python
import functools
import math

import jax
import jax.numpy as jnp
from jax import lax
from jax.experimental import pallas as pl
from jax.experimental.pallas import tpu as pltpu
from jax.sharding import PartitionSpec as P

HEAD_DIM = 64
MESH = pl.DeviceIdType.MESH
LOW = jnp.bfloat16
F32 = jnp.float32


def ring_chip(position, chips):
    position = lax.rem(position + 2 * chips, chips)
    half = chips // 2
    return jnp.where(position < half, 2 * position, 2 * (chips - 1 - position) + 1)


def ring_place(chips):
    me = lax.axis_index("dp")
    core = lax.rem(me, 2)
    chip = me // 2
    position = jnp.where(lax.rem(chip, 2) == 0, chip // 2, chips - 1 - chip // 2)
    right = ring_chip(position + 1, chips) * 2 + core
    left = ring_chip(position - 1, chips) * 2 + core
    return (me, core, position, right, left, me + 1 - 2 * core)


def greet(devices):
    barrier = pltpu.get_barrier_semaphore()
    for device in devices:
        pl.semaphore_signal(barrier, inc=1, device_id={"dp": device}, device_id_type=MESH)
    pl.semaphore_wait(barrier, len(devices))


def gather_kernel(chips, arrays, items, *refs):
    count = len(items)
    ring_send, ring_recv, pair_send, pair_recv, own_sem = refs[2 * arrays :]
    shards = [refs[array].at[pl.ds(start, rows)] for array, start, rows, _ in items]
    splits = [way for _, _, _, way in items]
    half = chips // 2
    me, core, position, right, left, sibling = ring_place(chips)
    greet((left, right, sibling))

    def out(item, block):
        array, start, rows, _ = items[item]
        return refs[arrays + array].at[block, pl.ds(start, rows)]

    def owner(step, way):
        return ring_chip(position - step if way == 0 else position + step, chips) * 2 + core

    def travels(item, way, step):
        return step < half or (step == half and splits[item] == way)

    def ring_copy(item, way, step):
        block = owner(step - 1, way)
        return pltpu.make_async_remote_copy(
            src_ref=shards[item] if step == 1 else out(item, block),
            dst_ref=out(item, block),
            send_sem=ring_send.at[item, way, step - 1],
            recv_sem=ring_recv.at[item, way, step - 1],
            device_id={"dp": right if way == 0 else left},
            device_id_type=MESH,
        )

    def pair_copy(item, offset, block, source):
        return pltpu.make_async_remote_copy(
            src_ref=source,
            dst_ref=out(item, block),
            send_sem=pair_send.at[item, offset],
            recv_sem=pair_recv.at[item, offset],
            device_id={"dp": sibling},
            device_id_type=MESH,
        )

    sent, paired, kept = ([], [], [])
    for item in range(count):
        for way in (0, 1):
            if travels(item, way, 1):
                sent.append(ring_copy(item, way, 1))
                sent[-1].start()
    for item in range(count):
        paired.append(pair_copy(item, 0, me, shards[item]))
        paired[-1].start()
        kept.append(pltpu.make_async_copy(shards[item], out(item, me), own_sem.at[item]))
        kept[-1].start()
    for step in range(1, half + 1):
        for item in range(count):
            for way in (0, 1):
                if not travels(item, way, step):
                    continue
                ring_copy(item, way, step).wait_recv()
                if travels(item, way, step + 1):
                    sent.append(ring_copy(item, way, step + 1))
                    sent[-1].start()
                block = owner(step, way)
                offset = step if way == 0 else chips - step
                paired.append(pair_copy(item, offset, block, out(item, block)))
                paired[-1].start()
    for copy in sent:
        copy.wait_send()
    for copy in paired:
        copy.wait()
    for copy in kept:
        copy.wait()


def gather(shards, items, count):
    chips = count // 2
    arrays, pieces = (len(shards), len(items))
    return pl.pallas_call(
        functools.partial(gather_kernel, chips, arrays, items),
        out_shape=[jax.ShapeDtypeStruct((count,) + shard.shape, shard.dtype) for shard in shards],
        in_specs=[pl.BlockSpec(memory_space=pl.ANY)] * arrays,
        out_specs=[pl.BlockSpec(memory_space=pl.ANY)] * arrays,
        scratch_shapes=[
            pltpu.SemaphoreType.DMA((pieces, 2, chips // 2)),
            pltpu.SemaphoreType.DMA((pieces, 2, chips // 2)),
            pltpu.SemaphoreType.DMA((pieces, chips)),
            pltpu.SemaphoreType.DMA((pieces, chips)),
            pltpu.SemaphoreType.DMA((pieces,)),
        ],
        compiler_params=pltpu.CompilerParams(collective_id=0, has_side_effects=True),
    )(*shards)


def scatter_kernel(chips, arrays, items, *refs):
    count = len(items)
    parts, outs, refs = (refs[:arrays], refs[arrays : 2 * arrays], refs[2 * arrays :])
    landed, paired, mine = (refs[:count], refs[count : 2 * count], refs[2 * count : 3 * count])
    ring_send, ring_recv, pair_send, pair_recv, mine_sem = refs[3 * count :]
    splits = [way for _, _, _, way in items]
    half = chips // 2
    me, core, position, right, left, sibling = ring_place(chips)
    greet((left, right, sibling))

    def part(item, block):
        array, start, rows, _ = items[item]
        return parts[array].at[block, pl.ds(start, rows)]

    def first(item, way):
        return 1 if splits[item] == way else 2

    def slot(item, way, step):
        return step - 1 if splits[item] == way else half + step - 2

    def offset_of(step, way):
        return half - step + 1 if way == 0 else chips - (half - step + 1)

    def pair_copy(item, offset):
        block = ring_chip(position + offset, chips) * 2 + 1 - core
        return pltpu.make_async_remote_copy(
            src_ref=part(item, block),
            dst_ref=paired[item].at[offset],
            send_sem=pair_send.at[item, offset],
            recv_sem=pair_recv.at[item, offset],
            device_id={"dp": sibling},
            device_id_type=MESH,
        )

    def ring_copy(item, way, step):
        if step == first(item, way):
            source = paired[item].at[offset_of(step, way)]
        else:
            source = landed[item].at[slot(item, way, step - 1)]
        here = slot(item, way, step)
        return pltpu.make_async_remote_copy(
            src_ref=source,
            dst_ref=landed[item].at[here],
            send_sem=ring_send.at[item, here],
            recv_sem=ring_recv.at[item, here],
            device_id={"dp": right if way == 0 else left},
            device_id_type=MESH,
        )

    def load(item, offset, buffer):
        block = ring_chip(position + offset, chips) * 2 + core
        return pltpu.make_async_copy(part(item, block), mine[item].at[buffer], mine_sem.at[item, buffer])

    plan, uses = ([], [0] * count)
    for step in range(1, half + 2):
        for item in range(count):
            for way in (0, 1):
                if step <= half and step >= first(item, way):
                    plan.append((step, item, way, offset_of(step, way), uses[item] % 2))
                    uses[item] += 1
            if step > half:
                plan.append((step, item, None, 0, uses[item] % 2))
                uses[item] += 1
    for step, item, way, offset, buffer in plan:
        pair_copy(item, offset).start()
    load(plan[0][1], plan[0][3], plan[0][4]).start()
    sent = []
    for number, (step, item, way, offset, buffer) in enumerate(plan):
        if number + 1 < len(plan):
            load(plan[number + 1][1], plan[number + 1][3], plan[number + 1][4]).start()
        load(item, offset, buffer).wait()
        pair_copy(item, offset).wait_recv()
        array, start, rows, _ = items[item]
        kind = parts[array].dtype
        chunk = 16 if rows % 16 == 0 else rows
        from_pair, from_mine, from_ring = (paired[item], mine[item], landed[item])
        if way is None:
            ring_copy(item, 0, half).wait_recv()
            ring_copy(item, 1, half).wait_recv()
            slot_a, slot_b = (slot(item, 0, half), slot(item, 1, half))

            @pl.loop(0, rows // chunk)
            def _(index):
                here = pl.ds(pl.multiple_of(index * chunk, chunk), chunk)
                outs[array][pl.ds(pl.multiple_of(start + index * chunk, chunk), chunk), :] = (
                    from_ring[slot_a, here, :].astype(F32) + from_ring[slot_b, here, :].astype(F32)
                ) + (from_mine[buffer, here, :].astype(F32) + from_pair[offset, here, :].astype(F32))

            continue
        if step == first(item, way):

            @pl.loop(0, rows // chunk)
            def _(index):
                here = pl.ds(pl.multiple_of(index * chunk, chunk), chunk)
                from_pair[offset, here, :] = (
                    from_mine[buffer, here, :].astype(F32) + from_pair[offset, here, :].astype(F32)
                ).astype(kind)

        else:
            ring_copy(item, way, step - 1).wait_recv()
            arrived = slot(item, way, step - 1)

            @pl.loop(0, rows // chunk)
            def _(index):
                here = pl.ds(pl.multiple_of(index * chunk, chunk), chunk)
                from_ring[arrived, here, :] = (
                    from_ring[arrived, here, :].astype(F32)
                    + (from_mine[buffer, here, :].astype(F32) + from_pair[offset, here, :].astype(F32))
                ).astype(kind)

        sent.append(ring_copy(item, way, step))
        sent[-1].start()
    for copy in sent:
        copy.wait_send()
    for step, item, way, offset, buffer in plan:
        pair_copy(item, offset).wait_send()


def scatter(parts, items, count):
    chips = count // 2
    arrays, pieces = (len(parts), len(items))
    shapes = [(rows,) + parts[array].shape[2:] for array, _, rows, _ in items]
    kinds = [parts[array].dtype for array, _, _, _ in items]
    return pl.pallas_call(
        functools.partial(scatter_kernel, chips, arrays, items),
        out_shape=[jax.ShapeDtypeStruct(part.shape[1:], F32) for part in parts],
        in_specs=[pl.BlockSpec(memory_space=pl.ANY)] * arrays,
        out_specs=[pl.BlockSpec(memory_space=pltpu.VMEM)] * arrays,
        scratch_shapes=[pltpu.VMEM((chips - 1,) + shape, kind) for shape, kind in zip(shapes, kinds)]
        + [pltpu.VMEM((chips,) + shape, kind) for shape, kind in zip(shapes, kinds)]
        + [pltpu.VMEM((2,) + shape, kind) for shape, kind in zip(shapes, kinds)]
        + [
            pltpu.SemaphoreType.DMA((pieces, chips - 1)),
            pltpu.SemaphoreType.DMA((pieces, chips - 1)),
            pltpu.SemaphoreType.DMA((pieces, chips)),
            pltpu.SemaphoreType.DMA((pieces, chips)),
            pltpu.SemaphoreType.DMA((pieces, 2)),
        ],
        compiler_params=pltpu.CompilerParams(
            collective_id=1, has_side_effects=True, vmem_limit_bytes=62 * 2**20
        ),
    )(*parts)


def block_shape(rows, columns):
    return (rows, columns) if rows % 16 == 0 else (rows * columns // 128, 128)


def small_pack(gains, shifts, bias, count):
    width = gains.shape[1] // count
    ups = bias.shape[0] // gains.shape[1]
    rows = [
        gains.reshape(2, count, width).swapaxes(0, 1),
        shifts.reshape(6, count, width).swapaxes(0, 1),
        bias.reshape(count, ups, width),
    ]
    blank = jnp.zeros((count, 8 - ups, width), gains.dtype)
    return jnp.concatenate(rows + [blank], axis=1)


def small_split(blocks, ups):
    count, _, width = blocks.shape
    gains = blocks[:, 0:2].swapaxes(0, 1).reshape(2, count * width)
    shifts = blocks[:, 2:8].swapaxes(0, 1).reshape(6, count * width)
    bias = blocks[:, 8 : 8 + ups].reshape(count * ups * width)
    return (gains, shifts, bias)


def row_norm(rows_in):
    center = rows_in - jnp.mean(rows_in, axis=-1, keepdims=True)
    inverse = lax.rsqrt(jnp.mean(center * center, axis=-1, keepdims=True) + 1e-05)
    return (center * inverse, inverse)


def norm_back(grad_rows, normed, inverse):
    return inverse * (
        grad_rows
        - jnp.mean(grad_rows, axis=-1, keepdims=True)
        - normed * jnp.mean(grad_rows * normed, axis=-1, keepdims=True)
    )


def gelu_parts(hidden):
    cumulative = 0.5 * (1.0 + lax.erf(hidden * (1.0 / math.sqrt(2.0))))
    slope = cumulative + hidden * jnp.exp(-0.5 * hidden * hidden) * (1.0 / math.sqrt(2.0 * math.pi))
    return (hidden * cumulative, slope)


def dot(left, right):
    return lax.dot_general(left, right, (((1,), (0,)), ((), ())), preferred_element_type=F32)


def dot_right(left, right):
    return lax.dot_general(left, right, (((1,), (1,)), ((), ())), preferred_element_type=F32)


def dot_left(left, right):
    return lax.dot_general(left, right, (((0,), (0,)), ((), ())), preferred_element_type=F32)


class Stream:
    def __init__(self, blocks, buffers, sems):
        self.blocks, self.buffers, self.sems = (blocks, buffers, sems)
        self.depth = buffers.shape[0]
        self.started = 0
        for _ in range(min(self.depth, len(blocks))):
            self.start()

    def copy(self, number):
        slot = number % self.depth
        return pltpu.make_async_copy(self.blocks[number], self.buffers.at[slot], self.sems.at[slot])

    def start(self):
        self.copy(self.started).start()
        self.started += 1

    def take(self, number):
        self.copy(number).wait()
        return self.buffers.at[number % self.depth]

    def release(self):
        if self.started < len(self.blocks):
            self.start()


def weight_blocks(w_qkv, w_out, w_up, w_down):
    width = w_out.shape[0]
    def cut(ref, axis, number):
        window = pl.ds(number * width, width)
        return ref.at[:, window] if axis else ref.at[window, :]
    heads = [cut(w_qkv, 1, number) for number in range(3)]
    ups = [cut(w_up, 1, number) for number in range(w_up.shape[1] // width)]
    downs = [cut(w_down, 0, number) for number in range(w_down.shape[0] // width)]
    return (heads, w_out, ups, downs)


def head_masks(length):
    return lax.broadcasted_iota(jnp.int32, (length, 128), 1) < HEAD_DIM


def two_heads(array, side):
    blank = jnp.zeros_like(array)
    return jnp.concatenate([jnp.where(side, array, blank), jnp.where(side, blank, array)], axis=0)


def attend(packed, mixed, width, low=0, high=None):
    length = packed.shape[0]
    side = head_masks(length)

    def pair_of(pair):
        start = pair * 128 if isinstance(pair, int) else pl.multiple_of(pair * 128, 128)
        queries = packed[:, pl.ds(start, 128)] * jnp.asarray(1.0 / math.sqrt(HEAD_DIM), LOW)
        keys = two_heads(packed[:, pl.ds(start + width, 128)], side)
        values = two_heads(packed[:, pl.ds(start + 2 * width, 128)], side)
        scores = dot_right(queries, keys)
        probs, totals = ([], [])
        for head in (0, 1):
            mine = scores[:, head * length : (head + 1) * length]
            shifted = jnp.exp(mine - jnp.max(mine, axis=-1, keepdims=True))
            totals.append(1.0 / jnp.sum(shifted, axis=-1, keepdims=True))
            probs.append(shifted.astype(LOW))
        result = dot(jnp.concatenate(probs, axis=1), values)
        mixed[:, pl.ds(start, 128)] = (result * jnp.where(side, totals[0], totals[1])).astype(LOW)

    if high is not None:
        for pair in range(low, high):
            pair_of(pair)
        return

    @pl.loop(0, width // 640)
    def _(index):
        for at in range(5):
            pair_of(index * 5 + at)


def attend_back(packed, grad_mixed, grad_packed, width, low=0, high=None):
    length = packed.shape[0]
    side = head_masks(length)
    scale = 1.0 / math.sqrt(HEAD_DIM)

    def pair_of(pair):
        start = pair * 128 if isinstance(pair, int) else pl.multiple_of(pair * 128, 128)
        queries = packed[:, pl.ds(start, 128)]
        keys = packed[:, pl.ds(start + width, 128)] * jnp.asarray(scale, LOW)
        grads = grad_mixed[:, pl.ds(start, 128)]
        keys_two = two_heads(keys, side)
        queries_two = two_heads(queries, side)
        grads_two = two_heads(grads, side)
        scores = dot_right(keys, queries_two)
        grad_probs = dot_right(packed[:, pl.ds(start + 2 * width, 128)], grads_two)
        probs, grad_scores = ([], [])
        for head in (0, 1):
            mine = slice(head * length, (head + 1) * length)
            shifted = jnp.exp(scores[:, mine] - jnp.max(scores[:, mine], axis=0, keepdims=True))
            prob = shifted * (1.0 / jnp.sum(shifted, axis=0, keepdims=True))
            product = grad_probs[:, mine] * prob
            weighted = jnp.sum(product, axis=0, keepdims=True)
            probs.append(prob.astype(LOW))
            grad_scores.append((product - prob * weighted).astype(LOW))
        beside = jnp.concatenate(grad_scores, axis=1)
        grad_packed[:, pl.ds(start, 128)] = dot_left(jnp.concatenate(grad_scores, axis=0), keys_two).astype(LOW)
        grad_packed[:, pl.ds(start + width, 128)] = (dot(beside, queries_two) * scale).astype(LOW)
        grad_packed[:, pl.ds(start + 2 * width, 128)] = dot(jnp.concatenate(probs, axis=1), grads_two).astype(LOW)

    if high is not None:
        for pair in range(low, high):
            pair_of(pair)
        return

    @pl.loop(0, width // 640)
    def _(index):
        for at in range(5):
            pair_of(index * 5 + at)


def forward_kernel(cell, held, at, active, entry_h, rows, w_qkv, w_out, w_up, w_down, *refs):
    sent_h = refs[held]
    out_h, lowered_h, packed_h, mixed_h, middle_h, second_h, active_h, slope_h = [
        ref.at[cell] for ref in refs[held + 1 : held + 9]
    ]
    (buffers, buffer_sems, save_sems, out_v, lowered_v, packed_v, mixed_v, middle_v) = refs[held + 9 : held + 17]
    (second_v, active_v, slope_v, hidden_v, total_v, entry, entry_sem) = refs[held + 17 :]
    entry = entry_h if at is None else entry
    width = entry.shape[1]
    gains, shifts, bias = (rows.at[0:2], rows.at[2:8], rows.at[8:16])
    ups = w_up.shape[1] // width

    @pl.when(active[0] != 0)
    def _():
        heads, outer, up, down = weight_blocks(w_qkv, w_out, w_up, w_down)
        order = heads + [outer]
        place_up, place_down = ({}, {})
        for number in range(ups + 1):
            if number < ups:
                place_up[number] = len(order)
                order.append(up[number])
            if number > 0:
                place_down[number - 1] = len(order)
                order.append(down[number - 1])
        if at is not None:
            fetched = pltpu.make_async_copy(entry_h.at[at], entry, entry_sem)
            fetched.start()
        saves = []

        def save(source, target):
            saves.append(pltpu.make_async_copy(source, target, save_sems.at[len(saves)]))
            saves[-1].start()

        if at is not None:
            fetched.wait()
        stream = Stream(order, buffers, buffer_sems)
        rows_in = entry[...].astype(F32)
        normed, _ = row_norm(rows_in)
        lowered_v[...] = (normed * gains[0:1, :] + shifts[0:1, :]).astype(LOW)
        save(lowered_v, lowered_h)
        for number in range(3):
            block = stream.take(number)
            window = pl.ds(number * width, width)
            part = dot(lowered_v[...], block[...])
            if number != 1:
                part = part + shifts[1 + number // 2 : 2 + number // 2, :]
            packed_v[:, window] = part.astype(LOW)
            stream.release()
        save(packed_v, packed_h)
        attend(packed_v, mixed_v, width)
        save(mixed_v, mixed_h)
        block = stream.take(3)
        middle = entry[...].astype(F32) + dot(mixed_v[...], block[...]) + shifts[3:4, :]
        middle_v[...] = middle
        stream.release()
        save(middle_v, middle_h)
        normed, _ = row_norm(middle_v[...])
        second_v[...] = (normed * gains[1:2, :] + shifts[4:5, :]).astype(LOW)
        save(second_v, second_h)
        for number in range(ups + 1):
            if number < ups:
                up_block = stream.take(place_up[number])
            if number > 0:
                down_block = stream.take(place_down[number - 1])
            if number < ups:
                hidden_v[number % 2] = dot(second_v[...], up_block[...]) + bias[number : number + 1, :]
            if number > 0:
                window = pl.ds((number - 1) * width, width)
                activated, slope = gelu_parts(hidden_v[(number - 1) % 2])
                active_v[:, window] = activated.astype(LOW)
                slope_v[:, window] = slope.astype(LOW)
                part = dot(active_v[:, window], down_block[...])
                if number == 1:
                    total_v[...] = part
                elif number < ups:
                    total_v[...] += part
                else:
                    out_v[...] = (middle_v[...] + (total_v[...] + part + shifts[5:6, :])).astype(LOW)
                save(active_v.at[:, window], active_h.at[:, window])
                save(slope_v.at[:, window], slope_h.at[:, window])
            if number < ups:
                stream.release()
            if number > 0:
                stream.release()
        save(out_v, sent_h)
        save(out_v, out_h)
        for copy in saves:
            copy.wait()


def kept_shapes(length, width, deep):
    return [
        ((length, width), LOW),
        ((length, width), LOW),
        ((length, 3 * width), LOW),
        ((length, width), LOW),
        ((length, width), F32),
        ((length, width), LOW),
        ((length, deep), LOW),
        ((length, deep), LOW),
    ]


def forward_tick(active, entry, rows, weights, kept, cell, cell_count):
    entry, at = entry
    length, width = entry.shape[-2:]
    deep = weights[2].shape[1]
    ups = deep // width
    shapes = kept_shapes(length, width, deep)
    outs = [jax.ShapeDtypeStruct(*shapes[0])] + [
        jax.ShapeDtypeStruct((cell_count,) + shape, kind) for shape, kind in shapes
    ]
    vmem, hbm = (pl.BlockSpec(memory_space=pltpu.VMEM), pl.BlockSpec(memory_space=pl.ANY))
    flops = 2 * length * width * (4 * width + 2 * deep) + 16 * length * length * width
    kept = () if kept is None else tuple(kept)
    held = len(kept)
    sent, *kept = pl.pallas_call(
        functools.partial(forward_kernel, cell, held, at),
        out_shape=outs,
        in_specs=[pl.BlockSpec(memory_space=pltpu.SMEM), vmem if at is None else hbm, vmem] + [hbm] * (4 + held),
        out_specs=[hbm] * 9,
        input_output_aliases={7 + number: 1 + number for number in range(held)},
        scratch_shapes=[
            pltpu.VMEM((4, width, width), LOW),
            pltpu.SemaphoreType.DMA((4,)),
            pltpu.SemaphoreType.DMA((7 + 2 * ups,)),
        ]
        + [pltpu.VMEM(*shape) for shape in shapes]
        + [
            pltpu.VMEM((2, length, width), F32),
            pltpu.VMEM((length, width), F32),
            pltpu.VMEM((length, width), LOW),
            pltpu.SemaphoreType.DMA,
        ],
        compiler_params=pltpu.CompilerParams(vmem_limit_bytes=60 * 2**20),
        cost_estimate=pl.CostEstimate(
            flops=flops, bytes_accessed=2 * width * (4 * width + 2 * deep), transcendentals=0
        ),
    )(active, entry, rows, *weights, *kept)
    return (sent, kept)


def backward_kernel(cell, held, grad_at, entry_at, active, scale, grad_h, entry_h, rows, *refs):
    packed, middle, slope = [ref.at[cell] for ref in refs[:3]]
    w_qkv, w_out, w_up, w_down = refs[3:7]
    refs = refs[7 + held :]
    sent_h = refs[0]
    rows_h, packed_h, branch_h, inner_h, low_h, sums_h = [ref.at[cell] for ref in refs[1:7]]
    (buffers, buffer_sems, load_sems, save_sems, rows_v, grad_packed_v, branch_v, inner_v, low_v, sums_v) = refs[7:17]
    (packed_v, middle_v, slope_v, mixed_v, grad_act_v, total_v, grad_middle_v, grad, entry) = refs[17:]
    gains = rows.at[0:2]
    grad = grad_h if grad_at is None else grad
    entry_h = entry_h if entry_at is None else entry_h.at[entry_at]
    length, width = entry.shape
    ups = w_up.shape[1] // width

    @pl.when(active[0] != 0)
    def _():
        heads, outer, up, down = weight_blocks(w_qkv, w_out, w_up, w_down)
        loads = [
            pltpu.make_async_copy(slope, slope_v, load_sems.at[0]),
            pltpu.make_async_copy(middle, middle_v, load_sems.at[1]),
            pltpu.make_async_copy(packed, packed_v, load_sems.at[2]),
            pltpu.make_async_copy(entry_h, entry, load_sems.at[3]),
        ]
        if grad_at is not None:
            loads.append(pltpu.make_async_copy(grad_h.at[grad_at], grad, load_sems.at[4]))
            loads[4].start()
        order, place_up, place_down = ([], {}, {})
        for number in range(ups + 1):
            if number < ups:
                place_down[number] = len(order)
                order.append(down[number])
            if number > 0:
                place_up[number - 1] = len(order)
                order.append(up[number - 1])
        place_out = len(order)
        order = order + [outer] + heads
        saves = []

        def save(source, target):
            saves.append(pltpu.make_async_copy(source, target, save_sems.at[len(saves)]))
            saves[-1].start()

        def column_sum(array):
            return jnp.sum(array.astype(F32), axis=0, keepdims=True)

        if grad_at is not None:
            loads[4].wait()
        stream = Stream(order, buffers, buffer_sems)
        loads[0].start()
        low_v[...] = (grad[...].astype(F32) * scale[0]).astype(LOW)
        save(low_v, low_h)
        sums_v[7:8, :] = column_sum(low_v[...])
        for number in range(ups + 1):
            if number == 1:
                loads[0].wait()
                loads[1].start()
            if number == 2:
                loads[2].start()
                loads[3].start()
            if number < ups:
                down_block = stream.take(place_down[number])
            if number > 0:
                up_block = stream.take(place_up[number - 1])
            if number < ups:
                grad_act_v[number % 2] = dot_right(low_v[...], down_block[...])
            if number > 0:
                window = pl.ds((number - 1) * width, width)
                inner = (grad_act_v[(number - 1) % 2] * slope_v[:, window].astype(F32)).astype(LOW)
                inner_v[:, window] = inner
                sums_v[7 + number : 8 + number, :] = column_sum(inner)
                part = dot_right(inner, up_block[...])
                if number == 1:
                    total_v[...] = part
                else:
                    total_v[...] += part
                save(inner_v.at[:, window], inner_h.at[:, window])
            if number < ups:
                stream.release()
            if number > 0:
                stream.release()
        loads[1].wait()
        normed, inverse = row_norm(middle_v[...])
        grad_second = total_v[...]
        sums_v[1:2, :] = column_sum(grad_second * normed)
        sums_v[6:7, :] = column_sum(grad_second)
        grad_middle = grad[...].astype(F32) * scale[0] + norm_back(grad_second * gains[1:2, :], normed, inverse)
        grad_middle_v[...] = grad_middle
        branch_v[...] = grad_middle.astype(LOW)
        sums_v[5:6, :] = column_sum(branch_v[...])
        save(branch_v, branch_h)
        block = stream.take(place_out)
        mixed_v[...] = dot_right(branch_v[...], block[...]).astype(LOW)
        stream.release()
        loads[2].wait()
        attend_back(packed_v, mixed_v, grad_packed_v, width)
        save(grad_packed_v, packed_h)
        sums_v[3:4, :] = column_sum(grad_packed_v[:, pl.ds(0, width)])
        sums_v[4:5, :] = column_sum(grad_packed_v[:, pl.ds(2 * width, width)])
        for number in range(3):
            block = stream.take(place_out + 1 + number)
            part = dot_right(grad_packed_v[:, pl.ds(number * width, width)], block[...])
            if number == 0:
                total_v[...] = part
            else:
                total_v[...] += part
            stream.release()
        loads[3].wait()
        normed, inverse = row_norm(entry[...].astype(F32))
        grad_lowered = total_v[...]
        sums_v[0:1, :] = column_sum(grad_lowered * normed)
        sums_v[2:3, :] = column_sum(grad_lowered)
        rows_v[...] = (grad_middle_v[...] + norm_back(grad_lowered * gains[0:1, :], normed, inverse)).astype(LOW)
        save(sums_v, sums_h)
        save(rows_v, sent_h)
        save(rows_v, rows_h)
        for copy in saves:
            copy.wait()


def backward_tick(active, incoming, entry, rows, saved, weights, kept, cell, cell_count):
    entry, entry_at = entry
    (grad, grad_at), scale = incoming
    length, width = entry.shape[-2:]
    deep = weights[2].shape[1]
    ups = deep // width
    shapes = [
        ((length, width), LOW),
        ((length, 3 * width), LOW),
        ((length, width), LOW),
        ((length, deep), LOW),
        ((length, width), LOW),
        ((16, width), F32),
    ]
    outs = [jax.ShapeDtypeStruct(*shapes[0])] + [
        jax.ShapeDtypeStruct((cell_count,) + shape, kind) for shape, kind in shapes
    ]
    vmem, hbm = (pl.BlockSpec(memory_space=pltpu.VMEM), pl.BlockSpec(memory_space=pl.ANY))
    smem = pl.BlockSpec(memory_space=pltpu.SMEM)
    flops = 2 * length * width * (4 * width + 2 * deep) + 40 * length * length * width
    kept = () if kept is None else tuple(kept)
    held = len(kept)
    sent, *kept = pl.pallas_call(
        functools.partial(backward_kernel, cell, held, grad_at, entry_at),
        out_shape=outs,
        in_specs=[smem] * 2 + [vmem if grad_at is None else hbm, hbm, vmem] + [hbm] * (7 + held),
        out_specs=[hbm] * 7,
        input_output_aliases={12 + number: 1 + number for number in range(held)},
        scratch_shapes=[
            pltpu.VMEM((4, width, width), LOW),
            pltpu.SemaphoreType.DMA((4,)),
            pltpu.SemaphoreType.DMA((5,)),
            pltpu.SemaphoreType.DMA((6 + ups,)),
        ]
        + [pltpu.VMEM(*shape) for shape in shapes]
        + [
            pltpu.VMEM((length, 3 * width), LOW),
            pltpu.VMEM((length, width), F32),
            pltpu.VMEM((length, deep), LOW),
            pltpu.VMEM((length, width), LOW),
            pltpu.VMEM((2, length, width), F32),
            pltpu.VMEM((length, width), F32),
            pltpu.VMEM((length, width), F32),
            pltpu.VMEM((length, width), LOW),
            pltpu.VMEM((length, width), LOW),
        ],
        compiler_params=pltpu.CompilerParams(vmem_limit_bytes=60 * 2**20),
        cost_estimate=pl.CostEstimate(
            flops=flops, bytes_accessed=2 * width * (4 * width + 2 * deep), transcendentals=0
        ),
    )(active, scale, grad, entry, rows, *saved, *weights, *kept)
    return (sent, kept)


def small_rows(small, rows, width, ups):
    devices, _, own = small.shape
    lane = lax.broadcasted_iota(jnp.int32, (own, width), 1)
    depth = lax.broadcasted_iota(jnp.int32, (own, width), 0)
    row = lax.broadcasted_iota(jnp.int32, (16, width), 0)
    across = lax.broadcasted_iota(jnp.int32, (16, width), 1)
    top = jnp.zeros((16, width), F32)
    for device in range(devices):
        spot = jnp.where(lane == depth + device * own, 1.0, 0.0).astype(LOW)
        top = top + dot(small[device], spot)
    rows[0:8, :] = top[0:8]
    share = devices // ups
    for block in range(ups):
        total = jnp.zeros((1, width), F32)
        for index in range(share):
            start = index * ups * own
            spot = jnp.zeros((own, width), F32)
            for up in range(ups):
                spot = spot + jnp.where(lane == depth + (start + up * own), 1.0, 0.0)
            low = start + (row - 8) * own
            inside = (row >= 8) & (row < 8 + ups) & (across >= low) & (across < low + own)
            placed = dot(small[block * share + index], spot.astype(LOW))
            total = total + jnp.sum(jnp.where(inside, placed, 0.0), axis=0, keepdims=True)
        rows[8 + block : 9 + block, :] = total


def gather_forward_kernel(chips, items, groups, cells, *refs):
    shards, inputs_h = (refs[:5], refs[5])
    outs, rows_h, arrived_h, later_h = (refs[6:11], refs[11], refs[12], refs[13])
    out_h, lowered_h, packed_h, mixed_h, middle_h, second_h, active_h, slope_h = refs[14:22]
    (ring_send, ring_recv, pair_send, pair_recv, own_sem, hop_send, hop_recv) = refs[22:29]
    (load_sem, save_sem, wide_sem, deep_sem) = refs[29:33]
    (small_v, rows_v, entry_v, out_v, lowered_v, packed_v, mixed_v, middle_v, second_v, active_v, slope_v) = refs[33:44]
    (total_v, hidden_v, wide_v, deep_v) = refs[44:]
    length, width = entry_v.shape[1:]
    ups = active_v.shape[2] // width
    half = chips // 2
    me, core, position, right, left, sibling = ring_place(chips)
    stage = lax.axis_index("pipe")
    first = stage == 0
    barrier = pltpu.get_barrier_semaphore()
    for device in (left, right, sibling):
        pl.semaphore_signal(barrier, inc=1, device_id={"dp": device}, device_id_type=MESH)
    pl.semaphore_signal(barrier, inc=1, device_id={"pipe": 1 - stage}, device_id_type=MESH)
    pl.semaphore_wait(barrier, 4)

    def shard(item):
        array, start, rows, _ = items[item]
        return shards[array].at[pl.ds(start, rows)]

    def out(item, block):
        array, start, rows, _ = items[item]
        return outs[array].at[block, pl.ds(start, rows)]

    def owner(step, way):
        return ring_chip(position - step if way == 0 else position + step, chips) * 2 + core

    def travels(item, way, step):
        return step < half or (step == half and items[item][3] == way)

    def ring_copy(item, way, step):
        block = owner(step - 1, way)
        return pltpu.make_async_remote_copy(
            src_ref=shard(item) if step == 1 else out(item, block),
            dst_ref=out(item, block),
            send_sem=ring_send.at[item, way, step - 1],
            recv_sem=ring_recv.at[item, way, step - 1],
            device_id={"dp": right if way == 0 else left},
            device_id_type=MESH,
        )

    def pair_copy(item, offset, block, source):
        return pltpu.make_async_remote_copy(
            src_ref=source,
            dst_ref=out(item, block),
            send_sem=pair_send.at[item, offset],
            recv_sem=pair_recv.at[item, offset],
            device_id={"dp": sibling},
            device_id_type=MESH,
        )

    def own_copy(item):
        return pltpu.make_async_copy(shard(item), out(item, me), own_sem.at[item])

    sent, paired = ([], [])

    def open_group(group):
        for item in group:
            for way in (0, 1):
                if travels(item, way, 1):
                    sent.append(ring_copy(item, way, 1))
                    sent[-1].start()
        for item in group:
            paired.append(pair_copy(item, 0, me, shard(item)))
            paired[-1].start()
            own_copy(item).start()

    def ring_step(item, way, step):
        ring_copy(item, way, step).wait_recv()
        if travels(item, way, step + 1):
            sent.append(ring_copy(item, way, step + 1))
            sent[-1].start()
        block = owner(step, way)
        offset = step if way == 0 else chips - step
        paired.append(pair_copy(item, offset, block, out(item, block)))
        paired[-1].start()

    def pair_arrived(item, offset):
        block = ring_chip(position - offset, chips) * 2 + core
        pair_copy(item, offset, block, out(item, block)).wait_recv()

    saves = []

    def save(source, target):
        number = len(saves)
        saves.append(lambda: pltpu.make_async_copy(source(), target(), save_sem.at[number]))
        saves[-1]().start()

    def entry_load(cell):
        return pltpu.make_async_copy(inputs_h.at[cell], entry_v.at[cell], load_sem.at[cell])

    def wide_load(array, column, slot):
        source = outs[array].at[:, :, pl.ds(column * width, width)]
        return pltpu.make_async_copy(source, wide_v.at[slot], wide_sem.at[slot])

    def wide(slot):
        return wide_v[slot].reshape(width, width)

    def gains(number):
        return rows_v[number : number + 1, :]

    def shifts(number):
        return rows_v[2 + number : 3 + number, :]

    def begin(cell):
        def step():
            entry_load(cell).wait()
            normed, _ = row_norm(entry_v[cell].astype(F32))
            lowered_v[cell] = (normed * gains(0) + shifts(0)).astype(LOW)
            save(lambda: lowered_v.at[cell], lambda: lowered_h.at[cell])

        return step

    def project(cell, number):
        def step():
            if cell == 0:
                wide_load(1, number, number).wait()
            part = dot(lowered_v[cell], wide(number))
            if number != 1:
                part = part + shifts(1 + number // 2)
            packed_v[cell, :, pl.ds(number * width, width)] = part.astype(LOW)
            if number == 2:
                save(lambda: packed_v.at[cell], lambda: packed_h.at[cell])

        return step

    def mix(cell, low, high, last):
        def step():
            attend(packed_v.at[cell], mixed_v.at[cell], width, low, high)
            if last:
                save(lambda: mixed_v.at[cell], lambda: mixed_h.at[cell])

        return step

    def join(cell):
        def step():
            if cell == 0:
                wide_load(2, 0, 3).wait()
            middle_v[cell] = entry_v[cell].astype(F32) + dot(mixed_v[cell], wide(3)) + shifts(3)
            save(lambda: middle_v.at[cell], lambda: middle_h.at[cell])

        return step

    def renorm(cell):
        def step():
            middle = middle_v[cell]
            normed, _ = row_norm(middle)
            second_v[cell] = (normed * gains(1) + shifts(4)).astype(LOW)
            total_v[cell] = middle + shifts(5)
            save(lambda: second_v.at[cell], lambda: second_h.at[cell])

        return step

    def rise(cell, number):
        def step():
            if cell == 0:
                wide_load(3, number, number).wait()
            hidden_v[...] = dot(second_v[cell], wide(number)) + rows_v[8 + number : 9 + number, :]

        return step

    def bend(cell, number):
        def step():
            window = pl.ds(number * width, width)
            activated, slope = gelu_parts(hidden_v[...])
            active_v[cell, :, window] = activated.astype(LOW)
            slope_v[cell, :, window] = slope.astype(LOW)
            if number == ups - 1:
                save(lambda: active_v.at[cell], lambda: active_h.at[cell])
                save(lambda: slope_v.at[cell], lambda: slope_h.at[cell])

        return step

    deep_rows = deep_v.shape[1] * deep_v.shape[2]

    def deep_load(offset, slot):
        chip = ring_chip(position - offset, chips)
        return pltpu.make_async_copy(outs[4].at[pl.ds(chip * 2, 2)], deep_v.at[slot], deep_sem.at[slot])

    def fall(cell, offset, slot):
        def step():
            if cell == 0:
                deep_load(offset, slot).wait()
            chip = ring_chip(position - offset, chips)
            window = pl.ds(pl.multiple_of(chip * deep_rows, 128), deep_rows)
            total_v[cell] += dot(active_v[cell, :, window], deep_v[slot].reshape(deep_rows, width))

        return step

    def hop():
        return pltpu.make_async_remote_copy(
            src_ref=out_v.at[0],
            dst_ref=arrived_h,
            send_sem=hop_send,
            recv_sem=hop_recv,
            device_id={"pipe": 1 - stage},
            device_id_type=MESH,
        )

    def finish(cell):
        def step():
            out_v[cell] = total_v[cell].astype(LOW)
            if cell == 0:
                hop().start()
            else:
                save(lambda: out_v.at[cell], lambda: later_h)
            save(lambda: out_v.at[cell], lambda: out_h.at[cell])

        return step

    def on_first(step):
        pl.when(first)(step)

    queue = []

    def ready(group, steps, loads):
        for item in group:
            own_copy(item).wait()
            for offset in range(chips):
                pair_arrived(item, offset)

        @pl.when(first)
        def _():
            for load in loads:
                load().start()

        queue.extend(steps)

    pairs = width // 128
    heads = []
    for cell in range(cells):
        heads.append(begin(cell))
        heads += [project(cell, number) for number in range(3)]
        heads += [mix(cell, low, low + 2, low + 2 >= pairs) for low in range(0, pairs, 2)]
    joins = [make(cell) for cell in range(cells) for make in (join, renorm)]
    def load_ups():
        for number in range(ups):
            wide_load(3, number, number).start()

    climbs = [load_ups]
    climbs += [make(0, number) for number in range(ups) for make in (rise, bend)]

    @pl.when(first)
    def _():
        for cell in range(cells):
            entry_load(cell).start()

    def lay_rows():
        copy = pltpu.make_async_copy(outs[0], small_v, load_sem.at[cells])
        copy.start()
        copy.wait()
        small_rows(small_v, rows_v, width, ups)
        pltpu.make_async_copy(rows_v, rows_h, load_sem.at[cells + 1]).start()

    def ready_small():
        for item in groups[0]:
            if items[item][0] == 0:
                own_copy(item).wait()
                for offset in range(chips):
                    pair_arrived(item, offset)
        lay_rows()

    plan = []
    for number, group in enumerate(groups):
        for step in range(1, half + 1):
            if step == half and number + 1 < len(groups):
                plan.append(("open", number + 1))
            for item in group:
                for way in (0, 1):
                    if travels(item, way, step):
                        plan.append(("ring", item, way, step))
            if number == len(groups) - 1:
                plan.append(("deep", step))
        plan.append(("done", number))
    open_group(groups[0])
    late = []
    slots = [0]

    def deep_ready(offsets):
        for offset in offsets:
            for item in groups[-1]:
                if offset == 0:
                    own_copy(item).wait()
                pair_arrived(item, offset)
            slot = slots[0] % deep_v.shape[0]
            slots[0] += 1

            def opening(offset=offset, slot=slot):
                deep_load(offset, slot).start()

            queue.append(opening)
            queue.append(fall(0, offset, slot))

    def serve(limit):
        for _ in range(limit):
            if queue:
                on_first(queue.pop(0))

    for entry in plan:
        if entry[0] == "open":
            open_group(groups[entry[1]])
        elif entry[0] == "ring":
            ring_step(*entry[1:])
            for wait in list(late):
                wait[0] -= 1
                if wait[0] == 0:
                    wait[1]()
                    late.remove(wait)
            serve(2)
        elif entry[0] == "done":
            if entry[1] == 0:
                rest = [item for item in groups[0] if items[item][0] != 0]
                late.append([1, ready_small])
                late.append(
                    [
                        2,
                        lambda: ready(
                            rest,
                            heads + joins,
                            [functools.partial(wide_load, 1, number, number) for number in range(3)]
                            + [functools.partial(wide_load, 2, 0, 3)],
                        ),
                    ]
                )
            elif entry[1] == 1:
                late.append([2, lambda: ready(groups[1], climbs, [])])
        elif entry[0] == "deep":
            step = entry[1]
            if step == 1:
                late.append([3, lambda: deep_ready([0])])
            if step < half:
                late.append([2, lambda step=step: deep_ready([step, chips - step])])
            else:
                for wait in late:
                    wait[1]()
                serve(len(queue))
                deep_ready([half])
    serve(len(queue))

    @pl.when(first)
    def _():
        finish(0)()
        for cell in range(1, cells):
            for offset in (0, 1):
                deep_load(offset, offset).start()
            for number in range(ups):
                rise(cell, number)()
                bend(cell, number)()
            for offset in range(chips):
                deep_load(offset, offset % 2).wait()
                fall(cell, offset, offset % 2)()
                if offset + 2 < chips:
                    deep_load(offset + 2, offset % 2).start()
            finish(cell)()

    for copy in sent:
        copy.wait_send()
    for copy in paired:
        copy.wait_send()
    pltpu.make_async_copy(rows_v, rows_h, load_sem.at[cells + 1]).wait()

    @pl.when(first)
    def _():
        for copy in saves:
            copy().wait()
        hop().wait_send()

    @pl.when(jnp.logical_not(first))
    def _():
        hop().wait_recv()


def gather_forward(shards, inputs, items, groups, count):
    chips = count // 2
    cells, length, width = inputs.shape
    deep = shards[3].shape[1]
    ups = deep // width
    pieces = len(items)
    shapes = kept_shapes(length, width, deep)
    hbm = pl.BlockSpec(memory_space=pl.ANY)
    flops = 2 * cells * length * width * (4 * width + 2 * deep)
    outs = pl.pallas_call(
        functools.partial(gather_forward_kernel, chips, items, groups, cells),
        out_shape=[jax.ShapeDtypeStruct((count,) + shard.shape, shard.dtype) for shard in shards]
        + [
            jax.ShapeDtypeStruct((16, width), F32),
            jax.ShapeDtypeStruct((length, width), LOW),
            jax.ShapeDtypeStruct((length, width), LOW),
        ]
        + [jax.ShapeDtypeStruct((cells,) + shape, kind) for shape, kind in shapes],
        in_specs=[hbm] * 6,
        out_specs=[hbm] * 16,
        scratch_shapes=[
            pltpu.SemaphoreType.DMA((pieces, 2, chips // 2)),
            pltpu.SemaphoreType.DMA((pieces, 2, chips // 2)),
            pltpu.SemaphoreType.DMA((pieces, chips)),
            pltpu.SemaphoreType.DMA((pieces, chips)),
            pltpu.SemaphoreType.DMA((pieces,)),
            pltpu.SemaphoreType.DMA,
            pltpu.SemaphoreType.DMA,
            pltpu.SemaphoreType.DMA((cells + 2,)),
            pltpu.SemaphoreType.DMA((9 * cells,)),
            pltpu.SemaphoreType.DMA((4,)),
            pltpu.SemaphoreType.DMA((2,)),
            pltpu.VMEM((count,) + shards[0].shape, LOW),
            pltpu.VMEM((16, width), F32),
            pltpu.VMEM((cells, length, width), LOW),
        ]
        + [pltpu.VMEM((cells,) + shape, kind) for shape, kind in shapes]
        + [
            pltpu.VMEM((cells, length, width), F32),
            pltpu.VMEM((length, width), F32),
            pltpu.VMEM((4, count, width // count, width), LOW),
            pltpu.VMEM((2, 2, shards[4].shape[0], width), LOW),
        ],
        compiler_params=pltpu.CompilerParams(
            collective_id=3, has_side_effects=True, vmem_limit_bytes=62 * 2**20
        ),
        cost_estimate=pl.CostEstimate(flops=flops, bytes_accessed=8 * width * (4 * width + 2 * deep), transcendentals=0),
    )(*shards, inputs)
    return (outs[:5], outs[5], outs[6], outs[7], list(outs[8:]))


class RingSum:
    def __init__(self, chips, items, parts, outs, landed, paired, buffers, final, sems):
        self.chips, self.items, self.parts, self.outs = (chips, items, parts, outs)
        self.landed, self.paired, self.final = (landed, paired, final)
        self.mine, self.pairs, self.rings = buffers
        self.ring_send, self.ring_recv, self.pair_send, self.pair_recv, self.load_sem, self.final_sem = sems
        self.half = chips // 2
        self.me, self.core, self.position, self.right, self.left, self.sibling = ring_place(chips)
        self.sent, self.final_copies, self.exchanged = ({}, [], [])
        self.uses = [0] * len(items)

    def part(self, item, block):
        array, start, rows, _ = self.items[item]
        return self.parts[array].at[block, pl.ds(start, rows)]

    def first(self, item, way):
        return 1 if self.items[item][3] == way else 2

    def slot_of(self, item, way, step):
        return step - 1 if self.items[item][3] == way else self.half + step - 2

    def offset_of(self, step, way):
        return self.half - step + 1 if way == 0 else self.chips - (self.half - step + 1)

    def pair_copy(self, item, offset):
        block = ring_chip(self.position + offset, self.chips) * 2 + 1 - self.core
        return pltpu.make_async_remote_copy(
            src_ref=self.part(item, block),
            dst_ref=self.paired[item].at[offset],
            send_sem=self.pair_send.at[item, offset],
            recv_sem=self.pair_recv.at[item, offset],
            device_id={"dp": self.sibling},
            device_id_type=MESH,
        )

    def ring_copy(self, item, way, step, buffer=0):
        here = self.slot_of(item, way, step)
        return pltpu.make_async_remote_copy(
            src_ref=self.mine[item].at[buffer],
            dst_ref=self.landed[item].at[here],
            send_sem=self.ring_send.at[item, here],
            recv_sem=self.ring_recv.at[item, here],
            device_id={"dp": self.right if way == 0 else self.left},
            device_id_type=MESH,
        )

    def load_mine(self, item, offset, buffer):
        block = ring_chip(self.position + offset, self.chips) * 2 + self.core
        return pltpu.make_async_copy(self.part(item, block), self.mine[item].at[buffer], self.load_sem.at[item, buffer])

    def load_pair(self, item, offset, buffer):
        return pltpu.make_async_copy(
            self.paired[item].at[offset], self.pairs[item].at[buffer], self.load_sem.at[item, 2 + buffer]
        )

    def load_ring(self, item, way, step, buffer):
        return pltpu.make_async_copy(
            self.landed[item].at[self.slot_of(item, way, step)], self.rings[item].at[buffer], self.load_sem.at[item, 4 + buffer]
        )

    def starts(self, wanted):
        return [
            (step, item, way, self.offset_of(step, way))
            for step in (1, 2)
            for item in wanted
            for way in (0, 1)
            if step == self.first(item, way)
        ]

    def rest(self, wanted, steps):
        return [
            (step, item, way, self.offset_of(step, way))
            for step in steps
            if step <= self.half
            for item in wanted
            for way in (0, 1)
            if step > self.first(item, way)
        ] + [(step, item, None, 0) for step in steps if step > self.half for item in wanted]

    def fetch(self, entry):
        step, item, way, offset, buffer = entry
        if (item, buffer) in self.sent:
            self.sent.pop((item, buffer)).wait_send()
        self.load_mine(item, offset, buffer).start()
        self.pair_copy(item, offset).wait_recv()
        self.load_pair(item, offset, buffer).start()

    def bytes_of(self, item):
        array, _, rows, _ = self.items[item]
        return rows * self.parts[array].shape[2] * self.parts[array].dtype.itemsize

    def arrange(self, steps, ends):
        waiting = self.starts(range(len(self.items)))
        waiting += self.rest(range(len(self.items)), range(2, self.half + 2))
        opened, arrival, sends, used = ({}, {}, {}, [0] * len(self.items))
        clock, link, order, steps = (0.0, [0.0, 0.0], [], list(steps))

        def ready_at(entry):
            step, item, way, offset = entry
            if (item, offset) not in opened:
                return None
            when = opened[(item, offset)]
            sides = (0, 1) if way is None else ((way,) if step > self.first(item, way) else ())
            for side in sides:
                if (item, side, step - 1) not in arrival:
                    return None
                when = max(when, arrival[(item, side, step - 1)])
            return max(when, sends.get((item, used[item] - 2), 0.0))

        while waiting or steps:
            best = None
            for entry in waiting:
                when = ready_at(entry)
                if when is None or (entry[2] is None and (steps or any(other[2] is not None for other in waiting if ready_at(other) is not None and ready_at(other) <= clock))):
                    continue
                backlog = 0.0 if entry[2] is None else max(0.0, link[entry[2]] - max(clock, when))
                rank = (max(when, clock) + 0.5 * backlog, entry[0])
                if best is None or rank < best[0]:
                    best = (rank, entry, when)
            far_off = best is None or best[2] > clock + 0.3
            idle = best is not None and best[1][2] is not None and link[best[1][2]] > clock + ends
            if steps and (far_off or idle):
                spent, step, opens = steps.pop(0)
                clock += spent
                for item, offset in opens:
                    opened[(item, offset)] = clock + 2.0 + self.bytes_of(item) / 2e5
                order.append((step, opens))
                continue
            _, entry, when = best
            waiting.remove(entry)
            step, item, way, offset = entry
            clock = max(clock, when) + 0.8 + self.bytes_of(item) * 1.6e-6
            if way is not None:
                link[way] = max(clock, link[way]) + 2 * self.bytes_of(item) / 9.1e4
                arrival[(item, way, step)] = link[way] + 1.5
                sends[(item, used[item])] = link[way]
            order.append(entry + (used[item] % 2,))
            used[item] += 1
        return order, clock

    def follow(self, order):
        entries = [number for number, action in enumerate(order) if len(action) == 5]
        fetched = set()
        for number, action in enumerate(order):
            if len(action) == 2:
                step, opens = action
                step()
                for item, offset in opens:
                    self.pair_copy(item, offset).start()
                    self.exchanged.append((item, offset))
                continue
            if number not in fetched:
                self.fetch(action)
                fetched.add(number)
            if number + 1 in entries:
                following = order[number + 1]
                if following[1] != action[1]:
                    self.fetch(following)
                    fetched.add(number + 1)
            self.work(action)

    def work(self, entry):
        step, item, way, offset, buffer = entry
        array, start, rows, _ = self.items[item]
        half, final = (self.half, self.final)
        kind = self.parts[array].dtype
        columns = self.parts[array].shape[2]
        chunk = 16
        mine, pairs, rings = (self.mine[item], self.pairs[item], self.rings[item])
        if way is None:
            for side in (0, 1):
                self.ring_copy(item, side, half).wait_recv()
                self.load_ring(item, side, half, side).start()
            self.load_mine(item, offset, buffer).wait()
            self.load_pair(item, offset, buffer).wait()
            for side in (0, 1):
                self.load_ring(item, side, half, side).wait()
            if kind == F32:
                total = (rings[0] + rings[1]) + (mine[buffer] + pairs[buffer])
                gains, shifts, bias = self.outs[array]
                gains[...] = total[0:2]
                for row in range(6):
                    shifts[row] = total[2 + row : 3 + row]
                ups = bias.shape[1] // total.shape[1]
                bias[...] = jnp.concatenate([total[8 + up : 9 + up] for up in range(ups)], axis=1)
                return
            high, wide = (min(rows, final.shape[1]), min(columns, final.shape[2]))
            for top in range(0, rows, high):
                for across in range(0, columns, wide):
                    number = len(self.final_copies)
                    turn = number % final.shape[0]
                    if number >= final.shape[0]:
                        self.final_copies[number - final.shape[0]].wait()
                    span = pl.ds(across, wide)

                    @pl.loop(0, high // chunk)
                    def _(index):
                        here = pl.ds(pl.multiple_of(top + index * chunk, chunk), chunk)
                        final[turn, pl.ds(pl.multiple_of(index * chunk, chunk), chunk), pl.ds(0, wide)] = (
                            rings[0, here, span].astype(F32) + rings[1, here, span].astype(F32)
                        ) + (mine[buffer, here, span].astype(F32) + pairs[buffer, here, span].astype(F32))

                    self.final_copies.append(
                        pltpu.make_async_copy(
                            final.at[turn, pl.ds(0, high), pl.ds(0, wide)],
                            self.outs[array].at[pl.ds(start + top, high), span],
                            self.final_sem.at[turn],
                        )
                    )
                    self.final_copies[-1].start()
            return
        carried = step > self.first(item, way)
        if carried:
            self.ring_copy(item, way, step - 1).wait_recv()
            self.load_ring(item, way, step - 1, buffer).start()
        self.load_mine(item, offset, buffer).wait()
        self.load_pair(item, offset, buffer).wait()
        if carried:
            self.load_ring(item, way, step - 1, buffer).wait()

        @pl.loop(0, rows // chunk)
        def _(index):
            here = pl.ds(pl.multiple_of(index * chunk, chunk), chunk)
            total = mine[buffer, here, :].astype(F32) + pairs[buffer, here, :].astype(F32)
            if carried:
                total = rings[buffer, here, :].astype(F32) + total
            mine[buffer, here, :] = total.astype(kind)

        copy = self.ring_copy(item, way, step, buffer)
        copy.start()
        self.sent[(item, buffer)] = copy

    def close(self):
        for copy in self.sent.values():
            copy.wait_send()
        for item, offset in self.exchanged:
            self.pair_copy(item, offset).wait_send()
        for copy in self.final_copies[-self.final.shape[0] :]:
            copy.wait()


class Products:
    def __init__(self, chips, width, own, cuts, big, stage, cut_sem, big_sem, stage_sem):
        self.chips, self.width, self.own = (chips, width, own)
        self.cuts, self.big, self.stage = (cuts, big, stage)
        self.cut_sem, self.big_sem, self.stage_sem = (cut_sem, big_sem, stage_sem)

    def load_cut(self, source, index, slot):
        cut = self.cuts.shape[2]
        window = pl.ds(pl.multiple_of(index * cut, cut), cut)
        return pltpu.make_async_copy(source.at[:, window], self.cuts.at[slot], self.cut_sem.at[slot])

    def block(self, source, index, slot):
        window = pl.ds(pl.multiple_of(index * self.width, self.width), self.width)
        return pltpu.make_async_copy(source.at[:, window], self.big.at[slot], self.big_sem.at[slot])

    def keep(self, target, index):
        window = pl.ds(index // 2 * self.width, self.width)
        return pltpu.make_async_copy(
            self.stage.at[index % 2],
            target.at[pl.ds(index % 2 * self.chips, self.chips), :, window],
            self.stage_sem.at[index % 2],
        )

    def open(self, left, right, slot):
        for index in (0, 1):
            self.load_cut(left, index, index).start()
        self.block(right, 0, slot).start()

    def run(self, target, left, right, shift, index):
        number = 2 * (right.shape[1] // self.width)
        slot, here = (index % 2, (index // 2 + shift) % 2)
        if index == 0:
            for side in (0, 1):
                self.load_cut(left, side, side).wait()
        if slot == 0:
            self.block(right, index // 2, here).wait()
            if index + 2 < number:
                self.block(right, index // 2 + 1, 1 - here).start()
        if index >= 2:
            self.keep(target, index - 2).wait()
        product = dot_left(self.cuts[slot], self.big[here]).astype(LOW)
        for device in range(self.chips):
            self.stage[slot, device] = product[device * self.own : (device + 1) * self.own]
        self.keep(target, index).start()

    def close(self, target, right):
        number = 2 * (right.shape[1] // self.width)
        for index in (number - 2, number - 1):
            self.keep(target, index).wait()


def last_backward_kernel(chips, items, cell, *refs):
    count = len(items)
    (grad, entry_h, rows, packed_h, middle_h, slope_h, w_qkv, w_out, w_up, w_down) = refs[:10]
    (activated_h, grad_ff_h, second_h, mixed_h, lowered_h) = refs[10:15]
    refs = refs[15 + 5 :]
    rows_o, packed_o, branch_o, inner_o, sums_o = refs[:5]
    outs, parts = ([refs[5:8]] + list(refs[8:12]), refs[12:16])
    landed, paired = (refs[16 : 16 + count], refs[16 + count : 16 + 2 * count])
    refs = refs[16 + 2 * count :]
    ring_buffers = (refs[:count], refs[count : 2 * count], refs[2 * count : 3 * count])
    final, small_v, both_v = refs[3 * count : 3 * count + 3]
    sems = refs[3 * count + 3 : 3 * count + 9]
    refs = refs[3 * count + 9 :]
    (big, cuts, stage, stage_down, big_sem, cut_sem, stage_sem) = refs[:7]
    (buffers, buffer_sems, load_sems, save_sems, slope_sems, inner_sems) = refs[7:13]
    (entry, packed_v, middle_v, slope_v, inner_v, grad_packed_v, mixed_v, branch_v, grad_act_v, total_v, sums_v) = refs[13:]
    parts = [small_v] + list(parts)
    down_part, up_part = (parts[4], parts[3])
    length, width = grad.shape
    devices = 2 * chips
    deep_own = down_part.shape[1]
    ups = w_up.shape[1] // width
    first = lax.axis_index("pipe") == 0
    ring = RingSum(chips, items, parts, outs, landed, paired, ring_buffers, final, sems)
    half, position = (ring.half, ring.position)
    products = Products(chips, width, width // devices, cuts, big, stage, cut_sem, big_sem, stage_sem)
    gains = rows.at[0:2]

    def farthest_first(index):
        step = index // 2
        return ring_chip(position + (half - step if index % 2 == 0 else half + step + 1), chips)

    def keep_down(index):
        return pltpu.make_async_copy(
            stage_down.at[index % 2],
            down_part.at[pl.ds(farthest_first(index) * 2, 2)],
            stage_sem.at[2 + index % 2],
        )

    def cut_down(index):
        return products.load_cut(activated_h, farthest_first(index), index % 2)

    def down_product(index):
        def step():
            slot = index % 2
            if index == 0:
                for at in range(cell + 1):
                    ff_load(at).wait()
            if index + 1 < chips:
                cut_down(index + 1).start()
            cut_down(index).wait()
            product = dot_left(cuts[slot], big[0]).astype(LOW)
            for side in (0, 1):
                stage_down[slot, side] = product[side * deep_own : (side + 1) * deep_own]
            keep_down(index).start()
            if index > 0:
                keep_down(index - 1).wait()

        return step

    def last_down():
        keep_down(chips - 1).wait()

    def far_offset(index):
        return (half - index // 2 if index % 2 == 0 else half + index // 2 + 1) % chips

    def here(ref, at):
        return ref.at[pl.ds(at * length, length)]

    def ff_load(at):
        return pltpu.make_async_copy(here(grad_ff_h, at), here(big.at[0], at), load_sems.at[at])

    def ff_arrived():
        return pltpu.make_async_copy(grad, here(big.at[0], cell), load_sems.at[cell])

    for at in range(cell):
        ff_load(at).start()
    pl.when(first)(lambda: ff_arrived().start())
    pl.when(jnp.logical_not(first))(lambda: ff_load(cell).start())
    cut_down(0).start()

    def own_load(number):
        source, target = ((entry_h, entry), (middle_h, middle_v), (packed_h, packed_v))[number - 1]
        return pltpu.make_async_copy(source.at[cell], target, load_sems.at[cell + 1 + number])

    def slope_load(number):
        window = pl.ds(number * width, width)
        return pltpu.make_async_copy(
            slope_h.at[cell].at[:, window], slope_v.at[number % 2], slope_sems.at[number % 2]
        )

    order, place_up, place_down = ([], {}, {})
    for number in range(ups + 1):
        if number < ups:
            place_down[number] = len(order)
            order.append((w_down, 0, number))
        if number > 0:
            place_up[number - 1] = len(order)
            order.append((w_up, 1, number - 1))
    place_out = len(order)
    order = order + [(w_out, 0, 0)] + [(w_qkv, 1, number) for number in range(3)]
    depth = buffers.shape[0]

    def weight_load(number):
        ref, axis, at = order[number]
        window = pl.ds(at * width, width)
        source = ref.at[:, window] if axis else ref.at[window, :]
        return pltpu.make_async_copy(source, buffers.at[number % depth], buffer_sems.at[number % depth])

    def take(number):
        weight_load(number).wait()
        return buffers.at[number % depth]

    def release(number):
        if number + depth < len(order):
            weight_load(number + depth).start()

    def save(number, wait=False):
        source, target = (
            (branch_v, branch_o.at[pl.ds(cell * length, length)]),
            (grad_packed_v, packed_o.at[pl.ds(cell * length, length)]),
            (sums_v, sums_o.at[cell]),
            (mixed_v, rows_o.at[cell]),
        )[number]
        copy = pltpu.make_async_copy(source, target, save_sems.at[number])
        copy.wait() if wait else copy.start()

    def inner_save(number):
        window = pl.ds(number * width, width)
        return pltpu.make_async_copy(
            inner_v.at[number % 2], inner_o.at[pl.ds(cell * length, length), window], inner_sems.at[number % 2]
        )

    def column_sum(array):
        return jnp.sum(array.astype(F32), axis=0, keepdims=True)

    def begin():
        slope_load(0).start()
        for number in range(depth):
            weight_load(number).start()
        for number in (1, 2, 3):
            own_load(number).start()
        sums_v[7:8, :] = column_sum(grad[...])

    def climb(number):
        def step():
            if number < ups:
                down_block = take(place_down[number])
                grad_act_v[number % 2] = dot_right(grad[...], down_block[...])
                release(place_down[number])
            if number > 0:
                at = number - 1
                slope_load(at).wait()
                if at + 1 < ups:
                    slope_load(at + 1).start()
                up_block = take(place_up[at])
                if at >= 2:
                    inner_save(at - 2).wait()
                inner = (grad_act_v[at % 2] * slope_v[at % 2].astype(F32)).astype(LOW)
                inner_v[at % 2] = inner
                sums_v[8 + at : 9 + at, :] = column_sum(inner)
                part = dot_right(inner, up_block[...])
                if at == 0:
                    total_v[...] = part
                else:
                    total_v[...] += part
                inner_save(at).start()
                release(place_up[at])

        return step

    def turn():
        own_load(2).wait()
        normed, inverse = row_norm(middle_v[...])
        grad_second = total_v[...]
        sums_v[1:2, :] = column_sum(grad_second * normed)
        sums_v[6:7, :] = column_sum(grad_second)
        grad_middle = grad[...].astype(F32) + norm_back(grad_second * gains[1:2, :], normed, inverse)
        middle_v[...] = grad_middle
        branch_v[...] = grad_middle.astype(LOW)
        sums_v[5:6, :] = column_sum(branch_v[...])
        save(0)
        save(0, wait=True)
        for at in range(max(0, ups - 2), ups):
            inner_save(at).wait()

    def outer():
        block = take(place_out)
        mixed_v[...] = dot_right(branch_v[...], block[...]).astype(LOW)
        release(place_out)
        own_load(3).wait()

    def heads(low, high):
        def step():
            attend_back(packed_v, mixed_v, grad_packed_v, width, low, high)

        return step

    def sums():
        save(1)
        sums_v[3:4, :] = column_sum(grad_packed_v[:, pl.ds(0, width)])
        sums_v[4:5, :] = column_sum(grad_packed_v[:, pl.ds(2 * width, width)])
        save(1, wait=True)

    def lower(number):
        def step():
            block = take(place_out + 1 + number)
            part = dot_right(grad_packed_v[:, pl.ds(number * width, width)], block[...])
            if number == 0:
                total_v[...] = part
            else:
                total_v[...] += part
            release(place_out + 1 + number)

        return step

    def finish():
        own_load(1).wait()
        normed, inverse = row_norm(entry[...].astype(F32))
        grad_lowered = total_v[...]
        sums_v[0:1, :] = column_sum(grad_lowered * normed)
        sums_v[2:3, :] = column_sum(grad_lowered)
        mixed_v[...] = (middle_v[...] + norm_back(grad_lowered * gains[0:1, :], normed, inverse)).astype(LOW)
        save(2)
        save(3)

    def lay_small():
        @pl.when(first)
        def _():
            save(2, wait=True)

        copy = pltpu.make_async_copy(sums_o, both_v, load_sems.at[0])
        copy.start()
        copy.wait()
        sums = both_v[0]
        for at in range(1, cell + 1):
            sums = sums + both_v[at]
        own = width // devices
        windows = [pltpu.roll(sums, (width - at * own) % width, 1)[:, :own] for at in range(devices)]
        share = devices // ups
        for device in range(devices):
            small_v[device, 0:8, :] = windows[device][0:8]
            for up in range(ups):
                row = 8 + device // share
                small_v[device, 8 + up : 9 + up, :] = windows[device % share * ups + up][row : row + 1]
            small_v[device, 8 + ups : 16, :] = jnp.zeros((8 - ups, own), F32)

    pairs = width // 128
    downs = [item for item in range(count) if items[item][0] == 4]
    up_items = [item for item in range(count) if items[item][0] == 3]
    outers = [item for item in range(count) if items[item][0] == 2]
    head_items = [item for item in range(count) if items[item][0] == 1]
    smalls = [item for item in range(count) if items[item][0] == 0]
    everywhere = [far_offset(index) for index in range(chips)]

    def only_first(step):
        return lambda: pl.when(first)(step)

    def product(target, left, right, shift, index):
        def step():
            products.run(target, left, right, shift, index)
            if index + 1 == 2 * (right.shape[1] // width):
                products.close(target, right)

        return step

    def all_of(wanted, offsets):
        return [(item, offset) for offset in offsets for item in wanted]

    def opening(left, right, shift):
        return lambda: products.open(left, right, shift)

    def blocks(target, left, right, shift, wanted):
        number = 2 * (right.shape[1] // width)
        made = [(0.3, opening(left, right, shift), [])]
        for index in range(number):
            opens = all_of(wanted, everywhere) if index + 1 == number else []
            made.append((1.9, product(target, left, right, shift, index), opens))
        return made

    steps = []
    for index in range(chips):
        steps.append((1.9, down_product(index), all_of(downs, [far_offset(index - 1)] if index else [])))
        if index == 3:
            steps.append((0.3, only_first(begin), []))
    steps.append((0.7, last_down, all_of(downs, [far_offset(chips - 1)])))
    steps += [(2.0 if number in (0, ups) else 3.5, only_first(climb(number)), []) for number in range(ups + 1)]
    steps.append((3.0, only_first(turn), []))
    steps += blocks(up_part, second_h, inner_o, 1, up_items)
    steps += blocks(parts[2], mixed_h, branch_o, 1, outers)
    steps.append((1.7, only_first(outer), []))
    steps += [(2.5, only_first(heads(low, low + 2)), []) for low in range(0, pairs, 2)]
    steps.append((0.8, only_first(sums), []))
    steps += blocks(parts[1], lowered_h, packed_o, 0, head_items)
    steps += [(1.8, only_first(lower(number)), []) for number in range(3)]
    steps.append((3.0, only_first(finish), []))
    steps.append((2.0, lay_small, all_of(smalls, everywhere)))
    greet((ring.left, ring.right, ring.sibling))
    schedule, _ = ring.arrange(steps, 8.0)
    ring.follow(schedule)
    ring.close()

    @pl.when(first)
    def _():
        save(3, wait=True)


def last_backward(arrived, entry, rows, saved, weights, kept, sides, items, shapes, count):
    chips = count // 2
    length, width = arrived.shape
    deep = weights[2].shape[1]
    cells = kept[0].shape[0]
    rows_in = cells * length
    own = width // count
    vmem, hbm = (pl.BlockSpec(memory_space=pltpu.VMEM), pl.BlockSpec(memory_space=pl.ANY))
    cut = width // 2
    wholes = [(16, own)] + [tuple(shape) for shape in shapes]
    held = [(many,) + wholes[array][1:] for array, _, many, _ in items]
    kinds = [F32 if array == 0 else LOW for array, _, _, _ in items]
    pieces = len(items)
    flops = 2 * length * width * (4 * width + 2 * deep) + 2 * rows_in * width * (4 * width + 2 * deep)
    outs = pl.pallas_call(
        functools.partial(last_backward_kernel, chips, items, cells - 1),
        out_shape=[jax.ShapeDtypeStruct(array.shape, array.dtype) for array in kept]
        + [jax.ShapeDtypeStruct(shape, F32) for shape in ((2, own), (6, 1, own), (1, deep // count))]
        + [jax.ShapeDtypeStruct(shape, F32) for shape in wholes[1:]]
        + [jax.ShapeDtypeStruct((count,) + shape, LOW) for shape in wholes[1:]]
        + [jax.ShapeDtypeStruct((chips - 1,) + shape, kind) for shape, kind in zip(held, kinds)]
        + [jax.ShapeDtypeStruct((chips,) + shape, kind) for shape, kind in zip(held, kinds)],
        in_specs=[vmem, hbm, vmem] + [hbm] * 17,
        out_specs=[hbm] * 5 + [vmem] * 3 + [hbm] * (8 + 2 * pieces),
        input_output_aliases={15 + number: number for number in range(5)},
        scratch_shapes=[pltpu.VMEM((2,) + shape, kind) for shape, kind in zip(held, kinds)] * 3
        + [
            pltpu.VMEM((4, 80, width), F32),
            pltpu.VMEM((count, 16, own), F32),
            pltpu.VMEM((cells, 16, width), F32),
            pltpu.SemaphoreType.DMA((pieces, chips - 1)),
            pltpu.SemaphoreType.DMA((pieces, chips - 1)),
            pltpu.SemaphoreType.DMA((pieces, chips)),
            pltpu.SemaphoreType.DMA((pieces, chips)),
            pltpu.SemaphoreType.DMA((pieces, 6)),
            pltpu.SemaphoreType.DMA((4,)),
            pltpu.VMEM((2, rows_in, width), LOW),
            pltpu.VMEM((2, rows_in, cut), LOW),
            pltpu.VMEM((2, chips, own, width), LOW),
            pltpu.VMEM((2, 2, shapes[3][0], width), LOW),
            pltpu.SemaphoreType.DMA((2,)),
            pltpu.SemaphoreType.DMA((2,)),
            pltpu.SemaphoreType.DMA((4,)),
            pltpu.VMEM((2, width, width), LOW),
            pltpu.SemaphoreType.DMA((2,)),
            pltpu.SemaphoreType.DMA((cells + 4,)),
            pltpu.SemaphoreType.DMA((4,)),
            pltpu.SemaphoreType.DMA((2,)),
            pltpu.SemaphoreType.DMA((2,)),
            pltpu.VMEM((length, width), LOW),
            pltpu.VMEM((length, 3 * width), LOW),
            pltpu.VMEM((length, width), F32),
            pltpu.VMEM((2, length, width), LOW),
            pltpu.VMEM((2, length, width), LOW),
            pltpu.VMEM((length, 3 * width), LOW),
            pltpu.VMEM((length, width), LOW),
            pltpu.VMEM((length, width), LOW),
            pltpu.VMEM((2, length, width), F32),
            pltpu.VMEM((length, width), F32),
            pltpu.VMEM((16, width), F32),
        ],
        compiler_params=pltpu.CompilerParams(
            collective_id=2, has_side_effects=True, vmem_limit_bytes=62 * 2**20
        ),
        cost_estimate=pl.CostEstimate(flops=flops, bytes_accessed=160 * width * width, transcendentals=0),
    )(arrived, entry, rows, *saved, *weights, *sides, *kept)
    return (list(outs[:5]), outs[5:8], outs[8:12])


def on_device(inputs, out_grad, query_counts, gains, shifts, w_qkv, w_out, w_up, b_up, w_down):
    stage = lax.axis_index("pipe")
    stages = lax.axis_size("pipe")
    count = lax.axis_size("dp")
    cell_count, length, width = inputs.shape
    own = width // count
    ups = b_up.shape[1] // own
    deep = ups * width
    deep_own = w_down.shape[1]
    shapes = [
        block_shape(own, 3 * width),
        block_shape(own, width),
        block_shape(own, deep),
        block_shape(deep_own, width),
    ]
    cut = (shapes[3][0] // 2 + 15) // 16 * 16
    items = (
        (0, 0, 16, 0),
        (1, 0, shapes[0][0], 0),
        (2, 0, shapes[1][0], 0),
        (3, 0, shapes[2][0], 1),
        (4, 0, cut, 0),
        (4, cut, shapes[3][0] - cut, 1),
    )
    shards = [small_pack(gains[0], shifts[0], b_up[0], 1)[0]] + [
        array[0].reshape(shape) for array, shape in zip((w_qkv, w_out, w_up, w_down), shapes)
    ]
    fused = stages == 2 and cell_count == 2 and own % 16 == 0 and width % 256 == 0 and 4 * deep_own == width
    if fused:
        piece = own // 2 // 16 * 16
        arrivals = (
            (0, 0, 16, 0),
            (1, 0, own - piece, 0),
            (1, own - piece, piece, 1),
            (2, 0, own, 1),
            (3, 0, own - piece, 0),
            (3, own - piece, piece, 1),
            (4, 0, cut, 0),
            (4, cut, deep_own - cut, 1),
        )
        packs, rows, arrived, later, kept = gather_forward(
            shards, inputs, arrivals, ((0, 1, 2, 3), (4, 5), (6, 7)), count
        )
    else:
        packs = gather(shards, items, count)
        gain_rows, shift_rows, bias = small_split(packs[0].astype(F32), ups)
        blank = jnp.zeros((8 - ups, width), F32)
        rows = jnp.concatenate([gain_rows, shift_rows, bias.reshape(ups, width), blank])
    weights = (
        packs[1].reshape(width, 3 * width),
        packs[2].reshape(width, width),
        packs[3].reshape(width, deep),
        packs[4].reshape(deep, width),
    )
    scales = jnp.sqrt(query_counts.astype(F32) / 500.0)

    def along(value, steps):
        pairs = [(source, source + steps) for source in range(stages) if 0 <= source + steps < stages]
        return lax.ppermute(value, "pipe", pairs)

    entries = [[(inputs, cell) for cell in range(cell_count)]]
    if fused:
        entries.append([(arrived, None), (along(later, 1), None)])
    else:
        kept = None
    for turn in range(1 if fused else 0, stages):
        active = (stage == turn).astype(jnp.int32)[None]
        arrived = []
        for cell in range(cell_count):
            sent, kept = forward_tick(active, entries[turn][cell], rows, weights, kept, cell, cell_count)
            if turn + 1 < stages:
                arrived.append((along(sent, 1), None))
        entries.append(arrived)
    section_out, lowered, packed, mixed, middle, second, activated, slope = kept
    incoming = [((out_grad, cell), scales[cell][None]) for cell in range(cell_count)]
    back = None
    for turn in range(stages - 1, -1, -1):
        active = (stage == turn).astype(jnp.int32)[None]
        arrived = []
        for cell in range(cell_count):
            if fused and turn == 0 and cell == cell_count - 1:
                continue
            sent, back = backward_tick(
                active, incoming[cell], entries[turn][cell], rows, (packed, middle, slope), weights, back, cell, cell_count
            )
            if turn > 0:
                arrived.append(((along(sent, -1), None), jnp.ones((1,), F32)))
        incoming = arrived if turn > 0 else incoming

    def flat(array):
        return array.reshape(cell_count * length, -1)

    input_grads, grad_packed, grad_branch, grad_inner, grad_ff, sums = back
    if fused:
        (input_grads, _, _, _, _), (grad_gains, grad_shifts, grad_bias), shares = last_backward(
            incoming[-1][0][0],
            inputs,
            rows,
            (packed, middle, slope),
            weights,
            (input_grads, flat(grad_packed), flat(grad_branch), flat(grad_inner), sums),
            [flat(array) for array in (activated, grad_ff, second, mixed, lowered)],
            arrivals,
            shapes,
            count,
        )
    else:
        sums = jnp.sum(sums, axis=0)
        small_part = small_pack(sums[0:2], sums[2:8], sums[8 : 8 + ups].reshape(deep), count)
        sides = [flat(array) for array in (lowered, grad_packed, mixed, grad_branch, second, grad_inner, activated, grad_ff)]
        products = [dot_left(sides[at], sides[at + 1]).astype(LOW) for at in (0, 2, 4, 6)]
        parts = [small_part] + [whole.reshape((count,) + shape) for whole, shape in zip(products, shapes)]
        small_share, *shares = scatter(parts, items, count)
        grad_gains, grad_shifts, grad_bias = small_split(small_share[None], ups)
        grad_shifts = grad_shifts[:, None]
    return (
        section_out[None],
        input_grads[None],
        grad_gains[None],
        grad_shifts.swapaxes(0, 1),
        shares[0].reshape(1, own, 3 * width),
        shares[1].reshape(1, own, width),
        shares[2].reshape(1, own, deep),
        grad_bias.reshape(1, ups * own),
        shares[3].reshape(1, deep_own, width),
    )


def solution(mesh):
    in_specs = (
        P("dp", None, None),
        P("dp", None, None),
        P("dp"),
        P("pipe", None, "dp"),
        P("pipe", None, "dp"),
        P("pipe", "dp", None),
        P("pipe", "dp", None),
        P("pipe", "dp", None),
        P("pipe", "dp"),
        P("pipe", "dp", None),
    )
    out_specs = (
        P("pipe", "dp", None, None),
        P("pipe", "dp", None, None),
        P("pipe", None, "dp"),
        P("pipe", None, "dp"),
        P("pipe", "dp", None),
        P("pipe", "dp", None),
        P("pipe", "dp", None),
        P("pipe", "dp"),
        P("pipe", "dp", None),
    )
    return jax.shard_map(
        on_device, mesh=mesh, in_specs=in_specs, out_specs=out_specs, check_vma=False
    )
```

```python
import functools
import math

import jax
import jax.numpy as jnp
from jax import lax
from jax.experimental import pallas as pl
from jax.experimental.pallas import tpu as pltpu
from jax.sharding import PartitionSpec as P

HEAD_DIM = 64
MESH = pl.DeviceIdType.MESH
LOW = jnp.bfloat16
F32 = jnp.float32


def ring_chip(position, chips):
    position = lax.rem(position + 2 * chips, chips)
    half = chips // 2
    return jnp.where(position < half, 2 * position, 2 * (chips - 1 - position) + 1)


def ring_place(chips):
    me = lax.axis_index("dp")
    core = lax.rem(me, 2)
    chip = me // 2
    position = jnp.where(lax.rem(chip, 2) == 0, chip // 2, chips - 1 - chip // 2)
    right = ring_chip(position + 1, chips) * 2 + core
    left = ring_chip(position - 1, chips) * 2 + core
    return (me, core, position, right, left, me + 1 - 2 * core)


def greet(devices):
    barrier = pltpu.get_barrier_semaphore()
    for device in devices:
        pl.semaphore_signal(barrier, inc=1, device_id={"dp": device}, device_id_type=MESH)
    pl.semaphore_wait(barrier, len(devices))


def gather_kernel(chips, arrays, items, *refs):
    count = len(items)
    ring_send, ring_recv, pair_send, pair_recv, own_sem = refs[2 * arrays :]
    shards = [refs[array].at[pl.ds(start, rows)] for array, start, rows, _ in items]
    splits = [way for _, _, _, way in items]
    half = chips // 2
    me, core, position, right, left, sibling = ring_place(chips)
    greet((left, right, sibling))

    def out(item, block):
        array, start, rows, _ = items[item]
        return refs[arrays + array].at[block, pl.ds(start, rows)]

    def owner(step, way):
        return ring_chip(position - step if way == 0 else position + step, chips) * 2 + core

    def travels(item, way, step):
        return step < half or (step == half and splits[item] == way)

    def ring_copy(item, way, step):
        block = owner(step - 1, way)
        return pltpu.make_async_remote_copy(
            src_ref=shards[item] if step == 1 else out(item, block),
            dst_ref=out(item, block),
            send_sem=ring_send.at[item, way, step - 1],
            recv_sem=ring_recv.at[item, way, step - 1],
            device_id={"dp": right if way == 0 else left},
            device_id_type=MESH,
        )

    def pair_copy(item, offset, block, source):
        return pltpu.make_async_remote_copy(
            src_ref=source,
            dst_ref=out(item, block),
            send_sem=pair_send.at[item, offset],
            recv_sem=pair_recv.at[item, offset],
            device_id={"dp": sibling},
            device_id_type=MESH,
        )

    sent, paired, kept = ([], [], [])
    for item in range(count):
        for way in (0, 1):
            if travels(item, way, 1):
                sent.append(ring_copy(item, way, 1))
                sent[-1].start()
    for item in range(count):
        paired.append(pair_copy(item, 0, me, shards[item]))
        paired[-1].start()
        kept.append(pltpu.make_async_copy(shards[item], out(item, me), own_sem.at[item]))
        kept[-1].start()
    for step in range(1, half + 1):
        for item in range(count):
            for way in (0, 1):
                if not travels(item, way, step):
                    continue
                ring_copy(item, way, step).wait_recv()
                if travels(item, way, step + 1):
                    sent.append(ring_copy(item, way, step + 1))
                    sent[-1].start()
                block = owner(step, way)
                offset = step if way == 0 else chips - step
                paired.append(pair_copy(item, offset, block, out(item, block)))
                paired[-1].start()
    for copy in sent:
        copy.wait_send()
    for copy in paired:
        copy.wait()
    for copy in kept:
        copy.wait()


def gather(shards, items, count):
    chips = count // 2
    arrays, pieces = (len(shards), len(items))
    return pl.pallas_call(
        functools.partial(gather_kernel, chips, arrays, items),
        out_shape=[jax.ShapeDtypeStruct((count,) + shard.shape, shard.dtype) for shard in shards],
        in_specs=[pl.BlockSpec(memory_space=pl.ANY)] * arrays,
        out_specs=[pl.BlockSpec(memory_space=pl.ANY)] * arrays,
        scratch_shapes=[
            pltpu.SemaphoreType.DMA((pieces, 2, chips // 2)),
            pltpu.SemaphoreType.DMA((pieces, 2, chips // 2)),
            pltpu.SemaphoreType.DMA((pieces, chips)),
            pltpu.SemaphoreType.DMA((pieces, chips)),
            pltpu.SemaphoreType.DMA((pieces,)),
        ],
        compiler_params=pltpu.CompilerParams(collective_id=0, has_side_effects=True),
    )(*shards)


def scatter_kernel(chips, arrays, items, *refs):
    count = len(items)
    parts, outs, refs = (refs[:arrays], refs[arrays : 2 * arrays], refs[2 * arrays :])
    landed, paired, mine = (refs[:count], refs[count : 2 * count], refs[2 * count : 3 * count])
    ring_send, ring_recv, pair_send, pair_recv, mine_sem = refs[3 * count :]
    splits = [way for _, _, _, way in items]
    half = chips // 2
    me, core, position, right, left, sibling = ring_place(chips)
    greet((left, right, sibling))

    def part(item, block):
        array, start, rows, _ = items[item]
        return parts[array].at[block, pl.ds(start, rows)]

    def first(item, way):
        return 1 if splits[item] == way else 2

    def slot(item, way, step):
        return step - 1 if splits[item] == way else half + step - 2

    def offset_of(step, way):
        return half - step + 1 if way == 0 else chips - (half - step + 1)

    def pair_copy(item, offset):
        block = ring_chip(position + offset, chips) * 2 + 1 - core
        return pltpu.make_async_remote_copy(
            src_ref=part(item, block),
            dst_ref=paired[item].at[offset],
            send_sem=pair_send.at[item, offset],
            recv_sem=pair_recv.at[item, offset],
            device_id={"dp": sibling},
            device_id_type=MESH,
        )

    def ring_copy(item, way, step):
        if step == first(item, way):
            source = paired[item].at[offset_of(step, way)]
        else:
            source = landed[item].at[slot(item, way, step - 1)]
        here = slot(item, way, step)
        return pltpu.make_async_remote_copy(
            src_ref=source,
            dst_ref=landed[item].at[here],
            send_sem=ring_send.at[item, here],
            recv_sem=ring_recv.at[item, here],
            device_id={"dp": right if way == 0 else left},
            device_id_type=MESH,
        )

    def load(item, offset, buffer):
        block = ring_chip(position + offset, chips) * 2 + core
        return pltpu.make_async_copy(part(item, block), mine[item].at[buffer], mine_sem.at[item, buffer])

    plan, uses = ([], [0] * count)
    for step in range(1, half + 2):
        for item in range(count):
            for way in (0, 1):
                if step <= half and step >= first(item, way):
                    plan.append((step, item, way, offset_of(step, way), uses[item] % 2))
                    uses[item] += 1
            if step > half:
                plan.append((step, item, None, 0, uses[item] % 2))
                uses[item] += 1
    for step, item, way, offset, buffer in plan:
        pair_copy(item, offset).start()
    load(plan[0][1], plan[0][3], plan[0][4]).start()
    sent = []
    for number, (step, item, way, offset, buffer) in enumerate(plan):
        if number + 1 < len(plan):
            load(plan[number + 1][1], plan[number + 1][3], plan[number + 1][4]).start()
        load(item, offset, buffer).wait()
        pair_copy(item, offset).wait_recv()
        array, start, rows, _ = items[item]
        kind = parts[array].dtype
        chunk = 16 if rows % 16 == 0 else rows
        from_pair, from_mine, from_ring = (paired[item], mine[item], landed[item])
        if way is None:
            ring_copy(item, 0, half).wait_recv()
            ring_copy(item, 1, half).wait_recv()
            slot_a, slot_b = (slot(item, 0, half), slot(item, 1, half))

            @pl.loop(0, rows // chunk)
            def _(index):
                here = pl.ds(pl.multiple_of(index * chunk, chunk), chunk)
                outs[array][pl.ds(pl.multiple_of(start + index * chunk, chunk), chunk), :] = (
                    from_ring[slot_a, here, :].astype(F32) + from_ring[slot_b, here, :].astype(F32)
                ) + (from_mine[buffer, here, :].astype(F32) + from_pair[offset, here, :].astype(F32))

            continue
        if step == first(item, way):

            @pl.loop(0, rows // chunk)
            def _(index):
                here = pl.ds(pl.multiple_of(index * chunk, chunk), chunk)
                from_pair[offset, here, :] = (
                    from_mine[buffer, here, :].astype(F32) + from_pair[offset, here, :].astype(F32)
                ).astype(kind)

        else:
            ring_copy(item, way, step - 1).wait_recv()
            arrived = slot(item, way, step - 1)

            @pl.loop(0, rows // chunk)
            def _(index):
                here = pl.ds(pl.multiple_of(index * chunk, chunk), chunk)
                from_ring[arrived, here, :] = (
                    from_ring[arrived, here, :].astype(F32)
                    + (from_mine[buffer, here, :].astype(F32) + from_pair[offset, here, :].astype(F32))
                ).astype(kind)

        sent.append(ring_copy(item, way, step))
        sent[-1].start()
    for copy in sent:
        copy.wait_send()
    for step, item, way, offset, buffer in plan:
        pair_copy(item, offset).wait_send()


def scatter(parts, items, count):
    chips = count // 2
    arrays, pieces = (len(parts), len(items))
    shapes = [(rows,) + parts[array].shape[2:] for array, _, rows, _ in items]
    kinds = [parts[array].dtype for array, _, _, _ in items]
    return pl.pallas_call(
        functools.partial(scatter_kernel, chips, arrays, items),
        out_shape=[jax.ShapeDtypeStruct(part.shape[1:], F32) for part in parts],
        in_specs=[pl.BlockSpec(memory_space=pl.ANY)] * arrays,
        out_specs=[pl.BlockSpec(memory_space=pltpu.VMEM)] * arrays,
        scratch_shapes=[pltpu.VMEM((chips - 1,) + shape, kind) for shape, kind in zip(shapes, kinds)]
        + [pltpu.VMEM((chips,) + shape, kind) for shape, kind in zip(shapes, kinds)]
        + [pltpu.VMEM((2,) + shape, kind) for shape, kind in zip(shapes, kinds)]
        + [
            pltpu.SemaphoreType.DMA((pieces, chips - 1)),
            pltpu.SemaphoreType.DMA((pieces, chips - 1)),
            pltpu.SemaphoreType.DMA((pieces, chips)),
            pltpu.SemaphoreType.DMA((pieces, chips)),
            pltpu.SemaphoreType.DMA((pieces, 2)),
        ],
        compiler_params=pltpu.CompilerParams(
            collective_id=1, has_side_effects=True, vmem_limit_bytes=62 * 2**20
        ),
    )(*parts)


def block_shape(rows, columns):
    return (rows, columns) if rows % 16 == 0 else (rows * columns // 128, 128)


def small_pack(gains, shifts, bias, count):
    width = gains.shape[1] // count
    ups = bias.shape[0] // gains.shape[1]
    rows = [
        gains.reshape(2, count, width).swapaxes(0, 1),
        shifts.reshape(6, count, width).swapaxes(0, 1),
        bias.reshape(count, ups, width),
    ]
    blank = jnp.zeros((count, 8 - ups, width), gains.dtype)
    return jnp.concatenate(rows + [blank], axis=1)


def small_split(blocks, ups):
    count, _, width = blocks.shape
    gains = blocks[:, 0:2].swapaxes(0, 1).reshape(2, count * width)
    shifts = blocks[:, 2:8].swapaxes(0, 1).reshape(6, count * width)
    bias = blocks[:, 8 : 8 + ups].reshape(count * ups * width)
    return (gains, shifts, bias)


def row_norm(rows_in):
    center = rows_in - jnp.mean(rows_in, axis=-1, keepdims=True)
    inverse = lax.rsqrt(jnp.mean(center * center, axis=-1, keepdims=True) + 1e-05)
    return (center * inverse, inverse)


def norm_back(grad_rows, normed, inverse):
    return inverse * (
        grad_rows
        - jnp.mean(grad_rows, axis=-1, keepdims=True)
        - normed * jnp.mean(grad_rows * normed, axis=-1, keepdims=True)
    )


def gelu_parts(hidden):
    cumulative = 0.5 * (1.0 + lax.erf(hidden * (1.0 / math.sqrt(2.0))))
    slope = cumulative + hidden * jnp.exp(-0.5 * hidden * hidden) * (1.0 / math.sqrt(2.0 * math.pi))
    return (hidden * cumulative, slope)


def dot(left, right):
    return lax.dot_general(left, right, (((1,), (0,)), ((), ())), preferred_element_type=F32)


def dot_right(left, right):
    return lax.dot_general(left, right, (((1,), (1,)), ((), ())), preferred_element_type=F32)


def dot_left(left, right):
    return lax.dot_general(left, right, (((0,), (0,)), ((), ())), preferred_element_type=F32)


class Stream:
    def __init__(self, blocks, buffers, sems):
        self.blocks, self.buffers, self.sems = (blocks, buffers, sems)
        self.depth = buffers.shape[0]
        self.started = 0
        for _ in range(min(self.depth, len(blocks))):
            self.start()

    def copy(self, number):
        slot = number % self.depth
        return pltpu.make_async_copy(self.blocks[number], self.buffers.at[slot], self.sems.at[slot])

    def start(self):
        self.copy(self.started).start()
        self.started += 1

    def take(self, number):
        self.copy(number).wait()
        return self.buffers.at[number % self.depth]

    def release(self):
        if self.started < len(self.blocks):
            self.start()


def weight_blocks(w_qkv, w_out, w_up, w_down):
    width = w_out.shape[0]
    def cut(ref, axis, number):
        window = pl.ds(number * width, width)
        return ref.at[:, window] if axis else ref.at[window, :]
    heads = [cut(w_qkv, 1, number) for number in range(3)]
    ups = [cut(w_up, 1, number) for number in range(w_up.shape[1] // width)]
    downs = [cut(w_down, 0, number) for number in range(w_down.shape[0] // width)]
    return (heads, w_out, ups, downs)


def head_masks(length):
    return lax.broadcasted_iota(jnp.int32, (length, 128), 1) < HEAD_DIM


def two_heads(array, side):
    blank = jnp.zeros_like(array)
    return jnp.concatenate([jnp.where(side, array, blank), jnp.where(side, blank, array)], axis=0)


def attend(packed, mixed, width, low=0, high=None):
    length = packed.shape[0]
    side = head_masks(length)

    def pair_of(pair):
        start = pair * 128 if isinstance(pair, int) else pl.multiple_of(pair * 128, 128)
        queries = packed[:, pl.ds(start, 128)] * jnp.asarray(1.0 / math.sqrt(HEAD_DIM), LOW)
        keys = two_heads(packed[:, pl.ds(start + width, 128)], side)
        values = two_heads(packed[:, pl.ds(start + 2 * width, 128)], side)
        scores = dot_right(queries, keys)
        probs, totals = ([], [])
        for head in (0, 1):
            mine = scores[:, head * length : (head + 1) * length]
            shifted = jnp.exp(mine - jnp.max(mine, axis=-1, keepdims=True))
            totals.append(1.0 / jnp.sum(shifted, axis=-1, keepdims=True))
            probs.append(shifted.astype(LOW))
        result = dot(jnp.concatenate(probs, axis=1), values)
        mixed[:, pl.ds(start, 128)] = (result * jnp.where(side, totals[0], totals[1])).astype(LOW)

    if high is not None:
        for pair in range(low, high):
            pair_of(pair)
        return

    @pl.loop(0, width // 640)
    def _(index):
        for at in range(5):
            pair_of(index * 5 + at)


def attend_back(packed, grad_mixed, grad_packed, width, low=0, high=None):
    length = packed.shape[0]
    side = head_masks(length)
    scale = 1.0 / math.sqrt(HEAD_DIM)

    def pair_of(pair):
        start = pair * 128 if isinstance(pair, int) else pl.multiple_of(pair * 128, 128)
        queries = packed[:, pl.ds(start, 128)]
        keys = packed[:, pl.ds(start + width, 128)] * jnp.asarray(scale, LOW)
        grads = grad_mixed[:, pl.ds(start, 128)]
        keys_two = two_heads(keys, side)
        queries_two = two_heads(queries, side)
        grads_two = two_heads(grads, side)
        scores = dot_right(keys, queries_two)
        grad_probs = dot_right(packed[:, pl.ds(start + 2 * width, 128)], grads_two)
        probs, grad_scores = ([], [])
        for head in (0, 1):
            mine = slice(head * length, (head + 1) * length)
            shifted = jnp.exp(scores[:, mine] - jnp.max(scores[:, mine], axis=0, keepdims=True))
            prob = shifted * (1.0 / jnp.sum(shifted, axis=0, keepdims=True))
            product = grad_probs[:, mine] * prob
            weighted = jnp.sum(product, axis=0, keepdims=True)
            probs.append(prob.astype(LOW))
            grad_scores.append((product - prob * weighted).astype(LOW))
        beside = jnp.concatenate(grad_scores, axis=1)
        grad_packed[:, pl.ds(start, 128)] = dot_left(jnp.concatenate(grad_scores, axis=0), keys_two).astype(LOW)
        grad_packed[:, pl.ds(start + width, 128)] = (dot(beside, queries_two) * scale).astype(LOW)
        grad_packed[:, pl.ds(start + 2 * width, 128)] = dot(jnp.concatenate(probs, axis=1), grads_two).astype(LOW)

    if high is not None:
        for pair in range(low, high):
            pair_of(pair)
        return

    @pl.loop(0, width // 640)
    def _(index):
        for at in range(5):
            pair_of(index * 5 + at)


def forward_kernel(cell, held, at, active, entry_h, rows, w_qkv, w_out, w_up, w_down, *refs):
    sent_h = refs[held]
    out_h, lowered_h, packed_h, mixed_h, middle_h, second_h, active_h, slope_h = [
        ref.at[cell] for ref in refs[held + 1 : held + 9]
    ]
    (buffers, buffer_sems, save_sems, out_v, lowered_v, packed_v, mixed_v, middle_v) = refs[held + 9 : held + 17]
    (second_v, active_v, slope_v, hidden_v, total_v, entry, entry_sem) = refs[held + 17 :]
    entry = entry_h if at is None else entry
    width = entry.shape[1]
    gains, shifts, bias = (rows.at[0:2], rows.at[2:8], rows.at[8:16])
    ups = w_up.shape[1] // width

    @pl.when(active[0] != 0)
    def _():
        heads, outer, up, down = weight_blocks(w_qkv, w_out, w_up, w_down)
        order = heads + [outer]
        place_up, place_down = ({}, {})
        for number in range(ups + 1):
            if number < ups:
                place_up[number] = len(order)
                order.append(up[number])
            if number > 0:
                place_down[number - 1] = len(order)
                order.append(down[number - 1])
        if at is not None:
            fetched = pltpu.make_async_copy(entry_h.at[at], entry, entry_sem)
            fetched.start()
        saves = []

        def save(source, target):
            saves.append(pltpu.make_async_copy(source, target, save_sems.at[len(saves)]))
            saves[-1].start()

        if at is not None:
            fetched.wait()
        stream = Stream(order, buffers, buffer_sems)
        rows_in = entry[...].astype(F32)
        normed, _ = row_norm(rows_in)
        lowered_v[...] = (normed * gains[0:1, :] + shifts[0:1, :]).astype(LOW)
        save(lowered_v, lowered_h)
        for number in range(3):
            block = stream.take(number)
            window = pl.ds(number * width, width)
            part = dot(lowered_v[...], block[...])
            if number != 1:
                part = part + shifts[1 + number // 2 : 2 + number // 2, :]
            packed_v[:, window] = part.astype(LOW)
            stream.release()
        save(packed_v, packed_h)
        attend(packed_v, mixed_v, width)
        save(mixed_v, mixed_h)
        block = stream.take(3)
        middle = entry[...].astype(F32) + dot(mixed_v[...], block[...]) + shifts[3:4, :]
        middle_v[...] = middle
        stream.release()
        save(middle_v, middle_h)
        normed, _ = row_norm(middle_v[...])
        second_v[...] = (normed * gains[1:2, :] + shifts[4:5, :]).astype(LOW)
        save(second_v, second_h)
        for number in range(ups + 1):
            if number < ups:
                up_block = stream.take(place_up[number])
            if number > 0:
                down_block = stream.take(place_down[number - 1])
            if number < ups:
                hidden_v[number % 2] = dot(second_v[...], up_block[...]) + bias[number : number + 1, :]
            if number > 0:
                window = pl.ds((number - 1) * width, width)
                activated, slope = gelu_parts(hidden_v[(number - 1) % 2])
                active_v[:, window] = activated.astype(LOW)
                slope_v[:, window] = slope.astype(LOW)
                part = dot(active_v[:, window], down_block[...])
                if number == 1:
                    total_v[...] = part
                elif number < ups:
                    total_v[...] += part
                else:
                    out_v[...] = (middle_v[...] + (total_v[...] + part + shifts[5:6, :])).astype(LOW)
                save(active_v.at[:, window], active_h.at[:, window])
                save(slope_v.at[:, window], slope_h.at[:, window])
            if number < ups:
                stream.release()
            if number > 0:
                stream.release()
        save(out_v, sent_h)
        save(out_v, out_h)
        for copy in saves:
            copy.wait()


def kept_shapes(length, width, deep):
    return [
        ((length, width), LOW),
        ((length, width), LOW),
        ((length, 3 * width), LOW),
        ((length, width), LOW),
        ((length, width), F32),
        ((length, width), LOW),
        ((length, deep), LOW),
        ((length, deep), LOW),
    ]


def forward_tick(active, entry, rows, weights, kept, cell, cell_count):
    entry, at = entry
    length, width = entry.shape[-2:]
    deep = weights[2].shape[1]
    ups = deep // width
    shapes = kept_shapes(length, width, deep)
    outs = [jax.ShapeDtypeStruct(*shapes[0])] + [
        jax.ShapeDtypeStruct((cell_count,) + shape, kind) for shape, kind in shapes
    ]
    vmem, hbm = (pl.BlockSpec(memory_space=pltpu.VMEM), pl.BlockSpec(memory_space=pl.ANY))
    flops = 2 * length * width * (4 * width + 2 * deep) + 16 * length * length * width
    kept = () if kept is None else tuple(kept)
    held = len(kept)
    sent, *kept = pl.pallas_call(
        functools.partial(forward_kernel, cell, held, at),
        out_shape=outs,
        in_specs=[pl.BlockSpec(memory_space=pltpu.SMEM), vmem if at is None else hbm, vmem] + [hbm] * (4 + held),
        out_specs=[hbm] * 9,
        input_output_aliases={7 + number: 1 + number for number in range(held)},
        scratch_shapes=[
            pltpu.VMEM((4, width, width), LOW),
            pltpu.SemaphoreType.DMA((4,)),
            pltpu.SemaphoreType.DMA((7 + 2 * ups,)),
        ]
        + [pltpu.VMEM(*shape) for shape in shapes]
        + [
            pltpu.VMEM((2, length, width), F32),
            pltpu.VMEM((length, width), F32),
            pltpu.VMEM((length, width), LOW),
            pltpu.SemaphoreType.DMA,
        ],
        compiler_params=pltpu.CompilerParams(vmem_limit_bytes=60 * 2**20),
        cost_estimate=pl.CostEstimate(
            flops=flops, bytes_accessed=2 * width * (4 * width + 2 * deep), transcendentals=0
        ),
    )(active, entry, rows, *weights, *kept)
    return (sent, kept)


def backward_kernel(cell, held, grad_at, entry_at, active, scale, grad_h, entry_h, rows, *refs):
    packed, middle, slope = [ref.at[cell] for ref in refs[:3]]
    w_qkv, w_out, w_up, w_down = refs[3:7]
    refs = refs[7 + held :]
    sent_h = refs[0]
    rows_h, packed_h, branch_h, inner_h, low_h, sums_h = [ref.at[cell] for ref in refs[1:7]]
    (buffers, buffer_sems, load_sems, save_sems, rows_v, grad_packed_v, branch_v, inner_v, low_v, sums_v) = refs[7:17]
    (packed_v, middle_v, slope_v, mixed_v, grad_act_v, total_v, grad_middle_v, grad, entry) = refs[17:]
    gains = rows.at[0:2]
    grad = grad_h if grad_at is None else grad
    entry_h = entry_h if entry_at is None else entry_h.at[entry_at]
    length, width = entry.shape
    ups = w_up.shape[1] // width

    @pl.when(active[0] != 0)
    def _():
        heads, outer, up, down = weight_blocks(w_qkv, w_out, w_up, w_down)
        loads = [
            pltpu.make_async_copy(slope, slope_v, load_sems.at[0]),
            pltpu.make_async_copy(middle, middle_v, load_sems.at[1]),
            pltpu.make_async_copy(packed, packed_v, load_sems.at[2]),
            pltpu.make_async_copy(entry_h, entry, load_sems.at[3]),
        ]
        if grad_at is not None:
            loads.append(pltpu.make_async_copy(grad_h.at[grad_at], grad, load_sems.at[4]))
            loads[4].start()
        order, place_up, place_down = ([], {}, {})
        for number in range(ups + 1):
            if number < ups:
                place_down[number] = len(order)
                order.append(down[number])
            if number > 0:
                place_up[number - 1] = len(order)
                order.append(up[number - 1])
        place_out = len(order)
        order = order + [outer] + heads
        saves = []

        def save(source, target):
            saves.append(pltpu.make_async_copy(source, target, save_sems.at[len(saves)]))
            saves[-1].start()

        def column_sum(array):
            return jnp.sum(array.astype(F32), axis=0, keepdims=True)

        if grad_at is not None:
            loads[4].wait()
        stream = Stream(order, buffers, buffer_sems)
        loads[0].start()
        low_v[...] = (grad[...].astype(F32) * scale[0]).astype(LOW)
        save(low_v, low_h)
        sums_v[7:8, :] = column_sum(low_v[...])
        for number in range(ups + 1):
            if number == 1:
                loads[0].wait()
                loads[1].start()
            if number == 2:
                loads[2].start()
                loads[3].start()
            if number < ups:
                down_block = stream.take(place_down[number])
            if number > 0:
                up_block = stream.take(place_up[number - 1])
            if number < ups:
                grad_act_v[number % 2] = dot_right(low_v[...], down_block[...])
            if number > 0:
                window = pl.ds((number - 1) * width, width)
                inner = (grad_act_v[(number - 1) % 2] * slope_v[:, window].astype(F32)).astype(LOW)
                inner_v[:, window] = inner
                sums_v[7 + number : 8 + number, :] = column_sum(inner)
                part = dot_right(inner, up_block[...])
                if number == 1:
                    total_v[...] = part
                else:
                    total_v[...] += part
                save(inner_v.at[:, window], inner_h.at[:, window])
            if number < ups:
                stream.release()
            if number > 0:
                stream.release()
        loads[1].wait()
        normed, inverse = row_norm(middle_v[...])
        grad_second = total_v[...]
        sums_v[1:2, :] = column_sum(grad_second * normed)
        sums_v[6:7, :] = column_sum(grad_second)
        grad_middle = grad[...].astype(F32) * scale[0] + norm_back(grad_second * gains[1:2, :], normed, inverse)
        grad_middle_v[...] = grad_middle
        branch_v[...] = grad_middle.astype(LOW)
        sums_v[5:6, :] = column_sum(branch_v[...])
        save(branch_v, branch_h)
        block = stream.take(place_out)
        mixed_v[...] = dot_right(branch_v[...], block[...]).astype(LOW)
        stream.release()
        loads[2].wait()
        attend_back(packed_v, mixed_v, grad_packed_v, width)
        save(grad_packed_v, packed_h)
        sums_v[3:4, :] = column_sum(grad_packed_v[:, pl.ds(0, width)])
        sums_v[4:5, :] = column_sum(grad_packed_v[:, pl.ds(2 * width, width)])
        for number in range(3):
            block = stream.take(place_out + 1 + number)
            part = dot_right(grad_packed_v[:, pl.ds(number * width, width)], block[...])
            if number == 0:
                total_v[...] = part
            else:
                total_v[...] += part
            stream.release()
        loads[3].wait()
        normed, inverse = row_norm(entry[...].astype(F32))
        grad_lowered = total_v[...]
        sums_v[0:1, :] = column_sum(grad_lowered * normed)
        sums_v[2:3, :] = column_sum(grad_lowered)
        rows_v[...] = (grad_middle_v[...] + norm_back(grad_lowered * gains[0:1, :], normed, inverse)).astype(LOW)
        save(sums_v, sums_h)
        save(rows_v, sent_h)
        save(rows_v, rows_h)
        for copy in saves:
            copy.wait()


def backward_tick(active, incoming, entry, rows, saved, weights, kept, cell, cell_count):
    entry, entry_at = entry
    (grad, grad_at), scale = incoming
    length, width = entry.shape[-2:]
    deep = weights[2].shape[1]
    ups = deep // width
    shapes = [
        ((length, width), LOW),
        ((length, 3 * width), LOW),
        ((length, width), LOW),
        ((length, deep), LOW),
        ((length, width), LOW),
        ((16, width), F32),
    ]
    outs = [jax.ShapeDtypeStruct(*shapes[0])] + [
        jax.ShapeDtypeStruct((cell_count,) + shape, kind) for shape, kind in shapes
    ]
    vmem, hbm = (pl.BlockSpec(memory_space=pltpu.VMEM), pl.BlockSpec(memory_space=pl.ANY))
    smem = pl.BlockSpec(memory_space=pltpu.SMEM)
    flops = 2 * length * width * (4 * width + 2 * deep) + 40 * length * length * width
    kept = () if kept is None else tuple(kept)
    held = len(kept)
    sent, *kept = pl.pallas_call(
        functools.partial(backward_kernel, cell, held, grad_at, entry_at),
        out_shape=outs,
        in_specs=[smem] * 2 + [vmem if grad_at is None else hbm, hbm, vmem] + [hbm] * (7 + held),
        out_specs=[hbm] * 7,
        input_output_aliases={12 + number: 1 + number for number in range(held)},
        scratch_shapes=[
            pltpu.VMEM((4, width, width), LOW),
            pltpu.SemaphoreType.DMA((4,)),
            pltpu.SemaphoreType.DMA((5,)),
            pltpu.SemaphoreType.DMA((6 + ups,)),
        ]
        + [pltpu.VMEM(*shape) for shape in shapes]
        + [
            pltpu.VMEM((length, 3 * width), LOW),
            pltpu.VMEM((length, width), F32),
            pltpu.VMEM((length, deep), LOW),
            pltpu.VMEM((length, width), LOW),
            pltpu.VMEM((2, length, width), F32),
            pltpu.VMEM((length, width), F32),
            pltpu.VMEM((length, width), F32),
            pltpu.VMEM((length, width), LOW),
            pltpu.VMEM((length, width), LOW),
        ],
        compiler_params=pltpu.CompilerParams(vmem_limit_bytes=60 * 2**20),
        cost_estimate=pl.CostEstimate(
            flops=flops, bytes_accessed=2 * width * (4 * width + 2 * deep), transcendentals=0
        ),
    )(active, scale, grad, entry, rows, *saved, *weights, *kept)
    return (sent, kept)


def small_rows(small, rows, width, ups):
    devices, _, own = small.shape
    lane = lax.broadcasted_iota(jnp.int32, (own, width), 1)
    depth = lax.broadcasted_iota(jnp.int32, (own, width), 0)
    row = lax.broadcasted_iota(jnp.int32, (16, width), 0)
    across = lax.broadcasted_iota(jnp.int32, (16, width), 1)
    top = jnp.zeros((16, width), F32)
    for device in range(devices):
        spot = jnp.where(lane == depth + device * own, 1.0, 0.0).astype(LOW)
        top = top + dot(small[device], spot)
    rows[0:8, :] = top[0:8]
    share = devices // ups
    for block in range(ups):
        total = jnp.zeros((1, width), F32)
        for index in range(share):
            start = index * ups * own
            spot = jnp.zeros((own, width), F32)
            for up in range(ups):
                spot = spot + jnp.where(lane == depth + (start + up * own), 1.0, 0.0)
            low = start + (row - 8) * own
            inside = (row >= 8) & (row < 8 + ups) & (across >= low) & (across < low + own)
            placed = dot(small[block * share + index], spot.astype(LOW))
            total = total + jnp.sum(jnp.where(inside, placed, 0.0), axis=0, keepdims=True)
        rows[8 + block : 9 + block, :] = total


def gather_forward_kernel(chips, items, groups, cells, *refs):
    shards, inputs_h = (refs[:5], refs[5])
    outs, rows_h, arrived_h, later_h = (refs[6:11], refs[11], refs[12], refs[13])
    out_h, lowered_h, packed_h, mixed_h, middle_h, second_h, active_h, slope_h = refs[14:22]
    (ring_send, ring_recv, pair_send, pair_recv, own_sem, hop_send, hop_recv) = refs[22:29]
    (load_sem, save_sem, wide_sem, deep_sem) = refs[29:33]
    (small_v, rows_v, entry_v, out_v, lowered_v, packed_v, mixed_v, middle_v, second_v, active_v, slope_v) = refs[33:44]
    (total_v, hidden_v, wide_v, deep_v) = refs[44:]
    length, width = entry_v.shape[1:]
    ups = active_v.shape[2] // width
    half = chips // 2
    me, core, position, right, left, sibling = ring_place(chips)
    stage = lax.axis_index("pipe")
    first = stage == 0
    barrier = pltpu.get_barrier_semaphore()
    for device in (left, right, sibling):
        pl.semaphore_signal(barrier, inc=1, device_id={"dp": device}, device_id_type=MESH)
    pl.semaphore_signal(barrier, inc=1, device_id={"pipe": 1 - stage}, device_id_type=MESH)
    pl.semaphore_wait(barrier, 4)

    def shard(item):
        array, start, rows, _ = items[item]
        return shards[array].at[pl.ds(start, rows)]

    def out(item, block):
        array, start, rows, _ = items[item]
        return outs[array].at[block, pl.ds(start, rows)]

    def owner(step, way):
        return ring_chip(position - step if way == 0 else position + step, chips) * 2 + core

    def travels(item, way, step):
        return step < half or (step == half and items[item][3] == way)

    def ring_copy(item, way, step):
        block = owner(step - 1, way)
        return pltpu.make_async_remote_copy(
            src_ref=shard(item) if step == 1 else out(item, block),
            dst_ref=out(item, block),
            send_sem=ring_send.at[item, way, step - 1],
            recv_sem=ring_recv.at[item, way, step - 1],
            device_id={"dp": right if way == 0 else left},
            device_id_type=MESH,
        )

    def pair_copy(item, offset, block, source):
        return pltpu.make_async_remote_copy(
            src_ref=source,
            dst_ref=out(item, block),
            send_sem=pair_send.at[item, offset],
            recv_sem=pair_recv.at[item, offset],
            device_id={"dp": sibling},
            device_id_type=MESH,
        )

    def own_copy(item):
        return pltpu.make_async_copy(shard(item), out(item, me), own_sem.at[item])

    sent, paired = ([], [])

    def open_group(group):
        for item in group:
            for way in (0, 1):
                if travels(item, way, 1):
                    sent.append(ring_copy(item, way, 1))
                    sent[-1].start()
        for item in group:
            paired.append(pair_copy(item, 0, me, shard(item)))
            paired[-1].start()
            own_copy(item).start()

    def ring_step(item, way, step):
        ring_copy(item, way, step).wait_recv()
        if travels(item, way, step + 1):
            sent.append(ring_copy(item, way, step + 1))
            sent[-1].start()
        block = owner(step, way)
        offset = step if way == 0 else chips - step
        paired.append(pair_copy(item, offset, block, out(item, block)))
        paired[-1].start()

    def pair_arrived(item, offset):
        block = ring_chip(position - offset, chips) * 2 + core
        pair_copy(item, offset, block, out(item, block)).wait_recv()

    saves = []

    def save(source, target):
        number = len(saves)
        saves.append(lambda: pltpu.make_async_copy(source(), target(), save_sem.at[number]))
        saves[-1]().start()

    def entry_load(cell):
        return pltpu.make_async_copy(inputs_h.at[cell], entry_v.at[cell], load_sem.at[cell])

    def wide_load(array, column, slot):
        source = outs[array].at[:, :, pl.ds(column * width, width)]
        return pltpu.make_async_copy(source, wide_v.at[slot], wide_sem.at[slot])

    def wide(slot):
        return wide_v[slot].reshape(width, width)

    def gains(number):
        return rows_v[number : number + 1, :]

    def shifts(number):
        return rows_v[2 + number : 3 + number, :]

    def begin(cell):
        def step():
            entry_load(cell).wait()
            normed, _ = row_norm(entry_v[cell].astype(F32))
            lowered_v[cell] = (normed * gains(0) + shifts(0)).astype(LOW)
            save(lambda: lowered_v.at[cell], lambda: lowered_h.at[cell])

        return step

    def project(cell, number):
        def step():
            if cell == 0:
                wide_load(1, number, number).wait()
            part = dot(lowered_v[cell], wide(number))
            if number != 1:
                part = part + shifts(1 + number // 2)
            packed_v[cell, :, pl.ds(number * width, width)] = part.astype(LOW)
            if number == 2:
                save(lambda: packed_v.at[cell], lambda: packed_h.at[cell])

        return step

    def mix(cell, low, high, last):
        def step():
            attend(packed_v.at[cell], mixed_v.at[cell], width, low, high)
            if last:
                save(lambda: mixed_v.at[cell], lambda: mixed_h.at[cell])

        return step

    def join(cell):
        def step():
            if cell == 0:
                wide_load(2, 0, 3).wait()
            middle_v[cell] = entry_v[cell].astype(F32) + dot(mixed_v[cell], wide(3)) + shifts(3)
            save(lambda: middle_v.at[cell], lambda: middle_h.at[cell])

        return step

    def renorm(cell):
        def step():
            middle = middle_v[cell]
            normed, _ = row_norm(middle)
            second_v[cell] = (normed * gains(1) + shifts(4)).astype(LOW)
            total_v[cell] = middle + shifts(5)
            save(lambda: second_v.at[cell], lambda: second_h.at[cell])

        return step

    def rise(cell, number):
        def step():
            if cell == 0:
                wide_load(3, number, number).wait()
            hidden_v[...] = dot(second_v[cell], wide(number)) + rows_v[8 + number : 9 + number, :]

        return step

    def bend(cell, number):
        def step():
            window = pl.ds(number * width, width)
            activated, slope = gelu_parts(hidden_v[...])
            active_v[cell, :, window] = activated.astype(LOW)
            slope_v[cell, :, window] = slope.astype(LOW)
            if number == ups - 1:
                save(lambda: active_v.at[cell], lambda: active_h.at[cell])
                save(lambda: slope_v.at[cell], lambda: slope_h.at[cell])

        return step

    deep_rows = deep_v.shape[1] * deep_v.shape[2]

    def deep_load(offset, slot):
        chip = ring_chip(position - offset, chips)
        return pltpu.make_async_copy(outs[4].at[pl.ds(chip * 2, 2)], deep_v.at[slot], deep_sem.at[slot])

    def fall(cell, offset, slot):
        def step():
            if cell == 0:
                deep_load(offset, slot).wait()
            chip = ring_chip(position - offset, chips)
            window = pl.ds(pl.multiple_of(chip * deep_rows, 128), deep_rows)
            total_v[cell] += dot(active_v[cell, :, window], deep_v[slot].reshape(deep_rows, width))

        return step

    def hop():
        return pltpu.make_async_remote_copy(
            src_ref=out_v.at[0],
            dst_ref=arrived_h,
            send_sem=hop_send,
            recv_sem=hop_recv,
            device_id={"pipe": 1 - stage},
            device_id_type=MESH,
        )

    def finish(cell):
        def step():
            out_v[cell] = total_v[cell].astype(LOW)
            if cell == 0:
                hop().start()
            else:
                save(lambda: out_v.at[cell], lambda: later_h)
            save(lambda: out_v.at[cell], lambda: out_h.at[cell])

        return step

    def on_first(step):
        pl.when(first)(step)

    queue = []

    def ready(group, steps, loads):
        for item in group:
            own_copy(item).wait()
            for offset in range(chips):
                pair_arrived(item, offset)

        @pl.when(first)
        def _():
            for load in loads:
                load().start()

        queue.extend(steps)

    pairs = width // 128
    heads = []
    for cell in range(cells):
        heads.append(begin(cell))
        heads += [project(cell, number) for number in range(3)]
        heads += [mix(cell, low, low + 2, low + 2 >= pairs) for low in range(0, pairs, 2)]
    joins = [make(cell) for cell in range(cells) for make in (join, renorm)]
    def load_ups():
        for number in range(ups):
            wide_load(3, number, number).start()

    climbs = [load_ups]
    climbs += [make(0, number) for number in range(ups) for make in (rise, bend)]

    @pl.when(first)
    def _():
        for cell in range(cells):
            entry_load(cell).start()

    def lay_rows():
        copy = pltpu.make_async_copy(outs[0], small_v, load_sem.at[cells])
        copy.start()
        copy.wait()
        small_rows(small_v, rows_v, width, ups)
        pltpu.make_async_copy(rows_v, rows_h, load_sem.at[cells + 1]).start()

    def ready_small():
        for item in groups[0]:
            if items[item][0] == 0:
                own_copy(item).wait()
                for offset in range(chips):
                    pair_arrived(item, offset)
        lay_rows()

    plan = []
    for number, group in enumerate(groups):
        for step in range(1, half + 1):
            if step == max(1, half - 1) and number + 1 < len(groups):
                plan.append(("open", number + 1))
            for item in group:
                for way in (0, 1):
                    if travels(item, way, step):
                        plan.append(("ring", item, way, step))
            if number == len(groups) - 1:
                plan.append(("deep", step))
        plan.append(("done", number))
    open_group(groups[0])
    late = []
    slots = [0]

    def deep_ready(offsets):
        for offset in offsets:
            for item in groups[-1]:
                if offset == 0:
                    own_copy(item).wait()
                pair_arrived(item, offset)
            slot = slots[0] % deep_v.shape[0]
            slots[0] += 1

            def opening(offset=offset, slot=slot):
                deep_load(offset, slot).start()

            queue.append(opening)
            queue.append(fall(0, offset, slot))

    def serve(limit):
        for _ in range(limit):
            if queue:
                on_first(queue.pop(0))

    for entry in plan:
        if entry[0] == "open":
            open_group(groups[entry[1]])
        elif entry[0] == "ring":
            ring_step(*entry[1:])
            for wait in list(late):
                wait[0] -= 1
                if wait[0] == 0:
                    wait[1]()
                    late.remove(wait)
            serve(2)
        elif entry[0] == "done":
            if entry[1] == 0:
                rest = [item for item in groups[0] if items[item][0] != 0]
                late.append([1, ready_small])
                late.append(
                    [
                        2,
                        lambda: ready(
                            rest,
                            heads + joins,
                            [functools.partial(wide_load, 1, number, number) for number in range(3)]
                            + [functools.partial(wide_load, 2, 0, 3)],
                        ),
                    ]
                )
            elif entry[1] == 1:
                late.append([2, lambda: ready(groups[1], climbs, [])])
        elif entry[0] == "deep":
            step = entry[1]
            if step == 1:
                late.append([3, lambda: deep_ready([0])])
            if step < half:
                late.append([2, lambda step=step: deep_ready([step, chips - step])])
            else:
                for wait in late:
                    wait[1]()
                serve(len(queue))
                deep_ready([half])
    serve(len(queue))

    @pl.when(first)
    def _():
        finish(0)()
        for cell in range(1, cells):
            for offset in (0, 1):
                deep_load(offset, offset).start()
            for number in range(ups):
                rise(cell, number)()
                bend(cell, number)()
            for offset in range(chips):
                deep_load(offset, offset % 2).wait()
                fall(cell, offset, offset % 2)()
                if offset + 2 < chips:
                    deep_load(offset + 2, offset % 2).start()
            finish(cell)()

    for copy in sent:
        copy.wait_send()
    for copy in paired:
        copy.wait_send()
    pltpu.make_async_copy(rows_v, rows_h, load_sem.at[cells + 1]).wait()

    @pl.when(first)
    def _():
        for copy in saves:
            copy().wait()
        hop().wait_send()

    @pl.when(jnp.logical_not(first))
    def _():
        hop().wait_recv()


def gather_forward(shards, inputs, items, groups, count):
    chips = count // 2
    cells, length, width = inputs.shape
    deep = shards[3].shape[1]
    ups = deep // width
    pieces = len(items)
    shapes = kept_shapes(length, width, deep)
    hbm = pl.BlockSpec(memory_space=pl.ANY)
    flops = 2 * cells * length * width * (4 * width + 2 * deep)
    outs = pl.pallas_call(
        functools.partial(gather_forward_kernel, chips, items, groups, cells),
        out_shape=[jax.ShapeDtypeStruct((count,) + shard.shape, shard.dtype) for shard in shards]
        + [
            jax.ShapeDtypeStruct((16, width), F32),
            jax.ShapeDtypeStruct((length, width), LOW),
            jax.ShapeDtypeStruct((length, width), LOW),
        ]
        + [jax.ShapeDtypeStruct((cells,) + shape, kind) for shape, kind in shapes],
        in_specs=[hbm] * 6,
        out_specs=[hbm] * 16,
        scratch_shapes=[
            pltpu.SemaphoreType.DMA((pieces, 2, chips // 2)),
            pltpu.SemaphoreType.DMA((pieces, 2, chips // 2)),
            pltpu.SemaphoreType.DMA((pieces, chips)),
            pltpu.SemaphoreType.DMA((pieces, chips)),
            pltpu.SemaphoreType.DMA((pieces,)),
            pltpu.SemaphoreType.DMA,
            pltpu.SemaphoreType.DMA,
            pltpu.SemaphoreType.DMA((cells + 2,)),
            pltpu.SemaphoreType.DMA((9 * cells,)),
            pltpu.SemaphoreType.DMA((4,)),
            pltpu.SemaphoreType.DMA((2,)),
            pltpu.VMEM((count,) + shards[0].shape, LOW),
            pltpu.VMEM((16, width), F32),
            pltpu.VMEM((cells, length, width), LOW),
        ]
        + [pltpu.VMEM((cells,) + shape, kind) for shape, kind in shapes]
        + [
            pltpu.VMEM((cells, length, width), F32),
            pltpu.VMEM((length, width), F32),
            pltpu.VMEM((4, count, width // count, width), LOW),
            pltpu.VMEM((2, 2, shards[4].shape[0], width), LOW),
        ],
        compiler_params=pltpu.CompilerParams(
            collective_id=3, has_side_effects=True, vmem_limit_bytes=62 * 2**20
        ),
        cost_estimate=pl.CostEstimate(flops=flops, bytes_accessed=8 * width * (4 * width + 2 * deep), transcendentals=0),
    )(*shards, inputs)
    return (outs[:5], outs[5], outs[6], outs[7], list(outs[8:]))


class RingSum:
    def __init__(self, chips, items, parts, outs, landed, paired, buffers, final, sems):
        self.chips, self.items, self.parts, self.outs = (chips, items, parts, outs)
        self.landed, self.paired, self.final = (landed, paired, final)
        self.mine, self.pairs, self.rings = buffers
        self.ring_send, self.ring_recv, self.pair_send, self.pair_recv, self.load_sem, self.final_sem = sems
        self.half = chips // 2
        self.me, self.core, self.position, self.right, self.left, self.sibling = ring_place(chips)
        self.sent, self.final_copies, self.exchanged = ({}, [], [])
        self.uses = [0] * len(items)

    def part(self, item, block):
        array, start, rows, _ = self.items[item]
        return self.parts[array].at[block, pl.ds(start, rows)]

    def first(self, item, way):
        return 1 if self.items[item][3] == way else 2

    def slot_of(self, item, way, step):
        return step - 1 if self.items[item][3] == way else self.half + step - 2

    def offset_of(self, step, way):
        return self.half - step + 1 if way == 0 else self.chips - (self.half - step + 1)

    def pair_copy(self, item, offset):
        block = ring_chip(self.position + offset, self.chips) * 2 + 1 - self.core
        return pltpu.make_async_remote_copy(
            src_ref=self.part(item, block),
            dst_ref=self.paired[item].at[offset],
            send_sem=self.pair_send.at[item, offset],
            recv_sem=self.pair_recv.at[item, offset],
            device_id={"dp": self.sibling},
            device_id_type=MESH,
        )

    def ring_copy(self, item, way, step, buffer=0):
        here = self.slot_of(item, way, step)
        return pltpu.make_async_remote_copy(
            src_ref=self.mine[item].at[buffer],
            dst_ref=self.landed[item].at[here],
            send_sem=self.ring_send.at[item, here],
            recv_sem=self.ring_recv.at[item, here],
            device_id={"dp": self.right if way == 0 else self.left},
            device_id_type=MESH,
        )

    def load_mine(self, item, offset, buffer):
        block = ring_chip(self.position + offset, self.chips) * 2 + self.core
        return pltpu.make_async_copy(self.part(item, block), self.mine[item].at[buffer], self.load_sem.at[item, buffer])

    def load_pair(self, item, offset, buffer):
        return pltpu.make_async_copy(
            self.paired[item].at[offset], self.pairs[item].at[buffer], self.load_sem.at[item, 2 + buffer]
        )

    def load_ring(self, item, way, step, buffer):
        return pltpu.make_async_copy(
            self.landed[item].at[self.slot_of(item, way, step)], self.rings[item].at[buffer], self.load_sem.at[item, 4 + buffer]
        )

    def starts(self, wanted):
        return [
            (step, item, way, self.offset_of(step, way))
            for step in (1, 2)
            for item in wanted
            for way in (0, 1)
            if step == self.first(item, way)
        ]

    def rest(self, wanted, steps):
        return [
            (step, item, way, self.offset_of(step, way))
            for step in steps
            if step <= self.half
            for item in wanted
            for way in (0, 1)
            if step > self.first(item, way)
        ] + [(step, item, None, 0) for step in steps if step > self.half for item in wanted]

    def fetch(self, entry):
        step, item, way, offset, buffer = entry
        if (item, buffer) in self.sent:
            self.sent.pop((item, buffer)).wait_send()
        self.load_mine(item, offset, buffer).start()
        self.pair_copy(item, offset).wait_recv()
        self.load_pair(item, offset, buffer).start()

    def bytes_of(self, item):
        array, _, rows, _ = self.items[item]
        return rows * self.parts[array].shape[2] * self.parts[array].dtype.itemsize

    def arrange(self, steps, ends):
        waiting = self.starts(range(len(self.items)))
        waiting += self.rest(range(len(self.items)), range(2, self.half + 2))
        opened, arrival, sends, used = ({}, {}, {}, [0] * len(self.items))
        clock, link, order, steps = (0.0, [0.0, 0.0], [], list(steps))

        def ready_at(entry):
            step, item, way, offset = entry
            if (item, offset) not in opened:
                return None
            when = opened[(item, offset)]
            sides = (0, 1) if way is None else ((way,) if step > self.first(item, way) else ())
            for side in sides:
                if (item, side, step - 1) not in arrival:
                    return None
                when = max(when, arrival[(item, side, step - 1)])
            return max(when, sends.get((item, used[item] - 2), 0.0))

        while waiting or steps:
            best = None
            for entry in waiting:
                when = ready_at(entry)
                if when is None or (entry[2] is None and (steps or any(other[2] is not None for other in waiting if ready_at(other) is not None and ready_at(other) <= clock))):
                    continue
                backlog = 0.0 if entry[2] is None else max(0.0, link[entry[2]] - max(clock, when))
                rank = (max(when, clock) + 0.5 * backlog, entry[0])
                if best is None or rank < best[0]:
                    best = (rank, entry, when)
            far_off = best is None or best[2] > clock + 0.3
            idle = best is not None and best[1][2] is not None and link[best[1][2]] > clock + ends
            if steps and (far_off or idle):
                spent, step, opens = steps.pop(0)
                clock += spent
                for item, offset in opens:
                    opened[(item, offset)] = clock + 2.0 + self.bytes_of(item) / 2e5
                order.append((step, opens))
                continue
            _, entry, when = best
            waiting.remove(entry)
            step, item, way, offset = entry
            clock = max(clock, when) + 0.8 + self.bytes_of(item) * 1.6e-6
            if way is not None:
                link[way] = max(clock, link[way]) + 2 * self.bytes_of(item) / 9.1e4
                arrival[(item, way, step)] = link[way] + 1.5
                sends[(item, used[item])] = link[way]
            order.append(entry + (used[item] % 2,))
            used[item] += 1
        return order, clock

    def follow(self, order):
        entries = [number for number, action in enumerate(order) if len(action) == 5]
        fetched = set()
        for number, action in enumerate(order):
            if len(action) == 2:
                step, opens = action
                step()
                for item, offset in opens:
                    self.pair_copy(item, offset).start()
                    self.exchanged.append((item, offset))
                continue
            if number not in fetched:
                self.fetch(action)
                fetched.add(number)
            if number + 1 in entries:
                following = order[number + 1]
                if following[1] != action[1]:
                    self.fetch(following)
                    fetched.add(number + 1)
            self.work(action)

    def work(self, entry):
        step, item, way, offset, buffer = entry
        array, start, rows, _ = self.items[item]
        half, final = (self.half, self.final)
        kind = self.parts[array].dtype
        columns = self.parts[array].shape[2]
        chunk = 16
        mine, pairs, rings = (self.mine[item], self.pairs[item], self.rings[item])
        if way is None:
            for side in (0, 1):
                self.ring_copy(item, side, half).wait_recv()
                self.load_ring(item, side, half, side).start()
            self.load_mine(item, offset, buffer).wait()
            self.load_pair(item, offset, buffer).wait()
            for side in (0, 1):
                self.load_ring(item, side, half, side).wait()
            if kind == F32:
                total = (rings[0] + rings[1]) + (mine[buffer] + pairs[buffer])
                gains, shifts, bias = self.outs[array]
                gains[...] = total[0:2]
                for row in range(6):
                    shifts[row] = total[2 + row : 3 + row]
                ups = bias.shape[1] // total.shape[1]
                bias[...] = jnp.concatenate([total[8 + up : 9 + up] for up in range(ups)], axis=1)
                return
            high, wide = (min(rows, final.shape[1]), min(columns, final.shape[2]))
            for top in range(0, rows, high):
                for across in range(0, columns, wide):
                    number = len(self.final_copies)
                    turn = number % final.shape[0]
                    if number >= final.shape[0]:
                        self.final_copies[number - final.shape[0]].wait()
                    span = pl.ds(across, wide)

                    @pl.loop(0, high // chunk)
                    def _(index):
                        here = pl.ds(pl.multiple_of(top + index * chunk, chunk), chunk)
                        final[turn, pl.ds(pl.multiple_of(index * chunk, chunk), chunk), pl.ds(0, wide)] = (
                            rings[0, here, span].astype(F32) + rings[1, here, span].astype(F32)
                        ) + (mine[buffer, here, span].astype(F32) + pairs[buffer, here, span].astype(F32))

                    self.final_copies.append(
                        pltpu.make_async_copy(
                            final.at[turn, pl.ds(0, high), pl.ds(0, wide)],
                            self.outs[array].at[pl.ds(start + top, high), span],
                            self.final_sem.at[turn],
                        )
                    )
                    self.final_copies[-1].start()
            return
        carried = step > self.first(item, way)
        if carried:
            self.ring_copy(item, way, step - 1).wait_recv()
            self.load_ring(item, way, step - 1, buffer).start()
        self.load_mine(item, offset, buffer).wait()
        self.load_pair(item, offset, buffer).wait()
        if carried:
            self.load_ring(item, way, step - 1, buffer).wait()

        @pl.loop(0, rows // chunk)
        def _(index):
            here = pl.ds(pl.multiple_of(index * chunk, chunk), chunk)
            total = mine[buffer, here, :].astype(F32) + pairs[buffer, here, :].astype(F32)
            if carried:
                total = rings[buffer, here, :].astype(F32) + total
            mine[buffer, here, :] = total.astype(kind)

        copy = self.ring_copy(item, way, step, buffer)
        copy.start()
        self.sent[(item, buffer)] = copy

    def close(self):
        for copy in self.sent.values():
            copy.wait_send()
        for item, offset in self.exchanged:
            self.pair_copy(item, offset).wait_send()
        for copy in self.final_copies[-self.final.shape[0] :]:
            copy.wait()


class Products:
    def __init__(self, chips, width, own, cuts, big, stage, cut_sem, big_sem, stage_sem):
        self.chips, self.width, self.own = (chips, width, own)
        self.cuts, self.big, self.stage = (cuts, big, stage)
        self.cut_sem, self.big_sem, self.stage_sem = (cut_sem, big_sem, stage_sem)

    def load_cut(self, source, index, slot):
        cut = self.cuts.shape[2]
        window = pl.ds(pl.multiple_of(index * cut, cut), cut)
        return pltpu.make_async_copy(source.at[:, window], self.cuts.at[slot], self.cut_sem.at[slot])

    def block(self, source, index, slot):
        window = pl.ds(pl.multiple_of(index * self.width, self.width), self.width)
        return pltpu.make_async_copy(source.at[:, window], self.big.at[slot], self.big_sem.at[slot])

    def keep(self, target, index):
        window = pl.ds(index // 2 * self.width, self.width)
        return pltpu.make_async_copy(
            self.stage.at[index % 2],
            target.at[pl.ds(index % 2 * self.chips, self.chips), :, window],
            self.stage_sem.at[index % 2],
        )

    def open(self, left, right, slot):
        for index in (0, 1):
            self.load_cut(left, index, index).start()
        self.block(right, 0, slot).start()

    def run(self, target, left, right, shift, index):
        number = 2 * (right.shape[1] // self.width)
        slot, here = (index % 2, (index // 2 + shift) % 2)
        if index == 0:
            for side in (0, 1):
                self.load_cut(left, side, side).wait()
        if slot == 0:
            self.block(right, index // 2, here).wait()
            if index + 2 < number:
                self.block(right, index // 2 + 1, 1 - here).start()
        if index >= 2:
            self.keep(target, index - 2).wait()
        product = dot_left(self.cuts[slot], self.big[here]).astype(LOW)
        for device in range(self.chips):
            self.stage[slot, device] = product[device * self.own : (device + 1) * self.own]
        self.keep(target, index).start()

    def close(self, target, right):
        number = 2 * (right.shape[1] // self.width)
        for index in (number - 2, number - 1):
            self.keep(target, index).wait()


def last_backward_kernel(chips, items, cell, *refs):
    count = len(items)
    (grad, entry_h, rows, packed_h, middle_h, slope_h, w_qkv, w_out, w_up, w_down) = refs[:10]
    (activated_h, grad_ff_h, second_h, mixed_h, lowered_h) = refs[10:15]
    refs = refs[15 + 5 :]
    rows_o, packed_o, branch_o, inner_o, sums_o = refs[:5]
    outs, parts = ([refs[5:8]] + list(refs[8:12]), refs[12:16])
    landed, paired = (refs[16 : 16 + count], refs[16 + count : 16 + 2 * count])
    refs = refs[16 + 2 * count :]
    ring_buffers = (refs[:count], refs[count : 2 * count], refs[2 * count : 3 * count])
    final, small_v, both_v = refs[3 * count : 3 * count + 3]
    sems = refs[3 * count + 3 : 3 * count + 9]
    refs = refs[3 * count + 9 :]
    (big, cuts, stage, stage_down, big_sem, cut_sem, stage_sem) = refs[:7]
    (buffers, buffer_sems, load_sems, save_sems, slope_sems, inner_sems) = refs[7:13]
    (entry, packed_v, middle_v, slope_v, inner_v, grad_packed_v, mixed_v, branch_v, grad_act_v, total_v, sums_v) = refs[13:]
    parts = [small_v] + list(parts)
    down_part, up_part = (parts[4], parts[3])
    length, width = grad.shape
    devices = 2 * chips
    deep_own = down_part.shape[1]
    ups = w_up.shape[1] // width
    first = lax.axis_index("pipe") == 0
    ring = RingSum(chips, items, parts, outs, landed, paired, ring_buffers, final, sems)
    half, position = (ring.half, ring.position)
    products = Products(chips, width, width // devices, cuts, big, stage, cut_sem, big_sem, stage_sem)
    gains = rows.at[0:2]

    def farthest_first(index):
        step = index // 2
        return ring_chip(position + (half - step if index % 2 == 0 else half + step + 1), chips)

    def keep_down(index):
        return pltpu.make_async_copy(
            stage_down.at[index % 2],
            down_part.at[pl.ds(farthest_first(index) * 2, 2)],
            stage_sem.at[2 + index % 2],
        )

    def cut_down(index):
        return products.load_cut(activated_h, farthest_first(index), index % 2)

    def down_product(index):
        def step():
            slot = index % 2
            if index == 0:
                for at in range(cell + 1):
                    ff_load(at).wait()
            if index + 1 < chips:
                cut_down(index + 1).start()
            cut_down(index).wait()
            product = dot_left(cuts[slot], big[0]).astype(LOW)
            for side in (0, 1):
                stage_down[slot, side] = product[side * deep_own : (side + 1) * deep_own]
            keep_down(index).start()
            if index > 0:
                keep_down(index - 1).wait()

        return step

    def last_down():
        keep_down(chips - 1).wait()

    def far_offset(index):
        return (half - index // 2 if index % 2 == 0 else half + index // 2 + 1) % chips

    def here(ref, at):
        return ref.at[pl.ds(at * length, length)]

    def ff_load(at):
        return pltpu.make_async_copy(here(grad_ff_h, at), here(big.at[0], at), load_sems.at[at])

    def ff_arrived():
        return pltpu.make_async_copy(grad, here(big.at[0], cell), load_sems.at[cell])

    for at in range(cell):
        ff_load(at).start()
    pl.when(first)(lambda: ff_arrived().start())
    pl.when(jnp.logical_not(first))(lambda: ff_load(cell).start())
    cut_down(0).start()

    def own_load(number):
        source, target = ((entry_h, entry), (middle_h, middle_v), (packed_h, packed_v))[number - 1]
        return pltpu.make_async_copy(source.at[cell], target, load_sems.at[cell + 1 + number])

    def slope_load(number):
        window = pl.ds(number * width, width)
        return pltpu.make_async_copy(
            slope_h.at[cell].at[:, window], slope_v.at[number % 2], slope_sems.at[number % 2]
        )

    order, place_up, place_down = ([], {}, {})
    for number in range(ups + 1):
        if number < ups:
            place_down[number] = len(order)
            order.append((w_down, 0, number))
        if number > 0:
            place_up[number - 1] = len(order)
            order.append((w_up, 1, number - 1))
    place_out = len(order)
    order = order + [(w_out, 0, 0)] + [(w_qkv, 1, number) for number in range(3)]
    depth = buffers.shape[0]

    def weight_load(number):
        ref, axis, at = order[number]
        window = pl.ds(at * width, width)
        source = ref.at[:, window] if axis else ref.at[window, :]
        return pltpu.make_async_copy(source, buffers.at[number % depth], buffer_sems.at[number % depth])

    def take(number):
        weight_load(number).wait()
        return buffers.at[number % depth]

    def release(number):
        if number + depth < len(order):
            weight_load(number + depth).start()

    def save(number, wait=False):
        source, target = (
            (branch_v, branch_o.at[pl.ds(cell * length, length)]),
            (grad_packed_v, packed_o.at[pl.ds(cell * length, length)]),
            (sums_v, sums_o.at[cell]),
            (mixed_v, rows_o.at[cell]),
        )[number]
        copy = pltpu.make_async_copy(source, target, save_sems.at[number])
        copy.wait() if wait else copy.start()

    def inner_save(number):
        window = pl.ds(number * width, width)
        return pltpu.make_async_copy(
            inner_v.at[number % 2], inner_o.at[pl.ds(cell * length, length), window], inner_sems.at[number % 2]
        )

    def column_sum(array):
        return jnp.sum(array.astype(F32), axis=0, keepdims=True)

    def begin():
        slope_load(0).start()
        for number in range(depth):
            weight_load(number).start()
        for number in (1, 2, 3):
            own_load(number).start()
        sums_v[7:8, :] = column_sum(grad[...])

    def climb(number):
        def step():
            if number < ups:
                down_block = take(place_down[number])
                grad_act_v[number % 2] = dot_right(grad[...], down_block[...])
                release(place_down[number])
            if number > 0:
                at = number - 1
                slope_load(at).wait()
                if at + 1 < ups:
                    slope_load(at + 1).start()
                up_block = take(place_up[at])
                if at >= 2:
                    inner_save(at - 2).wait()
                inner = (grad_act_v[at % 2] * slope_v[at % 2].astype(F32)).astype(LOW)
                inner_v[at % 2] = inner
                sums_v[8 + at : 9 + at, :] = column_sum(inner)
                part = dot_right(inner, up_block[...])
                if at == 0:
                    total_v[...] = part
                else:
                    total_v[...] += part
                inner_save(at).start()
                release(place_up[at])

        return step

    def turn():
        own_load(2).wait()
        normed, inverse = row_norm(middle_v[...])
        grad_second = total_v[...]
        sums_v[1:2, :] = column_sum(grad_second * normed)
        sums_v[6:7, :] = column_sum(grad_second)
        grad_middle = grad[...].astype(F32) + norm_back(grad_second * gains[1:2, :], normed, inverse)
        middle_v[...] = grad_middle
        branch_v[...] = grad_middle.astype(LOW)
        sums_v[5:6, :] = column_sum(branch_v[...])
        save(0)
        save(0, wait=True)
        for at in range(max(0, ups - 2), ups):
            inner_save(at).wait()

    def outer():
        block = take(place_out)
        mixed_v[...] = dot_right(branch_v[...], block[...]).astype(LOW)
        release(place_out)
        own_load(3).wait()

    def heads(low, high):
        def step():
            attend_back(packed_v, mixed_v, grad_packed_v, width, low, high)

        return step

    def sums():
        save(1)
        sums_v[3:4, :] = column_sum(grad_packed_v[:, pl.ds(0, width)])
        sums_v[4:5, :] = column_sum(grad_packed_v[:, pl.ds(2 * width, width)])
        save(1, wait=True)

    def lower(number):
        def step():
            block = take(place_out + 1 + number)
            part = dot_right(grad_packed_v[:, pl.ds(number * width, width)], block[...])
            if number == 0:
                total_v[...] = part
            else:
                total_v[...] += part
            release(place_out + 1 + number)

        return step

    def finish():
        own_load(1).wait()
        normed, inverse = row_norm(entry[...].astype(F32))
        grad_lowered = total_v[...]
        sums_v[0:1, :] = column_sum(grad_lowered * normed)
        sums_v[2:3, :] = column_sum(grad_lowered)
        mixed_v[...] = (middle_v[...] + norm_back(grad_lowered * gains[0:1, :], normed, inverse)).astype(LOW)
        save(2)
        save(3)

    def lay_small():
        @pl.when(first)
        def _():
            save(2, wait=True)

        copy = pltpu.make_async_copy(sums_o, both_v, load_sems.at[0])
        copy.start()
        copy.wait()
        sums = both_v[0]
        for at in range(1, cell + 1):
            sums = sums + both_v[at]
        own = width // devices
        windows = [pltpu.roll(sums, (width - at * own) % width, 1)[:, :own] for at in range(devices)]
        share = devices // ups
        for device in range(devices):
            small_v[device, 0:8, :] = windows[device][0:8]
            for up in range(ups):
                row = 8 + device // share
                small_v[device, 8 + up : 9 + up, :] = windows[device % share * ups + up][row : row + 1]
            small_v[device, 8 + ups : 16, :] = jnp.zeros((8 - ups, own), F32)

    pairs = width // 128
    downs = [item for item in range(count) if items[item][0] == 4]
    up_items = [item for item in range(count) if items[item][0] == 3]
    outers = [item for item in range(count) if items[item][0] == 2]
    head_items = [item for item in range(count) if items[item][0] == 1]
    smalls = [item for item in range(count) if items[item][0] == 0]
    everywhere = [far_offset(index) for index in range(chips)]

    def only_first(step):
        return lambda: pl.when(first)(step)

    def product(target, left, right, shift, index):
        def step():
            products.run(target, left, right, shift, index)
            if index + 1 == 2 * (right.shape[1] // width):
                products.close(target, right)

        return step

    def all_of(wanted, offsets):
        return [(item, offset) for offset in offsets for item in wanted]

    def opening(left, right, shift):
        return lambda: products.open(left, right, shift)

    def blocks(target, left, right, shift, wanted):
        number = 2 * (right.shape[1] // width)
        made = [(0.3, opening(left, right, shift), [])]
        for index in range(number):
            opens = all_of(wanted, everywhere) if index + 1 == number else []
            made.append((1.9, product(target, left, right, shift, index), opens))
        return made

    steps = []
    for index in range(chips):
        steps.append((1.9, down_product(index), all_of(downs, [far_offset(index - 1)] if index else [])))
        if index == 3:
            steps.append((0.3, only_first(begin), []))
    steps.append((0.7, last_down, all_of(downs, [far_offset(chips - 1)])))
    steps += [(2.0 if number in (0, ups) else 3.5, only_first(climb(number)), []) for number in range(ups + 1)]
    steps.append((3.0, only_first(turn), []))
    steps += blocks(up_part, second_h, inner_o, 1, up_items)
    steps += blocks(parts[2], mixed_h, branch_o, 1, outers)
    steps.append((1.7, only_first(outer), []))
    steps += [(2.5, only_first(heads(low, low + 2)), []) for low in range(0, pairs, 2)]
    steps.append((0.8, only_first(sums), []))
    steps += blocks(parts[1], lowered_h, packed_o, 0, head_items)
    steps += [(1.8, only_first(lower(number)), []) for number in range(3)]
    steps.append((3.0, only_first(finish), []))
    steps.append((2.0, lay_small, all_of(smalls, everywhere)))
    greet((ring.left, ring.right, ring.sibling))
    schedule, _ = ring.arrange(steps, 8.0)
    ring.follow(schedule)
    ring.close()

    @pl.when(first)
    def _():
        save(3, wait=True)


def last_backward(arrived, entry, rows, saved, weights, kept, sides, items, shapes, count):
    chips = count // 2
    length, width = arrived.shape
    deep = weights[2].shape[1]
    cells = kept[0].shape[0]
    rows_in = cells * length
    own = width // count
    vmem, hbm = (pl.BlockSpec(memory_space=pltpu.VMEM), pl.BlockSpec(memory_space=pl.ANY))
    cut = width // 2
    wholes = [(16, own)] + [tuple(shape) for shape in shapes]
    held = [(many,) + wholes[array][1:] for array, _, many, _ in items]
    kinds = [F32 if array == 0 else LOW for array, _, _, _ in items]
    pieces = len(items)
    flops = 2 * length * width * (4 * width + 2 * deep) + 2 * rows_in * width * (4 * width + 2 * deep)
    outs = pl.pallas_call(
        functools.partial(last_backward_kernel, chips, items, cells - 1),
        out_shape=[jax.ShapeDtypeStruct(array.shape, array.dtype) for array in kept]
        + [jax.ShapeDtypeStruct(shape, F32) for shape in ((2, own), (6, 1, own), (1, deep // count))]
        + [jax.ShapeDtypeStruct(shape, F32) for shape in wholes[1:]]
        + [jax.ShapeDtypeStruct((count,) + shape, LOW) for shape in wholes[1:]]
        + [jax.ShapeDtypeStruct((chips - 1,) + shape, kind) for shape, kind in zip(held, kinds)]
        + [jax.ShapeDtypeStruct((chips,) + shape, kind) for shape, kind in zip(held, kinds)],
        in_specs=[vmem, hbm, vmem] + [hbm] * 17,
        out_specs=[hbm] * 5 + [vmem] * 3 + [hbm] * (8 + 2 * pieces),
        input_output_aliases={15 + number: number for number in range(5)},
        scratch_shapes=[pltpu.VMEM((2,) + shape, kind) for shape, kind in zip(held, kinds)] * 3
        + [
            pltpu.VMEM((4, 80, width), F32),
            pltpu.VMEM((count, 16, own), F32),
            pltpu.VMEM((cells, 16, width), F32),
            pltpu.SemaphoreType.DMA((pieces, chips - 1)),
            pltpu.SemaphoreType.DMA((pieces, chips - 1)),
            pltpu.SemaphoreType.DMA((pieces, chips)),
            pltpu.SemaphoreType.DMA((pieces, chips)),
            pltpu.SemaphoreType.DMA((pieces, 6)),
            pltpu.SemaphoreType.DMA((4,)),
            pltpu.VMEM((2, rows_in, width), LOW),
            pltpu.VMEM((2, rows_in, cut), LOW),
            pltpu.VMEM((2, chips, own, width), LOW),
            pltpu.VMEM((2, 2, shapes[3][0], width), LOW),
            pltpu.SemaphoreType.DMA((2,)),
            pltpu.SemaphoreType.DMA((2,)),
            pltpu.SemaphoreType.DMA((4,)),
            pltpu.VMEM((2, width, width), LOW),
            pltpu.SemaphoreType.DMA((2,)),
            pltpu.SemaphoreType.DMA((cells + 4,)),
            pltpu.SemaphoreType.DMA((4,)),
            pltpu.SemaphoreType.DMA((2,)),
            pltpu.SemaphoreType.DMA((2,)),
            pltpu.VMEM((length, width), LOW),
            pltpu.VMEM((length, 3 * width), LOW),
            pltpu.VMEM((length, width), F32),
            pltpu.VMEM((2, length, width), LOW),
            pltpu.VMEM((2, length, width), LOW),
            pltpu.VMEM((length, 3 * width), LOW),
            pltpu.VMEM((length, width), LOW),
            pltpu.VMEM((length, width), LOW),
            pltpu.VMEM((2, length, width), F32),
            pltpu.VMEM((length, width), F32),
            pltpu.VMEM((16, width), F32),
        ],
        compiler_params=pltpu.CompilerParams(
            collective_id=2, has_side_effects=True, vmem_limit_bytes=62 * 2**20
        ),
        cost_estimate=pl.CostEstimate(flops=flops, bytes_accessed=160 * width * width, transcendentals=0),
    )(arrived, entry, rows, *saved, *weights, *sides, *kept)
    return (list(outs[:5]), outs[5:8], outs[8:12])


def on_device(inputs, out_grad, query_counts, gains, shifts, w_qkv, w_out, w_up, b_up, w_down):
    stage = lax.axis_index("pipe")
    stages = lax.axis_size("pipe")
    count = lax.axis_size("dp")
    cell_count, length, width = inputs.shape
    own = width // count
    ups = b_up.shape[1] // own
    deep = ups * width
    deep_own = w_down.shape[1]
    shapes = [
        block_shape(own, 3 * width),
        block_shape(own, width),
        block_shape(own, deep),
        block_shape(deep_own, width),
    ]
    cut = (shapes[3][0] // 2 + 15) // 16 * 16
    items = (
        (0, 0, 16, 0),
        (1, 0, shapes[0][0], 0),
        (2, 0, shapes[1][0], 0),
        (3, 0, shapes[2][0], 1),
        (4, 0, cut, 0),
        (4, cut, shapes[3][0] - cut, 1),
    )
    shards = [small_pack(gains[0], shifts[0], b_up[0], 1)[0]] + [
        array[0].reshape(shape) for array, shape in zip((w_qkv, w_out, w_up, w_down), shapes)
    ]
    fused = stages == 2 and cell_count == 2 and own % 16 == 0 and width % 256 == 0 and 4 * deep_own == width
    if fused:
        piece = own // 2 // 16 * 16
        arrivals = (
            (0, 0, 16, 0),
            (1, 0, own - piece, 0),
            (1, own - piece, piece, 1),
            (2, 0, own, 1),
            (3, 0, own - piece, 0),
            (3, own - piece, piece, 1),
            (4, 0, cut, 0),
            (4, cut, deep_own - cut, 1),
        )
        packs, rows, arrived, later, kept = gather_forward(
            shards, inputs, arrivals, ((0, 1, 2, 3), (4, 5), (6, 7)), count
        )
    else:
        packs = gather(shards, items, count)
        gain_rows, shift_rows, bias = small_split(packs[0].astype(F32), ups)
        blank = jnp.zeros((8 - ups, width), F32)
        rows = jnp.concatenate([gain_rows, shift_rows, bias.reshape(ups, width), blank])
    weights = (
        packs[1].reshape(width, 3 * width),
        packs[2].reshape(width, width),
        packs[3].reshape(width, deep),
        packs[4].reshape(deep, width),
    )
    scales = jnp.sqrt(query_counts.astype(F32) / 500.0)

    def along(value, steps):
        pairs = [(source, source + steps) for source in range(stages) if 0 <= source + steps < stages]
        return lax.ppermute(value, "pipe", pairs)

    entries = [[(inputs, cell) for cell in range(cell_count)]]
    if fused:
        entries.append([(arrived, None), (along(later, 1), None)])
    else:
        kept = None
    for turn in range(1 if fused else 0, stages):
        active = (stage == turn).astype(jnp.int32)[None]
        arrived = []
        for cell in range(cell_count):
            sent, kept = forward_tick(active, entries[turn][cell], rows, weights, kept, cell, cell_count)
            if turn + 1 < stages:
                arrived.append((along(sent, 1), None))
        entries.append(arrived)
    section_out, lowered, packed, mixed, middle, second, activated, slope = kept
    incoming = [((out_grad, cell), scales[cell][None]) for cell in range(cell_count)]
    back = None
    for turn in range(stages - 1, -1, -1):
        active = (stage == turn).astype(jnp.int32)[None]
        arrived = []
        for cell in range(cell_count):
            if fused and turn == 0 and cell == cell_count - 1:
                continue
            sent, back = backward_tick(
                active, incoming[cell], entries[turn][cell], rows, (packed, middle, slope), weights, back, cell, cell_count
            )
            if turn > 0:
                arrived.append(((along(sent, -1), None), jnp.ones((1,), F32)))
        incoming = arrived if turn > 0 else incoming

    def flat(array):
        return array.reshape(cell_count * length, -1)

    input_grads, grad_packed, grad_branch, grad_inner, grad_ff, sums = back
    if fused:
        (input_grads, _, _, _, _), (grad_gains, grad_shifts, grad_bias), shares = last_backward(
            incoming[-1][0][0],
            inputs,
            rows,
            (packed, middle, slope),
            weights,
            (input_grads, flat(grad_packed), flat(grad_branch), flat(grad_inner), sums),
            [flat(array) for array in (activated, grad_ff, second, mixed, lowered)],
            arrivals,
            shapes,
            count,
        )
    else:
        sums = jnp.sum(sums, axis=0)
        small_part = small_pack(sums[0:2], sums[2:8], sums[8 : 8 + ups].reshape(deep), count)
        sides = [flat(array) for array in (lowered, grad_packed, mixed, grad_branch, second, grad_inner, activated, grad_ff)]
        products = [dot_left(sides[at], sides[at + 1]).astype(LOW) for at in (0, 2, 4, 6)]
        parts = [small_part] + [whole.reshape((count,) + shape) for whole, shape in zip(products, shapes)]
        small_share, *shares = scatter(parts, items, count)
        grad_gains, grad_shifts, grad_bias = small_split(small_share[None], ups)
        grad_shifts = grad_shifts[:, None]
    return (
        section_out[None],
        input_grads[None],
        grad_gains[None],
        grad_shifts.swapaxes(0, 1),
        shares[0].reshape(1, own, 3 * width),
        shares[1].reshape(1, own, width),
        shares[2].reshape(1, own, deep),
        grad_bias.reshape(1, ups * own),
        shares[3].reshape(1, deep_own, width),
    )


def solution(mesh):
    in_specs = (
        P("dp", None, None),
        P("dp", None, None),
        P("dp"),
        P("pipe", None, "dp"),
        P("pipe", None, "dp"),
        P("pipe", "dp", None),
        P("pipe", "dp", None),
        P("pipe", "dp", None),
        P("pipe", "dp"),
        P("pipe", "dp", None),
    )
    out_specs = (
        P("pipe", "dp", None, None),
        P("pipe", "dp", None, None),
        P("pipe", None, "dp"),
        P("pipe", None, "dp"),
        P("pipe", "dp", None),
        P("pipe", "dp", None),
        P("pipe", "dp", None),
        P("pipe", "dp"),
        P("pipe", "dp", None),
    )
    return jax.shard_map(
        on_device, mesh=mesh, in_specs=in_specs, out_specs=out_specs, check_vma=False
    )
```
